32 devices in a mesh: dp: 16 (over z, x, core), mem: 2 (over y).
Axes of the slice: x: 2, y: 2, z: 4, core: 2. Of those that a mesh axis runs over, the one named last changes fastest.
Arguments:
- target: bfloat16 [16384, 512], P(('dp', 'mem')), may hold values from -6 to 6
- memory: bfloat16 [128, 512, 512], P('dp', 'mem'), may hold values from -6 to 6
- grad_out: bfloat16 [16384, 512], P(('dp', 'mem')), may hold values from -6 to 6
- tgt_len: int32 [32, 4], P('dp'), may hold values from 1 to 256, 512 in all within a row
- src_len: int32 [32, 4], P('dp'), may hold values from 1 to 512, as said below
- w_qkv: bfloat16 [512, 1536], replicated, may hold values from -0.375 to 0.375
- w_out: bfloat16 [512, 512], replicated, may hold values from -0.75 to 0.75
- wq_cross: bfloat16 [512, 512], replicated, may hold values from -0.375 to 0.375
- wkv_cross: bfloat16 [512, 1024], replicated, may hold values from -0.375 to 0.375
- wo_cross: bfloat16 [512, 512], replicated, may hold values from -0.75 to 0.75
- w_up: bfloat16 [512, 2048], replicated, may hold values from -0.25 to 0.25
- w_down: bfloat16 [2048, 512], replicated, may hold values from -0.125 to 0.125
- ln_gain: float32 [3, 512], replicated, may hold values from 0.5 to 1.5
- ln_bias: float32 [3, 512], replicated, may hold values from -2 to 2
Outputs:
- out: bfloat16 [16384, 512], P(('dp', 'mem'))
- grad_target: bfloat16 [16384, 512], P(('dp', 'mem'))
- grad_memory: bfloat16 [128, 512, 512], P('dp', 'mem')
- grad_w_qkv: float32 [512, 1536], replicated
- grad_w_out: float32 [512, 512], replicated
- grad_wq_cross: float32 [512, 512], replicated
- grad_wkv_cross: float32 [512, 1024], replicated
- grad_wo_cross: float32 [512, 512], replicated
- grad_w_up: float32 [512, 2048], replicated
- grad_w_down: float32 [2048, 512], replicated
- grad_ln_gain: float32 [3, 512], replicated
- grad_ln_bias: float32 [3, 512], replicated
The draws below stay inside these ranges and needn't reach their ends.
Inputs may be any that keep to these rules, and one draw needn't show every extreme that they name: `tgt_len`: each row of 4 lengths sums to 512, and its longest is exactly 256. `src_len`: in each group of 2 rows along dp, some sentence has exactly 512 source positions.
All inputs are finite; a program needn't handle non-finite values.
Results may differ from the reference program's by a relative error of at most 0.025.
The reference program's roundings to bfloat16 on the way count: a program that leaves them out, or rounds other values in their place, can miss the bound.
Values may be sent and summed in bfloat16 or wider, within the bound.
No kernel may reach another device: no remote copies, remote signals or barrier semaphores. Data moves between devices by JAX's collectives and lax.ppermute only.
A program may use at most 128 MiB of HBM per device.

```python
import math
import jax
import jax.numpy as jnp
import numpy as np
from jax import lax

D = 512
HEADS = 8
FF = 2048
HEAD_DIM = 64
TGT_DEV = 512
TGT_MOST = 256
SENT_DEV = 4
SRC_MAX = 512
TOKENS = 16384
SLOTS = 128
N_DP = 16
N_MEM = 2


def draw_src_len(key, part):
    key = jax.random.fold_in(key, 7)
    draw_key, pick_key = jax.random.split(key)
    group_width = N_MEM * SENT_DEV
    lengths = jax.random.randint(draw_key, (N_DP, group_width), 1, SRC_MAX + 1)
    chosen = jax.random.randint(pick_key, (N_DP, 1), 0, group_width)
    slot_index = jnp.arange(group_width)[None, :]
    lengths = jnp.where(slot_index == chosen, SRC_MAX, lengths)
    return lengths.reshape(N_DP * N_MEM, SENT_DEV).astype(jnp.int32)


def block_levels(rng, shape, cuts, low, high):
    def one(dim, shards_of):
        draws = jax.random.uniform(jax.random.fold_in(jax.random.fold_in(rng, 6), dim), (shards_of,), jnp.float32, low / len(cuts), high / len(cuts))
        return jnp.repeat(jnp.exp(draws), shape[dim] // shards_of).reshape((-1,) + (1,) * (len(shape) - dim - 1))

    loudness = one(*cuts[0])
    for cut in cuts[1:]:
        loudness = loudness * one(*cut)
    return loudness


def length_profile(count, total, limit, lean):
    portions = [(1 << 20) // math.isqrt(grade ** lean) + 1 for grade in range(2, count + 1)]
    rest, given = total - limit - (count - 1), [1] * (count - 1)
    while rest > 0:
        movable = [i for i in range(count - 1) if given[i] < limit]
        pool, remaining = sum([portions[i] for i in movable]), rest
        for i in movable:
            more = min(limit - given[i], max(1, remaining * portions[i] // pool), rest)
            given[i] = given[i] + more
            rest = rest - more
    return np.array([limit] + given)


def ragged(key, count, total, bound, slope):
    if count == 2:
        one = jax.random.randint(key, (), max(1, total - bound), min(bound, total - 1) + 1)
        return jnp.stack([one, total - one])
    sizes = jnp.asarray(length_profile(count, total, bound, slope), jnp.int32)
    twos = (count - 1) // 2
    source_of, receiver = sizes[1:1 + 2 * twos:2], sizes[2:2 + 2 * twos:2]
    slack = jnp.minimum(source_of - 1, bound - receiver)
    moved = jax.random.randint(jax.random.fold_in(key, 1), (twos,), 0, 1 << 20) % (slack + 1)
    sizes = sizes.at[1:1 + 2 * twos:2].set(source_of - moved).at[2:2 + 2 * twos:2].set(receiver + moved)
    return sizes[jax.random.permutation(jax.random.fold_in(key, 2), count)]


def scatter_about(rng, shape, deviation, bound, shards=(), kind=jnp.bfloat16):
    values = deviation * jax.random.normal(rng, shape, jnp.float32)
    if shards:
        values = values * block_levels(rng, shape, shards, -0.22, 0.18)
    return jnp.clip(values, -bound, bound).astype(kind)


def setup_inputs(seed: int = 0) -> dict:
    splits = jax.random.split(jax.random.key(seed), 15)
    return {
        "target": scatter_about(splits[0], (TOKENS, D), 1.0, 6.0, ((0, 32),)),
        "memory": scatter_about(splits[1], (SLOTS, SRC_MAX, D), 1.0, 6.0, ((0, 16), (1, 2))),
        "grad_out": scatter_about(splits[2], (TOKENS, D), 1.0, 6.0, ((0, 32),)),
        "tgt_len": jax.vmap(lambda own: ragged(own, SENT_DEV, TGT_DEV, TGT_MOST, 2))(jax.random.split(splits[3], (N_DP * N_MEM))).reshape((N_DP * N_MEM, SENT_DEV)).astype(jnp.int32),
        "src_len": draw_src_len(jax.random.fold_in(splits[14], 71), 0),
        "w_qkv": scatter_about(splits[5], (D, 3 * D), (D // 2) ** -0.5, 0.375),
        "w_out": scatter_about(splits[6], (D, D), (D // 8) ** -0.5, 0.75),
        "wq_cross": scatter_about(splits[7], (D, D), (D // 2) ** -0.5, 0.375),
        "wkv_cross": scatter_about(splits[8], (D, 2 * D), (D // 2) ** -0.5, 0.375),
        "wo_cross": scatter_about(splits[9], (D, D), (D // 8) ** -0.5, 0.75),
        "w_up": scatter_about(splits[10], (D, FF), D ** -0.5, 0.25),
        "w_down": scatter_about(splits[11], (FF, D), FF ** -0.5, 0.125),
        "ln_gain": jnp.clip(1.0 + 0.1 * jax.random.normal(splits[12], (3, D), jnp.float32), 0.5, 1.5),
        "ln_bias": scatter_about(splits[13], (3, D), 0.3, 2.0, (), jnp.float32),
    }


@jax.custom_vjp
def low(v):
    return lax.optimization_barrier(v.astype(jnp.bfloat16)).astype(jnp.float32)

@jax.custom_vjp
def low_back(v):
    return v

def low_keep(v):
    return (low(v), None)

def low_pass(kept, grad):
    return (grad,)

def back_keep(v):
    return (v, None)

def back_low(kept, grad):
    return (low(grad),)
low.defvjp(low_keep, low_pass)
low_back.defvjp(back_keep, back_low)
MASKED = -1e+30
EPSILON = 1e-05
HIGHEST = lax.Precision.HIGHEST

def both_ways(value):
    return low(low_back(value))

def matmul(left_side, right_side):
    return jnp.dot(left_side, right_side, precision=HIGHEST, preferred_element_type=jnp.float32)

def layer_norm(hidden, gain_row, bias_row):
    centre = hidden - lax.optimization_barrier(jnp.mean(hidden, axis=-1, keepdims=True))
    inverse = lax.rsqrt(lax.optimization_barrier(jnp.mean(centre * centre, axis=-1, keepdims=True)) + EPSILON)
    return centre * inverse * gain_row + bias_row

def slot_of_rows(lengths, row_total):
    bounds = jnp.cumsum(lengths)
    positions = jnp.arange(row_total)
    return lax.optimization_barrier(jnp.sum((positions[:, None] >= bounds[None, :]).astype(jnp.int32), axis=1))

def attend(queries, keys_all, values_all, allowed, factor):
    scores = low_back(jnp.einsum('qhd,khd->qhk', queries, keys_all, precision=HIGHEST) * factor)
    scores = jnp.where(allowed[:, None, :], scores, MASKED)
    probs_low = low(jax.nn.softmax(scores, axis=-1))
    return jnp.einsum('qhk,khd->qhd', probs_low, values_all, precision=HIGHEST)

def device_forward(params, rows_in, memory_in, lengths_row, source_row):
    w_qkv, w_out, wq_cross, wkv_cross, wo_cross, w_up, w_down, ln_gain, ln_bias = params
    row_total = rows_in.shape[0]
    model_width = rows_in.shape[1]
    factor = 1.0 / math.sqrt(HEAD_DIM)
    heads_shape = (row_total, HEADS, HEAD_DIM)
    row_slot = slot_of_rows(lengths_row, row_total)
    positions = jnp.arange(row_total)
    self_allowed = (row_slot[:, None] == row_slot[None, :]) & (positions[None, :] <= positions[:, None])
    triple = both_ways(matmul(rows_in, w_qkv))
    queries = triple[:, :model_width].reshape(heads_shape)
    keys_all = triple[:, model_width:2 * model_width].reshape(heads_shape)
    values_all = triple[:, 2 * model_width:].reshape(heads_shape)
    self_attn = both_ways(attend(queries, keys_all, values_all, self_allowed, factor).reshape(row_total, model_width))
    hidden_one = rows_in + low_back(matmul(self_attn, w_out))
    normed_one = layer_norm(hidden_one, ln_gain[0], ln_bias[0])
    cross_query = both_ways(matmul(low(normed_one), wq_cross)).reshape(heads_shape)
    memory_flat = memory_in.reshape(-1, model_width)
    memory_pair = both_ways(matmul(memory_flat, wkv_cross))
    key_count = memory_flat.shape[0]
    cross_key = memory_pair[:, :model_width].reshape(key_count, HEADS, HEAD_DIM)
    cross_value = memory_pair[:, model_width:].reshape(key_count, HEADS, HEAD_DIM)
    key_slot = jnp.arange(key_count) // SRC_MAX
    key_place = jnp.arange(key_count) % SRC_MAX
    live = key_place < jnp.broadcast_to(source_row[:, None], (SENT_DEV, SRC_MAX)).reshape(-1)
    cross_allowed = (row_slot[:, None] == key_slot[None, :]) & live[None, :]
    cross_attn = both_ways(attend(cross_query, cross_key, cross_value, cross_allowed, factor).reshape(row_total, model_width))
    hidden_two = normed_one + low_back(matmul(cross_attn, wo_cross))
    normed_two = layer_norm(hidden_two, ln_gain[1], ln_bias[1])
    upper_in = low_back(matmul(low(normed_two), w_up))
    activation = low(jax.nn.silu(upper_in))
    hidden_three = normed_two + low_back(matmul(activation, w_down))
    return layer_norm(hidden_three, ln_gain[2], ln_bias[2])

def reference(target, memory, grad_out, tgt_len, src_len, w_qkv, w_out, wq_cross, wkv_cross, wo_cross, w_up, w_down, ln_gain, ln_bias):
    devices = N_DP * N_MEM
    params = (w_qkv.astype(jnp.float32), w_out.astype(jnp.float32), wq_cross.astype(jnp.float32), wkv_cross.astype(jnp.float32), wo_cross.astype(jnp.float32), w_up.astype(jnp.float32), w_down.astype(jnp.float32), ln_gain.astype(jnp.float32), ln_bias.astype(jnp.float32))
    rows_all = target.astype(jnp.float32).reshape(devices, TGT_DEV, D)
    memory_all = memory.astype(jnp.float32).reshape(devices, SENT_DEV, SRC_MAX, D)

    def whole(params_in, rows_in, memory_in):

        def advance(unused, inputs):
            rows_one, memory_one, lengths_row, source_row = inputs
            return (unused, device_forward(params_in, rows_one, memory_one, lengths_row, source_row))
        _, outputs = lax.scan(jax.checkpoint(advance), jnp.int32(0), (rows_in, memory_in, tgt_len, src_len))
        return outputs
    outputs, pullback = jax.vjp(whole, params, rows_all, memory_all)
    grad_params, grad_rows, grad_memory = pullback(grad_out.astype(jnp.float32).reshape(devices, TGT_DEV, D))
    return (outputs.reshape(TOKENS, D).astype(jnp.bfloat16), grad_rows.reshape(TOKENS, D).astype(jnp.bfloat16), grad_memory.reshape(SLOTS, SRC_MAX, D).astype(jnp.bfloat16), grad_params[0], grad_params[1], grad_params[2], grad_params[3], grad_params[4], grad_params[5], grad_params[6], grad_params[7], grad_params[8])
```

```python
import functools

import jax
import jax.numpy as jnp
from jax import lax
from jax.experimental import pallas as pl
from jax.experimental.pallas import tpu as pltpu
from jax.sharding import PartitionSpec as P

HEADS = 8
SLAB = 128
MASKED = -1e30
EPSILON = 1e-05
F32 = jnp.float32
BF16 = jnp.bfloat16
VMEM_BYTES = 60 * 1024 * 1024


def dot(left, right):
    return jnp.dot(left, right, preferred_element_type=F32)


def dot_nt(left, right):
    return lax.dot_general(left, right, (((1,), (1,)), ((), ())), preferred_element_type=F32)


def dot_tn(left, right):
    return lax.dot_general(left, right, (((0,), (0,)), ((), ())), preferred_element_type=F32)


def iota(shape, axis):
    return lax.broadcasted_iota(jnp.int32, shape, axis)


def norm_parts(hidden):
    centre = hidden - jnp.mean(hidden, axis=-1, keepdims=True)
    inverse = lax.rsqrt(jnp.mean(centre * centre, axis=-1, keepdims=True) + EPSILON)
    return centre * inverse, inverse


def norm_backward(upstream, unit, inverse, gain_row):
    scaled = upstream * gain_row
    shifted = (
        scaled
        - jnp.mean(scaled, axis=-1, keepdims=True)
        - unit * jnp.mean(scaled * unit, axis=-1, keepdims=True)
    )
    gain_grad = jnp.sum(upstream * unit, axis=0, keepdims=True)
    return inverse * shifted, gain_grad, jnp.sum(upstream, axis=0, keepdims=True)


def sentence_order(me, len_ref):
    count = len_ref.shape[1]
    lengths = [len_ref[me, k] for k in range(count)]
    longest, best, start, running = jnp.int32(0), lengths[0], jnp.int32(0), jnp.int32(0)
    for k in range(1, count):
        running = running + lengths[k - 1]
        more = lengths[k] > best
        longest = jnp.where(more, k, longest)
        start = jnp.where(more, running, start)
        best = jnp.where(more, lengths[k], best)
    order = [longest] + [jnp.where(k < longest, k, k + 1) for k in range(count - 1)]
    bounds = [jnp.int32(0)]
    for k in range(1, count):
        bounds.append(bounds[-1] + len_ref[me, order[k]])
    return order, start, bounds


def moved_rows(index, start, half):
    return jnp.where(index < start, index + half, jnp.where(index < start + half, index - start, index))


def sort_matrix(rows, start):
    spot = moved_rows(iota((rows, rows), 1), start, rows // 2)
    return jnp.where(spot == iota((rows, rows), 0), 1.0, 0.0).astype(BF16)


def unsort_matrix(rows, start):
    spot = moved_rows(iota((rows, rows), 0), start, rows // 2)
    return jnp.where(spot == iota((rows, rows), 1), 1.0, 0.0).astype(BF16)


def side_masks(width):
    side = iota((1, width), 1) % SLAB
    first = jnp.where(side < SLAB // 2, 1.0, 0.0)
    return first.astype(BF16), (1.0 - first).astype(BF16)


def fill_self_bias(bias_ref, bounds, half):
    key = iota((half, half), 0)
    query = iota((half, half), 1)
    first = jnp.zeros((half, half), jnp.int32)
    for bound in bounds[1:-1]:
        first = jnp.where(query >= bound, bound, first)
    causal = key <= query
    bias_ref[0] = jnp.where(causal, 0.0, MASKED)
    bias_ref[1] = jnp.where(causal & (key >= first), 0.0, MASKED)


def fill_cross_bias(bias_ref, me, groups, span, src_ref, order, bounds, half):
    key = iota((span, half), 0)
    query = iota((span, half), 1)
    for j, sentence in enumerate(order):
        for part in range(groups):
            place = lax.rem(me - part + groups, groups) * span + key
            live = place < src_ref[me, sentence]
            if j > 0:
                live = live & (query >= bounds[j - 1]) & (query < bounds[j])
            bias_ref[j, pl.ds(part * span, span), :] = jnp.where(live, 0.0, MASKED)


def softmax_columns(scores):
    top = jnp.max(scores, axis=0, keepdims=True)
    weights = jnp.exp(scores - top)
    total = jnp.sum(weights, axis=0, keepdims=True)
    return (weights * (1.0 / total)).astype(BF16), top + jnp.log(total)


def self_forward_kernel(
    me_ref,
    len_ref,
    target_ref,
    w_qkv_ref,
    w_out_ref,
    wq_ref,
    gain_ref,
    bias_row_ref,
    memory_ref,
    wkv_ref,
    sorted_ref,
    qkv_ref,
    norm_ref,
    attn_t_ref,
    hidden_ref,
    query_ref,
    pair_ref,
    bias_ref,
    q_side_ref,
    value_t_ref,
):
    rows, width = target_ref.shape
    half = rows // 2
    me = me_ref[0]
    order, start, bounds = sentence_order(me, len_ref)
    sorted_rows = dot(sort_matrix(rows, start), target_ref[...]).astype(BF16)
    sorted_ref[...] = sorted_rows
    fill_self_bias(bias_ref, bounds, half)
    queries = dot(sorted_rows, w_qkv_ref[:, :width]).astype(BF16) * 0.125
    queries = queries.astype(BF16)
    qkv_ref[:, :width] = queries
    first, second = side_masks(width)
    q_side_ref[0] = queries * first
    q_side_ref[1] = queries * second
    qkv_ref[:, width : 2 * width] = dot(sorted_rows, w_qkv_ref[:, width : 2 * width]).astype(BF16)
    values = dot(sorted_rows, w_qkv_ref[:, 2 * width :]).astype(BF16)
    qkv_ref[:, 2 * width :] = values
    value_t_ref[...] = values.T

    def pair_step(pair, carry):
        slab = pl.ds(pl.multiple_of(pair * SLAB, SLAB), SLAB)
        key_slab = pl.ds(pl.multiple_of(width + pair * SLAB, SLAB), SLAB)
        for side in range(2):
            head = pair * 2 + side
            feats = pl.ds(pl.multiple_of(head * (SLAB // 2), SLAB // 2), SLAB // 2)
            for block in range(2):
                span = pl.ds(block * half, half)
                scores = dot_nt(qkv_ref[span, key_slab], q_side_ref[side, span, slab]) + bias_ref[block]
                probs, norm = softmax_columns(scores)
                attn_t_ref[feats, span] = dot(value_t_ref[feats, span], probs).astype(BF16)
                norm_ref[pl.ds(head, 1), span] = norm
        return carry

    lax.fori_loop(0, HEADS // 2, pair_step, 0)
    attn = attn_t_ref[...].T
    hidden = sorted_rows.astype(F32) + dot(attn, w_out_ref[...])
    hidden_ref[...] = hidden
    unit, _ = norm_parts(hidden)
    normed = (unit * gain_ref[0:1] + bias_row_ref[0:1]).astype(BF16)
    query_ref[...] = (dot(normed, wq_ref[...]).astype(BF16) * 0.125).astype(BF16)
    count = pair_ref.shape[0]
    for j in range(count):
        block = memory_ref[me * count + order[j]]
        pair_ref[j] = dot(block, wkv_ref[...]).astype(BF16)


def middle_kernel(
    groups,
    me_ref,
    len_ref,
    src_ref,
    hidden_one_ref,
    query_ref,
    pair_mine_ref,
    wkv_ref,
    wo_ref,
    w_up_ref,
    w_down_ref,
    gain_ref,
    bias_row_ref,
    grad_out_ref,
    *refs,
):
    came_refs = refs[: groups - 1]
    (
        out_ref,
        pair_ref,
        norm_ref,
        big_ref,
        wo_grad_ref,
        grad_hidden_ref,
        grad_attn_ref,
        ln_ref,
        bias_ref,
        q_side_ref,
        value_t_ref,
        attn_t_ref,
        active_ref,
        slope_ref,
        total_ref,
    ) = refs[groups - 1 :]
    rows, width = hidden_one_ref.shape
    half = rows // 2
    me = me_ref[0]
    count, span = pair_mine_ref.shape[0], pair_mine_ref.shape[1]
    places = groups * span
    order, start, bounds = sentence_order(me, len_ref)
    fill_cross_bias(bias_ref, me, groups, span, src_ref, order, bounds, half)
    first, second = side_masks(width)
    q_side_ref[0] = query_ref[...] * first
    q_side_ref[1] = query_ref[...] * second
    for j in range(count):
        pair_ref[j, pl.ds(0, span), :] = pair_mine_ref[j]
        for part in range(1, groups):
            block = came_refs[part - 1][order[j]]
            pair_ref[j, pl.ds(part * span, span), :] = dot(block, wkv_ref[...]).astype(BF16)
        value_t_ref[:, pl.ds(j * places, places)] = pair_ref[j, :, width:].T
    others = (count - 1) * places

    def pair_step(pair, carry):
        slab = pl.ds(pl.multiple_of(pair * SLAB, SLAB), SLAB)
        for side in range(2):
            head = pair * 2 + side
            feats = pl.ds(pl.multiple_of(head * (SLAB // 2), SLAB // 2), SLAB // 2)
            scores = dot_nt(pair_ref[0, :, slab], q_side_ref[side, :half, slab]) + bias_ref[0]
            probs, norm = softmax_columns(scores)
            attn_t_ref[feats, :half] = dot(value_t_ref[feats, :places], probs).astype(BF16)
            norm_ref[pl.ds(head, 1), :half] = norm
            keys = pair_ref[1:, :, slab].reshape(others, SLAB)
            scores = dot_nt(keys, q_side_ref[side, half:, slab]) + bias_ref[1:].reshape(others, half)
            probs, norm = softmax_columns(scores)
            attn_t_ref[feats, half:] = dot(value_t_ref[feats, places:], probs).astype(BF16)
            norm_ref[pl.ds(head, 1), half:] = norm
        return carry

    lax.fori_loop(0, HEADS // 2, pair_step, 0)
    attn = attn_t_ref[...].T
    unit_one, _ = norm_parts(hidden_one_ref[...])
    normed_one = unit_one * gain_ref[0:1] + bias_row_ref[0:1]
    hidden_two = normed_one + dot(attn, wo_ref[...])
    unit_two, inverse_two = norm_parts(hidden_two)
    normed_two = unit_two * gain_ref[1:2] + bias_row_ref[1:2]
    normed_two_low = normed_two.astype(BF16)
    total_ref[...] = normed_two
    chunk = width
    chunks = w_down_ref.shape[0] // chunk

    def up_step(c, carry):
        cols = pl.ds(pl.multiple_of(c * chunk, chunk), chunk)
        upper = dot(normed_two_low, w_up_ref[:, cols])
        sigma = 1.0 / (1.0 + jnp.exp(-upper))
        active = (upper * sigma).astype(BF16)
        active_ref[:, cols] = active
        slope_ref[:, cols] = sigma * (1.0 + upper * (1.0 - sigma))
        total_ref[...] += dot(active, w_down_ref[cols, :])
        return carry

    lax.fori_loop(0, chunks, up_step, 0)
    unit_three, inverse_three = norm_parts(total_ref[...])
    result = (unit_three * gain_ref[2:3] + bias_row_ref[2:3]).astype(BF16)
    out_ref[...] = dot(unsort_matrix(rows, start), result).astype(BF16)
    upstream = dot(sort_matrix(rows, start), grad_out_ref[...])
    grad_three, gain_three, bias_three = norm_backward(upstream, unit_three, inverse_three, gain_ref[2:3])
    grad_down = grad_three.astype(BF16)
    total_ref[...] = grad_three
    normed_two_t = normed_two_low.T
    hidden_width = w_down_ref.shape[0]

    def down_step(c, carry):
        cols = pl.ds(pl.multiple_of(c * chunk, chunk), chunk)
        grad_upper = (dot_nt(grad_down, w_down_ref[cols, :]) * slope_ref[:, cols]).astype(BF16)
        big_ref[cols, :] = dot_tn(active_ref[:, cols], grad_down).astype(BF16)
        up_rows = pl.ds(pl.multiple_of(hidden_width + c * chunk, chunk), chunk)
        big_ref[up_rows, :] = dot(normed_two_t, grad_upper).astype(BF16)
        total_ref[...] += dot_nt(grad_upper, w_up_ref[:, cols])
        return carry

    lax.fori_loop(0, chunks, down_step, 0)
    grad_two, gain_two, bias_two = norm_backward(total_ref[...], unit_two, inverse_two, gain_ref[1:2])
    grad_hidden_ref[...] = grad_two
    grad_two_low = grad_two.astype(BF16)
    wo_grad_ref[...] = dot(attn_t_ref[...], grad_two_low).astype(BF16)
    grad_attn_ref[...] = dot_nt(grad_two_low, wo_ref[...]).astype(BF16)
    ln_ref[...] = jnp.concatenate([gain_two, gain_three, bias_two, bias_three], axis=0)


def cross_backward_kernel(
    groups,
    me_ref,
    len_ref,
    src_ref,
    hidden_one_ref,
    query_ref,
    pair_ref,
    norm_ref,
    grad_attn_ref,
    grad_hidden_two_ref,
    wkv_ref,
    wq_ref,
    w_out_ref,
    self_attn_t_ref,
    gain_ref,
    bias_row_ref,
    ln_in_ref,
    wo_grad_ref,
    memory_ref,
    *refs,
):
    came_refs = refs[: groups - 1]
    memory_grad_refs = refs[groups - 1 : 2 * groups - 1]
    (
        mid_ref,
        grad_hidden_ref,
        grad_self_ref,
        bias_ref,
        q_side_ref,
        g_side_ref,
        key_t_ref,
        query_grad_t_ref,
        pair_grad_ref,
        total_ref,
    ) = refs[2 * groups - 1 :]
    rows, width = hidden_one_ref.shape
    half = rows // 2
    me = me_ref[0]
    count, places = pair_ref.shape[0], pair_ref.shape[1]
    span = places // groups
    order, start, bounds = sentence_order(me, len_ref)
    fill_cross_bias(bias_ref, me, groups, span, src_ref, order, bounds, half)
    first, second = side_masks(width)
    q_side_ref[0] = query_ref[...] * first
    q_side_ref[1] = query_ref[...] * second
    g_side_ref[0] = grad_attn_ref[...] * first
    g_side_ref[1] = grad_attn_ref[...] * second
    for j in range(count):
        key_t_ref[:, pl.ds(j * places, places)] = pair_ref[j, :, :width].T
    others = (count - 1) * places

    def pair_step(pair, carry):
        slab = pl.ds(pl.multiple_of(pair * SLAB, SLAB), SLAB)
        value_slab = pl.ds(pl.multiple_of(width + pair * SLAB, SLAB), SLAB)
        for block in range(2):
            span_rows = pl.ds(block * half, half)
            if block == 0:
                keys, values = pair_ref[0, :, slab], pair_ref[0, :, value_slab]
                bias = bias_ref[0]
                key_cols = pl.ds(0, places)
            else:
                keys = pair_ref[1:, :, slab].reshape(others, SLAB)
                values = pair_ref[1:, :, value_slab].reshape(others, SLAB)
                bias = bias_ref[1:].reshape(others, half)
                key_cols = pl.ds(places, others)
            key_sum = value_sum = None
            for side in range(2):
                head = pair * 2 + side
                feats = pl.ds(pl.multiple_of(head * (SLAB // 2), SLAB // 2), SLAB // 2)
                q_rows = q_side_ref[side, span_rows, slab]
                g_rows = g_side_ref[side, span_rows, slab]
                probs = jnp.exp(dot_nt(keys, q_rows) + bias - norm_ref[pl.ds(head, 1), span_rows])
                grad_probs = dot_nt(values, g_rows)
                along = jnp.sum(probs * grad_probs, axis=0, keepdims=True)
                grad_scores = (probs * (grad_probs - along)).astype(BF16)
                value_part = dot(probs.astype(BF16), g_rows)
                key_part = dot(grad_scores, q_rows)
                value_sum = value_part if value_sum is None else value_sum + value_part
                key_sum = key_part if key_sum is None else key_sum + key_part
                query_grad_t_ref[feats, span_rows] = (
                    dot(key_t_ref[feats, key_cols], grad_scores) * 0.125
                ).astype(BF16)
            if block == 0:
                pair_grad_ref[0, :, slab] = key_sum.astype(BF16)
                pair_grad_ref[0, :, value_slab] = value_sum.astype(BF16)
            else:
                pair_grad_ref[1:, :, slab] = key_sum.astype(BF16).reshape(count - 1, places, SLAB)
                pair_grad_ref[1:, :, value_slab] = value_sum.astype(BF16).reshape(count - 1, places, SLAB)
        return carry

    lax.fori_loop(0, HEADS // 2, pair_step, 0)
    for j in range(count):
        for part in range(groups):
            grads = pair_grad_ref[j, pl.ds(part * span, span), :]
            memory_grad_refs[part][order[j]] = dot_nt(grads, wkv_ref[...]).astype(BF16)
            if part == 0:
                block = memory_ref[me * count + order[j]]
            else:
                block = came_refs[part - 1][order[j]]
            term = dot_tn(block, grads)
            if j == 0 and part == 0:
                total_ref[...] = term
            else:
                total_ref[...] += term
    unit_one, inverse_one = norm_parts(hidden_one_ref[...])
    normed_one = (unit_one * gain_ref[0:1] + bias_row_ref[0:1]).astype(BF16)
    query_grad = query_grad_t_ref[...].T
    upstream = grad_hidden_two_ref[...] + dot_nt(query_grad, wq_ref[...])
    grad_one, gain_one, bias_one = norm_backward(upstream, unit_one, inverse_one, gain_ref[0:1])
    grad_hidden_ref[...] = grad_one
    grad_one_low = grad_one.astype(BF16)
    grad_self_ref[...] = dot_nt(grad_one_low, w_out_ref[...]).astype(BF16)
    mid_ref[:width] = wo_grad_ref[...]
    mid_ref[width : 2 * width] = dot_tn(normed_one, query_grad).astype(BF16)
    mid_ref[2 * width : 3 * width] = total_ref[:, :width].astype(BF16)
    mid_ref[3 * width : 4 * width] = total_ref[:, width:].astype(BF16)
    mid_ref[4 * width : 5 * width] = dot(self_attn_t_ref[...], grad_one_low).astype(BF16)
    norms = jnp.concatenate(
        [gain_one, ln_in_ref[0:2], bias_one, ln_in_ref[2:4], jnp.zeros((10, width), F32)], axis=0
    )
    mid_ref[5 * width :] = norms.astype(BF16)


def self_backward_kernel(
    me_ref,
    len_ref,
    qkv_ref,
    norm_ref,
    grad_attn_ref,
    sorted_ref,
    grad_triple_ref,
    last_ref,
    bias_ref,
    q_side_ref,
    g_side_ref,
    key_t_ref,
    query_grad_t_ref,
):
    rows, width = sorted_ref.shape
    half = rows // 2
    order, start, bounds = sentence_order(me_ref[0], len_ref)
    fill_self_bias(bias_ref, bounds, half)
    first, second = side_masks(width)
    q_side_ref[0] = qkv_ref[:, :width] * first
    q_side_ref[1] = qkv_ref[:, :width] * second
    g_side_ref[0] = grad_attn_ref[...] * first
    g_side_ref[1] = grad_attn_ref[...] * second
    key_t_ref[...] = qkv_ref[:, width : 2 * width].T

    def pair_step(pair, carry):
        slab = pl.ds(pl.multiple_of(pair * SLAB, SLAB), SLAB)
        key_slab = pl.ds(pl.multiple_of(width + pair * SLAB, SLAB), SLAB)
        value_slab = pl.ds(pl.multiple_of(2 * width + pair * SLAB, SLAB), SLAB)
        for block in range(2):
            span = pl.ds(block * half, half)
            keys, values = qkv_ref[span, key_slab], qkv_ref[span, value_slab]
            key_sum = value_sum = None
            for side in range(2):
                head = pair * 2 + side
                feats = pl.ds(pl.multiple_of(head * (SLAB // 2), SLAB // 2), SLAB // 2)
                q_rows = q_side_ref[side, span, slab]
                g_rows = g_side_ref[side, span, slab]
                scores = dot_nt(keys, q_rows) + bias_ref[block]
                probs = jnp.exp(scores - norm_ref[pl.ds(head, 1), span])
                grad_probs = dot_nt(values, g_rows)
                along = jnp.sum(probs * grad_probs, axis=0, keepdims=True)
                grad_scores = (probs * (grad_probs - along)).astype(BF16)
                value_part = dot(probs.astype(BF16), g_rows)
                key_part = dot(grad_scores, q_rows)
                value_sum = value_part if value_sum is None else value_sum + value_part
                key_sum = key_part if key_sum is None else key_sum + key_part
                query_grad_t_ref[feats, span] = (
                    dot(key_t_ref[feats, span], grad_scores) * 0.125
                ).astype(BF16)
            grad_triple_ref[span, key_slab] = key_sum.astype(BF16)
            grad_triple_ref[span, value_slab] = value_sum.astype(BF16)
        return carry

    lax.fori_loop(0, HEADS // 2, pair_step, 0)
    grad_triple_ref[:, :width] = query_grad_t_ref[...].T
    sorted_t = sorted_ref[...].T
    for part in range(3):
        cols = slice(part * width, (part + 1) * width)
        last_ref[cols, :] = dot(sorted_t, grad_triple_ref[:, cols]).astype(BF16)


def target_kernel(me_ref, len_ref, grad_triple_ref, w_qkv_ref, grad_hidden_ref, grad_target_ref):
    rows = grad_hidden_ref.shape[0]
    _, start, _ = sentence_order(me_ref[0], len_ref)
    result = grad_hidden_ref[...] + dot_nt(grad_triple_ref[...], w_qkv_ref[...])
    grad_target_ref[...] = dot(unsort_matrix(rows, start), result.astype(BF16)).astype(BF16)


def call(kernel, outs, scratch, scalars, *arrays):
    specs = [pl.BlockSpec(memory_space=pltpu.SMEM)] * scalars
    specs = specs + [pl.BlockSpec(memory_space=pltpu.VMEM)] * (len(arrays) - scalars)
    return pl.pallas_call(
        kernel,
        out_shape=[jax.ShapeDtypeStruct(shape, kind) for shape, kind in outs],
        in_specs=specs,
        out_specs=[pl.BlockSpec(memory_space=pltpu.VMEM)] * len(outs),
        scratch_shapes=[pltpu.VMEM(shape, kind) for shape, kind in scratch],
        compiler_params=pltpu.CompilerParams(vmem_limit_bytes=VMEM_BYTES),
    )(*arrays)


def body(
    target,
    memory,
    grad_out,
    tgt_len,
    src_len,
    w_qkv,
    w_out,
    wq_cross,
    wkv_cross,
    wo_cross,
    w_up,
    w_down,
    ln_gain,
    ln_bias,
):
    rows, width = target.shape
    half = rows // 2
    hidden_width = w_down.shape[0]
    groups = lax.axis_size("mem")
    me = lax.axis_index("mem")
    count = tgt_len.shape[1]
    span = memory.shape[1]
    places = groups * span
    me_array = me.reshape(1).astype(jnp.int32)

    came = []
    for shift in range(1, groups):
        pairs = [(i, (i + shift) % groups) for i in range(groups)]
        sent = lax.dynamic_slice_in_dim(memory, ((me + shift) % groups) * count, count, 0)
        came.append(lax.ppermute(sent, "mem", pairs))

    sorted_rows, qkv, self_norm, self_attn_t, hidden_one, query, pair_mine = call(
        self_forward_kernel,
        [
            ((rows, width), BF16),
            ((rows, 3 * width), BF16),
            ((HEADS, rows), F32),
            ((width, rows), BF16),
            ((rows, width), F32),
            ((rows, width), BF16),
            ((count, span, 2 * width), BF16),
        ],
        [
            ((2, half, half), F32),
            ((2, rows, width), BF16),
            ((width, rows), BF16),
        ],
        2,
        me_array,
        tgt_len,
        target,
        w_qkv,
        w_out,
        wq_cross,
        ln_gain,
        ln_bias,
        memory,
        wkv_cross,
    )
    result_out, pair_all, cross_norm, up_down, wo_grad, grad_hidden_two, grad_attn, ln_part = call(
        functools.partial(middle_kernel, groups),
        [
            ((rows, width), BF16),
            ((count, places, 2 * width), BF16),
            ((HEADS, rows), F32),
            ((2 * hidden_width, width), BF16),
            ((width, width), BF16),
            ((rows, width), F32),
            ((rows, width), BF16),
            ((4, width), F32),
        ],
        [
            ((count, places, half), F32),
            ((2, rows, width), BF16),
            ((width, count * places), BF16),
            ((width, rows), BF16),
            ((rows, hidden_width), BF16),
            ((rows, hidden_width), F32),
            ((rows, width), F32),
        ],
        3,
        me_array,
        tgt_len,
        src_len,
        hidden_one,
        query,
        pair_mine,
        wkv_cross,
        wo_cross,
        w_up,
        w_down,
        ln_gain,
        ln_bias,
        grad_out,
        *came,
    )
    up_down = lax.psum(up_down, ("dp", "mem"))
    *memory_grads, middle, grad_hidden_one, grad_self = call(
        functools.partial(cross_backward_kernel, groups),
        [((count, span, width), BF16)] * groups
        + [
            ((5 * width + 16, width), BF16),
            ((rows, width), F32),
            ((rows, width), BF16),
        ],
        [
            ((count, places, half), F32),
            ((2, rows, width), BF16),
            ((2, rows, width), BF16),
            ((width, count * places), BF16),
            ((width, rows), BF16),
            ((count, places, 2 * width), BF16),
            ((width, 2 * width), F32),
        ],
        3,
        me_array,
        tgt_len,
        src_len,
        hidden_one,
        query,
        pair_all,
        cross_norm,
        grad_attn,
        grad_hidden_two,
        wkv_cross,
        wq_cross,
        w_out,
        self_attn_t,
        ln_gain,
        ln_bias,
        ln_part,
        wo_grad,
        memory,
        *came,
    )
    grad_memory = jnp.zeros(memory.shape, BF16)
    grad_memory = lax.dynamic_update_slice_in_dim(grad_memory, memory_grads[0], me * count, 0)
    for shift in range(1, groups):
        pairs = [(i, (i - shift) % groups) for i in range(groups)]
        back = lax.ppermute(memory_grads[shift], "mem", pairs)
        grad_memory = lax.dynamic_update_slice_in_dim(
            grad_memory, back, ((me + shift) % groups) * count, 0
        )
    grad_triple, last = call(
        self_backward_kernel,
        [((rows, 3 * width), BF16), ((3 * width, width), BF16)],
        [
            ((2, half, half), F32),
            ((2, rows, width), BF16),
            ((2, rows, width), BF16),
            ((width, rows), BF16),
            ((width, rows), BF16),
        ],
        2,
        me_array,
        tgt_len,
        qkv,
        self_norm,
        grad_self,
        sorted_rows,
    )
    (grad_target,) = call(
        target_kernel,
        [((rows, width), BF16)],
        [],
        2,
        me_array,
        tgt_len,
        grad_triple,
        w_qkv,
        grad_hidden_one,
    )
    middle, up_down = lax.optimization_barrier((middle, up_down))
    middle = lax.psum(middle, ("dp", "mem"))
    last, middle = lax.optimization_barrier((last, middle))
    last = lax.psum(last, ("dp", "mem"))

    def unstack(array, parts):
        each = array.shape[0] // parts
        return jnp.concatenate([array[i * each : (i + 1) * each] for i in range(parts)], axis=1)

    up_down, middle, last = [array.astype(F32) for array in (up_down, middle, last)]
    norms = middle[5 * width :]
    return (
        result_out,
        grad_target,
        grad_memory,
        unstack(last, 3),
        middle[4 * width : 5 * width],
        middle[width : 2 * width],
        unstack(middle[2 * width : 4 * width], 2),
        middle[:width],
        unstack(up_down[hidden_width:], hidden_width // width),
        up_down[:hidden_width],
        norms[:3],
        norms[3:6],
    )


def solution(mesh):
    rows_spec = P(("dp", "mem"), None)
    memory_spec = P("dp", "mem", None)
    return jax.shard_map(
        body,
        mesh=mesh,
        in_specs=(rows_spec, memory_spec, rows_spec, P("dp", None), P("dp", None)) + (P(),) * 9,
        out_specs=(rows_spec, rows_spec, memory_spec) + (P(),) * 9,
        check_vma=False,
    )
```

```python
import functools

import jax
import jax.numpy as jnp
from jax import lax
from jax.experimental import pallas as pl
from jax.experimental.pallas import tpu as pltpu
from jax.sharding import PartitionSpec as P

HEADS = 8
SLAB = 128
MASKED = -1e30
EPSILON = 1e-05
F32 = jnp.float32
BF16 = jnp.bfloat16
VMEM_BYTES = 60 * 1024 * 1024
LN_ROWS = 16


def dot(left, right):
    return jnp.dot(left, right, preferred_element_type=F32)


def dot_nt(left, right):
    return lax.dot_general(left, right, (((1,), (1,)), ((), ())), preferred_element_type=F32)


def dot_tn(left, right):
    return lax.dot_general(left, right, (((0,), (0,)), ((), ())), preferred_element_type=F32)


def iota(shape, axis):
    return lax.broadcasted_iota(jnp.int32, shape, axis)


def norm_parts(hidden):
    centre = hidden - jnp.mean(hidden, axis=-1, keepdims=True)
    inverse = lax.rsqrt(jnp.mean(centre * centre, axis=-1, keepdims=True) + EPSILON)
    return centre * inverse, inverse


def norm_backward(upstream, unit, inverse, gain_row):
    scaled = upstream * gain_row
    shifted = (
        scaled
        - jnp.mean(scaled, axis=-1, keepdims=True)
        - unit * jnp.mean(scaled * unit, axis=-1, keepdims=True)
    )
    gain_grad = jnp.sum(upstream * unit, axis=0, keepdims=True)
    return inverse * shifted, gain_grad, jnp.sum(upstream, axis=0, keepdims=True)


def sentence_order(me, len_ref):
    count = len_ref.shape[1]
    lengths = [len_ref[me, k] for k in range(count)]
    longest, best, start, running = jnp.int32(0), lengths[0], jnp.int32(0), jnp.int32(0)
    for k in range(1, count):
        running = running + lengths[k - 1]
        more = lengths[k] > best
        longest = jnp.where(more, k, longest)
        start = jnp.where(more, running, start)
        best = jnp.where(more, lengths[k], best)
    order = [longest] + [jnp.where(k < longest, k, k + 1) for k in range(count - 1)]
    bounds = [jnp.int32(0)]
    for k in range(1, count):
        bounds.append(bounds[-1] + len_ref[me, order[k]])
    return order, start, bounds


def moved_rows(index, start, half):
    return jnp.where(index < start, index + half, jnp.where(index < start + half, index - start, index))


def sort_matrix(rows, start):
    spot = moved_rows(iota((rows, rows), 1), start, rows // 2)
    return jnp.where(spot == iota((rows, rows), 0), 1.0, 0.0).astype(BF16)


def unsort_matrix(rows, start):
    spot = moved_rows(iota((rows, rows), 0), start, rows // 2)
    return jnp.where(spot == iota((rows, rows), 1), 1.0, 0.0).astype(BF16)


def side_masks(width):
    side = iota((1, width), 1) % SLAB
    first = jnp.where(side < SLAB // 2, 1.0, 0.0)
    return first.astype(BF16), (1.0 - first).astype(BF16)


def fill_self_bias(bias_ref, bounds, half):
    key = iota((half, half), 0)
    query = iota((half, half), 1)
    first = jnp.zeros((half, half), jnp.int32)
    for bound in bounds[1:-1]:
        first = jnp.where(query >= bound, bound, first)
    causal = key <= query
    bias_ref[0] = jnp.where(causal, 0.0, MASKED)
    bias_ref[1] = jnp.where(causal & (key >= first), 0.0, MASKED)


def fill_cross_bias(bias_ref, me, groups, span, src_ref, order, bounds, half, rest_only=False):
    key = iota((span, half), 0)
    query = iota((span, half), 1)
    for j, sentence in enumerate(order):
        for part in range(groups):
            place = lax.rem(me - part + groups, groups) * span + key
            live = place < src_ref[me, sentence]
            if j > 0 or rest_only:
                k = j + 1 if rest_only else j
                live = live & (query >= bounds[k - 1]) & (query < bounds[k])
            bias_ref[j, pl.ds(part * span, span), :] = jnp.where(live, 0.0, MASKED)


def softmax_columns(scores):
    top = jnp.max(scores, axis=0, keepdims=True)
    weights = jnp.exp(scores - top)
    total = jnp.sum(weights, axis=0, keepdims=True)
    return (weights * (1.0 / total)).astype(BF16), top + jnp.log(total)


def self_forward_kernel(
    me_ref,
    len_ref,
    target_ref,
    w_qkv_ref,
    w_out_ref,
    wq_ref,
    gain_ref,
    bias_row_ref,
    memory_ref,
    wkv_ref,
    sorted_ref,
    qkv_ref,
    norm_ref,
    attn_t_ref,
    hidden_ref,
    query_ref,
    pair_ref,
    bias_ref,
    q_side_ref,
    value_t_ref,
):
    rows, width = target_ref.shape
    half = rows // 2
    me = me_ref[0]
    order, start, bounds = sentence_order(me, len_ref)
    sorted_rows = dot(sort_matrix(rows, start), target_ref[...]).astype(BF16)
    sorted_ref[...] = sorted_rows
    fill_self_bias(bias_ref, bounds, half)
    queries = dot(sorted_rows, w_qkv_ref[:, :width]).astype(BF16) * 0.125
    queries = queries.astype(BF16)
    qkv_ref[:, :width] = queries
    first, second = side_masks(width)
    q_side_ref[0] = queries * first
    q_side_ref[1] = queries * second
    qkv_ref[:, width : 2 * width] = dot(sorted_rows, w_qkv_ref[:, width : 2 * width]).astype(BF16)
    values = dot(sorted_rows, w_qkv_ref[:, 2 * width :]).astype(BF16)
    qkv_ref[:, 2 * width :] = values
    value_t_ref[...] = values.T

    def pair_step(pair, carry):
        slab = pl.ds(pl.multiple_of(pair * SLAB, SLAB), SLAB)
        key_slab = pl.ds(pl.multiple_of(width + pair * SLAB, SLAB), SLAB)
        for side in range(2):
            head = pair * 2 + side
            feats = pl.ds(pl.multiple_of(head * (SLAB // 2), SLAB // 2), SLAB // 2)
            for block in range(2):
                span = pl.ds(block * half, half)
                scores = dot_nt(qkv_ref[span, key_slab], q_side_ref[side, span, slab]) + bias_ref[block]
                probs, norm = softmax_columns(scores)
                attn_t_ref[feats, span] = dot(value_t_ref[feats, span], probs).astype(BF16)
                norm_ref[pl.ds(head, 1), span] = norm
        return carry

    lax.fori_loop(0, HEADS // 2, pair_step, 0)
    attn = attn_t_ref[...].T
    hidden = sorted_rows.astype(F32) + dot(attn, w_out_ref[...])
    hidden_ref[...] = hidden
    unit, _ = norm_parts(hidden)
    normed = (unit * gain_ref[0:1] + bias_row_ref[0:1]).astype(BF16)
    query_ref[...] = (dot(normed, wq_ref[...]).astype(BF16) * 0.125).astype(BF16)
    count = pair_ref.shape[0]
    for j in range(count):
        block = memory_ref[me * count + order[j]]
        pair_ref[j] = dot(block, wkv_ref[...]).astype(BF16)


def fill_padding(keep_ref, send_ref, used):
    total, width = keep_ref.shape
    if total > used:
        keep_ref[used:, :] = jnp.zeros((total - used, width), BF16)
        send_ref[used:, :] = jnp.zeros((total - used, width), BF16)


def middle_kernel(
    groups,
    me_ref,
    len_ref,
    src_ref,
    hidden_one_ref,
    query_ref,
    pair_mine_ref,
    wkv_ref,
    wo_ref,
    w_up_ref,
    w_down_ref,
    gain_ref,
    bias_row_ref,
    grad_out_ref,
    *refs,
):
    came_refs = refs[: groups - 1]
    (
        out_ref,
        pair_long_ref,
        pair_rest_ref,
        norm_ref,
        keep_ref,
        send_ref,
        grad_hidden_ref,
        grad_attn_ref,
        ln_ref,
        bias_ref,
        q_side_ref,
        value_t_ref,
        attn_t_ref,
        active_ref,
        slope_ref,
        total_ref,
    ) = refs[groups - 1 :]
    rows, width = hidden_one_ref.shape
    half = rows // 2
    me = me_ref[0]
    count, span = pair_mine_ref.shape[0], pair_mine_ref.shape[1]
    places = groups * span
    order, start, bounds = sentence_order(me, len_ref)
    fill_cross_bias(bias_ref, me, groups, span, src_ref, order, bounds, half)
    first, second = side_masks(width)
    q_side_ref[0] = query_ref[...] * first
    q_side_ref[1] = query_ref[...] * second
    for j in range(count):
        pair_ref = pair_long_ref if j == 0 else pair_rest_ref
        first_row = max(j - 1, 0) * places
        pair_ref[pl.ds(first_row, span), :] = pair_mine_ref[j]
        for part in range(1, groups):
            block = came_refs[part - 1][order[j]]
            here = pl.ds(first_row + part * span, span)
            pair_ref[here, :] = dot(block, wkv_ref[...]).astype(BF16)
        value_t_ref[:, pl.ds(j * places, places)] = pair_ref[pl.ds(first_row, places), width:].T
    others = (count - 1) * places

    def pair_step(pair, carry):
        slab = pl.ds(pl.multiple_of(pair * SLAB, SLAB), SLAB)
        for side in range(2):
            head = pair * 2 + side
            feats = pl.ds(pl.multiple_of(head * (SLAB // 2), SLAB // 2), SLAB // 2)
            scores = dot_nt(pair_long_ref[:, slab], q_side_ref[side, :half, slab]) + bias_ref[0]
            probs, norm = softmax_columns(scores)
            attn_t_ref[feats, :half] = dot(value_t_ref[feats, :places], probs).astype(BF16)
            norm_ref[pl.ds(head, 1), :half] = norm
            keys = pair_rest_ref[:, slab]
            scores = dot_nt(keys, q_side_ref[side, half:, slab]) + bias_ref[1:].reshape(others, half)
            probs, norm = softmax_columns(scores)
            attn_t_ref[feats, half:] = dot(value_t_ref[feats, places:], probs).astype(BF16)
            norm_ref[pl.ds(head, 1), half:] = norm
        return carry

    lax.fori_loop(0, HEADS // 2, pair_step, 0)
    attn = attn_t_ref[...].T
    unit_one, _ = norm_parts(hidden_one_ref[...])
    normed_one = unit_one * gain_ref[0:1] + bias_row_ref[0:1]
    hidden_two = normed_one + dot(attn, wo_ref[...])
    unit_two, inverse_two = norm_parts(hidden_two)
    normed_two = unit_two * gain_ref[1:2] + bias_row_ref[1:2]
    normed_two_low = normed_two.astype(BF16)
    total_ref[...] = normed_two
    chunk = width
    chunks = w_down_ref.shape[0] // chunk

    def up_step(c, carry):
        cols = pl.ds(pl.multiple_of(c * chunk, chunk), chunk)
        upper = dot(normed_two_low, w_up_ref[:, cols])
        sigma = 1.0 / (1.0 + jnp.exp(-upper))
        active = (upper * sigma).astype(BF16)
        active_ref[:, cols] = active
        slope_ref[:, cols] = sigma * (1.0 + upper * (1.0 - sigma))
        total_ref[...] += dot(active, w_down_ref[cols, :])
        return carry

    lax.fori_loop(0, chunks, up_step, 0)
    unit_three, inverse_three = norm_parts(total_ref[...])
    result = (unit_three * gain_ref[2:3] + bias_row_ref[2:3]).astype(BF16)
    out_ref[...] = dot(unsort_matrix(rows, start), result).astype(BF16)
    upstream = dot(sort_matrix(rows, start), grad_out_ref[...])
    grad_three, gain_three, bias_three = norm_backward(upstream, unit_three, inverse_three, gain_ref[2:3])
    grad_down = grad_three.astype(BF16)
    total_ref[...] = grad_three
    normed_two_t = normed_two_low.T

    def down_step(c, carry):
        cols = pl.ds(pl.multiple_of(c * chunk, chunk), chunk)
        grad_upper = (dot_nt(grad_down, w_down_ref[cols, :]) * slope_ref[:, cols]).astype(BF16)
        down_part = dot_tn(active_ref[:, cols], grad_down).astype(BF16)
        up_part = dot(normed_two_t, grad_upper).astype(BF16)
        here = lax.rem(c, chunks // 2)
        down_rows = pl.ds(pl.multiple_of(here * chunk, chunk), chunk)
        up_rows = pl.ds(pl.multiple_of((chunks // 2 + here) * chunk, chunk), chunk)
        mine = c // (chunks // 2) == me_ref[1]

        @pl.when(mine)
        def _():
            keep_ref[down_rows, :] = down_part
            keep_ref[up_rows, :] = up_part

        @pl.when(jnp.logical_not(mine))
        def _():
            send_ref[down_rows, :] = down_part
            send_ref[up_rows, :] = up_part

        total_ref[...] += dot_nt(grad_upper, w_up_ref[:, cols])
        return carry

    lax.fori_loop(0, chunks, down_step, 0)
    grad_two, gain_two, bias_two = norm_backward(total_ref[...], unit_two, inverse_two, gain_ref[1:2])
    grad_hidden_ref[...] = grad_two
    grad_two_low = grad_two.astype(BF16)
    wo_grad = dot(attn_t_ref[...], grad_two_low).astype(BF16)
    core = me_ref[1]
    low, high = wo_grad[: width // 2], wo_grad[width // 2 :]
    tail = pl.ds(chunks * chunk, width // 2)
    keep_ref[tail, :] = jnp.where(core == 0, low, high)
    send_ref[tail, :] = jnp.where(core == 0, high, low)
    fill_padding(keep_ref, send_ref, chunks * chunk + width // 2)
    grad_attn_ref[...] = dot_nt(grad_two_low, wo_ref[...]).astype(BF16)
    ln_ref[...] = jnp.concatenate([gain_two, gain_three, bias_two, bias_three], axis=0)


def cross_backward_kernel(
    groups,
    block,
    me_ref,
    len_ref,
    src_ref,
    query_ref,
    pair_ref,
    norm_ref,
    grad_attn_ref,
    pair_grad_ref,
    query_grad_t_ref,
    bias_ref,
    q_side_ref,
    g_side_ref,
    key_t_ref,
):
    width = query_ref.shape[1]
    half = query_ref.shape[0] // 2
    me = me_ref[0]
    count = len_ref.shape[1]
    keys_total = pair_ref.shape[0]
    sentences = 1 if block == 0 else count - 1
    places = keys_total // sentences
    order, start, bounds = sentence_order(me, len_ref)
    if block == 0:
        fill_cross_bias(bias_ref, me, groups, places // groups, src_ref, order[:1], bounds, half)
    else:
        fill_cross_bias(bias_ref, me, groups, places // groups, src_ref, order[1:], bounds, half, True)
    first, second = side_masks(width)
    rows_here = slice(block * half, (block + 1) * half)
    q_side_ref[0] = query_ref[rows_here, :] * first
    q_side_ref[1] = query_ref[rows_here, :] * second
    g_side_ref[0] = grad_attn_ref[rows_here, :] * first
    g_side_ref[1] = grad_attn_ref[rows_here, :] * second
    key_t_ref[...] = pair_ref[:, :width].T

    def pair_step(pair, carry):
        slab = pl.ds(pl.multiple_of(pair * SLAB, SLAB), SLAB)
        value_slab = pl.ds(pl.multiple_of(width + pair * SLAB, SLAB), SLAB)
        keys, values = pair_ref[:, slab], pair_ref[:, value_slab]
        key_sum = value_sum = None
        for side in range(2):
            head = pair * 2 + side
            feats = pl.ds(pl.multiple_of(head * (SLAB // 2), SLAB // 2), SLAB // 2)
            q_rows = q_side_ref[side, :, slab]
            g_rows = g_side_ref[side, :, slab]
            scores = dot_nt(keys, q_rows) + bias_ref[...].reshape(keys_total, half)
            probs = jnp.exp(scores - norm_ref[pl.ds(head, 1), rows_here])
            grad_probs = dot_nt(values, g_rows)
            along = jnp.sum(probs * grad_probs, axis=0, keepdims=True)
            grad_scores = (probs * (grad_probs - along)).astype(BF16)
            value_part = dot(probs.astype(BF16), g_rows)
            key_part = dot(grad_scores, q_rows)
            value_sum = value_part if value_sum is None else value_sum + value_part
            key_sum = key_part if key_sum is None else key_sum + key_part
            query_grad_t_ref[feats, :] = (dot(key_t_ref[feats, :], grad_scores) * 0.125).astype(BF16)
        pair_grad_ref[:, slab] = key_sum.astype(BF16)
        pair_grad_ref[:, value_slab] = value_sum.astype(BF16)
        return carry

    lax.fori_loop(0, HEADS // 2, pair_step, 0)


def memory_backward_kernel(
    groups,
    me_ref,
    len_ref,
    hidden_one_ref,
    pair_grad_long_ref,
    pair_grad_rest_ref,
    query_grad_t_long_ref,
    query_grad_t_rest_ref,
    grad_hidden_two_ref,
    wkv_ref,
    wq_ref,
    w_out_ref,
    self_attn_t_ref,
    gain_ref,
    bias_row_ref,
    ln_in_ref,
    memory_ref,
    *refs,
):
    came_refs = refs[: groups - 1]
    memory_grad_refs = refs[groups - 1 : 2 * groups - 1]
    mid_ref, ln_ref, grad_hidden_ref, grad_self_ref, total_ref = refs[2 * groups - 1 :]
    rows, width = hidden_one_ref.shape
    half = rows // 2
    me = me_ref[0]
    count = len_ref.shape[1]
    places = pair_grad_long_ref.shape[0]
    span = places // groups
    order, _, _ = sentence_order(me, len_ref)
    for j in range(count):
        pair_grad_ref = pair_grad_long_ref if j == 0 else pair_grad_rest_ref
        first_row = max(j - 1, 0) * places
        for part in range(groups):
            grads = pair_grad_ref[pl.ds(first_row + part * span, span), :]
            memory_grad_refs[part][order[j]] = dot_nt(grads, wkv_ref[...]).astype(BF16)
            if part == 0:
                block = memory_ref[me * count + order[j]]
            else:
                block = came_refs[part - 1][order[j]]
            term = dot_tn(block, grads)
            if j == 0 and part == 0:
                total_ref[...] = term
            else:
                total_ref[...] += term
    unit_one, inverse_one = norm_parts(hidden_one_ref[...])
    normed_one = (unit_one * gain_ref[0:1] + bias_row_ref[0:1]).astype(BF16)
    query_grad = jnp.concatenate([query_grad_t_long_ref[...].T, query_grad_t_rest_ref[...].T], axis=0)
    upstream = grad_hidden_two_ref[...] + dot_nt(query_grad, wq_ref[...])
    grad_one, gain_one, bias_one = norm_backward(upstream, unit_one, inverse_one, gain_ref[0:1])
    grad_hidden_ref[...] = grad_one
    grad_one_low = grad_one.astype(BF16)
    grad_self_ref[...] = dot_nt(grad_one_low, w_out_ref[...]).astype(BF16)
    mid_ref[:width] = dot_tn(normed_one, query_grad).astype(BF16)
    mid_ref[width : 2 * width] = total_ref[:, :width].astype(BF16)
    mid_ref[2 * width : 3 * width] = total_ref[:, width:].astype(BF16)
    mid_ref[3 * width :] = dot(self_attn_t_ref[...], grad_one_low).astype(BF16)
    norms = jnp.concatenate(
        [gain_one, ln_in_ref[0:2], bias_one, ln_in_ref[2:4], jnp.zeros((LN_ROWS - 6, width), F32)], axis=0
    )
    ln_ref[...] = norms.astype(BF16)


def self_backward_kernel(
    me_ref,
    len_ref,
    qkv_ref,
    norm_ref,
    grad_attn_ref,
    sorted_ref,
    mid_ref,
    ln_in_ref,
    grad_triple_ref,
    keep_ref,
    send_ref,
    bias_ref,
    q_side_ref,
    g_side_ref,
    key_t_ref,
    query_grad_t_ref,
):
    rows, width = sorted_ref.shape
    half = rows // 2
    order, start, bounds = sentence_order(me_ref[0], len_ref)
    fill_self_bias(bias_ref, bounds, half)
    first, second = side_masks(width)
    q_side_ref[0] = qkv_ref[:, :width] * first
    q_side_ref[1] = qkv_ref[:, :width] * second
    g_side_ref[0] = grad_attn_ref[...] * first
    g_side_ref[1] = grad_attn_ref[...] * second
    key_t_ref[...] = qkv_ref[:, width : 2 * width].T

    def pair_step(pair, carry):
        slab = pl.ds(pl.multiple_of(pair * SLAB, SLAB), SLAB)
        key_slab = pl.ds(pl.multiple_of(width + pair * SLAB, SLAB), SLAB)
        value_slab = pl.ds(pl.multiple_of(2 * width + pair * SLAB, SLAB), SLAB)
        for block in range(2):
            span = pl.ds(block * half, half)
            keys, values = qkv_ref[span, key_slab], qkv_ref[span, value_slab]
            key_sum = value_sum = None
            for side in range(2):
                head = pair * 2 + side
                feats = pl.ds(pl.multiple_of(head * (SLAB // 2), SLAB // 2), SLAB // 2)
                q_rows = q_side_ref[side, span, slab]
                g_rows = g_side_ref[side, span, slab]
                scores = dot_nt(keys, q_rows) + bias_ref[block]
                probs = jnp.exp(scores - norm_ref[pl.ds(head, 1), span])
                grad_probs = dot_nt(values, g_rows)
                along = jnp.sum(probs * grad_probs, axis=0, keepdims=True)
                grad_scores = (probs * (grad_probs - along)).astype(BF16)
                value_part = dot(probs.astype(BF16), g_rows)
                key_part = dot(grad_scores, q_rows)
                value_sum = value_part if value_sum is None else value_sum + value_part
                key_sum = key_part if key_sum is None else key_sum + key_part
                query_grad_t_ref[feats, span] = (
                    dot(key_t_ref[feats, span], grad_scores) * 0.125
                ).astype(BF16)
            grad_triple_ref[span, key_slab] = key_sum.astype(BF16)
            grad_triple_ref[span, value_slab] = value_sum.astype(BF16)
        return carry

    lax.fori_loop(0, HEADS // 2, pair_step, 0)
    grad_triple_ref[:, :width] = query_grad_t_ref[...].T
    sorted_t = sorted_ref[...].T
    core = me_ref[1]
    grads = [
        dot(sorted_t, grad_triple_ref[:, part * width : (part + 1) * width]).astype(BF16)
        for part in range(3)
    ]
    used = 3 * width + width // 2

    def halves(low_ref, high_ref):
        low_ref[: 3 * width, :] = mid_ref[: 3 * width, :]
        low_ref[3 * width : used, :] = grads[0][: width // 2]
        high_ref[:width, :] = mid_ref[3 * width :, :]
        high_ref[width : 2 * width, :] = grads[1]
        high_ref[2 * width : 3 * width, :] = grads[2]
        high_ref[3 * width : used, :] = grads[0][width // 2 :]

    @pl.when(core == 0)
    def _():
        halves(keep_ref, send_ref)

    @pl.when(core != 0)
    def _():
        halves(send_ref, keep_ref)

    fill_padding(keep_ref, send_ref, used)
    keep_ref[keep_ref.shape[0] - LN_ROWS :, :] = ln_in_ref[...]
    send_ref[send_ref.shape[0] - LN_ROWS :, :] = ln_in_ref[...]


def target_kernel(me_ref, len_ref, grad_triple_ref, w_qkv_ref, grad_hidden_ref, grad_target_ref):
    rows = grad_hidden_ref.shape[0]
    _, start, _ = sentence_order(me_ref[0], len_ref)
    result = grad_hidden_ref[...] + dot_nt(grad_triple_ref[...], w_qkv_ref[...])
    grad_target_ref[...] = dot(unsort_matrix(rows, start), result.astype(BF16)).astype(BF16)


def tree_sum(terms):
    while len(terms) > 1:
        terms = [terms[i] + terms[i + 1] for i in range(0, len(terms), 2)]
    return terms[0]


def rows_of(ref, first, count):
    return ref[pl.ds(pl.multiple_of(first, 16), count), :].astype(F32)


def split_kernel(a_rows, b_rows, ln, xy_size, z_size, spot_ref, keep_ref, came_ref, *outs):
    a_outs, b_outs = outs[:xy_size], outs[xy_size:]
    if ln:
        total = keep_ref.shape[0]
        tail = (rows_of(keep_ref, total - LN_ROWS, LN_ROWS) + rows_of(came_ref, total - LN_ROWS, LN_ROWS)).astype(BF16)
    for d, out in enumerate(a_outs):
        size = a_rows // xy_size
        first = (spot_ref[2] ^ d) * size
        out[:size, :] = (rows_of(keep_ref, first, size) + rows_of(came_ref, first, size)).astype(BF16)
        if ln:
            out[size:, :] = tail
    for d, out in enumerate(b_outs):
        size = b_rows // z_size
        first = a_rows + (spot_ref[3] ^ d) * size
        out[...] = (rows_of(keep_ref, first, size) + rows_of(came_ref, first, size)).astype(BF16)


def resplit_kernel(ln, xy_size, z_size, spot_ref, *refs):
    a_ins, refs = refs[:xy_size], refs[xy_size:]
    has_b = len(refs) > z_size
    b_ins, refs = (refs[:z_size], refs[z_size:]) if has_b else ([], refs)
    a_outs, b_outs = refs[:z_size], refs[z_size:]
    extra = LN_ROWS if ln else 0
    size = a_outs[0].shape[0] - extra
    if ln:
        tail = tree_sum([rows_of(ref, size * z_size, LN_ROWS) for ref in a_ins]).astype(BF16)
    for d, out in enumerate(a_outs):
        first = (spot_ref[3] ^ d) * size
        out[:size, :] = tree_sum([rows_of(ref, first, size) for ref in a_ins]).astype(BF16)
        if ln:
            out[size:, :] = tail
    for d, out in enumerate(b_outs):
        size = out.shape[0]
        first = (spot_ref[2] ^ d) * size
        out[...] = tree_sum([rows_of(ref, first, size) for ref in b_ins]).astype(BF16)


def total_kernel(ln, xy_size, z_size, *refs):
    a_ins, refs = refs[:z_size], refs[z_size:]
    has_b = len(refs) > xy_size
    b_ins, refs = (refs[:xy_size], refs[xy_size:]) if has_b else ([], refs)
    size = refs[0].shape[0]
    refs[0][...] = tree_sum([rows_of(ref, 0, size) for ref in a_ins]).astype(BF16)
    if has_b:
        refs[1][...] = tree_sum([rows_of(ref, 0, refs[1].shape[0]) for ref in b_ins]).astype(BF16)
    if ln:
        refs[-1][...] = tree_sum([rows_of(ref, size, LN_ROWS) for ref in a_ins])


def place(ins, out_ref, first, spot):
    for d, ref in enumerate(ins):
        size = ref.shape[0]
        out_ref[pl.ds(pl.multiple_of(first + (spot ^ d) * size, 16), size), :] = ref[...]


def join_kernel(xy_size, z_size, spot_ref, *refs):
    a_ins, refs = refs[:z_size], refs[z_size:]
    place(a_ins, refs[-1] if len(refs) == 1 else refs[-2], 0, spot_ref[3])
    if len(refs) > 1:
        place(refs[:xy_size], refs[-1], 0, spot_ref[2])


def rejoin_kernel(xy_size, z_size, spot_ref, *refs):
    a_ins, rest = refs[:xy_size], refs[xy_size:]
    place(a_ins, refs[-1], 0, spot_ref[2])
    if len(rest) > 1:
        place(rest[:z_size], refs[-1], a_ins[0].shape[0] * xy_size, spot_ref[3])


def finish_kernel(pieces, spot_ref, mine_ref, other_ref, *outs):
    def write(halves):
        for half, first, rows, out, row, col in pieces:
            width = halves[half].shape[1]
            outs[out][row : row + rows, col : col + width] = halves[half][first : first + rows, :].astype(F32)

    @pl.when(spot_ref[1] == 0)
    def _():
        write((mine_ref, other_ref))

    @pl.when(spot_ref[1] != 0)
    def _():
        write((other_ref, mine_ref))


class Summing:
    def __init__(self, rows, width, ln):
        self.width, self.ln = width, ln
        self.dp, self.mem = lax.axis_size("dp"), lax.axis_size("mem")
        self.z_size = 4
        self.x_size = self.dp // (2 * self.z_size)
        self.xy_size = self.x_size * self.mem
        unit = 16 * self.xy_size * self.z_size
        units = -(-rows // unit)
        a_units = max(1, round(units * 2 / 3))
        self.rows = units * unit
        self.a_rows, self.b_rows = a_units * unit, (units - a_units) * unit
        self.padded = self.rows + (LN_ROWS if ln else 0)

    def permute(self, array, group, offset):
        pairs = []
        for dp in range(self.dp):
            for mem in range(self.mem):
                z, x, core = dp // (2 * self.x_size), dp // 2 % self.x_size, dp % 2
                to_mem = mem
                if group == "core":
                    core ^= offset
                elif group == "z":
                    z ^= offset
                else:
                    spot = (x * self.mem + mem) ^ offset
                    x, to_mem = spot // self.mem, spot % self.mem
                to_dp = (z * self.x_size + x) * 2 + core
                pairs.append((dp * self.mem + mem, to_dp * self.mem + to_mem))
        return lax.ppermute(array, ("dp", "mem"), pairs)

    def swap(self, arrays, group):
        return [arrays[0]] + [self.permute(array, group, d) for d, array in enumerate(arrays) if d > 0]

    def spread(self, array, group):
        size = self.z_size if group == "z" else self.xy_size
        return [array] + [self.permute(array, group, d) for d in range(1, size)]

    def shape(self, rows, kind=BF16):
        return ((rows, self.width), kind)

    def core_swap(self, send):
        return self.permute(send, "core", 1)

    def split(self, spot, keep, came):
        extra = LN_ROWS if self.ln else 0
        outs = [self.shape(self.a_rows // self.xy_size + extra)] * self.xy_size
        if self.b_rows:
            outs = outs + [self.shape(self.b_rows // self.z_size)] * self.z_size
        kernel = functools.partial(
            split_kernel, self.a_rows, self.b_rows, self.ln, self.xy_size, self.z_size
        )
        parts = call(kernel, outs, [], 1, spot, keep, came)
        return parts[: self.xy_size], parts[self.xy_size :]

    def first_swap(self, parts):
        return self.swap(parts[0], "xy"), self.swap(parts[1], "z") if parts[1] else []

    def resplit(self, spot, parts):
        extra = LN_ROWS if self.ln else 0
        each = self.xy_size * self.z_size
        outs = [self.shape(self.a_rows // each + extra)] * self.z_size
        if self.b_rows:
            outs = outs + [self.shape(self.b_rows // each)] * self.xy_size
        kernel = functools.partial(resplit_kernel, self.ln, self.xy_size, self.z_size)
        parts = call(kernel, outs, [], 1, spot, *parts[0], *parts[1])
        return parts[: self.z_size], parts[self.z_size :]

    def second_swap(self, parts):
        return self.swap(parts[0], "z"), self.swap(parts[1], "xy") if parts[1] else []

    def total(self, parts):
        each = self.xy_size * self.z_size
        outs = [self.shape(self.a_rows // each)]
        if self.b_rows:
            outs.append(self.shape(self.b_rows // each))
        if self.ln:
            outs.append(self.shape(LN_ROWS, F32))
        kernel = functools.partial(total_kernel, self.ln, self.xy_size, self.z_size)
        return call(kernel, outs, [], 0, *parts[0], *parts[1])

    def first_spread(self, sums):
        return self.spread(sums[0], "z"), self.spread(sums[1], "xy") if self.b_rows else []

    def join(self, spot, parts):
        outs = [self.shape(self.a_rows // self.xy_size)]
        if self.b_rows:
            outs.append(self.shape(self.b_rows // self.z_size))
        kernel = functools.partial(join_kernel, self.xy_size, self.z_size)
        return call(kernel, outs, [], 1, spot, *parts[0], *parts[1])

    def second_spread(self, sums):
        return self.spread(sums[0], "xy"), self.spread(sums[1], "z") if self.b_rows else []

    def rejoin(self, spot, parts):
        kernel = functools.partial(rejoin_kernel, self.xy_size, self.z_size)
        return call(kernel, [self.shape(self.rows)], [], 1, spot, *parts[0], *parts[1])[0]

    def finish(self, spot, mine, other, pieces, outs):
        return call(functools.partial(finish_kernel, pieces), outs, [], 1, spot, mine, other)


def call(kernel, outs, scratch, scalars, *arrays):
    specs = [pl.BlockSpec(memory_space=pltpu.SMEM)] * scalars
    specs = specs + [pl.BlockSpec(memory_space=pltpu.VMEM)] * (len(arrays) - scalars)
    return pl.pallas_call(
        kernel,
        out_shape=[jax.ShapeDtypeStruct(shape, kind) for shape, kind in outs],
        in_specs=specs,
        out_specs=[pl.BlockSpec(memory_space=pltpu.VMEM)] * len(outs),
        scratch_shapes=[pltpu.VMEM(shape, kind) for shape, kind in scratch],
        compiler_params=pltpu.CompilerParams(vmem_limit_bytes=VMEM_BYTES),
    )(*arrays)


def body(
    target,
    memory,
    grad_out,
    tgt_len,
    src_len,
    w_qkv,
    w_out,
    wq_cross,
    wkv_cross,
    wo_cross,
    w_up,
    w_down,
    ln_gain,
    ln_bias,
):
    rows, width = target.shape
    half = rows // 2
    hidden_width = w_down.shape[0]
    groups = lax.axis_size("mem")
    me = lax.axis_index("mem")
    count = tgt_len.shape[1]
    span = memory.shape[1]
    places = groups * span
    dp = lax.axis_index("dp")
    first_sum = Summing(hidden_width + width // 2, width, False)
    second_sum = Summing(3 * width + width // 2, width, True)
    x_size = first_sum.x_size
    spot = jnp.stack([me, dp % 2, dp // 2 % x_size * groups + me, dp // (2 * x_size)]).astype(jnp.int32)

    came = []
    for shift in range(1, groups):
        pairs = [(i, (i + shift) % groups) for i in range(groups)]
        sent = lax.dynamic_slice_in_dim(memory, ((me + shift) % groups) * count, count, 0)
        came.append(lax.ppermute(sent, "mem", pairs))

    sorted_rows, qkv, self_norm, self_attn_t, hidden_one, query, pair_mine = call(
        self_forward_kernel,
        [
            ((rows, width), BF16),
            ((rows, 3 * width), BF16),
            ((HEADS, rows), F32),
            ((width, rows), BF16),
            ((rows, width), F32),
            ((rows, width), BF16),
            ((count, span, 2 * width), BF16),
        ],
        [
            ((2, half, half), F32),
            ((2, rows, width), BF16),
            ((width, rows), BF16),
        ],
        2,
        spot,
        tgt_len,
        target,
        w_qkv,
        w_out,
        wq_cross,
        ln_gain,
        ln_bias,
        memory,
        wkv_cross,
    )
    result_out, pair_long, pair_rest, cross_norm, keep_one, send_one, grad_hidden_two, grad_attn, ln_part = call(
        functools.partial(middle_kernel, groups),
        [
            ((rows, width), BF16),
            ((places, 2 * width), BF16),
            (((count - 1) * places, 2 * width), BF16),
            ((HEADS, rows), F32),
            ((first_sum.padded, width), BF16),
            ((first_sum.padded, width), BF16),
            ((rows, width), F32),
            ((rows, width), BF16),
            ((4, width), F32),
        ],
        [
            ((count, places, half), F32),
            ((2, rows, width), BF16),
            ((width, count * places), BF16),
            ((width, rows), BF16),
            ((rows, hidden_width), BF16),
            ((rows, hidden_width), F32),
            ((rows, width), F32),
        ],
        3,
        spot,
        tgt_len,
        src_len,
        hidden_one,
        query,
        pair_mine,
        wkv_cross,
        wo_cross,
        w_up,
        w_down,
        ln_gain,
        ln_bias,
        grad_out,
        *came,
    )
    came_one = first_sum.core_swap(send_one)

    def cross_backward(block, pair):
        keys = pair.shape[0]
        sentences = keys // places
        return call(
            functools.partial(cross_backward_kernel, groups, block),
            [((keys, 2 * width), BF16), ((width, half), BF16)],
            [
                ((sentences, places, half), F32),
                ((2, half, width), BF16),
                ((2, half, width), BF16),
                ((width, keys), BF16),
            ],
            3,
            spot,
            tgt_len,
            src_len,
            query,
            pair,
            cross_norm,
            grad_attn,
        )

    pair_grad_long, query_grad_t_long = cross_backward(0, pair_long)
    (came_one, pair_grad_long) = lax.optimization_barrier((came_one, pair_grad_long))
    parts_one = first_sum.split(spot, keep_one, came_one)
    (parts_one, pair_rest) = lax.optimization_barrier((parts_one, pair_rest))
    parts_one = first_sum.first_swap(parts_one)
    pair_grad_rest, query_grad_t_rest = cross_backward(1, pair_rest)
    *memory_grads, middle, ln_sums, grad_hidden_one, grad_self = call(
        functools.partial(memory_backward_kernel, groups),
        [((count, span, width), BF16)] * groups
        + [
            ((4 * width, width), BF16),
            ((LN_ROWS, width), BF16),
            ((rows, width), F32),
            ((rows, width), BF16),
        ],
        [((width, 2 * width), F32)],
        2,
        spot,
        tgt_len,
        hidden_one,
        pair_grad_long,
        pair_grad_rest,
        query_grad_t_long,
        query_grad_t_rest,
        grad_hidden_two,
        wkv_cross,
        wq_cross,
        w_out,
        self_attn_t,
        ln_gain,
        ln_bias,
        ln_part,
        memory,
        *came,
    )
    (parts_one, grad_self) = lax.optimization_barrier((parts_one, grad_self))
    parts_one = first_sum.resplit(spot, parts_one)
    (parts_one, grad_self) = lax.optimization_barrier((parts_one, grad_self))
    parts_one = first_sum.second_swap(parts_one)
    grad_triple, keep_two, send_two = call(
        self_backward_kernel,
        [
            ((rows, 3 * width), BF16),
            ((second_sum.padded, width), BF16),
            ((second_sum.padded, width), BF16),
        ],
        [
            ((2, half, half), F32),
            ((2, rows, width), BF16),
            ((2, rows, width), BF16),
            ((width, rows), BF16),
            ((width, rows), BF16),
        ],
        2,
        spot,
        tgt_len,
        qkv,
        self_norm,
        grad_self,
        sorted_rows,
        middle,
        ln_sums,
    )
    came_two = second_sum.core_swap(send_two)
    sums_one = first_sum.total(parts_one)
    spread_one = first_sum.first_spread(sums_one)
    (grad_target,) = call(
        target_kernel,
        [((rows, width), BF16)],
        [],
        2,
        spot,
        tgt_len,
        grad_triple,
        w_qkv,
        grad_hidden_one,
    )
    backs = []
    for shift in range(1, groups):
        pairs = [(i, (i - shift) % groups) for i in range(groups)]
        backs.append(lax.ppermute(memory_grads[shift], "mem", pairs))
    parts_two = second_sum.first_swap(second_sum.split(spot, keep_two, came_two))
    sums_one = first_sum.join(spot, spread_one)
    spread_one = first_sum.second_spread(sums_one)
    parts_two = second_sum.second_swap(second_sum.resplit(spot, parts_two))
    half_one = first_sum.rejoin(spot, spread_one)
    other_one = first_sum.core_swap(half_one)
    *sums_two, norm_sums = second_sum.total(parts_two)
    spread_two = second_sum.first_spread(sums_two)
    chunks = hidden_width // width
    pieces = []
    for chunk in range(chunks):
        side, here = chunk // (chunks // 2), chunk % (chunks // 2)
        pieces.append((side, here * width, width, 0, chunk * width, 0))
        pieces.append((side, (chunks // 2 + here) * width, width, 1, 0, chunk * width))
    for side in range(2):
        pieces.append((side, chunks * width, width // 2, 2, side * width // 2, 0))
    grad_w_down, grad_w_up, grad_wo = first_sum.finish(
        spot,
        half_one,
        other_one,
        pieces,
        [((hidden_width, width), F32), ((width, hidden_width), F32), ((width, width), F32)],
    )
    spread_two = second_sum.second_spread(second_sum.join(spot, spread_two))
    half_two = second_sum.rejoin(spot, spread_two)
    other_two = second_sum.core_swap(half_two)
    short = width // 2
    pieces = [
        (0, 0, width, 0, 0, 0),
        (0, width, width, 1, 0, 0),
        (0, 2 * width, width, 1, 0, width),
        (0, 3 * width, short, 2, 0, 0),
        (1, 0, width, 3, 0, 0),
        (1, width, width, 2, 0, width),
        (1, 2 * width, width, 2, 0, 2 * width),
        (1, 3 * width, short, 2, short, 0),
    ]
    grad_wq, grad_wkv, grad_w_qkv, grad_w_out = second_sum.finish(
        spot,
        half_two,
        other_two,
        pieces,
        [
            ((width, width), F32),
            ((width, 2 * width), F32),
            ((width, 3 * width), F32),
            ((width, width), F32),
        ],
    )
    grad_memory = jnp.zeros(memory.shape, BF16)
    grad_memory = lax.dynamic_update_slice_in_dim(grad_memory, memory_grads[0], me * count, 0)
    for shift in range(1, groups):
        grad_memory = lax.dynamic_update_slice_in_dim(
            grad_memory, backs[shift - 1], ((me + shift) % groups) * count, 0
        )
    return (
        result_out,
        grad_target,
        grad_memory,
        grad_w_qkv,
        grad_w_out,
        grad_wq,
        grad_wkv,
        grad_wo,
        grad_w_up,
        grad_w_down,
        norm_sums[:3],
        norm_sums[3:6],
    )


def solution(mesh):
    rows_spec = P(("dp", "mem"), None)
    memory_spec = P("dp", "mem", None)
    return jax.shard_map(
        body,
        mesh=mesh,
        in_specs=(rows_spec, memory_spec, rows_spec, P("dp", None), P("dp", None)) + (P(),) * 9,
        out_specs=(rows_spec, rows_spec, memory_spec) + (P(),) * 9,
        check_vma=False,
    )
```

```python
import functools

import jax
import jax.numpy as jnp
from jax import lax
from jax.experimental import pallas as pl
from jax.experimental.pallas import tpu as pltpu
from jax.sharding import PartitionSpec as P

HEADS = 8
SLAB = 128
MASKED = -1e30
EPSILON = 1e-05
F32 = jnp.float32
BF16 = jnp.bfloat16
VMEM_BYTES = 60 * 1024 * 1024
LN_ROWS = 16


def dot(left, right):
    return jnp.dot(left, right, preferred_element_type=F32)


def dot_nt(left, right):
    return lax.dot_general(left, right, (((1,), (1,)), ((), ())), preferred_element_type=F32)


def dot_tn(left, right):
    return lax.dot_general(left, right, (((0,), (0,)), ((), ())), preferred_element_type=F32)


def iota(shape, axis):
    return lax.broadcasted_iota(jnp.int32, shape, axis)


def norm_parts(hidden):
    centre = hidden - jnp.mean(hidden, axis=-1, keepdims=True)
    inverse = lax.rsqrt(jnp.mean(centre * centre, axis=-1, keepdims=True) + EPSILON)
    return centre * inverse, inverse


def norm_backward(upstream, unit, inverse, gain_row):
    scaled = upstream * gain_row
    shifted = (
        scaled
        - jnp.mean(scaled, axis=-1, keepdims=True)
        - unit * jnp.mean(scaled * unit, axis=-1, keepdims=True)
    )
    gain_grad = jnp.sum(upstream * unit, axis=0, keepdims=True)
    return inverse * shifted, gain_grad, jnp.sum(upstream, axis=0, keepdims=True)


def sentence_order(me, len_ref):
    count = len_ref.shape[1]
    lengths = [len_ref[me, k] for k in range(count)]
    longest, best, start, running = jnp.int32(0), lengths[0], jnp.int32(0), jnp.int32(0)
    for k in range(1, count):
        running = running + lengths[k - 1]
        more = lengths[k] > best
        longest = jnp.where(more, k, longest)
        start = jnp.where(more, running, start)
        best = jnp.where(more, lengths[k], best)
    order = [longest] + [jnp.where(k < longest, k, k + 1) for k in range(count - 1)]
    bounds = [jnp.int32(0)]
    for k in range(1, count):
        bounds.append(bounds[-1] + len_ref[me, order[k]])
    return order, start, bounds


def moved_rows(index, start, half):
    return jnp.where(index < start, index + half, jnp.where(index < start + half, index - start, index))


def sort_matrix(rows, start):
    spot = moved_rows(iota((rows, rows), 1), start, rows // 2)
    return jnp.where(spot == iota((rows, rows), 0), 1.0, 0.0).astype(BF16)


def unsort_matrix(rows, start):
    spot = moved_rows(iota((rows, rows), 0), start, rows // 2)
    return jnp.where(spot == iota((rows, rows), 1), 1.0, 0.0).astype(BF16)


def side_masks(width):
    side = iota((1, width), 1) % SLAB
    first = jnp.where(side < SLAB // 2, 1.0, 0.0)
    return first.astype(BF16), (1.0 - first).astype(BF16)


def fill_self_bias(bias_ref, bounds, half):
    key = iota((half, half), 0)
    query = iota((half, half), 1)
    first = jnp.zeros((half, half), jnp.int32)
    for bound in bounds[1:-1]:
        first = jnp.where(query >= bound, bound, first)
    causal = key <= query
    bias_ref[0] = jnp.where(causal, 0.0, MASKED)
    bias_ref[1] = jnp.where(causal & (key >= first), 0.0, MASKED)


def fill_cross_bias(bias_ref, me, groups, span, src_ref, order, bounds, half, rest_only=False):
    key = iota((span, half), 0)
    query = iota((span, half), 1)
    for j, sentence in enumerate(order):
        for part in range(groups):
            place = lax.rem(me - part + groups, groups) * span + key
            live = place < src_ref[me, sentence]
            if j > 0 or rest_only:
                k = j + 1 if rest_only else j
                live = live & (query >= bounds[k - 1]) & (query < bounds[k])
            bias_ref[j, pl.ds(part * span, span), :] = jnp.where(live, 0.0, MASKED)


def softmax_columns(scores):
    top = jnp.max(scores, axis=0, keepdims=True)
    weights = jnp.exp(scores - top)
    total = jnp.sum(weights, axis=0, keepdims=True)
    return (weights * (1.0 / total)).astype(BF16), top + jnp.log(total)


def self_forward_kernel(
    me_ref,
    len_ref,
    target_ref,
    w_qkv_ref,
    w_out_ref,
    wq_ref,
    gain_ref,
    bias_row_ref,
    memory_ref,
    wkv_ref,
    sorted_ref,
    qkv_ref,
    norm_ref,
    attn_t_ref,
    hidden_ref,
    query_ref,
    pair_ref,
    bias_ref,
    q_side_ref,
    value_t_ref,
):
    rows, width = target_ref.shape
    half = rows // 2
    me = me_ref[0]
    order, start, bounds = sentence_order(me, len_ref)
    sorted_rows = dot(sort_matrix(rows, start), target_ref[...]).astype(BF16)
    sorted_ref[...] = sorted_rows
    fill_self_bias(bias_ref, bounds, half)
    queries = dot(sorted_rows, w_qkv_ref[:, :width]).astype(BF16) * 0.125
    queries = queries.astype(BF16)
    qkv_ref[:, :width] = queries
    first, second = side_masks(width)
    q_side_ref[0] = queries * first
    q_side_ref[1] = queries * second
    qkv_ref[:, width : 2 * width] = dot(sorted_rows, w_qkv_ref[:, width : 2 * width]).astype(BF16)
    values = dot(sorted_rows, w_qkv_ref[:, 2 * width :]).astype(BF16)
    qkv_ref[:, 2 * width :] = values
    value_t_ref[...] = values.T

    def pair_step(pair, carry):
        slab = pl.ds(pl.multiple_of(pair * SLAB, SLAB), SLAB)
        key_slab = pl.ds(pl.multiple_of(width + pair * SLAB, SLAB), SLAB)
        for side in range(2):
            head = pair * 2 + side
            feats = pl.ds(pl.multiple_of(head * (SLAB // 2), SLAB // 2), SLAB // 2)
            for block in range(2):
                span = pl.ds(block * half, half)
                scores = dot_nt(qkv_ref[span, key_slab], q_side_ref[side, span, slab]) + bias_ref[block]
                probs, norm = softmax_columns(scores)
                attn_t_ref[feats, span] = dot(value_t_ref[feats, span], probs).astype(BF16)
                norm_ref[pl.ds(head, 1), span] = norm
        return carry

    lax.fori_loop(0, HEADS // 2, pair_step, 0)
    attn = attn_t_ref[...].T
    hidden = sorted_rows.astype(F32) + dot(attn, w_out_ref[...])
    hidden_ref[...] = hidden
    unit, _ = norm_parts(hidden)
    normed = (unit * gain_ref[0:1] + bias_row_ref[0:1]).astype(BF16)
    query_ref[...] = (dot(normed, wq_ref[...]).astype(BF16) * 0.125).astype(BF16)
    count = pair_ref.shape[0]
    for j in range(count):
        block = memory_ref[me * count + order[j]]
        pair_ref[j] = dot(block, wkv_ref[...]).astype(BF16)


def fill_padding(keep_ref, send_ref, used):
    total, width = keep_ref.shape
    if total > used:
        keep_ref[used:, :] = jnp.zeros((total - used, width), BF16)
        send_ref[used:, :] = jnp.zeros((total - used, width), BF16)


def middle_kernel(
    groups,
    me_ref,
    len_ref,
    src_ref,
    hidden_one_ref,
    query_ref,
    pair_mine_ref,
    wkv_ref,
    wo_ref,
    w_up_ref,
    w_down_ref,
    gain_ref,
    bias_row_ref,
    grad_out_ref,
    *refs,
):
    came_refs = refs[: groups - 1]
    (
        out_ref,
        pair_long_ref,
        pair_rest_ref,
        norm_ref,
        keep_ref,
        send_ref,
        grad_hidden_ref,
        grad_attn_ref,
        ln_ref,
        bias_ref,
        q_side_ref,
        value_t_ref,
        attn_t_ref,
        active_ref,
        slope_ref,
        total_ref,
    ) = refs[groups - 1 :]
    rows, width = hidden_one_ref.shape
    half = rows // 2
    me = me_ref[0]
    count, span = pair_mine_ref.shape[0], pair_mine_ref.shape[1]
    places = groups * span
    order, start, bounds = sentence_order(me, len_ref)
    fill_cross_bias(bias_ref, me, groups, span, src_ref, order, bounds, half)
    first, second = side_masks(width)
    q_side_ref[0] = query_ref[...] * first
    q_side_ref[1] = query_ref[...] * second
    for j in range(count):
        pair_ref = pair_long_ref if j == 0 else pair_rest_ref
        first_row = max(j - 1, 0) * places
        pair_ref[pl.ds(first_row, span), :] = pair_mine_ref[j]
        for part in range(1, groups):
            block = came_refs[part - 1][order[j]]
            here = pl.ds(first_row + part * span, span)
            pair_ref[here, :] = dot(block, wkv_ref[...]).astype(BF16)
        value_t_ref[:, pl.ds(j * places, places)] = pair_ref[pl.ds(first_row, places), width:].T
    others = (count - 1) * places

    def pair_step(pair, carry):
        slab = pl.ds(pl.multiple_of(pair * SLAB, SLAB), SLAB)
        for side in range(2):
            head = pair * 2 + side
            feats = pl.ds(pl.multiple_of(head * (SLAB // 2), SLAB // 2), SLAB // 2)
            scores = dot_nt(pair_long_ref[:, slab], q_side_ref[side, :half, slab]) + bias_ref[0]
            probs, norm = softmax_columns(scores)
            attn_t_ref[feats, :half] = dot(value_t_ref[feats, :places], probs).astype(BF16)
            norm_ref[pl.ds(head, 1), :half] = norm
            keys = pair_rest_ref[:, slab]
            scores = dot_nt(keys, q_side_ref[side, half:, slab]) + bias_ref[1:].reshape(others, half)
            probs, norm = softmax_columns(scores)
            attn_t_ref[feats, half:] = dot(value_t_ref[feats, places:], probs).astype(BF16)
            norm_ref[pl.ds(head, 1), half:] = norm
        return carry

    lax.fori_loop(0, HEADS // 2, pair_step, 0)
    attn = attn_t_ref[...].T
    unit_one, _ = norm_parts(hidden_one_ref[...])
    normed_one = unit_one * gain_ref[0:1] + bias_row_ref[0:1]
    hidden_two = normed_one + dot(attn, wo_ref[...])
    unit_two, inverse_two = norm_parts(hidden_two)
    normed_two = unit_two * gain_ref[1:2] + bias_row_ref[1:2]
    normed_two_low = normed_two.astype(BF16)
    total_ref[...] = normed_two
    chunk = width
    chunks = w_down_ref.shape[0] // chunk

    def up_step(c, carry):
        cols = pl.ds(pl.multiple_of(c * chunk, chunk), chunk)
        upper = dot(normed_two_low, w_up_ref[:, cols])
        sigma = 1.0 / (1.0 + jnp.exp(-upper))
        active = (upper * sigma).astype(BF16)
        active_ref[:, cols] = active
        slope_ref[:, cols] = sigma * (1.0 + upper * (1.0 - sigma))
        total_ref[...] += dot(active, w_down_ref[cols, :])
        return carry

    lax.fori_loop(0, chunks, up_step, 0)
    unit_three, inverse_three = norm_parts(total_ref[...])
    result = (unit_three * gain_ref[2:3] + bias_row_ref[2:3]).astype(BF16)
    out_ref[...] = dot(unsort_matrix(rows, start), result).astype(BF16)
    upstream = dot(sort_matrix(rows, start), grad_out_ref[...])
    grad_three, gain_three, bias_three = norm_backward(upstream, unit_three, inverse_three, gain_ref[2:3])
    grad_down = grad_three.astype(BF16)
    total_ref[...] = grad_three
    normed_two_t = normed_two_low.T

    def down_step(c, carry):
        cols = pl.ds(pl.multiple_of(c * chunk, chunk), chunk)
        grad_upper = (dot_nt(grad_down, w_down_ref[cols, :]) * slope_ref[:, cols]).astype(BF16)
        down_part = dot_tn(active_ref[:, cols], grad_down).astype(BF16)
        up_part = dot(normed_two_t, grad_upper).astype(BF16)
        here = lax.rem(c, chunks // 2)
        down_rows = pl.ds(pl.multiple_of(here * chunk, chunk), chunk)
        up_rows = pl.ds(pl.multiple_of((chunks // 2 + here) * chunk, chunk), chunk)
        mine = c // (chunks // 2) == me_ref[1]

        @pl.when(mine)
        def _():
            keep_ref[down_rows, :] = down_part
            keep_ref[up_rows, :] = up_part

        @pl.when(jnp.logical_not(mine))
        def _():
            send_ref[down_rows, :] = down_part
            send_ref[up_rows, :] = up_part

        total_ref[...] += dot_nt(grad_upper, w_up_ref[:, cols])
        return carry

    lax.fori_loop(0, chunks, down_step, 0)
    grad_two, gain_two, bias_two = norm_backward(total_ref[...], unit_two, inverse_two, gain_ref[1:2])
    grad_hidden_ref[...] = grad_two
    grad_two_low = grad_two.astype(BF16)
    wo_grad = dot(attn_t_ref[...], grad_two_low).astype(BF16)
    core = me_ref[1]
    low, high = wo_grad[: width // 2], wo_grad[width // 2 :]
    tail = pl.ds(chunks * chunk, width // 2)
    keep_ref[tail, :] = jnp.where(core == 0, low, high)
    send_ref[tail, :] = jnp.where(core == 0, high, low)
    fill_padding(keep_ref, send_ref, chunks * chunk + width // 2)
    grad_attn_ref[...] = dot_nt(grad_two_low, wo_ref[...]).astype(BF16)
    ln_ref[...] = jnp.concatenate([gain_two, gain_three, bias_two, bias_three], axis=0)


def cross_backward_kernel(
    groups,
    block,
    me_ref,
    len_ref,
    src_ref,
    query_ref,
    pair_ref,
    norm_ref,
    grad_attn_ref,
    pair_grad_ref,
    query_grad_t_ref,
    bias_ref,
    q_side_ref,
    g_side_ref,
    key_t_ref,
):
    width = query_ref.shape[1]
    half = query_ref.shape[0] // 2
    me = me_ref[0]
    count = len_ref.shape[1]
    keys_total = pair_ref.shape[0]
    sentences = 1 if block == 0 else count - 1
    places = keys_total // sentences
    order, start, bounds = sentence_order(me, len_ref)
    if block == 0:
        fill_cross_bias(bias_ref, me, groups, places // groups, src_ref, order[:1], bounds, half)
    else:
        fill_cross_bias(bias_ref, me, groups, places // groups, src_ref, order[1:], bounds, half, True)
    first, second = side_masks(width)
    rows_here = slice(block * half, (block + 1) * half)
    q_side_ref[0] = query_ref[rows_here, :] * first
    q_side_ref[1] = query_ref[rows_here, :] * second
    g_side_ref[0] = grad_attn_ref[rows_here, :] * first
    g_side_ref[1] = grad_attn_ref[rows_here, :] * second
    key_t_ref[...] = pair_ref[:, :width].T

    def pair_step(pair, carry):
        slab = pl.ds(pl.multiple_of(pair * SLAB, SLAB), SLAB)
        value_slab = pl.ds(pl.multiple_of(width + pair * SLAB, SLAB), SLAB)
        keys, values = pair_ref[:, slab], pair_ref[:, value_slab]
        key_sum = value_sum = None
        for side in range(2):
            head = pair * 2 + side
            feats = pl.ds(pl.multiple_of(head * (SLAB // 2), SLAB // 2), SLAB // 2)
            q_rows = q_side_ref[side, :, slab]
            g_rows = g_side_ref[side, :, slab]
            scores = dot_nt(keys, q_rows) + bias_ref[...].reshape(keys_total, half)
            probs = jnp.exp(scores - norm_ref[pl.ds(head, 1), rows_here])
            grad_probs = dot_nt(values, g_rows)
            along = jnp.sum(probs * grad_probs, axis=0, keepdims=True)
            grad_scores = (probs * (grad_probs - along)).astype(BF16)
            value_part = dot(probs.astype(BF16), g_rows)
            key_part = dot(grad_scores, q_rows)
            value_sum = value_part if value_sum is None else value_sum + value_part
            key_sum = key_part if key_sum is None else key_sum + key_part
            query_grad_t_ref[feats, :] = (dot(key_t_ref[feats, :], grad_scores) * 0.125).astype(BF16)
        pair_grad_ref[:, slab] = key_sum.astype(BF16)
        pair_grad_ref[:, value_slab] = value_sum.astype(BF16)
        return carry

    lax.fori_loop(0, HEADS // 2, pair_step, 0)


def memory_backward_kernel(
    groups,
    me_ref,
    len_ref,
    hidden_one_ref,
    pair_grad_long_ref,
    pair_grad_rest_ref,
    query_grad_t_long_ref,
    query_grad_t_rest_ref,
    grad_hidden_two_ref,
    wkv_ref,
    wq_ref,
    w_out_ref,
    self_attn_t_ref,
    gain_ref,
    bias_row_ref,
    ln_in_ref,
    memory_ref,
    *refs,
):
    came_refs = refs[: groups - 1]
    memory_grad_refs = refs[groups - 1 : 2 * groups - 1]
    mid_ref, ln_ref, grad_hidden_ref, grad_self_ref, total_ref = refs[2 * groups - 1 :]
    rows, width = hidden_one_ref.shape
    half = rows // 2
    me = me_ref[0]
    count = len_ref.shape[1]
    places = pair_grad_long_ref.shape[0]
    span = places // groups
    order, _, _ = sentence_order(me, len_ref)
    for j in range(count):
        pair_grad_ref = pair_grad_long_ref if j == 0 else pair_grad_rest_ref
        first_row = max(j - 1, 0) * places
        for part in range(groups):
            grads = pair_grad_ref[pl.ds(first_row + part * span, span), :]
            memory_grad_refs[part][order[j]] = dot_nt(grads, wkv_ref[...]).astype(BF16)
            if part == 0:
                block = memory_ref[me * count + order[j]]
            else:
                block = came_refs[part - 1][order[j]]
            term = dot_tn(block, grads)
            if j == 0 and part == 0:
                total_ref[...] = term
            else:
                total_ref[...] += term
    unit_one, inverse_one = norm_parts(hidden_one_ref[...])
    normed_one = (unit_one * gain_ref[0:1] + bias_row_ref[0:1]).astype(BF16)
    query_grad = jnp.concatenate([query_grad_t_long_ref[...].T, query_grad_t_rest_ref[...].T], axis=0)
    upstream = grad_hidden_two_ref[...] + dot_nt(query_grad, wq_ref[...])
    grad_one, gain_one, bias_one = norm_backward(upstream, unit_one, inverse_one, gain_ref[0:1])
    grad_hidden_ref[...] = grad_one
    grad_one_low = grad_one.astype(BF16)
    grad_self_ref[...] = dot_nt(grad_one_low, w_out_ref[...]).astype(BF16)
    mid_ref[:width] = dot_tn(normed_one, query_grad).astype(BF16)
    mid_ref[width : 2 * width] = total_ref[:, :width].astype(BF16)
    mid_ref[2 * width : 3 * width] = total_ref[:, width:].astype(BF16)
    mid_ref[3 * width :] = dot(self_attn_t_ref[...], grad_one_low).astype(BF16)
    norms = jnp.concatenate(
        [gain_one, ln_in_ref[0:2], bias_one, ln_in_ref[2:4], jnp.zeros((LN_ROWS - 6, width), F32)], axis=0
    )
    ln_ref[...] = norms.astype(BF16)


def self_backward_kernel(
    me_ref,
    len_ref,
    qkv_ref,
    norm_ref,
    grad_attn_ref,
    sorted_ref,
    mid_ref,
    ln_in_ref,
    grad_triple_ref,
    keep_ref,
    send_ref,
    bias_ref,
    q_side_ref,
    g_side_ref,
    key_t_ref,
    query_grad_t_ref,
):
    rows, width = sorted_ref.shape
    half = rows // 2
    order, start, bounds = sentence_order(me_ref[0], len_ref)
    fill_self_bias(bias_ref, bounds, half)
    first, second = side_masks(width)
    q_side_ref[0] = qkv_ref[:, :width] * first
    q_side_ref[1] = qkv_ref[:, :width] * second
    g_side_ref[0] = grad_attn_ref[...] * first
    g_side_ref[1] = grad_attn_ref[...] * second
    key_t_ref[...] = qkv_ref[:, width : 2 * width].T

    def pair_step(pair, carry):
        slab = pl.ds(pl.multiple_of(pair * SLAB, SLAB), SLAB)
        key_slab = pl.ds(pl.multiple_of(width + pair * SLAB, SLAB), SLAB)
        value_slab = pl.ds(pl.multiple_of(2 * width + pair * SLAB, SLAB), SLAB)
        for block in range(2):
            span = pl.ds(block * half, half)
            keys, values = qkv_ref[span, key_slab], qkv_ref[span, value_slab]
            key_sum = value_sum = None
            for side in range(2):
                head = pair * 2 + side
                feats = pl.ds(pl.multiple_of(head * (SLAB // 2), SLAB // 2), SLAB // 2)
                q_rows = q_side_ref[side, span, slab]
                g_rows = g_side_ref[side, span, slab]
                scores = dot_nt(keys, q_rows) + bias_ref[block]
                probs = jnp.exp(scores - norm_ref[pl.ds(head, 1), span])
                grad_probs = dot_nt(values, g_rows)
                along = jnp.sum(probs * grad_probs, axis=0, keepdims=True)
                grad_scores = (probs * (grad_probs - along)).astype(BF16)
                value_part = dot(probs.astype(BF16), g_rows)
                key_part = dot(grad_scores, q_rows)
                value_sum = value_part if value_sum is None else value_sum + value_part
                key_sum = key_part if key_sum is None else key_sum + key_part
                query_grad_t_ref[feats, span] = (
                    dot(key_t_ref[feats, span], grad_scores) * 0.125
                ).astype(BF16)
            grad_triple_ref[span, key_slab] = key_sum.astype(BF16)
            grad_triple_ref[span, value_slab] = value_sum.astype(BF16)
        return carry

    lax.fori_loop(0, HEADS // 2, pair_step, 0)
    grad_triple_ref[:, :width] = query_grad_t_ref[...].T
    sorted_t = sorted_ref[...].T
    core = me_ref[1]
    grads = [
        dot(sorted_t, grad_triple_ref[:, part * width : (part + 1) * width]).astype(BF16)
        for part in range(3)
    ]
    used = 3 * width + width // 2

    def halves(low_ref, high_ref):
        low_ref[: 3 * width, :] = mid_ref[: 3 * width, :]
        low_ref[3 * width : used, :] = grads[0][: width // 2]
        high_ref[:width, :] = mid_ref[3 * width :, :]
        high_ref[width : 2 * width, :] = grads[1]
        high_ref[2 * width : 3 * width, :] = grads[2]
        high_ref[3 * width : used, :] = grads[0][width // 2 :]

    @pl.when(core == 0)
    def _():
        halves(keep_ref, send_ref)

    @pl.when(core != 0)
    def _():
        halves(send_ref, keep_ref)

    fill_padding(keep_ref, send_ref, used)
    keep_ref[keep_ref.shape[0] - LN_ROWS :, :] = ln_in_ref[...]
    send_ref[send_ref.shape[0] - LN_ROWS :, :] = ln_in_ref[...]


def target_kernel(me_ref, len_ref, grad_triple_ref, w_qkv_ref, grad_hidden_ref, grad_target_ref):
    rows = grad_hidden_ref.shape[0]
    _, start, _ = sentence_order(me_ref[0], len_ref)
    result = grad_hidden_ref[...] + dot_nt(grad_triple_ref[...], w_qkv_ref[...])
    grad_target_ref[...] = dot(unsort_matrix(rows, start), result.astype(BF16)).astype(BF16)


def tree_sum(terms):
    while len(terms) > 1:
        terms = [terms[i] + terms[i + 1] for i in range(0, len(terms), 2)]
    return terms[0]


def rows_of(ref, first, count):
    return ref[pl.ds(pl.multiple_of(first, 16), count), :].astype(F32)


def add_kernel(mine_ref, came_ref, out_ref):
    out_ref[...] = (mine_ref[...].astype(F32) + came_ref[...].astype(F32)).astype(BF16)


def split_kernel(a_rows, b_rows, ln, xy_size, z_size, spot_ref, keep_ref, came_ref, *outs):
    a_outs, b_outs = outs[:xy_size], outs[xy_size:]
    if ln:
        total = keep_ref.shape[0]
        tail = (rows_of(keep_ref, total - LN_ROWS, LN_ROWS) + rows_of(came_ref, total - LN_ROWS, LN_ROWS)).astype(BF16)
    for d, out in enumerate(a_outs):
        size = a_rows // xy_size
        first = (spot_ref[2] ^ d) * size
        out[:size, :] = (rows_of(keep_ref, first, size) + rows_of(came_ref, first, size)).astype(BF16)
        if ln:
            out[size:, :] = tail
    for d, out in enumerate(b_outs):
        size = b_rows // z_size
        first = a_rows + (spot_ref[3] ^ d) * size
        out[...] = (rows_of(keep_ref, first, size) + rows_of(came_ref, first, size)).astype(BF16)


def resplit_kernel(ln, xy_size, z_size, spot_ref, *refs):
    a_ins, refs = refs[:xy_size], refs[xy_size:]
    has_b = len(refs) > z_size
    b_ins, refs = (refs[:z_size], refs[z_size:]) if has_b else ([], refs)
    a_outs, b_outs = refs[:z_size], refs[z_size:]
    extra = LN_ROWS if ln else 0
    size = a_outs[0].shape[0] - extra
    if ln:
        tail = tree_sum([rows_of(ref, size * z_size, LN_ROWS) for ref in a_ins]).astype(BF16)
    for d, out in enumerate(a_outs):
        first = (spot_ref[3] ^ d) * size
        out[:size, :] = tree_sum([rows_of(ref, first, size) for ref in a_ins]).astype(BF16)
        if ln:
            out[size:, :] = tail
    for d, out in enumerate(b_outs):
        size = out.shape[0]
        first = (spot_ref[2] ^ d) * size
        out[...] = tree_sum([rows_of(ref, first, size) for ref in b_ins]).astype(BF16)


def total_kernel(ln, xy_size, z_size, *refs):
    a_ins, refs = refs[:z_size], refs[z_size:]
    has_b = len(refs) > xy_size
    b_ins, refs = (refs[:xy_size], refs[xy_size:]) if has_b else ([], refs)
    size = refs[0].shape[0]
    refs[0][...] = tree_sum([rows_of(ref, 0, size) for ref in a_ins]).astype(BF16)
    if has_b:
        refs[1][...] = tree_sum([rows_of(ref, 0, refs[1].shape[0]) for ref in b_ins]).astype(BF16)
    if ln:
        refs[-1][...] = tree_sum([rows_of(ref, size, LN_ROWS) for ref in a_ins])


def place(ins, out_ref, first, spot):
    for d, ref in enumerate(ins):
        size = ref.shape[0]
        out_ref[pl.ds(pl.multiple_of(first + (spot ^ d) * size, 16), size), :] = ref[...]


def join_kernel(xy_size, z_size, spot_ref, *refs):
    a_ins, refs = refs[:z_size], refs[z_size:]
    place(a_ins, refs[-1] if len(refs) == 1 else refs[-2], 0, spot_ref[3])
    if len(refs) > 1:
        place(refs[:xy_size], refs[-1], 0, spot_ref[2])


def rejoin_kernel(xy_size, z_size, spot_ref, *refs):
    a_ins, rest = refs[:xy_size], refs[xy_size:]
    place(a_ins, refs[-1], 0, spot_ref[2])
    if len(rest) > 1:
        place(rest[:z_size], refs[-1], a_ins[0].shape[0] * xy_size, spot_ref[3])


def finish_kernel(pieces, spot_ref, mine_ref, other_ref, *outs):
    def write(halves):
        for half, first, rows, out, row, col in pieces:
            width = halves[half].shape[1]
            outs[out][row : row + rows, col : col + width] = halves[half][first : first + rows, :].astype(F32)

    @pl.when(spot_ref[1] == 0)
    def _():
        write((mine_ref, other_ref))

    @pl.when(spot_ref[1] != 0)
    def _():
        write((other_ref, mine_ref))


def gathered_kernel(pieces, both_ref, *outs):
    rows_total = both_ref.shape[0] // 2
    width = both_ref.shape[1]
    for half, first, rows, out, row, col in pieces:
        first = first + half * rows_total
        outs[out][row : row + rows, col : col + width] = both_ref[first : first + rows, :].astype(F32)


class Summing:
    def __init__(self, rows, width, ln):
        self.width, self.ln = width, ln
        self.dp, self.mem = lax.axis_size("dp"), lax.axis_size("mem")
        self.z_size = 4
        self.x_size = self.dp // (2 * self.z_size)
        self.xy_size = self.x_size * self.mem
        unit = 16 * self.xy_size * self.z_size
        units = -(-rows // unit)
        a_units = max(1, round(units * 2 / 3))
        self.rows = units * unit
        self.a_rows, self.b_rows = a_units * unit, (units - a_units) * unit
        self.padded = self.rows + (LN_ROWS if ln else 0)

    def permute(self, array, group, offset):
        pairs = []
        for dp in range(self.dp):
            for mem in range(self.mem):
                z, x, core = dp // (2 * self.x_size), dp // 2 % self.x_size, dp % 2
                to_mem = mem
                if group == "core":
                    core ^= offset
                elif group == "z":
                    z ^= offset
                else:
                    spot = (x * self.mem + mem) ^ offset
                    x, to_mem = spot // self.mem, spot % self.mem
                to_dp = (z * self.x_size + x) * 2 + core
                pairs.append((dp * self.mem + mem, to_dp * self.mem + to_mem))
        return lax.ppermute(array, ("dp", "mem"), pairs)

    def swap(self, arrays, group):
        return [arrays[0]] + [self.permute(array, group, d) for d, array in enumerate(arrays) if d > 0]

    def spread(self, array, group):
        size = self.z_size if group == "z" else self.xy_size
        return [array] + [self.permute(array, group, d) for d in range(1, size)]

    def shape(self, rows, kind=BF16):
        return ((rows, self.width), kind)

    def chip_sum(self, array):
        groups = [
            [dp * self.mem + mem for dp in range(core, self.dp, 2) for mem in range(self.mem)]
            for core in range(2)
        ]
        return lax.psum(array, ("dp", "mem"), axis_index_groups=groups)

    def core_gather(self, array):
        pairs = [
            [(dp + core) * self.mem + mem for core in range(2)]
            for dp in range(0, self.dp, 2)
            for mem in range(self.mem)
        ]
        return lax.all_gather(array, ("dp", "mem"), axis_index_groups=pairs, axis=0, tiled=True)

    def add(self, mine, came):
        return call(add_kernel, [self.shape(self.rows)], [], 0, mine, came)[0]

    def core_swap(self, send):
        return self.permute(send, "core", 1)

    def split(self, spot, keep, came):
        extra = LN_ROWS if self.ln else 0
        outs = [self.shape(self.a_rows // self.xy_size + extra)] * self.xy_size
        if self.b_rows:
            outs = outs + [self.shape(self.b_rows // self.z_size)] * self.z_size
        kernel = functools.partial(
            split_kernel, self.a_rows, self.b_rows, self.ln, self.xy_size, self.z_size
        )
        parts = call(kernel, outs, [], 1, spot, keep, came)
        return parts[: self.xy_size], parts[self.xy_size :]

    def first_swap(self, parts):
        return self.swap(parts[0], "xy"), self.swap(parts[1], "z") if parts[1] else []

    def resplit(self, spot, parts):
        extra = LN_ROWS if self.ln else 0
        each = self.xy_size * self.z_size
        outs = [self.shape(self.a_rows // each + extra)] * self.z_size
        if self.b_rows:
            outs = outs + [self.shape(self.b_rows // each)] * self.xy_size
        kernel = functools.partial(resplit_kernel, self.ln, self.xy_size, self.z_size)
        parts = call(kernel, outs, [], 1, spot, *parts[0], *parts[1])
        return parts[: self.z_size], parts[self.z_size :]

    def second_swap(self, parts):
        return self.swap(parts[0], "z"), self.swap(parts[1], "xy") if parts[1] else []

    def total(self, parts):
        each = self.xy_size * self.z_size
        outs = [self.shape(self.a_rows // each)]
        if self.b_rows:
            outs.append(self.shape(self.b_rows // each))
        if self.ln:
            outs.append(self.shape(LN_ROWS, F32))
        kernel = functools.partial(total_kernel, self.ln, self.xy_size, self.z_size)
        return call(kernel, outs, [], 0, *parts[0], *parts[1])

    def first_spread(self, sums):
        return self.spread(sums[0], "z"), self.spread(sums[1], "xy") if self.b_rows else []

    def join(self, spot, parts):
        outs = [self.shape(self.a_rows // self.xy_size)]
        if self.b_rows:
            outs.append(self.shape(self.b_rows // self.z_size))
        kernel = functools.partial(join_kernel, self.xy_size, self.z_size)
        return call(kernel, outs, [], 1, spot, *parts[0], *parts[1])

    def second_spread(self, sums):
        return self.spread(sums[0], "xy"), self.spread(sums[1], "z") if self.b_rows else []

    def rejoin(self, spot, parts):
        kernel = functools.partial(rejoin_kernel, self.xy_size, self.z_size)
        return call(kernel, [self.shape(self.rows)], [], 1, spot, *parts[0], *parts[1])[0]

    def finish(self, spot, mine, other, pieces, outs):
        if other is None:
            return call(functools.partial(gathered_kernel, pieces), outs, [], 0, mine)
        return call(functools.partial(finish_kernel, pieces), outs, [], 1, spot, mine, other)


def call(kernel, outs, scratch, scalars, *arrays):
    specs = [pl.BlockSpec(memory_space=pltpu.SMEM)] * scalars
    specs = specs + [pl.BlockSpec(memory_space=pltpu.VMEM)] * (len(arrays) - scalars)
    return pl.pallas_call(
        kernel,
        out_shape=[jax.ShapeDtypeStruct(shape, kind) for shape, kind in outs],
        in_specs=specs,
        out_specs=[pl.BlockSpec(memory_space=pltpu.VMEM)] * len(outs),
        scratch_shapes=[pltpu.VMEM(shape, kind) for shape, kind in scratch],
        compiler_params=pltpu.CompilerParams(vmem_limit_bytes=VMEM_BYTES),
        cost_estimate=pl.CostEstimate(flops=1, bytes_accessed=1, transcendentals=0),
    )(*arrays)


def body(
    target,
    memory,
    grad_out,
    tgt_len,
    src_len,
    w_qkv,
    w_out,
    wq_cross,
    wkv_cross,
    wo_cross,
    w_up,
    w_down,
    ln_gain,
    ln_bias,
):
    rows, width = target.shape
    half = rows // 2
    hidden_width = w_down.shape[0]
    groups = lax.axis_size("mem")
    me = lax.axis_index("mem")
    count = tgt_len.shape[1]
    span = memory.shape[1]
    places = groups * span
    dp = lax.axis_index("dp")
    first_sum = Summing(hidden_width + width // 2, width, False)
    second_sum = Summing(3 * width + width // 2, width, True)
    x_size = first_sum.x_size
    spot = jnp.stack([me, dp % 2, dp // 2 % x_size * groups + me, dp // (2 * x_size)]).astype(jnp.int32)

    came = []
    for shift in range(1, groups):
        pairs = [(i, (i + shift) % groups) for i in range(groups)]
        sent = lax.dynamic_slice_in_dim(memory, ((me + shift) % groups) * count, count, 0)
        came.append(lax.ppermute(sent, "mem", pairs))

    sorted_rows, qkv, self_norm, self_attn_t, hidden_one, query, pair_mine = call(
        self_forward_kernel,
        [
            ((rows, width), BF16),
            ((rows, 3 * width), BF16),
            ((HEADS, rows), F32),
            ((width, rows), BF16),
            ((rows, width), F32),
            ((rows, width), BF16),
            ((count, span, 2 * width), BF16),
        ],
        [
            ((2, half, half), F32),
            ((2, rows, width), BF16),
            ((width, rows), BF16),
        ],
        2,
        spot,
        tgt_len,
        target,
        w_qkv,
        w_out,
        wq_cross,
        ln_gain,
        ln_bias,
        memory,
        wkv_cross,
    )
    result_out, pair_long, pair_rest, cross_norm, keep_one, send_one, grad_hidden_two, grad_attn, ln_part = call(
        functools.partial(middle_kernel, groups),
        [
            ((rows, width), BF16),
            ((places, 2 * width), BF16),
            (((count - 1) * places, 2 * width), BF16),
            ((HEADS, rows), F32),
            ((first_sum.padded, width), BF16),
            ((first_sum.padded, width), BF16),
            ((rows, width), F32),
            ((rows, width), BF16),
            ((4, width), F32),
        ],
        [
            ((count, places, half), F32),
            ((2, rows, width), BF16),
            ((width, count * places), BF16),
            ((width, rows), BF16),
            ((rows, hidden_width), BF16),
            ((rows, hidden_width), F32),
            ((rows, width), F32),
        ],
        3,
        spot,
        tgt_len,
        src_len,
        hidden_one,
        query,
        pair_mine,
        wkv_cross,
        wo_cross,
        w_up,
        w_down,
        ln_gain,
        ln_bias,
        grad_out,
        *came,
    )
    came_one = first_sum.core_swap(send_one)

    def cross_backward(block, pair):
        keys = pair.shape[0]
        sentences = keys // places
        return call(
            functools.partial(cross_backward_kernel, groups, block),
            [((keys, 2 * width), BF16), ((width, half), BF16)],
            [
                ((sentences, places, half), F32),
                ((2, half, width), BF16),
                ((2, half, width), BF16),
                ((width, keys), BF16),
            ],
            3,
            spot,
            tgt_len,
            src_len,
            query,
            pair,
            cross_norm,
            grad_attn,
        )

    pair_grad_long, query_grad_t_long = cross_backward(0, pair_long)
    (came_one, pair_grad_long) = lax.optimization_barrier((came_one, pair_grad_long))
    sum_one = first_sum.add(keep_one, came_one)
    (sum_one, pair_rest) = lax.optimization_barrier((sum_one, pair_rest))
    half_one = first_sum.chip_sum(sum_one)
    pair_grad_rest, query_grad_t_rest = cross_backward(1, pair_rest)
    *memory_grads, middle, ln_sums, grad_hidden_one, grad_self = call(
        functools.partial(memory_backward_kernel, groups),
        [((count, span, width), BF16)] * groups
        + [
            ((4 * width, width), BF16),
            ((LN_ROWS, width), BF16),
            ((rows, width), F32),
            ((rows, width), BF16),
        ],
        [((width, 2 * width), F32)],
        2,
        spot,
        tgt_len,
        hidden_one,
        pair_grad_long,
        pair_grad_rest,
        query_grad_t_long,
        query_grad_t_rest,
        grad_hidden_two,
        wkv_cross,
        wq_cross,
        w_out,
        self_attn_t,
        ln_gain,
        ln_bias,
        ln_part,
        memory,
        *came,
    )
    grad_triple, keep_two, send_two = call(
        self_backward_kernel,
        [
            ((rows, 3 * width), BF16),
            ((second_sum.padded, width), BF16),
            ((second_sum.padded, width), BF16),
        ],
        [
            ((2, half, half), F32),
            ((2, rows, width), BF16),
            ((2, rows, width), BF16),
            ((width, rows), BF16),
            ((width, rows), BF16),
        ],
        2,
        spot,
        tgt_len,
        qkv,
        self_norm,
        grad_self,
        sorted_rows,
        middle,
        ln_sums,
    )
    (grad_target,) = call(
        target_kernel,
        [((rows, width), BF16)],
        [],
        2,
        spot,
        tgt_len,
        grad_triple,
        w_qkv,
        grad_hidden_one,
    )
    backs = []
    for shift in range(1, groups):
        pairs = [(i, (i - shift) % groups) for i in range(groups)]
        backs.append(lax.ppermute(memory_grads[shift], "mem", pairs))
    send_two, backs, grad_target = lax.optimization_barrier((send_two, backs, grad_target))
    came_two = second_sum.core_swap(send_two)
    parts_two = second_sum.first_swap(second_sum.split(spot, keep_two, came_two))
    parts_two = second_sum.second_swap(second_sum.resplit(spot, parts_two))
    both_one = first_sum.core_gather(half_one)
    *sums_two, norm_sums = second_sum.total(parts_two)
    spread_two = second_sum.first_spread(sums_two)
    chunks = hidden_width // width
    pieces = []
    for chunk in range(chunks):
        side, here = chunk // (chunks // 2), chunk % (chunks // 2)
        pieces.append((side, here * width, width, 0, chunk * width, 0))
        pieces.append((side, (chunks // 2 + here) * width, width, 1, 0, chunk * width))
    for side in range(2):
        pieces.append((side, chunks * width, width // 2, 2, side * width // 2, 0))
    grad_w_down, grad_w_up, grad_wo = first_sum.finish(
        spot,
        both_one,
        None,
        pieces,
        [((hidden_width, width), F32), ((width, hidden_width), F32), ((width, width), F32)],
    )
    (spread_two, both_one) = lax.optimization_barrier((spread_two, both_one))
    spread_two = second_sum.second_spread(second_sum.join(spot, spread_two))
    half_two = second_sum.rejoin(spot, spread_two)
    other_two = second_sum.core_swap(half_two)
    short = width // 2
    pieces = [
        (0, 0, width, 0, 0, 0),
        (0, width, width, 1, 0, 0),
        (0, 2 * width, width, 1, 0, width),
        (0, 3 * width, short, 2, 0, 0),
        (1, 0, width, 3, 0, 0),
        (1, width, width, 2, 0, width),
        (1, 2 * width, width, 2, 0, 2 * width),
        (1, 3 * width, short, 2, short, 0),
    ]
    grad_wq, grad_wkv, grad_w_qkv, grad_w_out = second_sum.finish(
        spot,
        half_two,
        other_two,
        pieces,
        [
            ((width, width), F32),
            ((width, 2 * width), F32),
            ((width, 3 * width), F32),
            ((width, width), F32),
        ],
    )
    grad_memory = jnp.zeros(memory.shape, BF16)
    grad_memory = lax.dynamic_update_slice_in_dim(grad_memory, memory_grads[0], me * count, 0)
    for shift in range(1, groups):
        grad_memory = lax.dynamic_update_slice_in_dim(
            grad_memory, backs[shift - 1], ((me + shift) % groups) * count, 0
        )
    return (
        result_out,
        grad_target,
        grad_memory,
        grad_w_qkv,
        grad_w_out,
        grad_wq,
        grad_wkv,
        grad_wo,
        grad_w_up,
        grad_w_down,
        norm_sums[:3],
        norm_sums[3:6],
    )


def solution(mesh):
    rows_spec = P(("dp", "mem"), None)
    memory_spec = P("dp", "mem", None)
    return jax.shard_map(
        body,
        mesh=mesh,
        in_specs=(rows_spec, memory_spec, rows_spec, P("dp", None), P("dp", None)) + (P(),) * 9,
        out_specs=(rows_spec, rows_spec, memory_spec) + (P(),) * 9,
        check_vma=False,
    )
```

```python
import functools

import jax
import jax.numpy as jnp
from jax import lax
from jax.experimental import pallas as pl
from jax.experimental.pallas import tpu as pltpu
from jax.sharding import PartitionSpec as P

HEADS = 8
SLAB = 128
MASKED = -1e30
EPSILON = 1e-05
F32 = jnp.float32
BF16 = jnp.bfloat16
VMEM_BYTES = 60 * 1024 * 1024
LN_ROWS = 16


def dot(left, right):
    return jnp.dot(left, right, preferred_element_type=F32)


def dot_nt(left, right):
    return lax.dot_general(left, right, (((1,), (1,)), ((), ())), preferred_element_type=F32)


def dot_tn(left, right):
    return lax.dot_general(left, right, (((0,), (0,)), ((), ())), preferred_element_type=F32)


def iota(shape, axis):
    return lax.broadcasted_iota(jnp.int32, shape, axis)


def norm_parts(hidden):
    centre = hidden - jnp.mean(hidden, axis=-1, keepdims=True)
    inverse = lax.rsqrt(jnp.mean(centre * centre, axis=-1, keepdims=True) + EPSILON)
    return centre * inverse, inverse


def norm_backward(upstream, unit, inverse, gain_row):
    scaled = upstream * gain_row
    shifted = (
        scaled
        - jnp.mean(scaled, axis=-1, keepdims=True)
        - unit * jnp.mean(scaled * unit, axis=-1, keepdims=True)
    )
    gain_grad = jnp.sum(upstream * unit, axis=0, keepdims=True)
    return inverse * shifted, gain_grad, jnp.sum(upstream, axis=0, keepdims=True)


def sentence_order(me, len_ref):
    count = len_ref.shape[1]
    lengths = [len_ref[me, k] for k in range(count)]
    longest, best, start, running = jnp.int32(0), lengths[0], jnp.int32(0), jnp.int32(0)
    for k in range(1, count):
        running = running + lengths[k - 1]
        more = lengths[k] > best
        longest = jnp.where(more, k, longest)
        start = jnp.where(more, running, start)
        best = jnp.where(more, lengths[k], best)
    order = [longest] + [jnp.where(k < longest, k, k + 1) for k in range(count - 1)]
    bounds = [jnp.int32(0)]
    for k in range(1, count):
        bounds.append(bounds[-1] + len_ref[me, order[k]])
    return order, start, bounds


def moved_rows(index, start, half):
    return jnp.where(index < start, index + half, jnp.where(index < start + half, index - start, index))


def sort_matrix(rows, start):
    spot = moved_rows(iota((rows, rows), 1), start, rows // 2)
    return jnp.where(spot == iota((rows, rows), 0), 1.0, 0.0).astype(BF16)


def unsort_matrix(rows, start):
    spot = moved_rows(iota((rows, rows), 0), start, rows // 2)
    return jnp.where(spot == iota((rows, rows), 1), 1.0, 0.0).astype(BF16)


def side_masks(width):
    side = iota((1, width), 1) % SLAB
    first = jnp.where(side < SLAB // 2, 1.0, 0.0)
    return first.astype(BF16), (1.0 - first).astype(BF16)


def fill_self_bias(bias_ref, bounds, half):
    key = iota((half, half), 0)
    query = iota((half, half), 1)
    first = jnp.zeros((half, half), jnp.int32)
    for bound in bounds[1:-1]:
        first = jnp.where(query >= bound, bound, first)
    causal = key <= query
    bias_ref[0] = jnp.where(causal, 0.0, MASKED)
    bias_ref[1] = jnp.where(causal & (key >= first), 0.0, MASKED)


def fill_cross_bias(bias_ref, me, groups, span, src_ref, order, bounds, half, rest_only=False):
    key = iota((span, half), 0)
    query = iota((span, half), 1)
    for j, sentence in enumerate(order):
        for part in range(groups):
            place = lax.rem(me - part + groups, groups) * span + key
            live = place < src_ref[me, sentence]
            if j > 0 or rest_only:
                k = j + 1 if rest_only else j
                live = live & (query >= bounds[k - 1]) & (query < bounds[k])
            bias_ref[j, pl.ds(part * span, span), :] = jnp.where(live, 0.0, MASKED)


def softmax_columns(scores):
    top = jnp.max(scores, axis=0, keepdims=True)
    weights = jnp.exp(scores - top)
    total = jnp.sum(weights, axis=0, keepdims=True)
    return (weights * (1.0 / total)).astype(BF16), top + jnp.log(total)


def self_forward_kernel(
    me_ref,
    len_ref,
    target_ref,
    w_qkv_ref,
    w_out_ref,
    wq_ref,
    gain_ref,
    bias_row_ref,
    memory_ref,
    wkv_ref,
    sorted_ref,
    qkv_ref,
    norm_ref,
    attn_t_ref,
    hidden_ref,
    query_ref,
    pair_ref,
    bias_ref,
    q_side_ref,
    value_t_ref,
):
    rows, width = target_ref.shape
    half = rows // 2
    me = me_ref[0]
    order, start, bounds = sentence_order(me, len_ref)
    sorted_rows = dot(sort_matrix(rows, start), target_ref[...]).astype(BF16)
    sorted_ref[...] = sorted_rows
    fill_self_bias(bias_ref, bounds, half)
    queries = dot(sorted_rows, w_qkv_ref[:, :width]).astype(BF16) * 0.125
    queries = queries.astype(BF16)
    qkv_ref[:, :width] = queries
    first, second = side_masks(width)
    q_side_ref[0] = queries * first
    q_side_ref[1] = queries * second
    qkv_ref[:, width : 2 * width] = dot(sorted_rows, w_qkv_ref[:, width : 2 * width]).astype(BF16)
    values = dot(sorted_rows, w_qkv_ref[:, 2 * width :]).astype(BF16)
    qkv_ref[:, 2 * width :] = values
    value_t_ref[...] = values.T

    def pair_step(pair, carry):
        slab = pl.ds(pl.multiple_of(pair * SLAB, SLAB), SLAB)
        key_slab = pl.ds(pl.multiple_of(width + pair * SLAB, SLAB), SLAB)
        for side in range(2):
            head = pair * 2 + side
            feats = pl.ds(pl.multiple_of(head * (SLAB // 2), SLAB // 2), SLAB // 2)
            for block in range(2):
                span = pl.ds(block * half, half)
                scores = dot_nt(qkv_ref[span, key_slab], q_side_ref[side, span, slab]) + bias_ref[block]
                probs, norm = softmax_columns(scores)
                attn_t_ref[feats, span] = dot(value_t_ref[feats, span], probs).astype(BF16)
                norm_ref[pl.ds(head, 1), span] = norm
        return carry

    lax.fori_loop(0, HEADS // 2, pair_step, 0)
    attn = attn_t_ref[...].T
    hidden = sorted_rows.astype(F32) + dot(attn, w_out_ref[...])
    hidden_ref[...] = hidden
    unit, _ = norm_parts(hidden)
    normed = (unit * gain_ref[0:1] + bias_row_ref[0:1]).astype(BF16)
    query_ref[...] = (dot(normed, wq_ref[...]).astype(BF16) * 0.125).astype(BF16)
    count = pair_ref.shape[0]
    for j in range(count):
        block = memory_ref[me * count + order[j]]
        pair_ref[j] = dot(block, wkv_ref[...]).astype(BF16)


def fill_padding(keep_ref, send_ref, used):
    total, width = keep_ref.shape
    if total > used:
        keep_ref[used:, :] = jnp.zeros((total - used, width), BF16)
        send_ref[used:, :] = jnp.zeros((total - used, width), BF16)


def middle_kernel(
    groups,
    me_ref,
    len_ref,
    src_ref,
    hidden_one_ref,
    query_ref,
    pair_mine_ref,
    wkv_ref,
    wo_ref,
    w_up_ref,
    w_down_ref,
    gain_ref,
    bias_row_ref,
    grad_out_ref,
    *refs,
):
    came_refs = refs[: groups - 1]
    (
        out_ref,
        pair_long_ref,
        pair_rest_ref,
        norm_ref,
        keep_ref,
        send_ref,
        grad_hidden_ref,
        grad_attn_ref,
        ln_ref,
        bias_ref,
        q_side_ref,
        value_t_ref,
        attn_t_ref,
        active_ref,
        slope_ref,
        total_ref,
    ) = refs[groups - 1 :]
    rows, width = hidden_one_ref.shape
    half = rows // 2
    me = me_ref[0]
    count, span = pair_mine_ref.shape[0], pair_mine_ref.shape[1]
    places = groups * span
    order, start, bounds = sentence_order(me, len_ref)
    fill_cross_bias(bias_ref, me, groups, span, src_ref, order, bounds, half)
    first, second = side_masks(width)
    q_side_ref[0] = query_ref[...] * first
    q_side_ref[1] = query_ref[...] * second
    for j in range(count):
        pair_ref = pair_long_ref if j == 0 else pair_rest_ref
        first_row = max(j - 1, 0) * places
        pair_ref[pl.ds(first_row, span), :] = pair_mine_ref[j]
        for part in range(1, groups):
            block = came_refs[part - 1][order[j]]
            here = pl.ds(first_row + part * span, span)
            pair_ref[here, :] = dot(block, wkv_ref[...]).astype(BF16)
        value_t_ref[:, pl.ds(j * places, places)] = pair_ref[pl.ds(first_row, places), width:].T
    others = (count - 1) * places

    def pair_step(pair, carry):
        slab = pl.ds(pl.multiple_of(pair * SLAB, SLAB), SLAB)
        for side in range(2):
            head = pair * 2 + side
            feats = pl.ds(pl.multiple_of(head * (SLAB // 2), SLAB // 2), SLAB // 2)
            scores = dot_nt(pair_long_ref[:, slab], q_side_ref[side, :half, slab]) + bias_ref[0]
            probs, norm = softmax_columns(scores)
            attn_t_ref[feats, :half] = dot(value_t_ref[feats, :places], probs).astype(BF16)
            norm_ref[pl.ds(head, 1), :half] = norm
            keys = pair_rest_ref[:, slab]
            scores = dot_nt(keys, q_side_ref[side, half:, slab]) + bias_ref[1:].reshape(others, half)
            probs, norm = softmax_columns(scores)
            attn_t_ref[feats, half:] = dot(value_t_ref[feats, places:], probs).astype(BF16)
            norm_ref[pl.ds(head, 1), half:] = norm
        return carry

    lax.fori_loop(0, HEADS // 2, pair_step, 0)
    attn = attn_t_ref[...].T
    unit_one, _ = norm_parts(hidden_one_ref[...])
    normed_one = unit_one * gain_ref[0:1] + bias_row_ref[0:1]
    hidden_two = normed_one + dot(attn, wo_ref[...])
    unit_two, inverse_two = norm_parts(hidden_two)
    normed_two = unit_two * gain_ref[1:2] + bias_row_ref[1:2]
    normed_two_low = normed_two.astype(BF16)
    total_ref[...] = normed_two
    chunk = width
    chunks = w_down_ref.shape[0] // chunk

    def up_step(c, carry):
        cols = pl.ds(pl.multiple_of(c * chunk, chunk), chunk)
        upper = dot(normed_two_low, w_up_ref[:, cols])
        sigma = 1.0 / (1.0 + jnp.exp(-upper))
        active = (upper * sigma).astype(BF16)
        active_ref[:, cols] = active
        slope_ref[:, cols] = sigma * (1.0 + upper * (1.0 - sigma))
        total_ref[...] += dot(active, w_down_ref[cols, :])
        return carry

    lax.fori_loop(0, chunks, up_step, 0)
    unit_three, inverse_three = norm_parts(total_ref[...])
    result = (unit_three * gain_ref[2:3] + bias_row_ref[2:3]).astype(BF16)
    out_ref[...] = dot(unsort_matrix(rows, start), result).astype(BF16)
    upstream = dot(sort_matrix(rows, start), grad_out_ref[...])
    grad_three, gain_three, bias_three = norm_backward(upstream, unit_three, inverse_three, gain_ref[2:3])
    grad_down = grad_three.astype(BF16)
    total_ref[...] = grad_three
    normed_two_t = normed_two_low.T

    def down_step(c, carry):
        cols = pl.ds(pl.multiple_of(c * chunk, chunk), chunk)
        grad_upper = (dot_nt(grad_down, w_down_ref[cols, :]) * slope_ref[:, cols]).astype(BF16)
        down_part = dot_tn(active_ref[:, cols], grad_down).astype(BF16)
        up_part = dot(normed_two_t, grad_upper).astype(BF16)
        here = lax.rem(c, chunks // 2)
        down_rows = pl.ds(pl.multiple_of(here * chunk, chunk), chunk)
        up_rows = pl.ds(pl.multiple_of((chunks // 2 + here) * chunk, chunk), chunk)
        mine = c // (chunks // 2) == me_ref[1]

        @pl.when(mine)
        def _():
            keep_ref[down_rows, :] = down_part
            keep_ref[up_rows, :] = up_part

        @pl.when(jnp.logical_not(mine))
        def _():
            send_ref[down_rows, :] = down_part
            send_ref[up_rows, :] = up_part

        total_ref[...] += dot_nt(grad_upper, w_up_ref[:, cols])
        return carry

    lax.fori_loop(0, chunks, down_step, 0)
    grad_two, gain_two, bias_two = norm_backward(total_ref[...], unit_two, inverse_two, gain_ref[1:2])
    grad_hidden_ref[...] = grad_two
    grad_two_low = grad_two.astype(BF16)
    wo_grad = dot(attn_t_ref[...], grad_two_low).astype(BF16)
    core = me_ref[1]
    low, high = wo_grad[: width // 2], wo_grad[width // 2 :]
    tail = pl.ds(chunks * chunk, width // 2)
    keep_ref[tail, :] = jnp.where(core == 0, low, high)
    send_ref[tail, :] = jnp.where(core == 0, high, low)
    fill_padding(keep_ref, send_ref, chunks * chunk + width // 2)
    grad_attn_ref[...] = dot_nt(grad_two_low, wo_ref[...]).astype(BF16)
    ln_ref[...] = jnp.concatenate([gain_two, gain_three, bias_two, bias_three], axis=0)


def cross_backward_kernel(
    groups,
    block,
    me_ref,
    len_ref,
    src_ref,
    query_ref,
    pair_ref,
    norm_ref,
    grad_attn_ref,
    pair_grad_ref,
    query_grad_t_ref,
    bias_ref,
    q_side_ref,
    g_side_ref,
    key_t_ref,
):
    width = query_ref.shape[1]
    half = query_ref.shape[0] // 2
    me = me_ref[0]
    count = len_ref.shape[1]
    keys_total = pair_ref.shape[0]
    sentences = 1 if block == 0 else count - 1
    places = keys_total // sentences
    order, start, bounds = sentence_order(me, len_ref)
    if block == 0:
        fill_cross_bias(bias_ref, me, groups, places // groups, src_ref, order[:1], bounds, half)
    else:
        fill_cross_bias(bias_ref, me, groups, places // groups, src_ref, order[1:], bounds, half, True)
    first, second = side_masks(width)
    rows_here = slice(block * half, (block + 1) * half)
    q_side_ref[0] = query_ref[rows_here, :] * first
    q_side_ref[1] = query_ref[rows_here, :] * second
    g_side_ref[0] = grad_attn_ref[rows_here, :] * first
    g_side_ref[1] = grad_attn_ref[rows_here, :] * second
    key_t_ref[...] = pair_ref[:, :width].T

    def pair_step(pair, carry):
        slab = pl.ds(pl.multiple_of(pair * SLAB, SLAB), SLAB)
        value_slab = pl.ds(pl.multiple_of(width + pair * SLAB, SLAB), SLAB)
        keys, values = pair_ref[:, slab], pair_ref[:, value_slab]
        key_sum = value_sum = None
        for side in range(2):
            head = pair * 2 + side
            feats = pl.ds(pl.multiple_of(head * (SLAB // 2), SLAB // 2), SLAB // 2)
            q_rows = q_side_ref[side, :, slab]
            g_rows = g_side_ref[side, :, slab]
            scores = dot_nt(keys, q_rows) + bias_ref[...].reshape(keys_total, half)
            probs = jnp.exp(scores - norm_ref[pl.ds(head, 1), rows_here])
            grad_probs = dot_nt(values, g_rows)
            along = jnp.sum(probs * grad_probs, axis=0, keepdims=True)
            grad_scores = (probs * (grad_probs - along)).astype(BF16)
            value_part = dot(probs.astype(BF16), g_rows)
            key_part = dot(grad_scores, q_rows)
            value_sum = value_part if value_sum is None else value_sum + value_part
            key_sum = key_part if key_sum is None else key_sum + key_part
            query_grad_t_ref[feats, :] = (dot(key_t_ref[feats, :], grad_scores) * 0.125).astype(BF16)
        pair_grad_ref[:, slab] = key_sum.astype(BF16)
        pair_grad_ref[:, value_slab] = value_sum.astype(BF16)
        return carry

    lax.fori_loop(0, HEADS // 2, pair_step, 0)


def memory_backward_kernel(
    groups,
    me_ref,
    len_ref,
    hidden_one_ref,
    pair_grad_long_ref,
    pair_grad_rest_ref,
    query_grad_t_long_ref,
    query_grad_t_rest_ref,
    grad_hidden_two_ref,
    wkv_ref,
    wq_ref,
    w_out_ref,
    self_attn_t_ref,
    gain_ref,
    bias_row_ref,
    ln_in_ref,
    memory_ref,
    *refs,
):
    came_refs = refs[: groups - 1]
    memory_grad_refs = refs[groups - 1 : 2 * groups - 1]
    mid_ref, ln_ref, grad_hidden_ref, grad_self_ref, total_ref = refs[2 * groups - 1 :]
    rows, width = hidden_one_ref.shape
    half = rows // 2
    me = me_ref[0]
    count = len_ref.shape[1]
    places = pair_grad_long_ref.shape[0]
    span = places // groups
    order, _, _ = sentence_order(me, len_ref)
    for j in range(count):
        pair_grad_ref = pair_grad_long_ref if j == 0 else pair_grad_rest_ref
        first_row = max(j - 1, 0) * places
        for part in range(groups):
            grads = pair_grad_ref[pl.ds(first_row + part * span, span), :]
            memory_grad_refs[part][order[j]] = dot_nt(grads, wkv_ref[...]).astype(BF16)
            if part == 0:
                block = memory_ref[me * count + order[j]]
            else:
                block = came_refs[part - 1][order[j]]
            term = dot_tn(block, grads)
            if j == 0 and part == 0:
                total_ref[...] = term
            else:
                total_ref[...] += term
    unit_one, inverse_one = norm_parts(hidden_one_ref[...])
    normed_one = (unit_one * gain_ref[0:1] + bias_row_ref[0:1]).astype(BF16)
    query_grad = jnp.concatenate([query_grad_t_long_ref[...].T, query_grad_t_rest_ref[...].T], axis=0)
    upstream = grad_hidden_two_ref[...] + dot_nt(query_grad, wq_ref[...])
    grad_one, gain_one, bias_one = norm_backward(upstream, unit_one, inverse_one, gain_ref[0:1])
    grad_hidden_ref[...] = grad_one
    grad_one_low = grad_one.astype(BF16)
    grad_self_ref[...] = dot_nt(grad_one_low, w_out_ref[...]).astype(BF16)
    mid_ref[:width] = dot_tn(normed_one, query_grad).astype(BF16)
    mid_ref[width : 2 * width] = total_ref[:, :width].astype(BF16)
    mid_ref[2 * width : 3 * width] = total_ref[:, width:].astype(BF16)
    mid_ref[3 * width :] = dot(self_attn_t_ref[...], grad_one_low).astype(BF16)
    norms = jnp.concatenate(
        [gain_one, ln_in_ref[0:2], bias_one, ln_in_ref[2:4], jnp.zeros((LN_ROWS - 6, width), F32)], axis=0
    )
    ln_ref[...] = norms.astype(BF16)


def self_backward_kernel(
    me_ref,
    len_ref,
    qkv_ref,
    norm_ref,
    grad_attn_ref,
    sorted_ref,
    mid_ref,
    ln_in_ref,
    grad_triple_ref,
    keep_ref,
    send_ref,
    bias_ref,
    q_side_ref,
    g_side_ref,
    key_t_ref,
    query_grad_t_ref,
):
    rows, width = sorted_ref.shape
    half = rows // 2
    order, start, bounds = sentence_order(me_ref[0], len_ref)
    fill_self_bias(bias_ref, bounds, half)
    first, second = side_masks(width)
    q_side_ref[0] = qkv_ref[:, :width] * first
    q_side_ref[1] = qkv_ref[:, :width] * second
    g_side_ref[0] = grad_attn_ref[...] * first
    g_side_ref[1] = grad_attn_ref[...] * second
    key_t_ref[...] = qkv_ref[:, width : 2 * width].T

    def pair_step(pair, carry):
        slab = pl.ds(pl.multiple_of(pair * SLAB, SLAB), SLAB)
        key_slab = pl.ds(pl.multiple_of(width + pair * SLAB, SLAB), SLAB)
        value_slab = pl.ds(pl.multiple_of(2 * width + pair * SLAB, SLAB), SLAB)
        for block in range(2):
            span = pl.ds(block * half, half)
            keys, values = qkv_ref[span, key_slab], qkv_ref[span, value_slab]
            key_sum = value_sum = None
            for side in range(2):
                head = pair * 2 + side
                feats = pl.ds(pl.multiple_of(head * (SLAB // 2), SLAB // 2), SLAB // 2)
                q_rows = q_side_ref[side, span, slab]
                g_rows = g_side_ref[side, span, slab]
                scores = dot_nt(keys, q_rows) + bias_ref[block]
                probs = jnp.exp(scores - norm_ref[pl.ds(head, 1), span])
                grad_probs = dot_nt(values, g_rows)
                along = jnp.sum(probs * grad_probs, axis=0, keepdims=True)
                grad_scores = (probs * (grad_probs - along)).astype(BF16)
                value_part = dot(probs.astype(BF16), g_rows)
                key_part = dot(grad_scores, q_rows)
                value_sum = value_part if value_sum is None else value_sum + value_part
                key_sum = key_part if key_sum is None else key_sum + key_part
                query_grad_t_ref[feats, span] = (
                    dot(key_t_ref[feats, span], grad_scores) * 0.125
                ).astype(BF16)
            grad_triple_ref[span, key_slab] = key_sum.astype(BF16)
            grad_triple_ref[span, value_slab] = value_sum.astype(BF16)
        return carry

    lax.fori_loop(0, HEADS // 2, pair_step, 0)
    grad_triple_ref[:, :width] = query_grad_t_ref[...].T
    sorted_t = sorted_ref[...].T
    core = me_ref[1]
    grads = [
        dot(sorted_t, grad_triple_ref[:, part * width : (part + 1) * width]).astype(BF16)
        for part in range(3)
    ]
    used = 3 * width + width // 2

    def halves(low_ref, high_ref):
        low_ref[: 3 * width, :] = mid_ref[: 3 * width, :]
        low_ref[3 * width : used, :] = grads[0][: width // 2]
        high_ref[:width, :] = mid_ref[3 * width :, :]
        high_ref[width : 2 * width, :] = grads[1]
        high_ref[2 * width : 3 * width, :] = grads[2]
        high_ref[3 * width : used, :] = grads[0][width // 2 :]

    @pl.when(core == 0)
    def _():
        halves(keep_ref, send_ref)

    @pl.when(core != 0)
    def _():
        halves(send_ref, keep_ref)

    fill_padding(keep_ref, send_ref, used)
    keep_ref[keep_ref.shape[0] - LN_ROWS :, :] = ln_in_ref[...]
    send_ref[send_ref.shape[0] - LN_ROWS :, :] = ln_in_ref[...]


def target_kernel(me_ref, len_ref, grad_triple_ref, w_qkv_ref, grad_hidden_ref, grad_target_ref):
    rows = grad_hidden_ref.shape[0]
    _, start, _ = sentence_order(me_ref[0], len_ref)
    result = grad_hidden_ref[...] + dot_nt(grad_triple_ref[...], w_qkv_ref[...])
    grad_target_ref[...] = dot(unsort_matrix(rows, start), result.astype(BF16)).astype(BF16)


def tree_sum(terms):
    while len(terms) > 1:
        terms = [terms[i] + terms[i + 1] for i in range(0, len(terms), 2)]
    return terms[0]


def rows_of(ref, first, count):
    return ref[pl.ds(pl.multiple_of(first, 16), count), :].astype(F32)


def split_kernel(stage, ln, spot_ref, *refs):
    if stage == 0:
        ins, outs = refs[:2], refs[2:]
    else:
        ins, outs = refs[: stage], refs[stage:]
    extra = LN_ROWS if ln else 0
    size = outs[0].shape[0] - extra
    whole = size * len(outs)
    here = spot_ref[2] if stage == 0 else spot_ref[3]
    if ln:
        tail = tree_sum([rows_of(ref, whole, LN_ROWS) for ref in ins]).astype(BF16)
    for d, out in enumerate(outs):
        first = (here ^ d) * size
        out[:size, :] = tree_sum([rows_of(ref, first, size) for ref in ins]).astype(BF16)
        if ln:
            out[size:, :] = tail


def total_kernel(ln, count, *refs):
    ins, outs = refs[:count], refs[count:]
    size = outs[0].shape[0]
    outs[0][...] = tree_sum([rows_of(ref, 0, size) for ref in ins]).astype(BF16)
    if ln:
        outs[1][...] = tree_sum([rows_of(ref, size, LN_ROWS) for ref in ins])


def finish_kernel(pieces, all_ref, *outs):
    width = all_ref.shape[1]
    for first, rows, out, row, col in pieces:
        outs[out][row : row + rows, col : col + width] = all_ref[first : first + rows, :].astype(F32)


class Summing:
    def __init__(self, rows, width, ln):
        self.width, self.ln = width, ln
        self.dp, self.mem = lax.axis_size("dp"), lax.axis_size("mem")
        self.z_size = 4
        self.x_size = self.dp // (2 * self.z_size)
        self.xy_size = self.x_size * self.mem
        self.twisted = self.xy_size == self.z_size
        unit = 16 * self.xy_size * self.z_size
        self.rows = -(-rows // unit) * unit
        self.padded = self.rows + (LN_ROWS if ln else 0)
        self.chunk = self.rows // (self.xy_size * self.z_size)

    def coords(self, dp, mem):
        return dp // (2 * self.x_size), (dp // 2 % self.x_size) * self.mem + mem, dp % 2

    def spot(self, me, dp):
        z, xy, core = self.coords(dp, me)
        first, second = xy, z
        if self.twisted:
            first, second = jnp.where(core == 0, xy, z), jnp.where(core == 0, z, xy)
        return jnp.stack([me, core, first, second]).astype(jnp.int32)

    def order(self, dp, mem):
        z, xy, core = self.coords(dp, mem)
        if self.twisted and core == 1:
            return core, z, xy
        return core, xy, z

    def permute(self, array, stage, offset):
        pairs = []
        for dp in range(self.dp):
            for mem in range(self.mem):
                z, xy, core = self.coords(dp, mem)
                if stage == "core":
                    core ^= offset
                elif (stage == 0) != (self.twisted and core == 1):
                    xy ^= offset
                else:
                    z ^= offset
                to_dp = (z * self.x_size + xy // self.mem) * 2 + core
                pairs.append((dp * self.mem + mem, to_dp * self.mem + xy % self.mem))
        return lax.ppermute(array, ("dp", "mem"), pairs)

    def swap(self, arrays, stage):
        return [arrays[0]] + [self.permute(array, stage, d) for d, array in enumerate(arrays) if d > 0]

    def core_swap(self, send):
        return self.permute(send, "core", 1)

    def split(self, stage, spot, *arrays):
        extra = LN_ROWS if self.ln else 0
        peers = self.xy_size if stage == 0 else self.z_size
        size = self.rows // self.xy_size if stage == 0 else self.chunk
        outs = [((size + extra, self.width), BF16)] * peers
        kernel = functools.partial(split_kernel, 0 if stage == 0 else self.xy_size, self.ln)
        return call(kernel, outs, [], 1, spot, *arrays)

    def total(self, arrays):
        outs = [((self.chunk, self.width), BF16)]
        if self.ln:
            outs.append(((LN_ROWS, self.width), F32))
        return call(functools.partial(total_kernel, self.ln, self.z_size), outs, [], 0, *arrays)

    def gather(self, array):
        return lax.all_gather(array, ("dp", "mem"), axis=0, tiled=True)

    def finish(self, everything, pieces, outs):
        cut = []
        for dp in range(self.dp):
            for mem in range(self.mem):
                device = dp * self.mem + mem
                half, first, second = self.order(dp, mem)
                inner = self.z_size
                if self.twisted and half == 1:
                    inner = self.xy_size
                low = (first * inner + second) * self.chunk
                for piece_half, start, rows, out, row, col in pieces:
                    begin, end = max(low, start), min(low + self.chunk, start + rows)
                    if piece_half == half and begin < end:
                        cut.append(
                            (device * self.chunk + begin - low, end - begin, out, row + begin - start, col)
                        )
        return call(functools.partial(finish_kernel, cut), outs, [], 0, everything)


def call(kernel, outs, scratch, scalars, *arrays, work=0.5):
    specs = [pl.BlockSpec(memory_space=pltpu.SMEM)] * scalars
    specs = specs + [pl.BlockSpec(memory_space=pltpu.VMEM)] * (len(arrays) - scalars)
    return pl.pallas_call(
        kernel,
        out_shape=[jax.ShapeDtypeStruct(shape, kind) for shape, kind in outs],
        in_specs=specs,
        out_specs=[pl.BlockSpec(memory_space=pltpu.VMEM)] * len(outs),
        scratch_shapes=[pltpu.VMEM(shape, kind) for shape, kind in scratch],
        compiler_params=pltpu.CompilerParams(vmem_limit_bytes=VMEM_BYTES),
        cost_estimate=pl.CostEstimate(flops=int(work * 1e9), bytes_accessed=int(work * 3e6), transcendentals=0),
    )(*arrays)


def body(
    target,
    memory,
    grad_out,
    tgt_len,
    src_len,
    w_qkv,
    w_out,
    wq_cross,
    wkv_cross,
    wo_cross,
    w_up,
    w_down,
    ln_gain,
    ln_bias,
):
    rows, width = target.shape
    half = rows // 2
    hidden_width = w_down.shape[0]
    groups = lax.axis_size("mem")
    me = lax.axis_index("mem")
    count = tgt_len.shape[1]
    span = memory.shape[1]
    places = groups * span
    dp = lax.axis_index("dp")
    first_sum = Summing(hidden_width + width // 2, width, False)
    second_sum = Summing(3 * width + width // 2, width, True)
    spot = first_sum.spot(me, dp)

    came = []
    for shift in range(1, groups):
        pairs = [(i, (i + shift) % groups) for i in range(groups)]
        sent = lax.dynamic_slice_in_dim(memory, ((me + shift) % groups) * count, count, 0)
        came.append(lax.ppermute(sent, "mem", pairs))

    sorted_rows, qkv, self_norm, self_attn_t, hidden_one, query, pair_mine = call(
        self_forward_kernel,
        [
            ((rows, width), BF16),
            ((rows, 3 * width), BF16),
            ((HEADS, rows), F32),
            ((width, rows), BF16),
            ((rows, width), F32),
            ((rows, width), BF16),
            ((count, span, 2 * width), BF16),
        ],
        [
            ((2, half, half), F32),
            ((2, rows, width), BF16),
            ((width, rows), BF16),
        ],
        2,
        spot,
        tgt_len,
        target,
        w_qkv,
        w_out,
        wq_cross,
        ln_gain,
        ln_bias,
        memory,
        wkv_cross,
    )
    result_out, pair_long, pair_rest, cross_norm, keep_one, send_one, grad_hidden_two, grad_attn, ln_part = call(
        functools.partial(middle_kernel, groups),
        [
            ((rows, width), BF16),
            ((places, 2 * width), BF16),
            (((count - 1) * places, 2 * width), BF16),
            ((HEADS, rows), F32),
            ((first_sum.padded, width), BF16),
            ((first_sum.padded, width), BF16),
            ((rows, width), F32),
            ((rows, width), BF16),
            ((4, width), F32),
        ],
        [
            ((count, places, half), F32),
            ((2, rows, width), BF16),
            ((width, count * places), BF16),
            ((width, rows), BF16),
            ((rows, hidden_width), BF16),
            ((rows, hidden_width), F32),
            ((rows, width), F32),
        ],
        3,
        spot,
        tgt_len,
        src_len,
        hidden_one,
        query,
        pair_mine,
        wkv_cross,
        wo_cross,
        w_up,
        w_down,
        ln_gain,
        ln_bias,
        grad_out,
        *came,
    )
    came_one = first_sum.core_swap(send_one)

    def cross_backward(block, pair):
        keys = pair.shape[0]
        sentences = keys // places
        return call(
            functools.partial(cross_backward_kernel, groups, block),
            [((keys, 2 * width), BF16), ((width, half), BF16)],
            [
                ((sentences, places, half), F32),
                ((2, half, width), BF16),
                ((2, half, width), BF16),
                ((width, keys), BF16),
            ],
            3,
            spot,
            tgt_len,
            src_len,
            query,
            pair,
            cross_norm,
            grad_attn,
            work=10,
        )

    pair_grad_long, query_grad_t_long = cross_backward(0, pair_long)
    came_one, pair_grad_long = lax.optimization_barrier((came_one, pair_grad_long))
    parts_one = first_sum.split(0, spot, keep_one, came_one)
    parts_one, pair_rest = lax.optimization_barrier((parts_one, pair_rest))
    parts_one = first_sum.swap(parts_one, 0)
    pair_grad_rest, query_grad_t_rest = cross_backward(1, pair_rest)
    *memory_grads, middle, ln_sums, grad_hidden_one, grad_self = call(
        functools.partial(memory_backward_kernel, groups),
        [((count, span, width), BF16)] * groups
        + [
            ((4 * width, width), BF16),
            ((LN_ROWS, width), BF16),
            ((rows, width), F32),
            ((rows, width), BF16),
        ],
        [((width, 2 * width), F32)],
        2,
        spot,
        tgt_len,
        hidden_one,
        pair_grad_long,
        pair_grad_rest,
        query_grad_t_long,
        query_grad_t_rest,
        grad_hidden_two,
        wkv_cross,
        wq_cross,
        w_out,
        self_attn_t,
        ln_gain,
        ln_bias,
        ln_part,
        memory,
        *came,
    )
    parts_one, grad_self = lax.optimization_barrier((parts_one, grad_self))
    parts_one = first_sum.split(1, spot, *parts_one)
    parts_one, grad_self = lax.optimization_barrier((parts_one, grad_self))
    parts_one = first_sum.swap(parts_one, 1)
    grad_triple, keep_two, send_two = call(
        self_backward_kernel,
        [
            ((rows, 3 * width), BF16),
            ((second_sum.padded, width), BF16),
            ((second_sum.padded, width), BF16),
        ],
        [
            ((2, half, half), F32),
            ((2, rows, width), BF16),
            ((2, rows, width), BF16),
            ((width, rows), BF16),
            ((width, rows), BF16),
        ],
        2,
        spot,
        tgt_len,
        qkv,
        self_norm,
        grad_self,
        sorted_rows,
        middle,
        ln_sums,
        work=6,
    )
    (grad_target,) = call(
        target_kernel,
        [((rows, width), BF16)],
        [],
        2,
        spot,
        tgt_len,
        grad_triple,
        w_qkv,
        grad_hidden_one,
        work=4,
    )
    backs = []
    for shift in range(1, groups):
        pairs = [(i, (i - shift) % groups) for i in range(groups)]
        backs.append(lax.ppermute(memory_grads[shift], "mem", pairs))
    send_two, backs, grad_target, parts_one = lax.optimization_barrier(
        (send_two, backs, grad_target, parts_one)
    )
    came_two = second_sum.core_swap(send_two)
    (sum_one,) = first_sum.total(parts_one)
    all_one = first_sum.gather(sum_one)
    parts_two = second_sum.swap(second_sum.split(0, spot, keep_two, came_two), 0)
    parts_two = second_sum.swap(second_sum.split(1, spot, *parts_two), 1)
    sum_two, norm_sums = second_sum.total(parts_two)
    chunks = hidden_width // width
    pieces = []
    for chunk in range(chunks):
        side, here = chunk // (chunks // 2), chunk % (chunks // 2)
        pieces.append((side, here * width, width, 0, chunk * width, 0))
        pieces.append((side, (chunks // 2 + here) * width, width, 1, 0, chunk * width))
    for side in range(2):
        pieces.append((side, chunks * width, width // 2, 2, side * width // 2, 0))
    all_one, sum_two = lax.optimization_barrier((all_one, sum_two))
    all_two = second_sum.gather(sum_two)
    grad_w_down, grad_w_up, grad_wo = first_sum.finish(
        all_one,
        pieces,
        [((hidden_width, width), F32), ((width, hidden_width), F32), ((width, width), F32)],
    )
    short = width // 2
    pieces = [
        (0, 0, width, 0, 0, 0),
        (0, width, width, 1, 0, 0),
        (0, 2 * width, width, 1, 0, width),
        (0, 3 * width, short, 2, 0, 0),
        (1, 0, width, 3, 0, 0),
        (1, width, width, 2, 0, width),
        (1, 2 * width, width, 2, 0, 2 * width),
        (1, 3 * width, short, 2, short, 0),
    ]
    grad_wq, grad_wkv, grad_w_qkv, grad_w_out = second_sum.finish(
        all_two,
        pieces,
        [
            ((width, width), F32),
            ((width, 2 * width), F32),
            ((width, 3 * width), F32),
            ((width, width), F32),
        ],
    )
    grad_memory = jnp.zeros(memory.shape, BF16)
    grad_memory = lax.dynamic_update_slice_in_dim(grad_memory, memory_grads[0], me * count, 0)
    for shift in range(1, groups):
        grad_memory = lax.dynamic_update_slice_in_dim(
            grad_memory, backs[shift - 1], ((me + shift) % groups) * count, 0
        )
    return (
        result_out,
        grad_target,
        grad_memory,
        grad_w_qkv,
        grad_w_out,
        grad_wq,
        grad_wkv,
        grad_wo,
        grad_w_up,
        grad_w_down,
        norm_sums[:3],
        norm_sums[3:6],
    )


def solution(mesh):
    rows_spec = P(("dp", "mem"), None)
    memory_spec = P("dp", "mem", None)
    return jax.shard_map(
        body,
        mesh=mesh,
        in_specs=(rows_spec, memory_spec, rows_spec, P("dp", None), P("dp", None)) + (P(),) * 9,
        out_specs=(rows_spec, rows_spec, memory_spec) + (P(),) * 9,
        check_vma=False,
    )
```

```python
import functools

import jax
import jax.numpy as jnp
from jax import lax
from jax.experimental import pallas as pl
from jax.experimental.pallas import tpu as pltpu
from jax.sharding import PartitionSpec as P

HEADS = 8
SLAB = 128
MASKED = -1e30
EPSILON = 1e-05
F32 = jnp.float32
BF16 = jnp.bfloat16
MIB = 1024 * 1024
LN_ROWS = 16


def dot(left, right):
    return jnp.dot(left, right, preferred_element_type=F32)


def dot_nt(left, right):
    return lax.dot_general(left, right, (((1,), (1,)), ((), ())), preferred_element_type=F32)


def dot_tn(left, right):
    return lax.dot_general(left, right, (((0,), (0,)), ((), ())), preferred_element_type=F32)


def iota(shape, axis):
    return lax.broadcasted_iota(jnp.int32, shape, axis)


def norm_parts(hidden):
    centre = hidden - jnp.mean(hidden, axis=-1, keepdims=True)
    inverse = lax.rsqrt(jnp.mean(centre * centre, axis=-1, keepdims=True) + EPSILON)
    return centre * inverse, inverse


def norm_backward(upstream, unit, inverse, gain_row):
    scaled = upstream * gain_row
    shifted = (
        scaled
        - jnp.mean(scaled, axis=-1, keepdims=True)
        - unit * jnp.mean(scaled * unit, axis=-1, keepdims=True)
    )
    gain_grad = jnp.sum(upstream * unit, axis=0, keepdims=True)
    return inverse * shifted, gain_grad, jnp.sum(upstream, axis=0, keepdims=True)


def sentence_order(me, len_ref):
    count = len_ref.shape[1]
    lengths = [len_ref[me, k] for k in range(count)]
    longest, best, start, running = jnp.int32(0), lengths[0], jnp.int32(0), jnp.int32(0)
    for k in range(1, count):
        running = running + lengths[k - 1]
        more = lengths[k] > best
        longest = jnp.where(more, k, longest)
        start = jnp.where(more, running, start)
        best = jnp.where(more, lengths[k], best)
    order = [longest] + [jnp.where(k < longest, k, k + 1) for k in range(count - 1)]
    bounds = [jnp.int32(0)]
    for k in range(1, count):
        bounds.append(bounds[-1] + len_ref[me, order[k]])
    return order, start, bounds


def moved_rows(index, start, half):
    return jnp.where(index < start, index + half, jnp.where(index < start + half, index - start, index))


def sort_matrix(rows, start):
    spot = moved_rows(iota((rows, rows), 1), start, rows // 2)
    return jnp.where(spot == iota((rows, rows), 0), 1.0, 0.0).astype(BF16)


def unsort_matrix(rows, start):
    spot = moved_rows(iota((rows, rows), 0), start, rows // 2)
    return jnp.where(spot == iota((rows, rows), 1), 1.0, 0.0).astype(BF16)


def side_masks(width):
    side = iota((1, width), 1) % SLAB
    first = jnp.where(side < SLAB // 2, 1.0, 0.0)
    return first.astype(BF16), (1.0 - first).astype(BF16)


def fill_self_bias(bias_ref, bounds, half):
    key = iota((half, half), 0)
    query = iota((half, half), 1)
    first = jnp.zeros((half, half), jnp.int32)
    for bound in bounds[1:-1]:
        first = jnp.where(query >= bound, bound, first)
    causal = key <= query
    bias_ref[0] = jnp.where(causal, 0.0, MASKED)
    bias_ref[1] = jnp.where(causal & (key >= first), 0.0, MASKED)


def fill_cross_bias(bias_ref, me, groups, span, src_ref, order, bounds, half, rest_only=False):
    key = iota((span, half), 0)
    query = iota((span, half), 1)
    for j, sentence in enumerate(order):
        for part in range(groups):
            place = lax.rem(me - part + groups, groups) * span + key
            live = place < src_ref[me, sentence]
            if j > 0 or rest_only:
                k = j + 1 if rest_only else j
                live = live & (query >= bounds[k - 1]) & (query < bounds[k])
            bias_ref[j, pl.ds(part * span, span), :] = jnp.where(live, 0.0, MASKED)


def softmax_columns(scores):
    top = jnp.max(scores, axis=0, keepdims=True)
    weights = jnp.exp(scores - top)
    total = jnp.sum(weights, axis=0, keepdims=True)
    return (weights * (1.0 / total)).astype(BF16), top + jnp.log(total)


def self_forward_kernel(
    me_ref,
    len_ref,
    target_ref,
    w_qkv_ref,
    w_out_ref,
    wq_ref,
    gain_ref,
    bias_row_ref,
    memory_ref,
    wkv_ref,
    sorted_ref,
    qkv_ref,
    norm_ref,
    attn_t_ref,
    hidden_ref,
    query_ref,
    pair_ref,
    bias_ref,
    q_side_ref,
    value_t_ref,
):
    rows, width = target_ref.shape
    half = rows // 2
    me = me_ref[0]
    order, start, bounds = sentence_order(me, len_ref)
    sorted_rows = dot(sort_matrix(rows, start), target_ref[...]).astype(BF16)
    sorted_ref[...] = sorted_rows
    fill_self_bias(bias_ref, bounds, half)
    queries = dot(sorted_rows, w_qkv_ref[:, :width]).astype(BF16) * 0.125
    queries = queries.astype(BF16)
    qkv_ref[:, :width] = queries
    first, second = side_masks(width)
    q_side_ref[0] = queries * first
    q_side_ref[1] = queries * second
    qkv_ref[:, width : 2 * width] = dot(sorted_rows, w_qkv_ref[:, width : 2 * width]).astype(BF16)
    values = dot(sorted_rows, w_qkv_ref[:, 2 * width :]).astype(BF16)
    qkv_ref[:, 2 * width :] = values
    value_t_ref[...] = values.T

    def pair_step(pair, carry):
        slab = pl.ds(pl.multiple_of(pair * SLAB, SLAB), SLAB)
        key_slab = pl.ds(pl.multiple_of(width + pair * SLAB, SLAB), SLAB)
        for side in range(2):
            head = pair * 2 + side
            feats = pl.ds(pl.multiple_of(head * (SLAB // 2), SLAB // 2), SLAB // 2)
            for block in range(2):
                span = pl.ds(block * half, half)
                scores = dot_nt(qkv_ref[span, key_slab], q_side_ref[side, span, slab]) + bias_ref[block]
                probs, norm = softmax_columns(scores)
                attn_t_ref[feats, span] = dot(value_t_ref[feats, span], probs).astype(BF16)
                norm_ref[pl.ds(head, 1), span] = norm
        return carry

    lax.fori_loop(0, HEADS // 2, pair_step, 0)
    attn = attn_t_ref[...].T
    hidden = sorted_rows.astype(F32) + dot(attn, w_out_ref[...])
    hidden_ref[...] = hidden
    unit, _ = norm_parts(hidden)
    normed = (unit * gain_ref[0:1] + bias_row_ref[0:1]).astype(BF16)
    query_ref[...] = (dot(normed, wq_ref[...]).astype(BF16) * 0.125).astype(BF16)
    count = pair_ref.shape[0]
    for j in range(count):
        block = memory_ref[me * count + order[j]]
        pair_ref[j] = dot(block, wkv_ref[...]).astype(BF16)


def fill_padding(keep_ref, send_ref, used):
    total, width = keep_ref.shape
    if total > used:
        keep_ref[used:, :] = jnp.zeros((total - used, width), BF16)
        send_ref[used:, :] = jnp.zeros((total - used, width), BF16)


def middle_kernel(
    groups,
    me_ref,
    len_ref,
    src_ref,
    hidden_one_ref,
    query_ref,
    pair_mine_ref,
    wkv_ref,
    wo_ref,
    w_up_ref,
    w_down_ref,
    gain_ref,
    bias_row_ref,
    grad_out_ref,
    *refs,
):
    came_refs = refs[: groups - 1]
    (
        out_ref,
        pair_long_ref,
        pair_rest_ref,
        norm_ref,
        keep_ref,
        send_ref,
        grad_hidden_ref,
        grad_attn_ref,
        ln_ref,
        bias_ref,
        q_side_ref,
        value_t_ref,
        attn_t_ref,
        active_ref,
        slope_ref,
        total_ref,
    ) = refs[groups - 1 :]
    rows, width = hidden_one_ref.shape
    half = rows // 2
    me = me_ref[0]
    count, span = pair_mine_ref.shape[0], pair_mine_ref.shape[1]
    places = groups * span
    order, start, bounds = sentence_order(me, len_ref)
    fill_cross_bias(bias_ref, me, groups, span, src_ref, order, bounds, half)
    first, second = side_masks(width)
    q_side_ref[0] = query_ref[...] * first
    q_side_ref[1] = query_ref[...] * second
    for j in range(count):
        pair_ref = pair_long_ref if j == 0 else pair_rest_ref
        first_row = max(j - 1, 0) * places
        pair_ref[pl.ds(first_row, span), :] = pair_mine_ref[j]
        for part in range(1, groups):
            block = came_refs[part - 1][order[j]]
            here = pl.ds(first_row + part * span, span)
            pair_ref[here, :] = dot(block, wkv_ref[...]).astype(BF16)
        value_t_ref[:, pl.ds(j * places, places)] = pair_ref[pl.ds(first_row, places), width:].T
    others = (count - 1) * places

    def pair_step(pair, carry):
        slab = pl.ds(pl.multiple_of(pair * SLAB, SLAB), SLAB)
        for side in range(2):
            head = pair * 2 + side
            feats = pl.ds(pl.multiple_of(head * (SLAB // 2), SLAB // 2), SLAB // 2)
            scores = dot_nt(pair_long_ref[:, slab], q_side_ref[side, :half, slab]) + bias_ref[0]
            probs, norm = softmax_columns(scores)
            attn_t_ref[feats, :half] = dot(value_t_ref[feats, :places], probs).astype(BF16)
            norm_ref[pl.ds(head, 1), :half] = norm
            keys = pair_rest_ref[:, slab]
            scores = dot_nt(keys, q_side_ref[side, half:, slab]) + bias_ref[1:].reshape(others, half)
            probs, norm = softmax_columns(scores)
            attn_t_ref[feats, half:] = dot(value_t_ref[feats, places:], probs).astype(BF16)
            norm_ref[pl.ds(head, 1), half:] = norm
        return carry

    lax.fori_loop(0, HEADS // 2, pair_step, 0)
    attn = attn_t_ref[...].T
    unit_one, _ = norm_parts(hidden_one_ref[...])
    normed_one = unit_one * gain_ref[0:1] + bias_row_ref[0:1]
    hidden_two = normed_one + dot(attn, wo_ref[...])
    unit_two, inverse_two = norm_parts(hidden_two)
    normed_two = unit_two * gain_ref[1:2] + bias_row_ref[1:2]
    normed_two_low = normed_two.astype(BF16)
    total_ref[...] = normed_two
    chunk = width
    chunks = w_down_ref.shape[0] // chunk

    def up_step(c, carry):
        cols = pl.ds(pl.multiple_of(c * chunk, chunk), chunk)
        upper = dot(normed_two_low, w_up_ref[:, cols])
        sigma = 1.0 / (1.0 + jnp.exp(-upper))
        active = (upper * sigma).astype(BF16)
        active_ref[:, cols] = active
        slope_ref[:, cols] = sigma * (1.0 + upper * (1.0 - sigma))
        total_ref[...] += dot(active, w_down_ref[cols, :])
        return carry

    lax.fori_loop(0, chunks, up_step, 0)
    unit_three, inverse_three = norm_parts(total_ref[...])
    result = (unit_three * gain_ref[2:3] + bias_row_ref[2:3]).astype(BF16)
    out_ref[...] = dot(unsort_matrix(rows, start), result).astype(BF16)
    upstream = dot(sort_matrix(rows, start), grad_out_ref[...])
    grad_three, gain_three, bias_three = norm_backward(upstream, unit_three, inverse_three, gain_ref[2:3])
    grad_down = grad_three.astype(BF16)
    total_ref[...] = grad_three
    normed_two_t = normed_two_low.T

    def down_step(c, carry):
        cols = pl.ds(pl.multiple_of(c * chunk, chunk), chunk)
        grad_upper = (dot_nt(grad_down, w_down_ref[cols, :]) * slope_ref[:, cols]).astype(BF16)
        down_part = dot_tn(active_ref[:, cols], grad_down).astype(BF16)
        up_part = dot(normed_two_t, grad_upper).astype(BF16)
        here = lax.rem(c, chunks // 2)
        down_rows = pl.ds(pl.multiple_of(here * chunk, chunk), chunk)
        up_rows = pl.ds(pl.multiple_of((chunks // 2 + here) * chunk, chunk), chunk)
        mine = c // (chunks // 2) == me_ref[1]

        @pl.when(mine)
        def _():
            keep_ref[down_rows, :] = down_part
            keep_ref[up_rows, :] = up_part

        @pl.when(jnp.logical_not(mine))
        def _():
            send_ref[down_rows, :] = down_part
            send_ref[up_rows, :] = up_part

        total_ref[...] += dot_nt(grad_upper, w_up_ref[:, cols])
        return carry

    lax.fori_loop(0, chunks, down_step, 0)
    grad_two, gain_two, bias_two = norm_backward(total_ref[...], unit_two, inverse_two, gain_ref[1:2])
    grad_hidden_ref[...] = grad_two
    grad_two_low = grad_two.astype(BF16)
    wo_grad = dot(attn_t_ref[...], grad_two_low).astype(BF16)
    core = me_ref[1]
    low, high = wo_grad[: width // 2], wo_grad[width // 2 :]
    tail = pl.ds(chunks * chunk, width // 2)
    keep_ref[tail, :] = jnp.where(core == 0, low, high)
    send_ref[tail, :] = jnp.where(core == 0, high, low)
    fill_padding(keep_ref, send_ref, chunks * chunk + width // 2)
    grad_attn_ref[...] = dot_nt(grad_two_low, wo_ref[...]).astype(BF16)
    ln_ref[...] = jnp.concatenate([gain_two, gain_three, bias_two, bias_three], axis=0)


def cross_backward_kernel(
    groups,
    block,
    me_ref,
    len_ref,
    src_ref,
    query_ref,
    pair_ref,
    norm_ref,
    grad_attn_ref,
    pair_grad_ref,
    query_grad_t_ref,
    bias_ref,
    q_side_ref,
    g_side_ref,
    key_t_ref,
):
    width = query_ref.shape[1]
    half = query_ref.shape[0] // 2
    me = me_ref[0]
    count = len_ref.shape[1]
    keys_total = pair_ref.shape[0]
    sentences = 1 if block == 0 else count - 1
    places = keys_total // sentences
    order, start, bounds = sentence_order(me, len_ref)
    if block == 0:
        fill_cross_bias(bias_ref, me, groups, places // groups, src_ref, order[:1], bounds, half)
    else:
        fill_cross_bias(bias_ref, me, groups, places // groups, src_ref, order[1:], bounds, half, True)
    first, second = side_masks(width)
    rows_here = slice(block * half, (block + 1) * half)
    q_side_ref[0] = query_ref[rows_here, :] * first
    q_side_ref[1] = query_ref[rows_here, :] * second
    g_side_ref[0] = grad_attn_ref[rows_here, :] * first
    g_side_ref[1] = grad_attn_ref[rows_here, :] * second
    key_t_ref[...] = pair_ref[:, :width].T

    def pair_step(pair, carry):
        slab = pl.ds(pl.multiple_of(pair * SLAB, SLAB), SLAB)
        value_slab = pl.ds(pl.multiple_of(width + pair * SLAB, SLAB), SLAB)
        keys, values = pair_ref[:, slab], pair_ref[:, value_slab]
        key_sum = value_sum = None
        for side in range(2):
            head = pair * 2 + side
            feats = pl.ds(pl.multiple_of(head * (SLAB // 2), SLAB // 2), SLAB // 2)
            q_rows = q_side_ref[side, :, slab]
            g_rows = g_side_ref[side, :, slab]
            scores = dot_nt(keys, q_rows) + bias_ref[...].reshape(keys_total, half)
            probs = jnp.exp(scores - norm_ref[pl.ds(head, 1), rows_here])
            grad_probs = dot_nt(values, g_rows)
            along = jnp.sum(probs * grad_probs, axis=0, keepdims=True)
            grad_scores = (probs * (grad_probs - along)).astype(BF16)
            value_part = dot(probs.astype(BF16), g_rows)
            key_part = dot(grad_scores, q_rows)
            value_sum = value_part if value_sum is None else value_sum + value_part
            key_sum = key_part if key_sum is None else key_sum + key_part
            query_grad_t_ref[feats, :] = (dot(key_t_ref[feats, :], grad_scores) * 0.125).astype(BF16)
        pair_grad_ref[:, slab] = key_sum.astype(BF16)
        pair_grad_ref[:, value_slab] = value_sum.astype(BF16)
        return carry

    lax.fori_loop(0, HEADS // 2, pair_step, 0)


def memory_backward_kernel(
    groups,
    me_ref,
    len_ref,
    hidden_one_ref,
    pair_grad_long_ref,
    pair_grad_rest_ref,
    query_grad_t_long_ref,
    query_grad_t_rest_ref,
    grad_hidden_two_ref,
    wkv_ref,
    wq_ref,
    w_out_ref,
    self_attn_t_ref,
    gain_ref,
    bias_row_ref,
    ln_in_ref,
    memory_ref,
    *refs,
):
    came_refs = refs[: groups - 1]
    memory_grad_refs = refs[groups - 1 : 2 * groups - 1]
    mid_ref, ln_ref, grad_hidden_ref, grad_self_ref, total_ref = refs[2 * groups - 1 :]
    rows, width = hidden_one_ref.shape
    half = rows // 2
    me = me_ref[0]
    count = len_ref.shape[1]
    places = pair_grad_long_ref.shape[0]
    span = places // groups
    order, _, _ = sentence_order(me, len_ref)
    for j in range(count):
        pair_grad_ref = pair_grad_long_ref if j == 0 else pair_grad_rest_ref
        first_row = max(j - 1, 0) * places
        for part in range(groups):
            grads = pair_grad_ref[pl.ds(first_row + part * span, span), :]
            memory_grad_refs[part][order[j]] = dot_nt(grads, wkv_ref[...]).astype(BF16)
            if part == 0:
                block = memory_ref[me * count + order[j]]
            else:
                block = came_refs[part - 1][order[j]]
            term = dot_tn(block, grads)
            if j == 0 and part == 0:
                total_ref[...] = term
            else:
                total_ref[...] += term
    unit_one, inverse_one = norm_parts(hidden_one_ref[...])
    normed_one = (unit_one * gain_ref[0:1] + bias_row_ref[0:1]).astype(BF16)
    query_grad = jnp.concatenate([query_grad_t_long_ref[...].T, query_grad_t_rest_ref[...].T], axis=0)
    upstream = grad_hidden_two_ref[...] + dot_nt(query_grad, wq_ref[...])
    grad_one, gain_one, bias_one = norm_backward(upstream, unit_one, inverse_one, gain_ref[0:1])
    grad_hidden_ref[...] = grad_one
    grad_one_low = grad_one.astype(BF16)
    grad_self_ref[...] = dot_nt(grad_one_low, w_out_ref[...]).astype(BF16)
    mid_ref[:width] = dot_tn(normed_one, query_grad).astype(BF16)
    mid_ref[width : 2 * width] = total_ref[:, :width].astype(BF16)
    mid_ref[2 * width : 3 * width] = total_ref[:, width:].astype(BF16)
    mid_ref[3 * width :] = dot(self_attn_t_ref[...], grad_one_low).astype(BF16)
    norms = jnp.concatenate(
        [gain_one, ln_in_ref[0:2], bias_one, ln_in_ref[2:4], jnp.zeros((LN_ROWS - 6, width), F32)], axis=0
    )
    ln_ref[...] = norms.astype(BF16)


def self_backward_kernel(
    me_ref,
    len_ref,
    qkv_ref,
    norm_ref,
    grad_attn_ref,
    sorted_ref,
    mid_ref,
    ln_in_ref,
    grad_triple_ref,
    keep_ref,
    send_ref,
    bias_ref,
    q_side_ref,
    g_side_ref,
    key_t_ref,
    query_grad_t_ref,
):
    rows, width = sorted_ref.shape
    half = rows // 2
    order, start, bounds = sentence_order(me_ref[0], len_ref)
    fill_self_bias(bias_ref, bounds, half)
    first, second = side_masks(width)
    q_side_ref[0] = qkv_ref[:, :width] * first
    q_side_ref[1] = qkv_ref[:, :width] * second
    g_side_ref[0] = grad_attn_ref[...] * first
    g_side_ref[1] = grad_attn_ref[...] * second
    key_t_ref[...] = qkv_ref[:, width : 2 * width].T

    def pair_step(pair, carry):
        slab = pl.ds(pl.multiple_of(pair * SLAB, SLAB), SLAB)
        key_slab = pl.ds(pl.multiple_of(width + pair * SLAB, SLAB), SLAB)
        value_slab = pl.ds(pl.multiple_of(2 * width + pair * SLAB, SLAB), SLAB)
        for block in range(2):
            span = pl.ds(block * half, half)
            keys, values = qkv_ref[span, key_slab], qkv_ref[span, value_slab]
            key_sum = value_sum = None
            for side in range(2):
                head = pair * 2 + side
                feats = pl.ds(pl.multiple_of(head * (SLAB // 2), SLAB // 2), SLAB // 2)
                q_rows = q_side_ref[side, span, slab]
                g_rows = g_side_ref[side, span, slab]
                scores = dot_nt(keys, q_rows) + bias_ref[block]
                probs = jnp.exp(scores - norm_ref[pl.ds(head, 1), span])
                grad_probs = dot_nt(values, g_rows)
                along = jnp.sum(probs * grad_probs, axis=0, keepdims=True)
                grad_scores = (probs * (grad_probs - along)).astype(BF16)
                value_part = dot(probs.astype(BF16), g_rows)
                key_part = dot(grad_scores, q_rows)
                value_sum = value_part if value_sum is None else value_sum + value_part
                key_sum = key_part if key_sum is None else key_sum + key_part
                query_grad_t_ref[feats, span] = (
                    dot(key_t_ref[feats, span], grad_scores) * 0.125
                ).astype(BF16)
            grad_triple_ref[span, key_slab] = key_sum.astype(BF16)
            grad_triple_ref[span, value_slab] = value_sum.astype(BF16)
        return carry

    lax.fori_loop(0, HEADS // 2, pair_step, 0)
    grad_triple_ref[:, :width] = query_grad_t_ref[...].T
    sorted_t = sorted_ref[...].T
    core = me_ref[1]
    grads = [
        dot(sorted_t, grad_triple_ref[:, part * width : (part + 1) * width]).astype(BF16)
        for part in range(3)
    ]
    used = 3 * width + width // 2

    def halves(low_ref, high_ref):
        low_ref[: 3 * width, :] = mid_ref[: 3 * width, :]
        low_ref[3 * width : used, :] = grads[0][: width // 2]
        high_ref[:width, :] = mid_ref[3 * width :, :]
        high_ref[width : 2 * width, :] = grads[1]
        high_ref[2 * width : 3 * width, :] = grads[2]
        high_ref[3 * width : used, :] = grads[0][width // 2 :]

    @pl.when(core == 0)
    def _():
        halves(keep_ref, send_ref)

    @pl.when(core != 0)
    def _():
        halves(send_ref, keep_ref)

    fill_padding(keep_ref, send_ref, used)
    keep_ref[keep_ref.shape[0] - LN_ROWS :, :] = ln_in_ref[...]
    send_ref[send_ref.shape[0] - LN_ROWS :, :] = ln_in_ref[...]


def target_kernel(me_ref, len_ref, grad_triple_ref, w_qkv_ref, grad_hidden_ref, grad_target_ref):
    rows = grad_hidden_ref.shape[0]
    _, start, _ = sentence_order(me_ref[0], len_ref)
    result = grad_hidden_ref[...] + dot_nt(grad_triple_ref[...], w_qkv_ref[...])
    grad_target_ref[...] = dot(unsort_matrix(rows, start), result.astype(BF16)).astype(BF16)


def tree_sum(terms):
    while len(terms) > 1:
        terms = [terms[i] + terms[i + 1] for i in range(0, len(terms), 2)]
    return terms[0]


def rows_of(ref, first, count):
    return ref[pl.ds(pl.multiple_of(first, 16), count), :].astype(F32)


def split_kernel(stage, ln, spot_ref, *refs):
    if stage == 0:
        ins, outs = refs[:2], refs[2:]
    else:
        ins, outs = refs[: stage], refs[stage:]
    extra = LN_ROWS if ln else 0
    size = outs[0].shape[0] - extra
    whole = size * len(outs)
    here = spot_ref[2] if stage == 0 else spot_ref[3]
    if ln:
        tail = tree_sum([rows_of(ref, whole, LN_ROWS) for ref in ins]).astype(BF16)
    for d, out in enumerate(outs):
        first = (here ^ d) * size
        out[:size, :] = tree_sum([rows_of(ref, first, size) for ref in ins]).astype(BF16)
        if ln:
            out[size:, :] = tail


def total_kernel(ln, count, *refs):
    ins, outs = refs[:count], refs[count:]
    size = outs[0].shape[0]
    outs[0][...] = tree_sum([rows_of(ref, 0, size) for ref in ins]).astype(BF16)
    if ln:
        outs[1][...] = tree_sum([rows_of(ref, size, LN_ROWS) for ref in ins])


def join_kernel(spot_ref, *refs):
    out_ref = refs[-1]
    for d, ref in enumerate(refs[:-1]):
        size = ref.shape[0]
        out_ref[pl.ds(pl.multiple_of((spot_ref[3] ^ d) * size, 16), size), :] = ref[...]


def finish_kernel(peers, twisted, pieces, spot_ref, *refs):
    mine, others, outs, both_ref = refs[:peers], refs[peers : 2 * peers], refs[2 * peers : -1], refs[-1]
    core = spot_ref[1]
    for half, arrays, here in ((core, mine, spot_ref[2]), (1 - core, others, spot_ref[3 if twisted else 2])):
        for d, ref in enumerate(arrays):
            size = ref.shape[0]
            both_ref[half, pl.ds(pl.multiple_of((here ^ d) * size, 16), size), :] = ref[...]
    width = both_ref.shape[2]
    for half, first, rows, out, row, col in pieces:
        outs[out][row : row + rows, col : col + width] = both_ref[half, first : first + rows, :].astype(F32)


class Summing:
    def __init__(self, rows, width, ln):
        self.width, self.ln = width, ln
        self.dp, self.mem = lax.axis_size("dp"), lax.axis_size("mem")
        self.z_size = 4
        self.x_size = self.dp // (2 * self.z_size)
        self.xy_size = self.x_size * self.mem
        self.twisted = self.xy_size == self.z_size
        unit = 16 * self.xy_size * self.z_size
        self.rows = -(-rows // unit) * unit
        self.padded = self.rows + (LN_ROWS if ln else 0)
        self.chunk = self.rows // (self.xy_size * self.z_size)

    def coords(self, dp, mem):
        return dp // (2 * self.x_size), (dp // 2 % self.x_size) * self.mem + mem, dp % 2

    def spot(self, me, dp):
        z, xy, core = self.coords(dp, me)
        first, second = xy, z
        if self.twisted:
            first, second = jnp.where(core == 0, xy, z), jnp.where(core == 0, z, xy)
        return jnp.stack([me, core, first, second]).astype(jnp.int32)

    def permute(self, array, stage, offset):
        pairs = []
        for dp in range(self.dp):
            for mem in range(self.mem):
                z, xy, core = self.coords(dp, mem)
                if stage == "core":
                    core ^= offset
                elif (stage == 0) != (self.twisted and core == 1):
                    xy ^= offset
                else:
                    z ^= offset
                to_dp = (z * self.x_size + xy // self.mem) * 2 + core
                pairs.append((dp * self.mem + mem, to_dp * self.mem + xy % self.mem))
        return lax.ppermute(array, ("dp", "mem"), pairs)

    def swap(self, arrays, stage):
        return [arrays[0]] + [self.permute(array, stage, d) for d, array in enumerate(arrays) if d > 0]

    def core_swap(self, send):
        return self.permute(send, "core", 1)

    def split(self, stage, spot, *arrays):
        extra = LN_ROWS if self.ln else 0
        peers = self.xy_size if stage == 0 else self.z_size
        size = self.rows // self.xy_size if stage == 0 else self.chunk
        outs = [((size + extra, self.width), BF16)] * peers
        kernel = functools.partial(split_kernel, 0 if stage == 0 else self.xy_size, self.ln)
        return call(kernel, outs, [], 1, spot, *arrays)

    def total(self, arrays):
        outs = [((self.chunk, self.width), BF16)]
        if self.ln:
            outs.append(((LN_ROWS, self.width), F32))
        return call(functools.partial(total_kernel, self.ln, self.z_size), outs, [], 0, *arrays)

    def spread(self, stage, array):
        size = self.xy_size if stage == 0 else self.z_size
        return [array] + [self.permute(array, stage, d) for d in range(1, size)]

    def join(self, spot, arrays):
        return call(join_kernel, [((self.rows // self.xy_size, self.width), BF16)], [], 1, spot, *arrays)[0]

    def finish(self, spot, mine, others, pieces, outs):
        kernel = functools.partial(finish_kernel, self.xy_size, self.twisted, pieces)
        scratch = [((2, self.rows, self.width), BF16)]
        return call(kernel, outs, scratch, 1, spot, *mine, *others, work=3, vmem=32)


def call(kernel, outs, scratch, scalars, *arrays, work=0.5, vmem=16):
    specs = [pl.BlockSpec(memory_space=pltpu.SMEM)] * scalars
    specs = specs + [pl.BlockSpec(memory_space=pltpu.VMEM)] * (len(arrays) - scalars)
    return pl.pallas_call(
        kernel,
        out_shape=[jax.ShapeDtypeStruct(shape, kind) for shape, kind in outs],
        in_specs=specs,
        out_specs=[pl.BlockSpec(memory_space=pltpu.VMEM)] * len(outs),
        scratch_shapes=[pltpu.VMEM(shape, kind) for shape, kind in scratch],
        compiler_params=pltpu.CompilerParams(vmem_limit_bytes=vmem * MIB),
        cost_estimate=pl.CostEstimate(flops=int(work * 1e9), bytes_accessed=int(work * 3e6), transcendentals=0),
    )(*arrays)


def body(
    target,
    memory,
    grad_out,
    tgt_len,
    src_len,
    w_qkv,
    w_out,
    wq_cross,
    wkv_cross,
    wo_cross,
    w_up,
    w_down,
    ln_gain,
    ln_bias,
):
    rows, width = target.shape
    half = rows // 2
    hidden_width = w_down.shape[0]
    groups = lax.axis_size("mem")
    me = lax.axis_index("mem")
    count = tgt_len.shape[1]
    span = memory.shape[1]
    places = groups * span
    dp = lax.axis_index("dp")
    first_sum = Summing(hidden_width + width // 2, width, False)
    second_sum = Summing(3 * width + width // 2, width, True)
    spot = first_sum.spot(me, dp)

    came = []
    for shift in range(1, groups):
        pairs = [(i, (i + shift) % groups) for i in range(groups)]
        sent = lax.dynamic_slice_in_dim(memory, ((me + shift) % groups) * count, count, 0)
        came.append(lax.ppermute(sent, "mem", pairs))

    sorted_rows, qkv, self_norm, self_attn_t, hidden_one, query, pair_mine = call(
        self_forward_kernel,
        [
            ((rows, width), BF16),
            ((rows, 3 * width), BF16),
            ((HEADS, rows), F32),
            ((width, rows), BF16),
            ((rows, width), F32),
            ((rows, width), BF16),
            ((count, span, 2 * width), BF16),
        ],
        [
            ((2, half, half), F32),
            ((2, rows, width), BF16),
            ((width, rows), BF16),
        ],
        2,
        spot,
        tgt_len,
        target,
        w_qkv,
        w_out,
        wq_cross,
        ln_gain,
        ln_bias,
        memory,
        wkv_cross,
        vmem=60,
    )
    result_out, pair_long, pair_rest, cross_norm, keep_one, send_one, grad_hidden_two, grad_attn, ln_part = call(
        functools.partial(middle_kernel, groups),
        [
            ((rows, width), BF16),
            ((places, 2 * width), BF16),
            (((count - 1) * places, 2 * width), BF16),
            ((HEADS, rows), F32),
            ((first_sum.padded, width), BF16),
            ((first_sum.padded, width), BF16),
            ((rows, width), F32),
            ((rows, width), BF16),
            ((4, width), F32),
        ],
        [
            ((count, places, half), F32),
            ((2, rows, width), BF16),
            ((width, count * places), BF16),
            ((width, rows), BF16),
            ((rows, hidden_width), BF16),
            ((rows, hidden_width), F32),
            ((rows, width), F32),
        ],
        3,
        spot,
        tgt_len,
        src_len,
        hidden_one,
        query,
        pair_mine,
        wkv_cross,
        wo_cross,
        w_up,
        w_down,
        ln_gain,
        ln_bias,
        grad_out,
        *came,
        vmem=60,
    )
    came_one = first_sum.core_swap(send_one)

    def cross_backward(block, pair):
        keys = pair.shape[0]
        sentences = keys // places
        return call(
            functools.partial(cross_backward_kernel, groups, block),
            [((keys, 2 * width), BF16), ((width, half), BF16)],
            [
                ((sentences, places, half), F32),
                ((2, half, width), BF16),
                ((2, half, width), BF16),
                ((width, keys), BF16),
            ],
            3,
            spot,
            tgt_len,
            src_len,
            query,
            pair,
            cross_norm,
            grad_attn,
            work=10,
            vmem=60,
        )

    pair_grad_long, query_grad_t_long = cross_backward(0, pair_long)
    came_one, pair_grad_long = lax.optimization_barrier((came_one, pair_grad_long))
    parts_one = first_sum.split(0, spot, keep_one, came_one)
    parts_one, pair_rest = lax.optimization_barrier((parts_one, pair_rest))
    parts_one = first_sum.swap(parts_one, 0)
    pair_grad_rest, query_grad_t_rest = cross_backward(1, pair_rest)
    *memory_grads, middle, ln_sums, grad_hidden_one, grad_self = call(
        functools.partial(memory_backward_kernel, groups),
        [((count, span, width), BF16)] * groups
        + [
            ((4 * width, width), BF16),
            ((LN_ROWS, width), BF16),
            ((rows, width), F32),
            ((rows, width), BF16),
        ],
        [((width, 2 * width), F32)],
        2,
        spot,
        tgt_len,
        hidden_one,
        pair_grad_long,
        pair_grad_rest,
        query_grad_t_long,
        query_grad_t_rest,
        grad_hidden_two,
        wkv_cross,
        wq_cross,
        w_out,
        self_attn_t,
        ln_gain,
        ln_bias,
        ln_part,
        memory,
        *came,
        vmem=60,
    )
    parts_one, grad_self = lax.optimization_barrier((parts_one, grad_self))
    parts_one = first_sum.split(1, spot, *parts_one)
    parts_one, grad_self = lax.optimization_barrier((parts_one, grad_self))
    parts_one = first_sum.swap(parts_one, 1)
    grad_triple, keep_two, send_two = call(
        self_backward_kernel,
        [
            ((rows, 3 * width), BF16),
            ((second_sum.padded, width), BF16),
            ((second_sum.padded, width), BF16),
        ],
        [
            ((2, half, half), F32),
            ((2, rows, width), BF16),
            ((2, rows, width), BF16),
            ((width, rows), BF16),
            ((width, rows), BF16),
        ],
        2,
        spot,
        tgt_len,
        qkv,
        self_norm,
        grad_self,
        sorted_rows,
        middle,
        ln_sums,
        work=6,
        vmem=60,
    )
    (grad_target,) = call(
        target_kernel,
        [((rows, width), BF16)],
        [],
        2,
        spot,
        tgt_len,
        grad_triple,
        w_qkv,
        grad_hidden_one,
        work=4,
        vmem=60,
    )
    backs = []
    for shift in range(1, groups):
        pairs = [(i, (i - shift) % groups) for i in range(groups)]
        backs.append(lax.ppermute(memory_grads[shift], "mem", pairs))
    send_two, backs, parts_one = lax.optimization_barrier((send_two, backs, parts_one))
    came_two = second_sum.core_swap(send_two)
    sum_one = first_sum.total(parts_one)[0]
    spread_one = first_sum.spread(1, sum_one)
    came_two, grad_target, spread_one = lax.optimization_barrier((came_two, grad_target, spread_one))
    parts_two = second_sum.split(0, spot, keep_two, came_two)
    parts_two, spread_one = lax.optimization_barrier((parts_two, spread_one))
    parts_two = second_sum.swap(parts_two, 0)
    spread_one = first_sum.spread(0, first_sum.join(spot, spread_one))
    other_one = [first_sum.core_swap(array) for array in spread_one]
    parts_two = second_sum.swap(second_sum.split(1, spot, *parts_two), 1)
    sum_two, norm_sums = second_sum.total(parts_two)
    spread_two = second_sum.spread(0, second_sum.join(spot, second_sum.spread(1, sum_two)))
    other_two = [second_sum.core_swap(array) for array in spread_two]
    chunks = hidden_width // width
    pieces = []
    for chunk in range(chunks):
        side, here = chunk // (chunks // 2), chunk % (chunks // 2)
        pieces.append((side, here * width, width, 0, chunk * width, 0))
        pieces.append((side, (chunks // 2 + here) * width, width, 1, 0, chunk * width))
    for side in range(2):
        pieces.append((side, chunks * width, width // 2, 2, side * width // 2, 0))
    grad_w_down, grad_w_up, grad_wo = first_sum.finish(
        spot,
        spread_one,
        other_one,
        pieces,
        [((hidden_width, width), F32), ((width, hidden_width), F32), ((width, width), F32)],
    )
    short = width // 2
    pieces = [
        (0, 0, width, 0, 0, 0),
        (0, width, width, 1, 0, 0),
        (0, 2 * width, width, 1, 0, width),
        (0, 3 * width, short, 2, 0, 0),
        (1, 0, width, 3, 0, 0),
        (1, width, width, 2, 0, width),
        (1, 2 * width, width, 2, 0, 2 * width),
        (1, 3 * width, short, 2, short, 0),
    ]
    grad_wq, grad_wkv, grad_w_qkv, grad_w_out = second_sum.finish(
        spot,
        spread_two,
        other_two,
        pieces,
        [
            ((width, width), F32),
            ((width, 2 * width), F32),
            ((width, 3 * width), F32),
            ((width, width), F32),
        ],
    )
    grad_memory = jnp.zeros(memory.shape, BF16)
    grad_memory = lax.dynamic_update_slice_in_dim(grad_memory, memory_grads[0], me * count, 0)
    for shift in range(1, groups):
        grad_memory = lax.dynamic_update_slice_in_dim(
            grad_memory, backs[shift - 1], ((me + shift) % groups) * count, 0
        )
    return (
        result_out,
        grad_target,
        grad_memory,
        grad_w_qkv,
        grad_w_out,
        grad_wq,
        grad_wkv,
        grad_wo,
        grad_w_up,
        grad_w_down,
        norm_sums[:3],
        norm_sums[3:6],
    )


def solution(mesh):
    rows_spec = P(("dp", "mem"), None)
    memory_spec = P("dp", "mem", None)
    return jax.shard_map(
        body,
        mesh=mesh,
        in_specs=(rows_spec, memory_spec, rows_spec, P("dp", None), P("dp", None)) + (P(),) * 9,
        out_specs=(rows_spec, rows_spec, memory_spec) + (P(),) * 9,
        check_vma=False,
    )
```

```python
import functools
import math

import jax
import jax.numpy as jnp
from jax import lax
from jax.experimental import pallas as pl
from jax.experimental.pallas import tpu as pltpu
from jax.sharding import PartitionSpec as P

HEADS = 8
PAIRS = HEADS // 2
SLAB = 128
SIDE = SLAB // 2
TILE = 128
MASKED = -1e30
EPSILON = 1e-05
F32 = jnp.float32
BF16 = jnp.bfloat16
MIB = 1024 * 1024
LN_ROWS = 16


def dot(left, right):
    return jnp.dot(left, right, preferred_element_type=F32)


def dot_nt(left, right):
    return lax.dot_general(left, right, (((1,), (1,)), ((), ())), preferred_element_type=F32)


def dot_tn(left, right):
    return lax.dot_general(left, right, (((0,), (0,)), ((), ())), preferred_element_type=F32)


def iota(shape, axis):
    return lax.broadcasted_iota(jnp.int32, shape, axis)


def norm_parts(hidden):
    centre = hidden - jnp.mean(hidden, axis=-1, keepdims=True)
    inverse = lax.rsqrt(jnp.mean(centre * centre, axis=-1, keepdims=True) + EPSILON)
    return centre * inverse, inverse


def norm_backward(upstream, unit, inverse, gain_row):
    scaled = upstream * gain_row
    shifted = (
        scaled
        - jnp.mean(scaled, axis=-1, keepdims=True)
        - unit * jnp.mean(scaled * unit, axis=-1, keepdims=True)
    )
    gain_grad = jnp.sum(upstream * unit, axis=0, keepdims=True)
    return inverse * shifted, gain_grad, jnp.sum(upstream, axis=0, keepdims=True)


def sentence_order(me, len_ref):
    count = len_ref.shape[1]
    lengths = [len_ref[me, k] for k in range(count)]
    longest, best, start, running = jnp.int32(0), lengths[0], jnp.int32(0), jnp.int32(0)
    for k in range(1, count):
        running = running + lengths[k - 1]
        more = lengths[k] > best
        longest = jnp.where(more, k, longest)
        start = jnp.where(more, running, start)
        best = jnp.where(more, lengths[k], best)
    order = [longest] + [jnp.where(k < longest, k, k + 1) for k in range(count - 1)]
    bounds = [jnp.int32(0)]
    for k in range(1, count):
        bounds.append(bounds[-1] + len_ref[me, order[k]])
    return order, start, bounds


def moved_rows(index, start, half):
    return jnp.where(index < start, index + half, jnp.where(index < start + half, index - start, index))


def sort_matrix(rows, start):
    spot = moved_rows(iota((rows, rows), 1), start, rows // 2)
    return jnp.where(spot == iota((rows, rows), 0), 1.0, 0.0).astype(BF16)


def unsort_matrix(rows, start):
    spot = moved_rows(iota((rows, rows), 0), start, rows // 2)
    return jnp.where(spot == iota((rows, rows), 1), 1.0, 0.0).astype(BF16)


def side_masks(width):
    side = iota((1, width), 1) % SLAB
    first = jnp.where(side < SLAB // 2, 1.0, 0.0)
    return first.astype(BF16), (1.0 - first).astype(BF16)


def slab_of(pair, first=0):
    return pl.ds(pl.multiple_of(first + pair * SLAB, SLAB), SLAB)


def pack_heads(out_ref, rows, width):
    even, odd = side_masks(width)
    for t in range(out_ref.shape[0]):
        tile = rows(t * TILE, TILE)
        out_ref[t, :TILE, :] = tile * even
        out_ref[t, TILE:, :] = tile * odd


def fill_self_bias(bias_ref, bounds, half):
    for t in range(bias_ref.shape[0]):
        block, inner = t // (half // TILE), t % (half // TILE)
        key = iota((half, 2 * TILE), 0)
        query = iota((half, 2 * TILE), 1) % TILE + inner * TILE
        allowed = key <= query
        if block == 1:
            first = jnp.zeros((half, 2 * TILE), jnp.int32)
            for bound in bounds[1:-1]:
                first = jnp.where(query >= bound, bound, first)
            allowed = allowed & (key >= first)
        bias_ref[t] = jnp.where(allowed, 0.0, MASKED)


def self_keys(t, half):
    per = half // TILE
    return (t // per) * half, (t % per + 1) * TILE


def fill_live_bias(bias_ref, me, groups, parts, span, src_ref, sentences):
    key = iota((span, bias_ref.shape[2]), 0)
    for j, sentence in enumerate(sentences):
        for i, part in enumerate(parts):
            place = lax.rem(me - part + groups, groups) * span + key
            live = place < src_ref[me, sentence]
            bias_ref[j, pl.ds(i * span, span), :] = jnp.where(live, 0.0, MASKED)


def cross_units(bounds, half):
    units = [(t, 0, None) for t in range(half // TILE)]
    middle = half // 2
    last = jnp.int32(1)
    for bound in bounds[1:-1]:
        last = last + jnp.where(bound < middle, 1, 0)
    ends = bounds[1:]
    column = iota((1, 2 * TILE), 1) % TILE
    for u in range(len(ends) + 1):
        early = u < last
        sentence = jnp.where(early, u + 1, u)
        tile = jnp.where(early, 0, 1)
        low, high = jnp.int32(0), ends[0]
        for k in range(1, len(ends)):
            low = jnp.where(sentence == k + 1, ends[k - 1], low)
            high = jnp.where(sentence == k + 1, ends[k], high)
        row = column + tile * TILE
        units.append((tile + half // TILE, sentence, (row >= low) & (row < high)))
    return units


def own_sides(both):
    return jnp.concatenate([both[:SIDE, :TILE], both[SIDE:, TILE:]], axis=0)


def side_rows(row):
    even = jnp.broadcast_to(row[:, :TILE], (SIDE, TILE))
    return jnp.concatenate([even, jnp.broadcast_to(row[:, TILE:], (SIDE, TILE))], axis=0)


def tile_columns(tile):
    if isinstance(tile, int):
        return pl.ds(tile * TILE, TILE)
    return pl.ds(pl.multiple_of(tile * TILE, TILE), TILE)


def self_forward_kernel(
    groups,
    me_ref,
    len_ref,
    src_ref,
    target_ref,
    w_qkv_ref,
    w_out_ref,
    wq_ref,
    gain_ref,
    bias_row_ref,
    memory_ref,
    wkv_ref,
    sorted_ref,
    qkv_ref,
    norm_ref,
    attn_t_ref,
    hidden_ref,
    query_ref,
    part_ref,
    top_ref,
    sum_ref,
    pair_out_ref,
    bias_ref,
    live_ref,
    q_pack_ref,
    value_t_ref,
    cross_value_t_ref,
    pair_ref,
    copy_sem,
):
    rows, width = target_ref.shape
    half = rows // 2
    me = me_ref[0]
    order, start, bounds = sentence_order(me, len_ref)
    count, span = pair_ref.shape[0], pair_ref.shape[1]
    copies = []
    for j in range(count):
        block = memory_ref[me * count + order[j]]
        pair_ref[j] = dot(block, wkv_ref[...]).astype(BF16)
        copy = pltpu.make_async_copy(
            pair_ref.at[j], pair_out_ref.at[j, pl.ds(0, span), :], copy_sem.at[j]
        )
        copy.start()
        copies.append(copy)
    sorted_rows = dot(sort_matrix(rows, start), target_ref[...]).astype(BF16)
    sorted_ref[...] = sorted_rows
    fill_self_bias(bias_ref, bounds, half)
    queries = (dot(sorted_rows, w_qkv_ref[:, :width]).astype(BF16) * 0.125).astype(BF16)
    qkv_ref[:, :width] = queries
    pack_heads(q_pack_ref, lambda first, size: queries[first : first + size], width)
    qkv_ref[:, width : 2 * width] = dot(sorted_rows, w_qkv_ref[:, width : 2 * width]).astype(BF16)
    values = dot(sorted_rows, w_qkv_ref[:, 2 * width :]).astype(BF16)
    qkv_ref[:, 2 * width :] = values
    value_t_ref[...] = values.T
    tiles = rows // TILE

    def self_step(pair, carry):
        slab = slab_of(pair)
        for t in range(tiles):
            first, size = self_keys(t, half)
            keys = qkv_ref[pl.ds(first, size), slab_of(pair, width)]
            scores = dot_nt(keys, q_pack_ref[t, :, slab]) + bias_ref[t, :size, :]
            top = jnp.max(scores, axis=0, keepdims=True)
            weights = jnp.exp(scores - top)
            total = jnp.sum(weights, axis=0, keepdims=True)
            probs = (weights * (1.0 / total)).astype(BF16)
            both = dot(value_t_ref[slab, pl.ds(first, size)], probs)
            attn_t_ref[slab, tile_columns(t)] = own_sides(both).astype(BF16)
            norm_ref[pl.ds(pair * tiles + t, 1), :] = top + jnp.log(total)
        return carry

    lax.fori_loop(0, PAIRS, self_step, 0)
    hidden = sorted_rows.astype(F32) + dot(attn_t_ref[...].T, w_out_ref[...])
    hidden_ref[...] = hidden
    unit, _ = norm_parts(hidden)
    normed = (unit * gain_ref[0:1] + bias_row_ref[0:1]).astype(BF16)
    query_ref[...] = (dot(normed, wq_ref[...]).astype(BF16) * 0.125).astype(BF16)

    pack_heads(q_pack_ref, lambda first, size: query_ref[first : first + size, :], width)
    fill_live_bias(live_ref, me, groups, [0], span, src_ref, order)
    for j in range(count):
        cross_value_t_ref[j] = pair_ref[j, :, width:].T
    units = cross_units(bounds, half)

    def cross_step(pair, carry):
        slab = slab_of(pair)
        for tile, sentence, columns in units:
            scores = dot_nt(pair_ref[sentence, :, slab], q_pack_ref[tile, :, slab]) + live_ref[sentence]
            top = jnp.max(scores, axis=0, keepdims=True)
            weights = jnp.exp(scores - top)
            total = jnp.sum(weights, axis=0, keepdims=True)
            result = own_sides(dot(cross_value_t_ref[sentence, slab, :], weights.astype(BF16)))
            here = tile_columns(tile)
            row = pl.ds(pair * tiles + tile, 1)
            if columns is not None:
                result = jnp.where(columns[:, :TILE], result, part_ref[slab, here])
                top = jnp.where(columns, top, top_ref[row, :])
                total = jnp.where(columns, total, sum_ref[row, :])
            part_ref[slab, here] = result
            top_ref[row, :] = top
            sum_ref[row, :] = total
        return carry

    part_ref[...] = jnp.zeros_like(part_ref)
    top_ref[...] = jnp.zeros_like(top_ref)
    sum_ref[...] = jnp.ones_like(sum_ref)
    lax.fori_loop(0, PAIRS, cross_step, 0)
    for copy in copies:
        copy.wait()


def middle_kernel(
    groups,
    me_ref,
    len_ref,
    src_ref,
    hidden_one_ref,
    query_ref,
    part_ref,
    top_ref,
    sum_ref,
    wkv_ref,
    gain_ref,
    bias_row_ref,
    wo_hbm,
    w_up_hbm,
    w_down_hbm,
    grad_out_hbm,
    pair_in_hbm,
    *refs,
):
    came_refs = refs[: groups - 1]
    (
        out_ref,
        norm_ref,
        along_ref,
        keep_hbm,
        send_hbm,
        grad_hidden_ref,
        grad_attn_ref,
        ln_ref,
        pair_hbm,
        wo_ref,
        w_up_ref,
        w_down_ref,
        grad_out_ref,
        pair_ref,
        keep_ref,
        send_ref,
        live_ref,
        q_pack_ref,
        value_t_ref,
        attn_t_ref,
        active_ref,
        slope_ref,
        total_ref,
        load_sem,
        pair_sem,
        store_sem,
    ) = refs[groups - 1 :]
    rows, width = hidden_one_ref.shape
    half = rows // 2
    me = me_ref[0]
    count, away = pair_ref.shape[0], pair_ref.shape[1]
    span = away // (groups - 1)
    loads = [
        pltpu.make_async_copy(source, there, load_sem.at[i])
        for i, (source, there) in enumerate(
            [(wo_hbm, wo_ref), (w_up_hbm, w_up_ref), (w_down_hbm, w_down_ref), (grad_out_hbm, grad_out_ref)]
        )
    ]
    for copy in loads:
        copy.start()
    order, start, bounds = sentence_order(me, len_ref)
    fill_live_bias(live_ref, me, groups, list(range(1, groups)), span, src_ref, order)
    pack_heads(q_pack_ref, lambda first, size: query_ref[first : first + size, :], width)
    pair_copies = []
    for j in range(count):
        for part in range(1, groups):
            block = came_refs[part - 1][order[j]]
            pair_ref[j, pl.ds((part - 1) * span, span), :] = dot(block, wkv_ref[...]).astype(BF16)
        value_t_ref[j] = pair_ref[j, :, width:].T
        copy = pltpu.make_async_copy(pair_ref.at[j], pair_hbm.at[j, pl.ds(span, away), :], pair_sem.at[j])
        copy.start()
        pair_copies.append(copy)
    units = cross_units(bounds, half)
    tiles = rows // TILE

    def cross_step(pair, carry):
        slab = slab_of(pair)
        for tile, sentence, columns in units:
            here = tile_columns(tile)
            row = pl.ds(pair * tiles + tile, 1)
            scores = dot_nt(pair_ref[sentence, :, slab], q_pack_ref[tile, :, slab]) + live_ref[sentence]
            before = top_ref[row, :]
            top = jnp.maximum(jnp.max(scores, axis=0, keepdims=True), before)
            weights = jnp.exp(scores - top)
            scale = jnp.exp(before - top)
            total = jnp.sum(weights, axis=0, keepdims=True) + sum_ref[row, :] * scale
            result = own_sides(dot(value_t_ref[sentence, slab, :], weights.astype(BF16)))
            result = (result + part_ref[slab, here] * side_rows(scale)) * side_rows(1.0 / total)
            norm = top + jnp.log(total)
            if columns is not None:
                result = jnp.where(columns[:, :TILE], result, attn_t_ref[slab, here])
                norm = jnp.where(columns, norm, norm_ref[row, :])
            attn_t_ref[slab, here] = result
            norm_ref[row, :] = norm
        return carry

    attn_t_ref[...] = jnp.zeros_like(attn_t_ref)
    norm_ref[...] = jnp.zeros_like(norm_ref)
    lax.fori_loop(0, PAIRS, cross_step, 0)
    attn_t_low = attn_t_ref[...].astype(BF16)
    loads[0].wait()
    unit_one, _ = norm_parts(hidden_one_ref[...])
    normed_one = unit_one * gain_ref[0:1] + bias_row_ref[0:1]
    hidden_two = normed_one + dot(attn_t_low.T, wo_ref[...])
    unit_two, inverse_two = norm_parts(hidden_two)
    normed_two = unit_two * gain_ref[1:2] + bias_row_ref[1:2]
    normed_two_low = normed_two.astype(BF16)
    total_ref[...] = normed_two
    chunk = width
    chunks = w_down_ref.shape[0] // chunk
    loads[1].wait()
    loads[2].wait()

    def up_step(c, carry):
        cols = pl.ds(pl.multiple_of(c * chunk, chunk), chunk)
        upper = dot(normed_two_low, w_up_ref[:, cols])
        sigma = 1.0 / (1.0 + jnp.exp(-upper))
        active = (upper * sigma).astype(BF16)
        active_ref[:, cols] = active
        slope_ref[:, cols] = sigma * (1.0 + upper * (1.0 - sigma))
        total_ref[...] += dot(active, w_down_ref[cols, :])
        return carry

    lax.fori_loop(0, chunks, up_step, 0)
    unit_three, inverse_three = norm_parts(total_ref[...])
    result = (unit_three * gain_ref[2:3] + bias_row_ref[2:3]).astype(BF16)
    out_ref[...] = dot(unsort_matrix(rows, start), result).astype(BF16)
    loads[3].wait()
    upstream = dot(sort_matrix(rows, start), grad_out_ref[...])
    grad_three, gain_three, bias_three = norm_backward(upstream, unit_three, inverse_three, gain_ref[2:3])
    grad_down = grad_three.astype(BF16)
    total_ref[...] = grad_three
    normed_two_t = normed_two_low.T

    def down_step(c, carry):
        cols = pl.ds(pl.multiple_of(c * chunk, chunk), chunk)
        grad_upper = (dot_nt(grad_down, w_down_ref[cols, :]) * slope_ref[:, cols]).astype(BF16)
        down_part = dot_tn(active_ref[:, cols], grad_down).astype(BF16)
        up_part = dot(normed_two_t, grad_upper).astype(BF16)
        here = lax.rem(c, chunks // 2)
        down_rows = pl.ds(pl.multiple_of(here * chunk, chunk), chunk)
        up_rows = pl.ds(pl.multiple_of((chunks // 2 + here) * chunk, chunk), chunk)
        mine = c // (chunks // 2) == me_ref[1]

        @pl.when(mine)
        def _():
            keep_ref[down_rows, :] = down_part
            keep_ref[up_rows, :] = up_part

        @pl.when(jnp.logical_not(mine))
        def _():
            send_ref[down_rows, :] = down_part
            send_ref[up_rows, :] = up_part

        total_ref[...] += dot_nt(grad_upper, w_up_ref[:, cols])
        return carry

    lax.fori_loop(0, chunks, down_step, 0)
    most = chunks * chunk
    stores = [
        pltpu.make_async_copy(ref.at[pl.ds(first, size)], there.at[pl.ds(first, size)], store_sem.at[i])
        for i, (ref, there, first, size) in enumerate(
            [
                (send_ref, send_hbm, 0, most),
                (keep_ref, keep_hbm, 0, most),
                (send_ref, send_hbm, most, keep_ref.shape[0] - most),
                (keep_ref, keep_hbm, most, keep_ref.shape[0] - most),
            ]
        )
    ]
    stores[0].start()
    stores[1].start()
    grad_two, gain_two, bias_two = norm_backward(total_ref[...], unit_two, inverse_two, gain_ref[1:2])
    grad_two_low = grad_two.astype(BF16)
    wo_grad = dot(attn_t_low, grad_two_low).astype(BF16)
    core = me_ref[1]
    low, high = wo_grad[: width // 2], wo_grad[width // 2 :]
    tail = pl.ds(most, width // 2)
    keep_ref[tail, :] = jnp.where(core == 0, low, high)
    send_ref[tail, :] = jnp.where(core == 0, high, low)
    used = most + width // 2
    if keep_ref.shape[0] > used:
        keep_ref[used:, :] = jnp.zeros((keep_ref.shape[0] - used, width), BF16)
        send_ref[used:, :] = jnp.zeros((keep_ref.shape[0] - used, width), BF16)
    stores[2].start()
    stores[3].start()
    grad_hidden_ref[...] = grad_two
    grad_attn = dot_nt(grad_two_low, wo_ref[...]).astype(BF16)
    grad_attn_ref[...] = grad_attn
    product = grad_attn.T.astype(F32) * attn_t_ref[...]
    for pair in range(PAIRS):
        for side in range(2):
            first = pair * SLAB + side * SIDE
            along = jnp.sum(product[first : first + SIDE], axis=0, keepdims=True)
            for t in range(tiles):
                along_ref[pair * tiles + t : pair * tiles + t + 1, side * TILE : (side + 1) * TILE] = along[
                    :, t * TILE : (t + 1) * TILE
                ]
    ln_ref[...] = jnp.concatenate([gain_two, gain_three, bias_two, bias_three], axis=0)
    for copy in pair_copies + stores:
        copy.wait()


def cross_backward_kernel(
    groups,
    block,
    me_ref,
    len_ref,
    src_ref,
    query_ref,
    norm_ref,
    along_ref,
    grad_attn_ref,
    pair_hbm,
    pair_grad_ref,
    query_grad_t_ref,
    pair_ref,
    live_ref,
    q_pack_ref,
    g_pack_ref,
    key_t_ref,
    query_sum_ref,
    sum_ref,
    load_sem,
):
    rows, width = query_ref.shape
    half = rows // 2
    me = me_ref[0]
    sentences, places = pair_ref.shape[0], pair_ref.shape[1]
    first_sentence = 0 if block == 0 else 1
    load = pltpu.make_async_copy(pair_hbm.at[pl.ds(first_sentence, sentences)], pair_ref, load_sem.at[0])
    load.start()
    order, start, bounds = sentence_order(me, len_ref)
    mine = order[:1] if block == 0 else order[1:]
    fill_live_bias(live_ref, me, groups, list(range(groups)), places // groups, src_ref, mine)
    low = block * half
    pack_heads(q_pack_ref, lambda first, size: query_ref[low + first : low + first + size, :], width)
    pack_heads(g_pack_ref, lambda first, size: grad_attn_ref[low + first : low + first + size, :], width)
    tiles, per = rows // TILE, half // TILE
    units = cross_units(bounds, half)
    units = units[:per] if block == 0 else units[per:]
    load.wait()
    for j in range(sentences):
        key_t_ref[j] = pair_ref[j, :, :width].T

    def pair_step(pair, carry):
        slab, value_slab = slab_of(pair), slab_of(pair, width)
        query_sum_ref[...] = jnp.zeros_like(query_sum_ref)
        sum_ref[...] = jnp.zeros_like(sum_ref)
        for tile, sentence, columns in units:
            j = sentence - first_sentence
            t = tile - block * per
            here = tile_columns(t)
            row = pl.ds(pair * tiles + tile, 1)
            q_rows, g_rows = q_pack_ref[t, :, slab], g_pack_ref[t, :, slab]
            norm = norm_ref[row, :]
            if columns is not None:
                norm = jnp.where(columns, norm, -MASKED)
            scores = dot_nt(pair_ref[j, :, slab], q_rows) + live_ref[j]
            probs = jnp.exp(scores - norm)
            grad_probs = dot_nt(pair_ref[j, :, value_slab], g_rows)
            grad_scores = (probs * (grad_probs - along_ref[row, :])).astype(BF16)
            sum_ref[j, :, :SLAB] += dot(grad_scores, q_rows)
            sum_ref[j, :, SLAB:] += dot(probs.astype(BF16), g_rows)
            query_sum_ref[:, here] += own_sides(dot(key_t_ref[j, slab, :], grad_scores))
        query_grad_t_ref[slab, :] = (query_sum_ref[...] * 0.125).astype(BF16)
        pair_grad_ref[:, :, slab] = sum_ref[:, :, :SLAB].astype(BF16)
        pair_grad_ref[:, :, value_slab] = sum_ref[:, :, SLAB:].astype(BF16)
        return carry

    lax.fori_loop(0, PAIRS, pair_step, 0)


def memory_backward_kernel(
    groups, me_ref, len_ref, pair_grad_long_ref, pair_grad_rest_ref, wkv_ref, memory_ref, *refs
):
    came_refs = refs[: groups - 1]
    memory_grad_refs = refs[groups - 1 : 2 * groups - 1]
    wkv_grad_ref, total_ref = refs[2 * groups - 1 :]
    width = wkv_ref.shape[0]
    me = me_ref[0]
    count = len_ref.shape[1]
    span = pair_grad_long_ref.shape[1] // groups
    order, _, _ = sentence_order(me, len_ref)
    for part in reversed(range(groups)):
        for j in range(count):
            pair_grad_ref, here = (pair_grad_long_ref, 0) if j == 0 else (pair_grad_rest_ref, j - 1)
            grads = pair_grad_ref[here, pl.ds(part * span, span), :]
            memory_grad_refs[part][order[j]] = dot_nt(grads, wkv_ref[...]).astype(BF16)
            if part == 0:
                block = memory_ref[me * count + order[j]]
            else:
                block = came_refs[part - 1][order[j]]
            term = dot_tn(block, grads)
            if j == 0 and part == groups - 1:
                total_ref[...] = term
            else:
                total_ref[...] += term
    wkv_grad_ref[0] = total_ref[:, :width].astype(BF16)
    wkv_grad_ref[1] = total_ref[:, width:].astype(BF16)


def first_norm_backward_kernel(
    me_ref,
    hidden_one_ref,
    query_grad_t_long_ref,
    query_grad_t_rest_ref,
    grad_hidden_two_ref,
    wq_ref,
    w_out_ref,
    self_attn_t_ref,
    gain_ref,
    bias_row_ref,
    ln_in_ref,
    wkv_grad_ref,
    keep_ref,
    send_ref,
    grad_hidden_ref,
    grad_self_ref,
):
    width = wq_ref.shape[0]
    unit_one, inverse_one = norm_parts(hidden_one_ref[...])
    normed_one = (unit_one * gain_ref[0:1] + bias_row_ref[0:1]).astype(BF16)
    query_grad = jnp.concatenate([query_grad_t_long_ref[...].T, query_grad_t_rest_ref[...].T], axis=0)
    upstream = grad_hidden_two_ref[...] + dot_nt(query_grad, wq_ref[...])
    grad_one, gain_one, bias_one = norm_backward(upstream, unit_one, inverse_one, gain_ref[0:1])
    grad_hidden_ref[...] = grad_one
    grad_one_low = grad_one.astype(BF16)
    grad_self_ref[...] = dot_nt(grad_one_low, w_out_ref[...]).astype(BF16)
    wq_grad = dot_tn(normed_one, query_grad).astype(BF16)
    w_out_grad = dot(self_attn_t_ref[...], grad_one_low).astype(BF16)
    norms = jnp.concatenate(
        [gain_one, ln_in_ref[0:2], bias_one, ln_in_ref[2:4], jnp.zeros((LN_ROWS - 6, width), F32)], axis=0
    ).astype(BF16)

    def halves(low_ref, high_ref):
        low_ref[:width, :] = wq_grad
        low_ref[width : 2 * width, :] = wkv_grad_ref[0]
        high_ref[:width, :] = wkv_grad_ref[1]
        high_ref[width : 2 * width, :] = w_out_grad

    @pl.when(me_ref[1] == 0)
    def _():
        halves(keep_ref, send_ref)

    @pl.when(me_ref[1] != 0)
    def _():
        halves(send_ref, keep_ref)

    keep_ref[2 * width :, :] = norms
    send_ref[2 * width :, :] = norms


def self_backward_kernel(
    me_ref,
    len_ref,
    qkv_ref,
    norm_ref,
    grad_attn_ref,
    sorted_ref,
    grad_triple_ref,
    keep_ref,
    send_ref,
    bias_ref,
    q_pack_ref,
    g_pack_ref,
    key_t_ref,
    query_grad_t_ref,
):
    rows, width = sorted_ref.shape
    half = rows // 2
    _, _, bounds = sentence_order(me_ref[0], len_ref)
    fill_self_bias(bias_ref, bounds, half)
    pack_heads(q_pack_ref, lambda first, size: qkv_ref[first : first + size, :width], width)
    pack_heads(g_pack_ref, lambda first, size: grad_attn_ref[first : first + size, :], width)
    key_t_ref[...] = qkv_ref[:, width : 2 * width].T
    tiles, per = rows // TILE, half // TILE

    def pair_step(pair, carry):
        slab, key_slab, value_slab = slab_of(pair), slab_of(pair, width), slab_of(pair, 2 * width)
        sums = [[None, None] for _ in range(tiles)]
        for t in range(tiles):
            first, size = self_keys(t, half)
            span = pl.ds(first, size)
            q_rows, g_rows = q_pack_ref[t, :, slab], g_pack_ref[t, :, slab]
            scores = dot_nt(qkv_ref[span, key_slab], q_rows) + bias_ref[t, :size, :]
            probs = jnp.exp(scores - norm_ref[pl.ds(pair * tiles + t, 1), :])
            grad_probs = dot_nt(qkv_ref[span, value_slab], g_rows)
            along = jnp.sum(probs * grad_probs, axis=0, keepdims=True)
            grad_scores = (probs * (grad_probs - along)).astype(BF16)
            parts = dot(grad_scores, q_rows), dot(probs.astype(BF16), g_rows)
            for i in range(size // TILE):
                spot = sums[first // TILE + i]
                for k in range(2):
                    piece = parts[k][i * TILE : (i + 1) * TILE]
                    spot[k] = piece if spot[k] is None else spot[k] + piece
            query_grad_t_ref[slab, tile_columns(t)] = (
                own_sides(dot(key_t_ref[slab, span], grad_scores)) * 0.125
            ).astype(BF16)
        for t in range(tiles):
            grad_triple_ref[pl.ds(t * TILE, TILE), key_slab] = sums[t][0].astype(BF16)
            grad_triple_ref[pl.ds(t * TILE, TILE), value_slab] = sums[t][1].astype(BF16)
        return carry

    lax.fori_loop(0, PAIRS, pair_step, 0)
    grad_triple_ref[:, :width] = query_grad_t_ref[...].T
    sorted_t = sorted_ref[...].T
    grads = [
        dot(sorted_t, grad_triple_ref[:, part * width : (part + 1) * width]).astype(BF16)
        for part in range(3)
    ]
    short = width // 2

    def halves(low_ref, high_ref):
        low_ref[:width, :] = grads[0]
        low_ref[width:, :] = grads[1][:short]
        high_ref[:short, :] = grads[1][short:]
        high_ref[short:, :] = grads[2]

    @pl.when(me_ref[1] == 0)
    def _():
        halves(keep_ref, send_ref)

    @pl.when(me_ref[1] != 0)
    def _():
        halves(send_ref, keep_ref)


def target_kernel(me_ref, len_ref, grad_triple_ref, w_qkv_ref, grad_hidden_ref, grad_target_ref):
    rows = grad_hidden_ref.shape[0]
    _, start, _ = sentence_order(me_ref[0], len_ref)
    result = grad_hidden_ref[...] + dot_nt(grad_triple_ref[...], w_qkv_ref[...])
    grad_target_ref[...] = dot(unsort_matrix(rows, start), result.astype(BF16)).astype(BF16)


def tree_sum(terms):
    while len(terms) > 1:
        terms = [terms[i] + terms[i + 1] for i in range(0, len(terms), 2)]
    return terms[0]


def rows_of(ref, first, count):
    return ref[pl.ds(pl.multiple_of(first, 16), count), :].astype(F32)


def first_split_kernel(segments, ln, peers, spot_ref, *refs):
    ins, outs, sum_ref = refs[: 2 * segments], refs[2 * segments : -1], refs[-1]
    extra = LN_ROWS if ln else 0
    size = outs[0].shape[0] - extra
    used = 0
    for i in range(segments):
        keep_ref, came_ref = ins[2 * i], ins[2 * i + 1]
        count = keep_ref.shape[0] - (extra if i == 0 else 0)
        sum_ref[used : used + count, :] = (rows_of(keep_ref, 0, count) + rows_of(came_ref, 0, count)).astype(BF16)
        if i == 0 and ln:
            tail = (rows_of(keep_ref, count, LN_ROWS) + rows_of(came_ref, count, LN_ROWS)).astype(BF16)
        used += count
    if sum_ref.shape[0] > used:
        sum_ref[used:, :] = jnp.zeros((sum_ref.shape[0] - used, sum_ref.shape[1]), BF16)
    for d, out in enumerate(outs):
        out[:size, :] = sum_ref[pl.ds(pl.multiple_of((spot_ref[2] ^ d) * size, 16), size), :]
        if ln:
            out[size:, :] = tail


def second_split_kernel(ln, peers, spot_ref, *refs):
    ins, outs = refs[:peers], refs[peers:]
    extra = LN_ROWS if ln else 0
    size = outs[0].shape[0] - extra
    if ln:
        tail = tree_sum([rows_of(ref, size * len(outs), LN_ROWS) for ref in ins]).astype(BF16)
    for d, out in enumerate(outs):
        first = (spot_ref[3] ^ d) * size
        out[:size, :] = tree_sum([rows_of(ref, first, size) for ref in ins]).astype(BF16)
        if ln:
            out[size:, :] = tail


def total_kernel(ln, count, *refs):
    ins, outs = refs[:count], refs[count:]
    size = outs[0].shape[0]
    outs[0][...] = tree_sum([rows_of(ref, 0, size) for ref in ins]).astype(BF16)
    if ln:
        outs[1][...] = tree_sum([rows_of(ref, size, LN_ROWS) for ref in ins])


def join_kernel(spot_ref, *refs):
    out_ref = refs[-1]
    for d, ref in enumerate(refs[:-1]):
        size = ref.shape[0]
        out_ref[pl.ds(pl.multiple_of((spot_ref[3] ^ d) * size, 16), size), :] = ref[...]


def finish_kernel(peers, twisted, pieces, spot_ref, *refs):
    mine, others, outs, both_ref = refs[:peers], refs[peers : 2 * peers], refs[2 * peers : -1], refs[-1]
    core = spot_ref[1]
    for half, arrays, here in ((core, mine, spot_ref[2]), (1 - core, others, spot_ref[3 if twisted else 2])):
        for d, ref in enumerate(arrays):
            size = ref.shape[0]
            both_ref[half, pl.ds(pl.multiple_of((here ^ d) * size, 16), size), :] = ref[...]
    width = both_ref.shape[2]
    for half, first, rows, out, row, col in pieces:
        outs[out][row : row + rows, col : col + width] = both_ref[half, first : first + rows, :].astype(F32)


class Summing:
    def __init__(self, rows, width, ln):
        self.width, self.ln = width, ln
        self.dp, self.mem = lax.axis_size("dp"), lax.axis_size("mem")
        self.z_size = 4
        self.x_size = self.dp // (2 * self.z_size)
        self.xy_size = self.x_size * self.mem
        self.twisted = self.xy_size == self.z_size
        unit = 16 * self.xy_size * self.z_size
        self.rows = -(-rows // unit) * unit
        self.chunk = self.rows // (self.xy_size * self.z_size)

    def coords(self, dp, mem):
        return dp // (2 * self.x_size), (dp // 2 % self.x_size) * self.mem + mem, dp % 2

    def spot(self, me, dp):
        z, xy, core = self.coords(dp, me)
        first, second = xy, z
        if self.twisted:
            first, second = jnp.where(core == 0, xy, z), jnp.where(core == 0, z, xy)
        return jnp.stack([me, core, first, second]).astype(jnp.int32)

    def permute(self, array, stage, offset):
        pairs = []
        for dp in range(self.dp):
            for mem in range(self.mem):
                z, xy, core = self.coords(dp, mem)
                if stage == "core":
                    core ^= offset
                elif (stage == 0) != (self.twisted and core == 1):
                    xy ^= offset
                else:
                    z ^= offset
                to_dp = (z * self.x_size + xy // self.mem) * 2 + core
                pairs.append((dp * self.mem + mem, to_dp * self.mem + xy % self.mem))
        return lax.ppermute(array, ("dp", "mem"), pairs)

    def swap(self, arrays, stage):
        return [arrays[0]] + [self.permute(array, stage, d) for d, array in enumerate(arrays) if d > 0]

    def core_swap(self, send):
        return self.permute(send, "core", 1)

    def first_split(self, spot, *arrays):
        size = self.rows // self.xy_size + (LN_ROWS if self.ln else 0)
        outs = [((size, self.width), BF16)] * self.xy_size
        kernel = functools.partial(first_split_kernel, len(arrays) // 2, self.ln, self.xy_size)
        return call(kernel, outs, [((self.rows, self.width), BF16)], 1, spot, *arrays)

    def second_split(self, spot, arrays):
        outs = [((self.chunk + (LN_ROWS if self.ln else 0), self.width), BF16)] * self.z_size
        kernel = functools.partial(second_split_kernel, self.ln, self.xy_size)
        return call(kernel, outs, [], 1, spot, *arrays)

    def total(self, arrays):
        outs = [((self.chunk, self.width), BF16)]
        if self.ln:
            outs.append(((LN_ROWS, self.width), F32))
        return call(functools.partial(total_kernel, self.ln, self.z_size), outs, [], 0, *arrays)

    def spread(self, stage, array):
        size = self.xy_size if stage == 0 else self.z_size
        return [array] + [self.permute(array, stage, d) for d in range(1, size)]

    def join(self, spot, arrays):
        return call(join_kernel, [((self.rows // self.xy_size, self.width), BF16)], [], 1, spot, *arrays)[0]

    def finish(self, spot, mine, others, pieces, outs):
        kernel = functools.partial(finish_kernel, self.xy_size, self.twisted, pieces)
        scratch = [((2, self.rows, self.width), BF16)]
        return call(kernel, outs, scratch, 1, spot, *mine, *others, work=3)


def call(kernel, outs, scratch, scalars, *arrays, work=0.5, vmem=0, hbm_in=0, hbm_out=0, aliases=None):
    plain = len(arrays) - scalars - hbm_in
    if not vmem:
        blocks = [(array.shape, array.dtype) for array in arrays[scalars:]] + outs + scratch
        vmem = max(16, sum(math.prod(shape) * jnp.dtype(kind).itemsize for shape, kind in blocks) // MIB + 7)
    specs = [pl.BlockSpec(memory_space=pltpu.SMEM)] * scalars
    specs = specs + [pl.BlockSpec(memory_space=pltpu.VMEM)] * plain
    specs = specs + [pl.BlockSpec(memory_space=pl.ANY)] * hbm_in
    out_specs = [pl.BlockSpec(memory_space=pltpu.VMEM)] * (len(outs) - hbm_out)
    out_specs = out_specs + [pl.BlockSpec(memory_space=pl.ANY)] * hbm_out
    return pl.pallas_call(
        kernel,
        out_shape=[jax.ShapeDtypeStruct(shape, kind) for shape, kind in outs],
        in_specs=specs,
        out_specs=out_specs,
        scratch_shapes=[pltpu.VMEM(*entry) if isinstance(entry, tuple) else entry for entry in scratch],
        input_output_aliases=aliases or {},
        compiler_params=pltpu.CompilerParams(vmem_limit_bytes=vmem * MIB),
        cost_estimate=pl.CostEstimate(flops=int(work * 1e9), bytes_accessed=int(work * 3e6), transcendentals=0),
    )(*arrays)


def middle(
    groups, first_sum, stats, spot, tgt_len, src_len, hidden_one, query, part, part_top, part_sum, wkv_cross,
    ln_gain, ln_bias, wo_cross, w_up, w_down, grad_out, pair_mine, came,
):
    rows, width = hidden_one.shape
    half, tiles = rows // 2, rows // TILE
    hidden_width = w_down.shape[0]
    count, places, _ = pair_mine.shape
    away = places // groups * (groups - 1)
    arrays = [spot, tgt_len, src_len, hidden_one, query, part, part_top, part_sum, wkv_cross, ln_gain, ln_bias]
    stay = [wo_cross, w_up, w_down, grad_out, pair_mine]

    def kernel(*refs):
        ins, refs = refs[: len(arrays)], refs[len(arrays) :]
        came_refs, refs = refs[: len(came)], refs[len(came) :]
        stay_refs, refs = refs[: len(stay)], refs[len(stay) :]
        outs, refs = refs[:9], refs[9:]
        middle_kernel(groups, *ins, *stay_refs, *came_refs, *outs[:3], *outs[6:8], *outs[3:6], outs[8], *refs)

    result_out, cross_norm, cross_along, grad_hidden_two, grad_attn, ln_part, keep_one, send_one, pair_all = call(
        kernel,
        [
            ((rows, width), BF16),
            (stats, F32),
            (stats, F32),
            ((rows, width), F32),
            ((rows, width), BF16),
            ((4, width), F32),
            ((first_sum.rows, width), BF16),
            ((first_sum.rows, width), BF16),
            ((count, places, 2 * width), BF16),
        ],
        [
            ((width, width), BF16),
            ((width, hidden_width), BF16),
            ((hidden_width, width), BF16),
            ((rows, width), BF16),
            ((count, away, 2 * width), BF16),
            ((first_sum.rows, width), BF16),
            ((first_sum.rows, width), BF16),
            ((count, away, 2 * TILE), F32),
            ((tiles, 2 * TILE, width), BF16),
            ((count, width, away), BF16),
            ((width, rows), F32),
            ((rows, hidden_width), BF16),
            ((rows, hidden_width), F32),
            ((rows, width), F32),
            pltpu.SemaphoreType.DMA((4,)),
            pltpu.SemaphoreType.DMA((count,)),
            pltpu.SemaphoreType.DMA((4,)),
        ],
        3,
        *arrays,
        *came,
        *stay,
        vmem=60,
        hbm_in=len(stay),
        hbm_out=3,
        aliases={len(arrays) + len(came) + len(stay) - 1: 8},
    )
    return result_out, cross_norm, cross_along, keep_one, send_one, grad_hidden_two, grad_attn, ln_part, pair_all


def body(
    target,
    memory,
    grad_out,
    tgt_len,
    src_len,
    w_qkv,
    w_out,
    wq_cross,
    wkv_cross,
    wo_cross,
    w_up,
    w_down,
    ln_gain,
    ln_bias,
):
    rows, width = target.shape
    half = rows // 2
    tiles = rows // TILE
    hidden_width = w_down.shape[0]
    groups = lax.axis_size("mem")
    me = lax.axis_index("mem")
    count = tgt_len.shape[1]
    span = memory.shape[1]
    places, away = groups * span, (groups - 1) * span
    dp = lax.axis_index("dp")
    short = width // 2
    first_sum = Summing(hidden_width + short, width, False)
    second_sum = Summing(3 * width + short, width, True)
    spot = first_sum.spot(me, dp)
    stats = (PAIRS * tiles, 2 * TILE)

    came = []
    for shift in range(1, groups):
        pairs = [(i, (i + shift) % groups) for i in range(groups)]
        sent = lax.dynamic_slice_in_dim(memory, ((me + shift) % groups) * count, count, 0)
        came.append(lax.ppermute(sent, "mem", pairs))

    sorted_rows, qkv, self_norm, self_attn_t, hidden_one, query, part, part_top, part_sum, pair_mine = call(
        functools.partial(self_forward_kernel, groups),
        [
            ((rows, width), BF16),
            ((rows, 3 * width), BF16),
            (stats, F32),
            ((width, rows), BF16),
            ((rows, width), F32),
            ((rows, width), BF16),
            ((width, rows), F32),
            (stats, F32),
            (stats, F32),
            ((count, places, 2 * width), BF16),
        ],
        [
            ((tiles, half, 2 * TILE), F32),
            ((count, span, 2 * TILE), F32),
            ((tiles, 2 * TILE, width), BF16),
            ((width, rows), BF16),
            ((count, width, span), BF16),
            ((count, span, 2 * width), BF16),
            pltpu.SemaphoreType.DMA((count,)),
        ],
        3,
        spot,
        tgt_len,
        src_len,
        target,
        w_qkv,
        w_out,
        wq_cross,
        ln_gain,
        ln_bias,
        memory,
        wkv_cross,
        vmem=60,
        hbm_out=1,
    )
    result_out, cross_norm, cross_along, keep_one, send_one, grad_hidden_two, grad_attn, ln_part, pair_all = middle(
        groups, first_sum, stats, spot, tgt_len, src_len, hidden_one, query, part, part_top, part_sum, wkv_cross,
        ln_gain, ln_bias, wo_cross, w_up, w_down, grad_out, pair_mine, came,
    )
    came_one = first_sum.core_swap(send_one)

    def cross_backward(block):
        sentences = 1 if block == 0 else count - 1
        return call(
            functools.partial(cross_backward_kernel, groups, block),
            [((sentences, places, 2 * width), BF16), ((width, half), BF16)],
            [
                ((sentences, places, 2 * width), BF16),
                ((sentences, places, 2 * TILE), F32),
                ((half // TILE, 2 * TILE, width), BF16),
                ((half // TILE, 2 * TILE, width), BF16),
                ((sentences, width, places), BF16),
                ((SLAB, half), F32),
                ((sentences, places, 2 * SLAB), F32),
                pltpu.SemaphoreType.DMA((1,)),
            ],
            3,
            spot,
            tgt_len,
            src_len,
            query,
            cross_norm,
            cross_along,
            grad_attn,
            pair_all,
            work=10,
            vmem=60,
            hbm_in=1,
        )

    pair_grad_long, query_grad_t_long = cross_backward(0)
    came_one, pair_grad_long = lax.optimization_barrier((came_one, pair_grad_long))
    parts_one = first_sum.first_split(spot, keep_one, came_one)
    parts_one, pair_all = lax.optimization_barrier((parts_one, pair_all))
    parts_one = first_sum.swap(parts_one, 0)
    pair_grad_rest, query_grad_t_rest = cross_backward(1)
    *memory_grads, wkv_grad = call(
        functools.partial(memory_backward_kernel, groups),
        [((count, span, width), BF16)] * groups + [((2, width, width), BF16)],
        [((width, 2 * width), F32)],
        2,
        spot,
        tgt_len,
        pair_grad_long,
        pair_grad_rest,
        wkv_cross,
        memory,
        *came,
        work=1,
        vmem=60,
    )
    backs = []
    for shift in range(1, groups):
        pairs = [(i, (i - shift) % groups) for i in range(groups)]
        backs.append(lax.ppermute(memory_grads[shift], "mem", pairs))
    parts_one, wkv_grad = lax.optimization_barrier((parts_one, wkv_grad))
    parts_one = first_sum.second_split(spot, parts_one)
    parts_one, wkv_grad = lax.optimization_barrier((parts_one, wkv_grad))
    parts_one = first_sum.swap(parts_one, 1)
    keep_mid, send_mid, grad_hidden_one, grad_self = call(
        first_norm_backward_kernel,
        [
            ((2 * width + LN_ROWS, width), BF16),
            ((2 * width + LN_ROWS, width), BF16),
            ((rows, width), F32),
            ((rows, width), BF16),
        ],
        [],
        1,
        spot,
        hidden_one,
        query_grad_t_long,
        query_grad_t_rest,
        grad_hidden_two,
        wq_cross,
        w_out,
        self_attn_t,
        ln_gain,
        ln_bias,
        ln_part,
        wkv_grad,
        work=5,
        vmem=60,
    )
    parts_one, grad_self = lax.optimization_barrier((parts_one, grad_self))
    sum_one = first_sum.total(parts_one)[0]
    sum_one, grad_self, send_mid = lax.optimization_barrier((sum_one, grad_self, send_mid))
    spread_one = first_sum.spread(1, sum_one)
    came_mid = second_sum.core_swap(send_mid)
    grad_triple, keep_last, send_last = call(
        self_backward_kernel,
        [
            ((rows, 3 * width), BF16),
            ((width + short, width), BF16),
            ((width + short, width), BF16),
        ],
        [
            ((tiles, half, 2 * TILE), F32),
            ((tiles, 2 * TILE, width), BF16),
            ((tiles, 2 * TILE, width), BF16),
            ((width, rows), BF16),
            ((width, rows), BF16),
        ],
        2,
        spot,
        tgt_len,
        qkv,
        self_norm,
        grad_self,
        sorted_rows,
        work=8,
        vmem=60,
    )
    send_last, spread_one, came_mid = lax.optimization_barrier(
        (send_last, spread_one, came_mid)
    )
    came_last = second_sum.core_swap(send_last)
    spread_one = first_sum.spread(0, first_sum.join(spot, spread_one))
    (grad_target,) = call(
        target_kernel,
        [((rows, width), BF16)],
        [],
        2,
        spot,
        tgt_len,
        grad_triple,
        w_qkv,
        grad_hidden_one,
        work=4,
        vmem=60,
    )
    came_last, grad_target, backs = lax.optimization_barrier((came_last, grad_target, backs))
    parts_two = second_sum.first_split(spot, keep_mid, came_mid, keep_last, came_last)
    parts_two = second_sum.swap(parts_two, 0)
    other_one = [first_sum.core_swap(array) for array in spread_one]
    parts_two = second_sum.swap(second_sum.second_split(spot, parts_two), 1)
    sum_two, norm_sums = second_sum.total(parts_two)
    spread_two = second_sum.spread(0, second_sum.join(spot, second_sum.spread(1, sum_two)))
    chunks = hidden_width // width
    pieces = []
    for chunk in range(chunks):
        side, here = chunk // (chunks // 2), chunk % (chunks // 2)
        pieces.append((side, here * width, width, 0, chunk * width, 0))
        pieces.append((side, (chunks // 2 + here) * width, width, 1, 0, chunk * width))
    for side in range(2):
        pieces.append((side, chunks * width, short, 2, side * short, 0))
    grad_w_down, grad_w_up, grad_wo = first_sum.finish(
        spot,
        spread_one,
        other_one,
        pieces,
        [((hidden_width, width), F32), ((width, hidden_width), F32), ((width, width), F32)],
    )
    spread_two, grad_w_down = lax.optimization_barrier((spread_two, grad_w_down))
    other_two = [second_sum.core_swap(array) for array in spread_two]
    pieces = [
        (0, 0, width, 0, 0, 0),
        (0, width, width, 1, 0, 0),
        (0, 2 * width, width, 2, 0, 0),
        (0, 3 * width, short, 2, 0, width),
        (1, 0, width, 1, 0, width),
        (1, width, width, 3, 0, 0),
        (1, 2 * width, short, 2, short, width),
        (1, 2 * width + short, width, 2, 0, 2 * width),
    ]
    grad_wq, grad_wkv, grad_w_qkv, grad_w_out = second_sum.finish(
        spot,
        spread_two,
        other_two,
        pieces,
        [
            ((width, width), F32),
            ((width, 2 * width), F32),
            ((width, 3 * width), F32),
            ((width, width), F32),
        ],
    )
    grad_memory = jnp.zeros(memory.shape, BF16)
    grad_memory = lax.dynamic_update_slice_in_dim(grad_memory, memory_grads[0], me * count, 0)
    for shift in range(1, groups):
        grad_memory = lax.dynamic_update_slice_in_dim(
            grad_memory, backs[shift - 1], ((me + shift) % groups) * count, 0
        )
    return (
        result_out,
        grad_target,
        grad_memory,
        grad_w_qkv,
        grad_w_out,
        grad_wq,
        grad_wkv,
        grad_wo,
        grad_w_up,
        grad_w_down,
        norm_sums[:3],
        norm_sums[3:6],
    )


def solution(mesh):
    rows_spec = P(("dp", "mem"), None)
    memory_spec = P("dp", "mem", None)
    return jax.shard_map(
        body,
        mesh=mesh,
        in_specs=(rows_spec, memory_spec, rows_spec, P("dp", None), P("dp", None)) + (P(),) * 9,
        out_specs=(rows_spec, rows_spec, memory_spec) + (P(),) * 9,
        check_vma=False,
    )
```

```python
import functools
import math

import jax
import jax.numpy as jnp
from jax import lax
from jax.experimental import pallas as pl
from jax.experimental.pallas import tpu as pltpu
from jax.sharding import PartitionSpec as P

HEADS = 8
PAIRS = HEADS // 2
SLAB = 128
SIDE = SLAB // 2
TILE = 128
MASKED = -1e30
EPSILON = 1e-05
F32 = jnp.float32
BF16 = jnp.bfloat16
MIB = 1024 * 1024
LN_ROWS = 16
LAST_PARTS = 2


def dot(left, right):
    return jnp.dot(left, right, preferred_element_type=F32)


def dot_nt(left, right):
    return lax.dot_general(left, right, (((1,), (1,)), ((), ())), preferred_element_type=F32)


def dot_tn(left, right):
    return lax.dot_general(left, right, (((0,), (0,)), ((), ())), preferred_element_type=F32)


def iota(shape, axis):
    return lax.broadcasted_iota(jnp.int32, shape, axis)


def norm_parts(hidden):
    centre = hidden - jnp.mean(hidden, axis=-1, keepdims=True)
    inverse = lax.rsqrt(jnp.mean(centre * centre, axis=-1, keepdims=True) + EPSILON)
    return centre * inverse, inverse


def norm_backward(upstream, unit, inverse, gain_row):
    scaled = upstream * gain_row
    shifted = (
        scaled
        - jnp.mean(scaled, axis=-1, keepdims=True)
        - unit * jnp.mean(scaled * unit, axis=-1, keepdims=True)
    )
    gain_grad = jnp.sum(upstream * unit, axis=0, keepdims=True)
    return inverse * shifted, gain_grad, jnp.sum(upstream, axis=0, keepdims=True)


def sentence_order(me, len_ref):
    count = len_ref.shape[1]
    lengths = [len_ref[me, k] for k in range(count)]
    longest, best, start, running = jnp.int32(0), lengths[0], jnp.int32(0), jnp.int32(0)
    for k in range(1, count):
        running = running + lengths[k - 1]
        more = lengths[k] > best
        longest = jnp.where(more, k, longest)
        start = jnp.where(more, running, start)
        best = jnp.where(more, lengths[k], best)
    order = [longest] + [jnp.where(k < longest, k, k + 1) for k in range(count - 1)]
    bounds = [jnp.int32(0)]
    for k in range(1, count):
        bounds.append(bounds[-1] + len_ref[me, order[k]])
    return order, start, bounds


def moved_rows(index, start, half):
    return jnp.where(index < start, index + half, jnp.where(index < start + half, index - start, index))


def sort_matrix(rows, start):
    spot = moved_rows(iota((rows, rows), 1), start, rows // 2)
    return jnp.where(spot == iota((rows, rows), 0), 1.0, 0.0).astype(BF16)


def unsort_matrix(rows, start):
    spot = moved_rows(iota((rows, rows), 0), start, rows // 2)
    return jnp.where(spot == iota((rows, rows), 1), 1.0, 0.0).astype(BF16)


def side_masks(width):
    side = iota((1, width), 1) % SLAB
    first = jnp.where(side < SLAB // 2, 1.0, 0.0)
    return first.astype(BF16), (1.0 - first).astype(BF16)


def slab_of(pair, first=0):
    return pl.ds(pl.multiple_of(first + pair * SLAB, SLAB), SLAB)


def pack_heads(out_ref, rows, width):
    even, odd = side_masks(width)
    for t in range(out_ref.shape[0]):
        tile = rows(t * TILE, TILE)
        out_ref[t, :TILE, :] = tile * even
        out_ref[t, TILE:, :] = tile * odd


def fill_self_bias(bias_ref, bounds, half):
    for t in range(bias_ref.shape[0]):
        block, inner = t // (half // TILE), t % (half // TILE)
        key = iota((half, 2 * TILE), 0)
        query = iota((half, 2 * TILE), 1) % TILE + inner * TILE
        allowed = key <= query
        if block == 1:
            first = jnp.zeros((half, 2 * TILE), jnp.int32)
            for bound in bounds[1:-1]:
                first = jnp.where(query >= bound, bound, first)
            allowed = allowed & (key >= first)
        bias_ref[t] = jnp.where(allowed, 0.0, MASKED)


def self_keys(t, half):
    per = half // TILE
    return (t // per) * half, (t % per + 1) * TILE


def fill_live_bias(bias_ref, me, groups, parts, span, src_ref, sentences):
    key = iota((span, bias_ref.shape[2]), 0)
    for j, sentence in enumerate(sentences):
        for i, part in enumerate(parts):
            place = lax.rem(me - part + groups, groups) * span + key
            live = place < src_ref[me, sentence]
            bias_ref[j, pl.ds(i * span, span), :] = jnp.where(live, 0.0, MASKED)


def cross_units(bounds, half):
    units = [(t, 0, None) for t in range(half // TILE)]
    middle = half // 2
    last = jnp.int32(1)
    for bound in bounds[1:-1]:
        last = last + jnp.where(bound < middle, 1, 0)
    ends = bounds[1:]
    column = iota((1, 2 * TILE), 1) % TILE
    for u in range(len(ends) + 1):
        early = u < last
        sentence = jnp.where(early, u + 1, u)
        tile = jnp.where(early, 0, 1)
        low, high = jnp.int32(0), ends[0]
        for k in range(1, len(ends)):
            low = jnp.where(sentence == k + 1, ends[k - 1], low)
            high = jnp.where(sentence == k + 1, ends[k], high)
        row = column + tile * TILE
        units.append((tile + half // TILE, sentence, (row >= low) & (row < high)))
    return units


def own_sides(both):
    return jnp.concatenate([both[:SIDE, :TILE], both[SIDE:, TILE:]], axis=0)


def side_rows(row):
    even = jnp.broadcast_to(row[:, :TILE], (SIDE, TILE))
    return jnp.concatenate([even, jnp.broadcast_to(row[:, TILE:], (SIDE, TILE))], axis=0)


def tile_columns(tile):
    if isinstance(tile, int):
        return pl.ds(tile * TILE, TILE)
    return pl.ds(pl.multiple_of(tile * TILE, TILE), TILE)


def self_forward_kernel(
    groups,
    me_ref,
    len_ref,
    src_ref,
    target_ref,
    w_qkv_ref,
    w_out_ref,
    wq_ref,
    gain_ref,
    bias_row_ref,
    memory_ref,
    wkv_ref,
    sorted_ref,
    qkv_ref,
    norm_ref,
    attn_t_ref,
    hidden_ref,
    query_ref,
    part_ref,
    top_ref,
    sum_ref,
    pair_out_ref,
    bias_ref,
    live_ref,
    q_pack_ref,
    value_t_ref,
    cross_value_t_ref,
    pair_ref,
    copy_sem,
):
    rows, width = target_ref.shape
    half = rows // 2
    me = me_ref[0]
    order, start, bounds = sentence_order(me, len_ref)
    count, span = pair_ref.shape[0], pair_ref.shape[1]
    copies = []
    for j in range(count):
        block = memory_ref[me * count + order[j]]
        pair_ref[j] = dot(block, wkv_ref[...]).astype(BF16)
        copy = pltpu.make_async_copy(
            pair_ref.at[j], pair_out_ref.at[j, pl.ds(0, span), :], copy_sem.at[j]
        )
        copy.start()
        copies.append(copy)
    sorted_rows = dot(sort_matrix(rows, start), target_ref[...]).astype(BF16)
    sorted_ref[...] = sorted_rows
    fill_self_bias(bias_ref, bounds, half)
    queries = (dot(sorted_rows, w_qkv_ref[:, :width]).astype(BF16) * 0.125).astype(BF16)
    qkv_ref[:, :width] = queries
    pack_heads(q_pack_ref, lambda first, size: queries[first : first + size], width)
    qkv_ref[:, width : 2 * width] = dot(sorted_rows, w_qkv_ref[:, width : 2 * width]).astype(BF16)
    values = dot(sorted_rows, w_qkv_ref[:, 2 * width :]).astype(BF16)
    qkv_ref[:, 2 * width :] = values
    value_t_ref[...] = values.T
    tiles = rows // TILE

    def self_step(pair, carry):
        slab = slab_of(pair)
        for t in range(tiles):
            first, size = self_keys(t, half)
            keys = qkv_ref[pl.ds(first, size), slab_of(pair, width)]
            scores = dot_nt(keys, q_pack_ref[t, :, slab]) + bias_ref[t, :size, :]
            top = jnp.max(scores, axis=0, keepdims=True)
            weights = jnp.exp(scores - top)
            total = jnp.sum(weights, axis=0, keepdims=True)
            probs = (weights * (1.0 / total)).astype(BF16)
            both = dot(value_t_ref[slab, pl.ds(first, size)], probs)
            attn_t_ref[slab, tile_columns(t)] = own_sides(both).astype(BF16)
            norm_ref[pl.ds(pair * tiles + t, 1), :] = top + jnp.log(total)
        return carry

    lax.fori_loop(0, PAIRS, self_step, 0)
    hidden = sorted_rows.astype(F32) + dot(attn_t_ref[...].T, w_out_ref[...])
    hidden_ref[...] = hidden
    unit, _ = norm_parts(hidden)
    normed = (unit * gain_ref[0:1] + bias_row_ref[0:1]).astype(BF16)
    query_ref[...] = (dot(normed, wq_ref[...]).astype(BF16) * 0.125).astype(BF16)

    pack_heads(q_pack_ref, lambda first, size: query_ref[first : first + size, :], width)
    fill_live_bias(live_ref, me, groups, [0], span, src_ref, order)
    for j in range(count):
        cross_value_t_ref[j] = pair_ref[j, :, width:].T
    units = cross_units(bounds, half)

    def cross_step(pair, carry):
        slab = slab_of(pair)
        for tile, sentence, columns in units:
            scores = dot_nt(pair_ref[sentence, :, slab], q_pack_ref[tile, :, slab]) + live_ref[sentence]
            top = jnp.max(scores, axis=0, keepdims=True)
            weights = jnp.exp(scores - top)
            total = jnp.sum(weights, axis=0, keepdims=True)
            result = own_sides(dot(cross_value_t_ref[sentence, slab, :], weights.astype(BF16)))
            here = tile_columns(tile)
            row = pl.ds(pair * tiles + tile, 1)
            if columns is not None:
                result = jnp.where(columns[:, :TILE], result, part_ref[slab, here])
                top = jnp.where(columns, top, top_ref[row, :])
                total = jnp.where(columns, total, sum_ref[row, :])
            part_ref[slab, here] = result
            top_ref[row, :] = top
            sum_ref[row, :] = total
        return carry

    part_ref[...] = jnp.zeros_like(part_ref)
    top_ref[...] = jnp.zeros_like(top_ref)
    sum_ref[...] = jnp.ones_like(sum_ref)
    lax.fori_loop(0, PAIRS, cross_step, 0)
    for copy in copies:
        copy.wait()


def middle_kernel(
    groups,
    me_ref,
    len_ref,
    src_ref,
    hidden_one_ref,
    query_ref,
    part_ref,
    top_ref,
    sum_ref,
    wkv_ref,
    gain_ref,
    bias_row_ref,
    wo_hbm,
    w_up_hbm,
    w_down_hbm,
    grad_out_hbm,
    pair_in_hbm,
    *refs,
):
    came_refs = refs[: groups - 1]
    (
        out_ref,
        norm_ref,
        along_ref,
        keep_hbm,
        send_hbm,
        grad_hidden_ref,
        grad_attn_ref,
        ln_ref,
        pair_hbm,
        wo_ref,
        w_up_ref,
        w_down_ref,
        grad_out_ref,
        pair_ref,
        keep_ref,
        send_ref,
        live_ref,
        q_pack_ref,
        value_t_ref,
        attn_t_ref,
        active_ref,
        slope_ref,
        total_ref,
        load_sem,
        pair_sem,
        store_sem,
    ) = refs[groups - 1 :]
    rows, width = hidden_one_ref.shape
    half = rows // 2
    me = me_ref[0]
    count, away = pair_ref.shape[0], pair_ref.shape[1]
    span = away // (groups - 1)
    loads = [
        pltpu.make_async_copy(source, there, load_sem.at[i])
        for i, (source, there) in enumerate(
            [(wo_hbm, wo_ref), (w_up_hbm, w_up_ref), (w_down_hbm, w_down_ref), (grad_out_hbm, grad_out_ref)]
        )
    ]
    for copy in loads:
        copy.start()
    order, start, bounds = sentence_order(me, len_ref)
    fill_live_bias(live_ref, me, groups, list(range(1, groups)), span, src_ref, order)
    pack_heads(q_pack_ref, lambda first, size: query_ref[first : first + size, :], width)
    pair_copies = []
    for j in range(count):
        for part in range(1, groups):
            block = came_refs[part - 1][order[j]]
            pair_ref[j, pl.ds((part - 1) * span, span), :] = dot(block, wkv_ref[...]).astype(BF16)
        value_t_ref[j] = pair_ref[j, :, width:].T
        copy = pltpu.make_async_copy(pair_ref.at[j], pair_hbm.at[j, pl.ds(span, away), :], pair_sem.at[j])
        copy.start()
        pair_copies.append(copy)
    units = cross_units(bounds, half)
    tiles = rows // TILE

    def cross_step(pair, carry):
        slab = slab_of(pair)
        for tile, sentence, columns in units:
            here = tile_columns(tile)
            row = pl.ds(pair * tiles + tile, 1)
            scores = dot_nt(pair_ref[sentence, :, slab], q_pack_ref[tile, :, slab]) + live_ref[sentence]
            before = top_ref[row, :]
            top = jnp.maximum(jnp.max(scores, axis=0, keepdims=True), before)
            weights = jnp.exp(scores - top)
            scale = jnp.exp(before - top)
            total = jnp.sum(weights, axis=0, keepdims=True) + sum_ref[row, :] * scale
            result = own_sides(dot(value_t_ref[sentence, slab, :], weights.astype(BF16)))
            result = (result + part_ref[slab, here] * side_rows(scale)) * side_rows(1.0 / total)
            norm = top + jnp.log(total)
            if columns is not None:
                result = jnp.where(columns[:, :TILE], result, attn_t_ref[slab, here])
                norm = jnp.where(columns, norm, norm_ref[row, :])
            attn_t_ref[slab, here] = result
            norm_ref[row, :] = norm
        return carry

    attn_t_ref[...] = jnp.zeros_like(attn_t_ref)
    norm_ref[...] = jnp.zeros_like(norm_ref)
    lax.fori_loop(0, PAIRS, cross_step, 0)
    attn_t_low = attn_t_ref[...].astype(BF16)
    loads[0].wait()
    unit_one, _ = norm_parts(hidden_one_ref[...])
    normed_one = unit_one * gain_ref[0:1] + bias_row_ref[0:1]
    hidden_two = normed_one + dot(attn_t_low.T, wo_ref[...])
    unit_two, inverse_two = norm_parts(hidden_two)
    normed_two = unit_two * gain_ref[1:2] + bias_row_ref[1:2]
    normed_two_low = normed_two.astype(BF16)
    total_ref[...] = normed_two
    chunk = width
    chunks = w_down_ref.shape[0] // chunk
    loads[1].wait()
    loads[2].wait()

    def up_step(c, carry):
        cols = pl.ds(pl.multiple_of(c * chunk, chunk), chunk)
        upper = dot(normed_two_low, w_up_ref[:, cols])
        sigma = 1.0 / (1.0 + jnp.exp(-upper))
        active = (upper * sigma).astype(BF16)
        active_ref[:, cols] = active
        slope_ref[:, cols] = sigma * (1.0 + upper * (1.0 - sigma))
        total_ref[...] += dot(active, w_down_ref[cols, :])
        return carry

    lax.fori_loop(0, chunks, up_step, 0)
    unit_three, inverse_three = norm_parts(total_ref[...])
    result = (unit_three * gain_ref[2:3] + bias_row_ref[2:3]).astype(BF16)
    out_ref[...] = dot(unsort_matrix(rows, start), result).astype(BF16)
    loads[3].wait()
    upstream = dot(sort_matrix(rows, start), grad_out_ref[...])
    grad_three, gain_three, bias_three = norm_backward(upstream, unit_three, inverse_three, gain_ref[2:3])
    grad_down = grad_three.astype(BF16)
    total_ref[...] = grad_three
    normed_two_t = normed_two_low.T

    def down_step(c, carry):
        cols = pl.ds(pl.multiple_of(c * chunk, chunk), chunk)
        grad_upper = (dot_nt(grad_down, w_down_ref[cols, :]) * slope_ref[:, cols]).astype(BF16)
        down_part = dot_tn(active_ref[:, cols], grad_down).astype(BF16)
        up_part = dot(normed_two_t, grad_upper).astype(BF16)
        here = lax.rem(c, chunks // 2)
        down_rows = pl.ds(pl.multiple_of(here * chunk, chunk), chunk)
        up_rows = pl.ds(pl.multiple_of((chunks // 2 + here) * chunk, chunk), chunk)
        mine = c // (chunks // 2) == me_ref[1]

        @pl.when(mine)
        def _():
            keep_ref[down_rows, :] = down_part
            keep_ref[up_rows, :] = up_part

        @pl.when(jnp.logical_not(mine))
        def _():
            send_ref[down_rows, :] = down_part
            send_ref[up_rows, :] = up_part

        total_ref[...] += dot_nt(grad_upper, w_up_ref[:, cols])
        return carry

    lax.fori_loop(0, chunks, down_step, 0)
    most = chunks * chunk
    stores = [
        pltpu.make_async_copy(ref.at[pl.ds(first, size)], there.at[pl.ds(first, size)], store_sem.at[i])
        for i, (ref, there, first, size) in enumerate(
            [
                (send_ref, send_hbm, 0, most),
                (keep_ref, keep_hbm, 0, most),
                (send_ref, send_hbm, most, keep_ref.shape[0] - most),
                (keep_ref, keep_hbm, most, keep_ref.shape[0] - most),
            ]
        )
    ]
    stores[0].start()
    stores[1].start()
    grad_two, gain_two, bias_two = norm_backward(total_ref[...], unit_two, inverse_two, gain_ref[1:2])
    grad_two_low = grad_two.astype(BF16)
    wo_grad = dot(attn_t_low, grad_two_low).astype(BF16)
    core = me_ref[1]
    low, high = wo_grad[: width // 2], wo_grad[width // 2 :]
    tail = pl.ds(most, width // 2)
    keep_ref[tail, :] = jnp.where(core == 0, low, high)
    send_ref[tail, :] = jnp.where(core == 0, high, low)
    used = most + width // 2
    if keep_ref.shape[0] > used:
        keep_ref[used:, :] = jnp.zeros((keep_ref.shape[0] - used, width), BF16)
        send_ref[used:, :] = jnp.zeros((keep_ref.shape[0] - used, width), BF16)
    stores[2].start()
    stores[3].start()
    grad_hidden_ref[...] = grad_two
    grad_attn = dot_nt(grad_two_low, wo_ref[...]).astype(BF16)
    grad_attn_ref[...] = grad_attn
    product = grad_attn.T.astype(F32) * attn_t_ref[...]
    for pair in range(PAIRS):
        for side in range(2):
            first = pair * SLAB + side * SIDE
            along = jnp.sum(product[first : first + SIDE], axis=0, keepdims=True)
            for t in range(tiles):
                along_ref[pair * tiles + t : pair * tiles + t + 1, side * TILE : (side + 1) * TILE] = along[
                    :, t * TILE : (t + 1) * TILE
                ]
    ln_ref[...] = jnp.concatenate([gain_two, gain_three, bias_two, bias_three], axis=0)
    for copy in pair_copies + stores:
        copy.wait()


def cross_backward_kernel(
    groups,
    block,
    me_ref,
    len_ref,
    src_ref,
    query_ref,
    norm_ref,
    along_ref,
    grad_attn_ref,
    pair_hbm,
    pair_grad_ref,
    query_grad_t_ref,
    pair_ref,
    live_ref,
    q_pack_ref,
    g_pack_ref,
    key_t_ref,
    query_sum_ref,
    sum_ref,
    load_sem,
):
    rows, width = query_ref.shape
    half = rows // 2
    me = me_ref[0]
    sentences, places = pair_ref.shape[0], pair_ref.shape[1]
    first_sentence = 0 if block == 0 else 1
    load = pltpu.make_async_copy(pair_hbm.at[pl.ds(first_sentence, sentences)], pair_ref, load_sem.at[0])
    load.start()
    order, start, bounds = sentence_order(me, len_ref)
    mine = order[:1] if block == 0 else order[1:]
    fill_live_bias(live_ref, me, groups, list(range(groups)), places // groups, src_ref, mine)
    low = block * half
    pack_heads(q_pack_ref, lambda first, size: query_ref[low + first : low + first + size, :], width)
    pack_heads(g_pack_ref, lambda first, size: grad_attn_ref[low + first : low + first + size, :], width)
    tiles, per = rows // TILE, half // TILE
    units = cross_units(bounds, half)
    units = units[:per] if block == 0 else units[per:]
    load.wait()
    for j in range(sentences):
        key_t_ref[j] = pair_ref[j, :, :width].T

    def pair_step(pair, carry):
        slab, value_slab = slab_of(pair), slab_of(pair, width)
        query_sum_ref[...] = jnp.zeros_like(query_sum_ref)
        sum_ref[...] = jnp.zeros_like(sum_ref)
        for tile, sentence, columns in units:
            j = sentence - first_sentence
            t = tile - block * per
            here = tile_columns(t)
            row = pl.ds(pair * tiles + tile, 1)
            q_rows, g_rows = q_pack_ref[t, :, slab], g_pack_ref[t, :, slab]
            norm = norm_ref[row, :]
            if columns is not None:
                norm = jnp.where(columns, norm, -MASKED)
            scores = dot_nt(pair_ref[j, :, slab], q_rows) + live_ref[j]
            probs = jnp.exp(scores - norm)
            grad_probs = dot_nt(pair_ref[j, :, value_slab], g_rows)
            grad_scores = (probs * (grad_probs - along_ref[row, :])).astype(BF16)
            sum_ref[j, :, :SLAB] += dot(grad_scores, q_rows)
            sum_ref[j, :, SLAB:] += dot(probs.astype(BF16), g_rows)
            query_sum_ref[:, here] += own_sides(dot(key_t_ref[j, slab, :], grad_scores))
        query_grad_t_ref[slab, :] = (query_sum_ref[...] * 0.125).astype(BF16)
        pair_grad_ref[:, :, slab] = sum_ref[:, :, :SLAB].astype(BF16)
        pair_grad_ref[:, :, value_slab] = sum_ref[:, :, SLAB:].astype(BF16)
        return carry

    lax.fori_loop(0, PAIRS, pair_step, 0)


def memory_weight_kernel(groups, me_ref, len_ref, pair_grad_long_ref, pair_grad_rest_ref, memory_ref, *refs):
    came_refs = refs[: groups - 1]
    wkv_grad_ref, total_ref = refs[groups - 1 :]
    width = memory_ref.shape[2]
    me = me_ref[0]
    count = len_ref.shape[1]
    span = pair_grad_long_ref.shape[1] // groups
    order, _, _ = sentence_order(me, len_ref)
    for j in range(count):
        pair_grad_ref, here = (pair_grad_long_ref, 0) if j == 0 else (pair_grad_rest_ref, j - 1)
        blocks = [memory_ref[me * count + order[j]]] + [ref[order[j]] for ref in came_refs]
        term = dot_tn(jnp.concatenate(blocks, axis=0), pair_grad_ref[here])
        if j == 0:
            total_ref[...] = term
        else:
            total_ref[...] += term
    wkv_grad_ref[0] = total_ref[:, :width].astype(BF16)
    wkv_grad_ref[1] = total_ref[:, width:].astype(BF16)


def memory_grad_kernel(
    groups, me_ref, len_ref, pair_grad_long_ref, pair_grad_rest_ref, wkv_ref, mine_ref, *away_refs
):
    count = len_ref.shape[1]
    span = pair_grad_long_ref.shape[1] // groups
    order, _, _ = sentence_order(me_ref[0], len_ref)
    for j in range(count):
        pair_grad_ref, here = (pair_grad_long_ref, 0) if j == 0 else (pair_grad_rest_ref, j - 1)
        grads = dot_nt(pair_grad_ref[here], wkv_ref[...]).astype(BF16)
        mine_ref[order[j]] = grads[:span]
        for i in range(2 * (groups - 1)):
            first = span + i * (span // 2)
            away_refs[i][order[j]] = grads[first : first + span // 2]


def first_norm_backward_kernel(
    me_ref,
    hidden_one_ref,
    query_grad_t_long_ref,
    query_grad_t_rest_ref,
    grad_hidden_two_ref,
    wq_ref,
    w_out_ref,
    self_attn_t_ref,
    gain_ref,
    bias_row_ref,
    ln_in_ref,
    wkv_grad_ref,
    keep_ref,
    send_ref,
    grad_hidden_ref,
    grad_self_ref,
):
    width = wq_ref.shape[0]
    unit_one, inverse_one = norm_parts(hidden_one_ref[...])
    normed_one = (unit_one * gain_ref[0:1] + bias_row_ref[0:1]).astype(BF16)
    query_grad = jnp.concatenate([query_grad_t_long_ref[...].T, query_grad_t_rest_ref[...].T], axis=0)
    upstream = grad_hidden_two_ref[...] + dot_nt(query_grad, wq_ref[...])
    grad_one, gain_one, bias_one = norm_backward(upstream, unit_one, inverse_one, gain_ref[0:1])
    grad_hidden_ref[...] = grad_one
    grad_one_low = grad_one.astype(BF16)
    grad_self_ref[...] = dot_nt(grad_one_low, w_out_ref[...]).astype(BF16)
    wq_grad = dot_tn(normed_one, query_grad).astype(BF16)
    w_out_grad = dot(self_attn_t_ref[...], grad_one_low).astype(BF16)
    norms = jnp.concatenate(
        [gain_one, ln_in_ref[0:2], bias_one, ln_in_ref[2:4], jnp.zeros((LN_ROWS - 6, width), F32)], axis=0
    ).astype(BF16)

    def halves(low_ref, high_ref):
        low_ref[:width, :] = wq_grad
        low_ref[width : 2 * width, :] = wkv_grad_ref[0]
        high_ref[:width, :] = wkv_grad_ref[1]
        high_ref[width : 2 * width, :] = w_out_grad

    @pl.when(me_ref[1] == 0)
    def _():
        halves(keep_ref, send_ref)

    @pl.when(me_ref[1] != 0)
    def _():
        halves(send_ref, keep_ref)

    keep_ref[2 * width :, :] = norms
    send_ref[2 * width :, :] = norms


def self_backward_kernel(
    me_ref,
    len_ref,
    qkv_ref,
    norm_ref,
    grad_attn_ref,
    sorted_ref,
    grad_triple_ref,
    *refs,
):
    keep_refs, send_refs = refs[:LAST_PARTS], refs[LAST_PARTS : 2 * LAST_PARTS]
    self_backward(
        me_ref,
        len_ref,
        qkv_ref,
        norm_ref,
        grad_attn_ref,
        sorted_ref,
        grad_triple_ref,
        keep_refs,
        send_refs,
        *refs[2 * LAST_PARTS :],
    )


def self_backward(
    me_ref,
    len_ref,
    qkv_ref,
    norm_ref,
    grad_attn_ref,
    sorted_ref,
    grad_triple_ref,
    keep_refs,
    send_refs,
    bias_ref,
    q_pack_ref,
    g_pack_ref,
    key_t_ref,
    query_grad_t_ref,
):
    rows, width = sorted_ref.shape
    half = rows // 2
    _, _, bounds = sentence_order(me_ref[0], len_ref)
    fill_self_bias(bias_ref, bounds, half)
    pack_heads(q_pack_ref, lambda first, size: qkv_ref[first : first + size, :width], width)
    pack_heads(g_pack_ref, lambda first, size: grad_attn_ref[first : first + size, :], width)
    key_t_ref[...] = qkv_ref[:, width : 2 * width].T
    tiles, per = rows // TILE, half // TILE

    def pair_step(pair, carry):
        slab, key_slab, value_slab = slab_of(pair), slab_of(pair, width), slab_of(pair, 2 * width)
        sums = [[None, None] for _ in range(tiles)]
        for t in range(tiles):
            first, size = self_keys(t, half)
            span = pl.ds(first, size)
            q_rows, g_rows = q_pack_ref[t, :, slab], g_pack_ref[t, :, slab]
            scores = dot_nt(qkv_ref[span, key_slab], q_rows) + bias_ref[t, :size, :]
            probs = jnp.exp(scores - norm_ref[pl.ds(pair * tiles + t, 1), :])
            grad_probs = dot_nt(qkv_ref[span, value_slab], g_rows)
            along = jnp.sum(probs * grad_probs, axis=0, keepdims=True)
            grad_scores = (probs * (grad_probs - along)).astype(BF16)
            parts = dot(grad_scores, q_rows), dot(probs.astype(BF16), g_rows)
            for i in range(size // TILE):
                spot = sums[first // TILE + i]
                for k in range(2):
                    piece = parts[k][i * TILE : (i + 1) * TILE]
                    spot[k] = piece if spot[k] is None else spot[k] + piece
            query_grad_t_ref[slab, tile_columns(t)] = (
                own_sides(dot(key_t_ref[slab, span], grad_scores)) * 0.125
            ).astype(BF16)
        for t in range(tiles):
            grad_triple_ref[pl.ds(t * TILE, TILE), key_slab] = sums[t][0].astype(BF16)
            grad_triple_ref[pl.ds(t * TILE, TILE), value_slab] = sums[t][1].astype(BF16)
        return carry

    lax.fori_loop(0, PAIRS, pair_step, 0)
    grad_triple_ref[:, :width] = query_grad_t_ref[...].T
    sorted_t = sorted_ref[...].T
    grads = [
        dot(sorted_t, grad_triple_ref[:, part * width : (part + 1) * width]).astype(BF16)
        for part in range(3)
    ]
    short = width // 2

    low = jnp.concatenate([grads[0], grads[1][:short]], axis=0)
    high = jnp.concatenate([grads[1][short:], grads[2]], axis=0)
    size = keep_refs[0].shape[0]

    def halves(low_refs, high_refs):
        for i in range(LAST_PARTS):
            low_refs[i][...] = low[i * size : (i + 1) * size]
            high_refs[i][...] = high[i * size : (i + 1) * size]

    @pl.when(me_ref[1] == 0)
    def _():
        halves(keep_refs, send_refs)

    @pl.when(me_ref[1] != 0)
    def _():
        halves(send_refs, keep_refs)


def target_kernel(me_ref, len_ref, grad_triple_ref, w_qkv_ref, grad_hidden_ref, grad_target_ref):
    rows = grad_hidden_ref.shape[0]
    _, start, _ = sentence_order(me_ref[0], len_ref)
    result = grad_hidden_ref[...] + dot_nt(grad_triple_ref[...], w_qkv_ref[...])
    grad_target_ref[...] = dot(unsort_matrix(rows, start), result.astype(BF16)).astype(BF16)


def tree_sum(terms):
    while len(terms) > 1:
        terms = [terms[i] + terms[i + 1] for i in range(0, len(terms), 2)]
    return terms[0]


def rows_of(ref, first, count):
    return ref[pl.ds(pl.multiple_of(first, 16), count), :].astype(F32)


def first_split_kernel(segments, ln, peers, spot_ref, *refs):
    ins, outs, sum_ref = refs[: 2 * segments], refs[2 * segments : -1], refs[-1]
    extra = LN_ROWS if ln else 0
    size = outs[0].shape[0] - extra
    used = 0
    for i in range(segments):
        keep_ref, came_ref = ins[2 * i], ins[2 * i + 1]
        count = keep_ref.shape[0] - (extra if i == 0 else 0)
        sum_ref[used : used + count, :] = (rows_of(keep_ref, 0, count) + rows_of(came_ref, 0, count)).astype(BF16)
        if i == 0 and ln:
            tail = (rows_of(keep_ref, count, LN_ROWS) + rows_of(came_ref, count, LN_ROWS)).astype(BF16)
        used += count
    if sum_ref.shape[0] > used:
        sum_ref[used:, :] = jnp.zeros((sum_ref.shape[0] - used, sum_ref.shape[1]), BF16)
    for d, out in enumerate(outs):
        out[:size, :] = sum_ref[pl.ds(pl.multiple_of((spot_ref[2] ^ d) * size, 16), size), :]
        if ln:
            out[size:, :] = tail


def second_split_kernel(ln, peers, spot_ref, *refs):
    ins, outs = refs[:peers], refs[peers:]
    extra = LN_ROWS if ln else 0
    size = outs[0].shape[0] - extra
    if ln:
        tail = tree_sum([rows_of(ref, size * len(outs), LN_ROWS) for ref in ins]).astype(BF16)
    for d, out in enumerate(outs):
        first = (spot_ref[3] ^ d) * size
        out[:size, :] = tree_sum([rows_of(ref, first, size) for ref in ins]).astype(BF16)
        if ln:
            out[size:, :] = tail


def total_kernel(ln, count, *refs):
    ins, outs = refs[:count], refs[count:]
    size = outs[0].shape[0]
    outs[0][...] = tree_sum([rows_of(ref, 0, size) for ref in ins]).astype(BF16)
    if ln:
        outs[1][...] = tree_sum([rows_of(ref, size, LN_ROWS) for ref in ins])


def join_kernel(spot_ref, *refs):
    out_ref = refs[-1]
    for d, ref in enumerate(refs[:-1]):
        size = ref.shape[0]
        out_ref[pl.ds(pl.multiple_of((spot_ref[3] ^ d) * size, 16), size), :] = ref[...]


def finish_kernel(peers, twisted, pieces, spot_ref, *refs):
    mine, others, outs, both_ref = refs[:peers], refs[peers : 2 * peers], refs[2 * peers : -1], refs[-1]
    core = spot_ref[1]
    for half, arrays, here in ((core, mine, spot_ref[2]), (1 - core, others, spot_ref[3 if twisted else 2])):
        for d, ref in enumerate(arrays):
            size = ref.shape[0]
            both_ref[half, pl.ds(pl.multiple_of((here ^ d) * size, 16), size), :] = ref[...]
    width = both_ref.shape[2]
    for half, first, rows, out, row, col in pieces:
        outs[out][row : row + rows, col : col + width] = both_ref[half, first : first + rows, :].astype(F32)


class Summing:
    def __init__(self, rows, width, ln):
        self.width, self.ln = width, ln
        self.dp, self.mem = lax.axis_size("dp"), lax.axis_size("mem")
        self.z_size = 4
        self.x_size = self.dp // (2 * self.z_size)
        self.xy_size = self.x_size * self.mem
        self.twisted = self.xy_size == self.z_size
        unit = 16 * self.xy_size * self.z_size
        self.rows = -(-rows // unit) * unit
        self.chunk = self.rows // (self.xy_size * self.z_size)

    def coords(self, dp, mem):
        return dp // (2 * self.x_size), (dp // 2 % self.x_size) * self.mem + mem, dp % 2

    def spot(self, me, dp):
        z, xy, core = self.coords(dp, me)
        first, second = xy, z
        if self.twisted:
            first, second = jnp.where(core == 0, xy, z), jnp.where(core == 0, z, xy)
        return jnp.stack([me, core, first, second]).astype(jnp.int32)

    def permute(self, array, stage, offset):
        pairs = []
        for dp in range(self.dp):
            for mem in range(self.mem):
                z, xy, core = self.coords(dp, mem)
                if stage == "core":
                    core ^= offset
                elif (stage == 0) != (self.twisted and core == 1):
                    xy ^= offset
                else:
                    z ^= offset
                to_dp = (z * self.x_size + xy // self.mem) * 2 + core
                pairs.append((dp * self.mem + mem, to_dp * self.mem + xy % self.mem))
        return lax.ppermute(array, ("dp", "mem"), pairs)

    def swap(self, arrays, stage):
        return [arrays[0]] + [self.permute(array, stage, d) for d, array in enumerate(arrays) if d > 0]

    def core_swap(self, send):
        return self.permute(send, "core", 1)

    def first_split(self, spot, *arrays):
        size = self.rows // self.xy_size + (LN_ROWS if self.ln else 0)
        outs = [((size, self.width), BF16)] * self.xy_size
        kernel = functools.partial(first_split_kernel, len(arrays) // 2, self.ln, self.xy_size)
        return call(kernel, outs, [((self.rows, self.width), BF16)], 1, spot, *arrays)

    def second_split(self, spot, arrays):
        outs = [((self.chunk + (LN_ROWS if self.ln else 0), self.width), BF16)] * self.z_size
        kernel = functools.partial(second_split_kernel, self.ln, self.xy_size)
        return call(kernel, outs, [], 1, spot, *arrays)

    def total(self, arrays):
        outs = [((self.chunk, self.width), BF16)]
        if self.ln:
            outs.append(((LN_ROWS, self.width), F32))
        return call(functools.partial(total_kernel, self.ln, self.z_size), outs, [], 0, *arrays)

    def spread(self, stage, array):
        size = self.xy_size if stage == 0 else self.z_size
        return [array] + [self.permute(array, stage, d) for d in range(1, size)]

    def join(self, spot, arrays):
        return call(join_kernel, [((self.rows // self.xy_size, self.width), BF16)], [], 1, spot, *arrays)[0]

    def finish(self, spot, mine, others, pieces, outs):
        kernel = functools.partial(finish_kernel, self.xy_size, self.twisted, pieces)
        scratch = [((2, self.rows, self.width), BF16)]
        return call(kernel, outs, scratch, 1, spot, *mine, *others, work=3)


def call(kernel, outs, scratch, scalars, *arrays, work=0.5, vmem=0, hbm_in=0, hbm_out=0, aliases=None):
    plain = len(arrays) - scalars - hbm_in
    if not vmem:
        blocks = [(array.shape, array.dtype) for array in arrays[scalars:]] + outs + scratch
        vmem = max(16, sum(math.prod(shape) * jnp.dtype(kind).itemsize for shape, kind in blocks) // MIB + 7)
    specs = [pl.BlockSpec(memory_space=pltpu.SMEM)] * scalars
    specs = specs + [pl.BlockSpec(memory_space=pltpu.VMEM)] * plain
    specs = specs + [pl.BlockSpec(memory_space=pl.ANY)] * hbm_in
    out_specs = [pl.BlockSpec(memory_space=pltpu.VMEM)] * (len(outs) - hbm_out)
    out_specs = out_specs + [pl.BlockSpec(memory_space=pl.ANY)] * hbm_out
    return pl.pallas_call(
        kernel,
        out_shape=[jax.ShapeDtypeStruct(shape, kind) for shape, kind in outs],
        in_specs=specs,
        out_specs=out_specs,
        scratch_shapes=[pltpu.VMEM(*entry) if isinstance(entry, tuple) else entry for entry in scratch],
        input_output_aliases=aliases or {},
        compiler_params=pltpu.CompilerParams(vmem_limit_bytes=vmem * MIB),
        cost_estimate=pl.CostEstimate(flops=int(work * 1e9), bytes_accessed=int(work * 3e6), transcendentals=0),
    )(*arrays)


def middle(
    groups, first_sum, stats, spot, tgt_len, src_len, hidden_one, query, part, part_top, part_sum, wkv_cross,
    ln_gain, ln_bias, wo_cross, w_up, w_down, grad_out, pair_mine, came,
):
    rows, width = hidden_one.shape
    half, tiles = rows // 2, rows // TILE
    hidden_width = w_down.shape[0]
    count, places, _ = pair_mine.shape
    away = places // groups * (groups - 1)
    arrays = [spot, tgt_len, src_len, hidden_one, query, part, part_top, part_sum, wkv_cross, ln_gain, ln_bias]
    stay = [wo_cross, w_up, w_down, grad_out, pair_mine]

    def kernel(*refs):
        ins, refs = refs[: len(arrays)], refs[len(arrays) :]
        came_refs, refs = refs[: len(came)], refs[len(came) :]
        stay_refs, refs = refs[: len(stay)], refs[len(stay) :]
        outs, refs = refs[:9], refs[9:]
        middle_kernel(groups, *ins, *stay_refs, *came_refs, *outs[:3], *outs[6:8], *outs[3:6], outs[8], *refs)

    result_out, cross_norm, cross_along, grad_hidden_two, grad_attn, ln_part, keep_one, send_one, pair_all = call(
        kernel,
        [
            ((rows, width), BF16),
            (stats, F32),
            (stats, F32),
            ((rows, width), F32),
            ((rows, width), BF16),
            ((4, width), F32),
            ((first_sum.rows, width), BF16),
            ((first_sum.rows, width), BF16),
            ((count, places, 2 * width), BF16),
        ],
        [
            ((width, width), BF16),
            ((width, hidden_width), BF16),
            ((hidden_width, width), BF16),
            ((rows, width), BF16),
            ((count, away, 2 * width), BF16),
            ((first_sum.rows, width), BF16),
            ((first_sum.rows, width), BF16),
            ((count, away, 2 * TILE), F32),
            ((tiles, 2 * TILE, width), BF16),
            ((count, width, away), BF16),
            ((width, rows), F32),
            ((rows, hidden_width), BF16),
            ((rows, hidden_width), F32),
            ((rows, width), F32),
            pltpu.SemaphoreType.DMA((4,)),
            pltpu.SemaphoreType.DMA((count,)),
            pltpu.SemaphoreType.DMA((4,)),
        ],
        3,
        *arrays,
        *came,
        *stay,
        vmem=60,
        hbm_in=len(stay),
        hbm_out=3,
        aliases={len(arrays) + len(came) + len(stay) - 1: 8},
    )
    return result_out, cross_norm, cross_along, keep_one, send_one, grad_hidden_two, grad_attn, ln_part, pair_all


def body(
    target,
    memory,
    grad_out,
    tgt_len,
    src_len,
    w_qkv,
    w_out,
    wq_cross,
    wkv_cross,
    wo_cross,
    w_up,
    w_down,
    ln_gain,
    ln_bias,
):
    rows, width = target.shape
    half = rows // 2
    tiles = rows // TILE
    hidden_width = w_down.shape[0]
    groups = lax.axis_size("mem")
    me = lax.axis_index("mem")
    count = tgt_len.shape[1]
    span = memory.shape[1]
    places, away = groups * span, (groups - 1) * span
    dp = lax.axis_index("dp")
    short = width // 2
    first_sum = Summing(hidden_width + short, width, False)
    second_sum = Summing(3 * width + short, width, True)
    spot = first_sum.spot(me, dp)
    stats = (PAIRS * tiles, 2 * TILE)

    came = []
    for shift in range(1, groups):
        pairs = [(i, (i + shift) % groups) for i in range(groups)]
        sent = lax.dynamic_slice_in_dim(memory, ((me + shift) % groups) * count, count, 0)
        came.append(lax.ppermute(sent, "mem", pairs))

    sorted_rows, qkv, self_norm, self_attn_t, hidden_one, query, part, part_top, part_sum, pair_mine = call(
        functools.partial(self_forward_kernel, groups),
        [
            ((rows, width), BF16),
            ((rows, 3 * width), BF16),
            (stats, F32),
            ((width, rows), BF16),
            ((rows, width), F32),
            ((rows, width), BF16),
            ((width, rows), F32),
            (stats, F32),
            (stats, F32),
            ((count, places, 2 * width), BF16),
        ],
        [
            ((tiles, half, 2 * TILE), F32),
            ((count, span, 2 * TILE), F32),
            ((tiles, 2 * TILE, width), BF16),
            ((width, rows), BF16),
            ((count, width, span), BF16),
            ((count, span, 2 * width), BF16),
            pltpu.SemaphoreType.DMA((count,)),
        ],
        3,
        spot,
        tgt_len,
        src_len,
        target,
        w_qkv,
        w_out,
        wq_cross,
        ln_gain,
        ln_bias,
        memory,
        wkv_cross,
        vmem=60,
        hbm_out=1,
    )
    result_out, cross_norm, cross_along, keep_one, send_one, grad_hidden_two, grad_attn, ln_part, pair_all = middle(
        groups, first_sum, stats, spot, tgt_len, src_len, hidden_one, query, part, part_top, part_sum, wkv_cross,
        ln_gain, ln_bias, wo_cross, w_up, w_down, grad_out, pair_mine, came,
    )
    came_one = first_sum.core_swap(send_one)

    def cross_backward(block):
        sentences = 1 if block == 0 else count - 1
        return call(
            functools.partial(cross_backward_kernel, groups, block),
            [((sentences, places, 2 * width), BF16), ((width, half), BF16)],
            [
                ((sentences, places, 2 * width), BF16),
                ((sentences, places, 2 * TILE), F32),
                ((half // TILE, 2 * TILE, width), BF16),
                ((half // TILE, 2 * TILE, width), BF16),
                ((sentences, width, places), BF16),
                ((SLAB, half), F32),
                ((sentences, places, 2 * SLAB), F32),
                pltpu.SemaphoreType.DMA((1,)),
            ],
            3,
            spot,
            tgt_len,
            src_len,
            query,
            cross_norm,
            cross_along,
            grad_attn,
            pair_all,
            work=10,
            vmem=24 if block == 0 else 32,
            hbm_in=1,
        )

    pair_grad_long, query_grad_t_long = cross_backward(0)
    came_one, pair_grad_long = lax.optimization_barrier((came_one, pair_grad_long))
    parts_one = first_sum.first_split(spot, keep_one, came_one)
    parts_one, pair_all = lax.optimization_barrier((parts_one, pair_all))
    parts_one = first_sum.swap(parts_one, 0)
    pair_grad_rest, query_grad_t_rest = cross_backward(1)
    (wkv_grad,) = call(
        functools.partial(memory_weight_kernel, groups),
        [((2, width, width), BF16)],
        [((width, 2 * width), F32)],
        2,
        spot,
        tgt_len,
        pair_grad_long,
        pair_grad_rest,
        memory,
        *came,
        work=1,
        vmem=32,
    )
    parts_one, wkv_grad = lax.optimization_barrier((parts_one, wkv_grad))
    parts_one = first_sum.second_split(spot, parts_one)
    parts_one, wkv_grad = lax.optimization_barrier((parts_one, wkv_grad))
    parts_one = first_sum.swap(parts_one, 1)
    keep_mid, send_mid, grad_hidden_one, grad_self = call(
        first_norm_backward_kernel,
        [
            ((2 * width + LN_ROWS, width), BF16),
            ((2 * width + LN_ROWS, width), BF16),
            ((rows, width), F32),
            ((rows, width), BF16),
        ],
        [],
        1,
        spot,
        hidden_one,
        query_grad_t_long,
        query_grad_t_rest,
        grad_hidden_two,
        wq_cross,
        w_out,
        self_attn_t,
        ln_gain,
        ln_bias,
        ln_part,
        wkv_grad,
        work=5,
        vmem=24,
    )
    parts_one, grad_self = lax.optimization_barrier((parts_one, grad_self))
    sum_one = first_sum.total(parts_one)[0]
    sum_one, pair_grad_long, send_mid = lax.optimization_barrier((sum_one, pair_grad_long, send_mid))
    spread_one = first_sum.spread(1, sum_one)
    came_mid = second_sum.core_swap(send_mid)
    grad_mine, *grad_away = call(
        functools.partial(memory_grad_kernel, groups),
        [((count, span, width), BF16)] + [((count, span // 2, width), BF16)] * (2 * (groups - 1)),
        [],
        2,
        spot,
        tgt_len,
        pair_grad_long,
        pair_grad_rest,
        wkv_cross,
        work=8,
        vmem=32,
    )
    spread_one, grad_away, came_mid = lax.optimization_barrier((spread_one, grad_away, came_mid))
    joined_one = first_sum.join(spot, spread_one)
    joined_one, grad_self = lax.optimization_barrier((joined_one, grad_self))
    spread_one = first_sum.spread(0, joined_one)
    backs = [[], []]
    for i, grads in enumerate(grad_away):
        shift = i // 2 + 1
        backs[i % 2].append(lax.ppermute(grads, "mem", [(k, (k - shift) % groups) for k in range(groups)]))
    grad_triple, *last = call(
        self_backward_kernel,
        [((rows, 3 * width), BF16)] + [(((width + short) // LAST_PARTS, width), BF16)] * (2 * LAST_PARTS),
        [
            ((tiles, half, 2 * TILE), F32),
            ((tiles, 2 * TILE, width), BF16),
            ((tiles, 2 * TILE, width), BF16),
            ((width, rows), BF16),
            ((width, rows), BF16),
        ],
        2,
        spot,
        tgt_len,
        qkv,
        self_norm,
        grad_self,
        sorted_rows,
        work=8,
        vmem=28,
    )
    keep_last = last[:LAST_PARTS]
    came_last = [second_sum.core_swap(part) for part in last[LAST_PARTS:]]
    (grad_target,) = call(
        target_kernel,
        [((rows, width), BF16)],
        [],
        2,
        spot,
        tgt_len,
        grad_triple,
        w_qkv,
        grad_hidden_one,
        work=0.5,
        vmem=16,
    )
    came_last, grad_target, spread_one = lax.optimization_barrier((came_last, grad_target, spread_one))
    parts_two = second_sum.first_split(
        spot, keep_mid, came_mid, *[part for both in zip(keep_last, came_last) for part in both]
    )
    parts_two = second_sum.swap(parts_two, 0)
    other_one = [first_sum.core_swap(array) for array in spread_one]
    chunks = hidden_width // width
    pieces = []
    for chunk in range(chunks):
        side, here = chunk // (chunks // 2), chunk % (chunks // 2)
        pieces.append((side, here * width, width, 0, chunk * width, 0))
        pieces.append((side, (chunks // 2 + here) * width, width, 1, 0, chunk * width))
    for side in range(2):
        pieces.append((side, chunks * width, short, 2, side * short, 0))
    grad_w_down, grad_w_up, grad_wo = first_sum.finish(
        spot,
        spread_one,
        other_one,
        pieces,
        [((hidden_width, width), F32), ((width, hidden_width), F32), ((width, width), F32)],
    )
    parts_two, grad_w_down, backs[0] = lax.optimization_barrier((parts_two, grad_w_down, backs[0]))
    parts_two = second_sum.swap(second_sum.second_split(spot, parts_two), 1)
    sum_two, norm_sums = second_sum.total(parts_two)
    spread_two = second_sum.spread(0, second_sum.join(spot, second_sum.spread(1, sum_two)))
    other_two = [second_sum.core_swap(array) for array in spread_two]
    pieces = [
        (0, 0, width, 0, 0, 0),
        (0, width, width, 1, 0, 0),
        (0, 2 * width, width, 2, 0, 0),
        (0, 3 * width, short, 2, 0, width),
        (1, 0, width, 1, 0, width),
        (1, width, width, 3, 0, 0),
        (1, 2 * width, short, 2, short, width),
        (1, 2 * width + short, width, 2, 0, 2 * width),
    ]
    grad_wq, grad_wkv, grad_w_qkv, grad_w_out = second_sum.finish(
        spot,
        spread_two,
        other_two,
        pieces,
        [
            ((width, width), F32),
            ((width, 2 * width), F32),
            ((width, 3 * width), F32),
            ((width, width), F32),
        ],
    )
    grad_memory = jnp.zeros(memory.shape, BF16)
    grad_memory = lax.dynamic_update_slice(grad_memory, grad_mine, (me * count, 0, 0))
    for part in range(2):
        for i, grads in enumerate(backs[part]):
            owner = (me + i + 1) % groups
            grad_memory = lax.dynamic_update_slice(grad_memory, grads, (owner * count, part * (span // 2), 0))
    return (
        result_out,
        grad_target,
        grad_memory,
        grad_w_qkv,
        grad_w_out,
        grad_wq,
        grad_wkv,
        grad_wo,
        grad_w_up,
        grad_w_down,
        norm_sums[:3],
        norm_sums[3:6],
    )


def solution(mesh):
    rows_spec = P(("dp", "mem"), None)
    memory_spec = P("dp", "mem", None)
    return jax.shard_map(
        body,
        mesh=mesh,
        in_specs=(rows_spec, memory_spec, rows_spec, P("dp", None), P("dp", None)) + (P(),) * 9,
        out_specs=(rows_spec, rows_spec, memory_spec) + (P(),) * 9,
        check_vma=False,
    )
```

```python
import functools
import math

import jax
import jax.numpy as jnp
from jax import lax
from jax.experimental import pallas as pl
from jax.experimental.pallas import tpu as pltpu
from jax.sharding import PartitionSpec as P

HEADS = 8
PAIRS = HEADS // 2
SLAB = 128
SIDE = SLAB // 2
TILE = 128
MASKED = -1e30
EPSILON = 1e-05
F32 = jnp.float32
BF16 = jnp.bfloat16
MIB = 1024 * 1024
LN_ROWS = 16
LAST_PARTS = 1


def dot(left, right):
    return jnp.dot(left, right, preferred_element_type=F32)


def dot_nt(left, right):
    return lax.dot_general(left, right, (((1,), (1,)), ((), ())), preferred_element_type=F32)


def dot_tn(left, right):
    return lax.dot_general(left, right, (((0,), (0,)), ((), ())), preferred_element_type=F32)


def iota(shape, axis):
    return lax.broadcasted_iota(jnp.int32, shape, axis)


def norm_parts(hidden):
    centre = hidden - jnp.mean(hidden, axis=-1, keepdims=True)
    inverse = lax.rsqrt(jnp.mean(centre * centre, axis=-1, keepdims=True) + EPSILON)
    return centre * inverse, inverse


def norm_backward(upstream, unit, inverse, gain_row):
    scaled = upstream * gain_row
    shifted = (
        scaled
        - jnp.mean(scaled, axis=-1, keepdims=True)
        - unit * jnp.mean(scaled * unit, axis=-1, keepdims=True)
    )
    gain_grad = jnp.sum(upstream * unit, axis=0, keepdims=True)
    return inverse * shifted, gain_grad, jnp.sum(upstream, axis=0, keepdims=True)


def sentence_order(me, len_ref):
    count = len_ref.shape[1]
    lengths = [len_ref[me, k] for k in range(count)]
    longest, best, start, running = jnp.int32(0), lengths[0], jnp.int32(0), jnp.int32(0)
    for k in range(1, count):
        running = running + lengths[k - 1]
        more = lengths[k] > best
        longest = jnp.where(more, k, longest)
        start = jnp.where(more, running, start)
        best = jnp.where(more, lengths[k], best)
    order = [longest] + [jnp.where(k < longest, k, k + 1) for k in range(count - 1)]
    bounds = [jnp.int32(0)]
    for k in range(1, count):
        bounds.append(bounds[-1] + len_ref[me, order[k]])
    return order, start, bounds


def moved_rows(index, start, half):
    return jnp.where(index < start, index + half, jnp.where(index < start + half, index - start, index))


def sort_matrix(rows, start):
    spot = moved_rows(iota((rows, rows), 1), start, rows // 2)
    return jnp.where(spot == iota((rows, rows), 0), 1.0, 0.0).astype(BF16)


def unsort_matrix(rows, start):
    spot = moved_rows(iota((rows, rows), 0), start, rows // 2)
    return jnp.where(spot == iota((rows, rows), 1), 1.0, 0.0).astype(BF16)


def side_masks(width):
    side = iota((1, width), 1) % SLAB
    first = jnp.where(side < SLAB // 2, 1.0, 0.0)
    return first.astype(BF16), (1.0 - first).astype(BF16)


def slab_of(pair, first=0):
    return pl.ds(pl.multiple_of(first + pair * SLAB, SLAB), SLAB)


def pack_heads(out_ref, rows, width):
    even, odd = side_masks(width)
    for t in range(out_ref.shape[0]):
        tile = rows(t * TILE, TILE)
        out_ref[t, :TILE, :] = tile * even
        out_ref[t, TILE:, :] = tile * odd


def fill_self_bias(bias_ref, bounds, half):
    for t in range(bias_ref.shape[0]):
        block, inner = t // (half // TILE), t % (half // TILE)
        key = iota((half, 2 * TILE), 0)
        query = iota((half, 2 * TILE), 1) % TILE + inner * TILE
        allowed = key <= query
        if block == 1:
            first = jnp.zeros((half, 2 * TILE), jnp.int32)
            for bound in bounds[1:-1]:
                first = jnp.where(query >= bound, bound, first)
            allowed = allowed & (key >= first)
        bias_ref[t] = jnp.where(allowed, 0.0, MASKED)


def self_keys(t, half):
    per = half // TILE
    return (t // per) * half, (t % per + 1) * TILE


def fill_live_bias(bias_ref, me, groups, parts, span, src_ref, sentences):
    key = iota((span, bias_ref.shape[2]), 0)
    for j, sentence in enumerate(sentences):
        for i, part in enumerate(parts):
            place = lax.rem(me - part + groups, groups) * span + key
            live = place < src_ref[me, sentence]
            bias_ref[j, pl.ds(i * span, span), :] = jnp.where(live, 0.0, MASKED)


def cross_units(bounds, half):
    units = [(t, 0, None) for t in range(half // TILE)]
    middle = half // 2
    last = jnp.int32(1)
    for bound in bounds[1:-1]:
        last = last + jnp.where(bound < middle, 1, 0)
    ends = bounds[1:]
    column = iota((1, 2 * TILE), 1) % TILE
    for u in range(len(ends) + 1):
        early = u < last
        sentence = jnp.where(early, u + 1, u)
        tile = jnp.where(early, 0, 1)
        low, high = jnp.int32(0), ends[0]
        for k in range(1, len(ends)):
            low = jnp.where(sentence == k + 1, ends[k - 1], low)
            high = jnp.where(sentence == k + 1, ends[k], high)
        row = column + tile * TILE
        units.append((tile + half // TILE, sentence, (row >= low) & (row < high)))
    return units


def own_sides(both):
    return jnp.concatenate([both[:SIDE, :TILE], both[SIDE:, TILE:]], axis=0)


def side_rows(row):
    even = jnp.broadcast_to(row[:, :TILE], (SIDE, TILE))
    return jnp.concatenate([even, jnp.broadcast_to(row[:, TILE:], (SIDE, TILE))], axis=0)


def tile_columns(tile):
    if isinstance(tile, int):
        return pl.ds(tile * TILE, TILE)
    return pl.ds(pl.multiple_of(tile * TILE, TILE), TILE)


def self_forward_kernel(
    groups,
    me_ref,
    len_ref,
    src_ref,
    target_ref,
    w_qkv_ref,
    w_out_ref,
    wq_ref,
    gain_ref,
    bias_row_ref,
    memory_ref,
    wkv_ref,
    sorted_ref,
    qkv_ref,
    norm_ref,
    attn_t_ref,
    hidden_ref,
    query_ref,
    part_ref,
    top_ref,
    sum_ref,
    pair_out_ref,
    bias_ref,
    live_ref,
    q_pack_ref,
    value_t_ref,
    cross_value_t_ref,
    pair_ref,
    copy_sem,
):
    rows, width = target_ref.shape
    half = rows // 2
    me = me_ref[0]
    order, start, bounds = sentence_order(me, len_ref)
    count, span = pair_ref.shape[0], pair_ref.shape[1]
    copies = []
    for j in range(count):
        block = memory_ref[me * count + order[j]]
        pair_ref[j] = dot(block, wkv_ref[...]).astype(BF16)
        copy = pltpu.make_async_copy(
            pair_ref.at[j], pair_out_ref.at[j, pl.ds(0, span), :], copy_sem.at[j]
        )
        copy.start()
        copies.append(copy)
    sorted_rows = dot(sort_matrix(rows, start), target_ref[...]).astype(BF16)
    sorted_ref[...] = sorted_rows
    fill_self_bias(bias_ref, bounds, half)
    queries = (dot(sorted_rows, w_qkv_ref[:, :width]).astype(BF16) * 0.125).astype(BF16)
    qkv_ref[:, :width] = queries
    pack_heads(q_pack_ref, lambda first, size: queries[first : first + size], width)
    qkv_ref[:, width : 2 * width] = dot(sorted_rows, w_qkv_ref[:, width : 2 * width]).astype(BF16)
    values = dot(sorted_rows, w_qkv_ref[:, 2 * width :]).astype(BF16)
    qkv_ref[:, 2 * width :] = values
    value_t_ref[...] = values.T
    tiles = rows // TILE

    def self_step(pair, carry):
        slab = slab_of(pair)
        for t in range(tiles):
            first, size = self_keys(t, half)
            keys = qkv_ref[pl.ds(first, size), slab_of(pair, width)]
            scores = dot_nt(keys, q_pack_ref[t, :, slab]) + bias_ref[t, :size, :]
            top = jnp.max(scores, axis=0, keepdims=True)
            weights = jnp.exp(scores - top)
            total = jnp.sum(weights, axis=0, keepdims=True)
            probs = (weights * (1.0 / total)).astype(BF16)
            both = dot(value_t_ref[slab, pl.ds(first, size)], probs)
            attn_t_ref[slab, tile_columns(t)] = own_sides(both).astype(BF16)
            norm_ref[pl.ds(pair * tiles + t, 1), :] = top + jnp.log(total)
        return carry

    lax.fori_loop(0, PAIRS, self_step, 0)
    hidden = sorted_rows.astype(F32) + dot(attn_t_ref[...].T, w_out_ref[...])
    hidden_ref[...] = hidden
    unit, _ = norm_parts(hidden)
    normed = (unit * gain_ref[0:1] + bias_row_ref[0:1]).astype(BF16)
    query_ref[...] = (dot(normed, wq_ref[...]).astype(BF16) * 0.125).astype(BF16)

    pack_heads(q_pack_ref, lambda first, size: query_ref[first : first + size, :], width)
    fill_live_bias(live_ref, me, groups, [0], span, src_ref, order)
    for j in range(count):
        cross_value_t_ref[j] = pair_ref[j, :, width:].T
    units = cross_units(bounds, half)

    def cross_step(pair, carry):
        slab = slab_of(pair)
        for tile, sentence, columns in units:
            scores = dot_nt(pair_ref[sentence, :, slab], q_pack_ref[tile, :, slab]) + live_ref[sentence]
            top = jnp.max(scores, axis=0, keepdims=True)
            weights = jnp.exp(scores - top)
            total = jnp.sum(weights, axis=0, keepdims=True)
            result = own_sides(dot(cross_value_t_ref[sentence, slab, :], weights.astype(BF16)))
            here = tile_columns(tile)
            row = pl.ds(pair * tiles + tile, 1)
            if columns is not None:
                result = jnp.where(columns[:, :TILE], result, part_ref[slab, here])
                top = jnp.where(columns, top, top_ref[row, :])
                total = jnp.where(columns, total, sum_ref[row, :])
            part_ref[slab, here] = result
            top_ref[row, :] = top
            sum_ref[row, :] = total
        return carry

    part_ref[...] = jnp.zeros_like(part_ref)
    top_ref[...] = jnp.zeros_like(top_ref)
    sum_ref[...] = jnp.ones_like(sum_ref)
    lax.fori_loop(0, PAIRS, cross_step, 0)
    for copy in copies:
        copy.wait()


def middle_kernel(
    groups,
    me_ref,
    len_ref,
    src_ref,
    hidden_one_ref,
    query_ref,
    part_ref,
    top_ref,
    sum_ref,
    wkv_ref,
    gain_ref,
    bias_row_ref,
    wo_hbm,
    w_up_hbm,
    w_down_hbm,
    grad_out_hbm,
    pair_in_hbm,
    *refs,
):
    came_refs = refs[: groups - 1]
    (
        out_ref,
        norm_ref,
        along_ref,
        keep_hbm,
        send_hbm,
        grad_hidden_ref,
        grad_attn_ref,
        ln_ref,
        pair_hbm,
        wo_ref,
        w_up_ref,
        w_down_ref,
        grad_out_ref,
        pair_ref,
        keep_ref,
        send_ref,
        live_ref,
        q_pack_ref,
        value_t_ref,
        attn_t_ref,
        active_ref,
        slope_ref,
        total_ref,
        load_sem,
        pair_sem,
        store_sem,
    ) = refs[groups - 1 :]
    rows, width = hidden_one_ref.shape
    half = rows // 2
    me = me_ref[0]
    count, away = pair_ref.shape[0], pair_ref.shape[1]
    span = away // (groups - 1)
    loads = [
        pltpu.make_async_copy(source, there, load_sem.at[i])
        for i, (source, there) in enumerate(
            [(wo_hbm, wo_ref), (w_up_hbm, w_up_ref), (w_down_hbm, w_down_ref), (grad_out_hbm, grad_out_ref)]
        )
    ]
    for copy in loads:
        copy.start()
    order, start, bounds = sentence_order(me, len_ref)
    fill_live_bias(live_ref, me, groups, list(range(1, groups)), span, src_ref, order)
    pack_heads(q_pack_ref, lambda first, size: query_ref[first : first + size, :], width)
    pair_copies = []
    for j in range(count):
        for part in range(1, groups):
            block = came_refs[part - 1][order[j]]
            pair_ref[j, pl.ds((part - 1) * span, span), :] = dot(block, wkv_ref[...]).astype(BF16)
        value_t_ref[j] = pair_ref[j, :, width:].T
        copy = pltpu.make_async_copy(pair_ref.at[j], pair_hbm.at[j, pl.ds(span, away), :], pair_sem.at[j])
        copy.start()
        pair_copies.append(copy)
    units = cross_units(bounds, half)
    tiles = rows // TILE

    def cross_step(pair, carry):
        slab = slab_of(pair)
        for tile, sentence, columns in units:
            here = tile_columns(tile)
            row = pl.ds(pair * tiles + tile, 1)
            scores = dot_nt(pair_ref[sentence, :, slab], q_pack_ref[tile, :, slab]) + live_ref[sentence]
            before = top_ref[row, :]
            top = jnp.maximum(jnp.max(scores, axis=0, keepdims=True), before)
            weights = jnp.exp(scores - top)
            scale = jnp.exp(before - top)
            total = jnp.sum(weights, axis=0, keepdims=True) + sum_ref[row, :] * scale
            result = own_sides(dot(value_t_ref[sentence, slab, :], weights.astype(BF16)))
            result = (result + part_ref[slab, here] * side_rows(scale)) * side_rows(1.0 / total)
            norm = top + jnp.log(total)
            if columns is not None:
                result = jnp.where(columns[:, :TILE], result, attn_t_ref[slab, here])
                norm = jnp.where(columns, norm, norm_ref[row, :])
            attn_t_ref[slab, here] = result
            norm_ref[row, :] = norm
        return carry

    attn_t_ref[...] = jnp.zeros_like(attn_t_ref)
    norm_ref[...] = jnp.zeros_like(norm_ref)
    lax.fori_loop(0, PAIRS, cross_step, 0)
    attn_t_low = attn_t_ref[...].astype(BF16)
    loads[0].wait()
    unit_one, _ = norm_parts(hidden_one_ref[...])
    normed_one = unit_one * gain_ref[0:1] + bias_row_ref[0:1]
    hidden_two = normed_one + dot(attn_t_low.T, wo_ref[...])
    unit_two, inverse_two = norm_parts(hidden_two)
    normed_two = unit_two * gain_ref[1:2] + bias_row_ref[1:2]
    normed_two_low = normed_two.astype(BF16)
    total_ref[...] = normed_two
    chunk = width
    chunks = w_down_ref.shape[0] // chunk
    loads[1].wait()
    loads[2].wait()

    def up_step(c, carry):
        cols = pl.ds(pl.multiple_of(c * chunk, chunk), chunk)
        upper = dot(normed_two_low, w_up_ref[:, cols])
        sigma = 1.0 / (1.0 + jnp.exp(-upper))
        active = (upper * sigma).astype(BF16)
        active_ref[:, cols] = active
        slope_ref[:, cols] = sigma * (1.0 + upper * (1.0 - sigma))
        total_ref[...] += dot(active, w_down_ref[cols, :])
        return carry

    lax.fori_loop(0, chunks, up_step, 0)
    unit_three, inverse_three = norm_parts(total_ref[...])
    result = (unit_three * gain_ref[2:3] + bias_row_ref[2:3]).astype(BF16)
    out_ref[...] = dot(unsort_matrix(rows, start), result).astype(BF16)
    loads[3].wait()
    upstream = dot(sort_matrix(rows, start), grad_out_ref[...])
    grad_three, gain_three, bias_three = norm_backward(upstream, unit_three, inverse_three, gain_ref[2:3])
    grad_down = grad_three.astype(BF16)
    total_ref[...] = grad_three
    normed_two_t = normed_two_low.T

    def down_step(c, carry):
        cols = pl.ds(pl.multiple_of(c * chunk, chunk), chunk)
        grad_upper = (dot_nt(grad_down, w_down_ref[cols, :]) * slope_ref[:, cols]).astype(BF16)
        down_part = dot_tn(active_ref[:, cols], grad_down).astype(BF16)
        up_part = dot(normed_two_t, grad_upper).astype(BF16)
        here = lax.rem(c, chunks // 2)
        down_rows = pl.ds(pl.multiple_of(here * chunk, chunk), chunk)
        up_rows = pl.ds(pl.multiple_of((chunks // 2 + here) * chunk, chunk), chunk)
        mine = c // (chunks // 2) == me_ref[1]

        @pl.when(mine)
        def _():
            keep_ref[down_rows, :] = down_part
            keep_ref[up_rows, :] = up_part

        @pl.when(jnp.logical_not(mine))
        def _():
            send_ref[down_rows, :] = down_part
            send_ref[up_rows, :] = up_part

        total_ref[...] += dot_nt(grad_upper, w_up_ref[:, cols])
        return carry

    lax.fori_loop(0, chunks, down_step, 0)
    most = chunks * chunk
    stores = [
        pltpu.make_async_copy(ref.at[pl.ds(first, size)], there.at[pl.ds(first, size)], store_sem.at[i])
        for i, (ref, there, first, size) in enumerate(
            [
                (send_ref, send_hbm, 0, most),
                (keep_ref, keep_hbm, 0, most),
                (send_ref, send_hbm, most, keep_ref.shape[0] - most),
                (keep_ref, keep_hbm, most, keep_ref.shape[0] - most),
            ]
        )
    ]
    stores[0].start()
    stores[1].start()
    grad_two, gain_two, bias_two = norm_backward(total_ref[...], unit_two, inverse_two, gain_ref[1:2])
    grad_two_low = grad_two.astype(BF16)
    wo_grad = dot(attn_t_low, grad_two_low).astype(BF16)
    core = me_ref[1]
    low, high = wo_grad[: width // 2], wo_grad[width // 2 :]
    tail = pl.ds(most, width // 2)
    keep_ref[tail, :] = jnp.where(core == 0, low, high)
    send_ref[tail, :] = jnp.where(core == 0, high, low)
    used = most + width // 2
    if keep_ref.shape[0] > used:
        keep_ref[used:, :] = jnp.zeros((keep_ref.shape[0] - used, width), BF16)
        send_ref[used:, :] = jnp.zeros((keep_ref.shape[0] - used, width), BF16)
    stores[2].start()
    stores[3].start()
    grad_hidden_ref[...] = grad_two
    grad_attn = dot_nt(grad_two_low, wo_ref[...]).astype(BF16)
    grad_attn_ref[...] = grad_attn
    product = grad_attn.T.astype(F32) * attn_t_ref[...]
    for pair in range(PAIRS):
        for side in range(2):
            first = pair * SLAB + side * SIDE
            along = jnp.sum(product[first : first + SIDE], axis=0, keepdims=True)
            for t in range(tiles):
                along_ref[pair * tiles + t : pair * tiles + t + 1, side * TILE : (side + 1) * TILE] = along[
                    :, t * TILE : (t + 1) * TILE
                ]
    ln_ref[...] = jnp.concatenate([gain_two, gain_three, bias_two, bias_three], axis=0)
    for copy in pair_copies + stores:
        copy.wait()


def cross_backward_kernel(
    groups,
    block,
    me_ref,
    len_ref,
    src_ref,
    query_ref,
    norm_ref,
    along_ref,
    grad_attn_ref,
    pair_hbm,
    pair_grad_ref,
    query_grad_t_ref,
    pair_ref,
    live_ref,
    q_pack_ref,
    g_pack_ref,
    key_t_ref,
    query_sum_ref,
    sum_ref,
    load_sem,
):
    rows, width = query_ref.shape
    half = rows // 2
    me = me_ref[0]
    sentences, places = pair_ref.shape[0], pair_ref.shape[1]
    first_sentence = 0 if block == 0 else 1
    load = pltpu.make_async_copy(pair_hbm.at[pl.ds(first_sentence, sentences)], pair_ref, load_sem.at[0])
    load.start()
    order, start, bounds = sentence_order(me, len_ref)
    mine = order[:1] if block == 0 else order[1:]
    fill_live_bias(live_ref, me, groups, list(range(groups)), places // groups, src_ref, mine)
    low = block * half
    pack_heads(q_pack_ref, lambda first, size: query_ref[low + first : low + first + size, :], width)
    pack_heads(g_pack_ref, lambda first, size: grad_attn_ref[low + first : low + first + size, :], width)
    tiles, per = rows // TILE, half // TILE
    units = cross_units(bounds, half)
    units = units[:per] if block == 0 else units[per:]
    load.wait()
    for j in range(sentences):
        key_t_ref[j] = pair_ref[j, :, :width].T

    def pair_step(pair, carry):
        slab, value_slab = slab_of(pair), slab_of(pair, width)
        query_sum_ref[...] = jnp.zeros_like(query_sum_ref)
        sum_ref[...] = jnp.zeros_like(sum_ref)
        for tile, sentence, columns in units:
            j = sentence - first_sentence
            t = tile - block * per
            here = tile_columns(t)
            row = pl.ds(pair * tiles + tile, 1)
            q_rows, g_rows = q_pack_ref[t, :, slab], g_pack_ref[t, :, slab]
            norm = norm_ref[row, :]
            if columns is not None:
                norm = jnp.where(columns, norm, -MASKED)
            scores = dot_nt(pair_ref[j, :, slab], q_rows) + live_ref[j]
            probs = jnp.exp(scores - norm)
            grad_probs = dot_nt(pair_ref[j, :, value_slab], g_rows)
            grad_scores = (probs * (grad_probs - along_ref[row, :])).astype(BF16)
            sum_ref[j, :, :SLAB] += dot(grad_scores, q_rows)
            sum_ref[j, :, SLAB:] += dot(probs.astype(BF16), g_rows)
            query_sum_ref[:, here] += own_sides(dot(key_t_ref[j, slab, :], grad_scores))
        query_grad_t_ref[slab, :] = (query_sum_ref[...] * 0.125).astype(BF16)
        pair_grad_ref[:, :, slab] = sum_ref[:, :, :SLAB].astype(BF16)
        pair_grad_ref[:, :, value_slab] = sum_ref[:, :, SLAB:].astype(BF16)
        return carry

    lax.fori_loop(0, PAIRS, pair_step, 0)


def memory_weight_kernel(groups, me_ref, len_ref, pair_grad_long_ref, pair_grad_rest_ref, memory_ref, *refs):
    came_refs = refs[: groups - 1]
    wkv_grad_ref, total_ref = refs[groups - 1 :]
    width = memory_ref.shape[2]
    me = me_ref[0]
    count = len_ref.shape[1]
    span = pair_grad_long_ref.shape[1] // groups
    order, _, _ = sentence_order(me, len_ref)
    for j in range(count):
        pair_grad_ref, here = (pair_grad_long_ref, 0) if j == 0 else (pair_grad_rest_ref, j - 1)
        blocks = [memory_ref[me * count + order[j]]] + [ref[order[j]] for ref in came_refs]
        term = dot_tn(jnp.concatenate(blocks, axis=0), pair_grad_ref[here])
        if j == 0:
            total_ref[...] = term
        else:
            total_ref[...] += term
    wkv_grad_ref[0] = total_ref[:, :width].astype(BF16)
    wkv_grad_ref[1] = total_ref[:, width:].astype(BF16)


def memory_grad_kernel(
    groups, me_ref, len_ref, pair_grad_long_ref, pair_grad_rest_ref, wkv_ref, mine_ref, *away_refs
):
    count = len_ref.shape[1]
    span = pair_grad_long_ref.shape[1] // groups
    order, _, _ = sentence_order(me_ref[0], len_ref)
    for j in range(count):
        pair_grad_ref, here = (pair_grad_long_ref, 0) if j == 0 else (pair_grad_rest_ref, j - 1)
        grads = dot_nt(pair_grad_ref[here], wkv_ref[...]).astype(BF16)
        mine_ref[order[j]] = grads[:span]
        for i, ref in enumerate(away_refs):
            ref[order[j]] = grads[(i + 1) * span : (i + 2) * span]


def first_norm_backward_kernel(
    me_ref,
    hidden_one_ref,
    query_grad_t_long_ref,
    query_grad_t_rest_ref,
    grad_hidden_two_ref,
    wq_ref,
    w_out_ref,
    self_attn_t_ref,
    gain_ref,
    bias_row_ref,
    ln_in_ref,
    wkv_grad_ref,
    keep_ref,
    send_ref,
    grad_hidden_ref,
    grad_self_ref,
):
    width = wq_ref.shape[0]
    unit_one, inverse_one = norm_parts(hidden_one_ref[...])
    normed_one = (unit_one * gain_ref[0:1] + bias_row_ref[0:1]).astype(BF16)
    query_grad = jnp.concatenate([query_grad_t_long_ref[...].T, query_grad_t_rest_ref[...].T], axis=0)
    upstream = grad_hidden_two_ref[...] + dot_nt(query_grad, wq_ref[...])
    grad_one, gain_one, bias_one = norm_backward(upstream, unit_one, inverse_one, gain_ref[0:1])
    grad_hidden_ref[...] = grad_one
    grad_one_low = grad_one.astype(BF16)
    grad_self_ref[...] = dot_nt(grad_one_low, w_out_ref[...]).astype(BF16)
    wq_grad = dot_tn(normed_one, query_grad).astype(BF16)
    w_out_grad = dot(self_attn_t_ref[...], grad_one_low).astype(BF16)
    norms = jnp.concatenate(
        [gain_one, ln_in_ref[0:2], bias_one, ln_in_ref[2:4], jnp.zeros((LN_ROWS - 6, width), F32)], axis=0
    ).astype(BF16)

    def halves(low_ref, high_ref):
        low_ref[:width, :] = wq_grad
        low_ref[width : 2 * width, :] = wkv_grad_ref[0]
        high_ref[:width, :] = wkv_grad_ref[1]
        high_ref[width : 2 * width, :] = w_out_grad

    @pl.when(me_ref[1] == 0)
    def _():
        halves(keep_ref, send_ref)

    @pl.when(me_ref[1] != 0)
    def _():
        halves(send_ref, keep_ref)

    keep_ref[2 * width :, :] = norms
    send_ref[2 * width :, :] = norms


def self_backward_kernel(
    me_ref,
    len_ref,
    qkv_ref,
    norm_ref,
    grad_attn_ref,
    sorted_ref,
    grad_triple_ref,
    *refs,
):
    keep_refs, send_refs = refs[:LAST_PARTS], refs[LAST_PARTS : 2 * LAST_PARTS]
    self_backward(
        me_ref,
        len_ref,
        qkv_ref,
        norm_ref,
        grad_attn_ref,
        sorted_ref,
        grad_triple_ref,
        keep_refs,
        send_refs,
        *refs[2 * LAST_PARTS :],
    )


def self_backward(
    me_ref,
    len_ref,
    qkv_ref,
    norm_ref,
    grad_attn_ref,
    sorted_ref,
    grad_triple_ref,
    keep_refs,
    send_refs,
    bias_ref,
    q_pack_ref,
    g_pack_ref,
    key_t_ref,
    query_grad_t_ref,
):
    rows, width = sorted_ref.shape
    half = rows // 2
    _, _, bounds = sentence_order(me_ref[0], len_ref)
    fill_self_bias(bias_ref, bounds, half)
    pack_heads(q_pack_ref, lambda first, size: qkv_ref[first : first + size, :width], width)
    pack_heads(g_pack_ref, lambda first, size: grad_attn_ref[first : first + size, :], width)
    key_t_ref[...] = qkv_ref[:, width : 2 * width].T
    tiles, per = rows // TILE, half // TILE

    def pair_step(pair, carry):
        slab, key_slab, value_slab = slab_of(pair), slab_of(pair, width), slab_of(pair, 2 * width)
        sums = [[None, None] for _ in range(tiles)]
        for t in range(tiles):
            first, size = self_keys(t, half)
            span = pl.ds(first, size)
            q_rows, g_rows = q_pack_ref[t, :, slab], g_pack_ref[t, :, slab]
            scores = dot_nt(qkv_ref[span, key_slab], q_rows) + bias_ref[t, :size, :]
            probs = jnp.exp(scores - norm_ref[pl.ds(pair * tiles + t, 1), :])
            grad_probs = dot_nt(qkv_ref[span, value_slab], g_rows)
            along = jnp.sum(probs * grad_probs, axis=0, keepdims=True)
            grad_scores = (probs * (grad_probs - along)).astype(BF16)
            parts = dot(grad_scores, q_rows), dot(probs.astype(BF16), g_rows)
            for i in range(size // TILE):
                spot = sums[first // TILE + i]
                for k in range(2):
                    piece = parts[k][i * TILE : (i + 1) * TILE]
                    spot[k] = piece if spot[k] is None else spot[k] + piece
            query_grad_t_ref[slab, tile_columns(t)] = (
                own_sides(dot(key_t_ref[slab, span], grad_scores)) * 0.125
            ).astype(BF16)
        for t in range(tiles):
            grad_triple_ref[pl.ds(t * TILE, TILE), key_slab] = sums[t][0].astype(BF16)
            grad_triple_ref[pl.ds(t * TILE, TILE), value_slab] = sums[t][1].astype(BF16)
        return carry

    lax.fori_loop(0, PAIRS, pair_step, 0)
    grad_triple_ref[:, :width] = query_grad_t_ref[...].T
    sorted_t = sorted_ref[...].T
    grads = [
        dot(sorted_t, grad_triple_ref[:, part * width : (part + 1) * width]).astype(BF16)
        for part in range(3)
    ]
    short = width // 2

    low = jnp.concatenate([grads[0], grads[1][:short]], axis=0)
    high = jnp.concatenate([grads[1][short:], grads[2]], axis=0)
    size = keep_refs[0].shape[0]

    def halves(low_refs, high_refs):
        for i in range(LAST_PARTS):
            low_refs[i][...] = low[i * size : (i + 1) * size]
            high_refs[i][...] = high[i * size : (i + 1) * size]

    @pl.when(me_ref[1] == 0)
    def _():
        halves(keep_refs, send_refs)

    @pl.when(me_ref[1] != 0)
    def _():
        halves(send_refs, keep_refs)


def target_kernel(me_ref, len_ref, grad_triple_ref, w_qkv_ref, grad_hidden_ref, grad_target_ref):
    rows = grad_hidden_ref.shape[0]
    _, start, _ = sentence_order(me_ref[0], len_ref)
    result = grad_hidden_ref[...] + dot_nt(grad_triple_ref[...], w_qkv_ref[...])
    grad_target_ref[...] = dot(unsort_matrix(rows, start), result.astype(BF16)).astype(BF16)


def tree_sum(terms):
    while len(terms) > 1:
        terms = [terms[i] + terms[i + 1] for i in range(0, len(terms), 2)]
    return terms[0]


def rows_of(ref, first, count):
    return ref[pl.ds(pl.multiple_of(first, 16), count), :].astype(F32)


def first_split_kernel(segments, ln, peers, spot_ref, *refs):
    ins, outs, sum_ref = refs[: 2 * segments], refs[2 * segments : -1], refs[-1]
    extra = LN_ROWS if ln else 0
    size = outs[0].shape[0] - extra
    used = 0
    for i in range(segments):
        keep_ref, came_ref = ins[2 * i], ins[2 * i + 1]
        count = keep_ref.shape[0] - (extra if i == 0 else 0)
        sum_ref[used : used + count, :] = (rows_of(keep_ref, 0, count) + rows_of(came_ref, 0, count)).astype(BF16)
        if i == 0 and ln:
            tail = (rows_of(keep_ref, count, LN_ROWS) + rows_of(came_ref, count, LN_ROWS)).astype(BF16)
        used += count
    if sum_ref.shape[0] > used:
        sum_ref[used:, :] = jnp.zeros((sum_ref.shape[0] - used, sum_ref.shape[1]), BF16)
    for d, out in enumerate(outs):
        out[:size, :] = sum_ref[pl.ds(pl.multiple_of((spot_ref[2] ^ d) * size, 16), size), :]
        if ln:
            out[size:, :] = tail


def split_kernel(stage, ln, peers, spot_ref, *refs):
    ins, outs = refs[:peers], refs[peers:]
    extra = LN_ROWS if ln else 0
    size = outs[0].shape[0] - extra
    if ln:
        tail = tree_sum([rows_of(ref, size * len(outs), LN_ROWS) for ref in ins]).astype(BF16)
    for d, out in enumerate(outs):
        first = (spot_ref[2 + stage] ^ d) * size
        out[:size, :] = tree_sum([rows_of(ref, first, size) for ref in ins]).astype(BF16)
        if ln:
            out[size:, :] = tail


def total_kernel(ln, count, *refs):
    ins, outs = refs[:count], refs[count:]
    size = outs[0].shape[0]
    outs[0][...] = tree_sum([rows_of(ref, 0, size) for ref in ins]).astype(BF16)
    if ln:
        outs[1][...] = tree_sum([rows_of(ref, size, LN_ROWS) for ref in ins])


def join_kernel(stage, spot_ref, *refs):
    out_ref = refs[-1]
    for d, ref in enumerate(refs[:-1]):
        size = ref.shape[0]
        out_ref[pl.ds(pl.multiple_of((spot_ref[2 + stage] ^ d) * size, 16), size), :] = ref[...]


def finish_kernel(peers, twisted, pieces, spot_ref, *refs):
    mine, others, outs, both_ref = refs[:peers], refs[peers : 2 * peers], refs[2 * peers : -1], refs[-1]
    core = spot_ref[1]
    for half, arrays, here in ((core, mine, spot_ref[2]), (1 - core, others, spot_ref[3 if twisted else 2])):
        for d, ref in enumerate(arrays):
            size = ref.shape[0]
            both_ref[half, pl.ds(pl.multiple_of((here ^ d) * size, 16), size), :] = ref[...]
    width = both_ref.shape[2]
    for half, first, rows, out, row, col in pieces:
        outs[out][row : row + rows, col : col + width] = both_ref[half, first : first + rows, :].astype(F32)


class Summing:
    def __init__(self, rows, width, ln):
        self.width, self.ln = width, ln
        self.dp, self.mem = lax.axis_size("dp"), lax.axis_size("mem")
        z_size = 4
        x_size = self.dp // (2 * z_size)
        self.sizes = (x_size, self.mem, z_size)
        self.twisted = x_size == self.mem
        self.chunk = -(-rows // (16 * math.prod(self.sizes))) * 16
        self.rows = self.chunk * math.prod(self.sizes)

    def after(self, stage):
        return self.rows // math.prod(self.sizes[:stage])

    def axis(self, stage, core):
        return 1 - stage if self.twisted and core == 1 and stage < 2 else stage

    def coords(self, dp, mem):
        return [dp // 2 % self.sizes[0], mem, dp // (2 * self.sizes[0])], dp % 2

    def spot(self, me, dp):
        (x, mem, z), core = self.coords(dp, me)
        if self.twisted:
            x, mem = jnp.where(core == 0, x, mem), jnp.where(core == 0, mem, x)
        return jnp.stack([me, core, x, mem, z]).astype(jnp.int32)

    def permute(self, array, stage, offset):
        pairs = []
        for dp in range(self.dp):
            for mem in range(self.mem):
                spots, core = self.coords(dp, mem)
                if stage is None:
                    core ^= offset
                else:
                    spots[self.axis(stage, core)] ^= offset
                to_dp = (spots[2] * self.sizes[0] + spots[0]) * 2 + core
                pairs.append((dp * self.mem + mem, to_dp * self.mem + spots[1]))
        return lax.ppermute(array, ("dp", "mem"), pairs)

    def core_swap(self, send):
        return self.permute(send, None, 1)

    def swap(self, arrays, stage):
        return [arrays[0]] + [self.permute(array, stage, d) for d, array in enumerate(arrays) if d > 0]

    def spread(self, stage, array):
        return [array] + [self.permute(array, stage, d) for d in range(1, self.sizes[stage])]

    def messages(self, stage):
        size = self.after(stage + 1) + (LN_ROWS if self.ln else 0)
        return [((size, self.width), BF16)] * self.sizes[stage]

    def first_split(self, spot, *arrays):
        kernel = functools.partial(first_split_kernel, len(arrays) // 2, self.ln, self.sizes[0])
        return call(kernel, self.messages(0), [((self.rows, self.width), BF16)], 1, spot, *arrays, work=0.01)

    def split(self, stage, spot, arrays):
        kernel = functools.partial(split_kernel, stage, self.ln, self.sizes[stage - 1])
        return call(kernel, self.messages(stage), [], 1, spot, *arrays, work=0.01)

    def total(self, arrays):
        outs = [((self.chunk, self.width), BF16)]
        if self.ln:
            outs.append(((LN_ROWS, self.width), F32))
        return call(functools.partial(total_kernel, self.ln, self.sizes[2]), outs, [], 0, *arrays, work=0.01)

    def join(self, stage, spot, arrays):
        outs = [((self.after(stage), self.width), BF16)]
        return call(functools.partial(join_kernel, stage), outs, [], 1, spot, *arrays, work=0.01)[0]

    def finish(self, spot, mine, others, pieces, outs):
        kernel = functools.partial(finish_kernel, self.sizes[0], self.twisted, pieces)
        scratch = [((2, self.rows, self.width), BF16)]
        return call(kernel, outs, scratch, 1, spot, *mine, *others, work=1)


def call(kernel, outs, scratch, scalars, *arrays, work=0.5, vmem=0, hbm_in=0, hbm_out=0, aliases=None):
    plain = len(arrays) - scalars - hbm_in
    if not vmem:
        blocks = [(array.shape, array.dtype) for array in arrays[scalars:]] + outs + scratch
        vmem = max(16, sum(math.prod(shape) * jnp.dtype(kind).itemsize for shape, kind in blocks) // MIB + 7)
    specs = [pl.BlockSpec(memory_space=pltpu.SMEM)] * scalars
    specs = specs + [pl.BlockSpec(memory_space=pltpu.VMEM)] * plain
    specs = specs + [pl.BlockSpec(memory_space=pl.ANY)] * hbm_in
    out_specs = [pl.BlockSpec(memory_space=pltpu.VMEM)] * (len(outs) - hbm_out)
    out_specs = out_specs + [pl.BlockSpec(memory_space=pl.ANY)] * hbm_out
    return pl.pallas_call(
        kernel,
        out_shape=[jax.ShapeDtypeStruct(shape, kind) for shape, kind in outs],
        in_specs=specs,
        out_specs=out_specs,
        scratch_shapes=[pltpu.VMEM(*entry) if isinstance(entry, tuple) else entry for entry in scratch],
        input_output_aliases=aliases or {},
        compiler_params=pltpu.CompilerParams(vmem_limit_bytes=vmem * MIB),
        cost_estimate=pl.CostEstimate(flops=int(work * 1e9), bytes_accessed=int(work * 3e6), transcendentals=0),
    )(*arrays)


def middle(
    groups, first_sum, stats, spot, tgt_len, src_len, hidden_one, query, part, part_top, part_sum, wkv_cross,
    ln_gain, ln_bias, wo_cross, w_up, w_down, grad_out, pair_mine, came,
):
    rows, width = hidden_one.shape
    half, tiles = rows // 2, rows // TILE
    hidden_width = w_down.shape[0]
    count, places, _ = pair_mine.shape
    away = places // groups * (groups - 1)
    arrays = [spot, tgt_len, src_len, hidden_one, query, part, part_top, part_sum, wkv_cross, ln_gain, ln_bias]
    stay = [wo_cross, w_up, w_down, grad_out, pair_mine]

    def kernel(*refs):
        ins, refs = refs[: len(arrays)], refs[len(arrays) :]
        came_refs, refs = refs[: len(came)], refs[len(came) :]
        stay_refs, refs = refs[: len(stay)], refs[len(stay) :]
        outs, refs = refs[:9], refs[9:]
        middle_kernel(groups, *ins, *stay_refs, *came_refs, *outs[:3], *outs[6:8], *outs[3:6], outs[8], *refs)

    result_out, cross_norm, cross_along, grad_hidden_two, grad_attn, ln_part, keep_one, send_one, pair_all = call(
        kernel,
        [
            ((rows, width), BF16),
            (stats, F32),
            (stats, F32),
            ((rows, width), F32),
            ((rows, width), BF16),
            ((4, width), F32),
            ((first_sum.rows, width), BF16),
            ((first_sum.rows, width), BF16),
            ((count, places, 2 * width), BF16),
        ],
        [
            ((width, width), BF16),
            ((width, hidden_width), BF16),
            ((hidden_width, width), BF16),
            ((rows, width), BF16),
            ((count, away, 2 * width), BF16),
            ((first_sum.rows, width), BF16),
            ((first_sum.rows, width), BF16),
            ((count, away, 2 * TILE), F32),
            ((tiles, 2 * TILE, width), BF16),
            ((count, width, away), BF16),
            ((width, rows), F32),
            ((rows, hidden_width), BF16),
            ((rows, hidden_width), F32),
            ((rows, width), F32),
            pltpu.SemaphoreType.DMA((4,)),
            pltpu.SemaphoreType.DMA((count,)),
            pltpu.SemaphoreType.DMA((4,)),
        ],
        3,
        *arrays,
        *came,
        *stay,
        vmem=60,
        hbm_in=len(stay),
        hbm_out=3,
        aliases={len(arrays) + len(came) + len(stay) - 1: 8},
    )
    return result_out, cross_norm, cross_along, keep_one, send_one, grad_hidden_two, grad_attn, ln_part, pair_all


def body(
    target,
    memory,
    grad_out,
    tgt_len,
    src_len,
    w_qkv,
    w_out,
    wq_cross,
    wkv_cross,
    wo_cross,
    w_up,
    w_down,
    ln_gain,
    ln_bias,
):
    rows, width = target.shape
    half = rows // 2
    tiles = rows // TILE
    hidden_width = w_down.shape[0]
    groups = lax.axis_size("mem")
    me = lax.axis_index("mem")
    count = tgt_len.shape[1]
    span = memory.shape[1]
    places, away = groups * span, (groups - 1) * span
    dp = lax.axis_index("dp")
    short = width // 2
    first_sum = Summing(hidden_width + short, width, False)
    second_sum = Summing(3 * width + short, width, True)
    spot = first_sum.spot(me, dp)
    stats = (PAIRS * tiles, 2 * TILE)

    came = []
    for shift in range(1, groups):
        pairs = [(i, (i + shift) % groups) for i in range(groups)]
        sent = lax.dynamic_slice_in_dim(memory, ((me + shift) % groups) * count, count, 0)
        came.append(lax.ppermute(sent, "mem", pairs))

    sorted_rows, qkv, self_norm, self_attn_t, hidden_one, query, part, part_top, part_sum, pair_mine = call(
        functools.partial(self_forward_kernel, groups),
        [
            ((rows, width), BF16),
            ((rows, 3 * width), BF16),
            (stats, F32),
            ((width, rows), BF16),
            ((rows, width), F32),
            ((rows, width), BF16),
            ((width, rows), F32),
            (stats, F32),
            (stats, F32),
            ((count, places, 2 * width), BF16),
        ],
        [
            ((tiles, half, 2 * TILE), F32),
            ((count, span, 2 * TILE), F32),
            ((tiles, 2 * TILE, width), BF16),
            ((width, rows), BF16),
            ((count, width, span), BF16),
            ((count, span, 2 * width), BF16),
            pltpu.SemaphoreType.DMA((count,)),
        ],
        3,
        spot,
        tgt_len,
        src_len,
        target,
        w_qkv,
        w_out,
        wq_cross,
        ln_gain,
        ln_bias,
        memory,
        wkv_cross,
        vmem=60,
        hbm_out=1,
    )
    result_out, cross_norm, cross_along, keep_one, send_one, grad_hidden_two, grad_attn, ln_part, pair_all = middle(
        groups, first_sum, stats, spot, tgt_len, src_len, hidden_one, query, part, part_top, part_sum, wkv_cross,
        ln_gain, ln_bias, wo_cross, w_up, w_down, grad_out, pair_mine, came,
    )
    came_one = first_sum.core_swap(send_one)

    def cross_backward(block):
        sentences = 1 if block == 0 else count - 1
        return call(
            functools.partial(cross_backward_kernel, groups, block),
            [((sentences, places, 2 * width), BF16), ((width, half), BF16)],
            [
                ((sentences, places, 2 * width), BF16),
                ((sentences, places, 2 * TILE), F32),
                ((half // TILE, 2 * TILE, width), BF16),
                ((half // TILE, 2 * TILE, width), BF16),
                ((sentences, width, places), BF16),
                ((SLAB, half), F32),
                ((sentences, places, 2 * SLAB), F32),
                pltpu.SemaphoreType.DMA((1,)),
            ],
            3,
            spot,
            tgt_len,
            src_len,
            query,
            cross_norm,
            cross_along,
            grad_attn,
            pair_all,
            work=10,
            vmem=24 if block == 0 else 32,
            hbm_in=1,
        )

    pair_grad_long, query_grad_t_long = cross_backward(0)
    came_one, pair_grad_long = lax.optimization_barrier((came_one, pair_grad_long))
    parts_one = first_sum.first_split(spot, keep_one, came_one)
    parts_one, pair_all = lax.optimization_barrier((parts_one, pair_all))
    parts_one = first_sum.swap(parts_one, 0)
    pair_grad_rest, query_grad_t_rest = cross_backward(1)
    (wkv_grad,) = call(
        functools.partial(memory_weight_kernel, groups),
        [((2, width, width), BF16)],
        [((width, 2 * width), F32)],
        2,
        spot,
        tgt_len,
        pair_grad_long,
        pair_grad_rest,
        memory,
        *came,
        work=1,
        vmem=32,
    )
    grad_mine, *grad_away = call(
        functools.partial(memory_grad_kernel, groups),
        [((count, span, width), BF16)] * groups,
        [],
        2,
        spot,
        tgt_len,
        pair_grad_long,
        pair_grad_rest,
        wkv_cross,
        work=0.01,
        vmem=32,
    )
    parts_one, wkv_grad, grad_away = lax.optimization_barrier((parts_one, wkv_grad, grad_away))
    parts_one = first_sum.split(1, spot, parts_one)
    parts_one, wkv_grad, grad_away = lax.optimization_barrier((parts_one, wkv_grad, grad_away))
    parts_one = first_sum.swap(parts_one, 1)
    keep_mid, send_mid, grad_hidden_one, grad_self = call(
        first_norm_backward_kernel,
        [
            ((2 * width + LN_ROWS, width), BF16),
            ((2 * width + LN_ROWS, width), BF16),
            ((rows, width), F32),
            ((rows, width), BF16),
        ],
        [],
        1,
        spot,
        hidden_one,
        query_grad_t_long,
        query_grad_t_rest,
        grad_hidden_two,
        wq_cross,
        w_out,
        self_attn_t,
        ln_gain,
        ln_bias,
        ln_part,
        wkv_grad,
        work=10,
        vmem=24,
    )
    grad_triple, *last = call(
        self_backward_kernel,
        [((rows, 3 * width), BF16)] + [(((width + short) // LAST_PARTS, width), BF16)] * (2 * LAST_PARTS),
        [
            ((tiles, half, 2 * TILE), F32),
            ((tiles, 2 * TILE, width), BF16),
            ((tiles, 2 * TILE, width), BF16),
            ((width, rows), BF16),
            ((width, rows), BF16),
        ],
        2,
        spot,
        tgt_len,
        qkv,
        self_norm,
        grad_self,
        sorted_rows,
        work=0.1,
        vmem=28,
    )
    backs = [
        lax.ppermute(grads, "mem", [(k, (k - 1 - i) % groups) for k in range(groups)])
        for i, grads in enumerate(grad_away)
    ]
    came_mid = second_sum.core_swap(send_mid)
    parts_one, last, came_mid = lax.optimization_barrier((parts_one, last, came_mid))
    keep_last = last[:LAST_PARTS]
    came_last = [second_sum.core_swap(part) for part in last[LAST_PARTS:]]
    parts_one = first_sum.swap(first_sum.split(2, spot, parts_one), 2)
    (grad_target,) = call(
        target_kernel,
        [((rows, width), BF16)],
        [],
        2,
        spot,
        tgt_len,
        grad_triple,
        w_qkv,
        grad_hidden_one,
        work=0.01,
        vmem=16,
    )
    came_last, grad_target = lax.optimization_barrier((came_last, grad_target))
    parts_two = second_sum.first_split(
        spot, keep_mid, came_mid, *[part for both in zip(keep_last, came_last) for part in both]
    )
    parts_two, parts_one, backs = lax.optimization_barrier((parts_two, parts_one, backs))
    parts_two = second_sum.swap(parts_two, 0)
    spread_one = first_sum.spread(2, first_sum.total(parts_one)[0])
    parts_two, spread_one = lax.optimization_barrier((parts_two, spread_one))
    parts_two = second_sum.swap(second_sum.split(1, spot, parts_two), 1)
    spread_one = first_sum.spread(1, first_sum.join(2, spot, spread_one))
    parts_two, spread_one = lax.optimization_barrier((parts_two, spread_one))
    parts_two = second_sum.swap(second_sum.split(2, spot, parts_two), 2)
    spread_one = first_sum.spread(0, first_sum.join(1, spot, spread_one))
    sum_two, norm_sums = second_sum.total(parts_two)
    spread_two = second_sum.spread(2, sum_two)
    spread_two, spread_one = lax.optimization_barrier((spread_two, spread_one))
    other_one = [first_sum.core_swap(array) for array in spread_one]
    spread_two = second_sum.spread(1, second_sum.join(2, spot, spread_two))
    chunks = hidden_width // width
    pieces = []
    for chunk in range(chunks):
        side, here = chunk // (chunks // 2), chunk % (chunks // 2)
        pieces.append((side, here * width, width, 0, chunk * width, 0))
        pieces.append((side, (chunks // 2 + here) * width, width, 1, 0, chunk * width))
    for side in range(2):
        pieces.append((side, chunks * width, short, 2, side * short, 0))
    grad_w_down, grad_w_up, grad_wo = first_sum.finish(
        spot,
        spread_one,
        other_one,
        pieces,
        [((hidden_width, width), F32), ((width, hidden_width), F32), ((width, width), F32)],
    )
    spread_two, grad_w_down = lax.optimization_barrier((spread_two, grad_w_down))
    spread_two = second_sum.spread(0, second_sum.join(1, spot, spread_two))
    other_two = [second_sum.core_swap(array) for array in spread_two]
    pieces = [
        (0, 0, width, 0, 0, 0),
        (0, width, width, 1, 0, 0),
        (0, 2 * width, width, 2, 0, 0),
        (0, 3 * width, short, 2, 0, width),
        (1, 0, width, 1, 0, width),
        (1, width, width, 3, 0, 0),
        (1, 2 * width, short, 2, short, width),
        (1, 2 * width + short, width, 2, 0, 2 * width),
    ]
    grad_wq, grad_wkv, grad_w_qkv, grad_w_out = second_sum.finish(
        spot,
        spread_two,
        other_two,
        pieces,
        [
            ((width, width), F32),
            ((width, 2 * width), F32),
            ((width, 3 * width), F32),
            ((width, width), F32),
        ],
    )
    grad_memory = jnp.zeros(memory.shape, BF16)
    grad_memory = lax.dynamic_update_slice(grad_memory, grad_mine, (me * count, 0, 0))
    for i, grads in enumerate(backs):
        grad_memory = lax.dynamic_update_slice(grad_memory, grads, ((me + i + 1) % groups * count, 0, 0))
    return (
        result_out,
        grad_target,
        grad_memory,
        grad_w_qkv,
        grad_w_out,
        grad_wq,
        grad_wkv,
        grad_wo,
        grad_w_up,
        grad_w_down,
        norm_sums[:3],
        norm_sums[3:6],
    )


def solution(mesh):
    rows_spec = P(("dp", "mem"), None)
    memory_spec = P("dp", "mem", None)
    return jax.shard_map(
        body,
        mesh=mesh,
        in_specs=(rows_spec, memory_spec, rows_spec, P("dp", None), P("dp", None)) + (P(),) * 9,
        out_specs=(rows_spec, rows_spec, memory_spec) + (P(),) * 9,
        check_vma=False,
    )
```

```python
import functools
import math

import jax
import jax.numpy as jnp
from jax import lax
from jax.experimental import pallas as pl
from jax.experimental.pallas import tpu as pltpu
from jax.sharding import PartitionSpec as P

HEADS = 8
PAIRS = HEADS // 2
SLAB = 128
SIDE = SLAB // 2
TILE = 128
MASKED = -1e30
EPSILON = 1e-05
F32 = jnp.float32
BF16 = jnp.bfloat16
MIB = 1024 * 1024
LN_ROWS = 16
LAST_PARTS = 1


def dot(left, right):
    return jnp.dot(left, right, preferred_element_type=F32)


def dot_nt(left, right):
    return lax.dot_general(left, right, (((1,), (1,)), ((), ())), preferred_element_type=F32)


def dot_tn(left, right):
    return lax.dot_general(left, right, (((0,), (0,)), ((), ())), preferred_element_type=F32)


def iota(shape, axis):
    return lax.broadcasted_iota(jnp.int32, shape, axis)


def norm_parts(hidden):
    centre = hidden - jnp.mean(hidden, axis=-1, keepdims=True)
    inverse = lax.rsqrt(jnp.mean(centre * centre, axis=-1, keepdims=True) + EPSILON)
    return centre * inverse, inverse


def norm_backward(upstream, unit, inverse, gain_row):
    scaled = upstream * gain_row
    shifted = (
        scaled
        - jnp.mean(scaled, axis=-1, keepdims=True)
        - unit * jnp.mean(scaled * unit, axis=-1, keepdims=True)
    )
    gain_grad = jnp.sum(upstream * unit, axis=0, keepdims=True)
    return inverse * shifted, gain_grad, jnp.sum(upstream, axis=0, keepdims=True)


def sentence_order(me, len_ref):
    count = len_ref.shape[1]
    lengths = [len_ref[me, k] for k in range(count)]
    longest, best, start, running = jnp.int32(0), lengths[0], jnp.int32(0), jnp.int32(0)
    for k in range(1, count):
        running = running + lengths[k - 1]
        more = lengths[k] > best
        longest = jnp.where(more, k, longest)
        start = jnp.where(more, running, start)
        best = jnp.where(more, lengths[k], best)
    order = [longest] + [jnp.where(k < longest, k, k + 1) for k in range(count - 1)]
    bounds = [jnp.int32(0)]
    for k in range(1, count):
        bounds.append(bounds[-1] + len_ref[me, order[k]])
    return order, start, bounds


def moved_rows(index, start, half):
    return jnp.where(index < start, index + half, jnp.where(index < start + half, index - start, index))


def sort_matrix(rows, start):
    spot = moved_rows(iota((rows, rows), 1), start, rows // 2)
    return jnp.where(spot == iota((rows, rows), 0), 1.0, 0.0).astype(BF16)


def unsort_matrix(rows, start):
    spot = moved_rows(iota((rows, rows), 0), start, rows // 2)
    return jnp.where(spot == iota((rows, rows), 1), 1.0, 0.0).astype(BF16)


def side_masks(width):
    side = iota((1, width), 1) % SLAB
    first = jnp.where(side < SLAB // 2, 1.0, 0.0)
    return first.astype(BF16), (1.0 - first).astype(BF16)


def slab_of(pair, first=0):
    return pl.ds(pl.multiple_of(first + pair * SLAB, SLAB), SLAB)


def pack_heads(out_ref, rows, width):
    even, odd = side_masks(width)
    for t in range(out_ref.shape[0]):
        tile = rows(t * TILE, TILE)
        out_ref[t, :TILE, :] = tile * even
        out_ref[t, TILE:, :] = tile * odd


def fill_self_bias(bias_ref, bounds, half):
    for t in range(bias_ref.shape[0]):
        block, inner = t // (half // TILE), t % (half // TILE)
        key = iota((half, 2 * TILE), 0)
        query = iota((half, 2 * TILE), 1) % TILE + inner * TILE
        allowed = key <= query
        if block == 1:
            first = jnp.zeros((half, 2 * TILE), jnp.int32)
            for bound in bounds[1:-1]:
                first = jnp.where(query >= bound, bound, first)
            allowed = allowed & (key >= first)
        bias_ref[t] = jnp.where(allowed, 0.0, MASKED)


def self_keys(t, half):
    per = half // TILE
    return (t // per) * half, (t % per + 1) * TILE


def fill_live_bias(bias_ref, me, groups, parts, span, src_ref, sentences):
    key = iota((span, bias_ref.shape[2]), 0)
    for j, sentence in enumerate(sentences):
        for i, part in enumerate(parts):
            place = lax.rem(me - part + groups, groups) * span + key
            live = place < src_ref[me, sentence]
            bias_ref[j, pl.ds(i * span, span), :] = jnp.where(live, 0.0, MASKED)


def cross_units(bounds, half):
    units = [(t, 0, None) for t in range(half // TILE)]
    middle = half // 2
    last = jnp.int32(1)
    for bound in bounds[1:-1]:
        last = last + jnp.where(bound < middle, 1, 0)
    ends = bounds[1:]
    column = iota((1, 2 * TILE), 1) % TILE
    for u in range(len(ends) + 1):
        early = u < last
        sentence = jnp.where(early, u + 1, u)
        tile = jnp.where(early, 0, 1)
        low, high = jnp.int32(0), ends[0]
        for k in range(1, len(ends)):
            low = jnp.where(sentence == k + 1, ends[k - 1], low)
            high = jnp.where(sentence == k + 1, ends[k], high)
        row = column + tile * TILE
        units.append((tile + half // TILE, sentence, (row >= low) & (row < high)))
    return units


def own_sides(both):
    return jnp.concatenate([both[:SIDE, :TILE], both[SIDE:, TILE:]], axis=0)


def side_rows(row):
    even = jnp.broadcast_to(row[:, :TILE], (SIDE, TILE))
    return jnp.concatenate([even, jnp.broadcast_to(row[:, TILE:], (SIDE, TILE))], axis=0)


def tile_columns(tile):
    if isinstance(tile, int):
        return pl.ds(tile * TILE, TILE)
    return pl.ds(pl.multiple_of(tile * TILE, TILE), TILE)


def self_forward_kernel(
    groups,
    me_ref,
    len_ref,
    src_ref,
    target_ref,
    w_qkv_ref,
    w_out_ref,
    wq_ref,
    gain_ref,
    bias_row_ref,
    memory_ref,
    wkv_ref,
    sorted_ref,
    qkv_ref,
    norm_ref,
    attn_t_ref,
    hidden_ref,
    query_ref,
    part_ref,
    top_ref,
    sum_ref,
    pair_out_ref,
    bias_ref,
    live_ref,
    q_pack_ref,
    value_t_ref,
    cross_value_t_ref,
    pair_ref,
    copy_sem,
):
    rows, width = target_ref.shape
    half = rows // 2
    me = me_ref[0]
    order, start, bounds = sentence_order(me, len_ref)
    count, span = pair_ref.shape[0], pair_ref.shape[1]
    copies = []
    for j in range(count):
        block = memory_ref[me * count + order[j]]
        pair_ref[j] = dot(block, wkv_ref[...]).astype(BF16)
        copy = pltpu.make_async_copy(
            pair_ref.at[j], pair_out_ref.at[j, pl.ds(0, span), :], copy_sem.at[j]
        )
        copy.start()
        copies.append(copy)
    sorted_rows = dot(sort_matrix(rows, start), target_ref[...]).astype(BF16)
    sorted_ref[...] = sorted_rows
    fill_self_bias(bias_ref, bounds, half)
    queries = (dot(sorted_rows, w_qkv_ref[:, :width]).astype(BF16) * 0.125).astype(BF16)
    qkv_ref[:, :width] = queries
    pack_heads(q_pack_ref, lambda first, size: queries[first : first + size], width)
    qkv_ref[:, width : 2 * width] = dot(sorted_rows, w_qkv_ref[:, width : 2 * width]).astype(BF16)
    values = dot(sorted_rows, w_qkv_ref[:, 2 * width :]).astype(BF16)
    qkv_ref[:, 2 * width :] = values
    value_t_ref[...] = values.T
    tiles = rows // TILE

    def self_step(pair, carry):
        slab = slab_of(pair)
        for t in range(tiles):
            first, size = self_keys(t, half)
            keys = qkv_ref[pl.ds(first, size), slab_of(pair, width)]
            scores = dot_nt(keys, q_pack_ref[t, :, slab]) + bias_ref[t, :size, :]
            top = jnp.max(scores, axis=0, keepdims=True)
            weights = jnp.exp(scores - top)
            total = jnp.sum(weights, axis=0, keepdims=True)
            probs = (weights * (1.0 / total)).astype(BF16)
            both = dot(value_t_ref[slab, pl.ds(first, size)], probs)
            attn_t_ref[slab, tile_columns(t)] = own_sides(both).astype(BF16)
            norm_ref[pl.ds(pair * tiles + t, 1), :] = top + jnp.log(total)
        return carry

    lax.fori_loop(0, PAIRS, self_step, 0)
    hidden = sorted_rows.astype(F32) + dot(attn_t_ref[...].T, w_out_ref[...])
    hidden_ref[...] = hidden
    unit, _ = norm_parts(hidden)
    normed = (unit * gain_ref[0:1] + bias_row_ref[0:1]).astype(BF16)
    query_ref[...] = (dot(normed, wq_ref[...]).astype(BF16) * 0.125).astype(BF16)

    pack_heads(q_pack_ref, lambda first, size: query_ref[first : first + size, :], width)
    fill_live_bias(live_ref, me, groups, [0], span, src_ref, order)
    for j in range(count):
        cross_value_t_ref[j] = pair_ref[j, :, width:].T
    units = cross_units(bounds, half)

    def cross_step(pair, carry):
        slab = slab_of(pair)
        for tile, sentence, columns in units:
            scores = dot_nt(pair_ref[sentence, :, slab], q_pack_ref[tile, :, slab]) + live_ref[sentence]
            top = jnp.max(scores, axis=0, keepdims=True)
            weights = jnp.exp(scores - top)
            total = jnp.sum(weights, axis=0, keepdims=True)
            result = own_sides(dot(cross_value_t_ref[sentence, slab, :], weights.astype(BF16)))
            here = tile_columns(tile)
            row = pl.ds(pair * tiles + tile, 1)
            if columns is not None:
                result = jnp.where(columns[:, :TILE], result, part_ref[slab, here])
                top = jnp.where(columns, top, top_ref[row, :])
                total = jnp.where(columns, total, sum_ref[row, :])
            part_ref[slab, here] = result
            top_ref[row, :] = top
            sum_ref[row, :] = total
        return carry

    part_ref[...] = jnp.zeros_like(part_ref)
    top_ref[...] = jnp.zeros_like(top_ref)
    sum_ref[...] = jnp.ones_like(sum_ref)
    lax.fori_loop(0, PAIRS, cross_step, 0)
    for copy in copies:
        copy.wait()


def middle_kernel(
    groups,
    me_ref,
    len_ref,
    src_ref,
    hidden_one_ref,
    query_ref,
    part_ref,
    top_ref,
    sum_ref,
    wkv_ref,
    gain_ref,
    bias_row_ref,
    wo_hbm,
    w_up_hbm,
    w_down_hbm,
    grad_out_hbm,
    pair_in_hbm,
    *refs,
):
    came_refs = refs[: groups - 1]
    (
        out_ref,
        norm_ref,
        along_ref,
        keep_hbm,
        send_hbm,
        grad_hidden_ref,
        grad_attn_ref,
        ln_ref,
        pair_hbm,
        wo_ref,
        w_up_ref,
        w_down_ref,
        grad_out_ref,
        pair_ref,
        keep_ref,
        send_ref,
        live_ref,
        q_pack_ref,
        value_t_ref,
        attn_t_ref,
        active_ref,
        slope_ref,
        total_ref,
        load_sem,
        pair_sem,
        store_sem,
    ) = refs[groups - 1 :]
    rows, width = hidden_one_ref.shape
    half = rows // 2
    me = me_ref[0]
    count, away = pair_ref.shape[0], pair_ref.shape[1]
    span = away // (groups - 1)
    loads = [
        pltpu.make_async_copy(source, there, load_sem.at[i])
        for i, (source, there) in enumerate(
            [(wo_hbm, wo_ref), (w_up_hbm, w_up_ref), (w_down_hbm, w_down_ref), (grad_out_hbm, grad_out_ref)]
        )
    ]
    for copy in loads:
        copy.start()
    order, start, bounds = sentence_order(me, len_ref)
    fill_live_bias(live_ref, me, groups, list(range(1, groups)), span, src_ref, order)
    pack_heads(q_pack_ref, lambda first, size: query_ref[first : first + size, :], width)
    pair_copies = []
    for j in range(count):
        for part in range(1, groups):
            block = came_refs[part - 1][order[j]]
            pair_ref[j, pl.ds((part - 1) * span, span), :] = dot(block, wkv_ref[...]).astype(BF16)
        value_t_ref[j] = pair_ref[j, :, width:].T
        copy = pltpu.make_async_copy(pair_ref.at[j], pair_hbm.at[j, pl.ds(span, away), :], pair_sem.at[j])
        copy.start()
        pair_copies.append(copy)
    units = cross_units(bounds, half)
    tiles = rows // TILE

    def cross_step(pair, carry):
        slab = slab_of(pair)
        for tile, sentence, columns in units:
            here = tile_columns(tile)
            row = pl.ds(pair * tiles + tile, 1)
            scores = dot_nt(pair_ref[sentence, :, slab], q_pack_ref[tile, :, slab]) + live_ref[sentence]
            before = top_ref[row, :]
            top = jnp.maximum(jnp.max(scores, axis=0, keepdims=True), before)
            weights = jnp.exp(scores - top)
            scale = jnp.exp(before - top)
            total = jnp.sum(weights, axis=0, keepdims=True) + sum_ref[row, :] * scale
            result = own_sides(dot(value_t_ref[sentence, slab, :], weights.astype(BF16)))
            result = (result + part_ref[slab, here] * side_rows(scale)) * side_rows(1.0 / total)
            norm = top + jnp.log(total)
            if columns is not None:
                result = jnp.where(columns[:, :TILE], result, attn_t_ref[slab, here])
                norm = jnp.where(columns, norm, norm_ref[row, :])
            attn_t_ref[slab, here] = result
            norm_ref[row, :] = norm
        return carry

    attn_t_ref[...] = jnp.zeros_like(attn_t_ref)
    norm_ref[...] = jnp.zeros_like(norm_ref)
    lax.fori_loop(0, PAIRS, cross_step, 0)
    attn_t_low = attn_t_ref[...].astype(BF16)
    loads[0].wait()
    unit_one, _ = norm_parts(hidden_one_ref[...])
    normed_one = unit_one * gain_ref[0:1] + bias_row_ref[0:1]
    hidden_two = normed_one + dot(attn_t_low.T, wo_ref[...])
    unit_two, inverse_two = norm_parts(hidden_two)
    normed_two = unit_two * gain_ref[1:2] + bias_row_ref[1:2]
    normed_two_low = normed_two.astype(BF16)
    total_ref[...] = normed_two
    chunk = width
    chunks = w_down_ref.shape[0] // chunk
    loads[1].wait()
    loads[2].wait()

    def up_step(c, carry):
        cols = pl.ds(pl.multiple_of(c * chunk, chunk), chunk)
        upper = dot(normed_two_low, w_up_ref[:, cols])
        sigma = 1.0 / (1.0 + jnp.exp(-upper))
        active = (upper * sigma).astype(BF16)
        active_ref[:, cols] = active
        slope_ref[:, cols] = sigma * (1.0 + upper * (1.0 - sigma))
        total_ref[...] += dot(active, w_down_ref[cols, :])
        return carry

    lax.fori_loop(0, chunks, up_step, 0)
    unit_three, inverse_three = norm_parts(total_ref[...])
    result = (unit_three * gain_ref[2:3] + bias_row_ref[2:3]).astype(BF16)
    out_ref[...] = dot(unsort_matrix(rows, start), result).astype(BF16)
    loads[3].wait()
    upstream = dot(sort_matrix(rows, start), grad_out_ref[...])
    grad_three, gain_three, bias_three = norm_backward(upstream, unit_three, inverse_three, gain_ref[2:3])
    grad_down = grad_three.astype(BF16)
    total_ref[...] = grad_three
    normed_two_t = normed_two_low.T

    def down_step(c, carry):
        cols = pl.ds(pl.multiple_of(c * chunk, chunk), chunk)
        grad_upper = (dot_nt(grad_down, w_down_ref[cols, :]) * slope_ref[:, cols]).astype(BF16)
        down_part = dot_tn(active_ref[:, cols], grad_down).astype(BF16)
        up_part = dot(normed_two_t, grad_upper).astype(BF16)
        here = lax.rem(c, chunks // 2)
        down_rows = pl.ds(pl.multiple_of(here * chunk, chunk), chunk)
        up_rows = pl.ds(pl.multiple_of((chunks // 2 + here) * chunk, chunk), chunk)
        mine = c // (chunks // 2) == me_ref[1]

        @pl.when(mine)
        def _():
            keep_ref[down_rows, :] = down_part
            keep_ref[up_rows, :] = up_part

        @pl.when(jnp.logical_not(mine))
        def _():
            send_ref[down_rows, :] = down_part
            send_ref[up_rows, :] = up_part

        total_ref[...] += dot_nt(grad_upper, w_up_ref[:, cols])
        return carry

    lax.fori_loop(0, chunks, down_step, 0)
    most = chunks * chunk
    stores = [
        pltpu.make_async_copy(ref.at[pl.ds(first, size)], there.at[pl.ds(first, size)], store_sem.at[i])
        for i, (ref, there, first, size) in enumerate(
            [
                (send_ref, send_hbm, 0, most),
                (keep_ref, keep_hbm, 0, most),
                (send_ref, send_hbm, most, keep_ref.shape[0] - most),
                (keep_ref, keep_hbm, most, keep_ref.shape[0] - most),
            ]
        )
    ]
    stores[0].start()
    stores[1].start()
    grad_two, gain_two, bias_two = norm_backward(total_ref[...], unit_two, inverse_two, gain_ref[1:2])
    grad_two_low = grad_two.astype(BF16)
    wo_grad = dot(attn_t_low, grad_two_low).astype(BF16)
    core = me_ref[1]
    low, high = wo_grad[: width // 2], wo_grad[width // 2 :]
    tail = pl.ds(most, width // 2)
    keep_ref[tail, :] = jnp.where(core == 0, low, high)
    send_ref[tail, :] = jnp.where(core == 0, high, low)
    used = most + width // 2
    if keep_ref.shape[0] > used:
        keep_ref[used:, :] = jnp.zeros((keep_ref.shape[0] - used, width), BF16)
        send_ref[used:, :] = jnp.zeros((keep_ref.shape[0] - used, width), BF16)
    stores[2].start()
    stores[3].start()
    grad_hidden_ref[...] = grad_two
    grad_attn = dot_nt(grad_two_low, wo_ref[...]).astype(BF16)
    grad_attn_ref[...] = grad_attn
    product = grad_attn.T.astype(F32) * attn_t_ref[...]
    for pair in range(PAIRS):
        for side in range(2):
            first = pair * SLAB + side * SIDE
            along = jnp.sum(product[first : first + SIDE], axis=0, keepdims=True)
            for t in range(tiles):
                along_ref[pair * tiles + t : pair * tiles + t + 1, side * TILE : (side + 1) * TILE] = along[
                    :, t * TILE : (t + 1) * TILE
                ]
    ln_ref[...] = jnp.concatenate([gain_two, gain_three, bias_two, bias_three], axis=0)
    for copy in pair_copies + stores:
        copy.wait()


def cross_backward_kernel(
    groups,
    block,
    me_ref,
    len_ref,
    src_ref,
    query_ref,
    norm_ref,
    along_ref,
    grad_attn_ref,
    pair_hbm,
    pair_grad_ref,
    query_grad_t_ref,
    pair_ref,
    live_ref,
    q_pack_ref,
    g_pack_ref,
    key_t_ref,
    query_sum_ref,
    sum_ref,
    load_sem,
):
    rows, width = query_ref.shape
    half = rows // 2
    me = me_ref[0]
    sentences, places = pair_ref.shape[0], pair_ref.shape[1]
    first_sentence = 0 if block == 0 else 1
    load = pltpu.make_async_copy(pair_hbm.at[pl.ds(first_sentence, sentences)], pair_ref, load_sem.at[0])
    load.start()
    order, start, bounds = sentence_order(me, len_ref)
    mine = order[:1] if block == 0 else order[1:]
    fill_live_bias(live_ref, me, groups, list(range(groups)), places // groups, src_ref, mine)
    low = block * half
    pack_heads(q_pack_ref, lambda first, size: query_ref[low + first : low + first + size, :], width)
    pack_heads(g_pack_ref, lambda first, size: grad_attn_ref[low + first : low + first + size, :], width)
    tiles, per = rows // TILE, half // TILE
    units = cross_units(bounds, half)
    units = units[:per] if block == 0 else units[per:]
    load.wait()
    for j in range(sentences):
        key_t_ref[j] = pair_ref[j, :, :width].T

    def pair_step(pair, carry):
        slab, value_slab = slab_of(pair), slab_of(pair, width)
        query_sum_ref[...] = jnp.zeros_like(query_sum_ref)
        sum_ref[...] = jnp.zeros_like(sum_ref)
        for tile, sentence, columns in units:
            j = sentence - first_sentence
            t = tile - block * per
            here = tile_columns(t)
            row = pl.ds(pair * tiles + tile, 1)
            q_rows, g_rows = q_pack_ref[t, :, slab], g_pack_ref[t, :, slab]
            norm = norm_ref[row, :]
            if columns is not None:
                norm = jnp.where(columns, norm, -MASKED)
            scores = dot_nt(pair_ref[j, :, slab], q_rows) + live_ref[j]
            probs = jnp.exp(scores - norm)
            grad_probs = dot_nt(pair_ref[j, :, value_slab], g_rows)
            grad_scores = (probs * (grad_probs - along_ref[row, :])).astype(BF16)
            sum_ref[j, :, :SLAB] += dot(grad_scores, q_rows)
            sum_ref[j, :, SLAB:] += dot(probs.astype(BF16), g_rows)
            query_sum_ref[:, here] += own_sides(dot(key_t_ref[j, slab, :], grad_scores))
        query_grad_t_ref[slab, :] = (query_sum_ref[...] * 0.125).astype(BF16)
        pair_grad_ref[:, :, slab] = sum_ref[:, :, :SLAB].astype(BF16)
        pair_grad_ref[:, :, value_slab] = sum_ref[:, :, SLAB:].astype(BF16)
        return carry

    lax.fori_loop(0, PAIRS, pair_step, 0)


def memory_weight_kernel(groups, me_ref, len_ref, pair_grad_long_ref, pair_grad_rest_ref, memory_ref, *refs):
    came_refs = refs[: groups - 1]
    wkv_grad_ref, total_ref = refs[groups - 1 :]
    width = memory_ref.shape[2]
    me = me_ref[0]
    count = len_ref.shape[1]
    span = pair_grad_long_ref.shape[1] // groups
    order, _, _ = sentence_order(me, len_ref)
    for j in range(count):
        pair_grad_ref, here = (pair_grad_long_ref, 0) if j == 0 else (pair_grad_rest_ref, j - 1)
        blocks = [memory_ref[me * count + order[j]]] + [ref[order[j]] for ref in came_refs]
        term = dot_tn(jnp.concatenate(blocks, axis=0), pair_grad_ref[here])
        if j == 0:
            total_ref[...] = term
        else:
            total_ref[...] += term
    wkv_grad_ref[0] = total_ref[:, :width].astype(BF16)
    wkv_grad_ref[1] = total_ref[:, width:].astype(BF16)


def memory_grad_kernel(
    groups, me_ref, len_ref, pair_grad_long_ref, pair_grad_rest_ref, wkv_ref, mine_ref, *away_refs
):
    count = len_ref.shape[1]
    span = pair_grad_long_ref.shape[1] // groups
    order, _, _ = sentence_order(me_ref[0], len_ref)
    for j in range(count):
        pair_grad_ref, here = (pair_grad_long_ref, 0) if j == 0 else (pair_grad_rest_ref, j - 1)
        grads = dot_nt(pair_grad_ref[here], wkv_ref[...]).astype(BF16)
        mine_ref[order[j]] = grads[:span]
        for i, ref in enumerate(away_refs):
            first = span + i * (span // 2)
            ref[order[j]] = grads[first : first + span // 2]


def first_norm_backward_kernel(
    me_ref,
    hidden_one_ref,
    query_grad_t_long_ref,
    query_grad_t_rest_ref,
    grad_hidden_two_ref,
    wq_ref,
    w_out_ref,
    self_attn_t_ref,
    gain_ref,
    bias_row_ref,
    ln_in_ref,
    wkv_grad_ref,
    keep_ref,
    send_ref,
    grad_hidden_ref,
    grad_self_ref,
):
    width = wq_ref.shape[0]
    unit_one, inverse_one = norm_parts(hidden_one_ref[...])
    normed_one = (unit_one * gain_ref[0:1] + bias_row_ref[0:1]).astype(BF16)
    query_grad = jnp.concatenate([query_grad_t_long_ref[...].T, query_grad_t_rest_ref[...].T], axis=0)
    upstream = grad_hidden_two_ref[...] + dot_nt(query_grad, wq_ref[...])
    grad_one, gain_one, bias_one = norm_backward(upstream, unit_one, inverse_one, gain_ref[0:1])
    grad_hidden_ref[...] = grad_one
    grad_one_low = grad_one.astype(BF16)
    grad_self_ref[...] = dot_nt(grad_one_low, w_out_ref[...]).astype(BF16)
    wq_grad = dot_tn(normed_one, query_grad).astype(BF16)
    w_out_grad = dot(self_attn_t_ref[...], grad_one_low).astype(BF16)
    norms = jnp.concatenate(
        [gain_one, ln_in_ref[0:2], bias_one, ln_in_ref[2:4], jnp.zeros((LN_ROWS - 6, width), F32)], axis=0
    ).astype(BF16)

    def halves(low_ref, high_ref):
        low_ref[:width, :] = wq_grad
        low_ref[width : 2 * width, :] = wkv_grad_ref[0]
        high_ref[:width, :] = wkv_grad_ref[1]
        high_ref[width : 2 * width, :] = w_out_grad

    @pl.when(me_ref[1] == 0)
    def _():
        halves(keep_ref, send_ref)

    @pl.when(me_ref[1] != 0)
    def _():
        halves(send_ref, keep_ref)

    keep_ref[2 * width :, :] = norms
    send_ref[2 * width :, :] = norms


def self_backward_kernel(
    me_ref,
    len_ref,
    qkv_ref,
    norm_ref,
    grad_attn_ref,
    sorted_ref,
    grad_triple_ref,
    *refs,
):
    keep_refs, send_refs = refs[:LAST_PARTS], refs[LAST_PARTS : 2 * LAST_PARTS]
    self_backward(
        me_ref,
        len_ref,
        qkv_ref,
        norm_ref,
        grad_attn_ref,
        sorted_ref,
        grad_triple_ref,
        keep_refs,
        send_refs,
        *refs[2 * LAST_PARTS :],
    )


def self_backward(
    me_ref,
    len_ref,
    qkv_ref,
    norm_ref,
    grad_attn_ref,
    sorted_ref,
    grad_triple_ref,
    keep_refs,
    send_refs,
    bias_ref,
    q_pack_ref,
    g_pack_ref,
    key_t_ref,
    query_grad_t_ref,
):
    rows, width = sorted_ref.shape
    half = rows // 2
    _, _, bounds = sentence_order(me_ref[0], len_ref)
    fill_self_bias(bias_ref, bounds, half)
    pack_heads(q_pack_ref, lambda first, size: qkv_ref[first : first + size, :width], width)
    pack_heads(g_pack_ref, lambda first, size: grad_attn_ref[first : first + size, :], width)
    key_t_ref[...] = qkv_ref[:, width : 2 * width].T
    tiles, per = rows // TILE, half // TILE

    def pair_step(pair, carry):
        slab, key_slab, value_slab = slab_of(pair), slab_of(pair, width), slab_of(pair, 2 * width)
        sums = [[None, None] for _ in range(tiles)]
        for t in range(tiles):
            first, size = self_keys(t, half)
            span = pl.ds(first, size)
            q_rows, g_rows = q_pack_ref[t, :, slab], g_pack_ref[t, :, slab]
            scores = dot_nt(qkv_ref[span, key_slab], q_rows) + bias_ref[t, :size, :]
            probs = jnp.exp(scores - norm_ref[pl.ds(pair * tiles + t, 1), :])
            grad_probs = dot_nt(qkv_ref[span, value_slab], g_rows)
            along = jnp.sum(probs * grad_probs, axis=0, keepdims=True)
            grad_scores = (probs * (grad_probs - along)).astype(BF16)
            parts = dot(grad_scores, q_rows), dot(probs.astype(BF16), g_rows)
            for i in range(size // TILE):
                spot = sums[first // TILE + i]
                for k in range(2):
                    piece = parts[k][i * TILE : (i + 1) * TILE]
                    spot[k] = piece if spot[k] is None else spot[k] + piece
            query_grad_t_ref[slab, tile_columns(t)] = (
                own_sides(dot(key_t_ref[slab, span], grad_scores)) * 0.125
            ).astype(BF16)
        for t in range(tiles):
            grad_triple_ref[pl.ds(t * TILE, TILE), key_slab] = sums[t][0].astype(BF16)
            grad_triple_ref[pl.ds(t * TILE, TILE), value_slab] = sums[t][1].astype(BF16)
        return carry

    lax.fori_loop(0, PAIRS, pair_step, 0)
    grad_triple_ref[:, :width] = query_grad_t_ref[...].T
    sorted_t = sorted_ref[...].T
    grads = [
        dot(sorted_t, grad_triple_ref[:, part * width : (part + 1) * width]).astype(BF16)
        for part in range(3)
    ]
    short = width // 2

    low = jnp.concatenate([grads[0], grads[1][:short]], axis=0)
    high = jnp.concatenate([grads[1][short:], grads[2]], axis=0)
    size = keep_refs[0].shape[0]

    def halves(low_refs, high_refs):
        for i in range(LAST_PARTS):
            low_refs[i][...] = low[i * size : (i + 1) * size]
            high_refs[i][...] = high[i * size : (i + 1) * size]

    @pl.when(me_ref[1] == 0)
    def _():
        halves(keep_refs, send_refs)

    @pl.when(me_ref[1] != 0)
    def _():
        halves(send_refs, keep_refs)


def target_kernel(me_ref, len_ref, grad_triple_ref, w_qkv_ref, grad_hidden_ref, grad_target_ref):
    rows = grad_hidden_ref.shape[0]
    _, start, _ = sentence_order(me_ref[0], len_ref)
    result = grad_hidden_ref[...] + dot_nt(grad_triple_ref[...], w_qkv_ref[...])
    grad_target_ref[...] = dot(unsort_matrix(rows, start), result.astype(BF16)).astype(BF16)


def tree_sum(terms):
    while len(terms) > 1:
        terms = [terms[i] + terms[i + 1] for i in range(0, len(terms), 2)]
    return terms[0]


def rows_of(ref, first, count):
    return ref[pl.ds(pl.multiple_of(first, 16), count), :].astype(F32)


def first_split_kernel(segments, ln, peers, spot_ref, *refs):
    ins, outs, sum_ref = refs[: 2 * segments], refs[2 * segments : -1], refs[-1]
    extra = LN_ROWS if ln else 0
    size = outs[0].shape[0] - extra
    used = 0
    for i in range(segments):
        keep_ref, came_ref = ins[2 * i], ins[2 * i + 1]
        count = keep_ref.shape[0] - (extra if i == 0 else 0)
        sum_ref[used : used + count, :] = (rows_of(keep_ref, 0, count) + rows_of(came_ref, 0, count)).astype(BF16)
        if i == 0 and ln:
            tail = (rows_of(keep_ref, count, LN_ROWS) + rows_of(came_ref, count, LN_ROWS)).astype(BF16)
        used += count
    if sum_ref.shape[0] > used:
        sum_ref[used:, :] = jnp.zeros((sum_ref.shape[0] - used, sum_ref.shape[1]), BF16)
    for d, out in enumerate(outs):
        out[:size, :] = sum_ref[pl.ds(pl.multiple_of((spot_ref[2] ^ d) * size, 16), size), :]
        if ln:
            out[size:, :] = tail


def split_kernel(stage, ln, peers, spot_ref, *refs):
    ins, outs = refs[:peers], refs[peers:]
    extra = LN_ROWS if ln else 0
    size = outs[0].shape[0] - extra
    if ln:
        tail = tree_sum([rows_of(ref, size * len(outs), LN_ROWS) for ref in ins]).astype(BF16)
    for d, out in enumerate(outs):
        first = (spot_ref[2 + stage] ^ d) * size
        out[:size, :] = tree_sum([rows_of(ref, first, size) for ref in ins]).astype(BF16)
        if ln:
            out[size:, :] = tail


def total_kernel(ln, count, *refs):
    ins, outs = refs[:count], refs[count:]
    size = outs[0].shape[0]
    outs[0][...] = tree_sum([rows_of(ref, 0, size) for ref in ins]).astype(BF16)
    if ln:
        outs[1][...] = tree_sum([rows_of(ref, size, LN_ROWS) for ref in ins])


def join_kernel(stage, spot_ref, *refs):
    out_ref = refs[-1]
    for d, ref in enumerate(refs[:-1]):
        size = ref.shape[0]
        out_ref[pl.ds(pl.multiple_of((spot_ref[2 + stage] ^ d) * size, 16), size), :] = ref[...]


def finish_kernel(peers, twisted, pieces, spot_ref, *refs):
    mine, others, outs, both_ref = refs[:peers], refs[peers : 2 * peers], refs[2 * peers : -1], refs[-1]
    core = spot_ref[1]
    for half, arrays, here in ((core, mine, spot_ref[2]), (1 - core, others, spot_ref[3 if twisted else 2])):
        for d, ref in enumerate(arrays):
            size = ref.shape[0]
            both_ref[half, pl.ds(pl.multiple_of((here ^ d) * size, 16), size), :] = ref[...]
    width = both_ref.shape[2]
    for half, first, rows, out, row, col in pieces:
        outs[out][row : row + rows, col : col + width] = both_ref[half, first : first + rows, :].astype(F32)


class Summing:
    def __init__(self, rows, width, ln):
        self.width, self.ln = width, ln
        self.dp, self.mem = lax.axis_size("dp"), lax.axis_size("mem")
        z_size = 4
        x_size = self.dp // (2 * z_size)
        self.sizes = (x_size, self.mem, z_size)
        self.twisted = x_size == self.mem
        self.chunk = -(-rows // (16 * math.prod(self.sizes))) * 16
        self.rows = self.chunk * math.prod(self.sizes)

    def after(self, stage):
        return self.rows // math.prod(self.sizes[:stage])

    def axis(self, stage, core):
        return 1 - stage if self.twisted and core == 1 and stage < 2 else stage

    def coords(self, dp, mem):
        return [dp // 2 % self.sizes[0], mem, dp // (2 * self.sizes[0])], dp % 2

    def spot(self, me, dp):
        (x, mem, z), core = self.coords(dp, me)
        if self.twisted:
            x, mem = jnp.where(core == 0, x, mem), jnp.where(core == 0, mem, x)
        return jnp.stack([me, core, x, mem, z]).astype(jnp.int32)

    def permute(self, array, stage, offset):
        pairs = []
        for dp in range(self.dp):
            for mem in range(self.mem):
                spots, core = self.coords(dp, mem)
                if stage is None:
                    core ^= offset
                else:
                    spots[self.axis(stage, core)] ^= offset
                to_dp = (spots[2] * self.sizes[0] + spots[0]) * 2 + core
                pairs.append((dp * self.mem + mem, to_dp * self.mem + spots[1]))
        return lax.ppermute(array, ("dp", "mem"), pairs)

    def core_swap(self, send):
        return self.permute(send, None, 1)

    def swap(self, arrays, stage):
        return [arrays[0]] + [self.permute(array, stage, d) for d, array in enumerate(arrays) if d > 0]

    def spread(self, stage, array):
        return [array] + [self.permute(array, stage, d) for d in range(1, self.sizes[stage])]

    def messages(self, stage):
        size = self.after(stage + 1) + (LN_ROWS if self.ln else 0)
        return [((size, self.width), BF16)] * self.sizes[stage]

    def first_split(self, spot, *arrays):
        kernel = functools.partial(first_split_kernel, len(arrays) // 2, self.ln, self.sizes[0])
        return call(kernel, self.messages(0), [((self.rows, self.width), BF16)], 1, spot, *arrays, work=0.01)

    def split(self, stage, spot, arrays):
        kernel = functools.partial(split_kernel, stage, self.ln, self.sizes[stage - 1])
        return call(kernel, self.messages(stage), [], 1, spot, *arrays, work=0.01)

    def total(self, arrays):
        outs = [((self.chunk, self.width), BF16)]
        if self.ln:
            outs.append(((LN_ROWS, self.width), F32))
        return call(functools.partial(total_kernel, self.ln, self.sizes[2]), outs, [], 0, *arrays, work=0.01)

    def join(self, stage, spot, arrays):
        outs = [((self.after(stage), self.width), BF16)]
        return call(functools.partial(join_kernel, stage), outs, [], 1, spot, *arrays, work=0.01)[0]

    def finish(self, spot, mine, others, pieces, outs):
        kernel = functools.partial(finish_kernel, self.sizes[0], self.twisted, pieces)
        scratch = [((2, self.rows, self.width), BF16)]
        return call(kernel, outs, scratch, 1, spot, *mine, *others, work=1)


def call(kernel, outs, scratch, scalars, *arrays, work=0.5, vmem=0, hbm_in=0, hbm_out=0, aliases=None):
    plain = len(arrays) - scalars - hbm_in
    if not vmem:
        blocks = [(array.shape, array.dtype) for array in arrays[scalars:]] + outs + scratch
        vmem = max(16, sum(math.prod(shape) * jnp.dtype(kind).itemsize for shape, kind in blocks) // MIB + 7)
    specs = [pl.BlockSpec(memory_space=pltpu.SMEM)] * scalars
    specs = specs + [pl.BlockSpec(memory_space=pltpu.VMEM)] * plain
    specs = specs + [pl.BlockSpec(memory_space=pl.ANY)] * hbm_in
    out_specs = [pl.BlockSpec(memory_space=pltpu.VMEM)] * (len(outs) - hbm_out)
    out_specs = out_specs + [pl.BlockSpec(memory_space=pl.ANY)] * hbm_out
    return pl.pallas_call(
        kernel,
        out_shape=[jax.ShapeDtypeStruct(shape, kind) for shape, kind in outs],
        in_specs=specs,
        out_specs=out_specs,
        scratch_shapes=[pltpu.VMEM(*entry) if isinstance(entry, tuple) else entry for entry in scratch],
        input_output_aliases=aliases or {},
        compiler_params=pltpu.CompilerParams(vmem_limit_bytes=vmem * MIB),
        cost_estimate=pl.CostEstimate(flops=int(work * 1e9), bytes_accessed=int(work * 3e6), transcendentals=0),
    )(*arrays)


def middle(
    groups, first_sum, stats, spot, tgt_len, src_len, hidden_one, query, part, part_top, part_sum, wkv_cross,
    ln_gain, ln_bias, wo_cross, w_up, w_down, grad_out, pair_mine, came,
):
    rows, width = hidden_one.shape
    half, tiles = rows // 2, rows // TILE
    hidden_width = w_down.shape[0]
    count, places, _ = pair_mine.shape
    away = places // groups * (groups - 1)
    arrays = [spot, tgt_len, src_len, hidden_one, query, part, part_top, part_sum, wkv_cross, ln_gain, ln_bias]
    stay = [wo_cross, w_up, w_down, grad_out, pair_mine]

    def kernel(*refs):
        ins, refs = refs[: len(arrays)], refs[len(arrays) :]
        came_refs, refs = refs[: len(came)], refs[len(came) :]
        stay_refs, refs = refs[: len(stay)], refs[len(stay) :]
        outs, refs = refs[:9], refs[9:]
        middle_kernel(groups, *ins, *stay_refs, *came_refs, *outs[:3], *outs[6:8], *outs[3:6], outs[8], *refs)

    result_out, cross_norm, cross_along, grad_hidden_two, grad_attn, ln_part, keep_one, send_one, pair_all = call(
        kernel,
        [
            ((rows, width), BF16),
            (stats, F32),
            (stats, F32),
            ((rows, width), F32),
            ((rows, width), BF16),
            ((4, width), F32),
            ((first_sum.rows, width), BF16),
            ((first_sum.rows, width), BF16),
            ((count, places, 2 * width), BF16),
        ],
        [
            ((width, width), BF16),
            ((width, hidden_width), BF16),
            ((hidden_width, width), BF16),
            ((rows, width), BF16),
            ((count, away, 2 * width), BF16),
            ((first_sum.rows, width), BF16),
            ((first_sum.rows, width), BF16),
            ((count, away, 2 * TILE), F32),
            ((tiles, 2 * TILE, width), BF16),
            ((count, width, away), BF16),
            ((width, rows), F32),
            ((rows, hidden_width), BF16),
            ((rows, hidden_width), F32),
            ((rows, width), F32),
            pltpu.SemaphoreType.DMA((4,)),
            pltpu.SemaphoreType.DMA((count,)),
            pltpu.SemaphoreType.DMA((4,)),
        ],
        3,
        *arrays,
        *came,
        *stay,
        vmem=60,
        hbm_in=len(stay),
        hbm_out=3,
        aliases={len(arrays) + len(came) + len(stay) - 1: 8},
    )
    return result_out, cross_norm, cross_along, keep_one, send_one, grad_hidden_two, grad_attn, ln_part, pair_all


def body(
    target,
    memory,
    grad_out,
    tgt_len,
    src_len,
    w_qkv,
    w_out,
    wq_cross,
    wkv_cross,
    wo_cross,
    w_up,
    w_down,
    ln_gain,
    ln_bias,
):
    rows, width = target.shape
    half = rows // 2
    tiles = rows // TILE
    hidden_width = w_down.shape[0]
    groups = lax.axis_size("mem")
    me = lax.axis_index("mem")
    count = tgt_len.shape[1]
    span = memory.shape[1]
    places, away = groups * span, (groups - 1) * span
    dp = lax.axis_index("dp")
    short = width // 2
    first_sum = Summing(hidden_width + short, width, False)
    second_sum = Summing(3 * width + short, width, True)
    spot = first_sum.spot(me, dp)
    stats = (PAIRS * tiles, 2 * TILE)

    came = []
    for shift in range(1, groups):
        pairs = [(i, (i + shift) % groups) for i in range(groups)]
        sent = lax.dynamic_slice_in_dim(memory, ((me + shift) % groups) * count, count, 0)
        came.append(lax.ppermute(sent, "mem", pairs))

    sorted_rows, qkv, self_norm, self_attn_t, hidden_one, query, part, part_top, part_sum, pair_mine = call(
        functools.partial(self_forward_kernel, groups),
        [
            ((rows, width), BF16),
            ((rows, 3 * width), BF16),
            (stats, F32),
            ((width, rows), BF16),
            ((rows, width), F32),
            ((rows, width), BF16),
            ((width, rows), F32),
            (stats, F32),
            (stats, F32),
            ((count, places, 2 * width), BF16),
        ],
        [
            ((tiles, half, 2 * TILE), F32),
            ((count, span, 2 * TILE), F32),
            ((tiles, 2 * TILE, width), BF16),
            ((width, rows), BF16),
            ((count, width, span), BF16),
            ((count, span, 2 * width), BF16),
            pltpu.SemaphoreType.DMA((count,)),
        ],
        3,
        spot,
        tgt_len,
        src_len,
        target,
        w_qkv,
        w_out,
        wq_cross,
        ln_gain,
        ln_bias,
        memory,
        wkv_cross,
        vmem=60,
        hbm_out=1,
    )
    result_out, cross_norm, cross_along, keep_one, send_one, grad_hidden_two, grad_attn, ln_part, pair_all = middle(
        groups, first_sum, stats, spot, tgt_len, src_len, hidden_one, query, part, part_top, part_sum, wkv_cross,
        ln_gain, ln_bias, wo_cross, w_up, w_down, grad_out, pair_mine, came,
    )
    came_one = first_sum.core_swap(send_one)

    def cross_backward(block):
        sentences = 1 if block == 0 else count - 1
        return call(
            functools.partial(cross_backward_kernel, groups, block),
            [((sentences, places, 2 * width), BF16), ((width, half), BF16)],
            [
                ((sentences, places, 2 * width), BF16),
                ((sentences, places, 2 * TILE), F32),
                ((half // TILE, 2 * TILE, width), BF16),
                ((half // TILE, 2 * TILE, width), BF16),
                ((sentences, width, places), BF16),
                ((SLAB, half), F32),
                ((sentences, places, 2 * SLAB), F32),
                pltpu.SemaphoreType.DMA((1,)),
            ],
            3,
            spot,
            tgt_len,
            src_len,
            query,
            cross_norm,
            cross_along,
            grad_attn,
            pair_all,
            work=10,
            vmem=24 if block == 0 else 32,
            hbm_in=1,
        )

    pair_grad_long, query_grad_t_long = cross_backward(0)
    came_one, pair_grad_long = lax.optimization_barrier((came_one, pair_grad_long))
    parts_one = first_sum.first_split(spot, keep_one, came_one)
    parts_one, pair_all = lax.optimization_barrier((parts_one, pair_all))
    parts_one = first_sum.swap(parts_one, 0)
    pair_grad_rest, query_grad_t_rest = cross_backward(1)
    (wkv_grad,) = call(
        functools.partial(memory_weight_kernel, groups),
        [((2, width, width), BF16)],
        [((width, 2 * width), F32)],
        2,
        spot,
        tgt_len,
        pair_grad_long,
        pair_grad_rest,
        memory,
        *came,
        work=1,
        vmem=32,
    )
    parts_one, wkv_grad = lax.optimization_barrier((parts_one, wkv_grad))
    parts_one = first_sum.split(1, spot, parts_one)
    parts_one, wkv_grad = lax.optimization_barrier((parts_one, wkv_grad))
    parts_one = first_sum.swap(parts_one, 1)
    keep_mid, send_mid, grad_hidden_one, grad_self = call(
        first_norm_backward_kernel,
        [
            ((2 * width + LN_ROWS, width), BF16),
            ((2 * width + LN_ROWS, width), BF16),
            ((rows, width), F32),
            ((rows, width), BF16),
        ],
        [],
        1,
        spot,
        hidden_one,
        query_grad_t_long,
        query_grad_t_rest,
        grad_hidden_two,
        wq_cross,
        w_out,
        self_attn_t,
        ln_gain,
        ln_bias,
        ln_part,
        wkv_grad,
        work=10,
        vmem=24,
    )
    grad_triple, *last = call(
        self_backward_kernel,
        [((rows, 3 * width), BF16)] + [(((width + short) // LAST_PARTS, width), BF16)] * (2 * LAST_PARTS),
        [
            ((tiles, half, 2 * TILE), F32),
            ((tiles, 2 * TILE, width), BF16),
            ((tiles, 2 * TILE, width), BF16),
            ((width, rows), BF16),
            ((width, rows), BF16),
        ],
        2,
        spot,
        tgt_len,
        qkv,
        self_norm,
        grad_self,
        sorted_rows,
        work=0.1,
        vmem=28,
    )
    parts_one, last, send_mid, pair_grad_long = lax.optimization_barrier(
        (parts_one, last, send_mid, pair_grad_long)
    )
    keep_last = last[:LAST_PARTS]
    came_last = [second_sum.core_swap(part) for part in last[LAST_PARTS:]]
    came_mid = second_sum.core_swap(send_mid)
    parts_one = first_sum.swap(first_sum.split(2, spot, parts_one), 2)
    grad_mine, *grad_away = call(
        functools.partial(memory_grad_kernel, groups),
        [((count, span, width), BF16)] + [((count, span // 2, width), BF16)] * (2 * (groups - 1)),
        [],
        2,
        spot,
        tgt_len,
        pair_grad_long,
        pair_grad_rest,
        wkv_cross,
        work=0.01,
        vmem=32,
    )
    backs = [[], []]
    for i, grads in enumerate(grad_away):
        shift = i // 2 + 1
        backs[i % 2].append(lax.ppermute(grads, "mem", [(k, (k - shift) % groups) for k in range(groups)]))
    (grad_target,) = call(
        target_kernel,
        [((rows, width), BF16)],
        [],
        2,
        spot,
        tgt_len,
        grad_triple,
        w_qkv,
        grad_hidden_one,
        work=0.01,
        vmem=16,
    )
    came_last, came_mid, grad_target, grad_away = lax.optimization_barrier(
        (came_last, came_mid, grad_target, grad_away)
    )
    parts_two = second_sum.first_split(
        spot, keep_mid, came_mid, *[part for both in zip(keep_last, came_last) for part in both]
    )
    parts_two, parts_one, backs[0] = lax.optimization_barrier((parts_two, parts_one, backs[0]))
    parts_two = second_sum.swap(parts_two, 0)
    spread_one = first_sum.spread(2, first_sum.total(parts_one)[0])
    parts_two, spread_one = lax.optimization_barrier((parts_two, spread_one))
    parts_two = second_sum.swap(second_sum.split(1, spot, parts_two), 1)
    spread_one = first_sum.spread(1, first_sum.join(2, spot, spread_one))
    parts_two, spread_one = lax.optimization_barrier((parts_two, spread_one))
    parts_two = second_sum.swap(second_sum.split(2, spot, parts_two), 2)
    spread_one = first_sum.spread(0, first_sum.join(1, spot, spread_one))
    sum_two, norm_sums = second_sum.total(parts_two)
    spread_two = second_sum.spread(2, sum_two)
    spread_two, spread_one, backs[1] = lax.optimization_barrier((spread_two, spread_one, backs[1]))
    other_one = [first_sum.core_swap(array) for array in spread_one]
    spread_two = second_sum.spread(1, second_sum.join(2, spot, spread_two))
    chunks = hidden_width // width
    pieces = []
    for chunk in range(chunks):
        side, here = chunk // (chunks // 2), chunk % (chunks // 2)
        pieces.append((side, here * width, width, 0, chunk * width, 0))
        pieces.append((side, (chunks // 2 + here) * width, width, 1, 0, chunk * width))
    for side in range(2):
        pieces.append((side, chunks * width, short, 2, side * short, 0))
    grad_w_down, grad_w_up, grad_wo = first_sum.finish(
        spot,
        spread_one,
        other_one,
        pieces,
        [((hidden_width, width), F32), ((width, hidden_width), F32), ((width, width), F32)],
    )
    spread_two, grad_w_down = lax.optimization_barrier((spread_two, grad_w_down))
    spread_two = second_sum.spread(0, second_sum.join(1, spot, spread_two))
    other_two = [second_sum.core_swap(array) for array in spread_two]
    pieces = [
        (0, 0, width, 0, 0, 0),
        (0, width, width, 1, 0, 0),
        (0, 2 * width, width, 2, 0, 0),
        (0, 3 * width, short, 2, 0, width),
        (1, 0, width, 1, 0, width),
        (1, width, width, 3, 0, 0),
        (1, 2 * width, short, 2, short, width),
        (1, 2 * width + short, width, 2, 0, 2 * width),
    ]
    grad_wq, grad_wkv, grad_w_qkv, grad_w_out = second_sum.finish(
        spot,
        spread_two,
        other_two,
        pieces,
        [
            ((width, width), F32),
            ((width, 2 * width), F32),
            ((width, 3 * width), F32),
            ((width, width), F32),
        ],
    )
    grad_memory = jnp.zeros(memory.shape, BF16)
    grad_memory = lax.dynamic_update_slice(grad_memory, grad_mine, (me * count, 0, 0))
    for part in range(2):
        for i, grads in enumerate(backs[part]):
            owner = (me + i + 1) % groups
            grad_memory = lax.dynamic_update_slice(grad_memory, grads, (owner * count, part * (span // 2), 0))
    return (
        result_out,
        grad_target,
        grad_memory,
        grad_w_qkv,
        grad_w_out,
        grad_wq,
        grad_wkv,
        grad_wo,
        grad_w_up,
        grad_w_down,
        norm_sums[:3],
        norm_sums[3:6],
    )


def solution(mesh):
    rows_spec = P(("dp", "mem"), None)
    memory_spec = P("dp", "mem", None)
    return jax.shard_map(
        body,
        mesh=mesh,
        in_specs=(rows_spec, memory_spec, rows_spec, P("dp", None), P("dp", None)) + (P(),) * 9,
        out_specs=(rows_spec, rows_spec, memory_spec) + (P(),) * 9,
        check_vma=False,
    )
```

```python
import functools
import math

import jax
import jax.numpy as jnp
from jax import lax
from jax.experimental import pallas as pl
from jax.experimental.pallas import tpu as pltpu
from jax.sharding import PartitionSpec as P

HEADS = 8
PAIRS = HEADS // 2
SLAB = 128
SIDE = SLAB // 2
TILE = 128
MASKED = -1e30
EPSILON = 1e-05
F32 = jnp.float32
BF16 = jnp.bfloat16
MIB = 1024 * 1024
LN_ROWS = 16
LAST_PARTS = 1


def dot(left, right):
    return jnp.dot(left, right, preferred_element_type=F32)


def dot_nt(left, right):
    return lax.dot_general(left, right, (((1,), (1,)), ((), ())), preferred_element_type=F32)


def dot_tn(left, right):
    return lax.dot_general(left, right, (((0,), (0,)), ((), ())), preferred_element_type=F32)


def iota(shape, axis):
    return lax.broadcasted_iota(jnp.int32, shape, axis)


def norm_parts(hidden):
    centre = hidden - jnp.mean(hidden, axis=-1, keepdims=True)
    inverse = lax.rsqrt(jnp.mean(centre * centre, axis=-1, keepdims=True) + EPSILON)
    return centre * inverse, inverse


def norm_backward(upstream, unit, inverse, gain_row):
    scaled = upstream * gain_row
    shifted = (
        scaled
        - jnp.mean(scaled, axis=-1, keepdims=True)
        - unit * jnp.mean(scaled * unit, axis=-1, keepdims=True)
    )
    gain_grad = jnp.sum(upstream * unit, axis=0, keepdims=True)
    return inverse * shifted, gain_grad, jnp.sum(upstream, axis=0, keepdims=True)


def sentence_order(me, len_ref):
    count = len_ref.shape[1]
    lengths = [len_ref[me, k] for k in range(count)]
    longest, best, start, running = jnp.int32(0), lengths[0], jnp.int32(0), jnp.int32(0)
    for k in range(1, count):
        running = running + lengths[k - 1]
        more = lengths[k] > best
        longest = jnp.where(more, k, longest)
        start = jnp.where(more, running, start)
        best = jnp.where(more, lengths[k], best)
    order = [longest] + [jnp.where(k < longest, k, k + 1) for k in range(count - 1)]
    bounds = [jnp.int32(0)]
    for k in range(1, count):
        bounds.append(bounds[-1] + len_ref[me, order[k]])
    return order, start, bounds


def moved_rows(index, start, half):
    return jnp.where(index < start, index + half, jnp.where(index < start + half, index - start, index))


def sort_matrix(rows, start):
    spot = moved_rows(iota((rows, rows), 1), start, rows // 2)
    return jnp.where(spot == iota((rows, rows), 0), 1.0, 0.0).astype(BF16)


def unsort_matrix(rows, start):
    spot = moved_rows(iota((rows, rows), 0), start, rows // 2)
    return jnp.where(spot == iota((rows, rows), 1), 1.0, 0.0).astype(BF16)


def side_masks(width):
    side = iota((1, width), 1) % SLAB
    first = jnp.where(side < SLAB // 2, 1.0, 0.0)
    return first.astype(BF16), (1.0 - first).astype(BF16)


def slab_of(pair, first=0):
    return pl.ds(pl.multiple_of(first + pair * SLAB, SLAB), SLAB)


def pack_heads(out_ref, rows, width):
    even, odd = side_masks(width)
    for t in range(out_ref.shape[0]):
        tile = rows(t * TILE, TILE)
        out_ref[t, :TILE, :] = tile * even
        out_ref[t, TILE:, :] = tile * odd


def fill_self_bias(bias_ref, bounds, half):
    for t in range(bias_ref.shape[0]):
        block, inner = t // (half // TILE), t % (half // TILE)
        key = iota((half, 2 * TILE), 0)
        query = iota((half, 2 * TILE), 1) % TILE + inner * TILE
        allowed = key <= query
        if block == 1:
            first = jnp.zeros((half, 2 * TILE), jnp.int32)
            for bound in bounds[1:-1]:
                first = jnp.where(query >= bound, bound, first)
            allowed = allowed & (key >= first)
        bias_ref[t] = jnp.where(allowed, 0.0, MASKED)


def self_keys(t, half):
    per = half // TILE
    return (t // per) * half, (t % per + 1) * TILE


def fill_live_bias(bias_ref, me, groups, parts, span, src_ref, sentences):
    key = iota((span, bias_ref.shape[2]), 0)
    for j, sentence in enumerate(sentences):
        for i, part in enumerate(parts):
            place = lax.rem(me - part + groups, groups) * span + key
            live = place < src_ref[me, sentence]
            bias_ref[j, pl.ds(i * span, span), :] = jnp.where(live, 0.0, MASKED)


def cross_units(bounds, half):
    units = [(t, 0, None) for t in range(half // TILE)]
    middle = half // 2
    last = jnp.int32(1)
    for bound in bounds[1:-1]:
        last = last + jnp.where(bound < middle, 1, 0)
    ends = bounds[1:]
    column = iota((1, 2 * TILE), 1) % TILE
    for u in range(len(ends) + 1):
        early = u < last
        sentence = jnp.where(early, u + 1, u)
        tile = jnp.where(early, 0, 1)
        low, high = jnp.int32(0), ends[0]
        for k in range(1, len(ends)):
            low = jnp.where(sentence == k + 1, ends[k - 1], low)
            high = jnp.where(sentence == k + 1, ends[k], high)
        row = column + tile * TILE
        units.append((tile + half // TILE, sentence, (row >= low) & (row < high)))
    return units


def own_sides(both):
    return jnp.concatenate([both[:SIDE, :TILE], both[SIDE:, TILE:]], axis=0)


def side_rows(row):
    even = jnp.broadcast_to(row[:, :TILE], (SIDE, TILE))
    return jnp.concatenate([even, jnp.broadcast_to(row[:, TILE:], (SIDE, TILE))], axis=0)


def tile_columns(tile):
    if isinstance(tile, int):
        return pl.ds(tile * TILE, TILE)
    return pl.ds(pl.multiple_of(tile * TILE, TILE), TILE)


def self_forward_kernel(
    groups,
    me_ref,
    len_ref,
    src_ref,
    target_ref,
    w_qkv_ref,
    w_out_ref,
    wq_ref,
    gain_ref,
    bias_row_ref,
    memory_ref,
    wkv_ref,
    sorted_ref,
    qkv_ref,
    norm_ref,
    attn_t_ref,
    hidden_ref,
    query_ref,
    part_ref,
    top_ref,
    sum_ref,
    pair_out_ref,
    bias_ref,
    live_ref,
    q_pack_ref,
    value_t_ref,
    cross_value_t_ref,
    pair_ref,
    copy_sem,
):
    rows, width = target_ref.shape
    half = rows // 2
    me = me_ref[0]
    order, start, bounds = sentence_order(me, len_ref)
    count, span = pair_ref.shape[0], pair_ref.shape[1]
    copies = []
    for j in range(count):
        block = memory_ref[me * count + order[j]]
        pair_ref[j] = dot(block, wkv_ref[...]).astype(BF16)
        copy = pltpu.make_async_copy(
            pair_ref.at[j], pair_out_ref.at[j, pl.ds(0, span), :], copy_sem.at[j]
        )
        copy.start()
        copies.append(copy)
    sorted_rows = dot(sort_matrix(rows, start), target_ref[...]).astype(BF16)
    sorted_ref[...] = sorted_rows
    fill_self_bias(bias_ref, bounds, half)
    queries = (dot(sorted_rows, w_qkv_ref[:, :width]).astype(BF16) * 0.125).astype(BF16)
    qkv_ref[:, :width] = queries
    pack_heads(q_pack_ref, lambda first, size: queries[first : first + size], width)
    qkv_ref[:, width : 2 * width] = dot(sorted_rows, w_qkv_ref[:, width : 2 * width]).astype(BF16)
    values = dot(sorted_rows, w_qkv_ref[:, 2 * width :]).astype(BF16)
    qkv_ref[:, 2 * width :] = values
    value_t_ref[...] = values.T
    tiles = rows // TILE

    def self_step(pair, carry):
        slab = slab_of(pair)
        for t in range(tiles):
            first, size = self_keys(t, half)
            keys = qkv_ref[pl.ds(first, size), slab_of(pair, width)]
            scores = dot_nt(keys, q_pack_ref[t, :, slab]) + bias_ref[t, :size, :]
            top = jnp.max(scores, axis=0, keepdims=True)
            weights = jnp.exp(scores - top)
            total = jnp.sum(weights, axis=0, keepdims=True)
            probs = (weights * (1.0 / total)).astype(BF16)
            both = dot(value_t_ref[slab, pl.ds(first, size)], probs)
            attn_t_ref[slab, tile_columns(t)] = own_sides(both).astype(BF16)
            norm_ref[pl.ds(pair * tiles + t, 1), :] = top + jnp.log(total)
        return carry

    lax.fori_loop(0, PAIRS, self_step, 0)
    hidden = sorted_rows.astype(F32) + dot(attn_t_ref[...].T, w_out_ref[...])
    hidden_ref[...] = hidden
    unit, _ = norm_parts(hidden)
    normed = (unit * gain_ref[0:1] + bias_row_ref[0:1]).astype(BF16)
    query_ref[...] = (dot(normed, wq_ref[...]).astype(BF16) * 0.125).astype(BF16)

    pack_heads(q_pack_ref, lambda first, size: query_ref[first : first + size, :], width)
    fill_live_bias(live_ref, me, groups, [0], span, src_ref, order)
    for j in range(count):
        cross_value_t_ref[j] = pair_ref[j, :, width:].T
    units = cross_units(bounds, half)

    def cross_step(pair, carry):
        slab = slab_of(pair)
        for tile, sentence, columns in units:
            scores = dot_nt(pair_ref[sentence, :, slab], q_pack_ref[tile, :, slab]) + live_ref[sentence]
            top = jnp.max(scores, axis=0, keepdims=True)
            weights = jnp.exp(scores - top)
            total = jnp.sum(weights, axis=0, keepdims=True)
            result = own_sides(dot(cross_value_t_ref[sentence, slab, :], weights.astype(BF16)))
            here = tile_columns(tile)
            row = pl.ds(pair * tiles + tile, 1)
            if columns is not None:
                result = jnp.where(columns[:, :TILE], result, part_ref[slab, here])
                top = jnp.where(columns, top, top_ref[row, :])
                total = jnp.where(columns, total, sum_ref[row, :])
            part_ref[slab, here] = result
            top_ref[row, :] = top
            sum_ref[row, :] = total
        return carry

    part_ref[...] = jnp.zeros_like(part_ref)
    top_ref[...] = jnp.zeros_like(top_ref)
    sum_ref[...] = jnp.ones_like(sum_ref)
    lax.fori_loop(0, PAIRS, cross_step, 0)
    for copy in copies:
        copy.wait()


def middle_kernel(
    groups,
    me_ref,
    len_ref,
    src_ref,
    hidden_one_ref,
    query_ref,
    part_ref,
    top_ref,
    sum_ref,
    wkv_ref,
    gain_ref,
    bias_row_ref,
    wo_hbm,
    w_up_hbm,
    w_down_hbm,
    grad_out_hbm,
    pair_in_hbm,
    *refs,
):
    came_refs = refs[: groups - 1]
    (
        out_ref,
        norm_ref,
        along_ref,
        keep_hbm,
        send_hbm,
        grad_hidden_ref,
        grad_attn_ref,
        ln_ref,
        pair_hbm,
        wo_ref,
        w_up_ref,
        w_down_ref,
        grad_out_ref,
        pair_ref,
        keep_ref,
        send_ref,
        live_ref,
        q_pack_ref,
        value_t_ref,
        attn_t_ref,
        active_ref,
        slope_ref,
        total_ref,
        load_sem,
        pair_sem,
        store_sem,
    ) = refs[groups - 1 :]
    rows, width = hidden_one_ref.shape
    half = rows // 2
    me = me_ref[0]
    count, away = pair_ref.shape[0], pair_ref.shape[1]
    span = away // (groups - 1)
    loads = [
        pltpu.make_async_copy(source, there, load_sem.at[i])
        for i, (source, there) in enumerate(
            [(wo_hbm, wo_ref), (w_up_hbm, w_up_ref), (w_down_hbm, w_down_ref), (grad_out_hbm, grad_out_ref)]
        )
    ]
    for copy in loads:
        copy.start()
    order, start, bounds = sentence_order(me, len_ref)
    fill_live_bias(live_ref, me, groups, list(range(1, groups)), span, src_ref, order)
    pack_heads(q_pack_ref, lambda first, size: query_ref[first : first + size, :], width)
    pair_copies = []
    for j in range(count):
        for part in range(1, groups):
            block = came_refs[part - 1][order[j]]
            pair_ref[j, pl.ds((part - 1) * span, span), :] = dot(block, wkv_ref[...]).astype(BF16)
        value_t_ref[j] = pair_ref[j, :, width:].T
        copy = pltpu.make_async_copy(pair_ref.at[j], pair_hbm.at[j, pl.ds(span, away), :], pair_sem.at[j])
        copy.start()
        pair_copies.append(copy)
    units = cross_units(bounds, half)
    tiles = rows // TILE

    def cross_step(pair, carry):
        slab = slab_of(pair)
        for tile, sentence, columns in units:
            here = tile_columns(tile)
            row = pl.ds(pair * tiles + tile, 1)
            scores = dot_nt(pair_ref[sentence, :, slab], q_pack_ref[tile, :, slab]) + live_ref[sentence]
            before = top_ref[row, :]
            top = jnp.maximum(jnp.max(scores, axis=0, keepdims=True), before)
            weights = jnp.exp(scores - top)
            scale = jnp.exp(before - top)
            total = jnp.sum(weights, axis=0, keepdims=True) + sum_ref[row, :] * scale
            result = own_sides(dot(value_t_ref[sentence, slab, :], weights.astype(BF16)))
            result = (result + part_ref[slab, here] * side_rows(scale)) * side_rows(1.0 / total)
            norm = top + jnp.log(total)
            if columns is not None:
                result = jnp.where(columns[:, :TILE], result, attn_t_ref[slab, here])
                norm = jnp.where(columns, norm, norm_ref[row, :])
            attn_t_ref[slab, here] = result
            norm_ref[row, :] = norm
        return carry

    attn_t_ref[...] = jnp.zeros_like(attn_t_ref)
    norm_ref[...] = jnp.zeros_like(norm_ref)
    lax.fori_loop(0, PAIRS, cross_step, 0)
    attn_t_low = attn_t_ref[...].astype(BF16)
    loads[0].wait()
    unit_one, _ = norm_parts(hidden_one_ref[...])
    normed_one = unit_one * gain_ref[0:1] + bias_row_ref[0:1]
    hidden_two = normed_one + dot(attn_t_low.T, wo_ref[...])
    unit_two, inverse_two = norm_parts(hidden_two)
    normed_two = unit_two * gain_ref[1:2] + bias_row_ref[1:2]
    normed_two_low = normed_two.astype(BF16)
    total_ref[...] = normed_two
    chunk = width
    chunks = w_down_ref.shape[0] // chunk
    loads[1].wait()
    loads[2].wait()

    def up_step(c, carry):
        cols = pl.ds(pl.multiple_of(c * chunk, chunk), chunk)
        upper = dot(normed_two_low, w_up_ref[:, cols])
        sigma = 1.0 / (1.0 + jnp.exp(-upper))
        active = (upper * sigma).astype(BF16)
        active_ref[:, cols] = active
        slope_ref[:, cols] = sigma * (1.0 + upper * (1.0 - sigma))
        total_ref[...] += dot(active, w_down_ref[cols, :])
        return carry

    lax.fori_loop(0, chunks, up_step, 0)
    unit_three, inverse_three = norm_parts(total_ref[...])
    result = (unit_three * gain_ref[2:3] + bias_row_ref[2:3]).astype(BF16)
    out_ref[...] = dot(unsort_matrix(rows, start), result).astype(BF16)
    loads[3].wait()
    upstream = dot(sort_matrix(rows, start), grad_out_ref[...])
    grad_three, gain_three, bias_three = norm_backward(upstream, unit_three, inverse_three, gain_ref[2:3])
    grad_down = grad_three.astype(BF16)
    total_ref[...] = grad_three
    normed_two_t = normed_two_low.T

    def down_step(c, carry):
        cols = pl.ds(pl.multiple_of(c * chunk, chunk), chunk)
        grad_upper = (dot_nt(grad_down, w_down_ref[cols, :]) * slope_ref[:, cols]).astype(BF16)
        down_part = dot_tn(active_ref[:, cols], grad_down).astype(BF16)
        up_part = dot(normed_two_t, grad_upper).astype(BF16)
        here = lax.rem(c, chunks // 2)
        down_rows = pl.ds(pl.multiple_of(here * chunk, chunk), chunk)
        up_rows = pl.ds(pl.multiple_of((chunks // 2 + here) * chunk, chunk), chunk)
        mine = c // (chunks // 2) == me_ref[1]

        @pl.when(mine)
        def _():
            keep_ref[down_rows, :] = down_part
            keep_ref[up_rows, :] = up_part

        @pl.when(jnp.logical_not(mine))
        def _():
            send_ref[down_rows, :] = down_part
            send_ref[up_rows, :] = up_part

        total_ref[...] += dot_nt(grad_upper, w_up_ref[:, cols])
        return carry

    lax.fori_loop(0, chunks, down_step, 0)
    most = chunks * chunk
    stores = [
        pltpu.make_async_copy(ref.at[pl.ds(first, size)], there.at[pl.ds(first, size)], store_sem.at[i])
        for i, (ref, there, first, size) in enumerate(
            [
                (send_ref, send_hbm, 0, most),
                (keep_ref, keep_hbm, 0, most),
                (send_ref, send_hbm, most, keep_ref.shape[0] - most),
                (keep_ref, keep_hbm, most, keep_ref.shape[0] - most),
            ]
        )
    ]
    stores[0].start()
    stores[1].start()
    grad_two, gain_two, bias_two = norm_backward(total_ref[...], unit_two, inverse_two, gain_ref[1:2])
    grad_two_low = grad_two.astype(BF16)
    wo_grad = dot(attn_t_low, grad_two_low).astype(BF16)
    core = me_ref[1]
    low, high = wo_grad[: width // 2], wo_grad[width // 2 :]
    tail = pl.ds(most, width // 2)
    keep_ref[tail, :] = jnp.where(core == 0, low, high)
    send_ref[tail, :] = jnp.where(core == 0, high, low)
    used = most + width // 2
    if keep_ref.shape[0] > used:
        keep_ref[used:, :] = jnp.zeros((keep_ref.shape[0] - used, width), BF16)
        send_ref[used:, :] = jnp.zeros((keep_ref.shape[0] - used, width), BF16)
    stores[2].start()
    stores[3].start()
    grad_hidden_ref[...] = grad_two
    grad_attn = dot_nt(grad_two_low, wo_ref[...]).astype(BF16)
    grad_attn_ref[...] = grad_attn
    product = grad_attn.T.astype(F32) * attn_t_ref[...]
    for pair in range(PAIRS):
        for side in range(2):
            first = pair * SLAB + side * SIDE
            along = jnp.sum(product[first : first + SIDE], axis=0, keepdims=True)
            for t in range(tiles):
                along_ref[pair * tiles + t : pair * tiles + t + 1, side * TILE : (side + 1) * TILE] = along[
                    :, t * TILE : (t + 1) * TILE
                ]
    ln_ref[...] = jnp.concatenate([gain_two, gain_three, bias_two, bias_three], axis=0)
    for copy in pair_copies + stores:
        copy.wait()


def cross_backward_kernel(
    groups,
    block,
    me_ref,
    len_ref,
    src_ref,
    query_ref,
    norm_ref,
    along_ref,
    grad_attn_ref,
    pair_hbm,
    pair_grad_ref,
    query_grad_t_ref,
    pair_ref,
    live_ref,
    q_pack_ref,
    g_pack_ref,
    key_t_ref,
    query_sum_ref,
    sum_ref,
    load_sem,
):
    rows, width = query_ref.shape
    half = rows // 2
    me = me_ref[0]
    sentences, places = pair_ref.shape[0], pair_ref.shape[1]
    first_sentence = 0 if block == 0 else 1
    load = pltpu.make_async_copy(pair_hbm.at[pl.ds(first_sentence, sentences)], pair_ref, load_sem.at[0])
    load.start()
    order, start, bounds = sentence_order(me, len_ref)
    mine = order[:1] if block == 0 else order[1:]
    fill_live_bias(live_ref, me, groups, list(range(groups)), places // groups, src_ref, mine)
    low = block * half
    pack_heads(q_pack_ref, lambda first, size: query_ref[low + first : low + first + size, :], width)
    pack_heads(g_pack_ref, lambda first, size: grad_attn_ref[low + first : low + first + size, :], width)
    tiles, per = rows // TILE, half // TILE
    units = cross_units(bounds, half)
    units = units[:per] if block == 0 else units[per:]
    load.wait()
    for j in range(sentences):
        key_t_ref[j] = pair_ref[j, :, :width].T

    def pair_step(pair, carry):
        slab, value_slab = slab_of(pair), slab_of(pair, width)
        query_sum_ref[...] = jnp.zeros_like(query_sum_ref)
        sum_ref[...] = jnp.zeros_like(sum_ref)
        for tile, sentence, columns in units:
            j = sentence - first_sentence
            t = tile - block * per
            here = tile_columns(t)
            row = pl.ds(pair * tiles + tile, 1)
            q_rows, g_rows = q_pack_ref[t, :, slab], g_pack_ref[t, :, slab]
            norm = norm_ref[row, :]
            if columns is not None:
                norm = jnp.where(columns, norm, -MASKED)
            scores = dot_nt(pair_ref[j, :, slab], q_rows) + live_ref[j]
            probs = jnp.exp(scores - norm)
            grad_probs = dot_nt(pair_ref[j, :, value_slab], g_rows)
            grad_scores = (probs * (grad_probs - along_ref[row, :])).astype(BF16)
            sum_ref[j, :, :SLAB] += dot(grad_scores, q_rows)
            sum_ref[j, :, SLAB:] += dot(probs.astype(BF16), g_rows)
            query_sum_ref[:, here] += own_sides(dot(key_t_ref[j, slab, :], grad_scores))
        query_grad_t_ref[slab, :] = (query_sum_ref[...] * 0.125).astype(BF16)
        pair_grad_ref[:, :, slab] = sum_ref[:, :, :SLAB].astype(BF16)
        pair_grad_ref[:, :, value_slab] = sum_ref[:, :, SLAB:].astype(BF16)
        return carry

    lax.fori_loop(0, PAIRS, pair_step, 0)


def memory_weight_kernel(groups, me_ref, len_ref, pair_grad_long_ref, pair_grad_rest_ref, memory_ref, *refs):
    came_refs = refs[: groups - 1]
    wkv_grad_ref, total_ref = refs[groups - 1 :]
    width = memory_ref.shape[2]
    me = me_ref[0]
    count = len_ref.shape[1]
    span = pair_grad_long_ref.shape[1] // groups
    order, _, _ = sentence_order(me, len_ref)
    for j in range(count):
        pair_grad_ref, here = (pair_grad_long_ref, 0) if j == 0 else (pair_grad_rest_ref, j - 1)
        blocks = [memory_ref[me * count + order[j]]] + [ref[order[j]] for ref in came_refs]
        term = dot_tn(jnp.concatenate(blocks, axis=0), pair_grad_ref[here])
        if j == 0:
            total_ref[...] = term
        else:
            total_ref[...] += term
    wkv_grad_ref[0] = total_ref[:, :width].astype(BF16)
    wkv_grad_ref[1] = total_ref[:, width:].astype(BF16)


def memory_grad_kernel(
    groups, me_ref, len_ref, pair_grad_long_ref, pair_grad_rest_ref, wkv_ref, mine_ref, *away_refs
):
    count = len_ref.shape[1]
    span = pair_grad_long_ref.shape[1] // groups
    order, _, _ = sentence_order(me_ref[0], len_ref)
    for j in range(count):
        pair_grad_ref, here = (pair_grad_long_ref, 0) if j == 0 else (pair_grad_rest_ref, j - 1)
        grads = dot_nt(pair_grad_ref[here], wkv_ref[...]).astype(BF16)
        mine_ref[order[j]] = grads[:span]
        for i, ref in enumerate(away_refs):
            first = span + i * (span // 2)
            ref[order[j]] = grads[first : first + span // 2]


def first_norm_backward_kernel(
    me_ref,
    hidden_one_ref,
    query_grad_t_long_ref,
    query_grad_t_rest_ref,
    grad_hidden_two_ref,
    wq_ref,
    w_out_ref,
    self_attn_t_ref,
    gain_ref,
    bias_row_ref,
    ln_in_ref,
    wkv_grad_ref,
    keep_ref,
    send_ref,
    grad_hidden_ref,
    grad_self_ref,
):
    width = wq_ref.shape[0]
    unit_one, inverse_one = norm_parts(hidden_one_ref[...])
    normed_one = (unit_one * gain_ref[0:1] + bias_row_ref[0:1]).astype(BF16)
    query_grad = jnp.concatenate([query_grad_t_long_ref[...].T, query_grad_t_rest_ref[...].T], axis=0)
    upstream = grad_hidden_two_ref[...] + dot_nt(query_grad, wq_ref[...])
    grad_one, gain_one, bias_one = norm_backward(upstream, unit_one, inverse_one, gain_ref[0:1])
    grad_hidden_ref[...] = grad_one
    grad_one_low = grad_one.astype(BF16)
    grad_self_ref[...] = dot_nt(grad_one_low, w_out_ref[...]).astype(BF16)
    wq_grad = dot_tn(normed_one, query_grad).astype(BF16)
    w_out_grad = dot(self_attn_t_ref[...], grad_one_low).astype(BF16)
    norms = jnp.concatenate(
        [gain_one, ln_in_ref[0:2], bias_one, ln_in_ref[2:4], jnp.zeros((LN_ROWS - 6, width), F32)], axis=0
    ).astype(BF16)

    def halves(low_ref, high_ref):
        low_ref[:width, :] = wq_grad
        low_ref[width : 2 * width, :] = wkv_grad_ref[0]
        high_ref[:width, :] = wkv_grad_ref[1]
        high_ref[width : 2 * width, :] = w_out_grad

    @pl.when(me_ref[1] == 0)
    def _():
        halves(keep_ref, send_ref)

    @pl.when(me_ref[1] != 0)
    def _():
        halves(send_ref, keep_ref)

    keep_ref[2 * width :, :] = norms
    send_ref[2 * width :, :] = norms


def self_backward_kernel(
    me_ref,
    len_ref,
    qkv_ref,
    norm_ref,
    grad_attn_ref,
    sorted_ref,
    grad_triple_ref,
    *refs,
):
    keep_refs, send_refs = refs[:LAST_PARTS], refs[LAST_PARTS : 2 * LAST_PARTS]
    self_backward(
        me_ref,
        len_ref,
        qkv_ref,
        norm_ref,
        grad_attn_ref,
        sorted_ref,
        grad_triple_ref,
        keep_refs,
        send_refs,
        *refs[2 * LAST_PARTS :],
    )


def self_backward(
    me_ref,
    len_ref,
    qkv_ref,
    norm_ref,
    grad_attn_ref,
    sorted_ref,
    grad_triple_ref,
    keep_refs,
    send_refs,
    bias_ref,
    q_pack_ref,
    g_pack_ref,
    key_t_ref,
    query_grad_t_ref,
):
    rows, width = sorted_ref.shape
    half = rows // 2
    _, _, bounds = sentence_order(me_ref[0], len_ref)
    fill_self_bias(bias_ref, bounds, half)
    pack_heads(q_pack_ref, lambda first, size: qkv_ref[first : first + size, :width], width)
    pack_heads(g_pack_ref, lambda first, size: grad_attn_ref[first : first + size, :], width)
    key_t_ref[...] = qkv_ref[:, width : 2 * width].T
    tiles, per = rows // TILE, half // TILE

    def pair_step(pair, carry):
        slab, key_slab, value_slab = slab_of(pair), slab_of(pair, width), slab_of(pair, 2 * width)
        sums = [[None, None] for _ in range(tiles)]
        for t in range(tiles):
            first, size = self_keys(t, half)
            span = pl.ds(first, size)
            q_rows, g_rows = q_pack_ref[t, :, slab], g_pack_ref[t, :, slab]
            scores = dot_nt(qkv_ref[span, key_slab], q_rows) + bias_ref[t, :size, :]
            probs = jnp.exp(scores - norm_ref[pl.ds(pair * tiles + t, 1), :])
            grad_probs = dot_nt(qkv_ref[span, value_slab], g_rows)
            along = jnp.sum(probs * grad_probs, axis=0, keepdims=True)
            grad_scores = (probs * (grad_probs - along)).astype(BF16)
            parts = dot(grad_scores, q_rows), dot(probs.astype(BF16), g_rows)
            for i in range(size // TILE):
                spot = sums[first // TILE + i]
                for k in range(2):
                    piece = parts[k][i * TILE : (i + 1) * TILE]
                    spot[k] = piece if spot[k] is None else spot[k] + piece
            query_grad_t_ref[slab, tile_columns(t)] = (
                own_sides(dot(key_t_ref[slab, span], grad_scores)) * 0.125
            ).astype(BF16)
        for t in range(tiles):
            grad_triple_ref[pl.ds(t * TILE, TILE), key_slab] = sums[t][0].astype(BF16)
            grad_triple_ref[pl.ds(t * TILE, TILE), value_slab] = sums[t][1].astype(BF16)
        return carry

    lax.fori_loop(0, PAIRS, pair_step, 0)
    grad_triple_ref[:, :width] = query_grad_t_ref[...].T
    sorted_t = sorted_ref[...].T
    grads = [
        dot(sorted_t, grad_triple_ref[:, part * width : (part + 1) * width]).astype(BF16)
        for part in range(3)
    ]
    short = width // 2

    low = jnp.concatenate([grads[0], grads[1][:short]], axis=0)
    high = jnp.concatenate([grads[1][short:], grads[2]], axis=0)
    size = keep_refs[0].shape[0]

    def halves(low_refs, high_refs):
        for i in range(LAST_PARTS):
            low_refs[i][...] = low[i * size : (i + 1) * size]
            high_refs[i][...] = high[i * size : (i + 1) * size]

    @pl.when(me_ref[1] == 0)
    def _():
        halves(keep_refs, send_refs)

    @pl.when(me_ref[1] != 0)
    def _():
        halves(send_refs, keep_refs)


def target_kernel(me_ref, len_ref, grad_triple_ref, w_qkv_ref, grad_hidden_ref, grad_target_ref):
    rows = grad_hidden_ref.shape[0]
    _, start, _ = sentence_order(me_ref[0], len_ref)
    result = grad_hidden_ref[...] + dot_nt(grad_triple_ref[...], w_qkv_ref[...])
    grad_target_ref[...] = dot(unsort_matrix(rows, start), result.astype(BF16)).astype(BF16)


def tree_sum(terms):
    while len(terms) > 1:
        terms = [terms[i] + terms[i + 1] for i in range(0, len(terms), 2)]
    return terms[0]


def rows_of(ref, first, count):
    return ref[pl.ds(pl.multiple_of(first, 16), count), :].astype(F32)


def first_split_kernel(segments, ln, peers, spot_ref, *refs):
    ins, outs, sum_ref = refs[: 2 * segments], refs[2 * segments : -1], refs[-1]
    extra = LN_ROWS if ln else 0
    size = outs[0].shape[0] - extra
    used = 0
    for i in range(segments):
        keep_ref, came_ref = ins[2 * i], ins[2 * i + 1]
        count = keep_ref.shape[0] - (extra if i == 0 else 0)
        sum_ref[used : used + count, :] = (rows_of(keep_ref, 0, count) + rows_of(came_ref, 0, count)).astype(BF16)
        if i == 0 and ln:
            tail = (rows_of(keep_ref, count, LN_ROWS) + rows_of(came_ref, count, LN_ROWS)).astype(BF16)
        used += count
    if sum_ref.shape[0] > used:
        sum_ref[used:, :] = jnp.zeros((sum_ref.shape[0] - used, sum_ref.shape[1]), BF16)
    for d, out in enumerate(outs):
        out[:size, :] = sum_ref[pl.ds(pl.multiple_of((spot_ref[2] ^ d) * size, 16), size), :]
        if ln:
            out[size:, :] = tail


def split_kernel(stage, ln, peers, spot_ref, *refs):
    ins, outs = refs[:peers], refs[peers:]
    extra = LN_ROWS if ln else 0
    size = outs[0].shape[0] - extra
    if ln:
        tail = tree_sum([rows_of(ref, size * len(outs), LN_ROWS) for ref in ins]).astype(BF16)
    for d, out in enumerate(outs):
        first = (spot_ref[2 + stage] ^ d) * size
        out[:size, :] = tree_sum([rows_of(ref, first, size) for ref in ins]).astype(BF16)
        if ln:
            out[size:, :] = tail


def total_kernel(ln, count, *refs):
    ins, outs = refs[:count], refs[count:]
    size = outs[0].shape[0]
    outs[0][...] = tree_sum([rows_of(ref, 0, size) for ref in ins]).astype(BF16)
    if ln:
        outs[1][...] = tree_sum([rows_of(ref, size, LN_ROWS) for ref in ins])


def join_kernel(stage, spot_ref, *refs):
    out_ref = refs[-1]
    for d, ref in enumerate(refs[:-1]):
        size = ref.shape[0]
        out_ref[pl.ds(pl.multiple_of((spot_ref[2 + stage] ^ d) * size, 16), size), :] = ref[...]


def finish_kernel(peers, twisted, pieces, spot_ref, *refs):
    mine, others, outs, both_ref = refs[:peers], refs[peers : 2 * peers], refs[2 * peers : -1], refs[-1]
    core = spot_ref[1]
    for half, arrays, here in ((core, mine, spot_ref[2]), (1 - core, others, spot_ref[3 if twisted else 2])):
        for d, ref in enumerate(arrays):
            size = ref.shape[0]
            both_ref[half, pl.ds(pl.multiple_of((here ^ d) * size, 16), size), :] = ref[...]
    width = both_ref.shape[2]
    for half, first, rows, out, row, col in pieces:
        outs[out][row : row + rows, col : col + width] = both_ref[half, first : first + rows, :].astype(F32)


class Summing:
    def __init__(self, rows, width, ln):
        self.width, self.ln = width, ln
        self.dp, self.mem = lax.axis_size("dp"), lax.axis_size("mem")
        z_size = 4
        x_size = self.dp // (2 * z_size)
        self.sizes = (x_size, self.mem, z_size)
        self.twisted = x_size == self.mem
        self.chunk = -(-rows // (16 * math.prod(self.sizes))) * 16
        self.rows = self.chunk * math.prod(self.sizes)

    def after(self, stage):
        return self.rows // math.prod(self.sizes[:stage])

    def axis(self, stage, core):
        return 1 - stage if self.twisted and core == 1 and stage < 2 else stage

    def coords(self, dp, mem):
        return [dp // 2 % self.sizes[0], mem, dp // (2 * self.sizes[0])], dp % 2

    def spot(self, me, dp):
        (x, mem, z), core = self.coords(dp, me)
        if self.twisted:
            x, mem = jnp.where(core == 0, x, mem), jnp.where(core == 0, mem, x)
        return jnp.stack([me, core, x, mem, z]).astype(jnp.int32)

    def permute(self, array, stage, offset):
        pairs = []
        for dp in range(self.dp):
            for mem in range(self.mem):
                spots, core = self.coords(dp, mem)
                if stage is None:
                    core ^= offset
                else:
                    spots[self.axis(stage, core)] ^= offset
                to_dp = (spots[2] * self.sizes[0] + spots[0]) * 2 + core
                pairs.append((dp * self.mem + mem, to_dp * self.mem + spots[1]))
        return lax.ppermute(array, ("dp", "mem"), pairs)

    def core_swap(self, send):
        return self.permute(send, None, 1)

    def swap(self, arrays, stage):
        return [arrays[0]] + [self.permute(array, stage, d) for d, array in enumerate(arrays) if d > 0]

    def spread(self, stage, array):
        return [array] + [self.permute(array, stage, d) for d in range(1, self.sizes[stage])]

    def messages(self, stage):
        size = self.after(stage + 1) + (LN_ROWS if self.ln else 0)
        return [((size, self.width), BF16)] * self.sizes[stage]

    def first_split(self, spot, *arrays):
        kernel = functools.partial(first_split_kernel, len(arrays) // 2, self.ln, self.sizes[0])
        return call(kernel, self.messages(0), [((self.rows, self.width), BF16)], 1, spot, *arrays, work=0.01)

    def split(self, stage, spot, arrays):
        kernel = functools.partial(split_kernel, stage, self.ln, self.sizes[stage - 1])
        return call(kernel, self.messages(stage), [], 1, spot, *arrays, work=0.01)

    def total(self, arrays):
        outs = [((self.chunk, self.width), BF16)]
        if self.ln:
            outs.append(((LN_ROWS, self.width), F32))
        return call(functools.partial(total_kernel, self.ln, self.sizes[2]), outs, [], 0, *arrays, work=0.01)

    def join(self, stage, spot, arrays):
        outs = [((self.after(stage), self.width), BF16)]
        return call(functools.partial(join_kernel, stage), outs, [], 1, spot, *arrays, work=0.01)[0]

    def finish(self, spot, mine, others, pieces, outs):
        kernel = functools.partial(finish_kernel, self.sizes[0], self.twisted, pieces)
        scratch = [((2, self.rows, self.width), BF16)]
        return call(kernel, outs, scratch, 1, spot, *mine, *others, work=1)


def call(kernel, outs, scratch, scalars, *arrays, work=0.5, vmem=0, hbm_in=0, hbm_out=0, aliases=None):
    plain = len(arrays) - scalars - hbm_in
    if not vmem:
        blocks = [(array.shape, array.dtype) for array in arrays[scalars:]] + outs + scratch
        vmem = max(16, sum(math.prod(shape) * jnp.dtype(kind).itemsize for shape, kind in blocks) // MIB + 7)
    specs = [pl.BlockSpec(memory_space=pltpu.SMEM)] * scalars
    specs = specs + [pl.BlockSpec(memory_space=pltpu.VMEM)] * plain
    specs = specs + [pl.BlockSpec(memory_space=pl.ANY)] * hbm_in
    out_specs = [pl.BlockSpec(memory_space=pltpu.VMEM)] * (len(outs) - hbm_out)
    out_specs = out_specs + [pl.BlockSpec(memory_space=pl.ANY)] * hbm_out
    return pl.pallas_call(
        kernel,
        out_shape=[jax.ShapeDtypeStruct(shape, kind) for shape, kind in outs],
        in_specs=specs,
        out_specs=out_specs,
        scratch_shapes=[pltpu.VMEM(*entry) if isinstance(entry, tuple) else entry for entry in scratch],
        input_output_aliases=aliases or {},
        compiler_params=pltpu.CompilerParams(vmem_limit_bytes=vmem * MIB),
        cost_estimate=pl.CostEstimate(flops=int(work * 1e9), bytes_accessed=int(work * 3e6), transcendentals=0),
    )(*arrays)


def middle(
    groups, first_sum, stats, spot, tgt_len, src_len, hidden_one, query, part, part_top, part_sum, wkv_cross,
    ln_gain, ln_bias, wo_cross, w_up, w_down, grad_out, pair_mine, came,
):
    rows, width = hidden_one.shape
    half, tiles = rows // 2, rows // TILE
    hidden_width = w_down.shape[0]
    count, places, _ = pair_mine.shape
    away = places // groups * (groups - 1)
    arrays = [spot, tgt_len, src_len, hidden_one, query, part, part_top, part_sum, wkv_cross, ln_gain, ln_bias]
    stay = [wo_cross, w_up, w_down, grad_out, pair_mine]

    def kernel(*refs):
        ins, refs = refs[: len(arrays)], refs[len(arrays) :]
        came_refs, refs = refs[: len(came)], refs[len(came) :]
        stay_refs, refs = refs[: len(stay)], refs[len(stay) :]
        outs, refs = refs[:9], refs[9:]
        middle_kernel(groups, *ins, *stay_refs, *came_refs, *outs[:3], *outs[6:8], *outs[3:6], outs[8], *refs)

    result_out, cross_norm, cross_along, grad_hidden_two, grad_attn, ln_part, keep_one, send_one, pair_all = call(
        kernel,
        [
            ((rows, width), BF16),
            (stats, F32),
            (stats, F32),
            ((rows, width), F32),
            ((rows, width), BF16),
            ((4, width), F32),
            ((first_sum.rows, width), BF16),
            ((first_sum.rows, width), BF16),
            ((count, places, 2 * width), BF16),
        ],
        [
            ((width, width), BF16),
            ((width, hidden_width), BF16),
            ((hidden_width, width), BF16),
            ((rows, width), BF16),
            ((count, away, 2 * width), BF16),
            ((first_sum.rows, width), BF16),
            ((first_sum.rows, width), BF16),
            ((count, away, 2 * TILE), F32),
            ((tiles, 2 * TILE, width), BF16),
            ((count, width, away), BF16),
            ((width, rows), F32),
            ((rows, hidden_width), BF16),
            ((rows, hidden_width), F32),
            ((rows, width), F32),
            pltpu.SemaphoreType.DMA((4,)),
            pltpu.SemaphoreType.DMA((count,)),
            pltpu.SemaphoreType.DMA((4,)),
        ],
        3,
        *arrays,
        *came,
        *stay,
        vmem=60,
        hbm_in=len(stay),
        hbm_out=3,
        aliases={len(arrays) + len(came) + len(stay) - 1: 8},
    )
    return result_out, cross_norm, cross_along, keep_one, send_one, grad_hidden_two, grad_attn, ln_part, pair_all


def body(
    target,
    memory,
    grad_out,
    tgt_len,
    src_len,
    w_qkv,
    w_out,
    wq_cross,
    wkv_cross,
    wo_cross,
    w_up,
    w_down,
    ln_gain,
    ln_bias,
):
    rows, width = target.shape
    half = rows // 2
    tiles = rows // TILE
    hidden_width = w_down.shape[0]
    groups = lax.axis_size("mem")
    me = lax.axis_index("mem")
    count = tgt_len.shape[1]
    span = memory.shape[1]
    places, away = groups * span, (groups - 1) * span
    dp = lax.axis_index("dp")
    short = width // 2
    first_sum = Summing(hidden_width + short, width, False)
    second_sum = Summing(3 * width + short, width, True)
    spot = first_sum.spot(me, dp)
    stats = (PAIRS * tiles, 2 * TILE)

    came = []
    for shift in range(1, groups):
        pairs = [(i, (i + shift) % groups) for i in range(groups)]
        sent = lax.dynamic_slice_in_dim(memory, ((me + shift) % groups) * count, count, 0)
        came.append(lax.ppermute(sent, "mem", pairs))

    sorted_rows, qkv, self_norm, self_attn_t, hidden_one, query, part, part_top, part_sum, pair_mine = call(
        functools.partial(self_forward_kernel, groups),
        [
            ((rows, width), BF16),
            ((rows, 3 * width), BF16),
            (stats, F32),
            ((width, rows), BF16),
            ((rows, width), F32),
            ((rows, width), BF16),
            ((width, rows), F32),
            (stats, F32),
            (stats, F32),
            ((count, places, 2 * width), BF16),
        ],
        [
            ((tiles, half, 2 * TILE), F32),
            ((count, span, 2 * TILE), F32),
            ((tiles, 2 * TILE, width), BF16),
            ((width, rows), BF16),
            ((count, width, span), BF16),
            ((count, span, 2 * width), BF16),
            pltpu.SemaphoreType.DMA((count,)),
        ],
        3,
        spot,
        tgt_len,
        src_len,
        target,
        w_qkv,
        w_out,
        wq_cross,
        ln_gain,
        ln_bias,
        memory,
        wkv_cross,
        vmem=60,
        hbm_out=1,
    )
    result_out, cross_norm, cross_along, keep_one, send_one, grad_hidden_two, grad_attn, ln_part, pair_all = middle(
        groups, first_sum, stats, spot, tgt_len, src_len, hidden_one, query, part, part_top, part_sum, wkv_cross,
        ln_gain, ln_bias, wo_cross, w_up, w_down, grad_out, pair_mine, came,
    )
    came_one = first_sum.core_swap(send_one)

    def cross_backward(block):
        sentences = 1 if block == 0 else count - 1
        return call(
            functools.partial(cross_backward_kernel, groups, block),
            [((sentences, places, 2 * width), BF16), ((width, half), BF16)],
            [
                ((sentences, places, 2 * width), BF16),
                ((sentences, places, 2 * TILE), F32),
                ((half // TILE, 2 * TILE, width), BF16),
                ((half // TILE, 2 * TILE, width), BF16),
                ((sentences, width, places), BF16),
                ((SLAB, half), F32),
                ((sentences, places, 2 * SLAB), F32),
                pltpu.SemaphoreType.DMA((1,)),
            ],
            3,
            spot,
            tgt_len,
            src_len,
            query,
            cross_norm,
            cross_along,
            grad_attn,
            pair_all,
            work=10,
            vmem=24 if block == 0 else 32,
            hbm_in=1,
        )

    pair_grad_long, query_grad_t_long = cross_backward(0)
    came_one, pair_grad_long = lax.optimization_barrier((came_one, pair_grad_long))
    parts_one = first_sum.first_split(spot, keep_one, came_one)
    parts_one, pair_all = lax.optimization_barrier((parts_one, pair_all))
    parts_one = first_sum.swap(parts_one, 0)
    pair_grad_rest, query_grad_t_rest = cross_backward(1)
    (wkv_grad,) = call(
        functools.partial(memory_weight_kernel, groups),
        [((2, width, width), BF16)],
        [((width, 2 * width), F32)],
        2,
        spot,
        tgt_len,
        pair_grad_long,
        pair_grad_rest,
        memory,
        *came,
        work=1,
        vmem=32,
    )
    parts_one, wkv_grad = lax.optimization_barrier((parts_one, wkv_grad))
    parts_one = first_sum.split(1, spot, parts_one)
    parts_one, wkv_grad = lax.optimization_barrier((parts_one, wkv_grad))
    parts_one = first_sum.swap(parts_one, 1)
    keep_mid, send_mid, grad_hidden_one, grad_self = call(
        first_norm_backward_kernel,
        [
            ((2 * width + LN_ROWS, width), BF16),
            ((2 * width + LN_ROWS, width), BF16),
            ((rows, width), F32),
            ((rows, width), BF16),
        ],
        [],
        1,
        spot,
        hidden_one,
        query_grad_t_long,
        query_grad_t_rest,
        grad_hidden_two,
        wq_cross,
        w_out,
        self_attn_t,
        ln_gain,
        ln_bias,
        ln_part,
        wkv_grad,
        work=10,
        vmem=24,
    )
    grad_triple, *last = call(
        self_backward_kernel,
        [((rows, 3 * width), BF16)] + [(((width + short) // LAST_PARTS, width), BF16)] * (2 * LAST_PARTS),
        [
            ((tiles, half, 2 * TILE), F32),
            ((tiles, 2 * TILE, width), BF16),
            ((tiles, 2 * TILE, width), BF16),
            ((width, rows), BF16),
            ((width, rows), BF16),
        ],
        2,
        spot,
        tgt_len,
        qkv,
        self_norm,
        grad_self,
        sorted_rows,
        work=0.1,
        vmem=28,
    )
    parts_one, last, send_mid, pair_grad_long = lax.optimization_barrier(
        (parts_one, last, send_mid, pair_grad_long)
    )
    keep_last = last[:LAST_PARTS]
    came_last = [second_sum.core_swap(part) for part in last[LAST_PARTS:]]
    came_mid = second_sum.core_swap(send_mid)
    parts_one = first_sum.split(2, spot, parts_one)
    came_mid, parts_one = lax.optimization_barrier((came_mid, parts_one))
    parts_two = second_sum.first_split(
        spot, keep_mid, came_mid, *[part for both in zip(keep_last, came_last) for part in both]
    )
    parts_one = first_sum.swap(parts_one, 2)
    parts_two, pair_grad_long, grad_triple = lax.optimization_barrier((parts_two, pair_grad_long, grad_triple))
    parts_two = second_sum.swap(parts_two, 0)
    grad_mine, *grad_away = call(
        functools.partial(memory_grad_kernel, groups),
        [((count, span, width), BF16)] + [((count, span // 2, width), BF16)] * (2 * (groups - 1)),
        [],
        2,
        spot,
        tgt_len,
        pair_grad_long,
        pair_grad_rest,
        wkv_cross,
        work=0.01,
        vmem=32,
    )
    (grad_target,) = call(
        target_kernel,
        [((rows, width), BF16)],
        [],
        2,
        spot,
        tgt_len,
        grad_triple,
        w_qkv,
        grad_hidden_one,
        work=0.01,
        vmem=16,
    )
    parts_one, parts_two, grad_away, grad_target = lax.optimization_barrier(
        (parts_one, parts_two, grad_away, grad_target)
    )
    backs = [[], []]
    for i, grads in enumerate(grad_away):
        shift = i // 2 + 1
        backs[i % 2].append(lax.ppermute(grads, "mem", [(k, (k - shift) % groups) for k in range(groups)]))
    parts_two = second_sum.swap(second_sum.split(1, spot, parts_two), 1)
    spread_one = first_sum.spread(2, first_sum.total(parts_one)[0])
    parts_two, spread_one, backs[0] = lax.optimization_barrier((parts_two, spread_one, backs[0]))
    spread_one = first_sum.spread(1, first_sum.join(2, spot, spread_one))
    parts_two = second_sum.swap(second_sum.split(2, spot, parts_two), 2)
    parts_two, spread_one, backs[1] = lax.optimization_barrier((parts_two, spread_one, backs[1]))
    spread_one = first_sum.spread(0, first_sum.join(1, spot, spread_one))
    sum_two, norm_sums = second_sum.total(parts_two)
    spread_two = second_sum.spread(2, sum_two)
    spread_two, spread_one = lax.optimization_barrier((spread_two, spread_one))
    other_one = [first_sum.core_swap(array) for array in spread_one]
    spread_two = second_sum.spread(1, second_sum.join(2, spot, spread_two))
    chunks = hidden_width // width
    pieces = []
    for chunk in range(chunks):
        side, here = chunk // (chunks // 2), chunk % (chunks // 2)
        pieces.append((side, here * width, width, 0, chunk * width, 0))
        pieces.append((side, (chunks // 2 + here) * width, width, 1, 0, chunk * width))
    for side in range(2):
        pieces.append((side, chunks * width, short, 2, side * short, 0))
    grad_w_down, grad_w_up, grad_wo = first_sum.finish(
        spot,
        spread_one,
        other_one,
        pieces,
        [((hidden_width, width), F32), ((width, hidden_width), F32), ((width, width), F32)],
    )
    spread_two, grad_w_down = lax.optimization_barrier((spread_two, grad_w_down))
    spread_two = second_sum.spread(0, second_sum.join(1, spot, spread_two))
    other_two = [second_sum.core_swap(array) for array in spread_two]
    pieces = [
        (0, 0, width, 0, 0, 0),
        (0, width, width, 1, 0, 0),
        (0, 2 * width, width, 2, 0, 0),
        (0, 3 * width, short, 2, 0, width),
        (1, 0, width, 1, 0, width),
        (1, width, width, 3, 0, 0),
        (1, 2 * width, short, 2, short, width),
        (1, 2 * width + short, width, 2, 0, 2 * width),
    ]
    grad_wq, grad_wkv, grad_w_qkv, grad_w_out = second_sum.finish(
        spot,
        spread_two,
        other_two,
        pieces,
        [
            ((width, width), F32),
            ((width, 2 * width), F32),
            ((width, 3 * width), F32),
            ((width, width), F32),
        ],
    )
    grad_memory = jnp.zeros(memory.shape, BF16)
    grad_memory = lax.dynamic_update_slice(grad_memory, grad_mine, (me * count, 0, 0))
    for part in range(2):
        for i, grads in enumerate(backs[part]):
            owner = (me + i + 1) % groups
            grad_memory = lax.dynamic_update_slice(grad_memory, grads, (owner * count, part * (span // 2), 0))
    return (
        result_out,
        grad_target,
        grad_memory,
        grad_w_qkv,
        grad_w_out,
        grad_wq,
        grad_wkv,
        grad_wo,
        grad_w_up,
        grad_w_down,
        norm_sums[:3],
        norm_sums[3:6],
    )


def solution(mesh):
    rows_spec = P(("dp", "mem"), None)
    memory_spec = P("dp", "mem", None)
    return jax.shard_map(
        body,
        mesh=mesh,
        in_specs=(rows_spec, memory_spec, rows_spec, P("dp", None), P("dp", None)) + (P(),) * 9,
        out_specs=(rows_spec, rows_spec, memory_spec) + (P(),) * 9,
        check_vma=False,
    )
```

```python
import functools
import math

import jax
import jax.numpy as jnp
from jax import lax
from jax.experimental import pallas as pl
from jax.experimental.pallas import tpu as pltpu
from jax.sharding import PartitionSpec as P

HEADS = 8
PAIRS = HEADS // 2
SLAB = 128
SIDE = SLAB // 2
TILE = 128
MASKED = -1e30
EPSILON = 1e-05
F32 = jnp.float32
BF16 = jnp.bfloat16
MIB = 1024 * 1024
LN_ROWS = 16
LAST_PARTS = 1


def dot(left, right):
    return jnp.dot(left, right, preferred_element_type=F32)


def dot_nt(left, right):
    return lax.dot_general(left, right, (((1,), (1,)), ((), ())), preferred_element_type=F32)


def dot_tn(left, right):
    return lax.dot_general(left, right, (((0,), (0,)), ((), ())), preferred_element_type=F32)


def iota(shape, axis):
    return lax.broadcasted_iota(jnp.int32, shape, axis)


def norm_parts(hidden):
    centre = hidden - jnp.mean(hidden, axis=-1, keepdims=True)
    inverse = lax.rsqrt(jnp.mean(centre * centre, axis=-1, keepdims=True) + EPSILON)
    return centre * inverse, inverse


def norm_backward(upstream, unit, inverse, gain_row):
    scaled = upstream * gain_row
    shifted = (
        scaled
        - jnp.mean(scaled, axis=-1, keepdims=True)
        - unit * jnp.mean(scaled * unit, axis=-1, keepdims=True)
    )
    gain_grad = jnp.sum(upstream * unit, axis=0, keepdims=True)
    return inverse * shifted, gain_grad, jnp.sum(upstream, axis=0, keepdims=True)


def sentence_order(me, len_ref):
    count = len_ref.shape[1]
    lengths = [len_ref[me, k] for k in range(count)]
    longest, best, start, running = jnp.int32(0), lengths[0], jnp.int32(0), jnp.int32(0)
    for k in range(1, count):
        running = running + lengths[k - 1]
        more = lengths[k] > best
        longest = jnp.where(more, k, longest)
        start = jnp.where(more, running, start)
        best = jnp.where(more, lengths[k], best)
    order = [longest] + [jnp.where(k < longest, k, k + 1) for k in range(count - 1)]
    bounds = [jnp.int32(0)]
    for k in range(1, count):
        bounds.append(bounds[-1] + len_ref[me, order[k]])
    return order, start, bounds


def moved_rows(index, start, half):
    return jnp.where(index < start, index + half, jnp.where(index < start + half, index - start, index))


def sort_matrix(rows, start):
    spot = moved_rows(iota((rows, rows), 1), start, rows // 2)
    return jnp.where(spot == iota((rows, rows), 0), 1.0, 0.0).astype(BF16)


def unsort_matrix(rows, start):
    spot = moved_rows(iota((rows, rows), 0), start, rows // 2)
    return jnp.where(spot == iota((rows, rows), 1), 1.0, 0.0).astype(BF16)


def side_masks(width):
    side = iota((1, width), 1) % SLAB
    first = jnp.where(side < SLAB // 2, 1.0, 0.0)
    return first.astype(BF16), (1.0 - first).astype(BF16)


def slab_of(pair, first=0):
    return pl.ds(pl.multiple_of(first + pair * SLAB, SLAB), SLAB)


def pack_heads(out_ref, rows, width):
    even, odd = side_masks(width)
    for t in range(out_ref.shape[0]):
        tile = rows(t * TILE, TILE)
        out_ref[t, :TILE, :] = tile * even
        out_ref[t, TILE:, :] = tile * odd


def fill_self_bias(bias_ref, bounds, half):
    for t in range(bias_ref.shape[0]):
        block, inner = t // (half // TILE), t % (half // TILE)
        key = iota((half, 2 * TILE), 0)
        query = iota((half, 2 * TILE), 1) % TILE + inner * TILE
        allowed = key <= query
        if block == 1:
            first = jnp.zeros((half, 2 * TILE), jnp.int32)
            for bound in bounds[1:-1]:
                first = jnp.where(query >= bound, bound, first)
            allowed = allowed & (key >= first)
        bias_ref[t] = jnp.where(allowed, 0.0, MASKED)


def self_keys(t, half):
    per = half // TILE
    return (t // per) * half, (t % per + 1) * TILE


def fill_live_bias(bias_ref, me, groups, parts, span, src_ref, sentences):
    key = iota((span, bias_ref.shape[2]), 0)
    for j, sentence in enumerate(sentences):
        for i, part in enumerate(parts):
            place = lax.rem(me - part + groups, groups) * span + key
            live = place < src_ref[me, sentence]
            bias_ref[j, pl.ds(i * span, span), :] = jnp.where(live, 0.0, MASKED)


def cross_units(bounds, half):
    units = [(t, 0, None) for t in range(half // TILE)]
    middle = half // 2
    last = jnp.int32(1)
    for bound in bounds[1:-1]:
        last = last + jnp.where(bound < middle, 1, 0)
    ends = bounds[1:]
    column = iota((1, 2 * TILE), 1) % TILE
    for u in range(len(ends) + 1):
        early = u < last
        sentence = jnp.where(early, u + 1, u)
        tile = jnp.where(early, 0, 1)
        low, high = jnp.int32(0), ends[0]
        for k in range(1, len(ends)):
            low = jnp.where(sentence == k + 1, ends[k - 1], low)
            high = jnp.where(sentence == k + 1, ends[k], high)
        row = column + tile * TILE
        units.append((tile + half // TILE, sentence, (row >= low) & (row < high)))
    return units


def own_sides(both):
    return jnp.concatenate([both[:SIDE, :TILE], both[SIDE:, TILE:]], axis=0)


def side_rows(row):
    even = jnp.broadcast_to(row[:, :TILE], (SIDE, TILE))
    return jnp.concatenate([even, jnp.broadcast_to(row[:, TILE:], (SIDE, TILE))], axis=0)


def tile_columns(tile):
    if isinstance(tile, int):
        return pl.ds(tile * TILE, TILE)
    return pl.ds(pl.multiple_of(tile * TILE, TILE), TILE)


def self_forward_kernel(
    groups,
    me_ref,
    len_ref,
    src_ref,
    target_ref,
    w_qkv_ref,
    w_out_ref,
    wq_ref,
    gain_ref,
    bias_row_ref,
    memory_ref,
    wkv_ref,
    sorted_ref,
    qkv_ref,
    norm_ref,
    attn_t_ref,
    hidden_ref,
    query_ref,
    part_ref,
    top_ref,
    sum_ref,
    pair_out_ref,
    bias_ref,
    live_ref,
    q_pack_ref,
    value_t_ref,
    cross_value_t_ref,
    pair_ref,
    copy_sem,
):
    rows, width = target_ref.shape
    half = rows // 2
    me = me_ref[0]
    order, start, bounds = sentence_order(me, len_ref)
    count, span = pair_ref.shape[0], pair_ref.shape[1]
    copies = []
    for j in range(count):
        block = memory_ref[me * count + order[j]]
        pair_ref[j] = dot(block, wkv_ref[...]).astype(BF16)
        copy = pltpu.make_async_copy(
            pair_ref.at[j], pair_out_ref.at[j, pl.ds(0, span), :], copy_sem.at[j]
        )
        copy.start()
        copies.append(copy)
    sorted_rows = dot(sort_matrix(rows, start), target_ref[...]).astype(BF16)
    sorted_ref[...] = sorted_rows
    fill_self_bias(bias_ref, bounds, half)
    queries = (dot(sorted_rows, w_qkv_ref[:, :width]).astype(BF16) * 0.125).astype(BF16)
    qkv_ref[:, :width] = queries
    pack_heads(q_pack_ref, lambda first, size: queries[first : first + size], width)
    qkv_ref[:, width : 2 * width] = dot(sorted_rows, w_qkv_ref[:, width : 2 * width]).astype(BF16)
    values = dot(sorted_rows, w_qkv_ref[:, 2 * width :]).astype(BF16)
    qkv_ref[:, 2 * width :] = values
    value_t_ref[...] = values.T
    tiles = rows // TILE

    def self_step(pair, carry):
        slab = slab_of(pair)
        for t in range(tiles):
            first, size = self_keys(t, half)
            keys = qkv_ref[pl.ds(first, size), slab_of(pair, width)]
            scores = dot_nt(keys, q_pack_ref[t, :, slab]) + bias_ref[t, :size, :]
            top = jnp.max(scores, axis=0, keepdims=True)
            weights = jnp.exp(scores - top)
            total = jnp.sum(weights, axis=0, keepdims=True)
            probs = (weights * (1.0 / total)).astype(BF16)
            both = dot(value_t_ref[slab, pl.ds(first, size)], probs)
            attn_t_ref[slab, tile_columns(t)] = own_sides(both).astype(BF16)
            norm_ref[pl.ds(pair * tiles + t, 1), :] = top + jnp.log(total)
        return carry

    lax.fori_loop(0, PAIRS, self_step, 0)
    hidden = sorted_rows.astype(F32) + dot(attn_t_ref[...].T, w_out_ref[...])
    hidden_ref[...] = hidden
    unit, _ = norm_parts(hidden)
    normed = (unit * gain_ref[0:1] + bias_row_ref[0:1]).astype(BF16)
    query_ref[...] = (dot(normed, wq_ref[...]).astype(BF16) * 0.125).astype(BF16)

    pack_heads(q_pack_ref, lambda first, size: query_ref[first : first + size, :], width)
    fill_live_bias(live_ref, me, groups, [0], span, src_ref, order)
    for j in range(count):
        cross_value_t_ref[j] = pair_ref[j, :, width:].T
    units = cross_units(bounds, half)

    def cross_step(pair, carry):
        slab = slab_of(pair)
        for tile, sentence, columns in units:
            scores = dot_nt(pair_ref[sentence, :, slab], q_pack_ref[tile, :, slab]) + live_ref[sentence]
            top = jnp.max(scores, axis=0, keepdims=True)
            weights = jnp.exp(scores - top)
            total = jnp.sum(weights, axis=0, keepdims=True)
            result = own_sides(dot(cross_value_t_ref[sentence, slab, :], weights.astype(BF16)))
            here = tile_columns(tile)
            row = pl.ds(pair * tiles + tile, 1)
            if columns is not None:
                result = jnp.where(columns[:, :TILE], result, part_ref[slab, here])
                top = jnp.where(columns, top, top_ref[row, :])
                total = jnp.where(columns, total, sum_ref[row, :])
            part_ref[slab, here] = result
            top_ref[row, :] = top
            sum_ref[row, :] = total
        return carry

    part_ref[...] = jnp.zeros_like(part_ref)
    top_ref[...] = jnp.zeros_like(top_ref)
    sum_ref[...] = jnp.ones_like(sum_ref)
    lax.fori_loop(0, PAIRS, cross_step, 0)
    for copy in copies:
        copy.wait()


def middle_kernel(
    groups,
    me_ref,
    len_ref,
    src_ref,
    hidden_one_ref,
    query_ref,
    part_ref,
    top_ref,
    sum_ref,
    wkv_ref,
    gain_ref,
    bias_row_ref,
    wo_hbm,
    w_up_hbm,
    w_down_hbm,
    grad_out_hbm,
    pair_in_hbm,
    *refs,
):
    came_refs = refs[: groups - 1]
    (
        out_ref,
        norm_ref,
        along_ref,
        keep_hbm,
        send_hbm,
        grad_hidden_ref,
        grad_attn_ref,
        ln_ref,
        pair_hbm,
        wo_ref,
        w_up_ref,
        w_down_ref,
        grad_out_ref,
        pair_ref,
        keep_ref,
        send_ref,
        live_ref,
        q_pack_ref,
        value_t_ref,
        attn_t_ref,
        active_ref,
        slope_ref,
        total_ref,
        load_sem,
        pair_sem,
        store_sem,
    ) = refs[groups - 1 :]
    rows, width = hidden_one_ref.shape
    half = rows // 2
    me = me_ref[0]
    count, away = pair_ref.shape[0], pair_ref.shape[1]
    span = away // (groups - 1)
    loads = [
        pltpu.make_async_copy(source, there, load_sem.at[i])
        for i, (source, there) in enumerate(
            [(wo_hbm, wo_ref), (w_up_hbm, w_up_ref), (w_down_hbm, w_down_ref), (grad_out_hbm, grad_out_ref)]
        )
    ]
    for copy in loads:
        copy.start()
    order, start, bounds = sentence_order(me, len_ref)
    fill_live_bias(live_ref, me, groups, list(range(1, groups)), span, src_ref, order)
    pack_heads(q_pack_ref, lambda first, size: query_ref[first : first + size, :], width)
    pair_copies = []
    for j in range(count):
        for part in range(1, groups):
            block = came_refs[part - 1][order[j]]
            pair_ref[j, pl.ds((part - 1) * span, span), :] = dot(block, wkv_ref[...]).astype(BF16)
        value_t_ref[j] = pair_ref[j, :, width:].T
        copy = pltpu.make_async_copy(pair_ref.at[j], pair_hbm.at[j, pl.ds(span, away), :], pair_sem.at[j])
        copy.start()
        pair_copies.append(copy)
    units = cross_units(bounds, half)
    tiles = rows // TILE

    def cross_step(pair, carry):
        slab = slab_of(pair)
        for tile, sentence, columns in units:
            here = tile_columns(tile)
            row = pl.ds(pair * tiles + tile, 1)
            scores = dot_nt(pair_ref[sentence, :, slab], q_pack_ref[tile, :, slab]) + live_ref[sentence]
            before = top_ref[row, :]
            top = jnp.maximum(jnp.max(scores, axis=0, keepdims=True), before)
            weights = jnp.exp(scores - top)
            scale = jnp.exp(before - top)
            total = jnp.sum(weights, axis=0, keepdims=True) + sum_ref[row, :] * scale
            result = own_sides(dot(value_t_ref[sentence, slab, :], weights.astype(BF16)))
            result = (result + part_ref[slab, here] * side_rows(scale)) * side_rows(1.0 / total)
            norm = top + jnp.log(total)
            if columns is not None:
                result = jnp.where(columns[:, :TILE], result, attn_t_ref[slab, here])
                norm = jnp.where(columns, norm, norm_ref[row, :])
            attn_t_ref[slab, here] = result
            norm_ref[row, :] = norm
        return carry

    attn_t_ref[...] = jnp.zeros_like(attn_t_ref)
    norm_ref[...] = jnp.zeros_like(norm_ref)
    lax.fori_loop(0, PAIRS, cross_step, 0)
    attn_t_low = attn_t_ref[...].astype(BF16)
    loads[0].wait()
    unit_one, _ = norm_parts(hidden_one_ref[...])
    normed_one = unit_one * gain_ref[0:1] + bias_row_ref[0:1]
    hidden_two = normed_one + dot(attn_t_low.T, wo_ref[...])
    unit_two, inverse_two = norm_parts(hidden_two)
    normed_two = unit_two * gain_ref[1:2] + bias_row_ref[1:2]
    normed_two_low = normed_two.astype(BF16)
    total_ref[...] = normed_two
    chunk = width
    chunks = w_down_ref.shape[0] // chunk
    loads[1].wait()
    loads[2].wait()

    def up_step(c, carry):
        cols = pl.ds(pl.multiple_of(c * chunk, chunk), chunk)
        upper = dot(normed_two_low, w_up_ref[:, cols])
        sigma = 0.5 * jnp.tanh(0.5 * upper) + 0.5
        active = (upper * sigma).astype(BF16)
        active_ref[:, cols] = active
        slope_ref[:, cols] = sigma * (1.0 + upper * (1.0 - sigma))
        total_ref[...] += dot(active, w_down_ref[cols, :])
        return carry

    lax.fori_loop(0, chunks, up_step, 0)
    unit_three, inverse_three = norm_parts(total_ref[...])
    result = (unit_three * gain_ref[2:3] + bias_row_ref[2:3]).astype(BF16)
    out_ref[...] = dot(unsort_matrix(rows, start), result).astype(BF16)
    loads[3].wait()
    upstream = dot(sort_matrix(rows, start), grad_out_ref[...])
    grad_three, gain_three, bias_three = norm_backward(upstream, unit_three, inverse_three, gain_ref[2:3])
    grad_down = grad_three.astype(BF16)
    total_ref[...] = grad_three
    normed_two_t = normed_two_low.T

    def down_step(c, carry):
        cols = pl.ds(pl.multiple_of(c * chunk, chunk), chunk)
        grad_upper = (dot_nt(grad_down, w_down_ref[cols, :]) * slope_ref[:, cols]).astype(BF16)
        down_part = dot_tn(active_ref[:, cols], grad_down).astype(BF16)
        up_part = dot(normed_two_t, grad_upper).astype(BF16)
        here = lax.rem(c, chunks // 2)
        down_rows = pl.ds(pl.multiple_of(here * chunk, chunk), chunk)
        up_rows = pl.ds(pl.multiple_of((chunks // 2 + here) * chunk, chunk), chunk)
        mine = c // (chunks // 2) == me_ref[1]

        @pl.when(mine)
        def _():
            keep_ref[down_rows, :] = down_part
            keep_ref[up_rows, :] = up_part

        @pl.when(jnp.logical_not(mine))
        def _():
            send_ref[down_rows, :] = down_part
            send_ref[up_rows, :] = up_part

        total_ref[...] += dot_nt(grad_upper, w_up_ref[:, cols])
        return carry

    lax.fori_loop(0, chunks, down_step, 0)
    most = chunks * chunk
    stores = [
        pltpu.make_async_copy(ref.at[pl.ds(first, size)], there.at[pl.ds(first, size)], store_sem.at[i])
        for i, (ref, there, first, size) in enumerate(
            [
                (send_ref, send_hbm, 0, most),
                (keep_ref, keep_hbm, 0, most),
                (send_ref, send_hbm, most, keep_ref.shape[0] - most),
                (keep_ref, keep_hbm, most, keep_ref.shape[0] - most),
            ]
        )
    ]
    stores[0].start()
    stores[1].start()
    grad_two, gain_two, bias_two = norm_backward(total_ref[...], unit_two, inverse_two, gain_ref[1:2])
    grad_two_low = grad_two.astype(BF16)
    wo_grad = dot(attn_t_low, grad_two_low).astype(BF16)
    core = me_ref[1]
    low, high = wo_grad[: width // 2], wo_grad[width // 2 :]
    tail = pl.ds(most, width // 2)
    keep_ref[tail, :] = jnp.where(core == 0, low, high)
    send_ref[tail, :] = jnp.where(core == 0, high, low)
    used = most + width // 2
    if keep_ref.shape[0] > used:
        keep_ref[used:, :] = jnp.zeros((keep_ref.shape[0] - used, width), BF16)
        send_ref[used:, :] = jnp.zeros((keep_ref.shape[0] - used, width), BF16)
    stores[2].start()
    stores[3].start()
    grad_hidden_ref[...] = grad_two
    grad_attn = dot_nt(grad_two_low, wo_ref[...]).astype(BF16)
    grad_attn_ref[...] = grad_attn
    product = grad_attn.T.astype(F32) * attn_t_ref[...]
    for pair in range(PAIRS):
        for side in range(2):
            first = pair * SLAB + side * SIDE
            along = jnp.sum(product[first : first + SIDE], axis=0, keepdims=True)
            for t in range(tiles):
                along_ref[pair * tiles + t : pair * tiles + t + 1, side * TILE : (side + 1) * TILE] = along[
                    :, t * TILE : (t + 1) * TILE
                ]
    ln_ref[...] = jnp.concatenate([gain_two, gain_three, bias_two, bias_three], axis=0)
    for copy in pair_copies + stores:
        copy.wait()


def cross_backward_kernel(
    groups,
    block,
    me_ref,
    len_ref,
    src_ref,
    query_ref,
    norm_ref,
    along_ref,
    grad_attn_ref,
    pair_hbm,
    pair_grad_ref,
    query_grad_t_ref,
    pair_ref,
    live_ref,
    q_pack_ref,
    g_pack_ref,
    key_t_ref,
    query_sum_ref,
    sum_ref,
    load_sem,
):
    rows, width = query_ref.shape
    half = rows // 2
    me = me_ref[0]
    sentences, places = pair_ref.shape[0], pair_ref.shape[1]
    first_sentence = 0 if block == 0 else 1
    load = pltpu.make_async_copy(pair_hbm.at[pl.ds(first_sentence, sentences)], pair_ref, load_sem.at[0])
    load.start()
    order, start, bounds = sentence_order(me, len_ref)
    mine = order[:1] if block == 0 else order[1:]
    fill_live_bias(live_ref, me, groups, list(range(groups)), places // groups, src_ref, mine)
    low = block * half
    pack_heads(q_pack_ref, lambda first, size: query_ref[low + first : low + first + size, :], width)
    pack_heads(g_pack_ref, lambda first, size: grad_attn_ref[low + first : low + first + size, :], width)
    tiles, per = rows // TILE, half // TILE
    units = cross_units(bounds, half)
    units = units[:per] if block == 0 else units[per:]
    load.wait()
    for j in range(sentences):
        key_t_ref[j] = pair_ref[j, :, :width].T

    def pair_step(pair, carry):
        slab, value_slab = slab_of(pair), slab_of(pair, width)
        query_sum_ref[...] = jnp.zeros_like(query_sum_ref)
        sum_ref[...] = jnp.zeros_like(sum_ref)
        for tile, sentence, columns in units:
            j = sentence - first_sentence
            t = tile - block * per
            here = tile_columns(t)
            row = pl.ds(pair * tiles + tile, 1)
            q_rows, g_rows = q_pack_ref[t, :, slab], g_pack_ref[t, :, slab]
            norm = norm_ref[row, :]
            if columns is not None:
                norm = jnp.where(columns, norm, -MASKED)
            scores = dot_nt(pair_ref[j, :, slab], q_rows) + live_ref[j]
            probs = jnp.exp(scores - norm)
            grad_probs = dot_nt(pair_ref[j, :, value_slab], g_rows)
            grad_scores = (probs * (grad_probs - along_ref[row, :])).astype(BF16)
            sum_ref[j, :, :SLAB] += dot(grad_scores, q_rows)
            sum_ref[j, :, SLAB:] += dot(probs.astype(BF16), g_rows)
            query_sum_ref[:, here] += own_sides(dot(key_t_ref[j, slab, :], grad_scores))
        query_grad_t_ref[slab, :] = (query_sum_ref[...] * 0.125).astype(BF16)
        pair_grad_ref[:, :, slab] = sum_ref[:, :, :SLAB].astype(BF16)
        pair_grad_ref[:, :, value_slab] = sum_ref[:, :, SLAB:].astype(BF16)
        return carry

    lax.fori_loop(0, PAIRS, pair_step, 0)


def memory_weight_kernel(groups, me_ref, len_ref, pair_grad_long_ref, pair_grad_rest_ref, memory_ref, *refs):
    came_refs = refs[: groups - 1]
    wkv_grad_ref, total_ref = refs[groups - 1 :]
    width = memory_ref.shape[2]
    me = me_ref[0]
    count = len_ref.shape[1]
    span = pair_grad_long_ref.shape[1] // groups
    order, _, _ = sentence_order(me, len_ref)
    for j in range(count):
        pair_grad_ref, here = (pair_grad_long_ref, 0) if j == 0 else (pair_grad_rest_ref, j - 1)
        blocks = [memory_ref[me * count + order[j]]] + [ref[order[j]] for ref in came_refs]
        term = dot_tn(jnp.concatenate(blocks, axis=0), pair_grad_ref[here])
        if j == 0:
            total_ref[...] = term
        else:
            total_ref[...] += term
    wkv_grad_ref[0] = total_ref[:, :width].astype(BF16)
    wkv_grad_ref[1] = total_ref[:, width:].astype(BF16)


def memory_grad_kernel(
    groups, me_ref, len_ref, pair_grad_long_ref, pair_grad_rest_ref, wkv_ref, mine_ref, *away_refs
):
    count = len_ref.shape[1]
    span = pair_grad_long_ref.shape[1] // groups
    order, _, _ = sentence_order(me_ref[0], len_ref)
    for j in range(count):
        pair_grad_ref, here = (pair_grad_long_ref, 0) if j == 0 else (pair_grad_rest_ref, j - 1)
        grads = dot_nt(pair_grad_ref[here], wkv_ref[...]).astype(BF16)
        mine_ref[order[j]] = grads[:span]
        for i, ref in enumerate(away_refs):
            first = span + i * (span // 2)
            ref[order[j]] = grads[first : first + span // 2]


def first_norm_backward_kernel(
    me_ref,
    hidden_one_ref,
    query_grad_t_long_ref,
    query_grad_t_rest_ref,
    grad_hidden_two_ref,
    wq_ref,
    w_out_ref,
    self_attn_t_ref,
    gain_ref,
    bias_row_ref,
    ln_in_ref,
    wkv_grad_ref,
    keep_ref,
    send_ref,
    grad_hidden_ref,
    grad_self_ref,
):
    width = wq_ref.shape[0]
    unit_one, inverse_one = norm_parts(hidden_one_ref[...])
    normed_one = (unit_one * gain_ref[0:1] + bias_row_ref[0:1]).astype(BF16)
    query_grad = jnp.concatenate([query_grad_t_long_ref[...].T, query_grad_t_rest_ref[...].T], axis=0)
    upstream = grad_hidden_two_ref[...] + dot_nt(query_grad, wq_ref[...])
    grad_one, gain_one, bias_one = norm_backward(upstream, unit_one, inverse_one, gain_ref[0:1])
    grad_hidden_ref[...] = grad_one
    grad_one_low = grad_one.astype(BF16)
    grad_self_ref[...] = dot_nt(grad_one_low, w_out_ref[...]).astype(BF16)
    wq_grad = dot_tn(normed_one, query_grad).astype(BF16)
    w_out_grad = dot(self_attn_t_ref[...], grad_one_low).astype(BF16)
    norms = jnp.concatenate(
        [gain_one, ln_in_ref[0:2], bias_one, ln_in_ref[2:4], jnp.zeros((LN_ROWS - 6, width), F32)], axis=0
    ).astype(BF16)

    def halves(low_ref, high_ref):
        low_ref[:width, :] = wq_grad
        low_ref[width : 2 * width, :] = wkv_grad_ref[0]
        high_ref[:width, :] = wkv_grad_ref[1]
        high_ref[width : 2 * width, :] = w_out_grad

    @pl.when(me_ref[1] == 0)
    def _():
        halves(keep_ref, send_ref)

    @pl.when(me_ref[1] != 0)
    def _():
        halves(send_ref, keep_ref)

    keep_ref[2 * width :, :] = norms
    send_ref[2 * width :, :] = norms


def self_backward_kernel(
    me_ref,
    len_ref,
    qkv_ref,
    norm_ref,
    grad_attn_ref,
    sorted_ref,
    grad_triple_ref,
    *refs,
):
    keep_refs, send_refs = refs[:LAST_PARTS], refs[LAST_PARTS : 2 * LAST_PARTS]
    self_backward(
        me_ref,
        len_ref,
        qkv_ref,
        norm_ref,
        grad_attn_ref,
        sorted_ref,
        grad_triple_ref,
        keep_refs,
        send_refs,
        *refs[2 * LAST_PARTS :],
    )


def self_backward(
    me_ref,
    len_ref,
    qkv_ref,
    norm_ref,
    grad_attn_ref,
    sorted_ref,
    grad_triple_ref,
    keep_refs,
    send_refs,
    bias_ref,
    q_pack_ref,
    g_pack_ref,
    key_t_ref,
    query_grad_t_ref,
):
    rows, width = sorted_ref.shape
    half = rows // 2
    _, _, bounds = sentence_order(me_ref[0], len_ref)
    fill_self_bias(bias_ref, bounds, half)
    pack_heads(q_pack_ref, lambda first, size: qkv_ref[first : first + size, :width], width)
    pack_heads(g_pack_ref, lambda first, size: grad_attn_ref[first : first + size, :], width)
    key_t_ref[...] = qkv_ref[:, width : 2 * width].T
    tiles, per = rows // TILE, half // TILE

    def pair_step(pair, carry):
        slab, key_slab, value_slab = slab_of(pair), slab_of(pair, width), slab_of(pair, 2 * width)
        sums = [[None, None] for _ in range(tiles)]
        for t in range(tiles):
            first, size = self_keys(t, half)
            span = pl.ds(first, size)
            q_rows, g_rows = q_pack_ref[t, :, slab], g_pack_ref[t, :, slab]
            scores = dot_nt(qkv_ref[span, key_slab], q_rows) + bias_ref[t, :size, :]
            probs = jnp.exp(scores - norm_ref[pl.ds(pair * tiles + t, 1), :])
            grad_probs = dot_nt(qkv_ref[span, value_slab], g_rows)
            along = jnp.sum(probs * grad_probs, axis=0, keepdims=True)
            grad_scores = (probs * (grad_probs - along)).astype(BF16)
            parts = dot(grad_scores, q_rows), dot(probs.astype(BF16), g_rows)
            for i in range(size // TILE):
                spot = sums[first // TILE + i]
                for k in range(2):
                    piece = parts[k][i * TILE : (i + 1) * TILE]
                    spot[k] = piece if spot[k] is None else spot[k] + piece
            query_grad_t_ref[slab, tile_columns(t)] = (
                own_sides(dot(key_t_ref[slab, span], grad_scores)) * 0.125
            ).astype(BF16)
        for t in range(tiles):
            grad_triple_ref[pl.ds(t * TILE, TILE), key_slab] = sums[t][0].astype(BF16)
            grad_triple_ref[pl.ds(t * TILE, TILE), value_slab] = sums[t][1].astype(BF16)
        return carry

    lax.fori_loop(0, PAIRS, pair_step, 0)
    grad_triple_ref[:, :width] = query_grad_t_ref[...].T
    sorted_t = sorted_ref[...].T
    grads = [
        dot(sorted_t, grad_triple_ref[:, part * width : (part + 1) * width]).astype(BF16)
        for part in range(3)
    ]
    short = width // 2

    low = jnp.concatenate([grads[0], grads[1][:short]], axis=0)
    high = jnp.concatenate([grads[1][short:], grads[2]], axis=0)
    size = keep_refs[0].shape[0]

    def halves(low_refs, high_refs):
        for i in range(LAST_PARTS):
            low_refs[i][...] = low[i * size : (i + 1) * size]
            high_refs[i][...] = high[i * size : (i + 1) * size]

    @pl.when(me_ref[1] == 0)
    def _():
        halves(keep_refs, send_refs)

    @pl.when(me_ref[1] != 0)
    def _():
        halves(send_refs, keep_refs)


def target_kernel(me_ref, len_ref, grad_triple_ref, w_qkv_ref, grad_hidden_ref, grad_target_ref):
    rows = grad_hidden_ref.shape[0]
    _, start, _ = sentence_order(me_ref[0], len_ref)
    result = grad_hidden_ref[...] + dot_nt(grad_triple_ref[...], w_qkv_ref[...])
    grad_target_ref[...] = dot(unsort_matrix(rows, start), result.astype(BF16)).astype(BF16)


def tree_sum(terms):
    while len(terms) > 1:
        terms = [terms[i] + terms[i + 1] for i in range(0, len(terms), 2)]
    return terms[0]


def rows_of(ref, first, count):
    return ref[pl.ds(pl.multiple_of(first, 16), count), :].astype(F32)


def first_split_kernel(segments, ln, peers, spot_ref, *refs):
    ins, outs, sum_ref = refs[: 2 * segments], refs[2 * segments : -1], refs[-1]
    extra = LN_ROWS if ln else 0
    size = outs[0].shape[0] - extra
    used = 0
    for i in range(segments):
        keep_ref, came_ref = ins[2 * i], ins[2 * i + 1]
        count = keep_ref.shape[0] - (extra if i == 0 else 0)
        sum_ref[used : used + count, :] = (rows_of(keep_ref, 0, count) + rows_of(came_ref, 0, count)).astype(BF16)
        if i == 0 and ln:
            tail = (rows_of(keep_ref, count, LN_ROWS) + rows_of(came_ref, count, LN_ROWS)).astype(BF16)
        used += count
    if sum_ref.shape[0] > used:
        sum_ref[used:, :] = jnp.zeros((sum_ref.shape[0] - used, sum_ref.shape[1]), BF16)
    for d, out in enumerate(outs):
        out[:size, :] = sum_ref[pl.ds(pl.multiple_of((spot_ref[2] ^ d) * size, 16), size), :]
        if ln:
            out[size:, :] = tail


def split_kernel(stage, ln, peers, spot_ref, *refs):
    ins, outs = refs[:peers], refs[peers:]
    extra = LN_ROWS if ln else 0
    size = outs[0].shape[0] - extra
    if ln:
        tail = tree_sum([rows_of(ref, size * len(outs), LN_ROWS) for ref in ins]).astype(BF16)
    for d, out in enumerate(outs):
        first = (spot_ref[2 + stage] ^ d) * size
        out[:size, :] = tree_sum([rows_of(ref, first, size) for ref in ins]).astype(BF16)
        if ln:
            out[size:, :] = tail


def total_kernel(ln, count, *refs):
    ins, outs = refs[:count], refs[count:]
    size = outs[0].shape[0]
    outs[0][...] = tree_sum([rows_of(ref, 0, size) for ref in ins]).astype(BF16)
    if ln:
        outs[1][...] = tree_sum([rows_of(ref, size, LN_ROWS) for ref in ins])


def join_kernel(stage, spot_ref, *refs):
    out_ref = refs[-1]
    for d, ref in enumerate(refs[:-1]):
        size = ref.shape[0]
        out_ref[pl.ds(pl.multiple_of((spot_ref[2 + stage] ^ d) * size, 16), size), :] = ref[...]


def finish_kernel(peers, twisted, pieces, spot_ref, *refs):
    mine, others, refs = refs[:peers], refs[peers : 2 * peers], refs[2 * peers :]
    outs, (both_ref, *wide, sem) = refs[: len(refs) // 2 - 1], refs[len(refs) // 2 - 1 :]
    core = spot_ref[1]
    for half, arrays, here in ((core, mine, spot_ref[2]), (1 - core, others, spot_ref[3 if twisted else 2])):
        for d, ref in enumerate(arrays):
            size = ref.shape[0]
            both_ref[half, pl.ds(pl.multiple_of((here ^ d) * size, 16), size), :] = ref[...]
    width = both_ref.shape[2]
    copies = []
    for i, (half, first, rows, out, row, col) in enumerate(pieces):
        spot = (pl.ds(row, rows), pl.ds(col, width))
        wide[out][spot] = both_ref[half, first : first + rows, :].astype(F32)
        copies.append(pltpu.make_async_copy(wide[out].at[spot], outs[out].at[spot], sem.at[i]))
        copies[-1].start()
    for copy in copies:
        copy.wait()


class Summing:
    def __init__(self, rows, width, ln):
        self.width, self.ln = width, ln
        self.dp, self.mem = lax.axis_size("dp"), lax.axis_size("mem")
        z_size = 4
        x_size = self.dp // (2 * z_size)
        self.sizes = (x_size, self.mem, z_size)
        self.twisted = x_size == self.mem
        self.chunk = -(-rows // (16 * math.prod(self.sizes))) * 16
        self.rows = self.chunk * math.prod(self.sizes)

    def after(self, stage):
        return self.rows // math.prod(self.sizes[:stage])

    def axis(self, stage, core):
        return 1 - stage if self.twisted and core == 1 and stage < 2 else stage

    def coords(self, dp, mem):
        return [dp // 2 % self.sizes[0], mem, dp // (2 * self.sizes[0])], dp % 2

    def spot(self, me, dp):
        (x, mem, z), core = self.coords(dp, me)
        if self.twisted:
            x, mem = jnp.where(core == 0, x, mem), jnp.where(core == 0, mem, x)
        return jnp.stack([me, core, x, mem, z]).astype(jnp.int32)

    def permute(self, array, stage, offset):
        pairs = []
        for dp in range(self.dp):
            for mem in range(self.mem):
                spots, core = self.coords(dp, mem)
                if stage is None:
                    core ^= offset
                else:
                    spots[self.axis(stage, core)] ^= offset
                to_dp = (spots[2] * self.sizes[0] + spots[0]) * 2 + core
                pairs.append((dp * self.mem + mem, to_dp * self.mem + spots[1]))
        return lax.ppermute(array, ("dp", "mem"), pairs)

    def core_swap(self, send):
        return self.permute(send, None, 1)

    def swap(self, arrays, stage):
        return [arrays[0]] + [self.permute(array, stage, d) for d, array in enumerate(arrays) if d > 0]

    def spread(self, stage, array):
        return [array] + [self.permute(array, stage, d) for d in range(1, self.sizes[stage])]

    def messages(self, stage):
        size = self.after(stage + 1) + (LN_ROWS if self.ln else 0)
        return [((size, self.width), BF16)] * self.sizes[stage]

    def first_split(self, spot, *arrays):
        kernel = functools.partial(first_split_kernel, len(arrays) // 2, self.ln, self.sizes[0])
        return call(kernel, self.messages(0), [((self.rows, self.width), BF16)], 1, spot, *arrays, work=0.01)

    def split(self, stage, spot, arrays):
        kernel = functools.partial(split_kernel, stage, self.ln, self.sizes[stage - 1])
        return call(kernel, self.messages(stage), [], 1, spot, *arrays, work=0.01)

    def total(self, arrays):
        outs = [((self.chunk, self.width), BF16)]
        if self.ln:
            outs.append(((LN_ROWS, self.width), F32))
        return call(functools.partial(total_kernel, self.ln, self.sizes[2]), outs, [], 0, *arrays, work=0.01)

    def join(self, stage, spot, arrays):
        outs = [((self.after(stage), self.width), BF16)]
        return call(functools.partial(join_kernel, stage), outs, [], 1, spot, *arrays, work=0.01)[0]

    def finish(self, spot, mine, others, pieces, outs):
        kernel = functools.partial(finish_kernel, self.sizes[0], self.twisted, pieces)
        scratch = [((2, self.rows, self.width), BF16)] + outs + [pltpu.SemaphoreType.DMA((len(pieces),))]
        return call(kernel, outs, scratch, 1, spot, *mine, *others, work=1, hbm_out=len(outs))


def call(kernel, outs, scratch, scalars, *arrays, work=0.5, vmem=0, hbm_in=0, hbm_out=0, aliases=None):
    plain = len(arrays) - scalars - hbm_in
    if not vmem:
        blocks = [(array.shape, array.dtype) for array in arrays[scalars:]] + outs
        blocks = blocks + [entry for entry in scratch if isinstance(entry, tuple)]
        vmem = max(16, sum(math.prod(shape) * jnp.dtype(kind).itemsize for shape, kind in blocks) // MIB + 7)
    specs = [pl.BlockSpec(memory_space=pltpu.SMEM)] * scalars
    specs = specs + [pl.BlockSpec(memory_space=pltpu.VMEM)] * plain
    specs = specs + [pl.BlockSpec(memory_space=pl.ANY)] * hbm_in
    out_specs = [pl.BlockSpec(memory_space=pltpu.VMEM)] * (len(outs) - hbm_out)
    out_specs = out_specs + [pl.BlockSpec(memory_space=pl.ANY)] * hbm_out
    return pl.pallas_call(
        kernel,
        out_shape=[jax.ShapeDtypeStruct(shape, kind) for shape, kind in outs],
        in_specs=specs,
        out_specs=out_specs,
        scratch_shapes=[pltpu.VMEM(*entry) if isinstance(entry, tuple) else entry for entry in scratch],
        input_output_aliases=aliases or {},
        compiler_params=pltpu.CompilerParams(vmem_limit_bytes=vmem * MIB),
        cost_estimate=pl.CostEstimate(flops=int(work * 1e9), bytes_accessed=int(work * 3e6), transcendentals=0),
    )(*arrays)


def middle(
    groups, first_sum, stats, spot, tgt_len, src_len, hidden_one, query, part, part_top, part_sum, wkv_cross,
    ln_gain, ln_bias, wo_cross, w_up, w_down, grad_out, pair_mine, came,
):
    rows, width = hidden_one.shape
    half, tiles = rows // 2, rows // TILE
    hidden_width = w_down.shape[0]
    count, places, _ = pair_mine.shape
    away = places // groups * (groups - 1)
    arrays = [spot, tgt_len, src_len, hidden_one, query, part, part_top, part_sum, wkv_cross, ln_gain, ln_bias]
    stay = [wo_cross, w_up, w_down, grad_out, pair_mine]

    def kernel(*refs):
        ins, refs = refs[: len(arrays)], refs[len(arrays) :]
        came_refs, refs = refs[: len(came)], refs[len(came) :]
        stay_refs, refs = refs[: len(stay)], refs[len(stay) :]
        outs, refs = refs[:9], refs[9:]
        middle_kernel(groups, *ins, *stay_refs, *came_refs, *outs[:3], *outs[6:8], *outs[3:6], outs[8], *refs)

    result_out, cross_norm, cross_along, grad_hidden_two, grad_attn, ln_part, keep_one, send_one, pair_all = call(
        kernel,
        [
            ((rows, width), BF16),
            (stats, F32),
            (stats, F32),
            ((rows, width), F32),
            ((rows, width), BF16),
            ((4, width), F32),
            ((first_sum.rows, width), BF16),
            ((first_sum.rows, width), BF16),
            ((count, places, 2 * width), BF16),
        ],
        [
            ((width, width), BF16),
            ((width, hidden_width), BF16),
            ((hidden_width, width), BF16),
            ((rows, width), BF16),
            ((count, away, 2 * width), BF16),
            ((first_sum.rows, width), BF16),
            ((first_sum.rows, width), BF16),
            ((count, away, 2 * TILE), F32),
            ((tiles, 2 * TILE, width), BF16),
            ((count, width, away), BF16),
            ((width, rows), F32),
            ((rows, hidden_width), BF16),
            ((rows, hidden_width), F32),
            ((rows, width), F32),
            pltpu.SemaphoreType.DMA((4,)),
            pltpu.SemaphoreType.DMA((count,)),
            pltpu.SemaphoreType.DMA((4,)),
        ],
        3,
        *arrays,
        *came,
        *stay,
        vmem=60,
        hbm_in=len(stay),
        hbm_out=3,
        aliases={len(arrays) + len(came) + len(stay) - 1: 8},
    )
    return result_out, cross_norm, cross_along, keep_one, send_one, grad_hidden_two, grad_attn, ln_part, pair_all


def body(
    target,
    memory,
    grad_out,
    tgt_len,
    src_len,
    w_qkv,
    w_out,
    wq_cross,
    wkv_cross,
    wo_cross,
    w_up,
    w_down,
    ln_gain,
    ln_bias,
):
    rows, width = target.shape
    half = rows // 2
    tiles = rows // TILE
    hidden_width = w_down.shape[0]
    groups = lax.axis_size("mem")
    me = lax.axis_index("mem")
    count = tgt_len.shape[1]
    span = memory.shape[1]
    places, away = groups * span, (groups - 1) * span
    dp = lax.axis_index("dp")
    short = width // 2
    first_sum = Summing(hidden_width + short, width, False)
    second_sum = Summing(3 * width + short, width, True)
    spot = first_sum.spot(me, dp)
    stats = (PAIRS * tiles, 2 * TILE)

    came = []
    for shift in range(1, groups):
        pairs = [(i, (i + shift) % groups) for i in range(groups)]
        sent = lax.dynamic_slice_in_dim(memory, ((me + shift) % groups) * count, count, 0)
        came.append(lax.ppermute(sent, "mem", pairs))

    sorted_rows, qkv, self_norm, self_attn_t, hidden_one, query, part, part_top, part_sum, pair_mine = call(
        functools.partial(self_forward_kernel, groups),
        [
            ((rows, width), BF16),
            ((rows, 3 * width), BF16),
            (stats, F32),
            ((width, rows), BF16),
            ((rows, width), F32),
            ((rows, width), BF16),
            ((width, rows), F32),
            (stats, F32),
            (stats, F32),
            ((count, places, 2 * width), BF16),
        ],
        [
            ((tiles, half, 2 * TILE), F32),
            ((count, span, 2 * TILE), F32),
            ((tiles, 2 * TILE, width), BF16),
            ((width, rows), BF16),
            ((count, width, span), BF16),
            ((count, span, 2 * width), BF16),
            pltpu.SemaphoreType.DMA((count,)),
        ],
        3,
        spot,
        tgt_len,
        src_len,
        target,
        w_qkv,
        w_out,
        wq_cross,
        ln_gain,
        ln_bias,
        memory,
        wkv_cross,
        vmem=60,
        hbm_out=1,
    )
    result_out, cross_norm, cross_along, keep_one, send_one, grad_hidden_two, grad_attn, ln_part, pair_all = middle(
        groups, first_sum, stats, spot, tgt_len, src_len, hidden_one, query, part, part_top, part_sum, wkv_cross,
        ln_gain, ln_bias, wo_cross, w_up, w_down, grad_out, pair_mine, came,
    )
    came_one = first_sum.core_swap(send_one)

    def cross_backward(block):
        sentences = 1 if block == 0 else count - 1
        return call(
            functools.partial(cross_backward_kernel, groups, block),
            [((sentences, places, 2 * width), BF16), ((width, half), BF16)],
            [
                ((sentences, places, 2 * width), BF16),
                ((sentences, places, 2 * TILE), F32),
                ((half // TILE, 2 * TILE, width), BF16),
                ((half // TILE, 2 * TILE, width), BF16),
                ((sentences, width, places), BF16),
                ((SLAB, half), F32),
                ((sentences, places, 2 * SLAB), F32),
                pltpu.SemaphoreType.DMA((1,)),
            ],
            3,
            spot,
            tgt_len,
            src_len,
            query,
            cross_norm,
            cross_along,
            grad_attn,
            pair_all,
            work=10,
            vmem=58 if block == 0 else 32,
            hbm_in=1,
        )

    pair_grad_long, query_grad_t_long = cross_backward(0)
    came_one, pair_grad_long = lax.optimization_barrier((came_one, pair_grad_long))
    parts_one = first_sum.first_split(spot, keep_one, came_one)
    parts_one, pair_all = lax.optimization_barrier((parts_one, pair_all))
    parts_one = first_sum.swap(parts_one, 0)
    pair_grad_rest, query_grad_t_rest = cross_backward(1)
    (wkv_grad,) = call(
        functools.partial(memory_weight_kernel, groups),
        [((2, width, width), BF16)],
        [((width, 2 * width), F32)],
        2,
        spot,
        tgt_len,
        pair_grad_long,
        pair_grad_rest,
        memory,
        *came,
        work=1,
        vmem=32,
    )
    parts_one, wkv_grad = lax.optimization_barrier((parts_one, wkv_grad))
    parts_one = first_sum.split(1, spot, parts_one)
    parts_one, wkv_grad = lax.optimization_barrier((parts_one, wkv_grad))
    parts_one = first_sum.swap(parts_one, 1)
    keep_mid, send_mid, grad_hidden_one, grad_self = call(
        first_norm_backward_kernel,
        [
            ((2 * width + LN_ROWS, width), BF16),
            ((2 * width + LN_ROWS, width), BF16),
            ((rows, width), F32),
            ((rows, width), BF16),
        ],
        [],
        1,
        spot,
        hidden_one,
        query_grad_t_long,
        query_grad_t_rest,
        grad_hidden_two,
        wq_cross,
        w_out,
        self_attn_t,
        ln_gain,
        ln_bias,
        ln_part,
        wkv_grad,
        work=10,
        vmem=24,
    )
    grad_triple, *last = call(
        self_backward_kernel,
        [((rows, 3 * width), BF16)] + [(((width + short) // LAST_PARTS, width), BF16)] * (2 * LAST_PARTS),
        [
            ((tiles, half, 2 * TILE), F32),
            ((tiles, 2 * TILE, width), BF16),
            ((tiles, 2 * TILE, width), BF16),
            ((width, rows), BF16),
            ((width, rows), BF16),
        ],
        2,
        spot,
        tgt_len,
        qkv,
        self_norm,
        grad_self,
        sorted_rows,
        work=0.1,
        vmem=28,
    )
    came_mid = second_sum.core_swap(send_mid)
    parts_one, last, came_mid, pair_grad_long = lax.optimization_barrier(
        (parts_one, last, came_mid, pair_grad_long)
    )
    keep_last = last[:LAST_PARTS]
    came_last = [second_sum.core_swap(part) for part in last[LAST_PARTS:]]
    parts_one = first_sum.split(2, spot, parts_one)
    came_mid, parts_one = lax.optimization_barrier((came_mid, parts_one))
    parts_two = second_sum.first_split(
        spot, keep_mid, came_mid, *[part for both in zip(keep_last, came_last) for part in both]
    )
    parts_one = first_sum.swap(parts_one, 2)
    parts_two, pair_grad_long, grad_triple = lax.optimization_barrier((parts_two, pair_grad_long, grad_triple))
    parts_two = second_sum.swap(parts_two, 0)
    grad_mine, *grad_away = call(
        functools.partial(memory_grad_kernel, groups),
        [((count, span, width), BF16)] + [((count, span // 2, width), BF16)] * (2 * (groups - 1)),
        [],
        2,
        spot,
        tgt_len,
        pair_grad_long,
        pair_grad_rest,
        wkv_cross,
        work=0.01,
        vmem=32,
    )
    (grad_target,) = call(
        target_kernel,
        [((rows, width), BF16)],
        [],
        2,
        spot,
        tgt_len,
        grad_triple,
        w_qkv,
        grad_hidden_one,
        work=0.01,
        vmem=16,
    )
    parts_one, parts_two, grad_away, grad_target = lax.optimization_barrier(
        (parts_one, parts_two, grad_away, grad_target)
    )
    backs = [[], []]
    for i, grads in enumerate(grad_away):
        shift = i // 2 + 1
        backs[i % 2].append(lax.ppermute(grads, "mem", [(k, (k - shift) % groups) for k in range(groups)]))
    parts_two = second_sum.swap(second_sum.split(1, spot, parts_two), 1)
    spread_one = first_sum.spread(2, first_sum.total(parts_one)[0])
    parts_two, spread_one, backs[0] = lax.optimization_barrier((parts_two, spread_one, backs[0]))
    spread_one = first_sum.spread(1, first_sum.join(2, spot, spread_one))
    parts_two = second_sum.swap(second_sum.split(2, spot, parts_two), 2)
    parts_two, spread_one, backs[1] = lax.optimization_barrier((parts_two, spread_one, backs[1]))
    spread_one = first_sum.spread(0, first_sum.join(1, spot, spread_one))
    sum_two, norm_sums = second_sum.total(parts_two)
    spread_two = second_sum.spread(2, sum_two)
    spread_two = second_sum.spread(1, second_sum.join(2, spot, spread_two))
    joined_two = second_sum.join(1, spot, spread_two)
    spread_one, joined_two = lax.optimization_barrier((spread_one, joined_two))
    other_one = [first_sum.core_swap(array) for array in spread_one]
    chunks = hidden_width // width
    pieces = []
    for chunk in range(chunks):
        side, here = chunk // (chunks // 2), chunk % (chunks // 2)
        pieces.append((side, here * width, width, 0, chunk * width, 0))
        pieces.append((side, (chunks // 2 + here) * width, width, 1, 0, chunk * width))
    for side in range(2):
        pieces.append((side, chunks * width, short, 2, side * short, 0))
    grad_w_down, grad_w_up, grad_wo = first_sum.finish(
        spot,
        spread_one,
        other_one,
        pieces,
        [((hidden_width, width), F32), ((width, hidden_width), F32), ((width, width), F32)],
    )
    spread_two = second_sum.spread(0, joined_two)
    spread_two, grad_w_down = lax.optimization_barrier((spread_two, grad_w_down))
    other_two = [second_sum.core_swap(array) for array in spread_two]
    pieces = [
        (0, 0, width, 0, 0, 0),
        (0, width, width, 1, 0, 0),
        (0, 2 * width, width, 2, 0, 0),
        (0, 3 * width, short, 2, 0, width),
        (1, 0, width, 1, 0, width),
        (1, width, width, 3, 0, 0),
        (1, 2 * width, short, 2, short, width),
        (1, 2 * width + short, width, 2, 0, 2 * width),
    ]
    grad_wq, grad_wkv, grad_w_qkv, grad_w_out = second_sum.finish(
        spot,
        spread_two,
        other_two,
        pieces,
        [
            ((width, width), F32),
            ((width, 2 * width), F32),
            ((width, 3 * width), F32),
            ((width, width), F32),
        ],
    )
    grad_memory = jnp.zeros(memory.shape, BF16)
    grad_memory = lax.dynamic_update_slice(grad_memory, grad_mine, (me * count, 0, 0))
    for part in range(2):
        for i, grads in enumerate(backs[part]):
            owner = (me + i + 1) % groups
            grad_memory = lax.dynamic_update_slice(grad_memory, grads, (owner * count, part * (span // 2), 0))
    return (
        result_out,
        grad_target,
        grad_memory,
        grad_w_qkv,
        grad_w_out,
        grad_wq,
        grad_wkv,
        grad_wo,
        grad_w_up,
        grad_w_down,
        norm_sums[:3],
        norm_sums[3:6],
    )


def solution(mesh):
    rows_spec = P(("dp", "mem"), None)
    memory_spec = P("dp", "mem", None)
    return jax.shard_map(
        body,
        mesh=mesh,
        in_specs=(rows_spec, memory_spec, rows_spec, P("dp", None), P("dp", None)) + (P(),) * 9,
        out_specs=(rows_spec, rows_spec, memory_spec) + (P(),) * 9,
        check_vma=False,
    )
```

```python
import functools
import math

import jax
import jax.numpy as jnp
from jax import lax
from jax.experimental import pallas as pl
from jax.experimental.pallas import tpu as pltpu
from jax.sharding import PartitionSpec as P

HEADS = 8
PAIRS = HEADS // 2
SLAB = 128
SIDE = SLAB // 2
TILE = 128
MASKED = -1e30
EPSILON = 1e-05
F32 = jnp.float32
BF16 = jnp.bfloat16
MIB = 1024 * 1024
LN_ROWS = 16
LAST_PARTS = 1


def dot(left, right):
    return jnp.dot(left, right, preferred_element_type=F32)


def dot_nt(left, right):
    return lax.dot_general(left, right, (((1,), (1,)), ((), ())), preferred_element_type=F32)


def dot_tn(left, right):
    return lax.dot_general(left, right, (((0,), (0,)), ((), ())), preferred_element_type=F32)


def iota(shape, axis):
    return lax.broadcasted_iota(jnp.int32, shape, axis)


def norm_parts(hidden):
    centre = hidden - jnp.mean(hidden, axis=-1, keepdims=True)
    inverse = lax.rsqrt(jnp.mean(centre * centre, axis=-1, keepdims=True) + EPSILON)
    return centre * inverse, inverse


def norm_backward(upstream, unit, inverse, gain_row):
    scaled = upstream * gain_row
    shifted = (
        scaled
        - jnp.mean(scaled, axis=-1, keepdims=True)
        - unit * jnp.mean(scaled * unit, axis=-1, keepdims=True)
    )
    gain_grad = jnp.sum(upstream * unit, axis=0, keepdims=True)
    return inverse * shifted, gain_grad, jnp.sum(upstream, axis=0, keepdims=True)


def sentence_order(me, len_ref):
    count = len_ref.shape[1]
    lengths = [len_ref[me, k] for k in range(count)]
    longest, best, start, running = jnp.int32(0), lengths[0], jnp.int32(0), jnp.int32(0)
    for k in range(1, count):
        running = running + lengths[k - 1]
        more = lengths[k] > best
        longest = jnp.where(more, k, longest)
        start = jnp.where(more, running, start)
        best = jnp.where(more, lengths[k], best)
    order = [longest] + [jnp.where(k < longest, k, k + 1) for k in range(count - 1)]
    bounds = [jnp.int32(0)]
    for k in range(1, count):
        bounds.append(bounds[-1] + len_ref[me, order[k]])
    return order, start, bounds


def moved_rows(index, start, half):
    return jnp.where(index < start, index + half, jnp.where(index < start + half, index - start, index))


def sort_matrix(rows, start):
    spot = moved_rows(iota((rows, rows), 1), start, rows // 2)
    return jnp.where(spot == iota((rows, rows), 0), 1.0, 0.0).astype(BF16)


def unsort_matrix(rows, start):
    spot = moved_rows(iota((rows, rows), 0), start, rows // 2)
    return jnp.where(spot == iota((rows, rows), 1), 1.0, 0.0).astype(BF16)


def side_masks(width):
    side = iota((1, width), 1) % SLAB
    first = jnp.where(side < SLAB // 2, 1.0, 0.0)
    return first.astype(BF16), (1.0 - first).astype(BF16)


def slab_of(pair, first=0):
    return pl.ds(first + pair * SLAB, SLAB)


def pack_heads(out_ref, rows, width):
    even, odd = side_masks(width)
    for t in range(out_ref.shape[0]):
        tile = rows(t * TILE, TILE)
        out_ref[t, :TILE, :] = tile * even
        out_ref[t, TILE:, :] = tile * odd


def fill_self_bias(bias_ref, bounds, half):
    for t in range(bias_ref.shape[0]):
        block, inner = t // (half // TILE), t % (half // TILE)
        key = iota((half, 2 * TILE), 0)
        query = iota((half, 2 * TILE), 1) % TILE + inner * TILE
        allowed = key <= query
        if block == 1:
            first = jnp.zeros((half, 2 * TILE), jnp.int32)
            for bound in bounds[1:-1]:
                first = jnp.where(query >= bound, bound, first)
            allowed = allowed & (key >= first)
        bias_ref[t] = jnp.where(allowed, 0.0, MASKED)


def self_keys(t, half):
    per = half // TILE
    return (t // per) * half, (t % per + 1) * TILE


def fill_live_bias(bias_ref, me, groups, parts, span, src_ref, sentences):
    key = iota((span, bias_ref.shape[2]), 0)
    for j, sentence in enumerate(sentences):
        for i, part in enumerate(parts):
            place = lax.rem(me - part + groups, groups) * span + key
            live = place < src_ref[me, sentence]
            bias_ref[j, pl.ds(i * span, span), :] = jnp.where(live, 0.0, MASKED)


def cross_units(bounds, half):
    units = [(t, 0, None) for t in range(half // TILE)]
    middle = half // 2
    last = jnp.int32(1)
    for bound in bounds[1:-1]:
        last = last + jnp.where(bound < middle, 1, 0)
    ends = bounds[1:]
    column = iota((1, 2 * TILE), 1) % TILE
    for u in range(len(ends) + 1):
        early = u < last
        sentence = jnp.where(early, u + 1, u)
        tile = jnp.where(early, 0, 1)
        low, high = jnp.int32(0), ends[0]
        for k in range(1, len(ends)):
            low = jnp.where(sentence == k + 1, ends[k - 1], low)
            high = jnp.where(sentence == k + 1, ends[k], high)
        row = column + tile * TILE
        units.append((tile + half // TILE, sentence, (row >= low) & (row < high)))
    return units


def own_sides(both):
    return jnp.concatenate([both[:SIDE, :TILE], both[SIDE:, TILE:]], axis=0)


def side_rows(row):
    even = jnp.broadcast_to(row[:, :TILE], (SIDE, TILE))
    return jnp.concatenate([even, jnp.broadcast_to(row[:, TILE:], (SIDE, TILE))], axis=0)


def tile_columns(tile):
    if isinstance(tile, int):
        return pl.ds(tile * TILE, TILE)
    return pl.ds(pl.multiple_of(tile * TILE, TILE), TILE)


def self_forward_kernel(
    groups,
    me_ref,
    len_ref,
    src_ref,
    target_ref,
    w_qkv_ref,
    w_out_ref,
    wq_ref,
    gain_ref,
    bias_row_ref,
    memory_ref,
    wkv_ref,
    sorted_ref,
    qkv_ref,
    norm_ref,
    attn_t_ref,
    hidden_ref,
    query_ref,
    part_ref,
    top_ref,
    sum_ref,
    pair_out_ref,
    bias_ref,
    live_ref,
    q_pack_ref,
    value_t_ref,
    cross_value_t_ref,
    pair_ref,
    copy_sem,
):
    rows, width = target_ref.shape
    half = rows // 2
    me = me_ref[0]
    order, start, bounds = sentence_order(me, len_ref)
    count, span = pair_ref.shape[0], pair_ref.shape[1]
    copies = []
    for j in range(count):
        block = memory_ref[me * count + order[j]]
        pair_ref[j] = dot(block, wkv_ref[...]).astype(BF16)
        copy = pltpu.make_async_copy(
            pair_ref.at[j], pair_out_ref.at[j, pl.ds(0, span), :], copy_sem.at[j]
        )
        copy.start()
        copies.append(copy)
    sorted_rows = dot(sort_matrix(rows, start), target_ref[...]).astype(BF16)
    sorted_ref[...] = sorted_rows
    fill_self_bias(bias_ref, bounds, half)
    queries = (dot(sorted_rows, w_qkv_ref[:, :width]).astype(BF16) * 0.125).astype(BF16)
    qkv_ref[:, :width] = queries
    pack_heads(q_pack_ref, lambda first, size: queries[first : first + size], width)
    qkv_ref[:, width : 2 * width] = dot(sorted_rows, w_qkv_ref[:, width : 2 * width]).astype(BF16)
    values = dot(sorted_rows, w_qkv_ref[:, 2 * width :]).astype(BF16)
    qkv_ref[:, 2 * width :] = values
    value_t_ref[...] = values.T
    tiles = rows // TILE

    def self_step(pair):
        slab = slab_of(pair)
        for t in range(tiles):
            first, size = self_keys(t, half)
            keys = qkv_ref[pl.ds(first, size), slab_of(pair, width)]
            scores = dot_nt(keys, q_pack_ref[t, :, slab]) + bias_ref[t, :size, :]
            top = jnp.max(scores, axis=0, keepdims=True)
            weights = jnp.exp(scores - top)
            total = jnp.sum(weights, axis=0, keepdims=True)
            probs = (weights * (1.0 / total)).astype(BF16)
            both = dot(value_t_ref[slab, pl.ds(first, size)], probs)
            attn_t_ref[slab, tile_columns(t)] = own_sides(both).astype(BF16)
            norm_ref[pl.ds(pair * tiles + t, 1), :] = top + jnp.log(total)

    for pair in range(PAIRS):
        self_step(pair)
    hidden = sorted_rows.astype(F32) + dot(attn_t_ref[...].T, w_out_ref[...])
    hidden_ref[...] = hidden
    unit, _ = norm_parts(hidden)
    normed = (unit * gain_ref[0:1] + bias_row_ref[0:1]).astype(BF16)
    query_ref[...] = (dot(normed, wq_ref[...]).astype(BF16) * 0.125).astype(BF16)

    pack_heads(q_pack_ref, lambda first, size: query_ref[first : first + size, :], width)
    fill_live_bias(live_ref, me, groups, [0], span, src_ref, order)
    for j in range(count):
        cross_value_t_ref[j] = pair_ref[j, :, width:].T
    units = cross_units(bounds, half)

    def cross_step(pair):
        slab = slab_of(pair)
        for tile, sentence, columns in units:
            scores = dot_nt(pair_ref[sentence, :, slab], q_pack_ref[tile, :, slab]) + live_ref[sentence]
            top = jnp.max(scores, axis=0, keepdims=True)
            weights = jnp.exp(scores - top)
            total = jnp.sum(weights, axis=0, keepdims=True)
            result = own_sides(dot(cross_value_t_ref[sentence, slab, :], weights.astype(BF16)))
            here = tile_columns(tile)
            row = pl.ds(pair * tiles + tile, 1)
            if columns is not None:
                result = jnp.where(columns[:, :TILE], result, part_ref[slab, here])
                top = jnp.where(columns, top, top_ref[row, :])
                total = jnp.where(columns, total, sum_ref[row, :])
            part_ref[slab, here] = result
            top_ref[row, :] = top
            sum_ref[row, :] = total

    part_ref[...] = jnp.zeros_like(part_ref)
    top_ref[...] = jnp.zeros_like(top_ref)
    sum_ref[...] = jnp.ones_like(sum_ref)
    for pair in range(PAIRS):
        cross_step(pair)
    for copy in copies:
        copy.wait()


def middle_kernel(
    groups,
    me_ref,
    len_ref,
    src_ref,
    hidden_one_ref,
    query_ref,
    part_ref,
    top_ref,
    sum_ref,
    wkv_ref,
    gain_ref,
    bias_row_ref,
    wo_hbm,
    w_up_hbm,
    w_down_hbm,
    grad_out_hbm,
    pair_in_hbm,
    *refs,
):
    came_refs = refs[: groups - 1]
    (
        out_ref,
        norm_ref,
        along_ref,
        keep_hbm,
        send_hbm,
        grad_hidden_ref,
        grad_attn_ref,
        ln_ref,
        pair_hbm,
        wo_ref,
        w_up_ref,
        w_down_ref,
        grad_out_ref,
        pair_ref,
        halves_ref,
        live_ref,
        q_pack_ref,
        value_t_ref,
        attn_t_ref,
        active_ref,
        slope_ref,
        total_ref,
        load_sem,
        pair_sem,
        store_sem,
    ) = refs[groups - 1 :]
    rows, width = hidden_one_ref.shape
    half = rows // 2
    me = me_ref[0]
    count, away = pair_ref.shape[0], pair_ref.shape[1]
    span = away // (groups - 1)
    loads = [
        pltpu.make_async_copy(source, there, load_sem.at[i])
        for i, (source, there) in enumerate(
            [(wo_hbm, wo_ref), (w_up_hbm, w_up_ref), (w_down_hbm, w_down_ref), (grad_out_hbm, grad_out_ref)]
        )
    ]
    for copy in loads:
        copy.start()
    order, start, bounds = sentence_order(me, len_ref)
    fill_live_bias(live_ref, me, groups, list(range(1, groups)), span, src_ref, order)
    pack_heads(q_pack_ref, lambda first, size: query_ref[first : first + size, :], width)
    pair_copies = []
    for j in range(count):
        for part in range(1, groups):
            block = came_refs[part - 1][order[j]]
            pair_ref[j, pl.ds((part - 1) * span, span), :] = dot(block, wkv_ref[...]).astype(BF16)
        value_t_ref[j] = pair_ref[j, :, width:].T
        copy = pltpu.make_async_copy(pair_ref.at[j], pair_hbm.at[j, pl.ds(span, away), :], pair_sem.at[j])
        copy.start()
        pair_copies.append(copy)
    units = cross_units(bounds, half)
    tiles = rows // TILE

    def cross_step(pair):
        slab = slab_of(pair)
        for tile, sentence, columns in units:
            here = tile_columns(tile)
            row = pl.ds(pair * tiles + tile, 1)
            scores = dot_nt(pair_ref[sentence, :, slab], q_pack_ref[tile, :, slab]) + live_ref[sentence]
            before = top_ref[row, :]
            top = jnp.maximum(jnp.max(scores, axis=0, keepdims=True), before)
            weights = jnp.exp(scores - top)
            scale = jnp.exp(before - top)
            total = jnp.sum(weights, axis=0, keepdims=True) + sum_ref[row, :] * scale
            result = own_sides(dot(value_t_ref[sentence, slab, :], weights.astype(BF16)))
            result = (result + part_ref[slab, here] * side_rows(scale)) * side_rows(1.0 / total)
            norm = top + jnp.log(total)
            if columns is not None:
                result = jnp.where(columns[:, :TILE], result, attn_t_ref[slab, here])
                norm = jnp.where(columns, norm, norm_ref[row, :])
            attn_t_ref[slab, here] = result
            norm_ref[row, :] = norm

    attn_t_ref[...] = jnp.zeros_like(attn_t_ref)
    norm_ref[...] = jnp.zeros_like(norm_ref)
    for pair in range(PAIRS):
        cross_step(pair)
    attn_t_low = attn_t_ref[...].astype(BF16)
    loads[0].wait()
    unit_one, _ = norm_parts(hidden_one_ref[...])
    normed_one = unit_one * gain_ref[0:1] + bias_row_ref[0:1]
    hidden_two = normed_one + dot(attn_t_low.T, wo_ref[...])
    unit_two, inverse_two = norm_parts(hidden_two)
    normed_two = unit_two * gain_ref[1:2] + bias_row_ref[1:2]
    normed_two_low = normed_two.astype(BF16)
    total_ref[...] = normed_two
    chunk = width
    chunks = w_down_ref.shape[0] // chunk
    loads[1].wait()
    loads[2].wait()

    for c in range(chunks):
        cols = pl.ds(c * chunk, chunk)
        upper = dot(normed_two_low, w_up_ref[:, cols])
        sigma = 0.5 * jnp.tanh(0.5 * upper) + 0.5
        active = (upper * sigma).astype(BF16)
        active_ref[:, cols] = active
        slope_ref[:, cols] = sigma * (1.0 + upper * (1.0 - sigma))
        total_ref[...] += dot(active, w_down_ref[cols, :])

    unit_three, inverse_three = norm_parts(total_ref[...])
    result = (unit_three * gain_ref[2:3] + bias_row_ref[2:3]).astype(BF16)
    out_ref[...] = dot(unsort_matrix(rows, start), result).astype(BF16)
    loads[3].wait()
    upstream = dot(sort_matrix(rows, start), grad_out_ref[...])
    grad_three, gain_three, bias_three = norm_backward(upstream, unit_three, inverse_three, gain_ref[2:3])
    grad_down = grad_three.astype(BF16)
    total_ref[...] = grad_three
    normed_two_t = normed_two_low.T

    for c in range(chunks):
        cols = pl.ds(c * chunk, chunk)
        grad_upper = (dot_nt(grad_down, w_down_ref[cols, :]) * slope_ref[:, cols]).astype(BF16)
        down_part = dot_tn(active_ref[:, cols], grad_down).astype(BF16)
        up_part = dot(normed_two_t, grad_upper).astype(BF16)
        half_index, here = c // (chunks // 2), c % (chunks // 2)
        halves_ref[half_index, pl.ds(here * chunk, chunk), :] = down_part
        halves_ref[half_index, pl.ds((chunks // 2 + here) * chunk, chunk), :] = up_part
        total_ref[...] += dot_nt(grad_upper, w_up_ref[:, cols])

    most = chunks * chunk
    core = me_ref[1]
    stores = [
        pltpu.make_async_copy(
            halves_ref.at[half_index, pl.ds(first, size)], there.at[pl.ds(first, size)], store_sem.at[i]
        )
        for i, (half_index, there, first, size) in enumerate(
            [
                (1 - core, send_hbm, 0, most),
                (core, keep_hbm, 0, most),
                (1 - core, send_hbm, most, halves_ref.shape[1] - most),
                (core, keep_hbm, most, halves_ref.shape[1] - most),
            ]
        )
    ]
    stores[0].start()
    stores[1].start()
    grad_two, gain_two, bias_two = norm_backward(total_ref[...], unit_two, inverse_two, gain_ref[1:2])
    grad_two_low = grad_two.astype(BF16)
    wo_grad = dot(attn_t_low, grad_two_low).astype(BF16)
    used = most + width // 2
    for half_index in range(2):
        piece = wo_grad[half_index * (width // 2) : (half_index + 1) * (width // 2)]
        halves_ref[half_index, pl.ds(most, width // 2), :] = piece
        if halves_ref.shape[1] > used:
            halves_ref[half_index, used:, :] = jnp.zeros((halves_ref.shape[1] - used, width), BF16)
    stores[2].start()
    stores[3].start()
    grad_hidden_ref[...] = grad_two
    grad_attn = dot_nt(grad_two_low, wo_ref[...]).astype(BF16)
    grad_attn_ref[...] = grad_attn
    product = grad_attn.T.astype(F32) * attn_t_ref[...]
    for pair in range(PAIRS):
        for side in range(2):
            first = pair * SLAB + side * SIDE
            along = jnp.sum(product[first : first + SIDE], axis=0, keepdims=True)
            for t in range(tiles):
                along_ref[pair * tiles + t : pair * tiles + t + 1, side * TILE : (side + 1) * TILE] = along[
                    :, t * TILE : (t + 1) * TILE
                ]
    ln_ref[...] = jnp.concatenate([gain_two, gain_three, bias_two, bias_three], axis=0)
    for copy in pair_copies + stores:
        copy.wait()


def cross_backward_kernel(
    groups,
    block,
    me_ref,
    len_ref,
    src_ref,
    query_ref,
    norm_ref,
    along_ref,
    grad_attn_ref,
    pair_hbm,
    pair_grad_ref,
    query_grad_t_ref,
    pair_ref,
    live_ref,
    q_pack_ref,
    g_pack_ref,
    key_t_ref,
    query_sum_ref,
    sum_ref,
    load_sem,
):
    rows, width = query_ref.shape
    half = rows // 2
    me = me_ref[0]
    sentences, places = pair_ref.shape[0], pair_ref.shape[1]
    first_sentence = 0 if block == 0 else 1
    load = pltpu.make_async_copy(pair_hbm.at[pl.ds(first_sentence, sentences)], pair_ref, load_sem.at[0])
    load.start()
    order, start, bounds = sentence_order(me, len_ref)
    mine = order[:1] if block == 0 else order[1:]
    fill_live_bias(live_ref, me, groups, list(range(groups)), places // groups, src_ref, mine)
    low = block * half
    pack_heads(q_pack_ref, lambda first, size: query_ref[low + first : low + first + size, :], width)
    pack_heads(g_pack_ref, lambda first, size: grad_attn_ref[low + first : low + first + size, :], width)
    tiles, per = rows // TILE, half // TILE
    units = cross_units(bounds, half)
    units = units[:per] if block == 0 else units[per:]
    load.wait()
    for j in range(sentences):
        key_t_ref[j] = pair_ref[j, :, :width].T

    def pair_step(pair):
        slab, value_slab = slab_of(pair), slab_of(pair, width)
        query_sum_ref[...] = jnp.zeros_like(query_sum_ref)
        sum_ref[...] = jnp.zeros_like(sum_ref)
        for tile, sentence, columns in units:
            j = sentence - first_sentence
            t = tile - block * per
            here = tile_columns(t)
            row = pl.ds(pair * tiles + tile, 1)
            q_rows, g_rows = q_pack_ref[t, :, slab], g_pack_ref[t, :, slab]
            norm = norm_ref[row, :]
            if columns is not None:
                norm = jnp.where(columns, norm, -MASKED)
            scores = dot_nt(pair_ref[j, :, slab], q_rows) + live_ref[j]
            probs = jnp.exp(scores - norm)
            grad_probs = dot_nt(pair_ref[j, :, value_slab], g_rows)
            grad_scores = (probs * (grad_probs - along_ref[row, :])).astype(BF16)
            sum_ref[j, :, :SLAB] += dot(grad_scores, q_rows)
            sum_ref[j, :, SLAB:] += dot(probs.astype(BF16), g_rows)
            query_sum_ref[:, here] += own_sides(dot(key_t_ref[j, slab, :], grad_scores))
        query_grad_t_ref[slab, :] = (query_sum_ref[...] * 0.125).astype(BF16)
        pair_grad_ref[:, :, slab] = sum_ref[:, :, :SLAB].astype(BF16)
        pair_grad_ref[:, :, value_slab] = sum_ref[:, :, SLAB:].astype(BF16)

    for pair in range(PAIRS):
        pair_step(pair)


def memory_weight_kernel(groups, me_ref, len_ref, pair_grad_long_ref, pair_grad_rest_ref, memory_ref, *refs):
    came_refs = refs[: groups - 1]
    wkv_grad_ref, total_ref = refs[groups - 1 :]
    width = memory_ref.shape[2]
    me = me_ref[0]
    count = len_ref.shape[1]
    span = pair_grad_long_ref.shape[1] // groups
    order, _, _ = sentence_order(me, len_ref)
    for j in range(count):
        pair_grad_ref, here = (pair_grad_long_ref, 0) if j == 0 else (pair_grad_rest_ref, j - 1)
        blocks = [memory_ref[me * count + order[j]]] + [ref[order[j]] for ref in came_refs]
        term = dot_tn(jnp.concatenate(blocks, axis=0), pair_grad_ref[here])
        if j == 0:
            total_ref[...] = term
        else:
            total_ref[...] += term
    wkv_grad_ref[0] = total_ref[:, :width].astype(BF16)
    wkv_grad_ref[1] = total_ref[:, width:].astype(BF16)


def memory_grad_kernel(
    groups, me_ref, len_ref, pair_grad_long_ref, pair_grad_rest_ref, wkv_ref, mine_ref, *away_refs
):
    count = len_ref.shape[1]
    span = pair_grad_long_ref.shape[1] // groups
    order, _, _ = sentence_order(me_ref[0], len_ref)
    for j in range(count):
        pair_grad_ref, here = (pair_grad_long_ref, 0) if j == 0 else (pair_grad_rest_ref, j - 1)
        grads = dot_nt(pair_grad_ref[here], wkv_ref[...]).astype(BF16)
        mine_ref[order[j]] = grads[:span]
        for i, ref in enumerate(away_refs):
            first = span + i * (span // 2)
            ref[order[j]] = grads[first : first + span // 2]


def first_norm_backward_kernel(
    me_ref,
    hidden_one_ref,
    query_grad_t_long_ref,
    query_grad_t_rest_ref,
    grad_hidden_two_ref,
    wq_ref,
    w_out_ref,
    self_attn_t_ref,
    gain_ref,
    bias_row_ref,
    ln_in_ref,
    wkv_grad_ref,
    keep_ref,
    send_ref,
    grad_hidden_ref,
    grad_self_ref,
):
    width = wq_ref.shape[0]
    unit_one, inverse_one = norm_parts(hidden_one_ref[...])
    normed_one = (unit_one * gain_ref[0:1] + bias_row_ref[0:1]).astype(BF16)
    query_grad = jnp.concatenate([query_grad_t_long_ref[...].T, query_grad_t_rest_ref[...].T], axis=0)
    upstream = grad_hidden_two_ref[...] + dot_nt(query_grad, wq_ref[...])
    grad_one, gain_one, bias_one = norm_backward(upstream, unit_one, inverse_one, gain_ref[0:1])
    grad_hidden_ref[...] = grad_one
    grad_one_low = grad_one.astype(BF16)
    grad_self_ref[...] = dot_nt(grad_one_low, w_out_ref[...]).astype(BF16)
    wq_grad = dot_tn(normed_one, query_grad).astype(BF16)
    w_out_grad = dot(self_attn_t_ref[...], grad_one_low).astype(BF16)
    norms = jnp.concatenate(
        [gain_one, ln_in_ref[0:2], bias_one, ln_in_ref[2:4], jnp.zeros((LN_ROWS - 6, width), F32)], axis=0
    ).astype(BF16)

    def halves(low_ref, high_ref):
        low_ref[:width, :] = wq_grad
        low_ref[width : 2 * width, :] = wkv_grad_ref[0]
        high_ref[:width, :] = wkv_grad_ref[1]
        high_ref[width : 2 * width, :] = w_out_grad

    @pl.when(me_ref[1] == 0)
    def _():
        halves(keep_ref, send_ref)

    @pl.when(me_ref[1] != 0)
    def _():
        halves(send_ref, keep_ref)

    keep_ref[2 * width :, :] = norms
    send_ref[2 * width :, :] = norms


def self_backward_kernel(
    me_ref,
    len_ref,
    qkv_ref,
    norm_ref,
    grad_attn_ref,
    sorted_ref,
    grad_triple_ref,
    *refs,
):
    keep_refs, send_refs = refs[:LAST_PARTS], refs[LAST_PARTS : 2 * LAST_PARTS]
    self_backward(
        me_ref,
        len_ref,
        qkv_ref,
        norm_ref,
        grad_attn_ref,
        sorted_ref,
        grad_triple_ref,
        keep_refs,
        send_refs,
        *refs[2 * LAST_PARTS :],
    )


def self_backward(
    me_ref,
    len_ref,
    qkv_ref,
    norm_ref,
    grad_attn_ref,
    sorted_ref,
    grad_triple_ref,
    keep_refs,
    send_refs,
    bias_ref,
    q_pack_ref,
    g_pack_ref,
    key_t_ref,
    query_grad_t_ref,
):
    rows, width = sorted_ref.shape
    half = rows // 2
    _, _, bounds = sentence_order(me_ref[0], len_ref)
    fill_self_bias(bias_ref, bounds, half)
    pack_heads(q_pack_ref, lambda first, size: qkv_ref[first : first + size, :width], width)
    pack_heads(g_pack_ref, lambda first, size: grad_attn_ref[first : first + size, :], width)
    key_t_ref[...] = qkv_ref[:, width : 2 * width].T
    tiles, per = rows // TILE, half // TILE

    def pair_step(pair):
        slab, key_slab, value_slab = slab_of(pair), slab_of(pair, width), slab_of(pair, 2 * width)
        sums = [[None, None] for _ in range(tiles)]
        for t in range(tiles):
            first, size = self_keys(t, half)
            span = pl.ds(first, size)
            q_rows, g_rows = q_pack_ref[t, :, slab], g_pack_ref[t, :, slab]
            scores = dot_nt(qkv_ref[span, key_slab], q_rows) + bias_ref[t, :size, :]
            probs = jnp.exp(scores - norm_ref[pl.ds(pair * tiles + t, 1), :])
            grad_probs = dot_nt(qkv_ref[span, value_slab], g_rows)
            along = jnp.sum(probs * grad_probs, axis=0, keepdims=True)
            grad_scores = (probs * (grad_probs - along)).astype(BF16)
            parts = dot(grad_scores, q_rows), dot(probs.astype(BF16), g_rows)
            for i in range(size // TILE):
                spot = sums[first // TILE + i]
                for k in range(2):
                    piece = parts[k][i * TILE : (i + 1) * TILE]
                    spot[k] = piece if spot[k] is None else spot[k] + piece
            query_grad_t_ref[slab, tile_columns(t)] = (
                own_sides(dot(key_t_ref[slab, span], grad_scores)) * 0.125
            ).astype(BF16)
        for t in range(tiles):
            grad_triple_ref[pl.ds(t * TILE, TILE), key_slab] = sums[t][0].astype(BF16)
            grad_triple_ref[pl.ds(t * TILE, TILE), value_slab] = sums[t][1].astype(BF16)

    for pair in range(PAIRS):
        pair_step(pair)
    grad_triple_ref[:, :width] = query_grad_t_ref[...].T
    sorted_t = sorted_ref[...].T
    grads = [
        dot(sorted_t, grad_triple_ref[:, part * width : (part + 1) * width]).astype(BF16)
        for part in range(3)
    ]
    short = width // 2

    low = jnp.concatenate([grads[0], grads[1][:short]], axis=0)
    high = jnp.concatenate([grads[1][short:], grads[2]], axis=0)
    size = keep_refs[0].shape[0]

    def halves(low_refs, high_refs):
        for i in range(LAST_PARTS):
            low_refs[i][...] = low[i * size : (i + 1) * size]
            high_refs[i][...] = high[i * size : (i + 1) * size]

    @pl.when(me_ref[1] == 0)
    def _():
        halves(keep_refs, send_refs)

    @pl.when(me_ref[1] != 0)
    def _():
        halves(send_refs, keep_refs)


def target_kernel(me_ref, len_ref, grad_triple_ref, w_qkv_ref, grad_hidden_ref, grad_target_ref):
    rows = grad_hidden_ref.shape[0]
    _, start, _ = sentence_order(me_ref[0], len_ref)
    result = grad_hidden_ref[...] + dot_nt(grad_triple_ref[...], w_qkv_ref[...])
    grad_target_ref[...] = dot(unsort_matrix(rows, start), result.astype(BF16)).astype(BF16)


def tree_sum(terms):
    while len(terms) > 1:
        terms = [terms[i] + terms[i + 1] for i in range(0, len(terms), 2)]
    return terms[0]


def rows_of(ref, first, count):
    return ref[pl.ds(pl.multiple_of(first, 16), count), :].astype(F32)


def first_split_kernel(segments, ln, peers, spot_ref, *refs):
    ins, outs, sum_ref = refs[: 2 * segments], refs[2 * segments : -1], refs[-1]
    extra = LN_ROWS if ln else 0
    size = outs[0].shape[0] - extra
    used = 0
    for i in range(segments):
        keep_ref, came_ref = ins[2 * i], ins[2 * i + 1]
        count = keep_ref.shape[0] - (extra if i == 0 else 0)
        sum_ref[used : used + count, :] = (rows_of(keep_ref, 0, count) + rows_of(came_ref, 0, count)).astype(BF16)
        if i == 0 and ln:
            tail = (rows_of(keep_ref, count, LN_ROWS) + rows_of(came_ref, count, LN_ROWS)).astype(BF16)
        used += count
    if sum_ref.shape[0] > used:
        sum_ref[used:, :] = jnp.zeros((sum_ref.shape[0] - used, sum_ref.shape[1]), BF16)
    for d, out in enumerate(outs):
        out[:size, :] = sum_ref[pl.ds(pl.multiple_of((spot_ref[2] ^ d) * size, 16), size), :]
        if ln:
            out[size:, :] = tail


def split_kernel(stage, ln, peers, spot_ref, *refs):
    ins, outs = refs[:peers], refs[peers:]
    extra = LN_ROWS if ln else 0
    size = outs[0].shape[0] - extra
    if ln:
        tail = tree_sum([rows_of(ref, size * len(outs), LN_ROWS) for ref in ins]).astype(BF16)
    for d, out in enumerate(outs):
        first = (spot_ref[2 + stage] ^ d) * size
        out[:size, :] = tree_sum([rows_of(ref, first, size) for ref in ins]).astype(BF16)
        if ln:
            out[size:, :] = tail


def total_kernel(ln, count, *refs):
    ins, outs = refs[:count], refs[count:]
    size = outs[0].shape[0]
    outs[0][...] = tree_sum([rows_of(ref, 0, size) for ref in ins]).astype(BF16)
    if ln:
        outs[1][...] = tree_sum([rows_of(ref, size, LN_ROWS) for ref in ins])


def join_kernel(stage, spot_ref, *refs):
    out_ref = refs[-1]
    for d, ref in enumerate(refs[:-1]):
        size = ref.shape[0]
        out_ref[pl.ds(pl.multiple_of((spot_ref[2 + stage] ^ d) * size, 16), size), :] = ref[...]


def finish_kernel(peers, twisted, pieces, spot_ref, *refs):
    mine, others, refs = refs[:peers], refs[peers : 2 * peers], refs[2 * peers :]
    outs, (both_ref, *wide, sem) = refs[: len(refs) // 2 - 1], refs[len(refs) // 2 - 1 :]
    core = spot_ref[1]
    for half, arrays, here in ((core, mine, spot_ref[2]), (1 - core, others, spot_ref[3 if twisted else 2])):
        for d, ref in enumerate(arrays):
            size = ref.shape[0]
            both_ref[half, pl.ds(pl.multiple_of((here ^ d) * size, 16), size), :] = ref[...]
    width = both_ref.shape[2]
    copies = []
    for i, (half, first, rows, out, row, col) in enumerate(pieces):
        spot = (pl.ds(row, rows), pl.ds(col, width))
        wide[out][spot] = both_ref[half, first : first + rows, :].astype(F32)
        copies.append(pltpu.make_async_copy(wide[out].at[spot], outs[out].at[spot], sem.at[i]))
        copies[-1].start()
    for copy in copies:
        copy.wait()


class Summing:
    def __init__(self, rows, width, ln):
        self.width, self.ln = width, ln
        self.dp, self.mem = lax.axis_size("dp"), lax.axis_size("mem")
        z_size = 4
        x_size = self.dp // (2 * z_size)
        self.sizes = (x_size, self.mem, z_size)
        self.twisted = x_size == self.mem
        self.chunk = -(-rows // (16 * math.prod(self.sizes))) * 16
        self.rows = self.chunk * math.prod(self.sizes)

    def after(self, stage):
        return self.rows // math.prod(self.sizes[:stage])

    def axis(self, stage, core):
        return 1 - stage if self.twisted and core == 1 and stage < 2 else stage

    def coords(self, dp, mem):
        return [dp // 2 % self.sizes[0], mem, dp // (2 * self.sizes[0])], dp % 2

    def spot(self, me, dp):
        (x, mem, z), core = self.coords(dp, me)
        if self.twisted:
            x, mem = jnp.where(core == 0, x, mem), jnp.where(core == 0, mem, x)
        return jnp.stack([me, core, x, mem, z]).astype(jnp.int32)

    def permute(self, array, stage, offset):
        pairs = []
        for dp in range(self.dp):
            for mem in range(self.mem):
                spots, core = self.coords(dp, mem)
                if stage is None:
                    core ^= offset
                else:
                    spots[self.axis(stage, core)] ^= offset
                to_dp = (spots[2] * self.sizes[0] + spots[0]) * 2 + core
                pairs.append((dp * self.mem + mem, to_dp * self.mem + spots[1]))
        return lax.ppermute(array, ("dp", "mem"), pairs)

    def core_swap(self, send):
        return self.permute(send, None, 1)

    def swap(self, arrays, stage):
        return [arrays[0]] + [self.permute(array, stage, d) for d, array in enumerate(arrays) if d > 0]

    def spread(self, stage, array):
        return [array] + [self.permute(array, stage, d) for d in range(1, self.sizes[stage])]

    def messages(self, stage):
        size = self.after(stage + 1) + (LN_ROWS if self.ln else 0)
        return [((size, self.width), BF16)] * self.sizes[stage]

    def first_split(self, spot, *arrays):
        kernel = functools.partial(first_split_kernel, len(arrays) // 2, self.ln, self.sizes[0])
        return call(kernel, self.messages(0), [((self.rows, self.width), BF16)], 1, spot, *arrays, work=0.01)

    def split(self, stage, spot, arrays):
        kernel = functools.partial(split_kernel, stage, self.ln, self.sizes[stage - 1])
        return call(kernel, self.messages(stage), [], 1, spot, *arrays, work=0.01)

    def total(self, arrays):
        outs = [((self.chunk, self.width), BF16)]
        if self.ln:
            outs.append(((LN_ROWS, self.width), F32))
        return call(functools.partial(total_kernel, self.ln, self.sizes[2]), outs, [], 0, *arrays, work=0.01)

    def join(self, stage, spot, arrays):
        outs = [((self.after(stage), self.width), BF16)]
        return call(functools.partial(join_kernel, stage), outs, [], 1, spot, *arrays, work=0.01)[0]

    def finish(self, spot, mine, others, pieces, outs):
        kernel = functools.partial(finish_kernel, self.sizes[0], self.twisted, pieces)
        scratch = [((2, self.rows, self.width), BF16)] + outs + [pltpu.SemaphoreType.DMA((len(pieces),))]
        return call(kernel, outs, scratch, 1, spot, *mine, *others, work=1, hbm_out=len(outs))


def call(kernel, outs, scratch, scalars, *arrays, work=0.5, vmem=0, hbm_in=0, hbm_out=0, aliases=None):
    plain = len(arrays) - scalars - hbm_in
    if not vmem:
        blocks = [(array.shape, array.dtype) for array in arrays[scalars:]] + outs
        blocks = blocks + [entry for entry in scratch if isinstance(entry, tuple)]
        vmem = max(16, sum(math.prod(shape) * jnp.dtype(kind).itemsize for shape, kind in blocks) // MIB + 7)
    specs = [pl.BlockSpec(memory_space=pltpu.SMEM)] * scalars
    specs = specs + [pl.BlockSpec(memory_space=pltpu.VMEM)] * plain
    specs = specs + [pl.BlockSpec(memory_space=pl.ANY)] * hbm_in
    out_specs = [pl.BlockSpec(memory_space=pltpu.VMEM)] * (len(outs) - hbm_out)
    out_specs = out_specs + [pl.BlockSpec(memory_space=pl.ANY)] * hbm_out
    return pl.pallas_call(
        kernel,
        out_shape=[jax.ShapeDtypeStruct(shape, kind) for shape, kind in outs],
        in_specs=specs,
        out_specs=out_specs,
        scratch_shapes=[pltpu.VMEM(*entry) if isinstance(entry, tuple) else entry for entry in scratch],
        input_output_aliases=aliases or {},
        compiler_params=pltpu.CompilerParams(vmem_limit_bytes=vmem * MIB),
        cost_estimate=pl.CostEstimate(flops=int(work * 1e9), bytes_accessed=int(work * 3e6), transcendentals=0),
    )(*arrays)


def middle(
    groups, first_sum, stats, spot, tgt_len, src_len, hidden_one, query, part, part_top, part_sum, wkv_cross,
    ln_gain, ln_bias, wo_cross, w_up, w_down, grad_out, pair_mine, came,
):
    rows, width = hidden_one.shape
    half, tiles = rows // 2, rows // TILE
    hidden_width = w_down.shape[0]
    count, places, _ = pair_mine.shape
    away = places // groups * (groups - 1)
    arrays = [spot, tgt_len, src_len, hidden_one, query, part, part_top, part_sum, wkv_cross, ln_gain, ln_bias]
    stay = [wo_cross, w_up, w_down, grad_out, pair_mine]

    def kernel(*refs):
        ins, refs = refs[: len(arrays)], refs[len(arrays) :]
        came_refs, refs = refs[: len(came)], refs[len(came) :]
        stay_refs, refs = refs[: len(stay)], refs[len(stay) :]
        outs, refs = refs[:9], refs[9:]
        middle_kernel(groups, *ins, *stay_refs, *came_refs, *outs[:3], *outs[6:8], *outs[3:6], outs[8], *refs)

    result_out, cross_norm, cross_along, grad_hidden_two, grad_attn, ln_part, keep_one, send_one, pair_all = call(
        kernel,
        [
            ((rows, width), BF16),
            (stats, F32),
            (stats, F32),
            ((rows, width), F32),
            ((rows, width), BF16),
            ((4, width), F32),
            ((first_sum.rows, width), BF16),
            ((first_sum.rows, width), BF16),
            ((count, places, 2 * width), BF16),
        ],
        [
            ((width, width), BF16),
            ((width, hidden_width), BF16),
            ((hidden_width, width), BF16),
            ((rows, width), BF16),
            ((count, away, 2 * width), BF16),
            ((2, first_sum.rows, width), BF16),
            ((count, away, 2 * TILE), F32),
            ((tiles, 2 * TILE, width), BF16),
            ((count, width, away), BF16),
            ((width, rows), F32),
            ((rows, hidden_width), BF16),
            ((rows, hidden_width), F32),
            ((rows, width), F32),
            pltpu.SemaphoreType.DMA((4,)),
            pltpu.SemaphoreType.DMA((count,)),
            pltpu.SemaphoreType.DMA((4,)),
        ],
        3,
        *arrays,
        *came,
        *stay,
        vmem=60,
        hbm_in=len(stay),
        hbm_out=3,
        aliases={len(arrays) + len(came) + len(stay) - 1: 8},
    )
    return result_out, cross_norm, cross_along, keep_one, send_one, grad_hidden_two, grad_attn, ln_part, pair_all


def body(
    target,
    memory,
    grad_out,
    tgt_len,
    src_len,
    w_qkv,
    w_out,
    wq_cross,
    wkv_cross,
    wo_cross,
    w_up,
    w_down,
    ln_gain,
    ln_bias,
):
    rows, width = target.shape
    half = rows // 2
    tiles = rows // TILE
    hidden_width = w_down.shape[0]
    groups = lax.axis_size("mem")
    me = lax.axis_index("mem")
    count = tgt_len.shape[1]
    span = memory.shape[1]
    places, away = groups * span, (groups - 1) * span
    dp = lax.axis_index("dp")
    short = width // 2
    first_sum = Summing(hidden_width + short, width, False)
    second_sum = Summing(3 * width + short, width, True)
    spot = first_sum.spot(me, dp)
    stats = (PAIRS * tiles, 2 * TILE)

    came = []
    for shift in range(1, groups):
        pairs = [(i, (i + shift) % groups) for i in range(groups)]
        sent = lax.dynamic_slice_in_dim(memory, ((me + shift) % groups) * count, count, 0)
        came.append(lax.ppermute(sent, "mem", pairs))

    sorted_rows, qkv, self_norm, self_attn_t, hidden_one, query, part, part_top, part_sum, pair_mine = call(
        functools.partial(self_forward_kernel, groups),
        [
            ((rows, width), BF16),
            ((rows, 3 * width), BF16),
            (stats, F32),
            ((width, rows), BF16),
            ((rows, width), F32),
            ((rows, width), BF16),
            ((width, rows), F32),
            (stats, F32),
            (stats, F32),
            ((count, places, 2 * width), BF16),
        ],
        [
            ((tiles, half, 2 * TILE), F32),
            ((count, span, 2 * TILE), F32),
            ((tiles, 2 * TILE, width), BF16),
            ((width, rows), BF16),
            ((count, width, span), BF16),
            ((count, span, 2 * width), BF16),
            pltpu.SemaphoreType.DMA((count,)),
        ],
        3,
        spot,
        tgt_len,
        src_len,
        target,
        w_qkv,
        w_out,
        wq_cross,
        ln_gain,
        ln_bias,
        memory,
        wkv_cross,
        vmem=60,
        hbm_out=1,
    )
    result_out, cross_norm, cross_along, keep_one, send_one, grad_hidden_two, grad_attn, ln_part, pair_all = middle(
        groups, first_sum, stats, spot, tgt_len, src_len, hidden_one, query, part, part_top, part_sum, wkv_cross,
        ln_gain, ln_bias, wo_cross, w_up, w_down, grad_out, pair_mine, came,
    )
    came_one = first_sum.core_swap(send_one)

    def cross_backward(block):
        sentences = 1 if block == 0 else count - 1
        return call(
            functools.partial(cross_backward_kernel, groups, block),
            [((sentences, places, 2 * width), BF16), ((width, half), BF16)],
            [
                ((sentences, places, 2 * width), BF16),
                ((sentences, places, 2 * TILE), F32),
                ((half // TILE, 2 * TILE, width), BF16),
                ((half // TILE, 2 * TILE, width), BF16),
                ((sentences, width, places), BF16),
                ((SLAB, half), F32),
                ((sentences, places, 2 * SLAB), F32),
                pltpu.SemaphoreType.DMA((1,)),
            ],
            3,
            spot,
            tgt_len,
            src_len,
            query,
            cross_norm,
            cross_along,
            grad_attn,
            pair_all,
            work=10,
            vmem=58 if block == 0 else 32,
            hbm_in=1,
        )

    pair_grad_long, query_grad_t_long = cross_backward(0)
    came_one, pair_grad_long = lax.optimization_barrier((came_one, pair_grad_long))
    parts_one = first_sum.first_split(spot, keep_one, came_one)
    parts_one, pair_all = lax.optimization_barrier((parts_one, pair_all))
    parts_one = first_sum.swap(parts_one, 0)
    pair_grad_rest, query_grad_t_rest = cross_backward(1)
    (wkv_grad,) = call(
        functools.partial(memory_weight_kernel, groups),
        [((2, width, width), BF16)],
        [((width, 2 * width), F32)],
        2,
        spot,
        tgt_len,
        pair_grad_long,
        pair_grad_rest,
        memory,
        *came,
        work=1,
        vmem=32,
    )
    parts_one, wkv_grad = lax.optimization_barrier((parts_one, wkv_grad))
    parts_one = first_sum.split(1, spot, parts_one)
    parts_one, wkv_grad = lax.optimization_barrier((parts_one, wkv_grad))
    parts_one = first_sum.swap(parts_one, 1)
    keep_mid, send_mid, grad_hidden_one, grad_self = call(
        first_norm_backward_kernel,
        [
            ((2 * width + LN_ROWS, width), BF16),
            ((2 * width + LN_ROWS, width), BF16),
            ((rows, width), F32),
            ((rows, width), BF16),
        ],
        [],
        1,
        spot,
        hidden_one,
        query_grad_t_long,
        query_grad_t_rest,
        grad_hidden_two,
        wq_cross,
        w_out,
        self_attn_t,
        ln_gain,
        ln_bias,
        ln_part,
        wkv_grad,
        work=10,
        vmem=24,
    )
    grad_triple, *last = call(
        self_backward_kernel,
        [((rows, 3 * width), BF16)] + [(((width + short) // LAST_PARTS, width), BF16)] * (2 * LAST_PARTS),
        [
            ((tiles, half, 2 * TILE), F32),
            ((tiles, 2 * TILE, width), BF16),
            ((tiles, 2 * TILE, width), BF16),
            ((width, rows), BF16),
            ((width, rows), BF16),
        ],
        2,
        spot,
        tgt_len,
        qkv,
        self_norm,
        grad_self,
        sorted_rows,
        work=0.1,
        vmem=28,
    )
    came_mid = second_sum.core_swap(send_mid)
    parts_one, last, came_mid, pair_grad_long = lax.optimization_barrier(
        (parts_one, last, came_mid, pair_grad_long)
    )
    keep_last = last[:LAST_PARTS]
    came_last = [second_sum.core_swap(part) for part in last[LAST_PARTS:]]
    parts_one = first_sum.split(2, spot, parts_one)
    came_mid, parts_one = lax.optimization_barrier((came_mid, parts_one))
    parts_two = second_sum.first_split(
        spot, keep_mid, came_mid, *[part for both in zip(keep_last, came_last) for part in both]
    )
    parts_one = first_sum.swap(parts_one, 2)
    parts_two, pair_grad_long, grad_triple = lax.optimization_barrier((parts_two, pair_grad_long, grad_triple))
    parts_two = second_sum.swap(parts_two, 0)
    grad_mine, *grad_away = call(
        functools.partial(memory_grad_kernel, groups),
        [((count, span, width), BF16)] + [((count, span // 2, width), BF16)] * (2 * (groups - 1)),
        [],
        2,
        spot,
        tgt_len,
        pair_grad_long,
        pair_grad_rest,
        wkv_cross,
        work=0.01,
        vmem=32,
    )
    (grad_target,) = call(
        target_kernel,
        [((rows, width), BF16)],
        [],
        2,
        spot,
        tgt_len,
        grad_triple,
        w_qkv,
        grad_hidden_one,
        work=0.01,
        vmem=16,
    )
    parts_one, parts_two, grad_away, grad_target = lax.optimization_barrier(
        (parts_one, parts_two, grad_away, grad_target)
    )
    backs = [[], []]
    for i, grads in enumerate(grad_away):
        shift = i // 2 + 1
        backs[i % 2].append(lax.ppermute(grads, "mem", [(k, (k - shift) % groups) for k in range(groups)]))
    parts_two = second_sum.swap(second_sum.split(1, spot, parts_two), 1)
    spread_one = first_sum.spread(2, first_sum.total(parts_one)[0])
    parts_two, spread_one, backs[0] = lax.optimization_barrier((parts_two, spread_one, backs[0]))
    spread_one = first_sum.spread(1, first_sum.join(2, spot, spread_one))
    parts_two = second_sum.swap(second_sum.split(2, spot, parts_two), 2)
    parts_two, spread_one, backs[1] = lax.optimization_barrier((parts_two, spread_one, backs[1]))
    spread_one = first_sum.spread(0, first_sum.join(1, spot, spread_one))
    sum_two, norm_sums = second_sum.total(parts_two)
    spread_two = second_sum.spread(2, sum_two)
    spread_two = second_sum.spread(1, second_sum.join(2, spot, spread_two))
    joined_two = second_sum.join(1, spot, spread_two)
    spread_one, joined_two = lax.optimization_barrier((spread_one, joined_two))
    other_one = [first_sum.core_swap(array) for array in spread_one]
    chunks = hidden_width // width
    pieces = []
    for chunk in range(chunks):
        side, here = chunk // (chunks // 2), chunk % (chunks // 2)
        pieces.append((side, here * width, width, 0, chunk * width, 0))
        pieces.append((side, (chunks // 2 + here) * width, width, 1, 0, chunk * width))
    for side in range(2):
        pieces.append((side, chunks * width, short, 2, side * short, 0))
    grad_w_down, grad_w_up, grad_wo = first_sum.finish(
        spot,
        spread_one,
        other_one,
        pieces,
        [((hidden_width, width), F32), ((width, hidden_width), F32), ((width, width), F32)],
    )
    spread_two = second_sum.spread(0, joined_two)
    spread_two, grad_w_down = lax.optimization_barrier((spread_two, grad_w_down))
    other_two = [second_sum.core_swap(array) for array in spread_two]
    pieces = [
        (0, 0, width, 0, 0, 0),
        (0, width, width, 1, 0, 0),
        (0, 2 * width, width, 2, 0, 0),
        (0, 3 * width, short, 2, 0, width),
        (1, 0, width, 1, 0, width),
        (1, width, width, 3, 0, 0),
        (1, 2 * width, short, 2, short, width),
        (1, 2 * width + short, width, 2, 0, 2 * width),
    ]
    grad_wq, grad_wkv, grad_w_qkv, grad_w_out = second_sum.finish(
        spot,
        spread_two,
        other_two,
        pieces,
        [
            ((width, width), F32),
            ((width, 2 * width), F32),
            ((width, 3 * width), F32),
            ((width, width), F32),
        ],
    )
    grad_memory = jnp.zeros(memory.shape, BF16)
    grad_memory = lax.dynamic_update_slice(grad_memory, grad_mine, (me * count, 0, 0))
    for part in range(2):
        for i, grads in enumerate(backs[part]):
            owner = (me + i + 1) % groups
            grad_memory = lax.dynamic_update_slice(grad_memory, grads, (owner * count, part * (span // 2), 0))
    return (
        result_out,
        grad_target,
        grad_memory,
        grad_w_qkv,
        grad_w_out,
        grad_wq,
        grad_wkv,
        grad_wo,
        grad_w_up,
        grad_w_down,
        norm_sums[:3],
        norm_sums[3:6],
    )


def solution(mesh):
    rows_spec = P(("dp", "mem"), None)
    memory_spec = P("dp", "mem", None)
    return jax.shard_map(
        body,
        mesh=mesh,
        in_specs=(rows_spec, memory_spec, rows_spec, P("dp", None), P("dp", None)) + (P(),) * 9,
        out_specs=(rows_spec, rows_spec, memory_spec) + (P(),) * 9,
        check_vma=False,
    )
```

```python
import functools
import math

import jax
import jax.numpy as jnp
from jax import lax
from jax.experimental import pallas as pl
from jax.experimental.pallas import tpu as pltpu
from jax.sharding import PartitionSpec as P

HEADS = 8
PAIRS = HEADS // 2
SLAB = 128
SIDE = SLAB // 2
TILE = 128
MASKED = -1e30
EPSILON = 1e-05
F32 = jnp.float32
BF16 = jnp.bfloat16
MIB = 1024 * 1024
LN_ROWS = 16
LAST_PARTS = 1


def dot(left, right):
    return jnp.dot(left, right, preferred_element_type=F32)


def dot_nt(left, right):
    return lax.dot_general(left, right, (((1,), (1,)), ((), ())), preferred_element_type=F32)


def dot_tn(left, right):
    return lax.dot_general(left, right, (((0,), (0,)), ((), ())), preferred_element_type=F32)


def iota(shape, axis):
    return lax.broadcasted_iota(jnp.int32, shape, axis)


def norm_parts(hidden):
    centre = hidden - jnp.mean(hidden, axis=-1, keepdims=True)
    inverse = lax.rsqrt(jnp.mean(centre * centre, axis=-1, keepdims=True) + EPSILON)
    return centre * inverse, inverse


def norm_backward(upstream, unit, inverse, gain_row):
    scaled = upstream * gain_row
    shifted = (
        scaled
        - jnp.mean(scaled, axis=-1, keepdims=True)
        - unit * jnp.mean(scaled * unit, axis=-1, keepdims=True)
    )
    gain_grad = jnp.sum(upstream * unit, axis=0, keepdims=True)
    return inverse * shifted, gain_grad, jnp.sum(upstream, axis=0, keepdims=True)


def sentence_order(me, len_ref):
    count = len_ref.shape[1]
    lengths = [len_ref[me, k] for k in range(count)]
    longest, best, start, running = jnp.int32(0), lengths[0], jnp.int32(0), jnp.int32(0)
    for k in range(1, count):
        running = running + lengths[k - 1]
        more = lengths[k] > best
        longest = jnp.where(more, k, longest)
        start = jnp.where(more, running, start)
        best = jnp.where(more, lengths[k], best)
    order = [longest] + [jnp.where(k < longest, k, k + 1) for k in range(count - 1)]
    bounds = [jnp.int32(0)]
    for k in range(1, count):
        bounds.append(bounds[-1] + len_ref[me, order[k]])
    return order, start, bounds


def moved_rows(index, start, half):
    return jnp.where(index < start, index + half, jnp.where(index < start + half, index - start, index))


def sort_matrix(rows, start):
    spot = moved_rows(iota((rows, rows), 1), start, rows // 2)
    return jnp.where(spot == iota((rows, rows), 0), 1.0, 0.0).astype(BF16)


def unsort_matrix(rows, start):
    spot = moved_rows(iota((rows, rows), 0), start, rows // 2)
    return jnp.where(spot == iota((rows, rows), 1), 1.0, 0.0).astype(BF16)


def side_masks(width):
    side = iota((1, width), 1) % SLAB
    first = jnp.where(side < SLAB // 2, 1.0, 0.0)
    return first.astype(BF16), (1.0 - first).astype(BF16)


def each_pair(step):
    def advance(pair, carry):
        step(pair)
        return carry

    lax.fori_loop(0, PAIRS, advance, 0)


def slab_of(pair, first=0):
    if isinstance(pair, int):
        return pl.ds(first + pair * SLAB, SLAB)
    return pl.ds(pl.multiple_of(first + pair * SLAB, SLAB), SLAB)


def pack_heads(out_ref, rows, width):
    even, odd = side_masks(width)
    for t in range(out_ref.shape[0]):
        tile = rows(t * TILE, TILE)
        out_ref[t, :TILE, :] = tile * even
        out_ref[t, TILE:, :] = tile * odd


def fill_self_bias(bias_ref, bounds, half):
    for t in range(bias_ref.shape[0]):
        block, inner = t // (half // TILE), t % (half // TILE)
        key = iota((half, 2 * TILE), 0)
        query = iota((half, 2 * TILE), 1) % TILE + inner * TILE
        allowed = key <= query
        if block == 1:
            first = jnp.zeros((half, 2 * TILE), jnp.int32)
            for bound in bounds[1:-1]:
                first = jnp.where(query >= bound, bound, first)
            allowed = allowed & (key >= first)
        bias_ref[t] = jnp.where(allowed, 0.0, MASKED)


def self_keys(t, half):
    per = half // TILE
    return (t // per) * half, (t % per + 1) * TILE


def fill_live_bias(bias_ref, me, groups, parts, span, src_ref, sentences):
    key = iota((span, bias_ref.shape[2]), 0)
    for j, sentence in enumerate(sentences):
        for i, part in enumerate(parts):
            place = lax.rem(me - part + groups, groups) * span + key
            live = place < src_ref[me, sentence]
            bias_ref[j, pl.ds(i * span, span), :] = jnp.where(live, 0.0, MASKED)


def cross_units(bounds, half):
    units = [(t, 0, None) for t in range(half // TILE)]
    middle = half // 2
    last = jnp.int32(1)
    for bound in bounds[1:-1]:
        last = last + jnp.where(bound < middle, 1, 0)
    ends = bounds[1:]
    column = iota((1, 2 * TILE), 1) % TILE
    for u in range(len(ends) + 1):
        early = u < last
        sentence = jnp.where(early, u + 1, u)
        tile = jnp.where(early, 0, 1)
        low, high = jnp.int32(0), ends[0]
        for k in range(1, len(ends)):
            low = jnp.where(sentence == k + 1, ends[k - 1], low)
            high = jnp.where(sentence == k + 1, ends[k], high)
        row = column + tile * TILE
        units.append((tile + half // TILE, sentence, (row >= low) & (row < high)))
    return units


def own_sides(both):
    return jnp.concatenate([both[:SIDE, :TILE], both[SIDE:, TILE:]], axis=0)


def side_rows(row):
    even = jnp.broadcast_to(row[:, :TILE], (SIDE, TILE))
    return jnp.concatenate([even, jnp.broadcast_to(row[:, TILE:], (SIDE, TILE))], axis=0)


def tile_columns(tile):
    if isinstance(tile, int):
        return pl.ds(tile * TILE, TILE)
    return pl.ds(pl.multiple_of(tile * TILE, TILE), TILE)


def self_forward_kernel(
    groups,
    me_ref,
    len_ref,
    src_ref,
    target_ref,
    w_qkv_ref,
    w_out_ref,
    wq_ref,
    gain_ref,
    bias_row_ref,
    memory_ref,
    wkv_ref,
    sorted_ref,
    qkv_ref,
    norm_ref,
    attn_t_ref,
    hidden_ref,
    query_ref,
    part_ref,
    top_ref,
    sum_ref,
    pair_out_ref,
    bias_ref,
    live_ref,
    q_pack_ref,
    value_t_ref,
    cross_value_t_ref,
    pair_ref,
    copy_sem,
):
    rows, width = target_ref.shape
    half = rows // 2
    me = me_ref[0]
    order, start, bounds = sentence_order(me, len_ref)
    count, span = pair_ref.shape[0], pair_ref.shape[1]
    copies = []
    for j in range(count):
        block = memory_ref[me * count + order[j]]
        pair_ref[j] = dot(block, wkv_ref[...]).astype(BF16)
        copy = pltpu.make_async_copy(
            pair_ref.at[j], pair_out_ref.at[j, pl.ds(0, span), :], copy_sem.at[j]
        )
        copy.start()
        copies.append(copy)
    sorted_rows = dot(sort_matrix(rows, start), target_ref[...]).astype(BF16)
    sorted_ref[...] = sorted_rows
    fill_self_bias(bias_ref, bounds, half)
    queries = (dot(sorted_rows, w_qkv_ref[:, :width]).astype(BF16) * 0.125).astype(BF16)
    qkv_ref[:, :width] = queries
    pack_heads(q_pack_ref, lambda first, size: queries[first : first + size], width)
    qkv_ref[:, width : 2 * width] = dot(sorted_rows, w_qkv_ref[:, width : 2 * width]).astype(BF16)
    values = dot(sorted_rows, w_qkv_ref[:, 2 * width :]).astype(BF16)
    qkv_ref[:, 2 * width :] = values
    value_t_ref[...] = values.T
    tiles = rows // TILE

    def self_step(pair):
        slab = slab_of(pair)
        for t in range(tiles):
            first, size = self_keys(t, half)
            keys = qkv_ref[pl.ds(first, size), slab_of(pair, width)]
            scores = dot_nt(keys, q_pack_ref[t, :, slab]) + bias_ref[t, :size, :]
            top = jnp.max(scores, axis=0, keepdims=True)
            weights = jnp.exp(scores - top)
            total = jnp.sum(weights, axis=0, keepdims=True)
            probs = (weights * (1.0 / total)).astype(BF16)
            both = dot(value_t_ref[slab, pl.ds(first, size)], probs)
            attn_t_ref[slab, tile_columns(t)] = own_sides(both).astype(BF16)
            norm_ref[pl.ds(pair * tiles + t, 1), :] = top + jnp.log(total)

    each_pair(self_step)
    hidden = sorted_rows.astype(F32) + dot(attn_t_ref[...].T, w_out_ref[...])
    hidden_ref[...] = hidden
    unit, _ = norm_parts(hidden)
    normed = (unit * gain_ref[0:1] + bias_row_ref[0:1]).astype(BF16)
    query_ref[...] = (dot(normed, wq_ref[...]).astype(BF16) * 0.125).astype(BF16)

    pack_heads(q_pack_ref, lambda first, size: query_ref[first : first + size, :], width)
    fill_live_bias(live_ref, me, groups, [0], span, src_ref, order)
    for j in range(count):
        cross_value_t_ref[j] = pair_ref[j, :, width:].T
    units = cross_units(bounds, half)

    def cross_step(pair):
        slab = slab_of(pair)
        for tile, sentence, columns in units:
            scores = dot_nt(pair_ref[sentence, :, slab], q_pack_ref[tile, :, slab]) + live_ref[sentence]
            top = jnp.max(scores, axis=0, keepdims=True)
            weights = jnp.exp(scores - top)
            total = jnp.sum(weights, axis=0, keepdims=True)
            result = own_sides(dot(cross_value_t_ref[sentence, slab, :], weights.astype(BF16)))
            here = tile_columns(tile)
            row = pl.ds(pair * tiles + tile, 1)
            if columns is not None:
                result = jnp.where(columns[:, :TILE], result, part_ref[slab, here])
                top = jnp.where(columns, top, top_ref[row, :])
                total = jnp.where(columns, total, sum_ref[row, :])
            part_ref[slab, here] = result
            top_ref[row, :] = top
            sum_ref[row, :] = total

    part_ref[...] = jnp.zeros_like(part_ref)
    top_ref[...] = jnp.zeros_like(top_ref)
    sum_ref[...] = jnp.ones_like(sum_ref)
    each_pair(cross_step)
    for copy in copies:
        copy.wait()


def middle_kernel(
    groups,
    me_ref,
    len_ref,
    src_ref,
    hidden_one_ref,
    query_ref,
    part_ref,
    top_ref,
    sum_ref,
    wkv_ref,
    gain_ref,
    bias_row_ref,
    wo_hbm,
    w_up_hbm,
    w_down_hbm,
    grad_out_hbm,
    pair_in_hbm,
    *refs,
):
    came_refs = refs[: groups - 1]
    (
        out_ref,
        norm_ref,
        along_ref,
        keep_hbm,
        send_hbm,
        grad_hidden_ref,
        grad_attn_ref,
        ln_ref,
        pair_hbm,
        wo_ref,
        w_up_ref,
        w_down_ref,
        grad_out_ref,
        pair_ref,
        halves_ref,
        live_ref,
        q_pack_ref,
        value_t_ref,
        attn_t_ref,
        active_ref,
        slope_ref,
        total_ref,
        load_sem,
        pair_sem,
        store_sem,
    ) = refs[groups - 1 :]
    rows, width = hidden_one_ref.shape
    half = rows // 2
    me = me_ref[0]
    count, away = pair_ref.shape[0], pair_ref.shape[1]
    span = away // (groups - 1)
    loads = [
        pltpu.make_async_copy(source, there, load_sem.at[i])
        for i, (source, there) in enumerate(
            [(wo_hbm, wo_ref), (w_up_hbm, w_up_ref), (w_down_hbm, w_down_ref), (grad_out_hbm, grad_out_ref)]
        )
    ]
    for copy in loads:
        copy.start()
    order, start, bounds = sentence_order(me, len_ref)
    fill_live_bias(live_ref, me, groups, list(range(1, groups)), span, src_ref, order)
    pack_heads(q_pack_ref, lambda first, size: query_ref[first : first + size, :], width)
    pair_copies = []
    for j in range(count):
        for part in range(1, groups):
            block = came_refs[part - 1][order[j]]
            pair_ref[j, pl.ds((part - 1) * span, span), :] = dot(block, wkv_ref[...]).astype(BF16)
        value_t_ref[j] = pair_ref[j, :, width:].T
        copy = pltpu.make_async_copy(pair_ref.at[j], pair_hbm.at[j, pl.ds(span, away), :], pair_sem.at[j])
        copy.start()
        pair_copies.append(copy)
    units = cross_units(bounds, half)
    tiles = rows // TILE

    def cross_step(pair):
        slab = slab_of(pair)
        for tile, sentence, columns in units:
            here = tile_columns(tile)
            row = pl.ds(pair * tiles + tile, 1)
            scores = dot_nt(pair_ref[sentence, :, slab], q_pack_ref[tile, :, slab]) + live_ref[sentence]
            before = top_ref[row, :]
            top = jnp.maximum(jnp.max(scores, axis=0, keepdims=True), before)
            weights = jnp.exp(scores - top)
            scale = jnp.exp(before - top)
            total = jnp.sum(weights, axis=0, keepdims=True) + sum_ref[row, :] * scale
            result = own_sides(dot(value_t_ref[sentence, slab, :], weights.astype(BF16)))
            result = (result + part_ref[slab, here] * side_rows(scale)) * side_rows(1.0 / total)
            norm = top + jnp.log(total)
            if columns is not None:
                result = jnp.where(columns[:, :TILE], result, attn_t_ref[slab, here])
                norm = jnp.where(columns, norm, norm_ref[row, :])
            attn_t_ref[slab, here] = result
            norm_ref[row, :] = norm

    attn_t_ref[...] = jnp.zeros_like(attn_t_ref)
    norm_ref[...] = jnp.zeros_like(norm_ref)
    for pair in range(PAIRS):
        cross_step(pair)
    attn_t_low = attn_t_ref[...].astype(BF16)
    loads[0].wait()
    unit_one, _ = norm_parts(hidden_one_ref[...])
    normed_one = unit_one * gain_ref[0:1] + bias_row_ref[0:1]
    hidden_two = normed_one + dot(attn_t_low.T, wo_ref[...])
    unit_two, inverse_two = norm_parts(hidden_two)
    normed_two = unit_two * gain_ref[1:2] + bias_row_ref[1:2]
    normed_two_low = normed_two.astype(BF16)
    total_ref[...] = normed_two
    chunk = width
    chunks = w_down_ref.shape[0] // chunk
    loads[1].wait()
    loads[2].wait()

    def up_step(c, carry):
        cols = pl.ds(pl.multiple_of(c * chunk, chunk), chunk)
        upper = dot(normed_two_low, w_up_ref[:, cols])
        sigma = 0.5 * jnp.tanh(0.5 * upper) + 0.5
        active = (upper * sigma).astype(BF16)
        active_ref[:, cols] = active
        slope_ref[:, cols] = sigma * (1.0 + upper * (1.0 - sigma))
        total_ref[...] += dot(active, w_down_ref[cols, :])
        return carry

    lax.fori_loop(0, chunks, up_step, 0)

    unit_three, inverse_three = norm_parts(total_ref[...])
    result = (unit_three * gain_ref[2:3] + bias_row_ref[2:3]).astype(BF16)
    out_ref[...] = dot(unsort_matrix(rows, start), result).astype(BF16)
    loads[3].wait()
    upstream = dot(sort_matrix(rows, start), grad_out_ref[...])
    grad_three, gain_three, bias_three = norm_backward(upstream, unit_three, inverse_three, gain_ref[2:3])
    grad_down = grad_three.astype(BF16)
    total_ref[...] = grad_three
    normed_two_t = normed_two_low.T

    def down_step(c, carry):
        cols = pl.ds(pl.multiple_of(c * chunk, chunk), chunk)
        grad_upper = (dot_nt(grad_down, w_down_ref[cols, :]) * slope_ref[:, cols]).astype(BF16)
        down_part = dot_tn(active_ref[:, cols], grad_down).astype(BF16)
        up_part = dot(normed_two_t, grad_upper).astype(BF16)
        half_index, here = c // (chunks // 2), lax.rem(c, chunks // 2)
        down_rows = pl.ds(pl.multiple_of(here * chunk, chunk), chunk)
        up_rows = pl.ds(pl.multiple_of((chunks // 2 + here) * chunk, chunk), chunk)
        halves_ref[half_index, down_rows, :] = down_part
        halves_ref[half_index, up_rows, :] = up_part
        total_ref[...] += dot_nt(grad_upper, w_up_ref[:, cols])
        return carry

    lax.fori_loop(0, chunks, down_step, 0)

    most = chunks * chunk
    core = me_ref[1]
    stores = [
        pltpu.make_async_copy(
            halves_ref.at[half_index, pl.ds(first, size)], there.at[pl.ds(first, size)], store_sem.at[i]
        )
        for i, (half_index, there, first, size) in enumerate(
            [
                (1 - core, send_hbm, 0, most),
                (core, keep_hbm, 0, most),
                (1 - core, send_hbm, most, halves_ref.shape[1] - most),
                (core, keep_hbm, most, halves_ref.shape[1] - most),
            ]
        )
    ]
    stores[0].start()
    stores[1].start()
    grad_two, gain_two, bias_two = norm_backward(total_ref[...], unit_two, inverse_two, gain_ref[1:2])
    grad_two_low = grad_two.astype(BF16)
    wo_grad = dot(attn_t_low, grad_two_low).astype(BF16)
    used = most + width // 2
    for half_index in range(2):
        piece = wo_grad[half_index * (width // 2) : (half_index + 1) * (width // 2)]
        halves_ref[half_index, pl.ds(most, width // 2), :] = piece
        if halves_ref.shape[1] > used:
            halves_ref[half_index, used:, :] = jnp.zeros((halves_ref.shape[1] - used, width), BF16)
    stores[2].start()
    stores[3].start()
    grad_hidden_ref[...] = grad_two
    grad_attn = dot_nt(grad_two_low, wo_ref[...]).astype(BF16)
    grad_attn_ref[...] = grad_attn
    product = grad_attn.T.astype(F32) * attn_t_ref[...]
    for pair in range(PAIRS):
        for side in range(2):
            first = pair * SLAB + side * SIDE
            along = jnp.sum(product[first : first + SIDE], axis=0, keepdims=True)
            for t in range(tiles):
                along_ref[pair * tiles + t : pair * tiles + t + 1, side * TILE : (side + 1) * TILE] = along[
                    :, t * TILE : (t + 1) * TILE
                ]
    ln_ref[...] = jnp.concatenate([gain_two, gain_three, bias_two, bias_three], axis=0)
    for copy in pair_copies + stores:
        copy.wait()


def cross_backward_kernel(
    groups,
    block,
    me_ref,
    len_ref,
    src_ref,
    query_ref,
    norm_ref,
    along_ref,
    grad_attn_ref,
    pair_hbm,
    pair_grad_ref,
    query_grad_t_ref,
    pair_ref,
    live_ref,
    q_pack_ref,
    g_pack_ref,
    key_t_ref,
    query_sum_ref,
    sum_ref,
    load_sem,
):
    rows, width = query_ref.shape
    half = rows // 2
    me = me_ref[0]
    sentences, places = pair_ref.shape[0], pair_ref.shape[1]
    first_sentence = 0 if block == 0 else 1
    load = pltpu.make_async_copy(pair_hbm.at[pl.ds(first_sentence, sentences)], pair_ref, load_sem.at[0])
    load.start()
    order, start, bounds = sentence_order(me, len_ref)
    mine = order[:1] if block == 0 else order[1:]
    fill_live_bias(live_ref, me, groups, list(range(groups)), places // groups, src_ref, mine)
    low = block * half
    pack_heads(q_pack_ref, lambda first, size: query_ref[low + first : low + first + size, :], width)
    pack_heads(g_pack_ref, lambda first, size: grad_attn_ref[low + first : low + first + size, :], width)
    tiles, per = rows // TILE, half // TILE
    units = cross_units(bounds, half)
    units = units[:per] if block == 0 else units[per:]
    load.wait()
    for j in range(sentences):
        key_t_ref[j] = pair_ref[j, :, :width].T

    def pair_step(pair):
        slab, value_slab = slab_of(pair), slab_of(pair, width)
        query_sum_ref[...] = jnp.zeros_like(query_sum_ref)
        sum_ref[...] = jnp.zeros_like(sum_ref)
        for tile, sentence, columns in units:
            j = sentence - first_sentence
            t = tile - block * per
            here = tile_columns(t)
            row = pl.ds(pair * tiles + tile, 1)
            q_rows, g_rows = q_pack_ref[t, :, slab], g_pack_ref[t, :, slab]
            norm = norm_ref[row, :]
            if columns is not None:
                norm = jnp.where(columns, norm, -MASKED)
            scores = dot_nt(pair_ref[j, :, slab], q_rows) + live_ref[j]
            probs = jnp.exp(scores - norm)
            grad_probs = dot_nt(pair_ref[j, :, value_slab], g_rows)
            grad_scores = (probs * (grad_probs - along_ref[row, :])).astype(BF16)
            sum_ref[j, :, :SLAB] += dot(grad_scores, q_rows)
            sum_ref[j, :, SLAB:] += dot(probs.astype(BF16), g_rows)
            query_sum_ref[:, here] += own_sides(dot(key_t_ref[j, slab, :], grad_scores))
        query_grad_t_ref[slab, :] = (query_sum_ref[...] * 0.125).astype(BF16)
        pair_grad_ref[:, :, slab] = sum_ref[:, :, :SLAB].astype(BF16)
        pair_grad_ref[:, :, value_slab] = sum_ref[:, :, SLAB:].astype(BF16)

    for pair in range(PAIRS):
        pair_step(pair)


def memory_weight_kernel(groups, me_ref, len_ref, pair_grad_long_ref, pair_grad_rest_ref, memory_ref, *refs):
    came_refs = refs[: groups - 1]
    wkv_grad_ref, total_ref = refs[groups - 1 :]
    width = memory_ref.shape[2]
    me = me_ref[0]
    count = len_ref.shape[1]
    span = pair_grad_long_ref.shape[1] // groups
    order, _, _ = sentence_order(me, len_ref)
    for j in range(count):
        pair_grad_ref, here = (pair_grad_long_ref, 0) if j == 0 else (pair_grad_rest_ref, j - 1)
        blocks = [memory_ref[me * count + order[j]]] + [ref[order[j]] for ref in came_refs]
        term = dot_tn(jnp.concatenate(blocks, axis=0), pair_grad_ref[here])
        if j == 0:
            total_ref[...] = term
        else:
            total_ref[...] += term
    wkv_grad_ref[0] = total_ref[:, :width].astype(BF16)
    wkv_grad_ref[1] = total_ref[:, width:].astype(BF16)


def memory_grad_kernel(pieces, me_ref, len_ref, pair_grad_long_ref, pair_grad_rest_ref, wkv_ref, *outs):
    count = len_ref.shape[1]
    order, _, _ = sentence_order(me_ref[0], len_ref)
    for j in range(count):
        pair_grad_ref, here = (pair_grad_long_ref, 0) if j == 0 else (pair_grad_rest_ref, j - 1)
        for (first, size), out in zip(pieces, outs):
            out[order[j]] = dot_nt(pair_grad_ref[here, pl.ds(first, size), :], wkv_ref[...]).astype(BF16)


def first_norm_backward_kernel(
    me_ref,
    hidden_one_ref,
    query_grad_t_long_ref,
    query_grad_t_rest_ref,
    grad_hidden_two_ref,
    wq_ref,
    w_out_ref,
    self_attn_t_ref,
    gain_ref,
    bias_row_ref,
    ln_in_ref,
    wkv_grad_ref,
    keep_ref,
    send_ref,
    grad_hidden_ref,
    grad_self_ref,
):
    width = wq_ref.shape[0]
    unit_one, inverse_one = norm_parts(hidden_one_ref[...])
    normed_one = (unit_one * gain_ref[0:1] + bias_row_ref[0:1]).astype(BF16)
    query_grad = jnp.concatenate([query_grad_t_long_ref[...].T, query_grad_t_rest_ref[...].T], axis=0)
    upstream = grad_hidden_two_ref[...] + dot_nt(query_grad, wq_ref[...])
    grad_one, gain_one, bias_one = norm_backward(upstream, unit_one, inverse_one, gain_ref[0:1])
    grad_hidden_ref[...] = grad_one
    grad_one_low = grad_one.astype(BF16)
    grad_self_ref[...] = dot_nt(grad_one_low, w_out_ref[...]).astype(BF16)
    wq_grad = dot_tn(normed_one, query_grad).astype(BF16)
    w_out_grad = dot(self_attn_t_ref[...], grad_one_low).astype(BF16)
    norms = jnp.concatenate(
        [gain_one, ln_in_ref[0:2], bias_one, ln_in_ref[2:4], jnp.zeros((LN_ROWS - 6, width), F32)], axis=0
    ).astype(BF16)

    def halves(low_ref, high_ref):
        low_ref[:width, :] = wq_grad
        low_ref[width : 2 * width, :] = wkv_grad_ref[0]
        high_ref[:width, :] = wkv_grad_ref[1]
        high_ref[width : 2 * width, :] = w_out_grad

    @pl.when(me_ref[1] == 0)
    def _():
        halves(keep_ref, send_ref)

    @pl.when(me_ref[1] != 0)
    def _():
        halves(send_ref, keep_ref)

    keep_ref[2 * width :, :] = norms
    send_ref[2 * width :, :] = norms


def self_backward_kernel(
    me_ref,
    len_ref,
    qkv_ref,
    norm_ref,
    grad_attn_ref,
    sorted_ref,
    grad_triple_ref,
    *refs,
):
    keep_refs, send_refs = refs[:LAST_PARTS], refs[LAST_PARTS : 2 * LAST_PARTS]
    self_backward(
        me_ref,
        len_ref,
        qkv_ref,
        norm_ref,
        grad_attn_ref,
        sorted_ref,
        grad_triple_ref,
        keep_refs,
        send_refs,
        *refs[2 * LAST_PARTS :],
    )


def self_backward(
    me_ref,
    len_ref,
    qkv_ref,
    norm_ref,
    grad_attn_ref,
    sorted_ref,
    grad_triple_ref,
    keep_refs,
    send_refs,
    bias_ref,
    q_pack_ref,
    g_pack_ref,
    key_t_ref,
    query_grad_t_ref,
):
    rows, width = sorted_ref.shape
    half = rows // 2
    _, _, bounds = sentence_order(me_ref[0], len_ref)
    fill_self_bias(bias_ref, bounds, half)
    pack_heads(q_pack_ref, lambda first, size: qkv_ref[first : first + size, :width], width)
    pack_heads(g_pack_ref, lambda first, size: grad_attn_ref[first : first + size, :], width)
    key_t_ref[...] = qkv_ref[:, width : 2 * width].T
    tiles, per = rows // TILE, half // TILE

    def pair_step(pair):
        slab, key_slab, value_slab = slab_of(pair), slab_of(pair, width), slab_of(pair, 2 * width)
        sums = [[None, None] for _ in range(tiles)]
        for t in range(tiles):
            first, size = self_keys(t, half)
            span = pl.ds(first, size)
            q_rows, g_rows = q_pack_ref[t, :, slab], g_pack_ref[t, :, slab]
            scores = dot_nt(qkv_ref[span, key_slab], q_rows) + bias_ref[t, :size, :]
            probs = jnp.exp(scores - norm_ref[pl.ds(pair * tiles + t, 1), :])
            grad_probs = dot_nt(qkv_ref[span, value_slab], g_rows)
            along = jnp.sum(probs * grad_probs, axis=0, keepdims=True)
            grad_scores = (probs * (grad_probs - along)).astype(BF16)
            parts = dot(grad_scores, q_rows), dot(probs.astype(BF16), g_rows)
            for i in range(size // TILE):
                spot = sums[first // TILE + i]
                for k in range(2):
                    piece = parts[k][i * TILE : (i + 1) * TILE]
                    spot[k] = piece if spot[k] is None else spot[k] + piece
            query_grad_t_ref[slab, tile_columns(t)] = (
                own_sides(dot(key_t_ref[slab, span], grad_scores)) * 0.125
            ).astype(BF16)
        for t in range(tiles):
            grad_triple_ref[pl.ds(t * TILE, TILE), key_slab] = sums[t][0].astype(BF16)
            grad_triple_ref[pl.ds(t * TILE, TILE), value_slab] = sums[t][1].astype(BF16)

    for pair in range(PAIRS):
        pair_step(pair)
    grad_triple_ref[:, :width] = query_grad_t_ref[...].T
    sorted_t = sorted_ref[...].T
    grads = [
        dot(sorted_t, grad_triple_ref[:, part * width : (part + 1) * width]).astype(BF16)
        for part in range(3)
    ]
    short = width // 2

    low = jnp.concatenate([grads[0], grads[1][:short]], axis=0)
    high = jnp.concatenate([grads[1][short:], grads[2]], axis=0)
    size = keep_refs[0].shape[0]

    def halves(low_refs, high_refs):
        for i in range(LAST_PARTS):
            low_refs[i][...] = low[i * size : (i + 1) * size]
            high_refs[i][...] = high[i * size : (i + 1) * size]

    @pl.when(me_ref[1] == 0)
    def _():
        halves(keep_refs, send_refs)

    @pl.when(me_ref[1] != 0)
    def _():
        halves(send_refs, keep_refs)


def target_kernel(me_ref, len_ref, grad_triple_ref, w_qkv_ref, grad_hidden_ref, grad_target_ref):
    rows = grad_hidden_ref.shape[0]
    _, start, _ = sentence_order(me_ref[0], len_ref)
    result = grad_hidden_ref[...] + dot_nt(grad_triple_ref[...], w_qkv_ref[...])
    grad_target_ref[...] = dot(unsort_matrix(rows, start), result.astype(BF16)).astype(BF16)


def tree_sum(terms):
    while len(terms) > 1:
        terms = [terms[i] + terms[i + 1] for i in range(0, len(terms), 2)]
    return terms[0]


def rows_of(ref, first, count):
    return ref[pl.ds(pl.multiple_of(first, 16), count), :].astype(F32)


def first_split_kernel(segments, ln, peers, spot_ref, *refs):
    ins, outs, sum_ref = refs[: 2 * segments], refs[2 * segments : -1], refs[-1]
    extra = LN_ROWS if ln else 0
    size = outs[0].shape[0] - extra
    used = 0
    for i in range(segments):
        keep_ref, came_ref = ins[2 * i], ins[2 * i + 1]
        count = keep_ref.shape[0] - (extra if i == 0 else 0)
        sum_ref[used : used + count, :] = (rows_of(keep_ref, 0, count) + rows_of(came_ref, 0, count)).astype(BF16)
        if i == 0 and ln:
            tail = (rows_of(keep_ref, count, LN_ROWS) + rows_of(came_ref, count, LN_ROWS)).astype(BF16)
        used += count
    if sum_ref.shape[0] > used:
        sum_ref[used:, :] = jnp.zeros((sum_ref.shape[0] - used, sum_ref.shape[1]), BF16)
    for d, out in enumerate(outs):
        out[:size, :] = sum_ref[pl.ds(pl.multiple_of((spot_ref[2] ^ d) * size, 16), size), :]
        if ln:
            out[size:, :] = tail


def split_kernel(stage, ln, peers, spot_ref, *refs):
    ins, outs = refs[:peers], refs[peers:]
    extra = LN_ROWS if ln else 0
    size = outs[0].shape[0] - extra
    if ln:
        tail = tree_sum([rows_of(ref, size * len(outs), LN_ROWS) for ref in ins]).astype(BF16)
    for d, out in enumerate(outs):
        first = (spot_ref[2 + stage] ^ d) * size
        out[:size, :] = tree_sum([rows_of(ref, first, size) for ref in ins]).astype(BF16)
        if ln:
            out[size:, :] = tail


def total_kernel(ln, count, *refs):
    ins, outs = refs[:count], refs[count:]
    size = outs[0].shape[0]
    outs[0][...] = tree_sum([rows_of(ref, 0, size) for ref in ins]).astype(BF16)
    if ln:
        outs[1][...] = tree_sum([rows_of(ref, size, LN_ROWS) for ref in ins])


def join_kernel(stage, spot_ref, *refs):
    out_ref = refs[-1]
    for d, ref in enumerate(refs[:-1]):
        size = ref.shape[0]
        out_ref[pl.ds(pl.multiple_of((spot_ref[2 + stage] ^ d) * size, 16), size), :] = ref[...]


def finish_kernel(offsets, peers, twisted, pieces, held, spot_ref, *refs):
    arrays, refs = refs[: 2 * len(offsets)], refs[2 * len(offsets) + held :]
    outs, (wide_ref, sem) = refs[:-2], refs[-2:]
    core = spot_ref[1]
    size, width = wide_ref.shape[1:]
    copies = []
    for k, ref in enumerate(arrays):
        wide_ref[k] = ref[...].astype(F32)
        d, other = offsets[k // 2], k % 2
        half = 1 - core if other else core
        place = spot_ref[3 if twisted and other else 2] ^ d
        for i in range(2):
            for j in range(peers):
                cut = []
                for piece_half, first, rows, out, row, col in pieces:
                    low, high = max(first, j * size), min(first + rows, (j + 1) * size)
                    if piece_half == i and low < high:
                        there = outs[out].at[pl.ds(row + low - first, high - low), pl.ds(col, width)]
                        here = wide_ref.at[k, pl.ds(low - j * size, high - low), :]
                        cut.append(pltpu.make_async_copy(here, there, sem.at[k, len(cut)]))
                copies.append(((half == i) & (place == j), cut))
                _start_all(*copies[-1])
    for chosen, cut in copies:
        _wait_all(chosen, cut)


def _start_all(chosen, cut):
    @pl.when(chosen)
    def _():
        for copy in cut:
            copy.start()


def _wait_all(chosen, cut):
    @pl.when(chosen)
    def _():
        for copy in cut:
            copy.wait()


class Summing:
    def __init__(self, rows, width, ln):
        self.width, self.ln = width, ln
        self.dp, self.mem = lax.axis_size("dp"), lax.axis_size("mem")
        z_size = 4
        x_size = self.dp // (2 * z_size)
        self.sizes = (x_size, self.mem, z_size)
        self.twisted = x_size == self.mem
        self.chunk = -(-rows // (16 * math.prod(self.sizes))) * 16
        self.rows = self.chunk * math.prod(self.sizes)

    def after(self, stage):
        return self.rows // math.prod(self.sizes[:stage])

    def axis(self, stage, core):
        return 1 - stage if self.twisted and core == 1 and stage < 2 else stage

    def coords(self, dp, mem):
        return [dp // 2 % self.sizes[0], mem, dp // (2 * self.sizes[0])], dp % 2

    def spot(self, me, dp):
        (x, mem, z), core = self.coords(dp, me)
        if self.twisted:
            x, mem = jnp.where(core == 0, x, mem), jnp.where(core == 0, mem, x)
        return jnp.stack([me, core, x, mem, z]).astype(jnp.int32)

    def permute(self, array, stage, offset):
        pairs = []
        for dp in range(self.dp):
            for mem in range(self.mem):
                spots, core = self.coords(dp, mem)
                if stage is None:
                    core ^= offset
                else:
                    spots[self.axis(stage, core)] ^= offset
                to_dp = (spots[2] * self.sizes[0] + spots[0]) * 2 + core
                pairs.append((dp * self.mem + mem, to_dp * self.mem + spots[1]))
        return lax.ppermute(array, ("dp", "mem"), pairs)

    def core_swap(self, send):
        return self.permute(send, None, 1)

    def swap(self, arrays, stage):
        return [arrays[0]] + [self.permute(array, stage, d) for d, array in enumerate(arrays) if d > 0]

    def spread(self, stage, array):
        return [array] + [self.permute(array, stage, d) for d in range(1, self.sizes[stage])]

    def messages(self, stage):
        size = self.after(stage + 1) + (LN_ROWS if self.ln else 0)
        return [((size, self.width), BF16)] * self.sizes[stage]

    def first_split(self, spot, *arrays):
        kernel = functools.partial(first_split_kernel, len(arrays) // 2, self.ln, self.sizes[0])
        return call(kernel, self.messages(0), [((self.rows, self.width), BF16)], 1, spot, *arrays, work=0.01)

    def split(self, stage, spot, arrays):
        kernel = functools.partial(split_kernel, stage, self.ln, self.sizes[stage - 1])
        return call(kernel, self.messages(stage), [], 1, spot, *arrays, work=0.01)

    def total(self, arrays):
        outs = [((self.chunk, self.width), BF16)]
        if self.ln:
            outs.append(((LN_ROWS, self.width), F32))
        return call(functools.partial(total_kernel, self.ln, self.sizes[2]), outs, [], 0, *arrays, work=0.01)

    def join(self, stage, spot, arrays):
        outs = [((self.after(stage), self.width), BF16)]
        return call(functools.partial(join_kernel, stage), outs, [], 1, spot, *arrays, work=0.01)[0]

    def finish(self, spot, mine, others, offsets, pieces, outs, held=()):
        kernel = functools.partial(finish_kernel, offsets, self.sizes[0], self.twisted, pieces, len(held))
        arrays = [array for d in offsets for array in (mine[d], others[d])]
        size = self.after(1)
        scratch = [((len(arrays), size, self.width), F32), pltpu.SemaphoreType.DMA((len(arrays), len(pieces)))]
        aliases = {1 + len(arrays) + i: i for i in range(len(held))}
        return call(
            kernel,
            outs,
            scratch,
            1,
            spot,
            *arrays,
            *held,
            work=1,
            vmem=40,
            hbm_in=len(held),
            hbm_out=len(outs),
            aliases=aliases,
        )


def call(kernel, outs, scratch, scalars, *arrays, work=0.5, vmem=0, hbm_in=0, hbm_out=0, aliases=None):
    plain = len(arrays) - scalars - hbm_in
    if not vmem:
        blocks = [(array.shape, array.dtype) for array in arrays[scalars:]] + outs
        blocks = blocks + [entry for entry in scratch if isinstance(entry, tuple)]
        vmem = max(16, sum(math.prod(shape) * jnp.dtype(kind).itemsize for shape, kind in blocks) // MIB + 7)
    specs = [pl.BlockSpec(memory_space=pltpu.SMEM)] * scalars
    specs = specs + [pl.BlockSpec(memory_space=pltpu.VMEM)] * plain
    specs = specs + [pl.BlockSpec(memory_space=pl.ANY)] * hbm_in
    out_specs = [pl.BlockSpec(memory_space=pltpu.VMEM)] * (len(outs) - hbm_out)
    out_specs = out_specs + [pl.BlockSpec(memory_space=pl.ANY)] * hbm_out
    return pl.pallas_call(
        kernel,
        out_shape=[jax.ShapeDtypeStruct(shape, kind) for shape, kind in outs],
        in_specs=specs,
        out_specs=out_specs,
        scratch_shapes=[pltpu.VMEM(*entry) if isinstance(entry, tuple) else entry for entry in scratch],
        input_output_aliases=aliases or {},
        compiler_params=pltpu.CompilerParams(vmem_limit_bytes=vmem * MIB),
        cost_estimate=pl.CostEstimate(flops=int(work * 1e9), bytes_accessed=int(work * 3e6), transcendentals=0),
    )(*arrays)


def middle(
    groups, first_sum, stats, spot, tgt_len, src_len, hidden_one, query, part, part_top, part_sum, wkv_cross,
    ln_gain, ln_bias, wo_cross, w_up, w_down, grad_out, pair_mine, came,
):
    rows, width = hidden_one.shape
    half, tiles = rows // 2, rows // TILE
    hidden_width = w_down.shape[0]
    count, places, _ = pair_mine.shape
    away = places // groups * (groups - 1)
    arrays = [spot, tgt_len, src_len, hidden_one, query, part, part_top, part_sum, wkv_cross, ln_gain, ln_bias]
    stay = [wo_cross, w_up, w_down, grad_out, pair_mine]

    def kernel(*refs):
        ins, refs = refs[: len(arrays)], refs[len(arrays) :]
        came_refs, refs = refs[: len(came)], refs[len(came) :]
        stay_refs, refs = refs[: len(stay)], refs[len(stay) :]
        outs, refs = refs[:9], refs[9:]
        middle_kernel(groups, *ins, *stay_refs, *came_refs, *outs[:3], *outs[6:8], *outs[3:6], outs[8], *refs)

    result_out, cross_norm, cross_along, grad_hidden_two, grad_attn, ln_part, keep_one, send_one, pair_all = call(
        kernel,
        [
            ((rows, width), BF16),
            (stats, F32),
            (stats, F32),
            ((rows, width), F32),
            ((rows, width), BF16),
            ((4, width), F32),
            ((first_sum.rows, width), BF16),
            ((first_sum.rows, width), BF16),
            ((count, places, 2 * width), BF16),
        ],
        [
            ((width, width), BF16),
            ((width, hidden_width), BF16),
            ((hidden_width, width), BF16),
            ((rows, width), BF16),
            ((count, away, 2 * width), BF16),
            ((2, first_sum.rows, width), BF16),
            ((count, away, 2 * TILE), F32),
            ((tiles, 2 * TILE, width), BF16),
            ((count, width, away), BF16),
            ((width, rows), F32),
            ((rows, hidden_width), BF16),
            ((rows, hidden_width), F32),
            ((rows, width), F32),
            pltpu.SemaphoreType.DMA((4,)),
            pltpu.SemaphoreType.DMA((count,)),
            pltpu.SemaphoreType.DMA((4,)),
        ],
        3,
        *arrays,
        *came,
        *stay,
        vmem=60,
        hbm_in=len(stay),
        hbm_out=3,
        aliases={len(arrays) + len(came) + len(stay) - 1: 8},
    )
    return result_out, cross_norm, cross_along, keep_one, send_one, grad_hidden_two, grad_attn, ln_part, pair_all


def body(
    target,
    memory,
    grad_out,
    tgt_len,
    src_len,
    w_qkv,
    w_out,
    wq_cross,
    wkv_cross,
    wo_cross,
    w_up,
    w_down,
    ln_gain,
    ln_bias,
):
    rows, width = target.shape
    half = rows // 2
    tiles = rows // TILE
    hidden_width = w_down.shape[0]
    groups = lax.axis_size("mem")
    me = lax.axis_index("mem")
    count = tgt_len.shape[1]
    span = memory.shape[1]
    places, away = groups * span, (groups - 1) * span
    dp = lax.axis_index("dp")
    short = width // 2
    first_sum = Summing(hidden_width + short, width, False)
    second_sum = Summing(3 * width + short, width, True)
    spot = first_sum.spot(me, dp)
    stats = (PAIRS * tiles, 2 * TILE)

    came = []
    for shift in range(1, groups):
        pairs = [(i, (i + shift) % groups) for i in range(groups)]
        sent = lax.dynamic_slice_in_dim(memory, ((me + shift) % groups) * count, count, 0)
        came.append(lax.ppermute(sent, "mem", pairs))

    sorted_rows, qkv, self_norm, self_attn_t, hidden_one, query, part, part_top, part_sum, pair_mine = call(
        functools.partial(self_forward_kernel, groups),
        [
            ((rows, width), BF16),
            ((rows, 3 * width), BF16),
            (stats, F32),
            ((width, rows), BF16),
            ((rows, width), F32),
            ((rows, width), BF16),
            ((width, rows), F32),
            (stats, F32),
            (stats, F32),
            ((count, places, 2 * width), BF16),
        ],
        [
            ((tiles, half, 2 * TILE), F32),
            ((count, span, 2 * TILE), F32),
            ((tiles, 2 * TILE, width), BF16),
            ((width, rows), BF16),
            ((count, width, span), BF16),
            ((count, span, 2 * width), BF16),
            pltpu.SemaphoreType.DMA((count,)),
        ],
        3,
        spot,
        tgt_len,
        src_len,
        target,
        w_qkv,
        w_out,
        wq_cross,
        ln_gain,
        ln_bias,
        memory,
        wkv_cross,
        vmem=60,
        hbm_out=1,
    )
    result_out, cross_norm, cross_along, keep_one, send_one, grad_hidden_two, grad_attn, ln_part, pair_all = middle(
        groups, first_sum, stats, spot, tgt_len, src_len, hidden_one, query, part, part_top, part_sum, wkv_cross,
        ln_gain, ln_bias, wo_cross, w_up, w_down, grad_out, pair_mine, came,
    )
    came_one = first_sum.core_swap(send_one)

    def cross_backward(block):
        sentences = 1 if block == 0 else count - 1
        return call(
            functools.partial(cross_backward_kernel, groups, block),
            [((sentences, places, 2 * width), BF16), ((width, half), BF16)],
            [
                ((sentences, places, 2 * width), BF16),
                ((sentences, places, 2 * TILE), F32),
                ((half // TILE, 2 * TILE, width), BF16),
                ((half // TILE, 2 * TILE, width), BF16),
                ((sentences, width, places), BF16),
                ((SLAB, half), F32),
                ((sentences, places, 2 * SLAB), F32),
                pltpu.SemaphoreType.DMA((1,)),
            ],
            3,
            spot,
            tgt_len,
            src_len,
            query,
            cross_norm,
            cross_along,
            grad_attn,
            pair_all,
            work=10,
            vmem=58 if block == 0 else 32,
            hbm_in=1,
        )

    pair_grad_long, query_grad_t_long = cross_backward(0)
    came_one, pair_grad_long = lax.optimization_barrier((came_one, pair_grad_long))
    parts_one = first_sum.first_split(spot, keep_one, came_one)
    parts_one, pair_all = lax.optimization_barrier((parts_one, pair_all))
    parts_one = first_sum.swap(parts_one, 0)
    pair_grad_rest, query_grad_t_rest = cross_backward(1)
    (wkv_grad,) = call(
        functools.partial(memory_weight_kernel, groups),
        [((2, width, width), BF16)],
        [((width, 2 * width), F32)],
        2,
        spot,
        tgt_len,
        pair_grad_long,
        pair_grad_rest,
        memory,
        *came,
        work=1,
        vmem=32,
    )
    parts_one, wkv_grad = lax.optimization_barrier((parts_one, wkv_grad))
    parts_one = first_sum.split(1, spot, parts_one)
    parts_one, wkv_grad = lax.optimization_barrier((parts_one, wkv_grad))
    parts_one = first_sum.swap(parts_one, 1)
    keep_mid, send_mid, grad_hidden_one, grad_self = call(
        first_norm_backward_kernel,
        [
            ((2 * width + LN_ROWS, width), BF16),
            ((2 * width + LN_ROWS, width), BF16),
            ((rows, width), F32),
            ((rows, width), BF16),
        ],
        [],
        1,
        spot,
        hidden_one,
        query_grad_t_long,
        query_grad_t_rest,
        grad_hidden_two,
        wq_cross,
        w_out,
        self_attn_t,
        ln_gain,
        ln_bias,
        ln_part,
        wkv_grad,
        work=10,
        vmem=24,
    )
    grad_triple, *last = call(
        self_backward_kernel,
        [((rows, 3 * width), BF16)] + [(((width + short) // LAST_PARTS, width), BF16)] * (2 * LAST_PARTS),
        [
            ((tiles, half, 2 * TILE), F32),
            ((tiles, 2 * TILE, width), BF16),
            ((tiles, 2 * TILE, width), BF16),
            ((width, rows), BF16),
            ((width, rows), BF16),
        ],
        2,
        spot,
        tgt_len,
        qkv,
        self_norm,
        grad_self,
        sorted_rows,
        work=0.1,
        vmem=28,
    )
    came_mid = second_sum.core_swap(send_mid)
    parts_one, last, came_mid, pair_grad_long = lax.optimization_barrier(
        (parts_one, last, came_mid, pair_grad_long)
    )
    keep_last = last[:LAST_PARTS]
    came_last = [second_sum.core_swap(part) for part in last[LAST_PARTS:]]
    parts_one = first_sum.split(2, spot, parts_one)

    def memory_grad(pieces, pair_grad_long):
        return call(
            functools.partial(memory_grad_kernel, pieces),
            [((count, size, width), BF16) for _, size in pieces],
            [],
            2,
            spot,
            tgt_len,
            pair_grad_long,
            pair_grad_rest,
            wkv_cross,
            work=0.01,
            vmem=32,
        )

    def send_back(grads):
        return [
            lax.ppermute(array, "mem", [(k, (k - 1 - i) % groups) for k in range(groups)])
            for i, array in enumerate(grads)
        ]

    parts_one, pair_grad_long = lax.optimization_barrier((parts_one, pair_grad_long))
    grad_late = memory_grad(
        [(part * span + span // 2, span // 2) for part in range(1, groups)], pair_grad_long
    )
    backs_late = send_back(grad_late)
    came_mid, grad_late = lax.optimization_barrier((came_mid, grad_late))
    parts_two = second_sum.first_split(
        spot, keep_mid, came_mid, *[part for both in zip(keep_last, came_last) for part in both]
    )
    parts_one = first_sum.swap(parts_one, 2)
    parts_two, pair_grad_long, grad_triple = lax.optimization_barrier((parts_two, pair_grad_long, grad_triple))
    parts_two = second_sum.swap(parts_two, 0)
    grad_mine, *grad_away = memory_grad(
        [(0, span)] + [(part * span, span // 2) for part in range(1, groups)], pair_grad_long
    )
    backs_late, grad_triple = lax.optimization_barrier((backs_late, grad_triple))
    (grad_target,) = call(
        target_kernel,
        [((rows, width), BF16)],
        [],
        2,
        spot,
        tgt_len,
        grad_triple,
        w_qkv,
        grad_hidden_one,
        work=8,
        vmem=16,
    )
    parts_one, parts_two, grad_away, grad_target = lax.optimization_barrier(
        (parts_one, parts_two, grad_away, grad_target)
    )
    backs_early = send_back(grad_away)
    parts_two = second_sum.swap(second_sum.split(1, spot, parts_two), 1)
    spread_one = first_sum.spread(2, first_sum.total(parts_one)[0])
    parts_two, spread_one, backs_early = lax.optimization_barrier((parts_two, spread_one, backs_early))
    spread_one = first_sum.spread(1, first_sum.join(2, spot, spread_one))
    parts_two = second_sum.swap(second_sum.split(2, spot, parts_two), 2)
    parts_two, spread_one = lax.optimization_barrier((parts_two, spread_one))
    spread_one = first_sum.spread(0, first_sum.join(1, spot, spread_one))
    sum_two, norm_sums = second_sum.total(parts_two)
    spread_two = second_sum.spread(2, sum_two)
    spread_two = second_sum.spread(1, second_sum.join(2, spot, spread_two))
    joined_two = second_sum.join(1, spot, spread_two)
    spread_one, joined_two = lax.optimization_barrier((spread_one, joined_two))
    other_one = [first_sum.core_swap(array) for array in spread_one]
    chunks = hidden_width // width
    pieces = []
    for chunk in range(chunks):
        side, here = chunk // (chunks // 2), chunk % (chunks // 2)
        pieces.append((side, here * width, width, 0, chunk * width, 0))
        pieces.append((side, (chunks // 2 + here) * width, width, 1, 0, chunk * width))
    for side in range(2):
        pieces.append((side, chunks * width, short, 2, side * short, 0))
    grad_w_down, grad_w_up, grad_wo = first_sum.finish(
        spot,
        spread_one,
        other_one,
        list(range(len(spread_one))),
        pieces,
        [((hidden_width, width), F32), ((width, hidden_width), F32), ((width, width), F32)],
    )
    spread_two = second_sum.spread(0, joined_two)
    pieces = [
        (0, 0, width, 0, 0, 0),
        (0, width, width, 1, 0, 0),
        (0, 2 * width, width, 2, 0, 0),
        (0, 3 * width, short, 2, 0, width),
        (1, 0, width, 1, 0, width),
        (1, width, width, 3, 0, 0),
        (1, 2 * width, short, 2, short, width),
        (1, 2 * width + short, width, 2, 0, 2 * width),
    ]
    outs = [
        ((width, width), F32),
        ((width, 2 * width), F32),
        ((width, 3 * width), F32),
        ((width, width), F32),
    ]
    other_two = [second_sum.core_swap(spread_two[0])]
    own_two, grad_w_down = lax.optimization_barrier((spread_two[0], grad_w_down))
    held = second_sum.finish(spot, [own_two], other_two, [0], pieces, outs)
    spread_two, held = lax.optimization_barrier((spread_two, held))
    other_two = other_two + [second_sum.core_swap(array) for array in spread_two[1:]]
    grad_wq, grad_wkv, grad_w_qkv, grad_w_out = second_sum.finish(
        spot, spread_two, other_two, list(range(1, len(spread_two))), pieces, outs, held
    )
    grad_memory = jnp.zeros(memory.shape, BF16)
    grad_memory = lax.dynamic_update_slice(grad_memory, grad_mine, (me * count, 0, 0))
    for part, backs in enumerate((backs_early, backs_late)):
        for i, grads in enumerate(backs):
            owner = (me + i + 1) % groups
            grad_memory = lax.dynamic_update_slice(grad_memory, grads, (owner * count, part * (span // 2), 0))
    return (
        result_out,
        grad_target,
        grad_memory,
        grad_w_qkv,
        grad_w_out,
        grad_wq,
        grad_wkv,
        grad_wo,
        grad_w_up,
        grad_w_down,
        norm_sums[:3],
        norm_sums[3:6],
    )


def solution(mesh):
    rows_spec = P(("dp", "mem"), None)
    memory_spec = P("dp", "mem", None)
    return jax.shard_map(
        body,
        mesh=mesh,
        in_specs=(rows_spec, memory_spec, rows_spec, P("dp", None), P("dp", None)) + (P(),) * 9,
        out_specs=(rows_spec, rows_spec, memory_spec) + (P(),) * 9,
        check_vma=False,
    )
```

```python
import functools
import math

import jax
import jax.numpy as jnp
from jax import lax
from jax.experimental import pallas as pl
from jax.experimental.pallas import tpu as pltpu
from jax.sharding import PartitionSpec as P

HEADS = 8
PAIRS = HEADS // 2
SLAB = 128
SIDE = SLAB // 2
TILE = 128
MASKED = -1e30
EPSILON = 1e-05
F32 = jnp.float32
BF16 = jnp.bfloat16
MIB = 1024 * 1024
LN_ROWS = 16
LAST_PARTS = 2


def dot(left, right):
    return jnp.dot(left, right, preferred_element_type=F32)


def dot_nt(left, right):
    return lax.dot_general(left, right, (((1,), (1,)), ((), ())), preferred_element_type=F32)


def dot_tn(left, right):
    return lax.dot_general(left, right, (((0,), (0,)), ((), ())), preferred_element_type=F32)


def iota(shape, axis):
    return lax.broadcasted_iota(jnp.int32, shape, axis)


def norm_parts(hidden):
    centre = hidden - jnp.mean(hidden, axis=-1, keepdims=True)
    inverse = lax.rsqrt(jnp.mean(centre * centre, axis=-1, keepdims=True) + EPSILON)
    return centre * inverse, inverse


def norm_backward(upstream, unit, inverse, gain_row):
    scaled = upstream * gain_row
    shifted = (
        scaled
        - jnp.mean(scaled, axis=-1, keepdims=True)
        - unit * jnp.mean(scaled * unit, axis=-1, keepdims=True)
    )
    gain_grad = jnp.sum(upstream * unit, axis=0, keepdims=True)
    return inverse * shifted, gain_grad, jnp.sum(upstream, axis=0, keepdims=True)


def sentence_order(me, len_ref):
    count = len_ref.shape[1]
    lengths = [len_ref[me, k] for k in range(count)]
    longest, best, start, running = jnp.int32(0), lengths[0], jnp.int32(0), jnp.int32(0)
    for k in range(1, count):
        running = running + lengths[k - 1]
        more = lengths[k] > best
        longest = jnp.where(more, k, longest)
        start = jnp.where(more, running, start)
        best = jnp.where(more, lengths[k], best)
    order = [longest] + [jnp.where(k < longest, k, k + 1) for k in range(count - 1)]
    bounds = [jnp.int32(0)]
    for k in range(1, count):
        bounds.append(bounds[-1] + len_ref[me, order[k]])
    return order, start, bounds


def moved_rows(index, start, half):
    return jnp.where(index < start, index + half, jnp.where(index < start + half, index - start, index))


def sort_matrix(rows, start):
    spot = moved_rows(iota((rows, rows), 1), start, rows // 2)
    return jnp.where(spot == iota((rows, rows), 0), 1.0, 0.0).astype(BF16)


def unsort_matrix(rows, start):
    spot = moved_rows(iota((rows, rows), 0), start, rows // 2)
    return jnp.where(spot == iota((rows, rows), 1), 1.0, 0.0).astype(BF16)


def side_masks(width):
    side = iota((1, width), 1) % SLAB
    first = jnp.where(side < SLAB // 2, 1.0, 0.0)
    return first.astype(BF16), (1.0 - first).astype(BF16)


def each_pair(step):
    def advance(pair, carry):
        step(pair)
        return carry

    lax.fori_loop(0, PAIRS, advance, 0)


def slab_of(pair, first=0):
    if isinstance(pair, int):
        return pl.ds(first + pair * SLAB, SLAB)
    return pl.ds(pl.multiple_of(first + pair * SLAB, SLAB), SLAB)


def pack_heads(out_ref, rows, width):
    even, odd = side_masks(width)
    for t in range(out_ref.shape[0]):
        tile = rows(t * TILE, TILE)
        out_ref[t, :TILE, :] = tile * even
        out_ref[t, TILE:, :] = tile * odd


def fill_self_bias(bias_ref, bounds, half):
    for t in range(bias_ref.shape[0]):
        block, inner = t // (half // TILE), t % (half // TILE)
        key = iota((half, 2 * TILE), 0)
        query = iota((half, 2 * TILE), 1) % TILE + inner * TILE
        allowed = key <= query
        if block == 1:
            first = jnp.zeros((half, 2 * TILE), jnp.int32)
            for bound in bounds[1:-1]:
                first = jnp.where(query >= bound, bound, first)
            allowed = allowed & (key >= first)
        bias_ref[t] = jnp.where(allowed, 0.0, MASKED)


def self_keys(t, half):
    per = half // TILE
    return (t // per) * half, (t % per + 1) * TILE


def fill_live_bias(bias_ref, me, groups, parts, span, src_ref, sentences):
    key = iota((span, bias_ref.shape[2]), 0)
    for j, sentence in enumerate(sentences):
        for i, part in enumerate(parts):
            place = lax.rem(me - part + groups, groups) * span + key
            live = place < src_ref[me, sentence]
            bias_ref[j, pl.ds(i * span, span), :] = jnp.where(live, 0.0, MASKED)


def cross_units(bounds, half):
    units = [(t, 0, None) for t in range(half // TILE)]
    middle = half // 2
    last = jnp.int32(1)
    for bound in bounds[1:-1]:
        last = last + jnp.where(bound < middle, 1, 0)
    ends = bounds[1:]
    column = iota((1, 2 * TILE), 1) % TILE
    for u in range(len(ends) + 1):
        early = u < last
        sentence = jnp.where(early, u + 1, u)
        tile = jnp.where(early, 0, 1)
        low, high = jnp.int32(0), ends[0]
        for k in range(1, len(ends)):
            low = jnp.where(sentence == k + 1, ends[k - 1], low)
            high = jnp.where(sentence == k + 1, ends[k], high)
        row = column + tile * TILE
        units.append((tile + half // TILE, sentence, (row >= low) & (row < high)))
    return units


def own_sides(both):
    return jnp.concatenate([both[:SIDE, :TILE], both[SIDE:, TILE:]], axis=0)


def side_rows(row):
    even = jnp.broadcast_to(row[:, :TILE], (SIDE, TILE))
    return jnp.concatenate([even, jnp.broadcast_to(row[:, TILE:], (SIDE, TILE))], axis=0)


def tile_columns(tile):
    if isinstance(tile, int):
        return pl.ds(tile * TILE, TILE)
    return pl.ds(pl.multiple_of(tile * TILE, TILE), TILE)


def self_forward_kernel(
    groups,
    me_ref,
    len_ref,
    src_ref,
    target_ref,
    w_qkv_ref,
    w_out_ref,
    wq_ref,
    gain_ref,
    bias_row_ref,
    memory_ref,
    wkv_ref,
    sorted_ref,
    qkv_ref,
    norm_ref,
    attn_t_ref,
    hidden_ref,
    query_ref,
    part_ref,
    top_ref,
    sum_ref,
    pair_out_ref,
    bias_ref,
    live_ref,
    q_pack_ref,
    value_t_ref,
    cross_value_t_ref,
    pair_ref,
    copy_sem,
):
    rows, width = target_ref.shape
    half = rows // 2
    me = me_ref[0]
    order, start, bounds = sentence_order(me, len_ref)
    count, span = pair_ref.shape[0], pair_ref.shape[1]
    copies = []
    for j in range(count):
        block = memory_ref[me * count + order[j]]
        pair_ref[j] = dot(block, wkv_ref[...]).astype(BF16)
        copy = pltpu.make_async_copy(
            pair_ref.at[j], pair_out_ref.at[j, pl.ds(0, span), :], copy_sem.at[j]
        )
        copy.start()
        copies.append(copy)
    sorted_rows = dot(sort_matrix(rows, start), target_ref[...]).astype(BF16)
    sorted_ref[...] = sorted_rows
    fill_self_bias(bias_ref, bounds, half)
    queries = (dot(sorted_rows, w_qkv_ref[:, :width]).astype(BF16) * 0.125).astype(BF16)
    qkv_ref[:, :width] = queries
    pack_heads(q_pack_ref, lambda first, size: queries[first : first + size], width)
    qkv_ref[:, width : 2 * width] = dot(sorted_rows, w_qkv_ref[:, width : 2 * width]).astype(BF16)
    values = dot(sorted_rows, w_qkv_ref[:, 2 * width :]).astype(BF16)
    qkv_ref[:, 2 * width :] = values
    value_t_ref[...] = values.T
    tiles = rows // TILE

    def self_step(pair):
        slab = slab_of(pair)
        for t in range(tiles):
            first, size = self_keys(t, half)
            keys = qkv_ref[pl.ds(first, size), slab_of(pair, width)]
            scores = dot_nt(keys, q_pack_ref[t, :, slab]) + bias_ref[t, :size, :]
            top = jnp.max(scores, axis=0, keepdims=True)
            weights = jnp.exp(scores - top)
            total = jnp.sum(weights, axis=0, keepdims=True)
            probs = (weights * (1.0 / total)).astype(BF16)
            both = dot(value_t_ref[slab, pl.ds(first, size)], probs)
            attn_t_ref[slab, tile_columns(t)] = own_sides(both).astype(BF16)
            norm_ref[pl.ds(pair * tiles + t, 1), :] = top + jnp.log(total)

    each_pair(self_step)
    hidden = sorted_rows.astype(F32) + dot(attn_t_ref[...].T, w_out_ref[...])
    hidden_ref[...] = hidden
    unit, _ = norm_parts(hidden)
    normed = (unit * gain_ref[0:1] + bias_row_ref[0:1]).astype(BF16)
    query_ref[...] = (dot(normed, wq_ref[...]).astype(BF16) * 0.125).astype(BF16)

    pack_heads(q_pack_ref, lambda first, size: query_ref[first : first + size, :], width)
    fill_live_bias(live_ref, me, groups, [0], span, src_ref, order)
    for j in range(count):
        cross_value_t_ref[j] = pair_ref[j, :, width:].T
    units = cross_units(bounds, half)

    def cross_step(pair):
        slab = slab_of(pair)
        for tile, sentence, columns in units:
            scores = dot_nt(pair_ref[sentence, :, slab], q_pack_ref[tile, :, slab]) + live_ref[sentence]
            top = jnp.max(scores, axis=0, keepdims=True)
            weights = jnp.exp(scores - top)
            total = jnp.sum(weights, axis=0, keepdims=True)
            result = own_sides(dot(cross_value_t_ref[sentence, slab, :], weights.astype(BF16)))
            here = tile_columns(tile)
            row = pl.ds(pair * tiles + tile, 1)
            if columns is not None:
                result = jnp.where(columns[:, :TILE], result, part_ref[slab, here])
                top = jnp.where(columns, top, top_ref[row, :])
                total = jnp.where(columns, total, sum_ref[row, :])
            part_ref[slab, here] = result
            top_ref[row, :] = top
            sum_ref[row, :] = total

    part_ref[...] = jnp.zeros_like(part_ref)
    top_ref[...] = jnp.zeros_like(top_ref)
    sum_ref[...] = jnp.ones_like(sum_ref)
    each_pair(cross_step)
    for copy in copies:
        copy.wait()


def middle_kernel(
    groups,
    me_ref,
    len_ref,
    src_ref,
    hidden_one_ref,
    query_ref,
    part_ref,
    top_ref,
    sum_ref,
    wkv_ref,
    gain_ref,
    bias_row_ref,
    wo_hbm,
    w_up_hbm,
    w_down_hbm,
    grad_out_hbm,
    pair_in_hbm,
    *refs,
):
    came_refs = refs[: groups - 1]
    (
        out_ref,
        norm_ref,
        along_ref,
        keep_hbm,
        send_hbm,
        grad_hidden_ref,
        grad_attn_ref,
        ln_ref,
        pair_hbm,
        wo_ref,
        w_up_ref,
        w_down_ref,
        grad_out_ref,
        pair_ref,
        halves_ref,
        live_ref,
        q_pack_ref,
        value_t_ref,
        attn_t_ref,
        active_ref,
        slope_ref,
        grad_upper_ref,
        load_sem,
        pair_sem,
        store_sem,
    ) = refs[groups - 1 :]
    rows, width = hidden_one_ref.shape
    half = rows // 2
    me = me_ref[0]
    count, away = pair_ref.shape[0], pair_ref.shape[1]
    span = away // (groups - 1)
    loads = [
        pltpu.make_async_copy(source, there, load_sem.at[i])
        for i, (source, there) in enumerate(
            [(wo_hbm, wo_ref), (w_up_hbm, w_up_ref), (w_down_hbm, w_down_ref), (grad_out_hbm, grad_out_ref)]
        )
    ]
    for copy in loads:
        copy.start()
    order, start, bounds = sentence_order(me, len_ref)
    fill_live_bias(live_ref, me, groups, list(range(1, groups)), span, src_ref, order)
    pack_heads(q_pack_ref, lambda first, size: query_ref[first : first + size, :], width)
    pair_copies = []
    for j in range(count):
        for part in range(1, groups):
            block = came_refs[part - 1][order[j]]
            pair_ref[j, pl.ds((part - 1) * span, span), :] = dot(block, wkv_ref[...]).astype(BF16)
        value_t_ref[j] = pair_ref[j, :, width:].T
        copy = pltpu.make_async_copy(pair_ref.at[j], pair_hbm.at[j, pl.ds(span, away), :], pair_sem.at[j])
        copy.start()
        pair_copies.append(copy)
    units = cross_units(bounds, half)
    tiles = rows // TILE

    def cross_step(pair):
        slab = slab_of(pair)
        for tile, sentence, columns in units:
            here = tile_columns(tile)
            row = pl.ds(pair * tiles + tile, 1)
            scores = dot_nt(pair_ref[sentence, :, slab], q_pack_ref[tile, :, slab]) + live_ref[sentence]
            before = top_ref[row, :]
            top = jnp.maximum(jnp.max(scores, axis=0, keepdims=True), before)
            weights = jnp.exp(scores - top)
            scale = jnp.exp(before - top)
            total = jnp.sum(weights, axis=0, keepdims=True) + sum_ref[row, :] * scale
            result = own_sides(dot(value_t_ref[sentence, slab, :], weights.astype(BF16)))
            result = (result + part_ref[slab, here] * side_rows(scale)) * side_rows(1.0 / total)
            norm = top + jnp.log(total)
            if columns is not None:
                result = jnp.where(columns[:, :TILE], result, attn_t_ref[slab, here])
                norm = jnp.where(columns, norm, norm_ref[row, :])
            attn_t_ref[slab, here] = result
            norm_ref[row, :] = norm

    attn_t_ref[...] = jnp.zeros_like(attn_t_ref)
    norm_ref[...] = jnp.zeros_like(norm_ref)
    each_pair(cross_step)
    attn_t_low = attn_t_ref[...].astype(BF16)
    loads[0].wait()
    unit_one, _ = norm_parts(hidden_one_ref[...])
    normed_one = unit_one * gain_ref[0:1] + bias_row_ref[0:1]
    hidden_two = normed_one + dot(attn_t_low.T, wo_ref[...])
    unit_two, inverse_two = norm_parts(hidden_two)
    normed_two = unit_two * gain_ref[1:2] + bias_row_ref[1:2]
    normed_two_low = normed_two.astype(BF16)
    chunk = width
    chunks = w_down_ref.shape[0] // chunk
    loads[1].wait()
    loads[2].wait()

    def up_step(c, carry):
        cols = pl.ds(pl.multiple_of(c * chunk, chunk), chunk)
        upper = dot(normed_two_low, w_up_ref[:, cols])
        sigma = 0.5 * jnp.tanh(0.5 * upper) + 0.5
        active = (upper * sigma).astype(BF16)
        active_ref[:, cols] = active
        slope_ref[:, cols] = sigma * (1.0 + upper * (1.0 - sigma))
        return carry

    lax.fori_loop(0, chunks, up_step, 0)

    unit_three, inverse_three = norm_parts(normed_two + dot(active_ref[...], w_down_ref[...]))
    result = (unit_three * gain_ref[2:3] + bias_row_ref[2:3]).astype(BF16)
    out_ref[...] = dot(unsort_matrix(rows, start), result).astype(BF16)
    loads[3].wait()
    upstream = dot(sort_matrix(rows, start), grad_out_ref[...])
    grad_three, gain_three, bias_three = norm_backward(upstream, unit_three, inverse_three, gain_ref[2:3])
    grad_down = grad_three.astype(BF16)
    normed_two_t = normed_two_low.T

    def down_step(c, carry):
        cols = pl.ds(pl.multiple_of(c * chunk, chunk), chunk)
        grad_upper = (dot_nt(grad_down, w_down_ref[cols, :]) * slope_ref[:, cols]).astype(BF16)
        down_part = dot_tn(active_ref[:, cols], grad_down).astype(BF16)
        up_part = dot(normed_two_t, grad_upper).astype(BF16)
        half_index, here = c // (chunks // 2), lax.rem(c, chunks // 2)
        down_rows = pl.ds(pl.multiple_of(here * chunk, chunk), chunk)
        up_rows = pl.ds(pl.multiple_of((chunks // 2 + here) * chunk, chunk), chunk)
        halves_ref[half_index, down_rows, :] = down_part
        halves_ref[half_index, up_rows, :] = up_part
        grad_upper_ref[:, cols] = grad_upper
        return carry

    lax.fori_loop(0, chunks, down_step, 0)

    most = chunks * chunk
    core = me_ref[1]
    stores = [
        pltpu.make_async_copy(
            halves_ref.at[half_index, pl.ds(first, size)], there.at[pl.ds(first, size)], store_sem.at[i]
        )
        for i, (half_index, there, first, size) in enumerate(
            [
                (1 - core, send_hbm, 0, most),
                (core, keep_hbm, 0, most),
                (1 - core, send_hbm, most, halves_ref.shape[1] - most),
                (core, keep_hbm, most, halves_ref.shape[1] - most),
            ]
        )
    ]
    stores[0].start()
    stores[1].start()
    upstream_two = grad_three + dot_nt(grad_upper_ref[...], w_up_ref[...])
    grad_two, gain_two, bias_two = norm_backward(upstream_two, unit_two, inverse_two, gain_ref[1:2])
    grad_two_low = grad_two.astype(BF16)
    wo_grad = dot(attn_t_low, grad_two_low).astype(BF16)
    used = most + width // 2
    for half_index in range(2):
        piece = wo_grad[half_index * (width // 2) : (half_index + 1) * (width // 2)]
        halves_ref[half_index, pl.ds(most, width // 2), :] = piece
        if halves_ref.shape[1] > used:
            halves_ref[half_index, used:, :] = jnp.zeros((halves_ref.shape[1] - used, width), BF16)
    stores[2].start()
    stores[3].start()
    grad_hidden_ref[...] = grad_two
    grad_attn = dot_nt(grad_two_low, wo_ref[...]).astype(BF16)
    grad_attn_ref[...] = grad_attn
    product = grad_attn.T.astype(F32) * attn_t_ref[...]
    for pair in range(PAIRS):
        for side in range(2):
            first = pair * SLAB + side * SIDE
            along = jnp.sum(product[first : first + SIDE], axis=0, keepdims=True)
            for t in range(tiles):
                along_ref[pair * tiles + t : pair * tiles + t + 1, side * TILE : (side + 1) * TILE] = along[
                    :, t * TILE : (t + 1) * TILE
                ]
    ln_ref[...] = jnp.concatenate([gain_two, gain_three, bias_two, bias_three], axis=0)
    for copy in pair_copies + stores:
        copy.wait()


def cross_backward_kernel(
    groups,
    block,
    me_ref,
    len_ref,
    src_ref,
    query_ref,
    norm_ref,
    along_ref,
    grad_attn_ref,
    pair_hbm,
    pair_grad_ref,
    query_grad_t_ref,
    pair_ref,
    live_ref,
    q_pack_ref,
    g_pack_ref,
    key_t_ref,
    query_sum_ref,
    sum_ref,
    load_sem,
):
    rows, width = query_ref.shape
    half = rows // 2
    me = me_ref[0]
    sentences, places = pair_ref.shape[0], pair_ref.shape[1]
    first_sentence = 0 if block == 0 else 1
    load = pltpu.make_async_copy(pair_hbm.at[pl.ds(first_sentence, sentences)], pair_ref, load_sem.at[0])
    load.start()
    order, start, bounds = sentence_order(me, len_ref)
    mine = order[:1] if block == 0 else order[1:]
    fill_live_bias(live_ref, me, groups, list(range(groups)), places // groups, src_ref, mine)
    low = block * half
    pack_heads(q_pack_ref, lambda first, size: query_ref[low + first : low + first + size, :], width)
    pack_heads(g_pack_ref, lambda first, size: grad_attn_ref[low + first : low + first + size, :], width)
    tiles, per = rows // TILE, half // TILE
    units = cross_units(bounds, half)
    units = units[:per] if block == 0 else units[per:]
    load.wait()
    for j in range(sentences):
        key_t_ref[j] = pair_ref[j, :, :width].T

    def pair_step(pair):
        slab, value_slab = slab_of(pair), slab_of(pair, width)
        query_sum_ref[...] = jnp.zeros_like(query_sum_ref)
        sum_ref[...] = jnp.zeros_like(sum_ref)
        for tile, sentence, columns in units:
            j = sentence - first_sentence
            t = tile - block * per
            here = tile_columns(t)
            row = pl.ds(pair * tiles + tile, 1)
            q_rows, g_rows = q_pack_ref[t, :, slab], g_pack_ref[t, :, slab]
            norm = norm_ref[row, :]
            if columns is not None:
                norm = jnp.where(columns, norm, -MASKED)
            scores = dot_nt(pair_ref[j, :, slab], q_rows) + live_ref[j]
            probs = jnp.exp(scores - norm)
            grad_probs = dot_nt(pair_ref[j, :, value_slab], g_rows)
            grad_scores = (probs * (grad_probs - along_ref[row, :])).astype(BF16)
            sum_ref[j, :, :SLAB] += dot(grad_scores, q_rows)
            sum_ref[j, :, SLAB:] += dot(probs.astype(BF16), g_rows)
            query_sum_ref[:, here] += own_sides(dot(key_t_ref[j, slab, :], grad_scores))
        query_grad_t_ref[slab, :] = (query_sum_ref[...] * 0.125).astype(BF16)
        pair_grad_ref[:, :, slab] = sum_ref[:, :, :SLAB].astype(BF16)
        pair_grad_ref[:, :, value_slab] = sum_ref[:, :, SLAB:].astype(BF16)

    for pair in range(PAIRS):
        pair_step(pair)


def memory_weight_kernel(groups, me_ref, len_ref, pair_grad_long_ref, pair_grad_rest_ref, memory_ref, *refs):
    came_refs = refs[: groups - 1]
    wkv_grad_ref, total_ref = refs[groups - 1 :]
    width = memory_ref.shape[2]
    me = me_ref[0]
    count = len_ref.shape[1]
    span = pair_grad_long_ref.shape[1] // groups
    order, _, _ = sentence_order(me, len_ref)
    for j in range(count):
        pair_grad_ref, here = (pair_grad_long_ref, 0) if j == 0 else (pair_grad_rest_ref, j - 1)
        blocks = [memory_ref[me * count + order[j]]] + [ref[order[j]] for ref in came_refs]
        term = dot_tn(jnp.concatenate(blocks, axis=0), pair_grad_ref[here])
        if j == 0:
            total_ref[...] = term
        else:
            total_ref[...] += term
    wkv_grad_ref[0] = total_ref[:, :width].astype(BF16)
    wkv_grad_ref[1] = total_ref[:, width:].astype(BF16)


def memory_grad_kernel(pieces, me_ref, len_ref, pair_grad_long_ref, pair_grad_rest_ref, wkv_ref, *outs):
    count = len_ref.shape[1]
    order, _, _ = sentence_order(me_ref[0], len_ref)
    for j in range(count):
        pair_grad_ref, here = (pair_grad_long_ref, 0) if j == 0 else (pair_grad_rest_ref, j - 1)
        for (first, size), out in zip(pieces, outs):
            out[order[j]] = dot_nt(pair_grad_ref[here, pl.ds(first, size), :], wkv_ref[...]).astype(BF16)


def first_norm_backward_kernel(
    me_ref,
    hidden_one_ref,
    query_grad_t_long_ref,
    query_grad_t_rest_ref,
    grad_hidden_two_ref,
    wq_ref,
    w_out_ref,
    self_attn_t_ref,
    gain_ref,
    bias_row_ref,
    ln_in_ref,
    wkv_grad_ref,
    keep_ref,
    send_ref,
    grad_hidden_ref,
    grad_self_ref,
):
    width = wq_ref.shape[0]
    unit_one, inverse_one = norm_parts(hidden_one_ref[...])
    normed_one = (unit_one * gain_ref[0:1] + bias_row_ref[0:1]).astype(BF16)
    query_grad = jnp.concatenate([query_grad_t_long_ref[...].T, query_grad_t_rest_ref[...].T], axis=0)
    upstream = grad_hidden_two_ref[...] + dot_nt(query_grad, wq_ref[...])
    grad_one, gain_one, bias_one = norm_backward(upstream, unit_one, inverse_one, gain_ref[0:1])
    grad_hidden_ref[...] = grad_one
    grad_one_low = grad_one.astype(BF16)
    grad_self_ref[...] = dot_nt(grad_one_low, w_out_ref[...]).astype(BF16)
    wq_grad = dot_tn(normed_one, query_grad).astype(BF16)
    w_out_grad = dot(self_attn_t_ref[...], grad_one_low).astype(BF16)
    norms = jnp.concatenate(
        [gain_one, ln_in_ref[0:2], bias_one, ln_in_ref[2:4], jnp.zeros((LN_ROWS - 6, width), F32)], axis=0
    ).astype(BF16)

    def halves(low_ref, high_ref):
        low_ref[:width, :] = wq_grad
        low_ref[width : 2 * width, :] = wkv_grad_ref[0]
        high_ref[:width, :] = wkv_grad_ref[1]
        high_ref[width : 2 * width, :] = w_out_grad

    @pl.when(me_ref[1] == 0)
    def _():
        halves(keep_ref, send_ref)

    @pl.when(me_ref[1] != 0)
    def _():
        halves(send_ref, keep_ref)

    keep_ref[2 * width :, :] = norms
    send_ref[2 * width :, :] = norms


def self_backward_kernel(
    me_ref,
    len_ref,
    qkv_ref,
    norm_ref,
    grad_attn_ref,
    sorted_ref,
    grad_triple_ref,
    *refs,
):
    keep_refs, send_refs = refs[:LAST_PARTS], refs[LAST_PARTS : 2 * LAST_PARTS]
    self_backward(
        me_ref,
        len_ref,
        qkv_ref,
        norm_ref,
        grad_attn_ref,
        sorted_ref,
        grad_triple_ref,
        keep_refs,
        send_refs,
        *refs[2 * LAST_PARTS :],
    )


def self_backward(
    me_ref,
    len_ref,
    qkv_ref,
    norm_ref,
    grad_attn_ref,
    sorted_ref,
    grad_triple_ref,
    keep_refs,
    send_refs,
    bias_ref,
    q_pack_ref,
    g_pack_ref,
    key_t_ref,
    query_grad_t_ref,
):
    rows, width = sorted_ref.shape
    half = rows // 2
    _, _, bounds = sentence_order(me_ref[0], len_ref)
    fill_self_bias(bias_ref, bounds, half)
    pack_heads(q_pack_ref, lambda first, size: qkv_ref[first : first + size, :width], width)
    pack_heads(g_pack_ref, lambda first, size: grad_attn_ref[first : first + size, :], width)
    key_t_ref[...] = qkv_ref[:, width : 2 * width].T
    tiles, per = rows // TILE, half // TILE

    def pair_step(pair):
        slab, key_slab, value_slab = slab_of(pair), slab_of(pair, width), slab_of(pair, 2 * width)
        sums = [[None, None] for _ in range(tiles)]
        for t in range(tiles):
            first, size = self_keys(t, half)
            span = pl.ds(first, size)
            q_rows, g_rows = q_pack_ref[t, :, slab], g_pack_ref[t, :, slab]
            scores = dot_nt(qkv_ref[span, key_slab], q_rows) + bias_ref[t, :size, :]
            probs = jnp.exp(scores - norm_ref[pl.ds(pair * tiles + t, 1), :])
            grad_probs = dot_nt(qkv_ref[span, value_slab], g_rows)
            along = jnp.sum(probs * grad_probs, axis=0, keepdims=True)
            grad_scores = (probs * (grad_probs - along)).astype(BF16)
            parts = dot(grad_scores, q_rows), dot(probs.astype(BF16), g_rows)
            for i in range(size // TILE):
                spot = sums[first // TILE + i]
                for k in range(2):
                    piece = parts[k][i * TILE : (i + 1) * TILE]
                    spot[k] = piece if spot[k] is None else spot[k] + piece
            query_grad_t_ref[slab, tile_columns(t)] = (
                own_sides(dot(key_t_ref[slab, span], grad_scores)) * 0.125
            ).astype(BF16)
        for t in range(tiles):
            grad_triple_ref[pl.ds(t * TILE, TILE), key_slab] = sums[t][0].astype(BF16)
            grad_triple_ref[pl.ds(t * TILE, TILE), value_slab] = sums[t][1].astype(BF16)

    for pair in range(PAIRS):
        pair_step(pair)
    grad_triple_ref[:, :width] = query_grad_t_ref[...].T
    sorted_t = sorted_ref[...].T
    grads = [
        dot(sorted_t, grad_triple_ref[:, part * width : (part + 1) * width]).astype(BF16)
        for part in range(3)
    ]
    short = width // 2

    low = jnp.concatenate([grads[0], grads[1][:short]], axis=0)
    high = jnp.concatenate([grads[1][short:], grads[2]], axis=0)
    size = keep_refs[0].shape[0]

    def halves(low_refs, high_refs):
        for i in range(LAST_PARTS):
            low_refs[i][...] = low[i * size : (i + 1) * size]
            high_refs[i][...] = high[i * size : (i + 1) * size]

    @pl.when(me_ref[1] == 0)
    def _():
        halves(keep_refs, send_refs)

    @pl.when(me_ref[1] != 0)
    def _():
        halves(send_refs, keep_refs)


def target_kernel(me_ref, len_ref, grad_triple_ref, w_qkv_ref, grad_hidden_ref, grad_target_ref):
    rows = grad_hidden_ref.shape[0]
    _, start, _ = sentence_order(me_ref[0], len_ref)
    result = grad_hidden_ref[...] + dot_nt(grad_triple_ref[...], w_qkv_ref[...])
    grad_target_ref[...] = dot(unsort_matrix(rows, start), result.astype(BF16)).astype(BF16)


def tree_sum(terms):
    while len(terms) > 1:
        terms = [terms[i] + terms[i + 1] for i in range(0, len(terms), 2)]
    return terms[0]


def rows_of(ref, first, count):
    return ref[pl.ds(pl.multiple_of(first, 16), count), :].astype(F32)


def first_split_kernel(segments, ln, peers, spot_ref, *refs):
    ins, outs, sum_ref = refs[: 2 * segments], refs[2 * segments : -1], refs[-1]
    extra = LN_ROWS if ln else 0
    size = outs[0].shape[0] - extra
    used = 0
    for i in range(segments):
        keep_ref, came_ref = ins[2 * i], ins[2 * i + 1]
        count = keep_ref.shape[0] - (extra if i == 0 else 0)
        sum_ref[used : used + count, :] = (rows_of(keep_ref, 0, count) + rows_of(came_ref, 0, count)).astype(BF16)
        if i == 0 and ln:
            tail = (rows_of(keep_ref, count, LN_ROWS) + rows_of(came_ref, count, LN_ROWS)).astype(BF16)
        used += count
    if sum_ref.shape[0] > used:
        sum_ref[used:, :] = jnp.zeros((sum_ref.shape[0] - used, sum_ref.shape[1]), BF16)
    for d, out in enumerate(outs):
        out[:size, :] = sum_ref[pl.ds(pl.multiple_of((spot_ref[2] ^ d) * size, 16), size), :]
        if ln:
            out[size:, :] = tail


def split_kernel(stage, ln, peers, spot_ref, *refs):
    ins, outs = refs[:peers], refs[peers:]
    extra = LN_ROWS if ln else 0
    size = outs[0].shape[0] - extra
    if ln:
        tail = tree_sum([rows_of(ref, size * len(outs), LN_ROWS) for ref in ins]).astype(BF16)
    for d, out in enumerate(outs):
        first = (spot_ref[2 + stage] ^ d) * size
        out[:size, :] = tree_sum([rows_of(ref, first, size) for ref in ins]).astype(BF16)
        if ln:
            out[size:, :] = tail


def total_kernel(ln, count, *refs):
    ins, outs = refs[:count], refs[count:]
    size = outs[0].shape[0]
    outs[0][...] = tree_sum([rows_of(ref, 0, size) for ref in ins]).astype(BF16)
    if ln:
        outs[1][...] = tree_sum([rows_of(ref, size, LN_ROWS) for ref in ins])


def join_kernel(stage, spot_ref, *refs):
    out_ref = refs[-1]
    for d, ref in enumerate(refs[:-1]):
        size = ref.shape[0]
        out_ref[pl.ds(pl.multiple_of((spot_ref[2 + stage] ^ d) * size, 16), size), :] = ref[...]


def finish_kernel(offsets, peers, twisted, pieces, held, spot_ref, *refs):
    arrays, refs = refs[: 2 * len(offsets)], refs[2 * len(offsets) + held :]
    outs, (wide_ref, sem) = refs[:-2], refs[-2:]
    core = spot_ref[1]
    size, width = wide_ref.shape[1:]
    copies = []
    for k, ref in enumerate(arrays):
        wide_ref[k] = ref[...].astype(F32)
        d, other = offsets[k // 2], k % 2
        half = 1 - core if other else core
        place = spot_ref[3 if twisted and other else 2] ^ d
        for i in range(2):
            for j in range(peers):
                cut = []
                for piece_half, first, rows, out, row, col in pieces:
                    low, high = max(first, j * size), min(first + rows, (j + 1) * size)
                    if piece_half == i and low < high:
                        there = outs[out].at[pl.ds(row + low - first, high - low), pl.ds(col, width)]
                        here = wide_ref.at[k, pl.ds(low - j * size, high - low), :]
                        cut.append(pltpu.make_async_copy(here, there, sem.at[k, len(cut)]))
                copies.append(((half == i) & (place == j), cut))
                _start_all(*copies[-1])
    for chosen, cut in copies:
        _wait_all(chosen, cut)


def _start_all(chosen, cut):
    @pl.when(chosen)
    def _():
        for copy in cut:
            copy.start()


def _wait_all(chosen, cut):
    @pl.when(chosen)
    def _():
        for copy in cut:
            copy.wait()


class Summing:
    def __init__(self, rows, width, ln):
        self.width, self.ln = width, ln
        self.dp, self.mem = lax.axis_size("dp"), lax.axis_size("mem")
        z_size = 4
        x_size = self.dp // (2 * z_size)
        self.sizes = (x_size, self.mem, z_size)
        self.twisted = x_size == self.mem
        self.chunk = -(-rows // (16 * math.prod(self.sizes))) * 16
        self.rows = self.chunk * math.prod(self.sizes)

    def after(self, stage):
        return self.rows // math.prod(self.sizes[:stage])

    def axis(self, stage, core):
        return 1 - stage if self.twisted and core == 1 and stage < 2 else stage

    def coords(self, dp, mem):
        return [dp // 2 % self.sizes[0], mem, dp // (2 * self.sizes[0])], dp % 2

    def spot(self, me, dp):
        (x, mem, z), core = self.coords(dp, me)
        if self.twisted:
            x, mem = jnp.where(core == 0, x, mem), jnp.where(core == 0, mem, x)
        return jnp.stack([me, core, x, mem, z]).astype(jnp.int32)

    def permute(self, array, stage, offset):
        pairs = []
        for dp in range(self.dp):
            for mem in range(self.mem):
                spots, core = self.coords(dp, mem)
                if stage is None:
                    core ^= offset
                else:
                    spots[self.axis(stage, core)] ^= offset
                to_dp = (spots[2] * self.sizes[0] + spots[0]) * 2 + core
                pairs.append((dp * self.mem + mem, to_dp * self.mem + spots[1]))
        return lax.ppermute(array, ("dp", "mem"), pairs)

    def core_swap(self, send):
        return self.permute(send, None, 1)

    def swap(self, arrays, stage):
        return [arrays[0]] + [self.permute(array, stage, d) for d, array in enumerate(arrays) if d > 0]

    def spread(self, stage, array):
        return [array] + [self.permute(array, stage, d) for d in range(1, self.sizes[stage])]

    def messages(self, stage):
        size = self.after(stage + 1) + (LN_ROWS if self.ln else 0)
        return [((size, self.width), BF16)] * self.sizes[stage]

    def first_split(self, spot, *arrays):
        kernel = functools.partial(first_split_kernel, len(arrays) // 2, self.ln, self.sizes[0])
        return call(kernel, self.messages(0), [((self.rows, self.width), BF16)], 1, spot, *arrays, work=0.01)

    def split(self, stage, spot, arrays):
        kernel = functools.partial(split_kernel, stage, self.ln, self.sizes[stage - 1])
        return call(kernel, self.messages(stage), [], 1, spot, *arrays, work=0.01)

    def total(self, arrays):
        outs = [((self.chunk, self.width), BF16)]
        if self.ln:
            outs.append(((LN_ROWS, self.width), F32))
        return call(functools.partial(total_kernel, self.ln, self.sizes[2]), outs, [], 0, *arrays, work=0.01)

    def join(self, stage, spot, arrays):
        outs = [((self.after(stage), self.width), BF16)]
        return call(functools.partial(join_kernel, stage), outs, [], 1, spot, *arrays, work=0.01)[0]

    def finish(self, spot, mine, others, offsets, pieces, outs, held=()):
        kernel = functools.partial(finish_kernel, offsets, self.sizes[0], self.twisted, pieces, len(held))
        arrays = [array for d in offsets for array in (mine[d], others[d])]
        size = self.after(1)
        scratch = [((len(arrays), size, self.width), F32), pltpu.SemaphoreType.DMA((len(arrays), len(pieces)))]
        aliases = {1 + len(arrays) + i: i for i in range(len(held))}
        return call(
            kernel,
            outs,
            scratch,
            1,
            spot,
            *arrays,
            *held,
            work=1,
            vmem=40,
            hbm_in=len(held),
            hbm_out=len(outs),
            aliases=aliases,
        )


def call(kernel, outs, scratch, scalars, *arrays, work=0.5, vmem=0, hbm_in=0, hbm_out=0, aliases=None):
    plain = len(arrays) - scalars - hbm_in
    if not vmem:
        blocks = [(array.shape, array.dtype) for array in arrays[scalars:]] + outs
        blocks = blocks + [entry for entry in scratch if isinstance(entry, tuple)]
        vmem = max(16, sum(math.prod(shape) * jnp.dtype(kind).itemsize for shape, kind in blocks) // MIB + 7)
    specs = [pl.BlockSpec(memory_space=pltpu.SMEM)] * scalars
    specs = specs + [pl.BlockSpec(memory_space=pltpu.VMEM)] * plain
    specs = specs + [pl.BlockSpec(memory_space=pl.ANY)] * hbm_in
    out_specs = [pl.BlockSpec(memory_space=pltpu.VMEM)] * (len(outs) - hbm_out)
    out_specs = out_specs + [pl.BlockSpec(memory_space=pl.ANY)] * hbm_out
    return pl.pallas_call(
        kernel,
        out_shape=[jax.ShapeDtypeStruct(shape, kind) for shape, kind in outs],
        in_specs=specs,
        out_specs=out_specs,
        scratch_shapes=[pltpu.VMEM(*entry) if isinstance(entry, tuple) else entry for entry in scratch],
        input_output_aliases=aliases or {},
        compiler_params=pltpu.CompilerParams(vmem_limit_bytes=vmem * MIB),
        cost_estimate=pl.CostEstimate(flops=int(work * 1e9), bytes_accessed=int(work * 3e6), transcendentals=0),
    )(*arrays)


def middle(
    groups, first_sum, stats, spot, tgt_len, src_len, hidden_one, query, part, part_top, part_sum, wkv_cross,
    ln_gain, ln_bias, wo_cross, w_up, w_down, grad_out, pair_mine, came,
):
    rows, width = hidden_one.shape
    half, tiles = rows // 2, rows // TILE
    hidden_width = w_down.shape[0]
    count, places, _ = pair_mine.shape
    away = places // groups * (groups - 1)
    arrays = [spot, tgt_len, src_len, hidden_one, query, part, part_top, part_sum, wkv_cross, ln_gain, ln_bias]
    stay = [wo_cross, w_up, w_down, grad_out, pair_mine]

    def kernel(*refs):
        ins, refs = refs[: len(arrays)], refs[len(arrays) :]
        came_refs, refs = refs[: len(came)], refs[len(came) :]
        stay_refs, refs = refs[: len(stay)], refs[len(stay) :]
        outs, refs = refs[:9], refs[9:]
        middle_kernel(groups, *ins, *stay_refs, *came_refs, *outs[:3], *outs[6:8], *outs[3:6], outs[8], *refs)

    result_out, cross_norm, cross_along, grad_hidden_two, grad_attn, ln_part, keep_one, send_one, pair_all = call(
        kernel,
        [
            ((rows, width), BF16),
            (stats, F32),
            (stats, F32),
            ((rows, width), F32),
            ((rows, width), BF16),
            ((4, width), F32),
            ((first_sum.rows, width), BF16),
            ((first_sum.rows, width), BF16),
            ((count, places, 2 * width), BF16),
        ],
        [
            ((width, width), BF16),
            ((width, hidden_width), BF16),
            ((hidden_width, width), BF16),
            ((rows, width), BF16),
            ((count, away, 2 * width), BF16),
            ((2, first_sum.rows, width), BF16),
            ((count, away, 2 * TILE), F32),
            ((tiles, 2 * TILE, width), BF16),
            ((count, width, away), BF16),
            ((width, rows), F32),
            ((rows, hidden_width), BF16),
            ((rows, hidden_width), F32),
            ((rows, hidden_width), BF16),
            pltpu.SemaphoreType.DMA((4,)),
            pltpu.SemaphoreType.DMA((count,)),
            pltpu.SemaphoreType.DMA((4,)),
        ],
        3,
        *arrays,
        *came,
        *stay,
        vmem=60,
        hbm_in=len(stay),
        hbm_out=3,
        aliases={len(arrays) + len(came) + len(stay) - 1: 8},
    )
    return result_out, cross_norm, cross_along, keep_one, send_one, grad_hidden_two, grad_attn, ln_part, pair_all


def body(
    target,
    memory,
    grad_out,
    tgt_len,
    src_len,
    w_qkv,
    w_out,
    wq_cross,
    wkv_cross,
    wo_cross,
    w_up,
    w_down,
    ln_gain,
    ln_bias,
):
    rows, width = target.shape
    half = rows // 2
    tiles = rows // TILE
    hidden_width = w_down.shape[0]
    groups = lax.axis_size("mem")
    me = lax.axis_index("mem")
    count = tgt_len.shape[1]
    span = memory.shape[1]
    places, away = groups * span, (groups - 1) * span
    dp = lax.axis_index("dp")
    short = width // 2
    first_sum = Summing(hidden_width + short, width, False)
    second_sum = Summing(3 * width + short, width, True)
    spot = first_sum.spot(me, dp)
    stats = (PAIRS * tiles, 2 * TILE)

    came = []
    for shift in range(1, groups):
        pairs = [(i, (i + shift) % groups) for i in range(groups)]
        sent = lax.dynamic_slice_in_dim(memory, ((me + shift) % groups) * count, count, 0)
        came.append(lax.ppermute(sent, "mem", pairs))

    sorted_rows, qkv, self_norm, self_attn_t, hidden_one, query, part, part_top, part_sum, pair_mine = call(
        functools.partial(self_forward_kernel, groups),
        [
            ((rows, width), BF16),
            ((rows, 3 * width), BF16),
            (stats, F32),
            ((width, rows), BF16),
            ((rows, width), F32),
            ((rows, width), BF16),
            ((width, rows), F32),
            (stats, F32),
            (stats, F32),
            ((count, places, 2 * width), BF16),
        ],
        [
            ((tiles, half, 2 * TILE), F32),
            ((count, span, 2 * TILE), F32),
            ((tiles, 2 * TILE, width), BF16),
            ((width, rows), BF16),
            ((count, width, span), BF16),
            ((count, span, 2 * width), BF16),
            pltpu.SemaphoreType.DMA((count,)),
        ],
        3,
        spot,
        tgt_len,
        src_len,
        target,
        w_qkv,
        w_out,
        wq_cross,
        ln_gain,
        ln_bias,
        memory,
        wkv_cross,
        vmem=60,
        hbm_out=1,
    )
    result_out, cross_norm, cross_along, keep_one, send_one, grad_hidden_two, grad_attn, ln_part, pair_all = middle(
        groups, first_sum, stats, spot, tgt_len, src_len, hidden_one, query, part, part_top, part_sum, wkv_cross,
        ln_gain, ln_bias, wo_cross, w_up, w_down, grad_out, pair_mine, came,
    )
    came_one = first_sum.core_swap(send_one)

    def cross_backward(block):
        sentences = 1 if block == 0 else count - 1
        return call(
            functools.partial(cross_backward_kernel, groups, block),
            [((sentences, places, 2 * width), BF16), ((width, half), BF16)],
            [
                ((sentences, places, 2 * width), BF16),
                ((sentences, places, 2 * TILE), F32),
                ((half // TILE, 2 * TILE, width), BF16),
                ((half // TILE, 2 * TILE, width), BF16),
                ((sentences, width, places), BF16),
                ((SLAB, half), F32),
                ((sentences, places, 2 * SLAB), F32),
                pltpu.SemaphoreType.DMA((1,)),
            ],
            3,
            spot,
            tgt_len,
            src_len,
            query,
            cross_norm,
            cross_along,
            grad_attn,
            pair_all,
            work=10,
            vmem=58 if block == 0 else 32,
            hbm_in=1,
        )

    pair_grad_long, query_grad_t_long = cross_backward(0)
    came_one, pair_grad_long = lax.optimization_barrier((came_one, pair_grad_long))
    parts_one = first_sum.first_split(spot, keep_one, came_one)
    parts_one, pair_all = lax.optimization_barrier((parts_one, pair_all))
    parts_one = first_sum.swap(parts_one, 0)
    pair_grad_rest, query_grad_t_rest = cross_backward(1)
    (wkv_grad,) = call(
        functools.partial(memory_weight_kernel, groups),
        [((2, width, width), BF16)],
        [((width, 2 * width), F32)],
        2,
        spot,
        tgt_len,
        pair_grad_long,
        pair_grad_rest,
        memory,
        *came,
        work=1,
        vmem=32,
    )
    keep_mid, send_mid, grad_hidden_one, grad_self = call(
        first_norm_backward_kernel,
        [
            ((2 * width + LN_ROWS, width), BF16),
            ((2 * width + LN_ROWS, width), BF16),
            ((rows, width), F32),
            ((rows, width), BF16),
        ],
        [],
        1,
        spot,
        hidden_one,
        query_grad_t_long,
        query_grad_t_rest,
        grad_hidden_two,
        wq_cross,
        w_out,
        self_attn_t,
        ln_gain,
        ln_bias,
        ln_part,
        wkv_grad,
        work=0.1,
        vmem=24,
    )
    def memory_grad(pieces, pair_grad_long):
        return call(
            functools.partial(memory_grad_kernel, pieces),
            [((count, size, width), BF16) for _, size in pieces],
            [],
            2,
            spot,
            tgt_len,
            pair_grad_long,
            pair_grad_rest,
            wkv_cross,
            work=0.01,
            vmem=32,
        )

    def send_back(grads):
        return [
            lax.ppermute(array, "mem", [(k, (k - 1 - i) % groups) for k in range(groups)])
            for i, array in enumerate(grads)
        ]

    parts_one, grad_self = lax.optimization_barrier((parts_one, grad_self))
    parts_one = first_sum.split(1, spot, parts_one)
    parts_one, grad_self, pair_grad_long = lax.optimization_barrier((parts_one, grad_self, pair_grad_long))
    parts_one = first_sum.swap(parts_one, 1)
    grad_late = memory_grad(
        [(part * span + span // 2, span // 2) for part in range(1, groups)], pair_grad_long
    )
    backs_late = send_back(grad_late)
    grad_late, grad_self = lax.optimization_barrier((grad_late, grad_self))
    grad_triple, *last = call(
        self_backward_kernel,
        [((rows, 3 * width), BF16)] + [(((width + short) // LAST_PARTS, width), BF16)] * (2 * LAST_PARTS),
        [
            ((tiles, half, 2 * TILE), F32),
            ((tiles, 2 * TILE, width), BF16),
            ((tiles, 2 * TILE, width), BF16),
            ((width, rows), BF16),
            ((width, rows), BF16),
        ],
        2,
        spot,
        tgt_len,
        qkv,
        self_norm,
        grad_self,
        sorted_rows,
        work=0.1,
        vmem=28,
    )
    came_mid = second_sum.core_swap(send_mid)
    parts_one, last, came_mid, pair_grad_long = lax.optimization_barrier(
        (parts_one, last, came_mid, pair_grad_long)
    )
    keep_last = last[:LAST_PARTS]
    came_last = [second_sum.core_swap(part) for part in last[LAST_PARTS:]]
    parts_one = first_sum.split(2, spot, parts_one)
    came_mid, parts_one = lax.optimization_barrier((came_mid, parts_one))
    parts_two = second_sum.first_split(
        spot, keep_mid, came_mid, *[part for both in zip(keep_last, came_last) for part in both]
    )
    parts_one = first_sum.swap(parts_one, 2)
    parts_two, pair_grad_long, grad_triple = lax.optimization_barrier((parts_two, pair_grad_long, grad_triple))
    parts_two = second_sum.swap(parts_two, 0)
    grad_mine, *grad_away = memory_grad(
        [(0, span)] + [(part * span, span // 2) for part in range(1, groups)], pair_grad_long
    )
    backs_late, grad_triple = lax.optimization_barrier((backs_late, grad_triple))
    (grad_target,) = call(
        target_kernel,
        [((rows, width), BF16)],
        [],
        2,
        spot,
        tgt_len,
        grad_triple,
        w_qkv,
        grad_hidden_one,
        work=30,
        vmem=16,
    )
    parts_one, parts_two, grad_away, grad_target = lax.optimization_barrier(
        (parts_one, parts_two, grad_away, grad_target)
    )
    backs_early = send_back(grad_away)
    parts_two = second_sum.swap(second_sum.split(1, spot, parts_two), 1)
    spread_one = first_sum.spread(2, first_sum.total(parts_one)[0])
    parts_two, spread_one, backs_early = lax.optimization_barrier((parts_two, spread_one, backs_early))
    spread_one = first_sum.spread(1, first_sum.join(2, spot, spread_one))
    parts_two = second_sum.swap(second_sum.split(2, spot, parts_two), 2)
    parts_two, spread_one = lax.optimization_barrier((parts_two, spread_one))
    spread_one = first_sum.spread(0, first_sum.join(1, spot, spread_one))
    sum_two, norm_sums = second_sum.total(parts_two)
    spread_two = second_sum.spread(2, sum_two)
    spread_two = second_sum.spread(1, second_sum.join(2, spot, spread_two))
    joined_two = second_sum.join(1, spot, spread_two)
    spread_one, joined_two = lax.optimization_barrier((spread_one, joined_two))
    other_one = [first_sum.core_swap(array) for array in spread_one]
    chunks = hidden_width // width
    pieces = []
    for chunk in range(chunks):
        side, here = chunk // (chunks // 2), chunk % (chunks // 2)
        pieces.append((side, here * width, width, 0, chunk * width, 0))
        pieces.append((side, (chunks // 2 + here) * width, width, 1, 0, chunk * width))
    for side in range(2):
        pieces.append((side, chunks * width, short, 2, side * short, 0))
    grad_w_down, grad_w_up, grad_wo = first_sum.finish(
        spot,
        spread_one,
        other_one,
        list(range(len(spread_one))),
        pieces,
        [((hidden_width, width), F32), ((width, hidden_width), F32), ((width, width), F32)],
    )
    spread_two = second_sum.spread(0, joined_two)
    pieces = [
        (0, 0, width, 0, 0, 0),
        (0, width, width, 1, 0, 0),
        (0, 2 * width, width, 2, 0, 0),
        (0, 3 * width, short, 2, 0, width),
        (1, 0, width, 1, 0, width),
        (1, width, width, 3, 0, 0),
        (1, 2 * width, short, 2, short, width),
        (1, 2 * width + short, width, 2, 0, 2 * width),
    ]
    outs = [
        ((width, width), F32),
        ((width, 2 * width), F32),
        ((width, 3 * width), F32),
        ((width, width), F32),
    ]
    other_two = [second_sum.core_swap(spread_two[0])]
    own_two, grad_w_down = lax.optimization_barrier((spread_two[0], grad_w_down))
    held = second_sum.finish(spot, [own_two], other_two, [0], pieces, outs)
    spread_two, held = lax.optimization_barrier((spread_two, held))
    other_two = other_two + [second_sum.core_swap(array) for array in spread_two[1:]]
    grad_wq, grad_wkv, grad_w_qkv, grad_w_out = second_sum.finish(
        spot, spread_two, other_two, list(range(1, len(spread_two))), pieces, outs, held
    )
    grad_memory = jnp.zeros(memory.shape, BF16)
    grad_memory = lax.dynamic_update_slice(grad_memory, grad_mine, (me * count, 0, 0))
    for part, backs in enumerate((backs_early, backs_late)):
        for i, grads in enumerate(backs):
            owner = (me + i + 1) % groups
            grad_memory = lax.dynamic_update_slice(grad_memory, grads, (owner * count, part * (span // 2), 0))
    return (
        result_out,
        grad_target,
        grad_memory,
        grad_w_qkv,
        grad_w_out,
        grad_wq,
        grad_wkv,
        grad_wo,
        grad_w_up,
        grad_w_down,
        norm_sums[:3],
        norm_sums[3:6],
    )


def solution(mesh):
    rows_spec = P(("dp", "mem"), None)
    memory_spec = P("dp", "mem", None)
    return jax.shard_map(
        body,
        mesh=mesh,
        in_specs=(rows_spec, memory_spec, rows_spec, P("dp", None), P("dp", None)) + (P(),) * 9,
        out_specs=(rows_spec, rows_spec, memory_spec) + (P(),) * 9,
        check_vma=False,
    )
```

```python
import functools
import math

import jax
import jax.numpy as jnp
from jax import lax
from jax.experimental import pallas as pl
from jax.experimental.pallas import tpu as pltpu
from jax.sharding import PartitionSpec as P

HEADS = 8
PAIRS = HEADS // 2
SLAB = 128
SIDE = SLAB // 2
TILE = 128
MASKED = -1e30
EPSILON = 1e-05
F32 = jnp.float32
BF16 = jnp.bfloat16
MIB = 1024 * 1024
LN_ROWS = 16
LAST_PARTS = 2


def dot(left, right):
    return jnp.dot(left, right, preferred_element_type=F32)


def dot_nt(left, right):
    return lax.dot_general(left, right, (((1,), (1,)), ((), ())), preferred_element_type=F32)


def dot_tn(left, right):
    return lax.dot_general(left, right, (((0,), (0,)), ((), ())), preferred_element_type=F32)


def iota(shape, axis):
    return lax.broadcasted_iota(jnp.int32, shape, axis)


def norm_parts(hidden):
    centre = hidden - jnp.mean(hidden, axis=-1, keepdims=True)
    inverse = lax.rsqrt(jnp.mean(centre * centre, axis=-1, keepdims=True) + EPSILON)
    return centre * inverse, inverse


def norm_backward(upstream, unit, inverse, gain_row):
    scaled = upstream * gain_row
    shifted = (
        scaled
        - jnp.mean(scaled, axis=-1, keepdims=True)
        - unit * jnp.mean(scaled * unit, axis=-1, keepdims=True)
    )
    gain_grad = jnp.sum(upstream * unit, axis=0, keepdims=True)
    return inverse * shifted, gain_grad, jnp.sum(upstream, axis=0, keepdims=True)


def sentence_order(me, len_ref):
    count = len_ref.shape[1]
    lengths = [len_ref[me, k] for k in range(count)]
    longest, best, start, running = jnp.int32(0), lengths[0], jnp.int32(0), jnp.int32(0)
    for k in range(1, count):
        running = running + lengths[k - 1]
        more = lengths[k] > best
        longest = jnp.where(more, k, longest)
        start = jnp.where(more, running, start)
        best = jnp.where(more, lengths[k], best)
    order = [longest] + [jnp.where(k < longest, k, k + 1) for k in range(count - 1)]
    bounds = [jnp.int32(0)]
    for k in range(1, count):
        bounds.append(bounds[-1] + len_ref[me, order[k]])
    return order, start, bounds


def moved_rows(index, start, half):
    return jnp.where(index < start, index + half, jnp.where(index < start + half, index - start, index))


def sort_matrix(rows, start):
    spot = moved_rows(iota((rows, rows), 1), start, rows // 2)
    return jnp.where(spot == iota((rows, rows), 0), 1.0, 0.0).astype(BF16)


def unsort_matrix(rows, start):
    spot = moved_rows(iota((rows, rows), 0), start, rows // 2)
    return jnp.where(spot == iota((rows, rows), 1), 1.0, 0.0).astype(BF16)


def side_masks(width):
    side = iota((1, width), 1) % SLAB
    first = jnp.where(side < SLAB // 2, 1.0, 0.0)
    return first.astype(BF16), (1.0 - first).astype(BF16)


def each_pair(step):
    def advance(pair, carry):
        step(pair)
        return carry

    lax.fori_loop(0, PAIRS, advance, 0)


def slab_of(pair, first=0):
    if isinstance(pair, int):
        return pl.ds(first + pair * SLAB, SLAB)
    return pl.ds(pl.multiple_of(first + pair * SLAB, SLAB), SLAB)


def pack_heads(out_ref, rows, width):
    even, odd = side_masks(width)
    for t in range(out_ref.shape[0]):
        tile = rows(t * TILE, TILE)
        out_ref[t, :TILE, :] = tile * even
        out_ref[t, TILE:, :] = tile * odd


def fill_self_bias(bias_ref, bounds, half):
    for t in range(bias_ref.shape[0]):
        block, inner = t // (half // TILE), t % (half // TILE)
        key = iota((half, 2 * TILE), 0)
        query = iota((half, 2 * TILE), 1) % TILE + inner * TILE
        allowed = key <= query
        if block == 1:
            first = jnp.zeros((half, 2 * TILE), jnp.int32)
            for bound in bounds[1:-1]:
                first = jnp.where(query >= bound, bound, first)
            allowed = allowed & (key >= first)
        bias_ref[t] = jnp.where(allowed, 0.0, MASKED)


def self_keys(t, half):
    per = half // TILE
    return (t // per) * half, (t % per + 1) * TILE


def fill_live_bias(bias_ref, me, groups, parts, span, src_ref, sentences):
    key = iota((span, bias_ref.shape[2]), 0)
    for j, sentence in enumerate(sentences):
        for i, part in enumerate(parts):
            place = lax.rem(me - part + groups, groups) * span + key
            live = place < src_ref[me, sentence]
            bias_ref[j, pl.ds(i * span, span), :] = jnp.where(live, 0.0, MASKED)


def cross_units(bounds, half):
    units = [(t, 0, None) for t in range(half // TILE)]
    middle = half // 2
    last = jnp.int32(1)
    for bound in bounds[1:-1]:
        last = last + jnp.where(bound < middle, 1, 0)
    ends = bounds[1:]
    column = iota((1, 2 * TILE), 1) % TILE
    for u in range(len(ends) + 1):
        early = u < last
        sentence = jnp.where(early, u + 1, u)
        tile = jnp.where(early, 0, 1)
        low, high = jnp.int32(0), ends[0]
        for k in range(1, len(ends)):
            low = jnp.where(sentence == k + 1, ends[k - 1], low)
            high = jnp.where(sentence == k + 1, ends[k], high)
        row = column + tile * TILE
        units.append((tile + half // TILE, sentence, (row >= low) & (row < high)))
    return units


def own_sides(both):
    return jnp.concatenate([both[:SIDE, :TILE], both[SIDE:, TILE:]], axis=0)


def side_rows(row):
    even = jnp.broadcast_to(row[:, :TILE], (SIDE, TILE))
    return jnp.concatenate([even, jnp.broadcast_to(row[:, TILE:], (SIDE, TILE))], axis=0)


def tile_columns(tile):
    if isinstance(tile, int):
        return pl.ds(tile * TILE, TILE)
    return pl.ds(pl.multiple_of(tile * TILE, TILE), TILE)


def self_forward_kernel(
    groups,
    me_ref,
    len_ref,
    src_ref,
    target_ref,
    w_qkv_ref,
    w_out_ref,
    wq_ref,
    gain_ref,
    bias_row_ref,
    memory_ref,
    wkv_ref,
    sorted_ref,
    qkv_ref,
    norm_ref,
    attn_t_ref,
    hidden_ref,
    query_ref,
    part_ref,
    top_ref,
    sum_ref,
    pair_out_ref,
    bias_ref,
    live_ref,
    q_pack_ref,
    value_t_ref,
    cross_value_t_ref,
    pair_ref,
    copy_sem,
):
    rows, width = target_ref.shape
    half = rows // 2
    me = me_ref[0]
    order, start, bounds = sentence_order(me, len_ref)
    count, span = pair_ref.shape[0], pair_ref.shape[1]
    copies = []
    for j in range(count):
        block = memory_ref[me * count + order[j]]
        pair_ref[j] = dot(block, wkv_ref[...]).astype(BF16)
        copy = pltpu.make_async_copy(
            pair_ref.at[j], pair_out_ref.at[j, pl.ds(0, span), :], copy_sem.at[j]
        )
        copy.start()
        copies.append(copy)
    sorted_rows = dot(sort_matrix(rows, start), target_ref[...]).astype(BF16)
    sorted_ref[...] = sorted_rows
    fill_self_bias(bias_ref, bounds, half)
    queries = (dot(sorted_rows, w_qkv_ref[:, :width]).astype(BF16) * 0.125).astype(BF16)
    qkv_ref[:, :width] = queries
    pack_heads(q_pack_ref, lambda first, size: queries[first : first + size], width)
    qkv_ref[:, width : 2 * width] = dot(sorted_rows, w_qkv_ref[:, width : 2 * width]).astype(BF16)
    values = dot(sorted_rows, w_qkv_ref[:, 2 * width :]).astype(BF16)
    qkv_ref[:, 2 * width :] = values
    value_t_ref[...] = values.T
    tiles = rows // TILE

    def self_step(pair):
        slab = slab_of(pair)
        for t in range(tiles):
            first, size = self_keys(t, half)
            keys = qkv_ref[pl.ds(first, size), slab_of(pair, width)]
            scores = dot_nt(keys, q_pack_ref[t, :, slab]) + bias_ref[t, :size, :]
            top = jnp.max(scores, axis=0, keepdims=True)
            weights = jnp.exp(scores - top)
            total = jnp.sum(weights, axis=0, keepdims=True)
            probs = (weights * (1.0 / total)).astype(BF16)
            both = dot(value_t_ref[slab, pl.ds(first, size)], probs)
            attn_t_ref[slab, tile_columns(t)] = own_sides(both).astype(BF16)
            norm_ref[pl.ds(pair * tiles + t, 1), :] = top + jnp.log(total)

    each_pair(self_step)
    hidden = sorted_rows.astype(F32) + dot(attn_t_ref[...].T, w_out_ref[...])
    hidden_ref[...] = hidden
    unit, _ = norm_parts(hidden)
    normed = (unit * gain_ref[0:1] + bias_row_ref[0:1]).astype(BF16)
    query_ref[...] = (dot(normed, wq_ref[...]).astype(BF16) * 0.125).astype(BF16)

    pack_heads(q_pack_ref, lambda first, size: query_ref[first : first + size, :], width)
    fill_live_bias(live_ref, me, groups, [0], span, src_ref, order)
    for j in range(count):
        cross_value_t_ref[j] = pair_ref[j, :, width:].T
    units = cross_units(bounds, half)

    def cross_step(pair):
        slab = slab_of(pair)
        for tile, sentence, columns in units:
            scores = dot_nt(pair_ref[sentence, :, slab], q_pack_ref[tile, :, slab]) + live_ref[sentence]
            top = jnp.max(scores, axis=0, keepdims=True)
            weights = jnp.exp(scores - top)
            total = jnp.sum(weights, axis=0, keepdims=True)
            result = own_sides(dot(cross_value_t_ref[sentence, slab, :], weights.astype(BF16)))
            here = tile_columns(tile)
            row = pl.ds(pair * tiles + tile, 1)
            if columns is not None:
                result = jnp.where(columns[:, :TILE], result, part_ref[slab, here])
                top = jnp.where(columns, top, top_ref[row, :])
                total = jnp.where(columns, total, sum_ref[row, :])
            part_ref[slab, here] = result
            top_ref[row, :] = top
            sum_ref[row, :] = total

    part_ref[...] = jnp.zeros_like(part_ref)
    top_ref[...] = jnp.zeros_like(top_ref)
    sum_ref[...] = jnp.ones_like(sum_ref)
    each_pair(cross_step)
    for copy in copies:
        copy.wait()


def middle_kernel(
    groups,
    me_ref,
    len_ref,
    src_ref,
    hidden_one_ref,
    query_ref,
    part_ref,
    top_ref,
    sum_ref,
    wkv_ref,
    gain_ref,
    bias_row_ref,
    wo_hbm,
    w_up_hbm,
    w_down_hbm,
    grad_out_hbm,
    pair_in_hbm,
    *refs,
):
    came_refs = refs[: groups - 1]
    (
        out_ref,
        norm_ref,
        along_ref,
        keep_hbm,
        send_hbm,
        grad_hidden_ref,
        grad_attn_ref,
        ln_ref,
        pair_hbm,
        wo_ref,
        w_up_ref,
        w_down_ref,
        grad_out_ref,
        pair_ref,
        halves_ref,
        live_ref,
        q_pack_ref,
        value_t_ref,
        attn_t_ref,
        active_ref,
        slope_ref,
        grad_upper_ref,
        load_sem,
        pair_sem,
        store_sem,
    ) = refs[groups - 1 :]
    rows, width = hidden_one_ref.shape
    half = rows // 2
    me = me_ref[0]
    count, away = pair_ref.shape[0], pair_ref.shape[1]
    span = away // (groups - 1)
    loads = [
        pltpu.make_async_copy(source, there, load_sem.at[i])
        for i, (source, there) in enumerate(
            [(wo_hbm, wo_ref), (w_up_hbm, w_up_ref), (w_down_hbm, w_down_ref), (grad_out_hbm, grad_out_ref)]
        )
    ]
    for copy in loads:
        copy.start()
    order, start, bounds = sentence_order(me, len_ref)
    fill_live_bias(live_ref, me, groups, list(range(1, groups)), span, src_ref, order)
    pack_heads(q_pack_ref, lambda first, size: query_ref[first : first + size, :], width)
    pair_copies = []
    for j in range(count):
        for part in range(1, groups):
            block = came_refs[part - 1][order[j]]
            pair_ref[j, pl.ds((part - 1) * span, span), :] = dot(block, wkv_ref[...]).astype(BF16)
        value_t_ref[j] = pair_ref[j, :, width:].T
        copy = pltpu.make_async_copy(pair_ref.at[j], pair_hbm.at[j, pl.ds(span, away), :], pair_sem.at[j])
        copy.start()
        pair_copies.append(copy)
    units = cross_units(bounds, half)
    tiles = rows // TILE

    def cross_step(pair):
        slab = slab_of(pair)
        for tile, sentence, columns in units:
            here = tile_columns(tile)
            row = pl.ds(pair * tiles + tile, 1)
            scores = dot_nt(pair_ref[sentence, :, slab], q_pack_ref[tile, :, slab]) + live_ref[sentence]
            before = top_ref[row, :]
            top = jnp.maximum(jnp.max(scores, axis=0, keepdims=True), before)
            weights = jnp.exp(scores - top)
            scale = jnp.exp(before - top)
            total = jnp.sum(weights, axis=0, keepdims=True) + sum_ref[row, :] * scale
            result = own_sides(dot(value_t_ref[sentence, slab, :], weights.astype(BF16)))
            result = (result + part_ref[slab, here] * side_rows(scale)) * side_rows(1.0 / total)
            norm = top + jnp.log(total)
            if columns is not None:
                result = jnp.where(columns[:, :TILE], result, attn_t_ref[slab, here])
                norm = jnp.where(columns, norm, norm_ref[row, :])
            attn_t_ref[slab, here] = result
            norm_ref[row, :] = norm

    attn_t_ref[...] = jnp.zeros_like(attn_t_ref)
    norm_ref[...] = jnp.zeros_like(norm_ref)
    each_pair(cross_step)
    attn_t_low = attn_t_ref[...].astype(BF16)
    loads[0].wait()
    unit_one, _ = norm_parts(hidden_one_ref[...])
    normed_one = unit_one * gain_ref[0:1] + bias_row_ref[0:1]
    hidden_two = normed_one + dot(attn_t_low.T, wo_ref[...])
    unit_two, inverse_two = norm_parts(hidden_two)
    normed_two = unit_two * gain_ref[1:2] + bias_row_ref[1:2]
    normed_two_low = normed_two.astype(BF16)
    chunk = width
    chunks = w_down_ref.shape[0] // chunk
    loads[1].wait()
    loads[2].wait()

    def up_step(c, carry):
        cols = pl.ds(pl.multiple_of(c * chunk, chunk), chunk)
        upper = dot(normed_two_low, w_up_ref[:, cols])
        sigma = 0.5 * jnp.tanh(0.5 * upper) + 0.5
        active = (upper * sigma).astype(BF16)
        active_ref[:, cols] = active
        slope_ref[:, cols] = sigma * (1.0 + upper * (1.0 - sigma))
        return carry

    lax.fori_loop(0, chunks, up_step, 0)

    unit_three, inverse_three = norm_parts(normed_two + dot(active_ref[...], w_down_ref[...]))
    result = (unit_three * gain_ref[2:3] + bias_row_ref[2:3]).astype(BF16)
    out_ref[...] = dot(unsort_matrix(rows, start), result).astype(BF16)
    loads[3].wait()
    upstream = dot(sort_matrix(rows, start), grad_out_ref[...])
    grad_three, gain_three, bias_three = norm_backward(upstream, unit_three, inverse_three, gain_ref[2:3])
    grad_down = grad_three.astype(BF16)
    normed_two_t = normed_two_low.T

    def down_step(c, carry):
        cols = pl.ds(pl.multiple_of(c * chunk, chunk), chunk)
        grad_upper = (dot_nt(grad_down, w_down_ref[cols, :]) * slope_ref[:, cols]).astype(BF16)
        down_part = dot_tn(active_ref[:, cols], grad_down).astype(BF16)
        up_part = dot(normed_two_t, grad_upper).astype(BF16)
        half_index, here = c // (chunks // 2), lax.rem(c, chunks // 2)
        down_rows = pl.ds(pl.multiple_of(here * chunk, chunk), chunk)
        up_rows = pl.ds(pl.multiple_of((chunks // 2 + here) * chunk, chunk), chunk)
        halves_ref[half_index, down_rows, :] = down_part
        halves_ref[half_index, up_rows, :] = up_part
        grad_upper_ref[:, cols] = grad_upper
        return carry

    lax.fori_loop(0, chunks, down_step, 0)

    most = chunks * chunk
    core = me_ref[1]
    stores = [
        pltpu.make_async_copy(
            halves_ref.at[half_index, pl.ds(first, size)], there.at[pl.ds(first, size)], store_sem.at[i]
        )
        for i, (half_index, there, first, size) in enumerate(
            [
                (1 - core, send_hbm, 0, most),
                (core, keep_hbm, 0, most),
                (1 - core, send_hbm, most, halves_ref.shape[1] - most),
                (core, keep_hbm, most, halves_ref.shape[1] - most),
            ]
        )
    ]
    stores[0].start()
    stores[1].start()
    upstream_two = grad_three + dot_nt(grad_upper_ref[...], w_up_ref[...])
    grad_two, gain_two, bias_two = norm_backward(upstream_two, unit_two, inverse_two, gain_ref[1:2])
    grad_two_low = grad_two.astype(BF16)
    wo_grad = dot(attn_t_low, grad_two_low).astype(BF16)
    used = most + width // 2
    for half_index in range(2):
        piece = wo_grad[half_index * (width // 2) : (half_index + 1) * (width // 2)]
        halves_ref[half_index, pl.ds(most, width // 2), :] = piece
        if halves_ref.shape[1] > used:
            halves_ref[half_index, used:, :] = jnp.zeros((halves_ref.shape[1] - used, width), BF16)
    stores[2].start()
    stores[3].start()
    grad_hidden_ref[...] = grad_two
    grad_attn = dot_nt(grad_two_low, wo_ref[...]).astype(BF16)
    grad_attn_ref[...] = grad_attn
    product = grad_attn.T.astype(F32) * attn_t_ref[...]
    for pair in range(PAIRS):
        for side in range(2):
            first = pair * SLAB + side * SIDE
            along = jnp.sum(product[first : first + SIDE], axis=0, keepdims=True)
            for t in range(tiles):
                along_ref[pair * tiles + t : pair * tiles + t + 1, side * TILE : (side + 1) * TILE] = along[
                    :, t * TILE : (t + 1) * TILE
                ]
    ln_ref[...] = jnp.concatenate([gain_two, gain_three, bias_two, bias_three], axis=0)
    for copy in pair_copies + stores:
        copy.wait()


def cross_backward_kernel(
    groups,
    block,
    me_ref,
    len_ref,
    src_ref,
    query_ref,
    norm_ref,
    along_ref,
    grad_attn_ref,
    pair_hbm,
    pair_grad_ref,
    query_grad_t_ref,
    pair_ref,
    live_ref,
    q_pack_ref,
    g_pack_ref,
    key_t_ref,
    query_sum_ref,
    sum_ref,
    load_sem,
):
    rows, width = query_ref.shape
    half = rows // 2
    me = me_ref[0]
    sentences, places = pair_ref.shape[0], pair_ref.shape[1]
    first_sentence = 0 if block == 0 else 1
    load = pltpu.make_async_copy(pair_hbm.at[pl.ds(first_sentence, sentences)], pair_ref, load_sem.at[0])
    load.start()
    order, start, bounds = sentence_order(me, len_ref)
    mine = order[:1] if block == 0 else order[1:]
    fill_live_bias(live_ref, me, groups, list(range(groups)), places // groups, src_ref, mine)
    low = block * half
    pack_heads(q_pack_ref, lambda first, size: query_ref[low + first : low + first + size, :], width)
    pack_heads(g_pack_ref, lambda first, size: grad_attn_ref[low + first : low + first + size, :], width)
    tiles, per = rows // TILE, half // TILE
    units = cross_units(bounds, half)
    units = units[:per] if block == 0 else units[per:]
    load.wait()
    for j in range(sentences):
        key_t_ref[j] = pair_ref[j, :, :width].T

    def pair_step(pair):
        slab, value_slab = slab_of(pair), slab_of(pair, width)
        query_sum_ref[...] = jnp.zeros_like(query_sum_ref)
        sum_ref[...] = jnp.zeros_like(sum_ref)
        for tile, sentence, columns in units:
            j = sentence - first_sentence
            t = tile - block * per
            here = tile_columns(t)
            row = pl.ds(pair * tiles + tile, 1)
            q_rows, g_rows = q_pack_ref[t, :, slab], g_pack_ref[t, :, slab]
            norm = norm_ref[row, :]
            if columns is not None:
                norm = jnp.where(columns, norm, -MASKED)
            scores = dot_nt(pair_ref[j, :, slab], q_rows) + live_ref[j]
            probs = jnp.exp(scores - norm)
            grad_probs = dot_nt(pair_ref[j, :, value_slab], g_rows)
            grad_scores = (probs * (grad_probs - along_ref[row, :])).astype(BF16)
            sum_ref[j, :, :SLAB] += dot(grad_scores, q_rows)
            sum_ref[j, :, SLAB:] += dot(probs.astype(BF16), g_rows)
            query_sum_ref[:, here] += own_sides(dot(key_t_ref[j, slab, :], grad_scores))
        query_grad_t_ref[slab, :] = (query_sum_ref[...] * 0.125).astype(BF16)
        pair_grad_ref[:, :, slab] = sum_ref[:, :, :SLAB].astype(BF16)
        pair_grad_ref[:, :, value_slab] = sum_ref[:, :, SLAB:].astype(BF16)

    for pair in range(PAIRS):
        pair_step(pair)


def memory_weight_kernel(groups, me_ref, len_ref, pair_grad_long_ref, pair_grad_rest_ref, memory_ref, *refs):
    came_refs = refs[: groups - 1]
    wkv_grad_ref, total_ref = refs[groups - 1 :]
    width = memory_ref.shape[2]
    me = me_ref[0]
    count = len_ref.shape[1]
    span = pair_grad_long_ref.shape[1] // groups
    order, _, _ = sentence_order(me, len_ref)
    for j in range(count):
        pair_grad_ref, here = (pair_grad_long_ref, 0) if j == 0 else (pair_grad_rest_ref, j - 1)
        blocks = [memory_ref[me * count + order[j]]] + [ref[order[j]] for ref in came_refs]
        term = dot_tn(jnp.concatenate(blocks, axis=0), pair_grad_ref[here])
        if j == 0:
            total_ref[...] = term
        else:
            total_ref[...] += term
    wkv_grad_ref[0] = total_ref[:, :width].astype(BF16)
    wkv_grad_ref[1] = total_ref[:, width:].astype(BF16)


def memory_grad_kernel(pieces, me_ref, len_ref, pair_grad_long_ref, pair_grad_rest_ref, wkv_ref, *outs):
    count = len_ref.shape[1]
    order, _, _ = sentence_order(me_ref[0], len_ref)
    for j in range(count):
        pair_grad_ref, here = (pair_grad_long_ref, 0) if j == 0 else (pair_grad_rest_ref, j - 1)
        for (first, size), out in zip(pieces, outs):
            out[order[j]] = dot_nt(pair_grad_ref[here, pl.ds(first, size), :], wkv_ref[...]).astype(BF16)


def first_norm_backward_kernel(
    me_ref,
    hidden_one_ref,
    query_grad_t_long_ref,
    query_grad_t_rest_ref,
    grad_hidden_two_ref,
    wq_ref,
    w_out_ref,
    self_attn_t_ref,
    gain_ref,
    bias_row_ref,
    ln_in_ref,
    wkv_grad_ref,
    keep_ref,
    send_ref,
    grad_hidden_ref,
    grad_self_ref,
):
    width = wq_ref.shape[0]
    unit_one, inverse_one = norm_parts(hidden_one_ref[...])
    normed_one = (unit_one * gain_ref[0:1] + bias_row_ref[0:1]).astype(BF16)
    query_grad = jnp.concatenate([query_grad_t_long_ref[...].T, query_grad_t_rest_ref[...].T], axis=0)
    upstream = grad_hidden_two_ref[...] + dot_nt(query_grad, wq_ref[...])
    grad_one, gain_one, bias_one = norm_backward(upstream, unit_one, inverse_one, gain_ref[0:1])
    grad_hidden_ref[...] = grad_one
    grad_one_low = grad_one.astype(BF16)
    grad_self_ref[...] = dot_nt(grad_one_low, w_out_ref[...]).astype(BF16)
    wq_grad = dot_tn(normed_one, query_grad).astype(BF16)
    w_out_grad = dot(self_attn_t_ref[...], grad_one_low).astype(BF16)
    norms = jnp.concatenate(
        [gain_one, ln_in_ref[0:2], bias_one, ln_in_ref[2:4], jnp.zeros((LN_ROWS - 6, width), F32)], axis=0
    ).astype(BF16)

    def halves(low_ref, high_ref):
        low_ref[:width, :] = wq_grad
        low_ref[width : 2 * width, :] = wkv_grad_ref[0]
        high_ref[:width, :] = wkv_grad_ref[1]
        high_ref[width : 2 * width, :] = w_out_grad

    @pl.when(me_ref[1] == 0)
    def _():
        halves(keep_ref, send_ref)

    @pl.when(me_ref[1] != 0)
    def _():
        halves(send_ref, keep_ref)

    keep_ref[2 * width :, :] = norms
    send_ref[2 * width :, :] = norms


def self_backward_kernel(
    me_ref,
    len_ref,
    qkv_ref,
    norm_ref,
    grad_attn_ref,
    sorted_ref,
    grad_triple_ref,
    *refs,
):
    keep_refs, send_refs = refs[:LAST_PARTS], refs[LAST_PARTS : 2 * LAST_PARTS]
    self_backward(
        me_ref,
        len_ref,
        qkv_ref,
        norm_ref,
        grad_attn_ref,
        sorted_ref,
        grad_triple_ref,
        keep_refs,
        send_refs,
        *refs[2 * LAST_PARTS :],
    )


def self_backward(
    me_ref,
    len_ref,
    qkv_ref,
    norm_ref,
    grad_attn_ref,
    sorted_ref,
    grad_triple_ref,
    keep_refs,
    send_refs,
    bias_ref,
    q_pack_ref,
    g_pack_ref,
    key_t_ref,
    query_grad_t_ref,
):
    rows, width = sorted_ref.shape
    half = rows // 2
    _, _, bounds = sentence_order(me_ref[0], len_ref)
    fill_self_bias(bias_ref, bounds, half)
    pack_heads(q_pack_ref, lambda first, size: qkv_ref[first : first + size, :width], width)
    pack_heads(g_pack_ref, lambda first, size: grad_attn_ref[first : first + size, :], width)
    key_t_ref[...] = qkv_ref[:, width : 2 * width].T
    tiles, per = rows // TILE, half // TILE

    def pair_step(pair):
        slab, key_slab, value_slab = slab_of(pair), slab_of(pair, width), slab_of(pair, 2 * width)
        sums = [[None, None] for _ in range(tiles)]
        for t in range(tiles):
            first, size = self_keys(t, half)
            span = pl.ds(first, size)
            q_rows, g_rows = q_pack_ref[t, :, slab], g_pack_ref[t, :, slab]
            scores = dot_nt(qkv_ref[span, key_slab], q_rows) + bias_ref[t, :size, :]
            probs = jnp.exp(scores - norm_ref[pl.ds(pair * tiles + t, 1), :])
            grad_probs = dot_nt(qkv_ref[span, value_slab], g_rows)
            along = jnp.sum(probs * grad_probs, axis=0, keepdims=True)
            grad_scores = (probs * (grad_probs - along)).astype(BF16)
            parts = dot(grad_scores, q_rows), dot(probs.astype(BF16), g_rows)
            for i in range(size // TILE):
                spot = sums[first // TILE + i]
                for k in range(2):
                    piece = parts[k][i * TILE : (i + 1) * TILE]
                    spot[k] = piece if spot[k] is None else spot[k] + piece
            query_grad_t_ref[slab, tile_columns(t)] = (
                own_sides(dot(key_t_ref[slab, span], grad_scores)) * 0.125
            ).astype(BF16)
        for t in range(tiles):
            grad_triple_ref[pl.ds(t * TILE, TILE), key_slab] = sums[t][0].astype(BF16)
            grad_triple_ref[pl.ds(t * TILE, TILE), value_slab] = sums[t][1].astype(BF16)

    for pair in range(PAIRS):
        pair_step(pair)
    grad_triple_ref[:, :width] = query_grad_t_ref[...].T
    sorted_t = sorted_ref[...].T
    grads = [
        dot(sorted_t, grad_triple_ref[:, part * width : (part + 1) * width]).astype(BF16)
        for part in range(3)
    ]
    short = width // 2

    low = jnp.concatenate([grads[0], grads[1][:short]], axis=0)
    high = jnp.concatenate([grads[1][short:], grads[2]], axis=0)
    size = keep_refs[0].shape[0]

    def halves(low_refs, high_refs):
        for i in range(LAST_PARTS):
            low_refs[i][...] = low[i * size : (i + 1) * size]
            high_refs[i][...] = high[i * size : (i + 1) * size]

    @pl.when(me_ref[1] == 0)
    def _():
        halves(keep_refs, send_refs)

    @pl.when(me_ref[1] != 0)
    def _():
        halves(send_refs, keep_refs)


def target_kernel(me_ref, len_ref, grad_triple_ref, w_qkv_ref, grad_hidden_ref, grad_target_ref):
    rows = grad_hidden_ref.shape[0]
    _, start, _ = sentence_order(me_ref[0], len_ref)
    result = grad_hidden_ref[...] + dot_nt(grad_triple_ref[...], w_qkv_ref[...])
    grad_target_ref[...] = dot(unsort_matrix(rows, start), result.astype(BF16)).astype(BF16)


def tree_sum(terms):
    while len(terms) > 1:
        terms = [terms[i] + terms[i + 1] for i in range(0, len(terms), 2)]
    return terms[0]


def rows_of(ref, first, count):
    return ref[pl.ds(pl.multiple_of(first, 16), count), :].astype(F32)


def first_split_kernel(segments, ln, peers, spot_ref, *refs):
    ins, outs, sum_ref = refs[: 2 * segments], refs[2 * segments : -1], refs[-1]
    extra = LN_ROWS if ln else 0
    size = outs[0].shape[0] - extra
    used = 0
    for i in range(segments):
        keep_ref, came_ref = ins[2 * i], ins[2 * i + 1]
        count = keep_ref.shape[0] - (extra if i == 0 else 0)
        sum_ref[used : used + count, :] = (rows_of(keep_ref, 0, count) + rows_of(came_ref, 0, count)).astype(BF16)
        if i == 0 and ln:
            tail = (rows_of(keep_ref, count, LN_ROWS) + rows_of(came_ref, count, LN_ROWS)).astype(BF16)
        used += count
    if sum_ref.shape[0] > used:
        sum_ref[used:, :] = jnp.zeros((sum_ref.shape[0] - used, sum_ref.shape[1]), BF16)
    for d, out in enumerate(outs):
        out[:size, :] = sum_ref[pl.ds(pl.multiple_of((spot_ref[2] ^ d) * size, 16), size), :]
        if ln:
            out[size:, :] = tail


def split_kernel(stage, ln, peers, spot_ref, *refs):
    ins, outs = refs[:peers], refs[peers:]
    extra = LN_ROWS if ln else 0
    size = outs[0].shape[0] - extra
    if ln:
        tail = tree_sum([rows_of(ref, size * len(outs), LN_ROWS) for ref in ins]).astype(BF16)
    for d, out in enumerate(outs):
        first = (spot_ref[2 + stage] ^ d) * size
        out[:size, :] = tree_sum([rows_of(ref, first, size) for ref in ins]).astype(BF16)
        if ln:
            out[size:, :] = tail


def total_kernel(ln, count, *refs):
    ins, outs = refs[:count], refs[count:]
    size = outs[0].shape[0]
    outs[0][...] = tree_sum([rows_of(ref, 0, size) for ref in ins]).astype(BF16)
    if ln:
        norms = tree_sum([rows_of(ref, size, LN_ROWS) for ref in ins])
        outs[1][...] = norms[:3]
        outs[2][...] = norms[3:6]


def join_kernel(stage, spot_ref, *refs):
    out_ref = refs[-1]
    for d, ref in enumerate(refs[:-1]):
        size = ref.shape[0]
        out_ref[pl.ds(pl.multiple_of((spot_ref[2 + stage] ^ d) * size, 16), size), :] = ref[...]


def finish_kernel(offsets, peers, twisted, pieces, held, spot_ref, *refs):
    arrays, refs = refs[: 2 * len(offsets)], refs[2 * len(offsets) + held :]
    outs, (wide_ref, sem) = refs[:-2], refs[-2:]
    core = spot_ref[1]
    size, width = wide_ref.shape[1:]
    copies = []
    for k, ref in enumerate(arrays):
        wide_ref[k] = ref[...].astype(F32)
        d, other = offsets[k // 2], k % 2
        half = 1 - core if other else core
        place = spot_ref[3 if twisted and other else 2] ^ d
        for i in range(2):
            for j in range(peers):
                cut = []
                for piece_half, first, rows, out, row, col in pieces:
                    low, high = max(first, j * size), min(first + rows, (j + 1) * size)
                    if piece_half == i and low < high:
                        there = outs[out].at[pl.ds(row + low - first, high - low), pl.ds(col, width)]
                        here = wide_ref.at[k, pl.ds(low - j * size, high - low), :]
                        cut.append(pltpu.make_async_copy(here, there, sem.at[k, len(cut)]))
                copies.append(((half == i) & (place == j), cut))
                _start_all(*copies[-1])
    for chosen, cut in copies:
        _wait_all(chosen, cut)


def _start_all(chosen, cut):
    @pl.when(chosen)
    def _():
        for copy in cut:
            copy.start()


def _wait_all(chosen, cut):
    @pl.when(chosen)
    def _():
        for copy in cut:
            copy.wait()


class Summing:
    def __init__(self, rows, width, ln):
        self.width, self.ln = width, ln
        self.dp, self.mem = lax.axis_size("dp"), lax.axis_size("mem")
        z_size = 4
        x_size = self.dp // (2 * z_size)
        self.sizes = (x_size, self.mem, z_size)
        self.twisted = x_size == self.mem
        self.chunk = -(-rows // (16 * math.prod(self.sizes))) * 16
        self.rows = self.chunk * math.prod(self.sizes)

    def after(self, stage):
        return self.rows // math.prod(self.sizes[:stage])

    def axis(self, stage, core):
        return 1 - stage if self.twisted and core == 1 and stage < 2 else stage

    def coords(self, dp, mem):
        return [dp // 2 % self.sizes[0], mem, dp // (2 * self.sizes[0])], dp % 2

    def spot(self, me, dp):
        (x, mem, z), core = self.coords(dp, me)
        if self.twisted:
            x, mem = jnp.where(core == 0, x, mem), jnp.where(core == 0, mem, x)
        return jnp.stack([me, core, x, mem, z]).astype(jnp.int32)

    def permute(self, array, stage, offset):
        pairs = []
        for dp in range(self.dp):
            for mem in range(self.mem):
                spots, core = self.coords(dp, mem)
                if stage is None:
                    core ^= offset
                else:
                    spots[self.axis(stage, core)] ^= offset
                to_dp = (spots[2] * self.sizes[0] + spots[0]) * 2 + core
                pairs.append((dp * self.mem + mem, to_dp * self.mem + spots[1]))
        return lax.ppermute(array, ("dp", "mem"), pairs)

    def core_swap(self, send):
        return self.permute(send, None, 1)

    def swap(self, arrays, stage):
        return [arrays[0]] + [self.permute(array, stage, d) for d, array in enumerate(arrays) if d > 0]

    def spread(self, stage, array):
        return [array] + [self.permute(array, stage, d) for d in range(1, self.sizes[stage])]

    def messages(self, stage):
        size = self.after(stage + 1) + (LN_ROWS if self.ln else 0)
        return [((size, self.width), BF16)] * self.sizes[stage]

    def first_split(self, spot, *arrays):
        kernel = functools.partial(first_split_kernel, len(arrays) // 2, self.ln, self.sizes[0])
        return call(kernel, self.messages(0), [((self.rows, self.width), BF16)], 1, spot, *arrays, work=0.01)

    def split(self, stage, spot, arrays, work=0.01):
        kernel = functools.partial(split_kernel, stage, self.ln, self.sizes[stage - 1])
        return call(kernel, self.messages(stage), [], 1, spot, *arrays, work=work)

    def total(self, arrays, work=0.01):
        outs = [((self.chunk, self.width), BF16)]
        if self.ln:
            outs = outs + [((3, self.width), F32)] * 2
        return call(functools.partial(total_kernel, self.ln, self.sizes[2]), outs, [], 0, *arrays, work=work)

    def join(self, stage, spot, arrays, work=0.01):
        outs = [((self.after(stage), self.width), BF16)]
        return call(functools.partial(join_kernel, stage), outs, [], 1, spot, *arrays, work=work)[0]

    def finish(self, spot, mine, others, offsets, pieces, outs, held=()):
        kernel = functools.partial(finish_kernel, offsets, self.sizes[0], self.twisted, pieces, len(held))
        arrays = [array for d in offsets for array in (mine[d], others[d])]
        size = self.after(1)
        scratch = [((len(arrays), size, self.width), F32), pltpu.SemaphoreType.DMA((len(arrays), len(pieces)))]
        aliases = {1 + len(arrays) + i: i for i in range(len(held))}
        return call(
            kernel,
            outs,
            scratch,
            1,
            spot,
            *arrays,
            *held,
            work=1,
            vmem=40,
            hbm_in=len(held),
            hbm_out=len(outs),
            aliases=aliases,
        )


def call(kernel, outs, scratch, scalars, *arrays, work=0.5, vmem=0, hbm_in=0, hbm_out=0, aliases=None):
    plain = len(arrays) - scalars - hbm_in
    if not vmem:
        blocks = [(array.shape, array.dtype) for array in arrays[scalars:]] + outs
        blocks = blocks + [entry for entry in scratch if isinstance(entry, tuple)]
        vmem = max(16, sum(math.prod(shape) * jnp.dtype(kind).itemsize for shape, kind in blocks) // MIB + 7)
    specs = [pl.BlockSpec(memory_space=pltpu.SMEM)] * scalars
    specs = specs + [pl.BlockSpec(memory_space=pltpu.VMEM)] * plain
    specs = specs + [pl.BlockSpec(memory_space=pl.ANY)] * hbm_in
    out_specs = [pl.BlockSpec(memory_space=pltpu.VMEM)] * (len(outs) - hbm_out)
    out_specs = out_specs + [pl.BlockSpec(memory_space=pl.ANY)] * hbm_out
    return pl.pallas_call(
        kernel,
        out_shape=[jax.ShapeDtypeStruct(shape, kind) for shape, kind in outs],
        in_specs=specs,
        out_specs=out_specs,
        scratch_shapes=[pltpu.VMEM(*entry) if isinstance(entry, tuple) else entry for entry in scratch],
        input_output_aliases=aliases or {},
        compiler_params=pltpu.CompilerParams(vmem_limit_bytes=vmem * MIB),
        cost_estimate=pl.CostEstimate(flops=int(work * 1e9), bytes_accessed=int(work * 3e6), transcendentals=0),
    )(*arrays)


def middle(
    groups, first_sum, stats, spot, tgt_len, src_len, hidden_one, query, part, part_top, part_sum, wkv_cross,
    ln_gain, ln_bias, wo_cross, w_up, w_down, grad_out, pair_mine, came,
):
    rows, width = hidden_one.shape
    half, tiles = rows // 2, rows // TILE
    hidden_width = w_down.shape[0]
    count, places, _ = pair_mine.shape
    away = places // groups * (groups - 1)
    arrays = [spot, tgt_len, src_len, hidden_one, query, part, part_top, part_sum, wkv_cross, ln_gain, ln_bias]
    stay = [wo_cross, w_up, w_down, grad_out, pair_mine]

    def kernel(*refs):
        ins, refs = refs[: len(arrays)], refs[len(arrays) :]
        came_refs, refs = refs[: len(came)], refs[len(came) :]
        stay_refs, refs = refs[: len(stay)], refs[len(stay) :]
        outs, refs = refs[:9], refs[9:]
        middle_kernel(groups, *ins, *stay_refs, *came_refs, *outs[:3], *outs[6:8], *outs[3:6], outs[8], *refs)

    result_out, cross_norm, cross_along, grad_hidden_two, grad_attn, ln_part, keep_one, send_one, pair_all = call(
        kernel,
        [
            ((rows, width), BF16),
            (stats, F32),
            (stats, F32),
            ((rows, width), F32),
            ((rows, width), BF16),
            ((4, width), F32),
            ((first_sum.rows, width), BF16),
            ((first_sum.rows, width), BF16),
            ((count, places, 2 * width), BF16),
        ],
        [
            ((width, width), BF16),
            ((width, hidden_width), BF16),
            ((hidden_width, width), BF16),
            ((rows, width), BF16),
            ((count, away, 2 * width), BF16),
            ((2, first_sum.rows, width), BF16),
            ((count, away, 2 * TILE), F32),
            ((tiles, 2 * TILE, width), BF16),
            ((count, width, away), BF16),
            ((width, rows), F32),
            ((rows, hidden_width), BF16),
            ((rows, hidden_width), F32),
            ((rows, hidden_width), BF16),
            pltpu.SemaphoreType.DMA((4,)),
            pltpu.SemaphoreType.DMA((count,)),
            pltpu.SemaphoreType.DMA((4,)),
        ],
        3,
        *arrays,
        *came,
        *stay,
        vmem=60,
        hbm_in=len(stay),
        hbm_out=3,
        aliases={len(arrays) + len(came) + len(stay) - 1: 8},
    )
    return result_out, cross_norm, cross_along, keep_one, send_one, grad_hidden_two, grad_attn, ln_part, pair_all


def body(
    target,
    memory,
    grad_out,
    tgt_len,
    src_len,
    w_qkv,
    w_out,
    wq_cross,
    wkv_cross,
    wo_cross,
    w_up,
    w_down,
    ln_gain,
    ln_bias,
):
    rows, width = target.shape
    half = rows // 2
    tiles = rows // TILE
    hidden_width = w_down.shape[0]
    groups = lax.axis_size("mem")
    me = lax.axis_index("mem")
    count = tgt_len.shape[1]
    span = memory.shape[1]
    places, away = groups * span, (groups - 1) * span
    dp = lax.axis_index("dp")
    short = width // 2
    first_sum = Summing(hidden_width + short, width, False)
    second_sum = Summing(3 * width + short, width, True)
    spot = first_sum.spot(me, dp)
    stats = (PAIRS * tiles, 2 * TILE)

    came = []
    for shift in range(1, groups):
        pairs = [(i, (i + shift) % groups) for i in range(groups)]
        sent = lax.dynamic_slice_in_dim(memory, ((me + shift) % groups) * count, count, 0)
        came.append(lax.ppermute(sent, "mem", pairs))

    sorted_rows, qkv, self_norm, self_attn_t, hidden_one, query, part, part_top, part_sum, pair_mine = call(
        functools.partial(self_forward_kernel, groups),
        [
            ((rows, width), BF16),
            ((rows, 3 * width), BF16),
            (stats, F32),
            ((width, rows), BF16),
            ((rows, width), F32),
            ((rows, width), BF16),
            ((width, rows), F32),
            (stats, F32),
            (stats, F32),
            ((count, places, 2 * width), BF16),
        ],
        [
            ((tiles, half, 2 * TILE), F32),
            ((count, span, 2 * TILE), F32),
            ((tiles, 2 * TILE, width), BF16),
            ((width, rows), BF16),
            ((count, width, span), BF16),
            ((count, span, 2 * width), BF16),
            pltpu.SemaphoreType.DMA((count,)),
        ],
        3,
        spot,
        tgt_len,
        src_len,
        target,
        w_qkv,
        w_out,
        wq_cross,
        ln_gain,
        ln_bias,
        memory,
        wkv_cross,
        vmem=60,
        hbm_out=1,
    )
    result_out, cross_norm, cross_along, keep_one, send_one, grad_hidden_two, grad_attn, ln_part, pair_all = middle(
        groups, first_sum, stats, spot, tgt_len, src_len, hidden_one, query, part, part_top, part_sum, wkv_cross,
        ln_gain, ln_bias, wo_cross, w_up, w_down, grad_out, pair_mine, came,
    )
    came_one = first_sum.core_swap(send_one)

    def cross_backward(block):
        sentences = 1 if block == 0 else count - 1
        return call(
            functools.partial(cross_backward_kernel, groups, block),
            [((sentences, places, 2 * width), BF16), ((width, half), BF16)],
            [
                ((sentences, places, 2 * width), BF16),
                ((sentences, places, 2 * TILE), F32),
                ((half // TILE, 2 * TILE, width), BF16),
                ((half // TILE, 2 * TILE, width), BF16),
                ((sentences, width, places), BF16),
                ((SLAB, half), F32),
                ((sentences, places, 2 * SLAB), F32),
                pltpu.SemaphoreType.DMA((1,)),
            ],
            3,
            spot,
            tgt_len,
            src_len,
            query,
            cross_norm,
            cross_along,
            grad_attn,
            pair_all,
            work=10,
            vmem=58 if block == 0 else 32,
            hbm_in=1,
        )

    pair_grad_long, query_grad_t_long = cross_backward(0)
    came_one, pair_grad_long = lax.optimization_barrier((came_one, pair_grad_long))
    parts_one = first_sum.first_split(spot, keep_one, came_one)
    parts_one, pair_all = lax.optimization_barrier((parts_one, pair_all))
    parts_one = first_sum.swap(parts_one, 0)
    pair_grad_rest, query_grad_t_rest = cross_backward(1)
    (wkv_grad,) = call(
        functools.partial(memory_weight_kernel, groups),
        [((2, width, width), BF16)],
        [((width, 2 * width), F32)],
        2,
        spot,
        tgt_len,
        pair_grad_long,
        pair_grad_rest,
        memory,
        *came,
        work=1,
        vmem=32,
    )
    keep_mid, send_mid, grad_hidden_one, grad_self = call(
        first_norm_backward_kernel,
        [
            ((2 * width + LN_ROWS, width), BF16),
            ((2 * width + LN_ROWS, width), BF16),
            ((rows, width), F32),
            ((rows, width), BF16),
        ],
        [],
        1,
        spot,
        hidden_one,
        query_grad_t_long,
        query_grad_t_rest,
        grad_hidden_two,
        wq_cross,
        w_out,
        self_attn_t,
        ln_gain,
        ln_bias,
        ln_part,
        wkv_grad,
        work=0.1,
        vmem=24,
    )
    def memory_grad(pieces, pair_grad_long):
        return call(
            functools.partial(memory_grad_kernel, pieces),
            [((count, size, width), BF16) for _, size in pieces],
            [],
            2,
            spot,
            tgt_len,
            pair_grad_long,
            pair_grad_rest,
            wkv_cross,
            work=0.01,
            vmem=32,
        )

    def send_back(grads):
        return [
            lax.ppermute(array, "mem", [(k, (k - 1 - i) % groups) for k in range(groups)])
            for i, array in enumerate(grads)
        ]

    parts_one, grad_self = lax.optimization_barrier((parts_one, grad_self))
    parts_one = first_sum.split(1, spot, parts_one)
    parts_one, grad_self, pair_grad_long = lax.optimization_barrier((parts_one, grad_self, pair_grad_long))
    parts_one = first_sum.swap(parts_one, 1)
    grad_late = memory_grad(
        [(part * span + span // 2, span // 2) for part in range(1, groups)], pair_grad_long
    )
    backs_late = send_back(grad_late)
    grad_late, grad_self = lax.optimization_barrier((grad_late, grad_self))
    grad_triple, *last = call(
        self_backward_kernel,
        [((rows, 3 * width), BF16)] + [(((width + short) // LAST_PARTS, width), BF16)] * (2 * LAST_PARTS),
        [
            ((tiles, half, 2 * TILE), F32),
            ((tiles, 2 * TILE, width), BF16),
            ((tiles, 2 * TILE, width), BF16),
            ((width, rows), BF16),
            ((width, rows), BF16),
        ],
        2,
        spot,
        tgt_len,
        qkv,
        self_norm,
        grad_self,
        sorted_rows,
        work=0.1,
        vmem=28,
    )
    came_mid = second_sum.core_swap(send_mid)
    parts_one, last, came_mid, pair_grad_long = lax.optimization_barrier(
        (parts_one, last, came_mid, pair_grad_long)
    )
    keep_last = last[:LAST_PARTS]
    came_last = [second_sum.core_swap(part) for part in last[LAST_PARTS:]]
    parts_one = first_sum.split(2, spot, parts_one)
    came_mid, parts_one = lax.optimization_barrier((came_mid, parts_one))
    parts_two = second_sum.first_split(
        spot, keep_mid, came_mid, *[part for both in zip(keep_last, came_last) for part in both]
    )
    parts_one = first_sum.swap(parts_one, 2)
    parts_two, pair_grad_long, grad_triple = lax.optimization_barrier((parts_two, pair_grad_long, grad_triple))
    parts_two = second_sum.swap(parts_two, 0)
    grad_mine, *grad_away = memory_grad(
        [(0, span)] + [(part * span, span // 2) for part in range(1, groups)], pair_grad_long
    )
    backs_late, grad_triple = lax.optimization_barrier((backs_late, grad_triple))
    (grad_target,) = call(
        target_kernel,
        [((rows, width), BF16)],
        [],
        2,
        spot,
        tgt_len,
        grad_triple,
        w_qkv,
        grad_hidden_one,
        work=30,
        vmem=16,
    )
    parts_one, grad_away, grad_target = lax.optimization_barrier((parts_one, grad_away, grad_target))
    spread_one = first_sum.spread(2, first_sum.total(parts_one)[0])
    backs_early = send_back(grad_away)
    parts_two = second_sum.swap(second_sum.split(1, spot, parts_two), 1)
    joined_one = first_sum.join(2, spot, spread_one, work=0.01)
    spread_one = first_sum.spread(1, joined_one)
    parts_two, joined_one = lax.optimization_barrier((parts_two, joined_one))
    parts_two = second_sum.split(2, spot, parts_two, work=0.01)
    spread_one, _ = lax.optimization_barrier((spread_one, parts_two))
    parts_two = second_sum.swap(parts_two, 2)
    joined_one = first_sum.join(1, spot, spread_one)
    spread_one = first_sum.spread(0, joined_one)
    parts_two, joined_one, backs_early = lax.optimization_barrier((parts_two, joined_one, backs_early))
    sum_two, *norm_sums = second_sum.total(parts_two, work=8)
    spread_two = second_sum.spread(2, sum_two)
    spread_two = second_sum.spread(1, second_sum.join(2, spot, spread_two))
    joined_two = second_sum.join(1, spot, spread_two)
    spread_one, joined_two = lax.optimization_barrier((spread_one, joined_two))
    other_one = [first_sum.core_swap(array) for array in spread_one]
    chunks = hidden_width // width
    pieces = []
    for chunk in range(chunks):
        side, here = chunk // (chunks // 2), chunk % (chunks // 2)
        pieces.append((side, here * width, width, 0, chunk * width, 0))
        pieces.append((side, (chunks // 2 + here) * width, width, 1, 0, chunk * width))
    for side in range(2):
        pieces.append((side, chunks * width, short, 2, side * short, 0))
    grad_w_down, grad_w_up, grad_wo = first_sum.finish(
        spot,
        spread_one,
        other_one,
        list(range(len(spread_one))),
        pieces,
        [((hidden_width, width), F32), ((width, hidden_width), F32), ((width, width), F32)],
    )
    spread_two = second_sum.spread(0, joined_two)
    pieces = [
        (0, 0, width, 0, 0, 0),
        (0, width, width, 1, 0, 0),
        (0, 2 * width, width, 2, 0, 0),
        (0, 3 * width, short, 2, 0, width),
        (1, 0, width, 1, 0, width),
        (1, width, width, 3, 0, 0),
        (1, 2 * width, short, 2, short, width),
        (1, 2 * width + short, width, 2, 0, 2 * width),
    ]
    outs = [
        ((width, width), F32),
        ((width, 2 * width), F32),
        ((width, 3 * width), F32),
        ((width, width), F32),
    ]
    other_two = [second_sum.core_swap(spread_two[0])]
    own_two, grad_w_down = lax.optimization_barrier((spread_two[0], grad_w_down))
    held = second_sum.finish(spot, [own_two], other_two, [0], pieces, outs)
    spread_two, held = lax.optimization_barrier((spread_two, held))
    other_two = other_two + [second_sum.core_swap(array) for array in spread_two[1:]]
    grad_wq, grad_wkv, grad_w_qkv, grad_w_out = second_sum.finish(
        spot, spread_two, other_two, list(range(1, len(spread_two))), pieces, outs, held
    )
    grad_memory = jnp.zeros(memory.shape, BF16)
    grad_memory = lax.dynamic_update_slice(grad_memory, grad_mine, (me * count, 0, 0))
    for part, backs in enumerate((backs_early, backs_late)):
        for i, grads in enumerate(backs):
            owner = (me + i + 1) % groups
            grad_memory = lax.dynamic_update_slice(grad_memory, grads, (owner * count, part * (span // 2), 0))
    return (
        result_out,
        grad_target,
        grad_memory,
        grad_w_qkv,
        grad_w_out,
        grad_wq,
        grad_wkv,
        grad_wo,
        grad_w_up,
        grad_w_down,
        *norm_sums,
    )


def solution(mesh):
    rows_spec = P(("dp", "mem"), None)
    memory_spec = P("dp", "mem", None)
    return jax.shard_map(
        body,
        mesh=mesh,
        in_specs=(rows_spec, memory_spec, rows_spec, P("dp", None), P("dp", None)) + (P(),) * 9,
        out_specs=(rows_spec, rows_spec, memory_spec) + (P(),) * 9,
        check_vma=False,
    )
```

```python
import functools
import math

import jax
import jax.numpy as jnp
from jax import lax
from jax.experimental import pallas as pl
from jax.experimental.pallas import tpu as pltpu
from jax.sharding import PartitionSpec as P

HEADS = 8
PAIRS = HEADS // 2
SLAB = 128
SIDE = SLAB // 2
TILE = 128
MASKED = -1e30
EPSILON = 1e-05
F32 = jnp.float32
BF16 = jnp.bfloat16
MIB = 1024 * 1024
LN_ROWS = 16
LAST_PARTS = 2


def dot(left, right):
    return jnp.dot(left, right, preferred_element_type=F32)


def dot_nt(left, right):
    return lax.dot_general(left, right, (((1,), (1,)), ((), ())), preferred_element_type=F32)


def dot_tn(left, right):
    return lax.dot_general(left, right, (((0,), (0,)), ((), ())), preferred_element_type=F32)


def iota(shape, axis):
    return lax.broadcasted_iota(jnp.int32, shape, axis)


def norm_parts(hidden):
    centre = hidden - jnp.mean(hidden, axis=-1, keepdims=True)
    inverse = lax.rsqrt(jnp.mean(centre * centre, axis=-1, keepdims=True) + EPSILON)
    return centre * inverse, inverse


def norm_backward(upstream, unit, inverse, gain_row):
    scaled = upstream * gain_row
    shifted = (
        scaled
        - jnp.mean(scaled, axis=-1, keepdims=True)
        - unit * jnp.mean(scaled * unit, axis=-1, keepdims=True)
    )
    gain_grad = jnp.sum(upstream * unit, axis=0, keepdims=True)
    return inverse * shifted, gain_grad, jnp.sum(upstream, axis=0, keepdims=True)


def sentence_order(me, len_ref):
    count = len_ref.shape[1]
    lengths = [len_ref[me, k] for k in range(count)]
    longest, best, start, running = jnp.int32(0), lengths[0], jnp.int32(0), jnp.int32(0)
    for k in range(1, count):
        running = running + lengths[k - 1]
        more = lengths[k] > best
        longest = jnp.where(more, k, longest)
        start = jnp.where(more, running, start)
        best = jnp.where(more, lengths[k], best)
    order = [longest] + [jnp.where(k < longest, k, k + 1) for k in range(count - 1)]
    bounds = [jnp.int32(0)]
    for k in range(1, count):
        bounds.append(bounds[-1] + len_ref[me, order[k]])
    return order, start, bounds


def moved_rows(index, start, half):
    return jnp.where(index < start, index + half, jnp.where(index < start + half, index - start, index))


def sort_matrix(rows, start):
    spot = moved_rows(iota((rows, rows), 1), start, rows // 2)
    return jnp.where(spot == iota((rows, rows), 0), 1.0, 0.0).astype(BF16)


def unsort_matrix(rows, start):
    spot = moved_rows(iota((rows, rows), 0), start, rows // 2)
    return jnp.where(spot == iota((rows, rows), 1), 1.0, 0.0).astype(BF16)


def side_masks(width):
    side = iota((1, width), 1) % SLAB
    first = jnp.where(side < SLAB // 2, 1.0, 0.0)
    return first.astype(BF16), (1.0 - first).astype(BF16)


def each_pair(step):
    def advance(pair, carry):
        step(pair)
        return carry

    lax.fori_loop(0, PAIRS, advance, 0)


def slab_of(pair, first=0):
    if isinstance(pair, int):
        return pl.ds(first + pair * SLAB, SLAB)
    return pl.ds(pl.multiple_of(first + pair * SLAB, SLAB), SLAB)


def pack_heads(out_ref, rows, width):
    even, odd = side_masks(width)
    for t in range(out_ref.shape[0]):
        tile = rows(t * TILE, TILE)
        out_ref[t, :TILE, :] = tile * even
        out_ref[t, TILE:, :] = tile * odd


def fill_self_bias(bias_ref, bounds, half):
    for t in range(bias_ref.shape[0]):
        block, inner = t // (half // TILE), t % (half // TILE)
        key = iota((half, 2 * TILE), 0)
        query = iota((half, 2 * TILE), 1) % TILE + inner * TILE
        allowed = key <= query
        if block == 1:
            first = jnp.zeros((half, 2 * TILE), jnp.int32)
            for bound in bounds[1:-1]:
                first = jnp.where(query >= bound, bound, first)
            allowed = allowed & (key >= first)
        bias_ref[t] = jnp.where(allowed, 0.0, MASKED)


def self_keys(t, half):
    per = half // TILE
    return (t // per) * half, (t % per + 1) * TILE


def fill_live_bias(bias_ref, me, groups, parts, span, src_ref, sentences):
    key = iota((span, bias_ref.shape[2]), 0)
    for j, sentence in enumerate(sentences):
        for i, part in enumerate(parts):
            place = lax.rem(me - part + groups, groups) * span + key
            live = place < src_ref[me, sentence]
            bias_ref[j, pl.ds(i * span, span), :] = jnp.where(live, 0.0, MASKED)


def cross_units(bounds, half):
    units = [(t, 0, None) for t in range(half // TILE)]
    middle = half // 2
    last = jnp.int32(1)
    for bound in bounds[1:-1]:
        last = last + jnp.where(bound < middle, 1, 0)
    ends = bounds[1:]
    column = iota((1, 2 * TILE), 1) % TILE
    for u in range(len(ends) + 1):
        early = u < last
        sentence = jnp.where(early, u + 1, u)
        tile = jnp.where(early, 0, 1)
        low, high = jnp.int32(0), ends[0]
        for k in range(1, len(ends)):
            low = jnp.where(sentence == k + 1, ends[k - 1], low)
            high = jnp.where(sentence == k + 1, ends[k], high)
        row = column + tile * TILE
        units.append((tile + half // TILE, sentence, (row >= low) & (row < high)))
    return units


def own_sides(both):
    return jnp.concatenate([both[:SIDE, :TILE], both[SIDE:, TILE:]], axis=0)


def side_rows(row):
    even = jnp.broadcast_to(row[:, :TILE], (SIDE, TILE))
    return jnp.concatenate([even, jnp.broadcast_to(row[:, TILE:], (SIDE, TILE))], axis=0)


def tile_columns(tile):
    if isinstance(tile, int):
        return pl.ds(tile * TILE, TILE)
    return pl.ds(pl.multiple_of(tile * TILE, TILE), TILE)


def self_forward_kernel(
    groups,
    me_ref,
    len_ref,
    src_ref,
    target_ref,
    w_qkv_ref,
    w_out_ref,
    wq_ref,
    gain_ref,
    bias_row_ref,
    memory_ref,
    wkv_ref,
    sorted_ref,
    qkv_ref,
    norm_ref,
    attn_t_ref,
    hidden_ref,
    query_ref,
    part_ref,
    top_ref,
    sum_ref,
    pair_out_ref,
    bias_ref,
    live_ref,
    q_pack_ref,
    value_t_ref,
    cross_value_t_ref,
    pair_ref,
    copy_sem,
):
    rows, width = target_ref.shape
    half = rows // 2
    me = me_ref[0]
    order, start, bounds = sentence_order(me, len_ref)
    count, span = pair_ref.shape[0], pair_ref.shape[1]
    copies = []
    for j in range(count):
        block = memory_ref[me * count + order[j]]
        pair_ref[j] = dot(block, wkv_ref[...]).astype(BF16)
        copy = pltpu.make_async_copy(
            pair_ref.at[j], pair_out_ref.at[j, pl.ds(0, span), :], copy_sem.at[j]
        )
        copy.start()
        copies.append(copy)
    sorted_rows = dot(sort_matrix(rows, start), target_ref[...]).astype(BF16)
    sorted_ref[...] = sorted_rows
    fill_self_bias(bias_ref, bounds, half)
    queries = (dot(sorted_rows, w_qkv_ref[:, :width]).astype(BF16) * 0.125).astype(BF16)
    qkv_ref[:, :width] = queries
    pack_heads(q_pack_ref, lambda first, size: queries[first : first + size], width)
    qkv_ref[:, width : 2 * width] = dot(sorted_rows, w_qkv_ref[:, width : 2 * width]).astype(BF16)
    values = dot(sorted_rows, w_qkv_ref[:, 2 * width :]).astype(BF16)
    qkv_ref[:, 2 * width :] = values
    value_t_ref[...] = values.T
    tiles = rows // TILE

    def self_step(pair):
        slab = slab_of(pair)
        for t in range(tiles):
            first, size = self_keys(t, half)
            keys = qkv_ref[pl.ds(first, size), slab_of(pair, width)]
            scores = dot_nt(keys, q_pack_ref[t, :, slab]) + bias_ref[t, :size, :]
            top = jnp.max(scores, axis=0, keepdims=True)
            weights = jnp.exp(scores - top)
            total = jnp.sum(weights, axis=0, keepdims=True)
            probs = (weights * (1.0 / total)).astype(BF16)
            both = dot(value_t_ref[slab, pl.ds(first, size)], probs)
            attn_t_ref[slab, tile_columns(t)] = own_sides(both).astype(BF16)
            norm_ref[pl.ds(pair * tiles + t, 1), :] = top + jnp.log(total)

    each_pair(self_step)
    hidden = sorted_rows.astype(F32) + dot(attn_t_ref[...].T, w_out_ref[...])
    hidden_ref[...] = hidden
    unit, _ = norm_parts(hidden)
    normed = (unit * gain_ref[0:1] + bias_row_ref[0:1]).astype(BF16)
    query_ref[...] = (dot(normed, wq_ref[...]).astype(BF16) * 0.125).astype(BF16)

    pack_heads(q_pack_ref, lambda first, size: query_ref[first : first + size, :], width)
    fill_live_bias(live_ref, me, groups, [0], span, src_ref, order)
    for j in range(count):
        cross_value_t_ref[j] = pair_ref[j, :, width:].T
    units = cross_units(bounds, half)

    def cross_step(pair):
        slab = slab_of(pair)
        for tile, sentence, columns in units:
            scores = dot_nt(pair_ref[sentence, :, slab], q_pack_ref[tile, :, slab]) + live_ref[sentence]
            top = jnp.max(scores, axis=0, keepdims=True)
            weights = jnp.exp(scores - top)
            total = jnp.sum(weights, axis=0, keepdims=True)
            result = own_sides(dot(cross_value_t_ref[sentence, slab, :], weights.astype(BF16)))
            here = tile_columns(tile)
            row = pl.ds(pair * tiles + tile, 1)
            if columns is not None:
                result = jnp.where(columns[:, :TILE], result, part_ref[slab, here])
                top = jnp.where(columns, top, top_ref[row, :])
                total = jnp.where(columns, total, sum_ref[row, :])
            part_ref[slab, here] = result
            top_ref[row, :] = top
            sum_ref[row, :] = total

    part_ref[...] = jnp.zeros_like(part_ref)
    top_ref[...] = jnp.zeros_like(top_ref)
    sum_ref[...] = jnp.ones_like(sum_ref)
    each_pair(cross_step)
    for copy in copies:
        copy.wait()


def middle_kernel(
    groups,
    me_ref,
    len_ref,
    src_ref,
    hidden_one_ref,
    query_ref,
    part_ref,
    top_ref,
    sum_ref,
    wkv_ref,
    gain_ref,
    bias_row_ref,
    wo_hbm,
    w_up_hbm,
    w_down_hbm,
    grad_out_hbm,
    pair_in_hbm,
    *refs,
):
    came_refs = refs[: groups - 1]
    (
        out_ref,
        norm_ref,
        along_ref,
        keep_hbm,
        send_hbm,
        grad_hidden_ref,
        grad_attn_ref,
        ln_ref,
        pair_hbm,
        wo_ref,
        w_up_ref,
        w_down_ref,
        grad_out_ref,
        pair_ref,
        halves_ref,
        live_ref,
        q_pack_ref,
        value_t_ref,
        attn_t_ref,
        active_ref,
        slope_ref,
        grad_upper_ref,
        load_sem,
        pair_sem,
        store_sem,
    ) = refs[groups - 1 :]
    rows, width = hidden_one_ref.shape
    half = rows // 2
    me = me_ref[0]
    count, away = pair_ref.shape[0], pair_ref.shape[1]
    span = away // (groups - 1)
    loads = [
        pltpu.make_async_copy(source, there, load_sem.at[i])
        for i, (source, there) in enumerate(
            [(wo_hbm, wo_ref), (w_up_hbm, w_up_ref), (w_down_hbm, w_down_ref), (grad_out_hbm, grad_out_ref)]
        )
    ]
    for copy in loads:
        copy.start()
    order, start, bounds = sentence_order(me, len_ref)
    fill_live_bias(live_ref, me, groups, list(range(1, groups)), span, src_ref, order)
    pack_heads(q_pack_ref, lambda first, size: query_ref[first : first + size, :], width)
    pair_copies = []
    for j in range(count):
        for part in range(1, groups):
            block = came_refs[part - 1][order[j]]
            pair_ref[j, pl.ds((part - 1) * span, span), :] = dot(block, wkv_ref[...]).astype(BF16)
        value_t_ref[j] = pair_ref[j, :, width:].T
        copy = pltpu.make_async_copy(pair_ref.at[j], pair_hbm.at[j, pl.ds(span, away), :], pair_sem.at[j])
        copy.start()
        pair_copies.append(copy)
    units = cross_units(bounds, half)
    tiles = rows // TILE

    def cross_step(pair):
        slab = slab_of(pair)
        for tile, sentence, columns in units:
            here = tile_columns(tile)
            row = pl.ds(pair * tiles + tile, 1)
            scores = dot_nt(pair_ref[sentence, :, slab], q_pack_ref[tile, :, slab]) + live_ref[sentence]
            before = top_ref[row, :]
            top = jnp.maximum(jnp.max(scores, axis=0, keepdims=True), before)
            weights = jnp.exp(scores - top)
            scale = jnp.exp(before - top)
            total = jnp.sum(weights, axis=0, keepdims=True) + sum_ref[row, :] * scale
            result = own_sides(dot(value_t_ref[sentence, slab, :], weights.astype(BF16)))
            result = (result + part_ref[slab, here] * side_rows(scale)) * side_rows(1.0 / total)
            norm = top + jnp.log(total)
            if columns is not None:
                result = jnp.where(columns[:, :TILE], result, attn_t_ref[slab, here])
                norm = jnp.where(columns, norm, norm_ref[row, :])
            attn_t_ref[slab, here] = result
            norm_ref[row, :] = norm

    attn_t_ref[...] = jnp.zeros_like(attn_t_ref)
    norm_ref[...] = jnp.zeros_like(norm_ref)
    each_pair(cross_step)
    attn_t_low = attn_t_ref[...].astype(BF16)
    loads[0].wait()
    unit_one, _ = norm_parts(hidden_one_ref[...])
    normed_one = unit_one * gain_ref[0:1] + bias_row_ref[0:1]
    hidden_two = normed_one + dot(attn_t_low.T, wo_ref[...])
    unit_two, inverse_two = norm_parts(hidden_two)
    normed_two = unit_two * gain_ref[1:2] + bias_row_ref[1:2]
    normed_two_low = normed_two.astype(BF16)
    chunk = width
    chunks = w_down_ref.shape[0] // chunk
    loads[1].wait()
    loads[2].wait()

    def up_step(c, carry):
        cols = pl.ds(pl.multiple_of(c * chunk, chunk), chunk)
        upper = dot(normed_two_low, w_up_ref[:, cols])
        sigma = 0.5 * jnp.tanh(0.5 * upper) + 0.5
        active = (upper * sigma).astype(BF16)
        active_ref[:, cols] = active
        slope_ref[:, cols] = sigma * (1.0 + upper * (1.0 - sigma))
        return carry

    lax.fori_loop(0, chunks, up_step, 0)

    unit_three, inverse_three = norm_parts(normed_two + dot(active_ref[...], w_down_ref[...]))
    result = (unit_three * gain_ref[2:3] + bias_row_ref[2:3]).astype(BF16)
    out_ref[...] = dot(unsort_matrix(rows, start), result).astype(BF16)
    loads[3].wait()
    upstream = dot(sort_matrix(rows, start), grad_out_ref[...])
    grad_three, gain_three, bias_three = norm_backward(upstream, unit_three, inverse_three, gain_ref[2:3])
    grad_down = grad_three.astype(BF16)
    normed_two_t = normed_two_low.T

    def down_step(c, carry):
        cols = pl.ds(pl.multiple_of(c * chunk, chunk), chunk)
        grad_upper = (dot_nt(grad_down, w_down_ref[cols, :]) * slope_ref[:, cols]).astype(BF16)
        down_part = dot_tn(active_ref[:, cols], grad_down).astype(BF16)
        up_part = dot(normed_two_t, grad_upper).astype(BF16)
        half_index, here = c // (chunks // 2), lax.rem(c, chunks // 2)
        down_rows = pl.ds(pl.multiple_of(here * chunk, chunk), chunk)
        up_rows = pl.ds(pl.multiple_of((chunks // 2 + here) * chunk, chunk), chunk)
        halves_ref[half_index, down_rows, :] = down_part
        halves_ref[half_index, up_rows, :] = up_part
        grad_upper_ref[:, cols] = grad_upper
        return carry

    lax.fori_loop(0, chunks, down_step, 0)

    most = chunks * chunk
    core = me_ref[1]
    stores = [
        pltpu.make_async_copy(
            halves_ref.at[half_index, pl.ds(first, size)], there.at[pl.ds(first, size)], store_sem.at[i]
        )
        for i, (half_index, there, first, size) in enumerate(
            [
                (1 - core, send_hbm, 0, most),
                (core, keep_hbm, 0, most),
                (1 - core, send_hbm, most, halves_ref.shape[1] - most),
                (core, keep_hbm, most, halves_ref.shape[1] - most),
            ]
        )
    ]
    stores[0].start()
    stores[1].start()
    upstream_two = grad_three + dot_nt(grad_upper_ref[...], w_up_ref[...])
    grad_two, gain_two, bias_two = norm_backward(upstream_two, unit_two, inverse_two, gain_ref[1:2])
    grad_two_low = grad_two.astype(BF16)
    wo_grad = dot(attn_t_low, grad_two_low).astype(BF16)
    used = most + width // 2
    for half_index in range(2):
        piece = wo_grad[half_index * (width // 2) : (half_index + 1) * (width // 2)]
        halves_ref[half_index, pl.ds(most, width // 2), :] = piece
        if halves_ref.shape[1] > used:
            halves_ref[half_index, used:, :] = jnp.zeros((halves_ref.shape[1] - used, width), BF16)
    stores[2].start()
    stores[3].start()
    grad_hidden_ref[...] = grad_two
    grad_attn = dot_nt(grad_two_low, wo_ref[...]).astype(BF16)
    grad_attn_ref[...] = grad_attn
    product = grad_attn.T.astype(F32) * attn_t_ref[...]
    for pair in range(PAIRS):
        for side in range(2):
            first = pair * SLAB + side * SIDE
            along = jnp.sum(product[first : first + SIDE], axis=0, keepdims=True)
            for t in range(tiles):
                along_ref[pair * tiles + t : pair * tiles + t + 1, side * TILE : (side + 1) * TILE] = along[
                    :, t * TILE : (t + 1) * TILE
                ]
    ln_ref[...] = jnp.concatenate([gain_two, gain_three, bias_two, bias_three], axis=0)
    for copy in pair_copies + stores:
        copy.wait()


def cross_backward_kernel(
    groups,
    block,
    me_ref,
    len_ref,
    src_ref,
    query_ref,
    norm_ref,
    along_ref,
    grad_attn_ref,
    pair_hbm,
    pair_grad_ref,
    query_grad_t_ref,
    pair_ref,
    live_ref,
    q_pack_ref,
    g_pack_ref,
    key_t_ref,
    query_sum_ref,
    sum_ref,
    load_sem,
):
    rows, width = query_ref.shape
    half = rows // 2
    me = me_ref[0]
    sentences, places = pair_ref.shape[0], pair_ref.shape[1]
    first_sentence = 0 if block == 0 else 1
    load = pltpu.make_async_copy(pair_hbm.at[pl.ds(first_sentence, sentences)], pair_ref, load_sem.at[0])
    load.start()
    order, start, bounds = sentence_order(me, len_ref)
    mine = order[:1] if block == 0 else order[1:]
    fill_live_bias(live_ref, me, groups, list(range(groups)), places // groups, src_ref, mine)
    low = block * half
    pack_heads(q_pack_ref, lambda first, size: query_ref[low + first : low + first + size, :], width)
    pack_heads(g_pack_ref, lambda first, size: grad_attn_ref[low + first : low + first + size, :], width)
    tiles, per = rows // TILE, half // TILE
    units = cross_units(bounds, half)
    units = units[:per] if block == 0 else units[per:]
    load.wait()
    for j in range(sentences):
        key_t_ref[j] = pair_ref[j, :, :width].T

    def pair_step(pair):
        slab, value_slab = slab_of(pair), slab_of(pair, width)
        query_sum_ref[...] = jnp.zeros_like(query_sum_ref)
        sum_ref[...] = jnp.zeros_like(sum_ref)
        for tile, sentence, columns in units:
            j = sentence - first_sentence
            t = tile - block * per
            here = tile_columns(t)
            row = pl.ds(pair * tiles + tile, 1)
            q_rows, g_rows = q_pack_ref[t, :, slab], g_pack_ref[t, :, slab]
            norm = norm_ref[row, :]
            if columns is not None:
                norm = jnp.where(columns, norm, -MASKED)
            scores = dot_nt(pair_ref[j, :, slab], q_rows) + live_ref[j]
            probs = jnp.exp(scores - norm)
            grad_probs = dot_nt(pair_ref[j, :, value_slab], g_rows)
            grad_scores = (probs * (grad_probs - along_ref[row, :])).astype(BF16)
            sum_ref[j, :, :SLAB] += dot(grad_scores, q_rows)
            sum_ref[j, :, SLAB:] += dot(probs.astype(BF16), g_rows)
            query_sum_ref[:, here] += own_sides(dot(key_t_ref[j, slab, :], grad_scores))
        query_grad_t_ref[slab, :] = (query_sum_ref[...] * 0.125).astype(BF16)
        pair_grad_ref[:, :, slab] = sum_ref[:, :, :SLAB].astype(BF16)
        pair_grad_ref[:, :, value_slab] = sum_ref[:, :, SLAB:].astype(BF16)

    for pair in range(PAIRS):
        pair_step(pair)


def memory_weight_kernel(groups, me_ref, len_ref, pair_grad_long_ref, pair_grad_rest_ref, memory_ref, *refs):
    came_refs = refs[: groups - 1]
    wkv_grad_ref, total_ref = refs[groups - 1 :]
    width = memory_ref.shape[2]
    me = me_ref[0]
    count = len_ref.shape[1]
    span = pair_grad_long_ref.shape[1] // groups
    order, _, _ = sentence_order(me, len_ref)
    for j in range(count):
        pair_grad_ref, here = (pair_grad_long_ref, 0) if j == 0 else (pair_grad_rest_ref, j - 1)
        blocks = [memory_ref[me * count + order[j]]] + [ref[order[j]] for ref in came_refs]
        term = dot_tn(jnp.concatenate(blocks, axis=0), pair_grad_ref[here])
        if j == 0:
            total_ref[...] = term
        else:
            total_ref[...] += term
    wkv_grad_ref[0] = total_ref[:, :width].astype(BF16)
    wkv_grad_ref[1] = total_ref[:, width:].astype(BF16)


def memory_grad_kernel(pieces, me_ref, len_ref, pair_grad_long_ref, pair_grad_rest_ref, wkv_ref, *outs):
    count = len_ref.shape[1]
    order, _, _ = sentence_order(me_ref[0], len_ref)
    for j in range(count):
        pair_grad_ref, here = (pair_grad_long_ref, 0) if j == 0 else (pair_grad_rest_ref, j - 1)
        for (first, size), out in zip(pieces, outs):
            out[order[j]] = dot_nt(pair_grad_ref[here, pl.ds(first, size), :], wkv_ref[...]).astype(BF16)


def first_norm_backward_kernel(
    me_ref,
    hidden_one_ref,
    query_grad_t_long_ref,
    query_grad_t_rest_ref,
    grad_hidden_two_ref,
    wq_ref,
    w_out_ref,
    self_attn_t_ref,
    gain_ref,
    bias_row_ref,
    ln_in_ref,
    wkv_grad_ref,
    keep_ref,
    send_ref,
    grad_hidden_ref,
    grad_self_ref,
):
    width = wq_ref.shape[0]
    unit_one, inverse_one = norm_parts(hidden_one_ref[...])
    normed_one = (unit_one * gain_ref[0:1] + bias_row_ref[0:1]).astype(BF16)
    query_grad = jnp.concatenate([query_grad_t_long_ref[...].T, query_grad_t_rest_ref[...].T], axis=0)
    upstream = grad_hidden_two_ref[...] + dot_nt(query_grad, wq_ref[...])
    grad_one, gain_one, bias_one = norm_backward(upstream, unit_one, inverse_one, gain_ref[0:1])
    grad_hidden_ref[...] = grad_one
    grad_one_low = grad_one.astype(BF16)
    grad_self_ref[...] = dot_nt(grad_one_low, w_out_ref[...]).astype(BF16)
    wq_grad = dot_tn(normed_one, query_grad).astype(BF16)
    w_out_grad = dot(self_attn_t_ref[...], grad_one_low).astype(BF16)
    norms = jnp.concatenate(
        [gain_one, ln_in_ref[0:2], bias_one, ln_in_ref[2:4], jnp.zeros((LN_ROWS - 6, width), F32)], axis=0
    ).astype(BF16)

    def halves(low_ref, high_ref):
        low_ref[:width, :] = wq_grad
        low_ref[width : 2 * width, :] = wkv_grad_ref[0]
        high_ref[:width, :] = wkv_grad_ref[1]
        high_ref[width : 2 * width, :] = w_out_grad

    @pl.when(me_ref[1] == 0)
    def _():
        halves(keep_ref, send_ref)

    @pl.when(me_ref[1] != 0)
    def _():
        halves(send_ref, keep_ref)

    keep_ref[2 * width :, :] = norms
    send_ref[2 * width :, :] = norms


def self_backward_kernel(
    me_ref,
    len_ref,
    qkv_ref,
    norm_ref,
    grad_attn_ref,
    sorted_ref,
    grad_triple_ref,
    *refs,
):
    keep_refs, send_refs = refs[:LAST_PARTS], refs[LAST_PARTS : 2 * LAST_PARTS]
    self_backward(
        me_ref,
        len_ref,
        qkv_ref,
        norm_ref,
        grad_attn_ref,
        sorted_ref,
        grad_triple_ref,
        keep_refs,
        send_refs,
        *refs[2 * LAST_PARTS :],
    )


def self_backward(
    me_ref,
    len_ref,
    qkv_ref,
    norm_ref,
    grad_attn_ref,
    sorted_ref,
    grad_triple_ref,
    keep_refs,
    send_refs,
    bias_ref,
    q_pack_ref,
    g_pack_ref,
    key_t_ref,
    query_grad_t_ref,
):
    rows, width = sorted_ref.shape
    half = rows // 2
    _, _, bounds = sentence_order(me_ref[0], len_ref)
    fill_self_bias(bias_ref, bounds, half)
    pack_heads(q_pack_ref, lambda first, size: qkv_ref[first : first + size, :width], width)
    pack_heads(g_pack_ref, lambda first, size: grad_attn_ref[first : first + size, :], width)
    key_t_ref[...] = qkv_ref[:, width : 2 * width].T
    tiles, per = rows // TILE, half // TILE

    def pair_step(pair):
        slab, key_slab, value_slab = slab_of(pair), slab_of(pair, width), slab_of(pair, 2 * width)
        sums = [[None, None] for _ in range(tiles)]
        for t in range(tiles):
            first, size = self_keys(t, half)
            span = pl.ds(first, size)
            q_rows, g_rows = q_pack_ref[t, :, slab], g_pack_ref[t, :, slab]
            scores = dot_nt(qkv_ref[span, key_slab], q_rows) + bias_ref[t, :size, :]
            probs = jnp.exp(scores - norm_ref[pl.ds(pair * tiles + t, 1), :])
            grad_probs = dot_nt(qkv_ref[span, value_slab], g_rows)
            along = jnp.sum(probs * grad_probs, axis=0, keepdims=True)
            grad_scores = (probs * (grad_probs - along)).astype(BF16)
            parts = dot(grad_scores, q_rows), dot(probs.astype(BF16), g_rows)
            for i in range(size // TILE):
                spot = sums[first // TILE + i]
                for k in range(2):
                    piece = parts[k][i * TILE : (i + 1) * TILE]
                    spot[k] = piece if spot[k] is None else spot[k] + piece
            query_grad_t_ref[slab, tile_columns(t)] = (
                own_sides(dot(key_t_ref[slab, span], grad_scores)) * 0.125
            ).astype(BF16)
        for t in range(tiles):
            grad_triple_ref[pl.ds(t * TILE, TILE), key_slab] = sums[t][0].astype(BF16)
            grad_triple_ref[pl.ds(t * TILE, TILE), value_slab] = sums[t][1].astype(BF16)

    for pair in range(PAIRS):
        pair_step(pair)
    grad_triple_ref[:, :width] = query_grad_t_ref[...].T
    sorted_t = sorted_ref[...].T
    grads = [
        dot(sorted_t, grad_triple_ref[:, part * width : (part + 1) * width]).astype(BF16)
        for part in range(3)
    ]
    short = width // 2

    low = jnp.concatenate([grads[0], grads[1][:short]], axis=0)
    high = jnp.concatenate([grads[1][short:], grads[2]], axis=0)
    size = keep_refs[0].shape[0]

    def halves(low_refs, high_refs):
        for i in range(LAST_PARTS):
            low_refs[i][...] = low[i * size : (i + 1) * size]
            high_refs[i][...] = high[i * size : (i + 1) * size]

    @pl.when(me_ref[1] == 0)
    def _():
        halves(keep_refs, send_refs)

    @pl.when(me_ref[1] != 0)
    def _():
        halves(send_refs, keep_refs)


def target_kernel(me_ref, len_ref, grad_triple_ref, w_qkv_ref, grad_hidden_ref, grad_target_ref):
    rows = grad_hidden_ref.shape[0]
    _, start, _ = sentence_order(me_ref[0], len_ref)
    result = grad_hidden_ref[...] + dot_nt(grad_triple_ref[...], w_qkv_ref[...])
    grad_target_ref[...] = dot(unsort_matrix(rows, start), result.astype(BF16)).astype(BF16)


def tree_sum(terms):
    while len(terms) > 1:
        terms = [terms[i] + terms[i + 1] for i in range(0, len(terms), 2)]
    return terms[0]


def rows_of(ref, first, count):
    return ref[pl.ds(pl.multiple_of(first, 16), count), :].astype(F32)


def first_split_kernel(segments, ln, peers, spot_ref, *refs):
    ins, outs, sum_ref = refs[: 2 * segments], refs[2 * segments : -1], refs[-1]
    extra = LN_ROWS if ln else 0
    size = outs[0].shape[0] - extra
    used = 0
    for i in range(segments):
        keep_ref, came_ref = ins[2 * i], ins[2 * i + 1]
        count = keep_ref.shape[0] - (extra if i == 0 else 0)
        sum_ref[used : used + count, :] = (rows_of(keep_ref, 0, count) + rows_of(came_ref, 0, count)).astype(BF16)
        if i == 0 and ln:
            tail = (rows_of(keep_ref, count, LN_ROWS) + rows_of(came_ref, count, LN_ROWS)).astype(BF16)
        used += count
    if sum_ref.shape[0] > used:
        sum_ref[used:, :] = jnp.zeros((sum_ref.shape[0] - used, sum_ref.shape[1]), BF16)
    for d, out in enumerate(outs):
        out[:size, :] = sum_ref[pl.ds(pl.multiple_of((spot_ref[2] ^ d) * size, 16), size), :]
        if ln:
            out[size:, :] = tail


def split_kernel(stage, ln, peers, spot_ref, *refs):
    ins, outs = refs[:peers], refs[peers:]
    extra = LN_ROWS if ln else 0
    size = outs[0].shape[0] - extra
    if ln:
        tail = tree_sum([rows_of(ref, size * len(outs), LN_ROWS) for ref in ins]).astype(BF16)
    for d, out in enumerate(outs):
        first = (spot_ref[2 + stage] ^ d) * size
        out[:size, :] = tree_sum([rows_of(ref, first, size) for ref in ins]).astype(BF16)
        if ln:
            out[size:, :] = tail


def total_kernel(ln, count, *refs):
    ins, outs = refs[:count], refs[count:]
    size = outs[0].shape[0]
    outs[0][...] = tree_sum([rows_of(ref, 0, size) for ref in ins]).astype(BF16)
    if ln:
        norms = tree_sum([rows_of(ref, size, LN_ROWS) for ref in ins])
        outs[1][...] = norms[:3]
        outs[2][...] = norms[3:6]


def join_kernel(stage, spot_ref, *refs):
    out_ref = refs[-1]
    for d, ref in enumerate(refs[:-1]):
        size = ref.shape[0]
        out_ref[pl.ds(pl.multiple_of((spot_ref[2 + stage] ^ d) * size, 16), size), :] = ref[...]


def finish_kernel(offsets, peers, twisted, pieces, held, spot_ref, *refs):
    arrays, refs = refs[: 2 * len(offsets)], refs[2 * len(offsets) + held :]
    outs, (wide_ref, sem) = refs[:-2], refs[-2:]
    core = spot_ref[1]
    size, width = wide_ref.shape[1:]
    copies = []
    for k, ref in enumerate(arrays):
        wide_ref[k] = ref[...].astype(F32)
        d, other = offsets[k // 2], k % 2
        half = 1 - core if other else core
        place = spot_ref[3 if twisted and other else 2] ^ d
        for i in range(2):
            for j in range(peers):
                cut = []
                for piece_half, first, rows, out, row, col in pieces:
                    low, high = max(first, j * size), min(first + rows, (j + 1) * size)
                    if piece_half == i and low < high:
                        there = outs[out].at[pl.ds(row + low - first, high - low), pl.ds(col, width)]
                        here = wide_ref.at[k, pl.ds(low - j * size, high - low), :]
                        cut.append(pltpu.make_async_copy(here, there, sem.at[k, len(cut)]))
                copies.append(((half == i) & (place == j), cut))
                _start_all(*copies[-1])
    for chosen, cut in copies:
        _wait_all(chosen, cut)


def _start_all(chosen, cut):
    @pl.when(chosen)
    def _():
        for copy in cut:
            copy.start()


def _wait_all(chosen, cut):
    @pl.when(chosen)
    def _():
        for copy in cut:
            copy.wait()


class Summing:
    def __init__(self, rows, width, ln):
        self.width, self.ln = width, ln
        self.dp, self.mem = lax.axis_size("dp"), lax.axis_size("mem")
        z_size = 4
        x_size = self.dp // (2 * z_size)
        self.sizes = (x_size, self.mem, z_size)
        self.twisted = x_size == self.mem
        self.chunk = -(-rows // (16 * math.prod(self.sizes))) * 16
        self.rows = self.chunk * math.prod(self.sizes)

    def after(self, stage):
        return self.rows // math.prod(self.sizes[:stage])

    def axis(self, stage, core):
        return 1 - stage if self.twisted and core == 1 and stage < 2 else stage

    def coords(self, dp, mem):
        return [dp // 2 % self.sizes[0], mem, dp // (2 * self.sizes[0])], dp % 2

    def spot(self, me, dp):
        (x, mem, z), core = self.coords(dp, me)
        if self.twisted:
            x, mem = jnp.where(core == 0, x, mem), jnp.where(core == 0, mem, x)
        return jnp.stack([me, core, x, mem, z]).astype(jnp.int32)

    def permute(self, array, stage, offset):
        pairs = []
        for dp in range(self.dp):
            for mem in range(self.mem):
                spots, core = self.coords(dp, mem)
                if stage is None:
                    core ^= offset
                else:
                    spots[self.axis(stage, core)] ^= offset
                to_dp = (spots[2] * self.sizes[0] + spots[0]) * 2 + core
                pairs.append((dp * self.mem + mem, to_dp * self.mem + spots[1]))
        return lax.ppermute(array, ("dp", "mem"), pairs)

    def core_swap(self, send):
        return self.permute(send, None, 1)

    def swap(self, arrays, stage):
        return [arrays[0]] + [self.permute(array, stage, d) for d, array in enumerate(arrays) if d > 0]

    def spread(self, stage, array):
        return [array] + [self.permute(array, stage, d) for d in range(1, self.sizes[stage])]

    def messages(self, stage):
        size = self.after(stage + 1) + (LN_ROWS if self.ln else 0)
        return [((size, self.width), BF16)] * self.sizes[stage]

    def first_split(self, spot, *arrays):
        kernel = functools.partial(first_split_kernel, len(arrays) // 2, self.ln, self.sizes[0])
        return call(kernel, self.messages(0), [((self.rows, self.width), BF16)], 1, spot, *arrays, work=0.01)

    def split(self, stage, spot, arrays, work=0.01):
        kernel = functools.partial(split_kernel, stage, self.ln, self.sizes[stage - 1])
        return call(kernel, self.messages(stage), [], 1, spot, *arrays, work=work)

    def total(self, arrays, work=0.01):
        outs = [((self.chunk, self.width), BF16)]
        if self.ln:
            outs = outs + [((3, self.width), F32)] * 2
        return call(functools.partial(total_kernel, self.ln, self.sizes[2]), outs, [], 0, *arrays, work=work)

    def join(self, stage, spot, arrays, work=0.01):
        outs = [((self.after(stage), self.width), BF16)]
        return call(functools.partial(join_kernel, stage), outs, [], 1, spot, *arrays, work=work)[0]

    def finish(self, spot, mine, others, offsets, pieces, outs, held=()):
        kernel = functools.partial(finish_kernel, offsets, self.sizes[0], self.twisted, pieces, len(held))
        arrays = [array for d in offsets for array in (mine[d], others[d])]
        size = self.after(1)
        scratch = [((len(arrays), size, self.width), F32), pltpu.SemaphoreType.DMA((len(arrays), len(pieces)))]
        aliases = {1 + len(arrays) + i: i for i in range(len(held))}
        return call(
            kernel,
            outs,
            scratch,
            1,
            spot,
            *arrays,
            *held,
            work=1,
            vmem=40,
            hbm_in=len(held),
            hbm_out=len(outs),
            aliases=aliases,
        )


def call(kernel, outs, scratch, scalars, *arrays, work=0.5, vmem=0, hbm_in=0, hbm_out=0, aliases=None):
    plain = len(arrays) - scalars - hbm_in
    if not vmem:
        blocks = [(array.shape, array.dtype) for array in arrays[scalars:]] + outs
        blocks = blocks + [entry for entry in scratch if isinstance(entry, tuple)]
        vmem = max(16, sum(math.prod(shape) * jnp.dtype(kind).itemsize for shape, kind in blocks) // MIB + 7)
    specs = [pl.BlockSpec(memory_space=pltpu.SMEM)] * scalars
    specs = specs + [pl.BlockSpec(memory_space=pltpu.VMEM)] * plain
    specs = specs + [pl.BlockSpec(memory_space=pl.ANY)] * hbm_in
    out_specs = [pl.BlockSpec(memory_space=pltpu.VMEM)] * (len(outs) - hbm_out)
    out_specs = out_specs + [pl.BlockSpec(memory_space=pl.ANY)] * hbm_out
    return pl.pallas_call(
        kernel,
        out_shape=[jax.ShapeDtypeStruct(shape, kind) for shape, kind in outs],
        in_specs=specs,
        out_specs=out_specs,
        scratch_shapes=[pltpu.VMEM(*entry) if isinstance(entry, tuple) else entry for entry in scratch],
        input_output_aliases=aliases or {},
        compiler_params=pltpu.CompilerParams(vmem_limit_bytes=vmem * MIB),
        cost_estimate=pl.CostEstimate(flops=int(work * 1e9), bytes_accessed=int(work * 3e6), transcendentals=0),
    )(*arrays)


def middle(
    groups, first_sum, stats, spot, tgt_len, src_len, hidden_one, query, part, part_top, part_sum, wkv_cross,
    ln_gain, ln_bias, wo_cross, w_up, w_down, grad_out, pair_mine, came,
):
    rows, width = hidden_one.shape
    half, tiles = rows // 2, rows // TILE
    hidden_width = w_down.shape[0]
    count, places, _ = pair_mine.shape
    away = places // groups * (groups - 1)
    arrays = [spot, tgt_len, src_len, hidden_one, query, part, part_top, part_sum, wkv_cross, ln_gain, ln_bias]
    stay = [wo_cross, w_up, w_down, grad_out, pair_mine]

    def kernel(*refs):
        ins, refs = refs[: len(arrays)], refs[len(arrays) :]
        came_refs, refs = refs[: len(came)], refs[len(came) :]
        stay_refs, refs = refs[: len(stay)], refs[len(stay) :]
        outs, refs = refs[:9], refs[9:]
        middle_kernel(groups, *ins, *stay_refs, *came_refs, *outs[:3], *outs[6:8], *outs[3:6], outs[8], *refs)

    result_out, cross_norm, cross_along, grad_hidden_two, grad_attn, ln_part, keep_one, send_one, pair_all = call(
        kernel,
        [
            ((rows, width), BF16),
            (stats, F32),
            (stats, F32),
            ((rows, width), F32),
            ((rows, width), BF16),
            ((4, width), F32),
            ((first_sum.rows, width), BF16),
            ((first_sum.rows, width), BF16),
            ((count, places, 2 * width), BF16),
        ],
        [
            ((width, width), BF16),
            ((width, hidden_width), BF16),
            ((hidden_width, width), BF16),
            ((rows, width), BF16),
            ((count, away, 2 * width), BF16),
            ((2, first_sum.rows, width), BF16),
            ((count, away, 2 * TILE), F32),
            ((tiles, 2 * TILE, width), BF16),
            ((count, width, away), BF16),
            ((width, rows), F32),
            ((rows, hidden_width), BF16),
            ((rows, hidden_width), F32),
            ((rows, hidden_width), BF16),
            pltpu.SemaphoreType.DMA((4,)),
            pltpu.SemaphoreType.DMA((count,)),
            pltpu.SemaphoreType.DMA((4,)),
        ],
        3,
        *arrays,
        *came,
        *stay,
        vmem=60,
        hbm_in=len(stay),
        hbm_out=3,
        aliases={len(arrays) + len(came) + len(stay) - 1: 8},
    )
    return result_out, cross_norm, cross_along, keep_one, send_one, grad_hidden_two, grad_attn, ln_part, pair_all


def body(
    target,
    memory,
    grad_out,
    tgt_len,
    src_len,
    w_qkv,
    w_out,
    wq_cross,
    wkv_cross,
    wo_cross,
    w_up,
    w_down,
    ln_gain,
    ln_bias,
):
    rows, width = target.shape
    half = rows // 2
    tiles = rows // TILE
    hidden_width = w_down.shape[0]
    groups = lax.axis_size("mem")
    me = lax.axis_index("mem")
    count = tgt_len.shape[1]
    span = memory.shape[1]
    places, away = groups * span, (groups - 1) * span
    dp = lax.axis_index("dp")
    short = width // 2
    first_sum = Summing(hidden_width + short, width, False)
    second_sum = Summing(3 * width + short, width, True)
    spot = first_sum.spot(me, dp)
    stats = (PAIRS * tiles, 2 * TILE)

    came = []
    for shift in range(1, groups):
        pairs = [(i, (i + shift) % groups) for i in range(groups)]
        sent = lax.dynamic_slice_in_dim(memory, ((me + shift) % groups) * count, count, 0)
        came.append(lax.ppermute(sent, "mem", pairs))

    sorted_rows, qkv, self_norm, self_attn_t, hidden_one, query, part, part_top, part_sum, pair_mine = call(
        functools.partial(self_forward_kernel, groups),
        [
            ((rows, width), BF16),
            ((rows, 3 * width), BF16),
            (stats, F32),
            ((width, rows), BF16),
            ((rows, width), F32),
            ((rows, width), BF16),
            ((width, rows), F32),
            (stats, F32),
            (stats, F32),
            ((count, places, 2 * width), BF16),
        ],
        [
            ((tiles, half, 2 * TILE), F32),
            ((count, span, 2 * TILE), F32),
            ((tiles, 2 * TILE, width), BF16),
            ((width, rows), BF16),
            ((count, width, span), BF16),
            ((count, span, 2 * width), BF16),
            pltpu.SemaphoreType.DMA((count,)),
        ],
        3,
        spot,
        tgt_len,
        src_len,
        target,
        w_qkv,
        w_out,
        wq_cross,
        ln_gain,
        ln_bias,
        memory,
        wkv_cross,
        vmem=60,
        hbm_out=1,
    )
    result_out, cross_norm, cross_along, keep_one, send_one, grad_hidden_two, grad_attn, ln_part, pair_all = middle(
        groups, first_sum, stats, spot, tgt_len, src_len, hidden_one, query, part, part_top, part_sum, wkv_cross,
        ln_gain, ln_bias, wo_cross, w_up, w_down, grad_out, pair_mine, came,
    )
    came_one = first_sum.core_swap(send_one)

    def cross_backward(block):
        sentences = 1 if block == 0 else count - 1
        return call(
            functools.partial(cross_backward_kernel, groups, block),
            [((sentences, places, 2 * width), BF16), ((width, half), BF16)],
            [
                ((sentences, places, 2 * width), BF16),
                ((sentences, places, 2 * TILE), F32),
                ((half // TILE, 2 * TILE, width), BF16),
                ((half // TILE, 2 * TILE, width), BF16),
                ((sentences, width, places), BF16),
                ((SLAB, half), F32),
                ((sentences, places, 2 * SLAB), F32),
                pltpu.SemaphoreType.DMA((1,)),
            ],
            3,
            spot,
            tgt_len,
            src_len,
            query,
            cross_norm,
            cross_along,
            grad_attn,
            pair_all,
            work=10,
            vmem=58 if block == 0 else 32,
            hbm_in=1,
        )

    pair_grad_long, query_grad_t_long = cross_backward(0)
    came_one, pair_grad_long = lax.optimization_barrier((came_one, pair_grad_long))
    parts_one = first_sum.first_split(spot, keep_one, came_one)
    parts_one, pair_all = lax.optimization_barrier((parts_one, pair_all))
    parts_one = first_sum.swap(parts_one, 0)
    pair_grad_rest, query_grad_t_rest = cross_backward(1)
    (wkv_grad,) = call(
        functools.partial(memory_weight_kernel, groups),
        [((2, width, width), BF16)],
        [((width, 2 * width), F32)],
        2,
        spot,
        tgt_len,
        pair_grad_long,
        pair_grad_rest,
        memory,
        *came,
        work=1,
        vmem=32,
    )
    keep_mid, send_mid, grad_hidden_one, grad_self = call(
        first_norm_backward_kernel,
        [
            ((2 * width + LN_ROWS, width), BF16),
            ((2 * width + LN_ROWS, width), BF16),
            ((rows, width), F32),
            ((rows, width), BF16),
        ],
        [],
        1,
        spot,
        hidden_one,
        query_grad_t_long,
        query_grad_t_rest,
        grad_hidden_two,
        wq_cross,
        w_out,
        self_attn_t,
        ln_gain,
        ln_bias,
        ln_part,
        wkv_grad,
        work=0.1,
        vmem=24,
    )
    def memory_grad(pieces, pair_grad_long):
        return call(
            functools.partial(memory_grad_kernel, pieces),
            [((count, size, width), BF16) for _, size in pieces],
            [],
            2,
            spot,
            tgt_len,
            pair_grad_long,
            pair_grad_rest,
            wkv_cross,
            work=0.01,
            vmem=32,
        )

    def send_back(grads):
        return [
            lax.ppermute(array, "mem", [(k, (k - 1 - i) % groups) for k in range(groups)])
            for i, array in enumerate(grads)
        ]

    parts_one, grad_self = lax.optimization_barrier((parts_one, grad_self))
    parts_one = first_sum.split(1, spot, parts_one)
    parts_one, grad_self, pair_grad_long = lax.optimization_barrier((parts_one, grad_self, pair_grad_long))
    parts_one = first_sum.swap(parts_one, 1)
    grad_late = memory_grad(
        [(part * span + span // 2, span // 2) for part in range(1, groups)], pair_grad_long
    )
    backs_late = send_back(grad_late)
    grad_late, grad_self = lax.optimization_barrier((grad_late, grad_self))
    grad_triple, *last = call(
        self_backward_kernel,
        [((rows, 3 * width), BF16)] + [(((width + short) // LAST_PARTS, width), BF16)] * (2 * LAST_PARTS),
        [
            ((tiles, half, 2 * TILE), F32),
            ((tiles, 2 * TILE, width), BF16),
            ((tiles, 2 * TILE, width), BF16),
            ((width, rows), BF16),
            ((width, rows), BF16),
        ],
        2,
        spot,
        tgt_len,
        qkv,
        self_norm,
        grad_self,
        sorted_rows,
        work=0.1,
        vmem=28,
    )
    came_mid = second_sum.core_swap(send_mid)
    parts_one, last, came_mid, pair_grad_long = lax.optimization_barrier(
        (parts_one, last, came_mid, pair_grad_long)
    )
    keep_last = last[:LAST_PARTS]
    came_last = [second_sum.core_swap(part) for part in last[LAST_PARTS:]]
    parts_one = first_sum.split(2, spot, parts_one)
    came_mid, parts_one = lax.optimization_barrier((came_mid, parts_one))
    parts_two = second_sum.first_split(
        spot, keep_mid, came_mid, *[part for both in zip(keep_last, came_last) for part in both]
    )
    parts_one = first_sum.swap(parts_one, 2)
    parts_two, pair_grad_long, grad_triple = lax.optimization_barrier((parts_two, pair_grad_long, grad_triple))
    parts_two = second_sum.swap(parts_two, 0)
    grad_mine, *grad_away = memory_grad(
        [(0, span)] + [(part * span, span // 2) for part in range(1, groups)], pair_grad_long
    )
    backs_late, grad_triple = lax.optimization_barrier((backs_late, grad_triple))
    (grad_target,) = call(
        target_kernel,
        [((rows, width), BF16)],
        [],
        2,
        spot,
        tgt_len,
        grad_triple,
        w_qkv,
        grad_hidden_one,
        work=30,
        vmem=16,
    )
    parts_one, grad_away, grad_target = lax.optimization_barrier((parts_one, grad_away, grad_target))
    spread_one = first_sum.spread(2, first_sum.total(parts_one)[0])
    backs_early = send_back(grad_away)
    parts_two = second_sum.swap(second_sum.split(1, spot, parts_two), 1)
    joined_one = first_sum.join(2, spot, spread_one, work=0.01)
    spread_one = first_sum.spread(1, joined_one)
    parts_two, joined_one = lax.optimization_barrier((parts_two, joined_one))
    parts_two = second_sum.split(2, spot, parts_two, work=0.01)
    spread_one, _ = lax.optimization_barrier((spread_one, parts_two))
    parts_two = second_sum.swap(parts_two, 2)
    joined_one = first_sum.join(1, spot, spread_one)
    spread_one = first_sum.spread(0, joined_one)
    parts_two, joined_one = lax.optimization_barrier((parts_two, joined_one))
    sum_two, *norm_sums = second_sum.total(parts_two, work=0.01)
    spread_two = second_sum.spread(2, sum_two)
    spread_two, backs_early = lax.optimization_barrier((spread_two, backs_early))
    spread_two = second_sum.spread(1, second_sum.join(2, spot, spread_two, work=8))
    joined_two = second_sum.join(1, spot, spread_two)
    spread_one, joined_two = lax.optimization_barrier((spread_one, joined_two))
    other_one = [first_sum.core_swap(array) for array in spread_one]
    chunks = hidden_width // width
    pieces = []
    for chunk in range(chunks):
        side, here = chunk // (chunks // 2), chunk % (chunks // 2)
        pieces.append((side, here * width, width, 0, chunk * width, 0))
        pieces.append((side, (chunks // 2 + here) * width, width, 1, 0, chunk * width))
    for side in range(2):
        pieces.append((side, chunks * width, short, 2, side * short, 0))
    grad_w_down, grad_w_up, grad_wo = first_sum.finish(
        spot,
        spread_one,
        other_one,
        list(range(len(spread_one))),
        pieces,
        [((hidden_width, width), F32), ((width, hidden_width), F32), ((width, width), F32)],
    )
    spread_two = second_sum.spread(0, joined_two)
    pieces = [
        (0, 0, width, 0, 0, 0),
        (0, width, width, 1, 0, 0),
        (0, 2 * width, width, 2, 0, 0),
        (0, 3 * width, short, 2, 0, width),
        (1, 0, width, 1, 0, width),
        (1, width, width, 3, 0, 0),
        (1, 2 * width, short, 2, short, width),
        (1, 2 * width + short, width, 2, 0, 2 * width),
    ]
    outs = [
        ((width, width), F32),
        ((width, 2 * width), F32),
        ((width, 3 * width), F32),
        ((width, width), F32),
    ]
    other_two = [second_sum.core_swap(spread_two[0])]
    own_two, grad_w_down = lax.optimization_barrier((spread_two[0], grad_w_down))
    held = second_sum.finish(spot, [own_two], other_two, [0], pieces, outs)
    spread_two, held = lax.optimization_barrier((spread_two, held))
    other_two = other_two + [second_sum.core_swap(array) for array in spread_two[1:]]
    grad_wq, grad_wkv, grad_w_qkv, grad_w_out = second_sum.finish(
        spot, spread_two, other_two, list(range(1, len(spread_two))), pieces, outs, held
    )
    grad_memory = jnp.zeros(memory.shape, BF16)
    grad_memory = lax.dynamic_update_slice(grad_memory, grad_mine, (me * count, 0, 0))
    for part, backs in enumerate((backs_early, backs_late)):
        for i, grads in enumerate(backs):
            owner = (me + i + 1) % groups
            grad_memory = lax.dynamic_update_slice(grad_memory, grads, (owner * count, part * (span // 2), 0))
    return (
        result_out,
        grad_target,
        grad_memory,
        grad_w_qkv,
        grad_w_out,
        grad_wq,
        grad_wkv,
        grad_wo,
        grad_w_up,
        grad_w_down,
        *norm_sums,
    )


def solution(mesh):
    rows_spec = P(("dp", "mem"), None)
    memory_spec = P("dp", "mem", None)
    return jax.shard_map(
        body,
        mesh=mesh,
        in_specs=(rows_spec, memory_spec, rows_spec, P("dp", None), P("dp", None)) + (P(),) * 9,
        out_specs=(rows_spec, rows_spec, memory_spec) + (P(),) * 9,
        check_vma=False,
    )
```

```python
import functools
import math

import jax
import jax.numpy as jnp
from jax import lax
from jax.experimental import pallas as pl
from jax.experimental.pallas import tpu as pltpu
from jax.sharding import PartitionSpec as P

HEADS = 8
PAIRS = HEADS // 2
SLAB = 128
SIDE = SLAB // 2
TILE = 128
MASKED = -1e30
EPSILON = 1e-05
F32 = jnp.float32
BF16 = jnp.bfloat16
MIB = 1024 * 1024
LN_ROWS = 16
LAST_PARTS = 2


def dot(left, right):
    return jnp.dot(left, right, preferred_element_type=F32)


def dot_nt(left, right):
    return lax.dot_general(left, right, (((1,), (1,)), ((), ())), preferred_element_type=F32)


def dot_tn(left, right):
    return lax.dot_general(left, right, (((0,), (0,)), ((), ())), preferred_element_type=F32)


def iota(shape, axis):
    return lax.broadcasted_iota(jnp.int32, shape, axis)


def norm_parts(hidden):
    centre = hidden - jnp.mean(hidden, axis=-1, keepdims=True)
    inverse = lax.rsqrt(jnp.mean(centre * centre, axis=-1, keepdims=True) + EPSILON)
    return centre * inverse, inverse


def norm_backward(upstream, unit, inverse, gain_row):
    scaled = upstream * gain_row
    shifted = (
        scaled
        - jnp.mean(scaled, axis=-1, keepdims=True)
        - unit * jnp.mean(scaled * unit, axis=-1, keepdims=True)
    )
    gain_grad = jnp.sum(upstream * unit, axis=0, keepdims=True)
    return inverse * shifted, gain_grad, jnp.sum(upstream, axis=0, keepdims=True)


def sentence_order(me, len_ref):
    count = len_ref.shape[1]
    lengths = [len_ref[me, k] for k in range(count)]
    longest, best, start, running = jnp.int32(0), lengths[0], jnp.int32(0), jnp.int32(0)
    for k in range(1, count):
        running = running + lengths[k - 1]
        more = lengths[k] > best
        longest = jnp.where(more, k, longest)
        start = jnp.where(more, running, start)
        best = jnp.where(more, lengths[k], best)
    order = [longest] + [jnp.where(k < longest, k, k + 1) for k in range(count - 1)]
    bounds = [jnp.int32(0)]
    for k in range(1, count):
        bounds.append(bounds[-1] + len_ref[me, order[k]])
    return order, start, bounds


def moved_rows(index, start, half):
    return jnp.where(index < start, index + half, jnp.where(index < start + half, index - start, index))


def sort_matrix(rows, start):
    spot = moved_rows(iota((rows, rows), 1), start, rows // 2)
    return jnp.where(spot == iota((rows, rows), 0), 1.0, 0.0).astype(BF16)


def unsort_matrix(rows, start):
    spot = moved_rows(iota((rows, rows), 0), start, rows // 2)
    return jnp.where(spot == iota((rows, rows), 1), 1.0, 0.0).astype(BF16)


def side_masks(width):
    side = iota((1, width), 1) % SLAB
    first = jnp.where(side < SLAB // 2, 1.0, 0.0)
    return first.astype(BF16), (1.0 - first).astype(BF16)


def each_pair(step):
    def advance(pair, carry):
        step(pair)
        return carry

    lax.fori_loop(0, PAIRS, advance, 0)


def slab_of(pair, first=0):
    if isinstance(pair, int):
        return pl.ds(first + pair * SLAB, SLAB)
    return pl.ds(pl.multiple_of(first + pair * SLAB, SLAB), SLAB)


def pack_heads(out_ref, rows, width):
    even, odd = side_masks(width)
    for t in range(out_ref.shape[0]):
        tile = rows(t * TILE, TILE)
        out_ref[t, :TILE, :] = tile * even
        out_ref[t, TILE:, :] = tile * odd


def fill_self_bias(bias_ref, bounds, half):
    for t in range(bias_ref.shape[0]):
        block, inner = t // (half // TILE), t % (half // TILE)
        key = iota((half, 2 * TILE), 0)
        query = iota((half, 2 * TILE), 1) % TILE + inner * TILE
        allowed = key <= query
        if block == 1:
            first = jnp.zeros((half, 2 * TILE), jnp.int32)
            for bound in bounds[1:-1]:
                first = jnp.where(query >= bound, bound, first)
            allowed = allowed & (key >= first)
        bias_ref[t] = jnp.where(allowed, 0.0, MASKED)


def self_keys(t, half):
    per = half // TILE
    return (t // per) * half, (t % per + 1) * TILE


def fill_live_bias(bias_ref, me, groups, parts, span, src_ref, sentences):
    key = iota((span, bias_ref.shape[2]), 0)
    for j, sentence in enumerate(sentences):
        for i, part in enumerate(parts):
            place = lax.rem(me - part + groups, groups) * span + key
            live = place < src_ref[me, sentence]
            bias_ref[j, pl.ds(i * span, span), :] = jnp.where(live, 0.0, MASKED)


def cross_units(bounds, half):
    units = [(t, 0, None) for t in range(half // TILE)]
    middle = half // 2
    last = jnp.int32(1)
    for bound in bounds[1:-1]:
        last = last + jnp.where(bound < middle, 1, 0)
    ends = bounds[1:]
    column = iota((1, 2 * TILE), 1) % TILE
    for u in range(len(ends) + 1):
        early = u < last
        sentence = jnp.where(early, u + 1, u)
        tile = jnp.where(early, 0, 1)
        low, high = jnp.int32(0), ends[0]
        for k in range(1, len(ends)):
            low = jnp.where(sentence == k + 1, ends[k - 1], low)
            high = jnp.where(sentence == k + 1, ends[k], high)
        row = column + tile * TILE
        units.append((tile + half // TILE, sentence, (row >= low) & (row < high)))
    return units


def own_sides(both):
    return jnp.concatenate([both[:SIDE, :TILE], both[SIDE:, TILE:]], axis=0)


def side_rows(row):
    even = jnp.broadcast_to(row[:, :TILE], (SIDE, TILE))
    return jnp.concatenate([even, jnp.broadcast_to(row[:, TILE:], (SIDE, TILE))], axis=0)


def tile_columns(tile):
    if isinstance(tile, int):
        return pl.ds(tile * TILE, TILE)
    return pl.ds(pl.multiple_of(tile * TILE, TILE), TILE)


def self_forward_kernel(
    groups,
    me_ref,
    len_ref,
    src_ref,
    target_ref,
    w_qkv_ref,
    w_out_ref,
    wq_ref,
    gain_ref,
    bias_row_ref,
    memory_ref,
    wkv_ref,
    sorted_ref,
    qkv_ref,
    norm_ref,
    attn_t_ref,
    hidden_ref,
    query_ref,
    part_ref,
    top_ref,
    sum_ref,
    pair_out_ref,
    bias_ref,
    live_ref,
    q_pack_ref,
    value_t_ref,
    cross_value_t_ref,
    pair_ref,
    copy_sem,
):
    rows, width = target_ref.shape
    half = rows // 2
    me = me_ref[0]
    order, start, bounds = sentence_order(me, len_ref)
    count, span = pair_ref.shape[0], pair_ref.shape[1]
    copies = []
    for j in range(count):
        block = memory_ref[me * count + order[j]]
        pair_ref[j] = dot(block, wkv_ref[...]).astype(BF16)
        copy = pltpu.make_async_copy(
            pair_ref.at[j], pair_out_ref.at[j, pl.ds(0, span), :], copy_sem.at[j]
        )
        copy.start()
        copies.append(copy)
    sorted_rows = dot(sort_matrix(rows, start), target_ref[...]).astype(BF16)
    sorted_ref[...] = sorted_rows
    fill_self_bias(bias_ref, bounds, half)
    queries = (dot(sorted_rows, w_qkv_ref[:, :width]).astype(BF16) * 0.125).astype(BF16)
    qkv_ref[:, :width] = queries
    pack_heads(q_pack_ref, lambda first, size: queries[first : first + size], width)
    qkv_ref[:, width : 2 * width] = dot(sorted_rows, w_qkv_ref[:, width : 2 * width]).astype(BF16)
    values = dot(sorted_rows, w_qkv_ref[:, 2 * width :]).astype(BF16)
    qkv_ref[:, 2 * width :] = values
    value_t_ref[...] = values.T
    tiles = rows // TILE

    def self_step(pair):
        slab = slab_of(pair)
        for t in range(tiles):
            first, size = self_keys(t, half)
            keys = qkv_ref[pl.ds(first, size), slab_of(pair, width)]
            scores = dot_nt(keys, q_pack_ref[t, :, slab]) + bias_ref[t, :size, :]
            top = jnp.max(scores, axis=0, keepdims=True)
            weights = jnp.exp(scores - top)
            total = jnp.sum(weights, axis=0, keepdims=True)
            probs = (weights * (1.0 / total)).astype(BF16)
            both = dot(value_t_ref[slab, pl.ds(first, size)], probs)
            attn_t_ref[slab, tile_columns(t)] = own_sides(both).astype(BF16)
            norm_ref[pl.ds(pair * tiles + t, 1), :] = top + jnp.log(total)

    each_pair(self_step)
    hidden = sorted_rows.astype(F32) + dot(attn_t_ref[...].T, w_out_ref[...])
    hidden_ref[...] = hidden
    unit, _ = norm_parts(hidden)
    normed = (unit * gain_ref[0:1] + bias_row_ref[0:1]).astype(BF16)
    query_ref[...] = (dot(normed, wq_ref[...]).astype(BF16) * 0.125).astype(BF16)

    pack_heads(q_pack_ref, lambda first, size: query_ref[first : first + size, :], width)
    fill_live_bias(live_ref, me, groups, [0], span, src_ref, order)
    for j in range(count):
        cross_value_t_ref[j] = pair_ref[j, :, width:].T
    units = cross_units(bounds, half)

    def cross_step(pair):
        slab = slab_of(pair)
        for tile, sentence, columns in units:
            scores = dot_nt(pair_ref[sentence, :, slab], q_pack_ref[tile, :, slab]) + live_ref[sentence]
            top = jnp.max(scores, axis=0, keepdims=True)
            weights = jnp.exp(scores - top)
            total = jnp.sum(weights, axis=0, keepdims=True)
            result = own_sides(dot(cross_value_t_ref[sentence, slab, :], weights.astype(BF16)))
            here = tile_columns(tile)
            row = pl.ds(pair * tiles + tile, 1)
            if columns is not None:
                result = jnp.where(columns[:, :TILE], result, part_ref[slab, here])
                top = jnp.where(columns, top, top_ref[row, :])
                total = jnp.where(columns, total, sum_ref[row, :])
            part_ref[slab, here] = result
            top_ref[row, :] = top
            sum_ref[row, :] = total

    part_ref[...] = jnp.zeros_like(part_ref)
    top_ref[...] = jnp.zeros_like(top_ref)
    sum_ref[...] = jnp.ones_like(sum_ref)
    each_pair(cross_step)
    for copy in copies:
        copy.wait()


def middle_kernel(
    groups,
    me_ref,
    len_ref,
    src_ref,
    hidden_one_ref,
    query_ref,
    part_ref,
    top_ref,
    sum_ref,
    wkv_ref,
    gain_ref,
    bias_row_ref,
    wo_hbm,
    w_up_hbm,
    w_down_hbm,
    grad_out_hbm,
    pair_in_hbm,
    *refs,
):
    came_refs = refs[: groups - 1]
    (
        out_ref,
        norm_ref,
        along_ref,
        keep_hbm,
        send_hbm,
        grad_hidden_ref,
        grad_attn_ref,
        ln_ref,
        pair_hbm,
        wo_ref,
        w_up_ref,
        w_down_ref,
        grad_out_ref,
        pair_ref,
        halves_ref,
        live_ref,
        q_pack_ref,
        value_t_ref,
        attn_t_ref,
        active_ref,
        slope_ref,
        grad_upper_ref,
        load_sem,
        pair_sem,
        store_sem,
    ) = refs[groups - 1 :]
    rows, width = hidden_one_ref.shape
    half = rows // 2
    me = me_ref[0]
    count, away = pair_ref.shape[0], pair_ref.shape[1]
    span = away // (groups - 1)
    loads = [
        pltpu.make_async_copy(source, there, load_sem.at[i])
        for i, (source, there) in enumerate(
            [(wo_hbm, wo_ref), (w_up_hbm, w_up_ref), (w_down_hbm, w_down_ref), (grad_out_hbm, grad_out_ref)]
        )
    ]
    for copy in loads:
        copy.start()
    order, start, bounds = sentence_order(me, len_ref)
    fill_live_bias(live_ref, me, groups, list(range(1, groups)), span, src_ref, order)
    pack_heads(q_pack_ref, lambda first, size: query_ref[first : first + size, :], width)
    pair_copies = []
    for j in range(count):
        for part in range(1, groups):
            block = came_refs[part - 1][order[j]]
            pair_ref[j, pl.ds((part - 1) * span, span), :] = dot(block, wkv_ref[...]).astype(BF16)
        value_t_ref[j] = pair_ref[j, :, width:].T
        copy = pltpu.make_async_copy(pair_ref.at[j], pair_hbm.at[j, pl.ds(span, away), :], pair_sem.at[j])
        copy.start()
        pair_copies.append(copy)
    units = cross_units(bounds, half)
    tiles = rows // TILE

    def cross_step(pair):
        slab = slab_of(pair)
        for tile, sentence, columns in units:
            here = tile_columns(tile)
            row = pl.ds(pair * tiles + tile, 1)
            scores = dot_nt(pair_ref[sentence, :, slab], q_pack_ref[tile, :, slab]) + live_ref[sentence]
            before = top_ref[row, :]
            top = jnp.maximum(jnp.max(scores, axis=0, keepdims=True), before)
            weights = jnp.exp(scores - top)
            scale = jnp.exp(before - top)
            total = jnp.sum(weights, axis=0, keepdims=True) + sum_ref[row, :] * scale
            result = own_sides(dot(value_t_ref[sentence, slab, :], weights.astype(BF16)))
            result = (result + part_ref[slab, here] * side_rows(scale)) * side_rows(1.0 / total)
            norm = top + jnp.log(total)
            if columns is not None:
                result = jnp.where(columns[:, :TILE], result, attn_t_ref[slab, here])
                norm = jnp.where(columns, norm, norm_ref[row, :])
            attn_t_ref[slab, here] = result
            norm_ref[row, :] = norm

    attn_t_ref[...] = jnp.zeros_like(attn_t_ref)
    norm_ref[...] = jnp.zeros_like(norm_ref)
    each_pair(cross_step)
    attn_t_low = attn_t_ref[...].astype(BF16)
    loads[0].wait()
    unit_one, _ = norm_parts(hidden_one_ref[...])
    normed_one = unit_one * gain_ref[0:1] + bias_row_ref[0:1]
    hidden_two = normed_one + dot(attn_t_low.T, wo_ref[...])
    unit_two, inverse_two = norm_parts(hidden_two)
    normed_two = unit_two * gain_ref[1:2] + bias_row_ref[1:2]
    normed_two_low = normed_two.astype(BF16)
    chunk = width
    chunks = w_down_ref.shape[0] // chunk
    loads[1].wait()
    loads[2].wait()

    def up_step(c, carry):
        cols = pl.ds(pl.multiple_of(c * chunk, chunk), chunk)
        upper = dot(normed_two_low, w_up_ref[:, cols])
        sigma = 0.5 * jnp.tanh(0.5 * upper) + 0.5
        active = (upper * sigma).astype(BF16)
        active_ref[:, cols] = active
        slope_ref[:, cols] = sigma * (1.0 + upper * (1.0 - sigma))
        return carry

    lax.fori_loop(0, chunks, up_step, 0)

    unit_three, inverse_three = norm_parts(normed_two + dot(active_ref[...], w_down_ref[...]))
    result = (unit_three * gain_ref[2:3] + bias_row_ref[2:3]).astype(BF16)
    out_ref[...] = dot(unsort_matrix(rows, start), result).astype(BF16)
    loads[3].wait()
    upstream = dot(sort_matrix(rows, start), grad_out_ref[...])
    grad_three, gain_three, bias_three = norm_backward(upstream, unit_three, inverse_three, gain_ref[2:3])
    grad_down = grad_three.astype(BF16)
    normed_two_t = normed_two_low.T

    def down_step(c, carry):
        cols = pl.ds(pl.multiple_of(c * chunk, chunk), chunk)
        grad_upper = (dot_nt(grad_down, w_down_ref[cols, :]) * slope_ref[:, cols]).astype(BF16)
        down_part = dot_tn(active_ref[:, cols], grad_down).astype(BF16)
        up_part = dot(normed_two_t, grad_upper).astype(BF16)
        half_index, here = c // (chunks // 2), lax.rem(c, chunks // 2)
        down_rows = pl.ds(pl.multiple_of(here * chunk, chunk), chunk)
        up_rows = pl.ds(pl.multiple_of((chunks // 2 + here) * chunk, chunk), chunk)
        halves_ref[half_index, down_rows, :] = down_part
        halves_ref[half_index, up_rows, :] = up_part
        grad_upper_ref[:, cols] = grad_upper
        return carry

    lax.fori_loop(0, chunks, down_step, 0)

    most = chunks * chunk
    core = me_ref[1]
    stores = [
        pltpu.make_async_copy(
            halves_ref.at[half_index, pl.ds(first, size)], there.at[pl.ds(first, size)], store_sem.at[i]
        )
        for i, (half_index, there, first, size) in enumerate(
            [
                (1 - core, send_hbm, 0, most),
                (core, keep_hbm, 0, most),
                (1 - core, send_hbm, most, halves_ref.shape[1] - most),
                (core, keep_hbm, most, halves_ref.shape[1] - most),
            ]
        )
    ]
    stores[0].start()
    stores[1].start()
    upstream_two = grad_three + dot_nt(grad_upper_ref[...], w_up_ref[...])
    grad_two, gain_two, bias_two = norm_backward(upstream_two, unit_two, inverse_two, gain_ref[1:2])
    grad_two_low = grad_two.astype(BF16)
    wo_grad = dot(attn_t_low, grad_two_low).astype(BF16)
    used = most + width // 2
    for half_index in range(2):
        piece = wo_grad[half_index * (width // 2) : (half_index + 1) * (width // 2)]
        halves_ref[half_index, pl.ds(most, width // 2), :] = piece
        if halves_ref.shape[1] > used:
            halves_ref[half_index, used:, :] = jnp.zeros((halves_ref.shape[1] - used, width), BF16)
    stores[2].start()
    stores[3].start()
    grad_hidden_ref[...] = grad_two
    grad_attn = dot_nt(grad_two_low, wo_ref[...]).astype(BF16)
    grad_attn_ref[...] = grad_attn
    product = grad_attn.T.astype(F32) * attn_t_ref[...]
    for pair in range(PAIRS):
        for side in range(2):
            first = pair * SLAB + side * SIDE
            along = jnp.sum(product[first : first + SIDE], axis=0, keepdims=True)
            for t in range(tiles):
                along_ref[pair * tiles + t : pair * tiles + t + 1, side * TILE : (side + 1) * TILE] = along[
                    :, t * TILE : (t + 1) * TILE
                ]
    ln_ref[...] = jnp.concatenate([gain_two, gain_three, bias_two, bias_three], axis=0)
    for copy in pair_copies + stores:
        copy.wait()


def cross_backward_kernel(
    groups,
    block,
    me_ref,
    len_ref,
    src_ref,
    query_ref,
    norm_ref,
    along_ref,
    grad_attn_ref,
    pair_hbm,
    pair_grad_ref,
    query_grad_t_ref,
    pair_ref,
    live_ref,
    q_pack_ref,
    g_pack_ref,
    key_t_ref,
    query_sum_ref,
    sum_ref,
    load_sem,
):
    rows, width = query_ref.shape
    half = rows // 2
    me = me_ref[0]
    sentences, places = pair_ref.shape[0], pair_ref.shape[1]
    first_sentence = 0 if block == 0 else 1
    load = pltpu.make_async_copy(pair_hbm.at[pl.ds(first_sentence, sentences)], pair_ref, load_sem.at[0])
    load.start()
    order, start, bounds = sentence_order(me, len_ref)
    mine = order[:1] if block == 0 else order[1:]
    fill_live_bias(live_ref, me, groups, list(range(groups)), places // groups, src_ref, mine)
    low = block * half
    pack_heads(q_pack_ref, lambda first, size: query_ref[low + first : low + first + size, :], width)
    pack_heads(g_pack_ref, lambda first, size: grad_attn_ref[low + first : low + first + size, :], width)
    tiles, per = rows // TILE, half // TILE
    units = cross_units(bounds, half)
    units = units[:per] if block == 0 else units[per:]
    load.wait()
    for j in range(sentences):
        key_t_ref[j] = pair_ref[j, :, :width].T

    def pair_step(pair):
        slab, value_slab = slab_of(pair), slab_of(pair, width)
        query_sum_ref[...] = jnp.zeros_like(query_sum_ref)
        sum_ref[...] = jnp.zeros_like(sum_ref)
        for tile, sentence, columns in units:
            j = sentence - first_sentence
            t = tile - block * per
            here = tile_columns(t)
            row = pl.ds(pair * tiles + tile, 1)
            q_rows, g_rows = q_pack_ref[t, :, slab], g_pack_ref[t, :, slab]
            norm = norm_ref[row, :]
            if columns is not None:
                norm = jnp.where(columns, norm, -MASKED)
            scores = dot_nt(pair_ref[j, :, slab], q_rows) + live_ref[j]
            probs = jnp.exp(scores - norm)
            grad_probs = dot_nt(pair_ref[j, :, value_slab], g_rows)
            grad_scores = (probs * (grad_probs - along_ref[row, :])).astype(BF16)
            sum_ref[j, :, :SLAB] += dot(grad_scores, q_rows)
            sum_ref[j, :, SLAB:] += dot(probs.astype(BF16), g_rows)
            query_sum_ref[:, here] += own_sides(dot(key_t_ref[j, slab, :], grad_scores))
        query_grad_t_ref[slab, :] = (query_sum_ref[...] * 0.125).astype(BF16)
        pair_grad_ref[:, :, slab] = sum_ref[:, :, :SLAB].astype(BF16)
        pair_grad_ref[:, :, value_slab] = sum_ref[:, :, SLAB:].astype(BF16)

    for pair in range(PAIRS):
        pair_step(pair)


def memory_weight_kernel(groups, me_ref, len_ref, pair_grad_long_ref, pair_grad_rest_ref, memory_ref, *refs):
    came_refs = refs[: groups - 1]
    wkv_grad_ref, total_ref = refs[groups - 1 :]
    width = memory_ref.shape[2]
    me = me_ref[0]
    count = len_ref.shape[1]
    span = pair_grad_long_ref.shape[1] // groups
    order, _, _ = sentence_order(me, len_ref)
    for j in range(count):
        pair_grad_ref, here = (pair_grad_long_ref, 0) if j == 0 else (pair_grad_rest_ref, j - 1)
        blocks = [memory_ref[me * count + order[j]]] + [ref[order[j]] for ref in came_refs]
        term = dot_tn(jnp.concatenate(blocks, axis=0), pair_grad_ref[here])
        if j == 0:
            total_ref[...] = term
        else:
            total_ref[...] += term
    wkv_grad_ref[0] = total_ref[:, :width].astype(BF16)
    wkv_grad_ref[1] = total_ref[:, width:].astype(BF16)


def memory_grad_kernel(pieces, me_ref, len_ref, pair_grad_long_ref, pair_grad_rest_ref, wkv_ref, *outs):
    count = len_ref.shape[1]
    order, _, _ = sentence_order(me_ref[0], len_ref)
    for j in range(count):
        pair_grad_ref, here = (pair_grad_long_ref, 0) if j == 0 else (pair_grad_rest_ref, j - 1)
        for (first, size), out in zip(pieces, outs):
            out[order[j]] = dot_nt(pair_grad_ref[here, pl.ds(first, size), :], wkv_ref[...]).astype(BF16)


def first_norm_backward_kernel(
    me_ref,
    hidden_one_ref,
    query_grad_t_long_ref,
    query_grad_t_rest_ref,
    grad_hidden_two_ref,
    wq_ref,
    w_out_ref,
    self_attn_t_ref,
    gain_ref,
    bias_row_ref,
    ln_in_ref,
    wkv_grad_ref,
    keep_ref,
    send_ref,
    grad_hidden_ref,
    grad_self_ref,
):
    width = wq_ref.shape[0]
    unit_one, inverse_one = norm_parts(hidden_one_ref[...])
    normed_one = (unit_one * gain_ref[0:1] + bias_row_ref[0:1]).astype(BF16)
    query_grad = jnp.concatenate([query_grad_t_long_ref[...].T, query_grad_t_rest_ref[...].T], axis=0)
    upstream = grad_hidden_two_ref[...] + dot_nt(query_grad, wq_ref[...])
    grad_one, gain_one, bias_one = norm_backward(upstream, unit_one, inverse_one, gain_ref[0:1])
    grad_hidden_ref[...] = grad_one
    grad_one_low = grad_one.astype(BF16)
    grad_self_ref[...] = dot_nt(grad_one_low, w_out_ref[...]).astype(BF16)
    wq_grad = dot_tn(normed_one, query_grad).astype(BF16)
    w_out_grad = dot(self_attn_t_ref[...], grad_one_low).astype(BF16)
    norms = jnp.concatenate(
        [gain_one, ln_in_ref[0:2], bias_one, ln_in_ref[2:4], jnp.zeros((LN_ROWS - 6, width), F32)], axis=0
    ).astype(BF16)

    def halves(low_ref, high_ref):
        low_ref[:width, :] = wq_grad
        low_ref[width : 2 * width, :] = wkv_grad_ref[0]
        high_ref[:width, :] = wkv_grad_ref[1]
        high_ref[width : 2 * width, :] = w_out_grad

    @pl.when(me_ref[1] == 0)
    def _():
        halves(keep_ref, send_ref)

    @pl.when(me_ref[1] != 0)
    def _():
        halves(send_ref, keep_ref)

    keep_ref[2 * width :, :] = norms
    send_ref[2 * width :, :] = norms


def self_backward_kernel(
    me_ref,
    len_ref,
    qkv_ref,
    norm_ref,
    grad_attn_ref,
    sorted_ref,
    grad_triple_ref,
    *refs,
):
    keep_refs, send_refs = refs[:LAST_PARTS], refs[LAST_PARTS : 2 * LAST_PARTS]
    self_backward(
        me_ref,
        len_ref,
        qkv_ref,
        norm_ref,
        grad_attn_ref,
        sorted_ref,
        grad_triple_ref,
        keep_refs,
        send_refs,
        *refs[2 * LAST_PARTS :],
    )


def self_backward(
    me_ref,
    len_ref,
    qkv_ref,
    norm_ref,
    grad_attn_ref,
    sorted_ref,
    grad_triple_ref,
    keep_refs,
    send_refs,
    bias_ref,
    q_pack_ref,
    g_pack_ref,
    key_t_ref,
    query_grad_t_ref,
):
    rows, width = sorted_ref.shape
    half = rows // 2
    _, _, bounds = sentence_order(me_ref[0], len_ref)
    fill_self_bias(bias_ref, bounds, half)
    pack_heads(q_pack_ref, lambda first, size: qkv_ref[first : first + size, :width], width)
    pack_heads(g_pack_ref, lambda first, size: grad_attn_ref[first : first + size, :], width)
    key_t_ref[...] = qkv_ref[:, width : 2 * width].T
    tiles, per = rows // TILE, half // TILE

    def pair_step(pair):
        slab, key_slab, value_slab = slab_of(pair), slab_of(pair, width), slab_of(pair, 2 * width)
        sums = [[None, None] for _ in range(tiles)]
        for t in range(tiles):
            first, size = self_keys(t, half)
            span = pl.ds(first, size)
            q_rows, g_rows = q_pack_ref[t, :, slab], g_pack_ref[t, :, slab]
            scores = dot_nt(qkv_ref[span, key_slab], q_rows) + bias_ref[t, :size, :]
            probs = jnp.exp(scores - norm_ref[pl.ds(pair * tiles + t, 1), :])
            grad_probs = dot_nt(qkv_ref[span, value_slab], g_rows)
            along = jnp.sum(probs * grad_probs, axis=0, keepdims=True)
            grad_scores = (probs * (grad_probs - along)).astype(BF16)
            parts = dot(grad_scores, q_rows), dot(probs.astype(BF16), g_rows)
            for i in range(size // TILE):
                spot = sums[first // TILE + i]
                for k in range(2):
                    piece = parts[k][i * TILE : (i + 1) * TILE]
                    spot[k] = piece if spot[k] is None else spot[k] + piece
            query_grad_t_ref[slab, tile_columns(t)] = (
                own_sides(dot(key_t_ref[slab, span], grad_scores)) * 0.125
            ).astype(BF16)
        for t in range(tiles):
            grad_triple_ref[pl.ds(t * TILE, TILE), key_slab] = sums[t][0].astype(BF16)
            grad_triple_ref[pl.ds(t * TILE, TILE), value_slab] = sums[t][1].astype(BF16)

    for pair in range(PAIRS):
        pair_step(pair)
    grad_triple_ref[:, :width] = query_grad_t_ref[...].T
    sorted_t = sorted_ref[...].T
    grads = [
        dot(sorted_t, grad_triple_ref[:, part * width : (part + 1) * width]).astype(BF16)
        for part in range(3)
    ]
    short = width // 2

    low = jnp.concatenate([grads[0], grads[1][:short]], axis=0)
    high = jnp.concatenate([grads[1][short:], grads[2]], axis=0)
    size = keep_refs[0].shape[0]

    def halves(low_refs, high_refs):
        for i in range(LAST_PARTS):
            low_refs[i][...] = low[i * size : (i + 1) * size]
            high_refs[i][...] = high[i * size : (i + 1) * size]

    @pl.when(me_ref[1] == 0)
    def _():
        halves(keep_refs, send_refs)

    @pl.when(me_ref[1] != 0)
    def _():
        halves(send_refs, keep_refs)


def target_kernel(me_ref, len_ref, grad_triple_ref, w_qkv_ref, grad_hidden_ref, grad_target_ref):
    rows = grad_hidden_ref.shape[0]
    _, start, _ = sentence_order(me_ref[0], len_ref)
    result = grad_hidden_ref[...] + dot_nt(grad_triple_ref[...], w_qkv_ref[...])
    grad_target_ref[...] = dot(unsort_matrix(rows, start), result.astype(BF16)).astype(BF16)


def tree_sum(terms):
    while len(terms) > 1:
        terms = [terms[i] + terms[i + 1] for i in range(0, len(terms), 2)]
    return terms[0]


def rows_of(ref, first, count):
    return ref[pl.ds(pl.multiple_of(first, 16), count), :].astype(F32)


def first_split_kernel(segments, ln, peers, spot_ref, *refs):
    ins, outs, sum_ref = refs[: 2 * segments], refs[2 * segments : -1], refs[-1]
    extra = LN_ROWS if ln else 0
    size = outs[0].shape[0] - extra
    used = 0
    for i in range(segments):
        keep_ref, came_ref = ins[2 * i], ins[2 * i + 1]
        count = keep_ref.shape[0] - (extra if i == 0 else 0)
        sum_ref[used : used + count, :] = (rows_of(keep_ref, 0, count) + rows_of(came_ref, 0, count)).astype(BF16)
        if i == 0 and ln:
            tail = (rows_of(keep_ref, count, LN_ROWS) + rows_of(came_ref, count, LN_ROWS)).astype(BF16)
        used += count
    if sum_ref.shape[0] > used:
        sum_ref[used:, :] = jnp.zeros((sum_ref.shape[0] - used, sum_ref.shape[1]), BF16)
    for d, out in enumerate(outs):
        out[:size, :] = sum_ref[pl.ds(pl.multiple_of((spot_ref[2] ^ d) * size, 16), size), :]
        if ln:
            out[size:, :] = tail


def split_kernel(stage, ln, peers, spot_ref, *refs):
    ins, outs = refs[:peers], refs[peers:]
    extra = LN_ROWS if ln else 0
    size = outs[0].shape[0] - extra
    if ln:
        tail = tree_sum([rows_of(ref, size * len(outs), LN_ROWS) for ref in ins]).astype(BF16)
    for d, out in enumerate(outs):
        first = (spot_ref[2 + stage] ^ d) * size
        out[:size, :] = tree_sum([rows_of(ref, first, size) for ref in ins]).astype(BF16)
        if ln:
            out[size:, :] = tail


def total_kernel(ln, count, *refs):
    ins, outs = refs[:count], refs[count:]
    size = outs[0].shape[0]
    outs[0][...] = tree_sum([rows_of(ref, 0, size) for ref in ins]).astype(BF16)
    if ln:
        norms = tree_sum([rows_of(ref, size, LN_ROWS) for ref in ins])
        outs[1][...] = norms[:3]
        outs[2][...] = norms[3:6]


def join_kernel(index, spot_ref, *refs):
    out_ref = refs[-1]
    for d, ref in enumerate(refs[:-1]):
        size = ref.shape[0]
        out_ref[pl.ds(pl.multiple_of((spot_ref[index] ^ d) * size, 16), size), :] = ref[...]


def finish_kernel(offsets, cuts, index, held, spot_ref, *refs):
    arrays, refs = refs[: 2 * len(offsets)], refs[2 * len(offsets) + held :]
    outs, (wide_ref, sem) = refs[:-2], refs[-2:]
    core = spot_ref[1]
    width = wide_ref.shape[2]
    copies = []
    for k, ref in enumerate(arrays):
        wide_ref[k] = ref[...].astype(F32)
        d, other = offsets[k // 2], k % 2
        half = 1 - core if other else core
        place = spot_ref[index + other] ^ d
        for i in range(2):
            for j, cut in enumerate(cuts[i]):
                copies.append(
                    (
                        (half == i) & (place == j),
                        [
                            pltpu.make_async_copy(
                                wide_ref.at[k, pl.ds(first, rows), :],
                                outs[out].at[pl.ds(row, rows), pl.ds(col, width)],
                                sem.at[k, m],
                            )
                            for m, (first, rows, out, row, col) in enumerate(cut)
                        ],
                    )
                )
                _start_all(*copies[-1])
    for chosen, cut in copies:
        _wait_all(chosen, cut)


def _start_all(chosen, cut):
    @pl.when(chosen)
    def _():
        for copy in cut:
            copy.start()


def _wait_all(chosen, cut):
    @pl.when(chosen)
    def _():
        for copy in cut:
            copy.wait()


class Summing:
    def __init__(self, rows, width, ln, scatter, gather):
        self.width, self.ln = width, ln
        self.dp, self.mem = lax.axis_size("dp"), lax.axis_size("mem")
        z_size = 4
        self.x_size = self.dp // (2 * z_size)
        size_of = {"x": self.x_size, "mem": self.mem, "z": z_size, "near": 2, "far": 2}
        sizes = [[[size_of[dim] for dim in dims] for dims in side] for side in (scatter, gather)]
        if sizes[0][0] != sizes[0][1] or sizes[1][0] != sizes[1][1]:
            scatter, gather = (scatter[0],) * 2, (gather[0],) * 2
        self.size_of, self.scatter, self.gather = size_of, scatter, gather
        self.sizes, self.gather_sizes = sizes[0][0], sizes[1][0]
        self.chunk = -(-rows // (16 * math.prod(self.sizes))) * 16
        self.rows = self.chunk * math.prod(self.sizes)

    def after(self, stage):
        return self.rows // math.prod(self.sizes[:stage])

    def coords(self, dp, mem):
        z = dp // (2 * self.x_size)
        return {"x": dp // 2 % self.x_size, "mem": mem, "z": z, "near": z % 2, "far": z // 2}

    def spot(self, me, dp):
        coords, core = self.coords(dp, me), dp % 2

        def pick(dims, which):
            return jnp.where(which == 0, coords[dims[0]], coords[dims[1]])

        stages = list(zip(*self.scatter)) + list(zip(*self.gather))
        spots = [pick(dims, core) for dims in stages] + [pick(stages[-1], 1 - core)]
        return jnp.stack([me, core] + spots).astype(jnp.int32)

    def permute(self, array, dims, offset):
        pairs = []
        for dp in range(self.dp):
            for mem in range(self.mem):
                spots, core = self.coords(dp, mem), dp % 2
                if dims is None:
                    core ^= offset
                elif dims[core] in ("near", "far"):
                    spots["z"] ^= offset * (1 if dims[core] == "near" else 2)
                else:
                    spots[dims[core]] ^= offset
                to_dp = (spots["z"] * self.x_size + spots["x"]) * 2 + core
                pairs.append((dp * self.mem + mem, to_dp * self.mem + spots["mem"]))
        return lax.ppermute(array, ("dp", "mem"), pairs)

    def core_swap(self, send):
        return self.permute(send, None, 1)

    def swap(self, arrays, stage):
        dims = [side[stage] for side in self.scatter]
        return [arrays[0]] + [self.permute(array, dims, d) for d, array in enumerate(arrays) if d > 0]

    def spread(self, stage, array):
        dims = [side[stage] for side in self.gather]
        return [array] + [self.permute(array, dims, d) for d in range(1, self.gather_sizes[stage])]

    def messages(self, stage):
        size = self.after(stage + 1) + (LN_ROWS if self.ln else 0)
        return [((size, self.width), BF16)] * self.sizes[stage]

    def first_split(self, spot, *arrays):
        kernel = functools.partial(first_split_kernel, len(arrays) // 2, self.ln, self.sizes[0])
        return call(kernel, self.messages(0), [((self.rows, self.width), BF16)], 1, spot, *arrays, work=0.01)

    def split(self, stage, spot, arrays, work=0.01):
        kernel = functools.partial(split_kernel, stage, self.ln, self.sizes[stage - 1])
        return call(kernel, self.messages(stage), [], 1, spot, *arrays, work=work)

    def total(self, arrays, work=0.01):
        outs = [((self.chunk, self.width), BF16)]
        if self.ln:
            outs = outs + [((3, self.width), F32)] * 2
        return call(functools.partial(total_kernel, self.ln, self.sizes[-1]), outs, [], 0, *arrays, work=work)

    def join(self, stage, spot, arrays, work=0.01):
        outs = [((len(arrays) * arrays[0].shape[0], self.width), BF16)]
        kernel = functools.partial(join_kernel, 2 + len(self.sizes) + stage)
        return call(kernel, outs, [], 1, spot, *arrays, work=work)[0]

    def cuts(self, half, place, pieces):
        dims, blocks = self.gather[half], [{self.gather[half][-1]: place}]
        for dim in reversed(dims[:-1]):
            blocks = [{**block, dim: i} for block in blocks for i in range(self.size_of[dim])]
        spans = []
        for position, block in enumerate(blocks):
            first = sum(block[dim] * self.after(k + 1) for k, dim in enumerate(self.scatter[half]))
            if spans and spans[-1][1] + spans[-1][2] == first:
                spans[-1][2] += self.chunk
            else:
                spans.append([position * self.chunk, first, self.chunk])
        cut = []
        for source, begin, size in spans:
            for piece_half, first, rows, out, row, col in pieces:
                low, high = max(begin, first), min(begin + size, first + rows)
                if piece_half == half and low < high:
                    cut.append((source + low - begin, high - low, out, row + low - first, col))
        return cut

    def finish(self, spot, mine, others, offsets, pieces, outs, held=()):
        places = range(self.gather_sizes[-1])
        cuts = [[self.cuts(half, place, pieces) for place in places] for half in range(2)]
        index = 1 + len(self.sizes) + len(self.gather_sizes)
        kernel = functools.partial(finish_kernel, offsets, cuts, index, len(held))
        arrays = [array for d in offsets for array in (mine[d], others[d])]
        most = max(len(cut) for side in cuts for cut in side)
        scratch = [
            ((len(arrays), *arrays[0].shape), F32),
            pltpu.SemaphoreType.DMA((len(arrays), most)),
        ]
        aliases = {1 + len(arrays) + i: i for i in range(len(held))}
        return call(
            kernel,
            outs,
            scratch,
            1,
            spot,
            *arrays,
            *held,
            work=1,
            vmem=40,
            hbm_in=len(held),
            hbm_out=len(outs),
            aliases=aliases,
        )


def call(kernel, outs, scratch, scalars, *arrays, work=0.5, vmem=0, hbm_in=0, hbm_out=0, aliases=None):
    plain = len(arrays) - scalars - hbm_in
    if not vmem:
        blocks = [(array.shape, array.dtype) for array in arrays[scalars:]] + outs
        blocks = blocks + [entry for entry in scratch if isinstance(entry, tuple)]
        vmem = max(16, sum(math.prod(shape) * jnp.dtype(kind).itemsize for shape, kind in blocks) // MIB + 7)
    specs = [pl.BlockSpec(memory_space=pltpu.SMEM)] * scalars
    specs = specs + [pl.BlockSpec(memory_space=pltpu.VMEM)] * plain
    specs = specs + [pl.BlockSpec(memory_space=pl.ANY)] * hbm_in
    out_specs = [pl.BlockSpec(memory_space=pltpu.VMEM)] * (len(outs) - hbm_out)
    out_specs = out_specs + [pl.BlockSpec(memory_space=pl.ANY)] * hbm_out
    return pl.pallas_call(
        kernel,
        out_shape=[jax.ShapeDtypeStruct(shape, kind) for shape, kind in outs],
        in_specs=specs,
        out_specs=out_specs,
        scratch_shapes=[pltpu.VMEM(*entry) if isinstance(entry, tuple) else entry for entry in scratch],
        input_output_aliases=aliases or {},
        compiler_params=pltpu.CompilerParams(vmem_limit_bytes=vmem * MIB),
        cost_estimate=pl.CostEstimate(flops=int(work * 1e9), bytes_accessed=int(work * 3e6), transcendentals=0),
    )(*arrays)


def middle(
    groups, first_sum, stats, spot, tgt_len, src_len, hidden_one, query, part, part_top, part_sum, wkv_cross,
    ln_gain, ln_bias, wo_cross, w_up, w_down, grad_out, pair_mine, came,
):
    rows, width = hidden_one.shape
    half, tiles = rows // 2, rows // TILE
    hidden_width = w_down.shape[0]
    count, places, _ = pair_mine.shape
    away = places // groups * (groups - 1)
    arrays = [spot, tgt_len, src_len, hidden_one, query, part, part_top, part_sum, wkv_cross, ln_gain, ln_bias]
    stay = [wo_cross, w_up, w_down, grad_out, pair_mine]

    def kernel(*refs):
        ins, refs = refs[: len(arrays)], refs[len(arrays) :]
        came_refs, refs = refs[: len(came)], refs[len(came) :]
        stay_refs, refs = refs[: len(stay)], refs[len(stay) :]
        outs, refs = refs[:9], refs[9:]
        middle_kernel(groups, *ins, *stay_refs, *came_refs, *outs[:3], *outs[6:8], *outs[3:6], outs[8], *refs)

    result_out, cross_norm, cross_along, grad_hidden_two, grad_attn, ln_part, keep_one, send_one, pair_all = call(
        kernel,
        [
            ((rows, width), BF16),
            (stats, F32),
            (stats, F32),
            ((rows, width), F32),
            ((rows, width), BF16),
            ((4, width), F32),
            ((first_sum.rows, width), BF16),
            ((first_sum.rows, width), BF16),
            ((count, places, 2 * width), BF16),
        ],
        [
            ((width, width), BF16),
            ((width, hidden_width), BF16),
            ((hidden_width, width), BF16),
            ((rows, width), BF16),
            ((count, away, 2 * width), BF16),
            ((2, first_sum.rows, width), BF16),
            ((count, away, 2 * TILE), F32),
            ((tiles, 2 * TILE, width), BF16),
            ((count, width, away), BF16),
            ((width, rows), F32),
            ((rows, hidden_width), BF16),
            ((rows, hidden_width), F32),
            ((rows, hidden_width), BF16),
            pltpu.SemaphoreType.DMA((4,)),
            pltpu.SemaphoreType.DMA((count,)),
            pltpu.SemaphoreType.DMA((4,)),
        ],
        3,
        *arrays,
        *came,
        *stay,
        vmem=60,
        hbm_in=len(stay),
        hbm_out=3,
        aliases={len(arrays) + len(came) + len(stay) - 1: 8},
    )
    return result_out, cross_norm, cross_along, keep_one, send_one, grad_hidden_two, grad_attn, ln_part, pair_all


def body(
    target,
    memory,
    grad_out,
    tgt_len,
    src_len,
    w_qkv,
    w_out,
    wq_cross,
    wkv_cross,
    wo_cross,
    w_up,
    w_down,
    ln_gain,
    ln_bias,
):
    rows, width = target.shape
    half = rows // 2
    tiles = rows // TILE
    hidden_width = w_down.shape[0]
    groups = lax.axis_size("mem")
    me = lax.axis_index("mem")
    count = tgt_len.shape[1]
    span = memory.shape[1]
    places, away = groups * span, (groups - 1) * span
    dp = lax.axis_index("dp")
    short = width // 2
    first_sum = Summing(
        hidden_width + short,
        width,
        False,
        (("x", "mem", "near", "far"), ("near", "far", "x", "mem")),
        (("far", "near", "mem", "x"), ("far", "near", "x", "mem")),
    )
    second_sum = Summing(
        3 * width + short, width, True, (("x", "mem", "z"), ("mem", "x", "z")), (("z", "mem", "x"), ("z", "x", "mem"))
    )
    spot, spot_two = first_sum.spot(me, dp), second_sum.spot(me, dp)
    stats = (PAIRS * tiles, 2 * TILE)

    came = []
    for shift in range(1, groups):
        pairs = [(i, (i + shift) % groups) for i in range(groups)]
        sent = lax.dynamic_slice_in_dim(memory, ((me + shift) % groups) * count, count, 0)
        came.append(lax.ppermute(sent, "mem", pairs))

    sorted_rows, qkv, self_norm, self_attn_t, hidden_one, query, part, part_top, part_sum, pair_mine = call(
        functools.partial(self_forward_kernel, groups),
        [
            ((rows, width), BF16),
            ((rows, 3 * width), BF16),
            (stats, F32),
            ((width, rows), BF16),
            ((rows, width), F32),
            ((rows, width), BF16),
            ((width, rows), F32),
            (stats, F32),
            (stats, F32),
            ((count, places, 2 * width), BF16),
        ],
        [
            ((tiles, half, 2 * TILE), F32),
            ((count, span, 2 * TILE), F32),
            ((tiles, 2 * TILE, width), BF16),
            ((width, rows), BF16),
            ((count, width, span), BF16),
            ((count, span, 2 * width), BF16),
            pltpu.SemaphoreType.DMA((count,)),
        ],
        3,
        spot,
        tgt_len,
        src_len,
        target,
        w_qkv,
        w_out,
        wq_cross,
        ln_gain,
        ln_bias,
        memory,
        wkv_cross,
        vmem=60,
        hbm_out=1,
    )
    result_out, cross_norm, cross_along, keep_one, send_one, grad_hidden_two, grad_attn, ln_part, pair_all = middle(
        groups, first_sum, stats, spot, tgt_len, src_len, hidden_one, query, part, part_top, part_sum, wkv_cross,
        ln_gain, ln_bias, wo_cross, w_up, w_down, grad_out, pair_mine, came,
    )
    came_one = first_sum.core_swap(send_one)

    def cross_backward(block):
        sentences = 1 if block == 0 else count - 1
        return call(
            functools.partial(cross_backward_kernel, groups, block),
            [((sentences, places, 2 * width), BF16), ((width, half), BF16)],
            [
                ((sentences, places, 2 * width), BF16),
                ((sentences, places, 2 * TILE), F32),
                ((half // TILE, 2 * TILE, width), BF16),
                ((half // TILE, 2 * TILE, width), BF16),
                ((sentences, width, places), BF16),
                ((SLAB, half), F32),
                ((sentences, places, 2 * SLAB), F32),
                pltpu.SemaphoreType.DMA((1,)),
            ],
            3,
            spot,
            tgt_len,
            src_len,
            query,
            cross_norm,
            cross_along,
            grad_attn,
            pair_all,
            work=10,
            vmem=58 if block == 0 else 32,
            hbm_in=1,
        )

    pair_grad_long, query_grad_t_long = cross_backward(0)
    came_one, pair_grad_long = lax.optimization_barrier((came_one, pair_grad_long))
    parts_one = first_sum.first_split(spot, keep_one, came_one)
    parts_one, pair_all = lax.optimization_barrier((parts_one, pair_all))
    parts_one = first_sum.swap(parts_one, 0)
    pair_grad_rest, query_grad_t_rest = cross_backward(1)
    (wkv_grad,) = call(
        functools.partial(memory_weight_kernel, groups),
        [((2, width, width), BF16)],
        [((width, 2 * width), F32)],
        2,
        spot,
        tgt_len,
        pair_grad_long,
        pair_grad_rest,
        memory,
        *came,
        work=1,
        vmem=32,
    )
    keep_mid, send_mid, grad_hidden_one, grad_self = call(
        first_norm_backward_kernel,
        [
            ((2 * width + LN_ROWS, width), BF16),
            ((2 * width + LN_ROWS, width), BF16),
            ((rows, width), F32),
            ((rows, width), BF16),
        ],
        [],
        1,
        spot,
        hidden_one,
        query_grad_t_long,
        query_grad_t_rest,
        grad_hidden_two,
        wq_cross,
        w_out,
        self_attn_t,
        ln_gain,
        ln_bias,
        ln_part,
        wkv_grad,
        work=0.1,
        vmem=24,
    )

    def memory_grad(pieces, pair_grad_long, work=0.01):
        return call(
            functools.partial(memory_grad_kernel, pieces),
            [((count, size, width), BF16) for _, size in pieces],
            [],
            2,
            spot,
            tgt_len,
            pair_grad_long,
            pair_grad_rest,
            wkv_cross,
            work=work,
            vmem=32,
        )

    def send_back(grads):
        return [
            lax.ppermute(array, "mem", [(k, (k - 1 - i) % groups) for k in range(groups)])
            for i, array in enumerate(grads)
        ]

    parts_one, grad_self = lax.optimization_barrier((parts_one, grad_self))
    parts_one = first_sum.split(1, spot, parts_one)
    parts_one, grad_self, pair_grad_long = lax.optimization_barrier((parts_one, grad_self, pair_grad_long))
    parts_one = first_sum.swap(parts_one, 1)
    grad_late = memory_grad(
        [(part * span + span // 2, span // 2) for part in range(1, groups)], pair_grad_long
    )
    backs_late = send_back(grad_late)
    grad_late, grad_self = lax.optimization_barrier((grad_late, grad_self))
    grad_triple, *last = call(
        self_backward_kernel,
        [((rows, 3 * width), BF16)] + [(((width + short) // LAST_PARTS, width), BF16)] * (2 * LAST_PARTS),
        [
            ((tiles, half, 2 * TILE), F32),
            ((tiles, 2 * TILE, width), BF16),
            ((tiles, 2 * TILE, width), BF16),
            ((width, rows), BF16),
            ((width, rows), BF16),
        ],
        2,
        spot,
        tgt_len,
        qkv,
        self_norm,
        grad_self,
        sorted_rows,
        work=0.1,
        vmem=28,
    )
    came_mid = second_sum.core_swap(send_mid)
    last, came_mid, pair_grad_long = lax.optimization_barrier((last, came_mid, pair_grad_long))
    keep_last = last[:LAST_PARTS]
    came_last = [second_sum.core_swap(part) for part in last[LAST_PARTS:]]
    parts_one, _ = lax.optimization_barrier((parts_one, keep_last))
    parts_one = first_sum.split(2, spot, parts_one)
    came_mid, _ = lax.optimization_barrier((came_mid, parts_one))
    parts_two = second_sum.first_split(
        spot_two, keep_mid, came_mid, *[part for both in zip(keep_last, came_last) for part in both]
    )
    parts_one = first_sum.swap(parts_one, 2)
    grad_triple, _ = lax.optimization_barrier((grad_triple, parts_two))
    parts_two = second_sum.swap(parts_two, 0)
    backs_late, grad_triple = lax.optimization_barrier((backs_late, grad_triple))
    (grad_target,) = call(
        target_kernel,
        [((rows, width), BF16)],
        [],
        2,
        spot,
        tgt_len,
        grad_triple,
        w_qkv,
        grad_hidden_one,
        work=30,
        vmem=16,
    )
    parts_one, grad_target = lax.optimization_barrier((parts_one, grad_target))
    parts_one = first_sum.split(3, spot, parts_one)
    pair_grad_long, _ = lax.optimization_barrier((pair_grad_long, parts_one))
    parts_one = first_sum.swap(parts_one, 3)
    grad_mine, *grad_away = memory_grad(
        [(0, span)] + [(part * span, span // 2) for part in range(1, groups)], pair_grad_long, 5
    )
    parts_one, grad_away = lax.optimization_barrier((parts_one, grad_away))
    sum_one = first_sum.total(parts_one)[0]
    spread_one = first_sum.spread(0, sum_one)
    parts_two, _ = lax.optimization_barrier((parts_two, sum_one))
    parts_two = second_sum.split(1, spot_two, parts_two)
    spread_one, _ = lax.optimization_barrier((spread_one, parts_two))
    parts_two = second_sum.swap(parts_two, 1)
    joined_one = first_sum.join(0, spot, spread_one)
    spread_one = first_sum.spread(1, joined_one)
    parts_two, _ = lax.optimization_barrier((parts_two, joined_one))
    parts_two = second_sum.split(2, spot_two, parts_two)
    spread_one, _ = lax.optimization_barrier((spread_one, parts_two))
    parts_two = second_sum.swap(parts_two, 2)
    joined_one = first_sum.join(1, spot, spread_one)
    grad_away, _ = lax.optimization_barrier((grad_away, joined_one))
    spread_one = first_sum.spread(2, joined_one)
    backs_early = send_back(grad_away)
    joined_one = first_sum.join(2, spot, spread_one)
    spread_one = first_sum.spread(3, joined_one)
    parts_two, _ = lax.optimization_barrier((parts_two, joined_one))
    sum_two, *norm_sums = second_sum.total(parts_two, work=0.01)
    spread_two = second_sum.spread(0, sum_two)
    spread_two, backs_early = lax.optimization_barrier((spread_two, backs_early))
    spread_two = second_sum.spread(1, second_sum.join(0, spot_two, spread_two, work=6))
    joined_two = second_sum.join(1, spot_two, spread_two)
    spread_one, joined_two = lax.optimization_barrier((spread_one, joined_two))
    other_one = [first_sum.core_swap(array) for array in spread_one]
    chunks = hidden_width // width
    pieces = []
    for chunk in range(chunks):
        side, here = chunk // (chunks // 2), chunk % (chunks // 2)
        pieces.append((side, here * width, width, 0, chunk * width, 0))
        pieces.append((side, (chunks // 2 + here) * width, width, 1, 0, chunk * width))
    for side in range(2):
        pieces.append((side, chunks * width, short, 2, side * short, 0))
    grad_w_down, grad_w_up, grad_wo = first_sum.finish(
        spot,
        spread_one,
        other_one,
        list(range(len(spread_one))),
        pieces,
        [((hidden_width, width), F32), ((width, hidden_width), F32), ((width, width), F32)],
    )
    spread_two = second_sum.spread(2, joined_two)
    pieces = [
        (0, 0, width, 0, 0, 0),
        (0, width, width, 1, 0, 0),
        (0, 2 * width, width, 2, 0, 0),
        (0, 3 * width, short, 2, 0, width),
        (1, 0, width, 1, 0, width),
        (1, width, width, 3, 0, 0),
        (1, 2 * width, short, 2, short, width),
        (1, 2 * width + short, width, 2, 0, 2 * width),
    ]
    outs = [
        ((width, width), F32),
        ((width, 2 * width), F32),
        ((width, 3 * width), F32),
        ((width, width), F32),
    ]
    other_two = [second_sum.core_swap(spread_two[0])]
    own_two, grad_w_down = lax.optimization_barrier((spread_two[0], grad_w_down))
    held = second_sum.finish(spot_two, [own_two], other_two, [0], pieces, outs)
    spread_two, held = lax.optimization_barrier((spread_two, held))
    other_two = other_two + [second_sum.core_swap(array) for array in spread_two[1:]]
    grad_wq, grad_wkv, grad_w_qkv, grad_w_out = second_sum.finish(
        spot_two, spread_two, other_two, list(range(1, len(spread_two))), pieces, outs, held
    )
    grad_memory = jnp.zeros(memory.shape, BF16)
    grad_memory = lax.dynamic_update_slice(grad_memory, grad_mine, (me * count, 0, 0))
    for part, backs in enumerate((backs_early, backs_late)):
        for i, grads in enumerate(backs):
            owner = (me + i + 1) % groups
            grad_memory = lax.dynamic_update_slice(grad_memory, grads, (owner * count, part * (span // 2), 0))
    return (
        result_out,
        grad_target,
        grad_memory,
        grad_w_qkv,
        grad_w_out,
        grad_wq,
        grad_wkv,
        grad_wo,
        grad_w_up,
        grad_w_down,
        *norm_sums,
    )


def solution(mesh):
    rows_spec = P(("dp", "mem"), None)
    memory_spec = P("dp", "mem", None)
    return jax.shard_map(
        body,
        mesh=mesh,
        in_specs=(rows_spec, memory_spec, rows_spec, P("dp", None), P("dp", None)) + (P(),) * 9,
        out_specs=(rows_spec, rows_spec, memory_spec) + (P(),) * 9,
        check_vma=False,
    )
```

```python
import functools
import math

import jax
import jax.numpy as jnp
from jax import lax
from jax.experimental import pallas as pl
from jax.experimental.pallas import tpu as pltpu
from jax.sharding import PartitionSpec as P

HEADS = 8
PAIRS = HEADS // 2
SLAB = 128
SIDE = SLAB // 2
TILE = 128
MASKED = -1e30
EPSILON = 1e-05
F32 = jnp.float32
BF16 = jnp.bfloat16
MIB = 1024 * 1024
LN_ROWS = 16
LAST_PARTS = 2


def dot(left, right):
    return jnp.dot(left, right, preferred_element_type=F32)


def dot_nt(left, right):
    return lax.dot_general(left, right, (((1,), (1,)), ((), ())), preferred_element_type=F32)


def dot_tn(left, right):
    return lax.dot_general(left, right, (((0,), (0,)), ((), ())), preferred_element_type=F32)


def iota(shape, axis):
    return lax.broadcasted_iota(jnp.int32, shape, axis)


def norm_parts(hidden):
    centre = hidden - jnp.mean(hidden, axis=-1, keepdims=True)
    inverse = lax.rsqrt(jnp.mean(centre * centre, axis=-1, keepdims=True) + EPSILON)
    return centre * inverse, inverse


def norm_backward(upstream, unit, inverse, gain_row):
    scaled = upstream * gain_row
    shifted = (
        scaled
        - jnp.mean(scaled, axis=-1, keepdims=True)
        - unit * jnp.mean(scaled * unit, axis=-1, keepdims=True)
    )
    gain_grad = jnp.sum(upstream * unit, axis=0, keepdims=True)
    return inverse * shifted, gain_grad, jnp.sum(upstream, axis=0, keepdims=True)


def sentence_order(me, len_ref):
    count = len_ref.shape[1]
    lengths = [len_ref[me, k] for k in range(count)]
    longest, best, start, running = jnp.int32(0), lengths[0], jnp.int32(0), jnp.int32(0)
    for k in range(1, count):
        running = running + lengths[k - 1]
        more = lengths[k] > best
        longest = jnp.where(more, k, longest)
        start = jnp.where(more, running, start)
        best = jnp.where(more, lengths[k], best)
    order = [longest] + [jnp.where(k < longest, k, k + 1) for k in range(count - 1)]
    bounds = [jnp.int32(0)]
    for k in range(1, count):
        bounds.append(bounds[-1] + len_ref[me, order[k]])
    return order, start, bounds


def moved_rows(index, start, half):
    return jnp.where(index < start, index + half, jnp.where(index < start + half, index - start, index))


def sort_matrix(rows, start):
    spot = moved_rows(iota((rows, rows), 1), start, rows // 2)
    return jnp.where(spot == iota((rows, rows), 0), 1.0, 0.0).astype(BF16)


def unsort_matrix(rows, start):
    spot = moved_rows(iota((rows, rows), 0), start, rows // 2)
    return jnp.where(spot == iota((rows, rows), 1), 1.0, 0.0).astype(BF16)


def side_masks(width):
    side = iota((1, width), 1) % SLAB
    first = jnp.where(side < SLAB // 2, 1.0, 0.0)
    return first.astype(BF16), (1.0 - first).astype(BF16)


def each_pair(step):
    def advance(pair, carry):
        step(pair)
        return carry

    lax.fori_loop(0, PAIRS, advance, 0)


def slab_of(pair, first=0):
    if isinstance(pair, int):
        return pl.ds(first + pair * SLAB, SLAB)
    return pl.ds(pl.multiple_of(first + pair * SLAB, SLAB), SLAB)


def pack_heads(out_ref, rows, width):
    even, odd = side_masks(width)
    for t in range(out_ref.shape[0]):
        tile = rows(t * TILE, TILE)
        out_ref[t, :TILE, :] = tile * even
        out_ref[t, TILE:, :] = tile * odd


def fill_self_bias(bias_ref, bounds, half):
    for t in range(bias_ref.shape[0]):
        block, inner = t // (half // TILE), t % (half // TILE)
        key = iota((half, 2 * TILE), 0)
        query = iota((half, 2 * TILE), 1) % TILE + inner * TILE
        allowed = key <= query
        if block == 1:
            first = jnp.zeros((half, 2 * TILE), jnp.int32)
            for bound in bounds[1:-1]:
                first = jnp.where(query >= bound, bound, first)
            allowed = allowed & (key >= first)
        bias_ref[t] = jnp.where(allowed, 0.0, MASKED)


def self_keys(t, half):
    per = half // TILE
    return (t // per) * half, (t % per + 1) * TILE


def fill_live_bias(bias_ref, me, groups, parts, span, src_ref, sentences):
    key = iota((span, bias_ref.shape[2]), 0)
    for j, sentence in enumerate(sentences):
        for i, part in enumerate(parts):
            place = lax.rem(me - part + groups, groups) * span + key
            live = place < src_ref[me, sentence]
            bias_ref[j, pl.ds(i * span, span), :] = jnp.where(live, 0.0, MASKED)


def cross_units(bounds, half):
    units = [(t, 0, None) for t in range(half // TILE)]
    middle = half // 2
    last = jnp.int32(1)
    for bound in bounds[1:-1]:
        last = last + jnp.where(bound < middle, 1, 0)
    ends = bounds[1:]
    column = iota((1, 2 * TILE), 1) % TILE
    for u in range(len(ends) + 1):
        early = u < last
        sentence = jnp.where(early, u + 1, u)
        tile = jnp.where(early, 0, 1)
        low, high = jnp.int32(0), ends[0]
        for k in range(1, len(ends)):
            low = jnp.where(sentence == k + 1, ends[k - 1], low)
            high = jnp.where(sentence == k + 1, ends[k], high)
        row = column + tile * TILE
        units.append((tile + half // TILE, sentence, (row >= low) & (row < high)))
    return units


def own_sides(both):
    return jnp.concatenate([both[:SIDE, :TILE], both[SIDE:, TILE:]], axis=0)


def side_rows(row):
    even = jnp.broadcast_to(row[:, :TILE], (SIDE, TILE))
    return jnp.concatenate([even, jnp.broadcast_to(row[:, TILE:], (SIDE, TILE))], axis=0)


def tile_columns(tile):
    if isinstance(tile, int):
        return pl.ds(tile * TILE, TILE)
    return pl.ds(pl.multiple_of(tile * TILE, TILE), TILE)


def self_forward_kernel(
    groups,
    me_ref,
    len_ref,
    src_ref,
    target_ref,
    grad_out_ref,
    w_qkv_ref,
    w_out_ref,
    wq_ref,
    gain_ref,
    bias_row_ref,
    memory_ref,
    wkv_ref,
    sorted_ref,
    qkv_ref,
    norm_ref,
    attn_t_ref,
    hidden_ref,
    normed_ref,
    grad_sorted_ref,
    query_ref,
    part_ref,
    top_ref,
    sum_ref,
    pair_out_ref,
    bias_ref,
    live_ref,
    q_pack_ref,
    value_t_ref,
    cross_value_t_ref,
    pair_ref,
    copy_sem,
):
    rows, width = target_ref.shape
    half = rows // 2
    me = me_ref[0]
    order, start, bounds = sentence_order(me, len_ref)
    count, span = pair_ref.shape[0], pair_ref.shape[1]
    copies = []
    for j in range(count):
        block = memory_ref[me * count + order[j]]
        pair_ref[j] = dot(block, wkv_ref[...]).astype(BF16)
        copy = pltpu.make_async_copy(
            pair_ref.at[j], pair_out_ref.at[j, pl.ds(0, span), :], copy_sem.at[j]
        )
        copy.start()
        copies.append(copy)
    sorting = sort_matrix(rows, start)
    grad_sorted_ref[...] = dot(sorting, grad_out_ref[...]).astype(BF16)
    sorted_rows = dot(sorting, target_ref[...]).astype(BF16)
    sorted_ref[...] = sorted_rows
    fill_self_bias(bias_ref, bounds, half)
    queries = (dot(sorted_rows, w_qkv_ref[:, :width]).astype(BF16) * 0.125).astype(BF16)
    qkv_ref[:, :width] = queries
    pack_heads(q_pack_ref, lambda first, size: queries[first : first + size], width)
    qkv_ref[:, width : 2 * width] = dot(sorted_rows, w_qkv_ref[:, width : 2 * width]).astype(BF16)
    values = dot(sorted_rows, w_qkv_ref[:, 2 * width :]).astype(BF16)
    qkv_ref[:, 2 * width :] = values
    value_t_ref[...] = values.T
    tiles = rows // TILE

    def self_step(pair):
        slab = slab_of(pair)
        for t in range(tiles):
            first, size = self_keys(t, half)
            keys = qkv_ref[pl.ds(first, size), slab_of(pair, width)]
            scores = dot_nt(keys, q_pack_ref[t, :, slab]) + bias_ref[t, :size, :]
            top = jnp.max(scores, axis=0, keepdims=True)
            weights = jnp.exp(scores - top)
            total = jnp.sum(weights, axis=0, keepdims=True)
            probs = (weights * (1.0 / total)).astype(BF16)
            both = dot(value_t_ref[slab, pl.ds(first, size)], probs)
            attn_t_ref[slab, tile_columns(t)] = own_sides(both).astype(BF16)
            norm_ref[pl.ds(pair * tiles + t, 1), :] = top + jnp.log(total)

    each_pair(self_step)
    hidden = sorted_rows.astype(F32) + dot(attn_t_ref[...].T, w_out_ref[...])
    hidden_ref[...] = hidden
    unit, _ = norm_parts(hidden)
    normed = unit * gain_ref[0:1] + bias_row_ref[0:1]
    normed_ref[...] = normed
    normed = normed.astype(BF16)
    query_ref[...] = (dot(normed, wq_ref[...]).astype(BF16) * 0.125).astype(BF16)

    pack_heads(q_pack_ref, lambda first, size: query_ref[first : first + size, :], width)
    fill_live_bias(live_ref, me, groups, [0], span, src_ref, order)
    for j in range(count):
        cross_value_t_ref[j] = pair_ref[j, :, width:].T
    units = cross_units(bounds, half)

    def cross_step(pair):
        slab = slab_of(pair)
        for tile, sentence, columns in units:
            scores = dot_nt(pair_ref[sentence, :, slab], q_pack_ref[tile, :, slab]) + live_ref[sentence]
            top = jnp.max(scores, axis=0, keepdims=True)
            weights = jnp.exp(scores - top)
            total = jnp.sum(weights, axis=0, keepdims=True)
            result = own_sides(dot(cross_value_t_ref[sentence, slab, :], weights.astype(BF16)))
            here = tile_columns(tile)
            row = pl.ds(pair * tiles + tile, 1)
            if columns is not None:
                result = jnp.where(columns[:, :TILE], result, part_ref[slab, here])
                top = jnp.where(columns, top, top_ref[row, :])
                total = jnp.where(columns, total, sum_ref[row, :])
            part_ref[slab, here] = result
            top_ref[row, :] = top
            sum_ref[row, :] = total

    part_ref[...] = jnp.zeros_like(part_ref)
    top_ref[...] = jnp.zeros_like(top_ref)
    sum_ref[...] = jnp.ones_like(sum_ref)
    each_pair(cross_step)
    for copy in copies:
        copy.wait()


def middle_kernel(
    groups,
    me_ref,
    len_ref,
    src_ref,
    normed_one_ref,
    query_ref,
    part_ref,
    top_ref,
    sum_ref,
    wkv_ref,
    gain_ref,
    bias_row_ref,
    wo_hbm,
    w_up_hbm,
    w_down_hbm,
    grad_out_hbm,
    pair_in_hbm,
    *refs,
):
    came_refs = refs[: groups - 1]
    (
        out_ref,
        norm_ref,
        along_ref,
        keep_hbm,
        send_hbm,
        grad_hidden_ref,
        grad_attn_ref,
        ln_ref,
        pair_hbm,
        wo_ref,
        w_up_ref,
        w_down_ref,
        grad_out_ref,
        pair_ref,
        halves_ref,
        live_ref,
        q_pack_ref,
        value_t_ref,
        attn_t_ref,
        active_ref,
        slope_ref,
        grad_upper_ref,
        load_sem,
        pair_sem,
        store_sem,
    ) = refs[groups - 1 :]
    rows, width = normed_one_ref.shape
    half = rows // 2
    me = me_ref[0]
    count, away = pair_ref.shape[0], pair_ref.shape[1]
    span = away // (groups - 1)
    loads = [
        pltpu.make_async_copy(source, there, load_sem.at[i])
        for i, (source, there) in enumerate(
            [(wo_hbm, wo_ref), (w_up_hbm, w_up_ref), (w_down_hbm, w_down_ref), (grad_out_hbm, grad_out_ref)]
        )
    ]
    for copy in loads:
        copy.start()
    order, start, bounds = sentence_order(me, len_ref)
    fill_live_bias(live_ref, me, groups, list(range(1, groups)), span, src_ref, order)
    pack_heads(q_pack_ref, lambda first, size: query_ref[first : first + size, :], width)
    pair_copies = []
    for j in range(count):
        for part in range(1, groups):
            block = came_refs[part - 1][order[j]]
            pair_ref[j, pl.ds((part - 1) * span, span), :] = dot(block, wkv_ref[...]).astype(BF16)
        value_t_ref[j] = pair_ref[j, :, width:].T
        copy = pltpu.make_async_copy(pair_ref.at[j], pair_hbm.at[j, pl.ds(span, away), :], pair_sem.at[j])
        copy.start()
        pair_copies.append(copy)
    units = cross_units(bounds, half)
    tiles = rows // TILE

    def cross_step(pair):
        slab = slab_of(pair)
        for tile, sentence, columns in units:
            here = tile_columns(tile)
            row = pl.ds(pair * tiles + tile, 1)
            scores = dot_nt(pair_ref[sentence, :, slab], q_pack_ref[tile, :, slab]) + live_ref[sentence]
            before = top_ref[row, :]
            top = jnp.maximum(jnp.max(scores, axis=0, keepdims=True), before)
            weights = jnp.exp(scores - top)
            scale = jnp.exp(before - top)
            total = jnp.sum(weights, axis=0, keepdims=True) + sum_ref[row, :] * scale
            result = own_sides(dot(value_t_ref[sentence, slab, :], weights.astype(BF16)))
            result = (result + part_ref[slab, here] * side_rows(scale)) * side_rows(1.0 / total)
            norm = top + jnp.log(total)
            if columns is not None:
                result = jnp.where(columns[:, :TILE], result, attn_t_ref[slab, here])
                norm = jnp.where(columns, norm, norm_ref[row, :])
            attn_t_ref[slab, here] = result
            norm_ref[row, :] = norm

    attn_t_ref[...] = jnp.zeros_like(attn_t_ref)
    norm_ref[...] = jnp.zeros_like(norm_ref)
    each_pair(cross_step)
    attn_t_low = attn_t_ref[...].astype(BF16)
    loads[0].wait()
    hidden_two = normed_one_ref[...] + dot(attn_t_low.T, wo_ref[...])
    unit_two, inverse_two = norm_parts(hidden_two)
    normed_two = unit_two * gain_ref[1:2] + bias_row_ref[1:2]
    normed_two_low = normed_two.astype(BF16)
    chunk = width
    chunks = w_down_ref.shape[0] // chunk
    loads[1].wait()
    loads[2].wait()

    def up_step(c, carry):
        cols = pl.ds(pl.multiple_of(c * chunk, chunk), chunk)
        upper = dot(normed_two_low, w_up_ref[:, cols])
        sigma = 0.5 * jnp.tanh(0.5 * upper) + 0.5
        active = (upper * sigma).astype(BF16)
        active_ref[:, cols] = active
        slope_ref[:, cols] = sigma * (1.0 + upper * (1.0 - sigma))
        return carry

    lax.fori_loop(0, chunks, up_step, 0)

    unit_three, inverse_three = norm_parts(normed_two + dot(active_ref[...], w_down_ref[...]))
    out_ref[...] = (unit_three * gain_ref[2:3] + bias_row_ref[2:3]).astype(BF16)
    loads[3].wait()
    upstream = grad_out_ref[...].astype(F32)
    grad_three, gain_three, bias_three = norm_backward(upstream, unit_three, inverse_three, gain_ref[2:3])
    grad_down = grad_three.astype(BF16)
    normed_two_t = normed_two_low.T

    def down_step(c, carry):
        cols = pl.ds(pl.multiple_of(c * chunk, chunk), chunk)
        grad_upper = (dot_nt(grad_down, w_down_ref[cols, :]) * slope_ref[:, cols]).astype(BF16)
        down_part = dot_tn(active_ref[:, cols], grad_down).astype(BF16)
        up_part = dot(normed_two_t, grad_upper).astype(BF16)
        half_index, here = c // (chunks // 2), lax.rem(c, chunks // 2)
        down_rows = pl.ds(pl.multiple_of(here * chunk, chunk), chunk)
        up_rows = pl.ds(pl.multiple_of((chunks // 2 + here) * chunk, chunk), chunk)
        halves_ref[half_index, down_rows, :] = down_part
        halves_ref[half_index, up_rows, :] = up_part
        grad_upper_ref[:, cols] = grad_upper
        return carry

    lax.fori_loop(0, chunks, down_step, 0)

    most = chunks * chunk
    core = me_ref[1]
    stores = [
        pltpu.make_async_copy(
            halves_ref.at[half_index, pl.ds(first, size)], there.at[pl.ds(first, size)], store_sem.at[i]
        )
        for i, (half_index, there, first, size) in enumerate(
            [
                (1 - core, send_hbm, 0, most),
                (core, keep_hbm, 0, most),
                (1 - core, send_hbm, most, halves_ref.shape[1] - most),
                (core, keep_hbm, most, halves_ref.shape[1] - most),
            ]
        )
    ]
    stores[0].start()
    stores[1].start()
    upstream_two = grad_three + dot_nt(grad_upper_ref[...], w_up_ref[...])
    grad_two, gain_two, bias_two = norm_backward(upstream_two, unit_two, inverse_two, gain_ref[1:2])
    grad_two_low = grad_two.astype(BF16)
    wo_grad = dot(attn_t_low, grad_two_low).astype(BF16)
    used = most + width // 2
    for half_index in range(2):
        piece = wo_grad[half_index * (width // 2) : (half_index + 1) * (width // 2)]
        halves_ref[half_index, pl.ds(most, width // 2), :] = piece
        if halves_ref.shape[1] > used:
            halves_ref[half_index, used:, :] = jnp.zeros((halves_ref.shape[1] - used, width), BF16)
    stores[2].start()
    stores[3].start()
    grad_hidden_ref[...] = grad_two
    grad_attn = dot_nt(grad_two_low, wo_ref[...]).astype(BF16)
    grad_attn_ref[...] = grad_attn
    product = grad_attn.T.astype(F32) * attn_t_ref[...]
    for pair in range(PAIRS):
        for side in range(2):
            first = pair * SLAB + side * SIDE
            along = jnp.sum(product[first : first + SIDE], axis=0, keepdims=True)
            for t in range(tiles):
                along_ref[pair * tiles + t : pair * tiles + t + 1, side * TILE : (side + 1) * TILE] = along[
                    :, t * TILE : (t + 1) * TILE
                ]
    ln_ref[...] = jnp.concatenate([gain_two, gain_three, bias_two, bias_three], axis=0)
    for copy in pair_copies + stores:
        copy.wait()


def cross_backward_kernel(
    groups,
    block,
    me_ref,
    len_ref,
    src_ref,
    query_ref,
    norm_ref,
    along_ref,
    grad_attn_ref,
    pair_hbm,
    pair_grad_ref,
    query_grad_t_ref,
    pair_ref,
    live_ref,
    q_pack_ref,
    g_pack_ref,
    key_t_ref,
    query_sum_ref,
    sum_ref,
    load_sem,
):
    rows, width = query_ref.shape
    half = rows // 2
    me = me_ref[0]
    sentences, places = pair_ref.shape[0], pair_ref.shape[1]
    first_sentence = 0 if block == 0 else 1
    load = pltpu.make_async_copy(pair_hbm.at[pl.ds(first_sentence, sentences)], pair_ref, load_sem.at[0])
    load.start()
    order, start, bounds = sentence_order(me, len_ref)
    mine = order[:1] if block == 0 else order[1:]
    fill_live_bias(live_ref, me, groups, list(range(groups)), places // groups, src_ref, mine)
    low = block * half
    pack_heads(q_pack_ref, lambda first, size: query_ref[low + first : low + first + size, :], width)
    pack_heads(g_pack_ref, lambda first, size: grad_attn_ref[low + first : low + first + size, :], width)
    tiles, per = rows // TILE, half // TILE
    units = cross_units(bounds, half)
    units = units[:per] if block == 0 else units[per:]
    load.wait()
    for j in range(sentences):
        key_t_ref[j] = pair_ref[j, :, :width].T

    def pair_step(pair):
        slab, value_slab = slab_of(pair), slab_of(pair, width)
        query_sum_ref[...] = jnp.zeros_like(query_sum_ref)
        sum_ref[...] = jnp.zeros_like(sum_ref)
        for tile, sentence, columns in units:
            j = sentence - first_sentence
            t = tile - block * per
            here = tile_columns(t)
            row = pl.ds(pair * tiles + tile, 1)
            q_rows, g_rows = q_pack_ref[t, :, slab], g_pack_ref[t, :, slab]
            norm = norm_ref[row, :]
            if columns is not None:
                norm = jnp.where(columns, norm, -MASKED)
            scores = dot_nt(pair_ref[j, :, slab], q_rows) + live_ref[j]
            probs = jnp.exp(scores - norm)
            grad_probs = dot_nt(pair_ref[j, :, value_slab], g_rows)
            grad_scores = (probs * (grad_probs - along_ref[row, :])).astype(BF16)
            sum_ref[j, :, :SLAB] += dot(grad_scores, q_rows)
            sum_ref[j, :, SLAB:] += dot(probs.astype(BF16), g_rows)
            query_sum_ref[:, here] += own_sides(dot(key_t_ref[j, slab, :], grad_scores))
        query_grad_t_ref[slab, :] = (query_sum_ref[...] * 0.125).astype(BF16)
        pair_grad_ref[:, :, slab] = sum_ref[:, :, :SLAB].astype(BF16)
        pair_grad_ref[:, :, value_slab] = sum_ref[:, :, SLAB:].astype(BF16)

    for pair in range(PAIRS):
        pair_step(pair)


def memory_weight_kernel(groups, me_ref, len_ref, pair_grad_long_ref, pair_grad_rest_ref, memory_ref, *refs):
    came_refs = refs[: groups - 1]
    wkv_grad_ref, total_ref = refs[groups - 1 :]
    width = memory_ref.shape[2]
    me = me_ref[0]
    count = len_ref.shape[1]
    span = pair_grad_long_ref.shape[1] // groups
    order, _, _ = sentence_order(me, len_ref)
    for j in range(count):
        pair_grad_ref, here = (pair_grad_long_ref, 0) if j == 0 else (pair_grad_rest_ref, j - 1)
        blocks = [memory_ref[me * count + order[j]]] + [ref[order[j]] for ref in came_refs]
        term = dot_tn(jnp.concatenate(blocks, axis=0), pair_grad_ref[here])
        if j == 0:
            total_ref[...] = term
        else:
            total_ref[...] += term
    wkv_grad_ref[0] = total_ref[:, :width].astype(BF16)
    wkv_grad_ref[1] = total_ref[:, width:].astype(BF16)


def memory_grad_kernel(pieces, me_ref, len_ref, pair_grad_long_ref, pair_grad_rest_ref, wkv_ref, *outs):
    count = len_ref.shape[1]
    order, _, _ = sentence_order(me_ref[0], len_ref)
    for j in range(count):
        pair_grad_ref, here = (pair_grad_long_ref, 0) if j == 0 else (pair_grad_rest_ref, j - 1)
        for (first, size), out in zip(pieces, outs):
            out[order[j]] = dot_nt(pair_grad_ref[here, pl.ds(first, size), :], wkv_ref[...]).astype(BF16)


def first_norm_backward_kernel(
    me_ref,
    hidden_one_ref,
    query_grad_t_long_ref,
    query_grad_t_rest_ref,
    grad_hidden_two_ref,
    wq_ref,
    w_out_ref,
    self_attn_t_ref,
    gain_ref,
    bias_row_ref,
    ln_in_ref,
    wkv_grad_ref,
    keep_ref,
    send_ref,
    grad_hidden_ref,
    grad_self_ref,
):
    width = wq_ref.shape[0]
    unit_one, inverse_one = norm_parts(hidden_one_ref[...])
    normed_one = (unit_one * gain_ref[0:1] + bias_row_ref[0:1]).astype(BF16)
    query_grad = jnp.concatenate([query_grad_t_long_ref[...].T, query_grad_t_rest_ref[...].T], axis=0)
    upstream = grad_hidden_two_ref[...] + dot_nt(query_grad, wq_ref[...])
    grad_one, gain_one, bias_one = norm_backward(upstream, unit_one, inverse_one, gain_ref[0:1])
    grad_hidden_ref[...] = grad_one
    grad_one_low = grad_one.astype(BF16)
    grad_self_ref[...] = dot_nt(grad_one_low, w_out_ref[...]).astype(BF16)
    wq_grad = dot_tn(normed_one, query_grad).astype(BF16)
    w_out_grad = dot(self_attn_t_ref[...], grad_one_low).astype(BF16)
    norms = jnp.concatenate(
        [gain_one, ln_in_ref[0:2], bias_one, ln_in_ref[2:4], jnp.zeros((LN_ROWS - 6, width), F32)], axis=0
    ).astype(BF16)

    def halves(low_ref, high_ref):
        low_ref[:width, :] = wq_grad
        low_ref[width : 2 * width, :] = wkv_grad_ref[0]
        high_ref[:width, :] = wkv_grad_ref[1]
        high_ref[width : 2 * width, :] = w_out_grad

    @pl.when(me_ref[1] == 0)
    def _():
        halves(keep_ref, send_ref)

    @pl.when(me_ref[1] != 0)
    def _():
        halves(send_ref, keep_ref)

    keep_ref[2 * width :, :] = norms
    send_ref[2 * width :, :] = norms


def self_backward_kernel(
    me_ref,
    len_ref,
    qkv_ref,
    norm_ref,
    grad_attn_ref,
    sorted_ref,
    grad_triple_ref,
    *refs,
):
    keep_refs, send_refs = refs[:LAST_PARTS], refs[LAST_PARTS : 2 * LAST_PARTS]
    self_backward(
        me_ref,
        len_ref,
        qkv_ref,
        norm_ref,
        grad_attn_ref,
        sorted_ref,
        grad_triple_ref,
        keep_refs,
        send_refs,
        *refs[2 * LAST_PARTS :],
    )


def self_backward(
    me_ref,
    len_ref,
    qkv_ref,
    norm_ref,
    grad_attn_ref,
    sorted_ref,
    grad_triple_ref,
    keep_refs,
    send_refs,
    bias_ref,
    q_pack_ref,
    g_pack_ref,
    key_t_ref,
    query_grad_t_ref,
):
    rows, width = sorted_ref.shape
    half = rows // 2
    _, _, bounds = sentence_order(me_ref[0], len_ref)
    fill_self_bias(bias_ref, bounds, half)
    pack_heads(q_pack_ref, lambda first, size: qkv_ref[first : first + size, :width], width)
    pack_heads(g_pack_ref, lambda first, size: grad_attn_ref[first : first + size, :], width)
    key_t_ref[...] = qkv_ref[:, width : 2 * width].T
    tiles, per = rows // TILE, half // TILE

    def pair_step(pair):
        slab, key_slab, value_slab = slab_of(pair), slab_of(pair, width), slab_of(pair, 2 * width)
        sums = [[None, None] for _ in range(tiles)]
        for t in range(tiles):
            first, size = self_keys(t, half)
            span = pl.ds(first, size)
            q_rows, g_rows = q_pack_ref[t, :, slab], g_pack_ref[t, :, slab]
            scores = dot_nt(qkv_ref[span, key_slab], q_rows) + bias_ref[t, :size, :]
            probs = jnp.exp(scores - norm_ref[pl.ds(pair * tiles + t, 1), :])
            grad_probs = dot_nt(qkv_ref[span, value_slab], g_rows)
            along = jnp.sum(probs * grad_probs, axis=0, keepdims=True)
            grad_scores = (probs * (grad_probs - along)).astype(BF16)
            parts = dot(grad_scores, q_rows), dot(probs.astype(BF16), g_rows)
            for i in range(size // TILE):
                spot = sums[first // TILE + i]
                for k in range(2):
                    piece = parts[k][i * TILE : (i + 1) * TILE]
                    spot[k] = piece if spot[k] is None else spot[k] + piece
            query_grad_t_ref[slab, tile_columns(t)] = (
                own_sides(dot(key_t_ref[slab, span], grad_scores)) * 0.125
            ).astype(BF16)
        for t in range(tiles):
            grad_triple_ref[pl.ds(t * TILE, TILE), key_slab] = sums[t][0].astype(BF16)
            grad_triple_ref[pl.ds(t * TILE, TILE), value_slab] = sums[t][1].astype(BF16)

    for pair in range(PAIRS):
        pair_step(pair)
    grad_triple_ref[:, :width] = query_grad_t_ref[...].T
    sorted_t = sorted_ref[...].T
    grads = [
        dot(sorted_t, grad_triple_ref[:, part * width : (part + 1) * width]).astype(BF16)
        for part in range(3)
    ]
    short = width // 2

    low = jnp.concatenate([grads[0], grads[1][:short]], axis=0)
    high = jnp.concatenate([grads[1][short:], grads[2]], axis=0)
    size = keep_refs[0].shape[0]

    def halves(low_refs, high_refs):
        for i in range(LAST_PARTS):
            low_refs[i][...] = low[i * size : (i + 1) * size]
            high_refs[i][...] = high[i * size : (i + 1) * size]

    @pl.when(me_ref[1] == 0)
    def _():
        halves(keep_refs, send_refs)

    @pl.when(me_ref[1] != 0)
    def _():
        halves(send_refs, keep_refs)


def target_kernel(me_ref, len_ref, grad_triple_ref, w_qkv_ref, grad_hidden_ref, sorted_ref, grad_target_ref, out_ref):
    rows = grad_hidden_ref.shape[0]
    _, start, _ = sentence_order(me_ref[0], len_ref)
    result = grad_hidden_ref[...] + dot_nt(grad_triple_ref[...], w_qkv_ref[...])
    unsorting = unsort_matrix(rows, start)
    grad_target_ref[...] = dot(unsorting, result.astype(BF16)).astype(BF16)
    out_ref[...] = dot(unsorting, sorted_ref[...]).astype(BF16)


def tree_sum(terms):
    while len(terms) > 1:
        terms = [terms[i] + terms[i + 1] for i in range(0, len(terms), 2)]
    return terms[0]


def rows_of(ref, first, count):
    return ref[pl.ds(pl.multiple_of(first, 16), count), :].astype(F32)


def first_split_kernel(segments, ln, peers, spot_ref, *refs):
    ins, outs, sum_ref = refs[: 2 * segments], refs[2 * segments : -1], refs[-1]
    extra = LN_ROWS if ln else 0
    size = outs[0].shape[0] - extra
    used = 0
    for i in range(segments):
        keep_ref, came_ref = ins[2 * i], ins[2 * i + 1]
        count = keep_ref.shape[0] - (extra if i == 0 else 0)
        sum_ref[used : used + count, :] = (rows_of(keep_ref, 0, count) + rows_of(came_ref, 0, count)).astype(BF16)
        if i == 0 and ln:
            tail = (rows_of(keep_ref, count, LN_ROWS) + rows_of(came_ref, count, LN_ROWS)).astype(BF16)
        used += count
    if sum_ref.shape[0] > used:
        sum_ref[used:, :] = jnp.zeros((sum_ref.shape[0] - used, sum_ref.shape[1]), BF16)
    for d, out in enumerate(outs):
        out[:size, :] = sum_ref[pl.ds(pl.multiple_of((spot_ref[2] ^ d) * size, 16), size), :]
        if ln:
            out[size:, :] = tail


def split_kernel(stage, ln, peers, spot_ref, *refs):
    ins, outs = refs[:peers], refs[peers:]
    extra = LN_ROWS if ln else 0
    size = outs[0].shape[0] - extra
    if ln:
        tail = tree_sum([rows_of(ref, size * len(outs), LN_ROWS) for ref in ins]).astype(BF16)
    for d, out in enumerate(outs):
        first = (spot_ref[2 + stage] ^ d) * size
        out[:size, :] = tree_sum([rows_of(ref, first, size) for ref in ins]).astype(BF16)
        if ln:
            out[size:, :] = tail


def total_kernel(ln, count, *refs):
    ins, outs = refs[:count], refs[count:]
    size = outs[0].shape[0]
    outs[0][...] = tree_sum([rows_of(ref, 0, size) for ref in ins]).astype(BF16)
    if ln:
        norms = tree_sum([rows_of(ref, size, LN_ROWS) for ref in ins])
        outs[1][...] = norms[:3]
        outs[2][...] = norms[3:6]


def join_kernel(stage, spot_ref, *refs):
    out_ref = refs[-1]
    for d, ref in enumerate(refs[:-1]):
        size = ref.shape[0]
        out_ref[pl.ds(pl.multiple_of((spot_ref[2 + stage] ^ d) * size, 16), size), :] = ref[...]


def finish_kernel(offsets, peers, twisted, pieces, held, spot_ref, *refs):
    arrays, refs = refs[: 2 * len(offsets)], refs[2 * len(offsets) + held :]
    outs, (wide_ref, sem) = refs[:-2], refs[-2:]
    core = spot_ref[1]
    size, width = wide_ref.shape[1:]
    copies = []
    for k, ref in enumerate(arrays):
        wide_ref[k] = ref[...].astype(F32)
        d, other = offsets[k // 2], k % 2
        half = 1 - core if other else core
        place = spot_ref[3 if twisted and other else 2] ^ d
        for i in range(2):
            for j in range(peers):
                cut = []
                for piece_half, first, rows, out, row, col in pieces:
                    low, high = max(first, j * size), min(first + rows, (j + 1) * size)
                    if piece_half == i and low < high:
                        there = outs[out].at[pl.ds(row + low - first, high - low), pl.ds(col, width)]
                        here = wide_ref.at[k, pl.ds(low - j * size, high - low), :]
                        cut.append(pltpu.make_async_copy(here, there, sem.at[k, len(cut)]))
                copies.append(((half == i) & (place == j), cut))
                _start_all(*copies[-1])
    for chosen, cut in copies:
        _wait_all(chosen, cut)


def _start_all(chosen, cut):
    @pl.when(chosen)
    def _():
        for copy in cut:
            copy.start()


def _wait_all(chosen, cut):
    @pl.when(chosen)
    def _():
        for copy in cut:
            copy.wait()


class Summing:
    def __init__(self, rows, width, ln):
        self.width, self.ln = width, ln
        self.dp, self.mem = lax.axis_size("dp"), lax.axis_size("mem")
        z_size = 4
        x_size = self.dp // (2 * z_size)
        self.sizes = (x_size, self.mem, z_size)
        self.twisted = x_size == self.mem
        self.chunk = -(-rows // (16 * math.prod(self.sizes))) * 16
        self.rows = self.chunk * math.prod(self.sizes)

    def after(self, stage):
        return self.rows // math.prod(self.sizes[:stage])

    def axis(self, stage, core):
        return 1 - stage if self.twisted and core == 1 and stage < 2 else stage

    def coords(self, dp, mem):
        return [dp // 2 % self.sizes[0], mem, dp // (2 * self.sizes[0])], dp % 2

    def spot(self, me, dp):
        (x, mem, z), core = self.coords(dp, me)
        if self.twisted:
            x, mem = jnp.where(core == 0, x, mem), jnp.where(core == 0, mem, x)
        return jnp.stack([me, core, x, mem, z]).astype(jnp.int32)

    def permute(self, array, stage, offset):
        pairs = []
        for dp in range(self.dp):
            for mem in range(self.mem):
                spots, core = self.coords(dp, mem)
                if stage is None:
                    core ^= offset
                else:
                    spots[self.axis(stage, core)] ^= offset
                to_dp = (spots[2] * self.sizes[0] + spots[0]) * 2 + core
                pairs.append((dp * self.mem + mem, to_dp * self.mem + spots[1]))
        return lax.ppermute(array, ("dp", "mem"), pairs)

    def core_swap(self, send):
        return self.permute(send, None, 1)

    def swap(self, arrays, stage):
        return [arrays[0]] + [self.permute(array, stage, d) for d, array in enumerate(arrays) if d > 0]

    def spread(self, stage, array):
        return [array] + [self.permute(array, stage, d) for d in range(1, self.sizes[stage])]

    def messages(self, stage):
        size = self.after(stage + 1) + (LN_ROWS if self.ln else 0)
        return [((size, self.width), BF16)] * self.sizes[stage]

    def first_split(self, spot, *arrays):
        kernel = functools.partial(first_split_kernel, len(arrays) // 2, self.ln, self.sizes[0])
        return call(kernel, self.messages(0), [((self.rows, self.width), BF16)], 1, spot, *arrays, work=0.01)

    def split(self, stage, spot, arrays, work=0.01):
        kernel = functools.partial(split_kernel, stage, self.ln, self.sizes[stage - 1])
        return call(kernel, self.messages(stage), [], 1, spot, *arrays, work=work)

    def total(self, arrays, work=0.01):
        outs = [((self.chunk, self.width), BF16)]
        if self.ln:
            outs = outs + [((3, self.width), F32)] * 2
        return call(functools.partial(total_kernel, self.ln, self.sizes[2]), outs, [], 0, *arrays, work=work)

    def join(self, stage, spot, arrays, work=0.01):
        outs = [((self.after(stage), self.width), BF16)]
        return call(functools.partial(join_kernel, stage), outs, [], 1, spot, *arrays, work=work)[0]

    def finish(self, spot, mine, others, offsets, pieces, outs, held=()):
        kernel = functools.partial(finish_kernel, offsets, self.sizes[0], self.twisted, pieces, len(held))
        arrays = [array for d in offsets for array in (mine[d], others[d])]
        size = self.after(1)
        scratch = [((len(arrays), size, self.width), F32), pltpu.SemaphoreType.DMA((len(arrays), len(pieces)))]
        aliases = {1 + len(arrays) + i: i for i in range(len(held))}
        return call(
            kernel,
            outs,
            scratch,
            1,
            spot,
            *arrays,
            *held,
            work=1,
            vmem=40,
            hbm_in=len(held),
            hbm_out=len(outs),
            aliases=aliases,
        )


def call(kernel, outs, scratch, scalars, *arrays, work=0.5, vmem=0, hbm_in=0, hbm_out=0, aliases=None):
    plain = len(arrays) - scalars - hbm_in
    if not vmem:
        blocks = [(array.shape, array.dtype) for array in arrays[scalars:]] + outs
        blocks = blocks + [entry for entry in scratch if isinstance(entry, tuple)]
        vmem = max(16, sum(math.prod(shape) * jnp.dtype(kind).itemsize for shape, kind in blocks) // MIB + 7)
    specs = [pl.BlockSpec(memory_space=pltpu.SMEM)] * scalars
    specs = specs + [pl.BlockSpec(memory_space=pltpu.VMEM)] * plain
    specs = specs + [pl.BlockSpec(memory_space=pl.ANY)] * hbm_in
    out_specs = [pl.BlockSpec(memory_space=pltpu.VMEM)] * (len(outs) - hbm_out)
    out_specs = out_specs + [pl.BlockSpec(memory_space=pl.ANY)] * hbm_out
    return pl.pallas_call(
        kernel,
        out_shape=[jax.ShapeDtypeStruct(shape, kind) for shape, kind in outs],
        in_specs=specs,
        out_specs=out_specs,
        scratch_shapes=[pltpu.VMEM(*entry) if isinstance(entry, tuple) else entry for entry in scratch],
        input_output_aliases=aliases or {},
        compiler_params=pltpu.CompilerParams(vmem_limit_bytes=vmem * MIB),
        cost_estimate=pl.CostEstimate(flops=int(work * 1e9), bytes_accessed=int(work * 3e6), transcendentals=0),
    )(*arrays)


def middle(
    groups, first_sum, stats, spot, tgt_len, src_len, normed_one, query, part, part_top, part_sum, wkv_cross,
    ln_gain, ln_bias, wo_cross, w_up, w_down, grad_out, pair_mine, came,
):
    rows, width = normed_one.shape
    half, tiles = rows // 2, rows // TILE
    hidden_width = w_down.shape[0]
    count, places, _ = pair_mine.shape
    away = places // groups * (groups - 1)
    arrays = [spot, tgt_len, src_len, normed_one, query, part, part_top, part_sum, wkv_cross, ln_gain, ln_bias]
    stay = [wo_cross, w_up, w_down, grad_out, pair_mine]

    def kernel(*refs):
        ins, refs = refs[: len(arrays)], refs[len(arrays) :]
        came_refs, refs = refs[: len(came)], refs[len(came) :]
        stay_refs, refs = refs[: len(stay)], refs[len(stay) :]
        outs, refs = refs[:9], refs[9:]
        middle_kernel(groups, *ins, *stay_refs, *came_refs, *outs[:3], *outs[6:8], *outs[3:6], outs[8], *refs)

    result_out, cross_norm, cross_along, grad_hidden_two, grad_attn, ln_part, keep_one, send_one, pair_all = call(
        kernel,
        [
            ((rows, width), BF16),
            (stats, F32),
            (stats, F32),
            ((rows, width), F32),
            ((rows, width), BF16),
            ((4, width), F32),
            ((first_sum.rows, width), BF16),
            ((first_sum.rows, width), BF16),
            ((count, places, 2 * width), BF16),
        ],
        [
            ((width, width), BF16),
            ((width, hidden_width), BF16),
            ((hidden_width, width), BF16),
            ((rows, width), BF16),
            ((count, away, 2 * width), BF16),
            ((2, first_sum.rows, width), BF16),
            ((count, away, 2 * TILE), F32),
            ((tiles, 2 * TILE, width), BF16),
            ((count, width, away), BF16),
            ((width, rows), F32),
            ((rows, hidden_width), BF16),
            ((rows, hidden_width), F32),
            ((rows, hidden_width), BF16),
            pltpu.SemaphoreType.DMA((4,)),
            pltpu.SemaphoreType.DMA((count,)),
            pltpu.SemaphoreType.DMA((4,)),
        ],
        3,
        *arrays,
        *came,
        *stay,
        vmem=60,
        hbm_in=len(stay),
        hbm_out=3,
        aliases={len(arrays) + len(came) + len(stay) - 1: 8},
    )
    return result_out, cross_norm, cross_along, keep_one, send_one, grad_hidden_two, grad_attn, ln_part, pair_all


def body(
    target,
    memory,
    grad_out,
    tgt_len,
    src_len,
    w_qkv,
    w_out,
    wq_cross,
    wkv_cross,
    wo_cross,
    w_up,
    w_down,
    ln_gain,
    ln_bias,
):
    rows, width = target.shape
    half = rows // 2
    tiles = rows // TILE
    hidden_width = w_down.shape[0]
    groups = lax.axis_size("mem")
    me = lax.axis_index("mem")
    count = tgt_len.shape[1]
    span = memory.shape[1]
    places, away = groups * span, (groups - 1) * span
    dp = lax.axis_index("dp")
    short = width // 2
    first_sum = Summing(hidden_width + short, width, False)
    second_sum = Summing(3 * width + short, width, True)
    spot = first_sum.spot(me, dp)
    stats = (PAIRS * tiles, 2 * TILE)

    came = []
    for shift in range(1, groups):
        pairs = [(i, (i + shift) % groups) for i in range(groups)]
        sent = lax.dynamic_slice_in_dim(memory, ((me + shift) % groups) * count, count, 0)
        came.append(lax.ppermute(sent, "mem", pairs))

    sorted_rows, qkv, self_norm, self_attn_t, hidden_one, normed_one, grad_sorted, query, part, part_top, part_sum, pair_mine = call(
        functools.partial(self_forward_kernel, groups),
        [
            ((rows, width), BF16),
            ((rows, 3 * width), BF16),
            (stats, F32),
            ((width, rows), BF16),
            ((rows, width), F32),
            ((rows, width), F32),
            ((rows, width), BF16),
            ((rows, width), BF16),
            ((width, rows), F32),
            (stats, F32),
            (stats, F32),
            ((count, places, 2 * width), BF16),
        ],
        [
            ((tiles, half, 2 * TILE), F32),
            ((count, span, 2 * TILE), F32),
            ((tiles, 2 * TILE, width), BF16),
            ((width, rows), BF16),
            ((count, width, span), BF16),
            ((count, span, 2 * width), BF16),
            pltpu.SemaphoreType.DMA((count,)),
        ],
        3,
        spot,
        tgt_len,
        src_len,
        target,
        grad_out,
        w_qkv,
        w_out,
        wq_cross,
        ln_gain,
        ln_bias,
        memory,
        wkv_cross,
        vmem=60,
        hbm_out=1,
    )
    result_sorted, cross_norm, cross_along, keep_one, send_one, grad_hidden_two, grad_attn, ln_part, pair_all = middle(
        groups, first_sum, stats, spot, tgt_len, src_len, normed_one, query, part, part_top, part_sum, wkv_cross,
        ln_gain, ln_bias, wo_cross, w_up, w_down, grad_sorted, pair_mine, came,
    )
    came_one = first_sum.core_swap(send_one)

    def cross_backward(block):
        sentences = 1 if block == 0 else count - 1
        return call(
            functools.partial(cross_backward_kernel, groups, block),
            [((sentences, places, 2 * width), BF16), ((width, half), BF16)],
            [
                ((sentences, places, 2 * width), BF16),
                ((sentences, places, 2 * TILE), F32),
                ((half // TILE, 2 * TILE, width), BF16),
                ((half // TILE, 2 * TILE, width), BF16),
                ((sentences, width, places), BF16),
                ((SLAB, half), F32),
                ((sentences, places, 2 * SLAB), F32),
                pltpu.SemaphoreType.DMA((1,)),
            ],
            3,
            spot,
            tgt_len,
            src_len,
            query,
            cross_norm,
            cross_along,
            grad_attn,
            pair_all,
            work=10,
            vmem=58 if block == 0 else 32,
            hbm_in=1,
        )

    pair_grad_long, query_grad_t_long = cross_backward(0)
    came_one, pair_grad_long = lax.optimization_barrier((came_one, pair_grad_long))
    parts_one = first_sum.first_split(spot, keep_one, came_one)
    parts_one, pair_all = lax.optimization_barrier((parts_one, pair_all))
    parts_one = first_sum.swap(parts_one, 0)
    pair_grad_rest, query_grad_t_rest = cross_backward(1)
    (wkv_grad,) = call(
        functools.partial(memory_weight_kernel, groups),
        [((2, width, width), BF16)],
        [((width, 2 * width), F32)],
        2,
        spot,
        tgt_len,
        pair_grad_long,
        pair_grad_rest,
        memory,
        *came,
        work=1,
        vmem=32,
    )
    keep_mid, send_mid, grad_hidden_one, grad_self = call(
        first_norm_backward_kernel,
        [
            ((2 * width + LN_ROWS, width), BF16),
            ((2 * width + LN_ROWS, width), BF16),
            ((rows, width), F32),
            ((rows, width), BF16),
        ],
        [],
        1,
        spot,
        hidden_one,
        query_grad_t_long,
        query_grad_t_rest,
        grad_hidden_two,
        wq_cross,
        w_out,
        self_attn_t,
        ln_gain,
        ln_bias,
        ln_part,
        wkv_grad,
        work=0.1,
        vmem=24,
    )
    def memory_grad(pieces, pair_grad_long):
        return call(
            functools.partial(memory_grad_kernel, pieces),
            [((count, size, width), BF16) for _, size in pieces],
            [],
            2,
            spot,
            tgt_len,
            pair_grad_long,
            pair_grad_rest,
            wkv_cross,
            work=0.01,
            vmem=32,
        )

    def send_back(grads):
        return [
            lax.ppermute(array, "mem", [(k, (k - 1 - i) % groups) for k in range(groups)])
            for i, array in enumerate(grads)
        ]

    parts_one, grad_self = lax.optimization_barrier((parts_one, grad_self))
    parts_one = first_sum.split(1, spot, parts_one)
    parts_one, grad_self, pair_grad_long = lax.optimization_barrier((parts_one, grad_self, pair_grad_long))
    parts_one = first_sum.swap(parts_one, 1)
    grad_late = memory_grad(
        [(part * span + span // 2, span // 2) for part in range(1, groups)], pair_grad_long
    )
    backs_late = send_back(grad_late)
    grad_late, grad_self = lax.optimization_barrier((grad_late, grad_self))
    grad_triple, *last = call(
        self_backward_kernel,
        [((rows, 3 * width), BF16)] + [(((width + short) // LAST_PARTS, width), BF16)] * (2 * LAST_PARTS),
        [
            ((tiles, half, 2 * TILE), F32),
            ((tiles, 2 * TILE, width), BF16),
            ((tiles, 2 * TILE, width), BF16),
            ((width, rows), BF16),
            ((width, rows), BF16),
        ],
        2,
        spot,
        tgt_len,
        qkv,
        self_norm,
        grad_self,
        sorted_rows,
        work=0.1,
        vmem=28,
    )
    came_mid = second_sum.core_swap(send_mid)
    parts_one, last, came_mid, pair_grad_long = lax.optimization_barrier(
        (parts_one, last, came_mid, pair_grad_long)
    )
    keep_last = last[:LAST_PARTS]
    came_last = [second_sum.core_swap(part) for part in last[LAST_PARTS:]]
    parts_one = first_sum.split(2, spot, parts_one)
    came_mid, parts_one = lax.optimization_barrier((came_mid, parts_one))
    parts_two = second_sum.first_split(
        spot, keep_mid, came_mid, *[part for both in zip(keep_last, came_last) for part in both]
    )
    parts_one = first_sum.swap(parts_one, 2)
    parts_two, pair_grad_long, grad_triple = lax.optimization_barrier((parts_two, pair_grad_long, grad_triple))
    parts_two = second_sum.swap(parts_two, 0)
    grad_mine, *grad_away = memory_grad(
        [(0, span)] + [(part * span, span // 2) for part in range(1, groups)], pair_grad_long
    )
    backs_late, grad_triple = lax.optimization_barrier((backs_late, grad_triple))
    grad_target, result_out = call(
        target_kernel,
        [((rows, width), BF16)] * 2,
        [],
        2,
        spot,
        tgt_len,
        grad_triple,
        w_qkv,
        grad_hidden_one,
        result_sorted,
        work=30,
        vmem=16,
    )
    parts_one, grad_away, grad_target = lax.optimization_barrier((parts_one, grad_away, grad_target))
    spread_one = first_sum.spread(2, first_sum.total(parts_one)[0])
    backs_early = send_back(grad_away)
    parts_two = second_sum.swap(second_sum.split(1, spot, parts_two), 1)
    joined_one = first_sum.join(2, spot, spread_one, work=0.01)
    spread_one = first_sum.spread(1, joined_one)
    parts_two, joined_one = lax.optimization_barrier((parts_two, joined_one))
    parts_two = second_sum.split(2, spot, parts_two, work=0.01)
    spread_one, _ = lax.optimization_barrier((spread_one, parts_two))
    parts_two = second_sum.swap(parts_two, 2)
    joined_one = first_sum.join(1, spot, spread_one)
    spread_one = first_sum.spread(0, joined_one)
    parts_two, joined_one = lax.optimization_barrier((parts_two, joined_one))
    sum_two, *norm_sums = second_sum.total(parts_two, work=0.01)
    spread_two = second_sum.spread(2, sum_two)
    spread_two, backs_early = lax.optimization_barrier((spread_two, backs_early))
    spread_two = second_sum.spread(1, second_sum.join(2, spot, spread_two, work=6.3))
    joined_two = second_sum.join(1, spot, spread_two)
    spread_one, joined_two = lax.optimization_barrier((spread_one, joined_two))
    other_one = [first_sum.core_swap(array) for array in spread_one]
    chunks = hidden_width // width
    pieces = []
    for chunk in range(chunks):
        side, here = chunk // (chunks // 2), chunk % (chunks // 2)
        pieces.append((side, here * width, width, 0, chunk * width, 0))
        pieces.append((side, (chunks // 2 + here) * width, width, 1, 0, chunk * width))
    for side in range(2):
        pieces.append((side, chunks * width, short, 2, side * short, 0))
    grad_w_down, grad_w_up, grad_wo = first_sum.finish(
        spot,
        spread_one,
        other_one,
        list(range(len(spread_one))),
        pieces,
        [((hidden_width, width), F32), ((width, hidden_width), F32), ((width, width), F32)],
    )
    spread_two = second_sum.spread(0, joined_two)
    pieces = [
        (0, 0, width, 0, 0, 0),
        (0, width, width, 1, 0, 0),
        (0, 2 * width, width, 2, 0, 0),
        (0, 3 * width, short, 2, 0, width),
        (1, 0, width, 1, 0, width),
        (1, width, width, 3, 0, 0),
        (1, 2 * width, short, 2, short, width),
        (1, 2 * width + short, width, 2, 0, 2 * width),
    ]
    outs = [
        ((width, width), F32),
        ((width, 2 * width), F32),
        ((width, 3 * width), F32),
        ((width, width), F32),
    ]
    other_two = [second_sum.core_swap(spread_two[0])]
    own_two, grad_w_down = lax.optimization_barrier((spread_two[0], grad_w_down))
    held = second_sum.finish(spot, [own_two], other_two, [0], pieces, outs)
    spread_two, held = lax.optimization_barrier((spread_two, held))
    other_two = other_two + [second_sum.core_swap(array) for array in spread_two[1:]]
    grad_wq, grad_wkv, grad_w_qkv, grad_w_out = second_sum.finish(
        spot, spread_two, other_two, list(range(1, len(spread_two))), pieces, outs, held
    )
    grad_memory = jnp.zeros(memory.shape, BF16)
    grad_memory = lax.dynamic_update_slice(grad_memory, grad_mine, (me * count, 0, 0))
    for part, backs in enumerate((backs_early, backs_late)):
        for i, grads in enumerate(backs):
            owner = (me + i + 1) % groups
            grad_memory = lax.dynamic_update_slice(grad_memory, grads, (owner * count, part * (span // 2), 0))
    return (
        result_out,
        grad_target,
        grad_memory,
        grad_w_qkv,
        grad_w_out,
        grad_wq,
        grad_wkv,
        grad_wo,
        grad_w_up,
        grad_w_down,
        *norm_sums,
    )


def solution(mesh):
    rows_spec = P(("dp", "mem"), None)
    memory_spec = P("dp", "mem", None)
    return jax.shard_map(
        body,
        mesh=mesh,
        in_specs=(rows_spec, memory_spec, rows_spec, P("dp", None), P("dp", None)) + (P(),) * 9,
        out_specs=(rows_spec, rows_spec, memory_spec) + (P(),) * 9,
        check_vma=False,
    )
```

```python
import functools
import math

import jax
import jax.numpy as jnp
from jax import lax
from jax.experimental import pallas as pl
from jax.experimental.pallas import tpu as pltpu
from jax.sharding import PartitionSpec as P

HEADS = 8
PAIRS = HEADS // 2
SLAB = 128
SIDE = SLAB // 2
TILE = 128
MASKED = -1e30
EPSILON = 1e-05
F32 = jnp.float32
BF16 = jnp.bfloat16
MIB = 1024 * 1024
LN_ROWS = 16
LAST_PARTS = 2


def dot(left, right):
    return jnp.dot(left, right, preferred_element_type=F32)


def dot_nt(left, right):
    return lax.dot_general(left, right, (((1,), (1,)), ((), ())), preferred_element_type=F32)


def dot_tn(left, right):
    return lax.dot_general(left, right, (((0,), (0,)), ((), ())), preferred_element_type=F32)


def iota(shape, axis):
    return lax.broadcasted_iota(jnp.int32, shape, axis)


def norm_parts(hidden):
    centre = hidden - jnp.mean(hidden, axis=-1, keepdims=True)
    inverse = lax.rsqrt(jnp.mean(centre * centre, axis=-1, keepdims=True) + EPSILON)
    return centre * inverse, inverse


def norm_backward(upstream, unit, inverse, gain_row):
    scaled = upstream * gain_row
    shifted = (
        scaled
        - jnp.mean(scaled, axis=-1, keepdims=True)
        - unit * jnp.mean(scaled * unit, axis=-1, keepdims=True)
    )
    gain_grad = jnp.sum(upstream * unit, axis=0, keepdims=True)
    return inverse * shifted, gain_grad, jnp.sum(upstream, axis=0, keepdims=True)


def sentence_order(me, len_ref):
    count = len_ref.shape[1]
    lengths = [len_ref[me, k] for k in range(count)]
    longest, best, start, running = jnp.int32(0), lengths[0], jnp.int32(0), jnp.int32(0)
    for k in range(1, count):
        running = running + lengths[k - 1]
        more = lengths[k] > best
        longest = jnp.where(more, k, longest)
        start = jnp.where(more, running, start)
        best = jnp.where(more, lengths[k], best)
    order = [longest] + [jnp.where(k < longest, k, k + 1) for k in range(count - 1)]
    bounds = [jnp.int32(0)]
    for k in range(1, count):
        bounds.append(bounds[-1] + len_ref[me, order[k]])
    return order, start, bounds


def moved_rows(index, start, half):
    return jnp.where(index < start, index + half, jnp.where(index < start + half, index - start, index))


def sort_matrix(rows, start):
    spot = moved_rows(iota((rows, rows), 1), start, rows // 2)
    return jnp.where(spot == iota((rows, rows), 0), 1.0, 0.0).astype(BF16)


def unsort_matrix(rows, start):
    spot = moved_rows(iota((rows, rows), 0), start, rows // 2)
    return jnp.where(spot == iota((rows, rows), 1), 1.0, 0.0).astype(BF16)


def side_masks(width):
    side = iota((1, width), 1) % SLAB
    first = jnp.where(side < SLAB // 2, 1.0, 0.0)
    return first.astype(BF16), (1.0 - first).astype(BF16)


def each_pair(step):
    def advance(pair, carry):
        step(pair)
        return carry

    lax.fori_loop(0, PAIRS, advance, 0)


def slab_of(pair, first=0):
    if isinstance(pair, int):
        return pl.ds(first + pair * SLAB, SLAB)
    return pl.ds(pl.multiple_of(first + pair * SLAB, SLAB), SLAB)


def pack_heads(out_ref, rows, width):
    even, odd = side_masks(width)
    for t in range(out_ref.shape[0]):
        tile = rows(t * TILE, TILE)
        out_ref[t, :TILE, :] = tile * even
        out_ref[t, TILE:, :] = tile * odd


def fill_self_bias(bias_ref, bounds, half):
    for t in range(bias_ref.shape[0]):
        block, inner = t // (half // TILE), t % (half // TILE)
        key = iota((half, 2 * TILE), 0)
        query = iota((half, 2 * TILE), 1) % TILE + inner * TILE
        allowed = key <= query
        if block == 1:
            first = jnp.zeros((half, 2 * TILE), jnp.int32)
            for bound in bounds[1:-1]:
                first = jnp.where(query >= bound, bound, first)
            allowed = allowed & (key >= first)
        bias_ref[t] = jnp.where(allowed, 0.0, MASKED)


def self_keys(t, half):
    per = half // TILE
    return (t // per) * half, (t % per + 1) * TILE


def fill_live_bias(bias_ref, me, groups, parts, span, src_ref, sentences):
    key = iota((span, bias_ref.shape[2]), 0)
    for j, sentence in enumerate(sentences):
        for i, part in enumerate(parts):
            place = lax.rem(me - part + groups, groups) * span + key
            live = place < src_ref[me, sentence]
            bias_ref[j, pl.ds(i * span, span), :] = jnp.where(live, 0.0, MASKED)


def cross_units(bounds, half):
    units = [(t, 0, None) for t in range(half // TILE)]
    middle = half // 2
    last = jnp.int32(1)
    for bound in bounds[1:-1]:
        last = last + jnp.where(bound < middle, 1, 0)
    ends = bounds[1:]
    column = iota((1, 2 * TILE), 1) % TILE
    for u in range(len(ends) + 1):
        early = u < last
        sentence = jnp.where(early, u + 1, u)
        tile = jnp.where(early, 0, 1)
        low, high = jnp.int32(0), ends[0]
        for k in range(1, len(ends)):
            low = jnp.where(sentence == k + 1, ends[k - 1], low)
            high = jnp.where(sentence == k + 1, ends[k], high)
        row = column + tile * TILE
        units.append((tile + half // TILE, sentence, (row >= low) & (row < high)))
    return units


def own_sides(both):
    return jnp.concatenate([both[:SIDE, :TILE], both[SIDE:, TILE:]], axis=0)


def side_rows(row):
    even = jnp.broadcast_to(row[:, :TILE], (SIDE, TILE))
    return jnp.concatenate([even, jnp.broadcast_to(row[:, TILE:], (SIDE, TILE))], axis=0)


def tile_columns(tile):
    if isinstance(tile, int):
        return pl.ds(tile * TILE, TILE)
    return pl.ds(pl.multiple_of(tile * TILE, TILE), TILE)


def self_forward_kernel(
    groups,
    me_ref,
    len_ref,
    src_ref,
    target_ref,
    w_qkv_ref,
    w_out_ref,
    wq_ref,
    gain_ref,
    bias_row_ref,
    memory_ref,
    wkv_ref,
    sorted_ref,
    qkv_ref,
    norm_ref,
    attn_t_ref,
    hidden_ref,
    query_ref,
    part_ref,
    top_ref,
    sum_ref,
    pair_out_ref,
    bias_ref,
    live_ref,
    q_pack_ref,
    value_t_ref,
    cross_value_t_ref,
    pair_ref,
    copy_sem,
):
    rows, width = target_ref.shape
    half = rows // 2
    me = me_ref[0]
    order, start, bounds = sentence_order(me, len_ref)
    count, span = pair_ref.shape[0], pair_ref.shape[1]
    copies = []
    for j in range(count):
        block = memory_ref[me * count + order[j]]
        pair_ref[j] = dot(block, wkv_ref[...]).astype(BF16)
        copy = pltpu.make_async_copy(
            pair_ref.at[j], pair_out_ref.at[j, pl.ds(0, span), :], copy_sem.at[j]
        )
        copy.start()
        copies.append(copy)
    sorted_rows = dot(sort_matrix(rows, start), target_ref[...]).astype(BF16)
    sorted_ref[...] = sorted_rows
    fill_self_bias(bias_ref, bounds, half)
    queries = (dot(sorted_rows, w_qkv_ref[:, :width]).astype(BF16) * 0.125).astype(BF16)
    qkv_ref[:, :width] = queries
    pack_heads(q_pack_ref, lambda first, size: queries[first : first + size], width)
    qkv_ref[:, width : 2 * width] = dot(sorted_rows, w_qkv_ref[:, width : 2 * width]).astype(BF16)
    values = dot(sorted_rows, w_qkv_ref[:, 2 * width :]).astype(BF16)
    qkv_ref[:, 2 * width :] = values
    value_t_ref[...] = values.T
    tiles = rows // TILE

    def self_step(pair):
        slab = slab_of(pair)
        for t in range(tiles):
            first, size = self_keys(t, half)
            keys = qkv_ref[pl.ds(first, size), slab_of(pair, width)]
            scores = dot_nt(keys, q_pack_ref[t, :, slab]) + bias_ref[t, :size, :]
            top = jnp.max(scores, axis=0, keepdims=True)
            weights = jnp.exp(scores - top)
            total = jnp.sum(weights, axis=0, keepdims=True)
            probs = (weights * (1.0 / total)).astype(BF16)
            both = dot(value_t_ref[slab, pl.ds(first, size)], probs)
            attn_t_ref[slab, tile_columns(t)] = own_sides(both).astype(BF16)
            norm_ref[pl.ds(pair * tiles + t, 1), :] = top + jnp.log(total)

    each_pair(self_step)
    hidden = sorted_rows.astype(F32) + dot(attn_t_ref[...].T, w_out_ref[...])
    hidden_ref[...] = hidden
    unit, _ = norm_parts(hidden)
    normed = (unit * gain_ref[0:1] + bias_row_ref[0:1]).astype(BF16)
    query_ref[...] = (dot(normed, wq_ref[...]).astype(BF16) * 0.125).astype(BF16)

    pack_heads(q_pack_ref, lambda first, size: query_ref[first : first + size, :], width)
    fill_live_bias(live_ref, me, groups, [0], span, src_ref, order)
    for j in range(count):
        cross_value_t_ref[j] = pair_ref[j, :, width:].T
    units = cross_units(bounds, half)

    def cross_step(pair):
        slab = slab_of(pair)
        for tile, sentence, columns in units:
            scores = dot_nt(pair_ref[sentence, :, slab], q_pack_ref[tile, :, slab]) + live_ref[sentence]
            top = jnp.max(scores, axis=0, keepdims=True)
            weights = jnp.exp(scores - top)
            total = jnp.sum(weights, axis=0, keepdims=True)
            result = own_sides(dot(cross_value_t_ref[sentence, slab, :], weights.astype(BF16)))
            here = tile_columns(tile)
            row = pl.ds(pair * tiles + tile, 1)
            if columns is not None:
                result = jnp.where(columns[:, :TILE], result, part_ref[slab, here])
                top = jnp.where(columns, top, top_ref[row, :])
                total = jnp.where(columns, total, sum_ref[row, :])
            part_ref[slab, here] = result
            top_ref[row, :] = top
            sum_ref[row, :] = total

    part_ref[...] = jnp.zeros_like(part_ref)
    top_ref[...] = jnp.zeros_like(top_ref)
    sum_ref[...] = jnp.ones_like(sum_ref)
    each_pair(cross_step)
    for copy in copies:
        copy.wait()


def middle_kernel(
    groups,
    me_ref,
    len_ref,
    src_ref,
    hidden_one_ref,
    query_ref,
    part_ref,
    top_ref,
    sum_ref,
    wkv_ref,
    gain_ref,
    bias_row_ref,
    wo_hbm,
    w_up_hbm,
    w_down_hbm,
    grad_out_hbm,
    pair_in_hbm,
    *refs,
):
    came_refs = refs[: groups - 1]
    (
        out_ref,
        norm_ref,
        along_ref,
        keep_hbm,
        send_hbm,
        grad_hidden_ref,
        grad_attn_ref,
        ln_ref,
        pair_hbm,
        wo_ref,
        w_up_ref,
        w_down_ref,
        grad_out_ref,
        pair_ref,
        halves_ref,
        live_ref,
        q_pack_ref,
        value_t_ref,
        attn_t_ref,
        active_ref,
        slope_ref,
        grad_upper_ref,
        load_sem,
        pair_sem,
        store_sem,
    ) = refs[groups - 1 :]
    rows, width = hidden_one_ref.shape
    half = rows // 2
    me = me_ref[0]
    count, away = pair_ref.shape[0], pair_ref.shape[1]
    span = away // (groups - 1)
    loads = [
        pltpu.make_async_copy(source, there, load_sem.at[i])
        for i, (source, there) in enumerate(
            [(wo_hbm, wo_ref), (w_up_hbm, w_up_ref), (w_down_hbm, w_down_ref), (grad_out_hbm, grad_out_ref)]
        )
    ]
    for copy in loads:
        copy.start()
    order, start, bounds = sentence_order(me, len_ref)
    fill_live_bias(live_ref, me, groups, list(range(1, groups)), span, src_ref, order)
    pack_heads(q_pack_ref, lambda first, size: query_ref[first : first + size, :], width)
    pair_copies = []
    for j in range(count):
        for part in range(1, groups):
            block = came_refs[part - 1][order[j]]
            pair_ref[j, pl.ds((part - 1) * span, span), :] = dot(block, wkv_ref[...]).astype(BF16)
        value_t_ref[j] = pair_ref[j, :, width:].T
        copy = pltpu.make_async_copy(pair_ref.at[j], pair_hbm.at[j, pl.ds(span, away), :], pair_sem.at[j])
        copy.start()
        pair_copies.append(copy)
    units = cross_units(bounds, half)
    tiles = rows // TILE

    def cross_step(pair):
        slab = slab_of(pair)
        for tile, sentence, columns in units:
            here = tile_columns(tile)
            row = pl.ds(pair * tiles + tile, 1)
            scores = dot_nt(pair_ref[sentence, :, slab], q_pack_ref[tile, :, slab]) + live_ref[sentence]
            before = top_ref[row, :]
            top = jnp.maximum(jnp.max(scores, axis=0, keepdims=True), before)
            weights = jnp.exp(scores - top)
            scale = jnp.exp(before - top)
            total = jnp.sum(weights, axis=0, keepdims=True) + sum_ref[row, :] * scale
            result = own_sides(dot(value_t_ref[sentence, slab, :], weights.astype(BF16)))
            result = (result + part_ref[slab, here] * side_rows(scale)) * side_rows(1.0 / total)
            norm = top + jnp.log(total)
            if columns is not None:
                result = jnp.where(columns[:, :TILE], result, attn_t_ref[slab, here])
                norm = jnp.where(columns, norm, norm_ref[row, :])
            attn_t_ref[slab, here] = result
            norm_ref[row, :] = norm

    attn_t_ref[...] = jnp.zeros_like(attn_t_ref)
    norm_ref[...] = jnp.zeros_like(norm_ref)
    each_pair(cross_step)
    attn_t_low = attn_t_ref[...].astype(BF16)
    loads[0].wait()
    unit_one, _ = norm_parts(hidden_one_ref[...])
    normed_one = unit_one * gain_ref[0:1] + bias_row_ref[0:1]
    hidden_two = normed_one + dot(attn_t_low.T, wo_ref[...])
    unit_two, inverse_two = norm_parts(hidden_two)
    normed_two = unit_two * gain_ref[1:2] + bias_row_ref[1:2]
    normed_two_low = normed_two.astype(BF16)
    chunk = width
    chunks = w_down_ref.shape[0] // chunk
    loads[1].wait()
    loads[2].wait()

    def up_step(c, carry):
        cols = pl.ds(pl.multiple_of(c * chunk, chunk), chunk)
        upper = dot(normed_two_low, w_up_ref[:, cols])
        sigma = 0.5 * jnp.tanh(0.5 * upper) + 0.5
        active = (upper * sigma).astype(BF16)
        active_ref[:, cols] = active
        slope_ref[:, cols] = sigma * (1.0 + upper * (1.0 - sigma))
        return carry

    lax.fori_loop(0, chunks, up_step, 0)

    unit_three, inverse_three = norm_parts(normed_two + dot(active_ref[...], w_down_ref[...]))
    result = (unit_three * gain_ref[2:3] + bias_row_ref[2:3]).astype(BF16)
    out_ref[...] = dot(unsort_matrix(rows, start), result).astype(BF16)
    loads[3].wait()
    upstream = dot(sort_matrix(rows, start), grad_out_ref[...])
    grad_three, gain_three, bias_three = norm_backward(upstream, unit_three, inverse_three, gain_ref[2:3])
    grad_down = grad_three.astype(BF16)
    normed_two_t = normed_two_low.T

    def down_step(c, carry):
        cols = pl.ds(pl.multiple_of(c * chunk, chunk), chunk)
        grad_upper = (dot_nt(grad_down, w_down_ref[cols, :]) * slope_ref[:, cols]).astype(BF16)
        down_part = dot_tn(active_ref[:, cols], grad_down).astype(BF16)
        up_part = dot(normed_two_t, grad_upper).astype(BF16)
        half_index, here = c // (chunks // 2), lax.rem(c, chunks // 2)
        down_rows = pl.ds(pl.multiple_of(here * chunk, chunk), chunk)
        up_rows = pl.ds(pl.multiple_of((chunks // 2 + here) * chunk, chunk), chunk)
        halves_ref[half_index, down_rows, :] = down_part
        halves_ref[half_index, up_rows, :] = up_part
        grad_upper_ref[:, cols] = grad_upper
        return carry

    lax.fori_loop(0, chunks, down_step, 0)

    most = chunks * chunk
    core = me_ref[1]
    stores = [
        pltpu.make_async_copy(
            halves_ref.at[half_index, pl.ds(first, size)], there.at[pl.ds(first, size)], store_sem.at[i]
        )
        for i, (half_index, there, first, size) in enumerate(
            [
                (1 - core, send_hbm, 0, most),
                (core, keep_hbm, 0, most),
                (1 - core, send_hbm, most, halves_ref.shape[1] - most),
                (core, keep_hbm, most, halves_ref.shape[1] - most),
            ]
        )
    ]
    stores[0].start()
    stores[1].start()
    upstream_two = grad_three + dot_nt(grad_upper_ref[...], w_up_ref[...])
    grad_two, gain_two, bias_two = norm_backward(upstream_two, unit_two, inverse_two, gain_ref[1:2])
    grad_two_low = grad_two.astype(BF16)
    wo_grad = dot(attn_t_low, grad_two_low).astype(BF16)
    used = most + width // 2
    for half_index in range(2):
        piece = wo_grad[half_index * (width // 2) : (half_index + 1) * (width // 2)]
        halves_ref[half_index, pl.ds(most, width // 2), :] = piece
        if halves_ref.shape[1] > used:
            halves_ref[half_index, used:, :] = jnp.zeros((halves_ref.shape[1] - used, width), BF16)
    stores[2].start()
    stores[3].start()
    grad_hidden_ref[...] = grad_two
    grad_attn = dot_nt(grad_two_low, wo_ref[...]).astype(BF16)
    grad_attn_ref[...] = grad_attn
    product = grad_attn.T.astype(F32) * attn_t_ref[...]
    for pair in range(PAIRS):
        for side in range(2):
            first = pair * SLAB + side * SIDE
            along = jnp.sum(product[first : first + SIDE], axis=0, keepdims=True)
            for t in range(tiles):
                along_ref[pair * tiles + t : pair * tiles + t + 1, side * TILE : (side + 1) * TILE] = along[
                    :, t * TILE : (t + 1) * TILE
                ]
    ln_ref[...] = jnp.concatenate([gain_two, gain_three, bias_two, bias_three], axis=0)
    for copy in pair_copies + stores:
        copy.wait()


def cross_backward_kernel(
    groups,
    block,
    me_ref,
    len_ref,
    src_ref,
    query_ref,
    norm_ref,
    along_ref,
    grad_attn_ref,
    pair_hbm,
    pair_grad_ref,
    query_grad_t_ref,
    pair_ref,
    live_ref,
    q_pack_ref,
    g_pack_ref,
    key_t_ref,
    query_sum_ref,
    sum_ref,
    load_sem,
):
    rows, width = query_ref.shape
    half = rows // 2
    me = me_ref[0]
    sentences, places = pair_ref.shape[0], pair_ref.shape[1]
    first_sentence = 0 if block == 0 else 1
    load = pltpu.make_async_copy(pair_hbm.at[pl.ds(first_sentence, sentences)], pair_ref, load_sem.at[0])
    load.start()
    order, start, bounds = sentence_order(me, len_ref)
    mine = order[:1] if block == 0 else order[1:]
    fill_live_bias(live_ref, me, groups, list(range(groups)), places // groups, src_ref, mine)
    low = block * half
    pack_heads(q_pack_ref, lambda first, size: query_ref[low + first : low + first + size, :], width)
    pack_heads(g_pack_ref, lambda first, size: grad_attn_ref[low + first : low + first + size, :], width)
    tiles, per = rows // TILE, half // TILE
    units = cross_units(bounds, half)
    units = units[:per] if block == 0 else units[per:]
    load.wait()
    for j in range(sentences):
        key_t_ref[j] = pair_ref[j, :, :width].T

    def pair_step(pair):
        slab, value_slab = slab_of(pair), slab_of(pair, width)
        query_sum_ref[...] = jnp.zeros_like(query_sum_ref)
        sum_ref[...] = jnp.zeros_like(sum_ref)
        for tile, sentence, columns in units:
            j = sentence - first_sentence
            t = tile - block * per
            here = tile_columns(t)
            row = pl.ds(pair * tiles + tile, 1)
            q_rows, g_rows = q_pack_ref[t, :, slab], g_pack_ref[t, :, slab]
            norm = norm_ref[row, :]
            if columns is not None:
                norm = jnp.where(columns, norm, -MASKED)
            scores = dot_nt(pair_ref[j, :, slab], q_rows) + live_ref[j]
            probs = jnp.exp(scores - norm)
            grad_probs = dot_nt(pair_ref[j, :, value_slab], g_rows)
            grad_scores = (probs * (grad_probs - along_ref[row, :])).astype(BF16)
            sum_ref[j, :, :SLAB] += dot(grad_scores, q_rows)
            sum_ref[j, :, SLAB:] += dot(probs.astype(BF16), g_rows)
            query_sum_ref[:, here] += own_sides(dot(key_t_ref[j, slab, :], grad_scores))
        query_grad_t_ref[slab, :] = (query_sum_ref[...] * 0.125).astype(BF16)
        pair_grad_ref[:, :, slab] = sum_ref[:, :, :SLAB].astype(BF16)
        pair_grad_ref[:, :, value_slab] = sum_ref[:, :, SLAB:].astype(BF16)

    for pair in range(PAIRS):
        pair_step(pair)


def memory_weight_kernel(groups, me_ref, len_ref, pair_grad_long_ref, pair_grad_rest_ref, memory_ref, *refs):
    came_refs = refs[: groups - 1]
    wkv_grad_ref, total_ref = refs[groups - 1 :]
    width = memory_ref.shape[2]
    me = me_ref[0]
    count = len_ref.shape[1]
    span = pair_grad_long_ref.shape[1] // groups
    order, _, _ = sentence_order(me, len_ref)
    for j in range(count):
        pair_grad_ref, here = (pair_grad_long_ref, 0) if j == 0 else (pair_grad_rest_ref, j - 1)
        blocks = [memory_ref[me * count + order[j]]] + [ref[order[j]] for ref in came_refs]
        term = dot_tn(jnp.concatenate(blocks, axis=0), pair_grad_ref[here])
        if j == 0:
            total_ref[...] = term
        else:
            total_ref[...] += term
    wkv_grad_ref[0] = total_ref[:, :width].astype(BF16)
    wkv_grad_ref[1] = total_ref[:, width:].astype(BF16)


def memory_grad_kernel(pieces, me_ref, len_ref, pair_grad_long_ref, pair_grad_rest_ref, wkv_ref, *outs):
    count = len_ref.shape[1]
    order, _, _ = sentence_order(me_ref[0], len_ref)
    for j in range(count):
        pair_grad_ref, here = (pair_grad_long_ref, 0) if j == 0 else (pair_grad_rest_ref, j - 1)
        for (first, size), out in zip(pieces, outs):
            out[order[j]] = dot_nt(pair_grad_ref[here, pl.ds(first, size), :], wkv_ref[...]).astype(BF16)


def first_norm_backward_kernel(
    me_ref,
    hidden_one_ref,
    query_grad_t_long_ref,
    query_grad_t_rest_ref,
    grad_hidden_two_ref,
    wq_ref,
    w_out_ref,
    self_attn_t_ref,
    gain_ref,
    bias_row_ref,
    ln_in_ref,
    wkv_grad_ref,
    keep_ref,
    send_ref,
    grad_hidden_ref,
    grad_self_ref,
):
    width = wq_ref.shape[0]
    unit_one, inverse_one = norm_parts(hidden_one_ref[...])
    normed_one = (unit_one * gain_ref[0:1] + bias_row_ref[0:1]).astype(BF16)
    query_grad = jnp.concatenate([query_grad_t_long_ref[...].T, query_grad_t_rest_ref[...].T], axis=0)
    upstream = grad_hidden_two_ref[...] + dot_nt(query_grad, wq_ref[...])
    grad_one, gain_one, bias_one = norm_backward(upstream, unit_one, inverse_one, gain_ref[0:1])
    grad_hidden_ref[...] = grad_one
    grad_one_low = grad_one.astype(BF16)
    grad_self_ref[...] = dot_nt(grad_one_low, w_out_ref[...]).astype(BF16)
    wq_grad = dot_tn(normed_one, query_grad).astype(BF16)
    w_out_grad = dot(self_attn_t_ref[...], grad_one_low).astype(BF16)
    norms = jnp.concatenate(
        [gain_one, ln_in_ref[0:2], bias_one, ln_in_ref[2:4], jnp.zeros((LN_ROWS - 6, width), F32)], axis=0
    ).astype(BF16)

    def halves(low_ref, high_ref):
        low_ref[:width, :] = wq_grad
        low_ref[width : 2 * width, :] = wkv_grad_ref[0]
        high_ref[:width, :] = wkv_grad_ref[1]
        high_ref[width : 2 * width, :] = w_out_grad

    @pl.when(me_ref[1] == 0)
    def _():
        halves(keep_ref, send_ref)

    @pl.when(me_ref[1] != 0)
    def _():
        halves(send_ref, keep_ref)

    keep_ref[2 * width :, :] = norms
    send_ref[2 * width :, :] = norms


def self_backward_kernel(
    me_ref,
    len_ref,
    qkv_ref,
    norm_ref,
    grad_attn_ref,
    sorted_ref,
    grad_triple_ref,
    *refs,
):
    keep_refs, send_refs = refs[:LAST_PARTS], refs[LAST_PARTS : 2 * LAST_PARTS]
    self_backward(
        me_ref,
        len_ref,
        qkv_ref,
        norm_ref,
        grad_attn_ref,
        sorted_ref,
        grad_triple_ref,
        keep_refs,
        send_refs,
        *refs[2 * LAST_PARTS :],
    )


def self_backward(
    me_ref,
    len_ref,
    qkv_ref,
    norm_ref,
    grad_attn_ref,
    sorted_ref,
    grad_triple_ref,
    keep_refs,
    send_refs,
    bias_ref,
    q_pack_ref,
    g_pack_ref,
    key_t_ref,
    query_grad_t_ref,
):
    rows, width = sorted_ref.shape
    half = rows // 2
    _, _, bounds = sentence_order(me_ref[0], len_ref)
    fill_self_bias(bias_ref, bounds, half)
    pack_heads(q_pack_ref, lambda first, size: qkv_ref[first : first + size, :width], width)
    pack_heads(g_pack_ref, lambda first, size: grad_attn_ref[first : first + size, :], width)
    key_t_ref[...] = qkv_ref[:, width : 2 * width].T
    tiles, per = rows // TILE, half // TILE

    def pair_step(pair):
        slab, key_slab, value_slab = slab_of(pair), slab_of(pair, width), slab_of(pair, 2 * width)
        sums = [[None, None] for _ in range(tiles)]
        for t in range(tiles):
            first, size = self_keys(t, half)
            span = pl.ds(first, size)
            q_rows, g_rows = q_pack_ref[t, :, slab], g_pack_ref[t, :, slab]
            scores = dot_nt(qkv_ref[span, key_slab], q_rows) + bias_ref[t, :size, :]
            probs = jnp.exp(scores - norm_ref[pl.ds(pair * tiles + t, 1), :])
            grad_probs = dot_nt(qkv_ref[span, value_slab], g_rows)
            along = jnp.sum(probs * grad_probs, axis=0, keepdims=True)
            grad_scores = (probs * (grad_probs - along)).astype(BF16)
            parts = dot(grad_scores, q_rows), dot(probs.astype(BF16), g_rows)
            for i in range(size // TILE):
                spot = sums[first // TILE + i]
                for k in range(2):
                    piece = parts[k][i * TILE : (i + 1) * TILE]
                    spot[k] = piece if spot[k] is None else spot[k] + piece
            query_grad_t_ref[slab, tile_columns(t)] = (
                own_sides(dot(key_t_ref[slab, span], grad_scores)) * 0.125
            ).astype(BF16)
        for t in range(tiles):
            grad_triple_ref[pl.ds(t * TILE, TILE), key_slab] = sums[t][0].astype(BF16)
            grad_triple_ref[pl.ds(t * TILE, TILE), value_slab] = sums[t][1].astype(BF16)

    for pair in range(PAIRS):
        pair_step(pair)
    grad_triple_ref[:, :width] = query_grad_t_ref[...].T
    sorted_t = sorted_ref[...].T
    grads = [
        dot(sorted_t, grad_triple_ref[:, part * width : (part + 1) * width]).astype(BF16)
        for part in range(3)
    ]
    short = width // 2

    low = jnp.concatenate([grads[0], grads[1][:short]], axis=0)
    high = jnp.concatenate([grads[1][short:], grads[2]], axis=0)
    size = keep_refs[0].shape[0]

    def halves(low_refs, high_refs):
        for i in range(LAST_PARTS):
            low_refs[i][...] = low[i * size : (i + 1) * size]
            high_refs[i][...] = high[i * size : (i + 1) * size]

    @pl.when(me_ref[1] == 0)
    def _():
        halves(keep_refs, send_refs)

    @pl.when(me_ref[1] != 0)
    def _():
        halves(send_refs, keep_refs)


def target_kernel(me_ref, len_ref, grad_triple_ref, w_qkv_ref, grad_hidden_ref, grad_target_ref):
    rows = grad_hidden_ref.shape[0]
    _, start, _ = sentence_order(me_ref[0], len_ref)
    result = grad_hidden_ref[...] + dot_nt(grad_triple_ref[...], w_qkv_ref[...])
    grad_target_ref[...] = dot(unsort_matrix(rows, start), result.astype(BF16)).astype(BF16)


def tree_sum(terms):
    while len(terms) > 1:
        terms = [terms[i] + terms[i + 1] for i in range(0, len(terms), 2)]
    return terms[0]


def rows_of(ref, first, count):
    return ref[pl.ds(pl.multiple_of(first, 16), count), :].astype(F32)


def first_split_kernel(segments, ln, peers, spot_ref, *refs):
    ins, outs, sum_ref = refs[: 2 * segments], refs[2 * segments : -1], refs[-1]
    extra = LN_ROWS if ln else 0
    size = outs[0].shape[0] - extra
    used = 0
    for i in range(segments):
        keep_ref, came_ref = ins[2 * i], ins[2 * i + 1]
        count = keep_ref.shape[0] - (extra if i == 0 else 0)
        sum_ref[used : used + count, :] = (rows_of(keep_ref, 0, count) + rows_of(came_ref, 0, count)).astype(BF16)
        if i == 0 and ln:
            tail = (rows_of(keep_ref, count, LN_ROWS) + rows_of(came_ref, count, LN_ROWS)).astype(BF16)
        used += count
    if sum_ref.shape[0] > used:
        sum_ref[used:, :] = jnp.zeros((sum_ref.shape[0] - used, sum_ref.shape[1]), BF16)
    for d, out in enumerate(outs):
        out[:size, :] = sum_ref[pl.ds(pl.multiple_of((spot_ref[2] ^ d) * size, 16), size), :]
        if ln:
            out[size:, :] = tail


def split_kernel(stage, ln, peers, spot_ref, *refs):
    ins, outs = refs[:peers], refs[peers:]
    extra = LN_ROWS if ln else 0
    size = outs[0].shape[0] - extra
    if ln:
        tail = tree_sum([rows_of(ref, size * len(outs), LN_ROWS) for ref in ins]).astype(BF16)
    for d, out in enumerate(outs):
        first = (spot_ref[2 + stage] ^ d) * size
        out[:size, :] = tree_sum([rows_of(ref, first, size) for ref in ins]).astype(BF16)
        if ln:
            out[size:, :] = tail


def total_kernel(ln, count, *refs):
    ins, outs = refs[:count], refs[count:]
    size = outs[0].shape[0]
    outs[0][...] = tree_sum([rows_of(ref, 0, size) for ref in ins]).astype(BF16)
    if ln:
        norms = tree_sum([rows_of(ref, size, LN_ROWS) for ref in ins])
        outs[1][...] = norms[:3]
        outs[2][...] = norms[3:6]


def join_kernel(stage, spot_ref, *refs):
    out_ref = refs[-1]
    for d, ref in enumerate(refs[:-1]):
        size = ref.shape[0]
        out_ref[pl.ds(pl.multiple_of((spot_ref[2 + stage] ^ d) * size, 16), size), :] = ref[...]


def finish_kernel(offsets, peers, twisted, pieces, held, spot_ref, *refs):
    arrays, refs = refs[: 2 * len(offsets)], refs[2 * len(offsets) + held :]
    outs, (wide_ref, sem) = refs[:-2], refs[-2:]
    core = spot_ref[1]
    size, width = wide_ref.shape[1:]
    copies = []
    for k, ref in enumerate(arrays):
        wide_ref[k] = ref[...].astype(F32)
        d, other = offsets[k // 2], k % 2
        half = 1 - core if other else core
        place = spot_ref[3 if twisted and other else 2] ^ d
        for i in range(2):
            for j in range(peers):
                cut = []
                for piece_half, first, rows, out, row, col in pieces:
                    low, high = max(first, j * size), min(first + rows, (j + 1) * size)
                    if piece_half == i and low < high:
                        there = outs[out].at[pl.ds(row + low - first, high - low), pl.ds(col, width)]
                        here = wide_ref.at[k, pl.ds(low - j * size, high - low), :]
                        cut.append(pltpu.make_async_copy(here, there, sem.at[k, len(cut)]))
                copies.append(((half == i) & (place == j), cut))
                _start_all(*copies[-1])
    for chosen, cut in copies:
        _wait_all(chosen, cut)


def _start_all(chosen, cut):
    @pl.when(chosen)
    def _():
        for copy in cut:
            copy.start()


def _wait_all(chosen, cut):
    @pl.when(chosen)
    def _():
        for copy in cut:
            copy.wait()


class Summing:
    def __init__(self, rows, width, ln):
        self.width, self.ln = width, ln
        self.dp, self.mem = lax.axis_size("dp"), lax.axis_size("mem")
        z_size = 4
        x_size = self.dp // (2 * z_size)
        self.sizes = (x_size, self.mem, z_size)
        self.twisted = x_size == self.mem
        self.chunk = -(-rows // (16 * math.prod(self.sizes))) * 16
        self.rows = self.chunk * math.prod(self.sizes)

    def after(self, stage):
        return self.rows // math.prod(self.sizes[:stage])

    def axis(self, stage, core):
        return 1 - stage if self.twisted and core == 1 and stage < 2 else stage

    def coords(self, dp, mem):
        return [dp // 2 % self.sizes[0], mem, dp // (2 * self.sizes[0])], dp % 2

    def spot(self, me, dp):
        (x, mem, z), core = self.coords(dp, me)
        if self.twisted:
            x, mem = jnp.where(core == 0, x, mem), jnp.where(core == 0, mem, x)
        return jnp.stack([me, core, x, mem, z]).astype(jnp.int32)

    def permute(self, array, stage, offset):
        pairs = []
        for dp in range(self.dp):
            for mem in range(self.mem):
                spots, core = self.coords(dp, mem)
                if stage is None:
                    core ^= offset
                else:
                    spots[self.axis(stage, core)] ^= offset
                to_dp = (spots[2] * self.sizes[0] + spots[0]) * 2 + core
                pairs.append((dp * self.mem + mem, to_dp * self.mem + spots[1]))
        return lax.ppermute(array, ("dp", "mem"), pairs)

    def core_swap(self, send):
        return self.permute(send, None, 1)

    def swap(self, arrays, stage):
        return [arrays[0]] + [self.permute(array, stage, d) for d, array in enumerate(arrays) if d > 0]

    def spread(self, stage, array):
        return [array] + [self.permute(array, stage, d) for d in range(1, self.sizes[stage])]

    def messages(self, stage):
        size = self.after(stage + 1) + (LN_ROWS if self.ln else 0)
        return [((size, self.width), BF16)] * self.sizes[stage]

    def first_split(self, spot, *arrays):
        kernel = functools.partial(first_split_kernel, len(arrays) // 2, self.ln, self.sizes[0])
        return call(kernel, self.messages(0), [((self.rows, self.width), BF16)], 1, spot, *arrays, work=0.01)

    def split(self, stage, spot, arrays, work=0.01):
        kernel = functools.partial(split_kernel, stage, self.ln, self.sizes[stage - 1])
        return call(kernel, self.messages(stage), [], 1, spot, *arrays, work=work)

    def total(self, arrays, work=0.01):
        outs = [((self.chunk, self.width), BF16)]
        if self.ln:
            outs = outs + [((3, self.width), F32)] * 2
        return call(functools.partial(total_kernel, self.ln, self.sizes[2]), outs, [], 0, *arrays, work=work)

    def join(self, stage, spot, arrays, work=0.01):
        outs = [((self.after(stage), self.width), BF16)]
        return call(functools.partial(join_kernel, stage), outs, [], 1, spot, *arrays, work=work)[0]

    def finish(self, spot, mine, others, offsets, pieces, outs, held=()):
        kernel = functools.partial(finish_kernel, offsets, self.sizes[0], self.twisted, pieces, len(held))
        arrays = [array for d in offsets for array in (mine[d], others[d])]
        size = self.after(1)
        scratch = [((len(arrays), size, self.width), F32), pltpu.SemaphoreType.DMA((len(arrays), len(pieces)))]
        aliases = {1 + len(arrays) + i: i for i in range(len(held))}
        return call(
            kernel,
            outs,
            scratch,
            1,
            spot,
            *arrays,
            *held,
            work=1,
            vmem=40,
            hbm_in=len(held),
            hbm_out=len(outs),
            aliases=aliases,
        )


def call(kernel, outs, scratch, scalars, *arrays, work=0.5, vmem=0, hbm_in=0, hbm_out=0, aliases=None):
    plain = len(arrays) - scalars - hbm_in
    if not vmem:
        blocks = [(array.shape, array.dtype) for array in arrays[scalars:]] + outs
        blocks = blocks + [entry for entry in scratch if isinstance(entry, tuple)]
        vmem = max(16, sum(math.prod(shape) * jnp.dtype(kind).itemsize for shape, kind in blocks) // MIB + 7)
    specs = [pl.BlockSpec(memory_space=pltpu.SMEM)] * scalars
    specs = specs + [pl.BlockSpec(memory_space=pltpu.VMEM)] * plain
    specs = specs + [pl.BlockSpec(memory_space=pl.ANY)] * hbm_in
    out_specs = [pl.BlockSpec(memory_space=pltpu.VMEM)] * (len(outs) - hbm_out)
    out_specs = out_specs + [pl.BlockSpec(memory_space=pl.ANY)] * hbm_out
    return pl.pallas_call(
        kernel,
        out_shape=[jax.ShapeDtypeStruct(shape, kind) for shape, kind in outs],
        in_specs=specs,
        out_specs=out_specs,
        scratch_shapes=[pltpu.VMEM(*entry) if isinstance(entry, tuple) else entry for entry in scratch],
        input_output_aliases=aliases or {},
        compiler_params=pltpu.CompilerParams(vmem_limit_bytes=vmem * MIB),
        cost_estimate=pl.CostEstimate(flops=int(work * 1e9), bytes_accessed=int(work * 3e6), transcendentals=0),
    )(*arrays)


def middle(
    groups, first_sum, stats, spot, tgt_len, src_len, hidden_one, query, part, part_top, part_sum, wkv_cross,
    ln_gain, ln_bias, wo_cross, w_up, w_down, grad_out, pair_mine, came,
):
    rows, width = hidden_one.shape
    half, tiles = rows // 2, rows // TILE
    hidden_width = w_down.shape[0]
    count, places, _ = pair_mine.shape
    away = places // groups * (groups - 1)
    arrays = [spot, tgt_len, src_len, hidden_one, query, part, part_top, part_sum, wkv_cross, ln_gain, ln_bias]
    stay = [wo_cross, w_up, w_down, grad_out, pair_mine]

    def kernel(*refs):
        ins, refs = refs[: len(arrays)], refs[len(arrays) :]
        came_refs, refs = refs[: len(came)], refs[len(came) :]
        stay_refs, refs = refs[: len(stay)], refs[len(stay) :]
        outs, refs = refs[:9], refs[9:]
        middle_kernel(groups, *ins, *stay_refs, *came_refs, *outs[:3], *outs[6:8], *outs[3:6], outs[8], *refs)

    result_out, cross_norm, cross_along, grad_hidden_two, grad_attn, ln_part, keep_one, send_one, pair_all = call(
        kernel,
        [
            ((rows, width), BF16),
            (stats, F32),
            (stats, F32),
            ((rows, width), F32),
            ((rows, width), BF16),
            ((4, width), F32),
            ((first_sum.rows, width), BF16),
            ((first_sum.rows, width), BF16),
            ((count, places, 2 * width), BF16),
        ],
        [
            ((width, width), BF16),
            ((width, hidden_width), BF16),
            ((hidden_width, width), BF16),
            ((rows, width), BF16),
            ((count, away, 2 * width), BF16),
            ((2, first_sum.rows, width), BF16),
            ((count, away, 2 * TILE), F32),
            ((tiles, 2 * TILE, width), BF16),
            ((count, width, away), BF16),
            ((width, rows), F32),
            ((rows, hidden_width), BF16),
            ((rows, hidden_width), F32),
            ((rows, hidden_width), BF16),
            pltpu.SemaphoreType.DMA((4,)),
            pltpu.SemaphoreType.DMA((count,)),
            pltpu.SemaphoreType.DMA((4,)),
        ],
        3,
        *arrays,
        *came,
        *stay,
        vmem=60,
        hbm_in=len(stay),
        hbm_out=3,
        aliases={len(arrays) + len(came) + len(stay) - 1: 8},
    )
    return result_out, cross_norm, cross_along, keep_one, send_one, grad_hidden_two, grad_attn, ln_part, pair_all


def body(
    target,
    memory,
    grad_out,
    tgt_len,
    src_len,
    w_qkv,
    w_out,
    wq_cross,
    wkv_cross,
    wo_cross,
    w_up,
    w_down,
    ln_gain,
    ln_bias,
):
    rows, width = target.shape
    half = rows // 2
    tiles = rows // TILE
    hidden_width = w_down.shape[0]
    groups = lax.axis_size("mem")
    me = lax.axis_index("mem")
    count = tgt_len.shape[1]
    span = memory.shape[1]
    places, away = groups * span, (groups - 1) * span
    dp = lax.axis_index("dp")
    short = width // 2
    first_sum = Summing(hidden_width + short, width, False)
    second_sum = Summing(3 * width + short, width, True)
    spot = first_sum.spot(me, dp)
    stats = (PAIRS * tiles, 2 * TILE)

    came = []
    for shift in range(1, groups):
        pairs = [(i, (i + shift) % groups) for i in range(groups)]
        sent = lax.dynamic_slice_in_dim(memory, ((me + shift) % groups) * count, count, 0)
        came.append(lax.ppermute(sent, "mem", pairs))

    sorted_rows, qkv, self_norm, self_attn_t, hidden_one, query, part, part_top, part_sum, pair_mine = call(
        functools.partial(self_forward_kernel, groups),
        [
            ((rows, width), BF16),
            ((rows, 3 * width), BF16),
            (stats, F32),
            ((width, rows), BF16),
            ((rows, width), F32),
            ((rows, width), BF16),
            ((width, rows), F32),
            (stats, F32),
            (stats, F32),
            ((count, places, 2 * width), BF16),
        ],
        [
            ((tiles, half, 2 * TILE), F32),
            ((count, span, 2 * TILE), F32),
            ((tiles, 2 * TILE, width), BF16),
            ((width, rows), BF16),
            ((count, width, span), BF16),
            ((count, span, 2 * width), BF16),
            pltpu.SemaphoreType.DMA((count,)),
        ],
        3,
        spot,
        tgt_len,
        src_len,
        target,
        w_qkv,
        w_out,
        wq_cross,
        ln_gain,
        ln_bias,
        memory,
        wkv_cross,
        vmem=60,
        hbm_out=1,
    )
    result_out, cross_norm, cross_along, keep_one, send_one, grad_hidden_two, grad_attn, ln_part, pair_all = middle(
        groups, first_sum, stats, spot, tgt_len, src_len, hidden_one, query, part, part_top, part_sum, wkv_cross,
        ln_gain, ln_bias, wo_cross, w_up, w_down, grad_out, pair_mine, came,
    )
    came_one = first_sum.core_swap(send_one)

    def cross_backward(block):
        sentences = 1 if block == 0 else count - 1
        return call(
            functools.partial(cross_backward_kernel, groups, block),
            [((sentences, places, 2 * width), BF16), ((width, half), BF16)],
            [
                ((sentences, places, 2 * width), BF16),
                ((sentences, places, 2 * TILE), F32),
                ((half // TILE, 2 * TILE, width), BF16),
                ((half // TILE, 2 * TILE, width), BF16),
                ((sentences, width, places), BF16),
                ((SLAB, half), F32),
                ((sentences, places, 2 * SLAB), F32),
                pltpu.SemaphoreType.DMA((1,)),
            ],
            3,
            spot,
            tgt_len,
            src_len,
            query,
            cross_norm,
            cross_along,
            grad_attn,
            pair_all,
            work=10,
            vmem=58 if block == 0 else 32,
            hbm_in=1,
        )

    pair_grad_long, query_grad_t_long = cross_backward(0)
    came_one, pair_grad_long = lax.optimization_barrier((came_one, pair_grad_long))
    parts_one = first_sum.first_split(spot, keep_one, came_one)
    parts_one, pair_all = lax.optimization_barrier((parts_one, pair_all))
    parts_one = first_sum.swap(parts_one, 0)
    pair_grad_rest, query_grad_t_rest = cross_backward(1)
    (wkv_grad,) = call(
        functools.partial(memory_weight_kernel, groups),
        [((2, width, width), BF16)],
        [((width, 2 * width), F32)],
        2,
        spot,
        tgt_len,
        pair_grad_long,
        pair_grad_rest,
        memory,
        *came,
        work=1,
        vmem=32,
    )
    keep_mid, send_mid, grad_hidden_one, grad_self = call(
        first_norm_backward_kernel,
        [
            ((2 * width + LN_ROWS, width), BF16),
            ((2 * width + LN_ROWS, width), BF16),
            ((rows, width), F32),
            ((rows, width), BF16),
        ],
        [],
        1,
        spot,
        hidden_one,
        query_grad_t_long,
        query_grad_t_rest,
        grad_hidden_two,
        wq_cross,
        w_out,
        self_attn_t,
        ln_gain,
        ln_bias,
        ln_part,
        wkv_grad,
        work=0.1,
        vmem=24,
    )
    def memory_grad(pieces, pair_grad_long):
        return call(
            functools.partial(memory_grad_kernel, pieces),
            [((count, size, width), BF16) for _, size in pieces],
            [],
            2,
            spot,
            tgt_len,
            pair_grad_long,
            pair_grad_rest,
            wkv_cross,
            work=0.01,
            vmem=32,
        )

    def send_back(grads):
        return [
            lax.ppermute(array, "mem", [(k, (k - 1 - i) % groups) for k in range(groups)])
            for i, array in enumerate(grads)
        ]

    parts_one, grad_self = lax.optimization_barrier((parts_one, grad_self))
    parts_one = first_sum.split(1, spot, parts_one)
    parts_one, grad_self, pair_grad_long = lax.optimization_barrier((parts_one, grad_self, pair_grad_long))
    parts_one = first_sum.swap(parts_one, 1)
    grad_late = memory_grad(
        [(part * span + span // 2, span // 2) for part in range(1, groups)], pair_grad_long
    )
    backs_late = send_back(grad_late)
    grad_late, grad_self = lax.optimization_barrier((grad_late, grad_self))
    grad_triple, *last = call(
        self_backward_kernel,
        [((rows, 3 * width), BF16)] + [(((width + short) // LAST_PARTS, width), BF16)] * (2 * LAST_PARTS),
        [
            ((tiles, half, 2 * TILE), F32),
            ((tiles, 2 * TILE, width), BF16),
            ((tiles, 2 * TILE, width), BF16),
            ((width, rows), BF16),
            ((width, rows), BF16),
        ],
        2,
        spot,
        tgt_len,
        qkv,
        self_norm,
        grad_self,
        sorted_rows,
        work=0.1,
        vmem=28,
    )
    came_mid = second_sum.core_swap(send_mid)
    parts_one, last, came_mid, pair_grad_long = lax.optimization_barrier(
        (parts_one, last, came_mid, pair_grad_long)
    )
    keep_last = last[:LAST_PARTS]
    came_last = [second_sum.core_swap(part) for part in last[LAST_PARTS:]]
    parts_one = first_sum.split(2, spot, parts_one)
    came_mid, parts_one = lax.optimization_barrier((came_mid, parts_one))
    parts_two = second_sum.first_split(
        spot, keep_mid, came_mid, *[part for both in zip(keep_last, came_last) for part in both]
    )
    parts_one = first_sum.swap(parts_one, 2)
    parts_two, pair_grad_long, grad_triple = lax.optimization_barrier((parts_two, pair_grad_long, grad_triple))
    parts_two = second_sum.swap(parts_two, 0)
    grad_mine, *grad_away = memory_grad(
        [(0, span)] + [(part * span, span // 2) for part in range(1, groups)], pair_grad_long
    )
    backs_late, grad_triple = lax.optimization_barrier((backs_late, grad_triple))
    (grad_target,) = call(
        target_kernel,
        [((rows, width), BF16)],
        [],
        2,
        spot,
        tgt_len,
        grad_triple,
        w_qkv,
        grad_hidden_one,
        work=30,
        vmem=16,
    )
    parts_one, grad_away, grad_target = lax.optimization_barrier((parts_one, grad_away, grad_target))
    spread_one = first_sum.spread(2, first_sum.total(parts_one)[0])
    backs_early = send_back(grad_away)
    parts_two = second_sum.swap(second_sum.split(1, spot, parts_two), 1)
    joined_one = first_sum.join(2, spot, spread_one, work=0.01)
    spread_one = first_sum.spread(1, joined_one)
    parts_two, joined_one = lax.optimization_barrier((parts_two, joined_one))
    parts_two = second_sum.split(2, spot, parts_two, work=0.01)
    spread_one, _ = lax.optimization_barrier((spread_one, parts_two))
    parts_two = second_sum.swap(parts_two, 2)
    joined_one = first_sum.join(1, spot, spread_one)
    spread_one = first_sum.spread(0, joined_one)
    parts_two, joined_one = lax.optimization_barrier((parts_two, joined_one))
    sum_two, *norm_sums = second_sum.total(parts_two, work=0.01)
    spread_two = second_sum.spread(2, sum_two)
    spread_two, backs_early = lax.optimization_barrier((spread_two, backs_early))
    spread_two = second_sum.spread(1, second_sum.join(2, spot, spread_two, work=6.3))
    joined_two = second_sum.join(1, spot, spread_two)
    spread_one, joined_two = lax.optimization_barrier((spread_one, joined_two))
    other_one = [first_sum.core_swap(array) for array in spread_one]
    chunks = hidden_width // width
    pieces = []
    for chunk in range(chunks):
        side, here = chunk // (chunks // 2), chunk % (chunks // 2)
        pieces.append((side, here * width, width, 0, chunk * width, 0))
        pieces.append((side, (chunks // 2 + here) * width, width, 1, 0, chunk * width))
    for side in range(2):
        pieces.append((side, chunks * width, short, 2, side * short, 0))
    grad_w_down, grad_w_up, grad_wo = first_sum.finish(
        spot,
        spread_one,
        other_one,
        list(range(len(spread_one))),
        pieces,
        [((hidden_width, width), F32), ((width, hidden_width), F32), ((width, width), F32)],
    )
    spread_two = second_sum.spread(0, joined_two)
    pieces = [
        (0, 0, width, 0, 0, 0),
        (0, width, width, 1, 0, 0),
        (0, 2 * width, width, 2, 0, 0),
        (0, 3 * width, short, 2, 0, width),
        (1, 0, width, 1, 0, width),
        (1, width, width, 3, 0, 0),
        (1, 2 * width, short, 2, short, width),
        (1, 2 * width + short, width, 2, 0, 2 * width),
    ]
    outs = [
        ((width, width), F32),
        ((width, 2 * width), F32),
        ((width, 3 * width), F32),
        ((width, width), F32),
    ]
    other_two = [second_sum.core_swap(spread_two[0])]
    own_two, grad_w_down = lax.optimization_barrier((spread_two[0], grad_w_down))
    held = second_sum.finish(spot, [own_two], other_two, [0], pieces, outs)
    spread_two, held = lax.optimization_barrier((spread_two, held))
    other_two = other_two + [second_sum.core_swap(array) for array in spread_two[1:]]
    grad_wq, grad_wkv, grad_w_qkv, grad_w_out = second_sum.finish(
        spot, spread_two, other_two, list(range(1, len(spread_two))), pieces, outs, held
    )
    grad_memory = jnp.zeros(memory.shape, BF16)
    grad_memory = lax.dynamic_update_slice(grad_memory, grad_mine, (me * count, 0, 0))
    for part, backs in enumerate((backs_early, backs_late)):
        for i, grads in enumerate(backs):
            owner = (me + i + 1) % groups
            grad_memory = lax.dynamic_update_slice(grad_memory, grads, (owner * count, part * (span // 2), 0))
    return (
        result_out,
        grad_target,
        grad_memory,
        grad_w_qkv,
        grad_w_out,
        grad_wq,
        grad_wkv,
        grad_wo,
        grad_w_up,
        grad_w_down,
        *norm_sums,
    )


def solution(mesh):
    rows_spec = P(("dp", "mem"), None)
    memory_spec = P("dp", "mem", None)
    return jax.shard_map(
        body,
        mesh=mesh,
        in_specs=(rows_spec, memory_spec, rows_spec, P("dp", None), P("dp", None)) + (P(),) * 9,
        out_specs=(rows_spec, rows_spec, memory_spec) + (P(),) * 9,
        check_vma=False,
    )
```

```python
import functools
import math

import jax
import jax.numpy as jnp
from jax import lax
from jax.experimental import pallas as pl
from jax.experimental.pallas import tpu as pltpu
from jax.sharding import PartitionSpec as P

HEADS = 8
PAIRS = HEADS // 2
SLAB = 128
SIDE = SLAB // 2
TILE = 128
MASKED = -1e30
EPSILON = 1e-05
F32 = jnp.float32
BF16 = jnp.bfloat16
MIB = 1024 * 1024
LN_ROWS = 16
LAST_PARTS = 2


def dot(left, right):
    return jnp.dot(left, right, preferred_element_type=F32)


def dot_nt(left, right):
    return lax.dot_general(left, right, (((1,), (1,)), ((), ())), preferred_element_type=F32)


def dot_tn(left, right):
    return lax.dot_general(left, right, (((0,), (0,)), ((), ())), preferred_element_type=F32)


def iota(shape, axis):
    return lax.broadcasted_iota(jnp.int32, shape, axis)


def norm_parts(hidden):
    centre = hidden - jnp.mean(hidden, axis=-1, keepdims=True)
    inverse = lax.rsqrt(jnp.mean(centre * centre, axis=-1, keepdims=True) + EPSILON)
    return centre * inverse, inverse


def norm_backward(upstream, unit, inverse, gain_row):
    scaled = upstream * gain_row
    shifted = (
        scaled
        - jnp.mean(scaled, axis=-1, keepdims=True)
        - unit * jnp.mean(scaled * unit, axis=-1, keepdims=True)
    )
    gain_grad = jnp.sum(upstream * unit, axis=0, keepdims=True)
    return inverse * shifted, gain_grad, jnp.sum(upstream, axis=0, keepdims=True)


def sentence_order(me, len_ref):
    count = len_ref.shape[1]
    lengths = [len_ref[me, k] for k in range(count)]
    longest, best, start, running = jnp.int32(0), lengths[0], jnp.int32(0), jnp.int32(0)
    for k in range(1, count):
        running = running + lengths[k - 1]
        more = lengths[k] > best
        longest = jnp.where(more, k, longest)
        start = jnp.where(more, running, start)
        best = jnp.where(more, lengths[k], best)
    order = [longest] + [jnp.where(k < longest, k, k + 1) for k in range(count - 1)]
    bounds = [jnp.int32(0)]
    for k in range(1, count):
        bounds.append(bounds[-1] + len_ref[me, order[k]])
    return order, start, bounds


def moved_rows(index, start, half):
    return jnp.where(index < start, index + half, jnp.where(index < start + half, index - start, index))


def sort_matrix(rows, start):
    spot = moved_rows(iota((rows, rows), 1), start, rows // 2)
    return jnp.where(spot == iota((rows, rows), 0), 1.0, 0.0).astype(BF16)


def unsort_matrix(rows, start):
    spot = moved_rows(iota((rows, rows), 0), start, rows // 2)
    return jnp.where(spot == iota((rows, rows), 1), 1.0, 0.0).astype(BF16)


def side_masks(width):
    side = iota((1, width), 1) % SLAB
    first = jnp.where(side < SLAB // 2, 1.0, 0.0)
    return first.astype(BF16), (1.0 - first).astype(BF16)


def each_pair(step):
    def advance(pair, carry):
        step(pair)
        return carry

    lax.fori_loop(0, PAIRS, advance, 0)


def slab_of(pair, first=0):
    if isinstance(pair, int):
        return pl.ds(first + pair * SLAB, SLAB)
    return pl.ds(pl.multiple_of(first + pair * SLAB, SLAB), SLAB)


def pack_heads(out_ref, rows, width):
    even, odd = side_masks(width)
    for t in range(out_ref.shape[0]):
        tile = rows(t * TILE, TILE)
        out_ref[t, :TILE, :] = tile * even
        out_ref[t, TILE:, :] = tile * odd


def fill_self_bias(bias_ref, bounds, half):
    for t in range(bias_ref.shape[0]):
        block, inner = t // (half // TILE), t % (half // TILE)
        key = iota((half, 2 * TILE), 0)
        query = iota((half, 2 * TILE), 1) % TILE + inner * TILE
        allowed = key <= query
        if block == 1:
            first = jnp.zeros((half, 2 * TILE), jnp.int32)
            for bound in bounds[1:-1]:
                first = jnp.where(query >= bound, bound, first)
            allowed = allowed & (key >= first)
        bias_ref[t] = jnp.where(allowed, 0.0, MASKED)


def self_keys(t, half):
    per = half // TILE
    return (t // per) * half, (t % per + 1) * TILE


def fill_live_bias(bias_ref, me, groups, parts, span, src_ref, sentences):
    key = iota((span, bias_ref.shape[2]), 0)
    for j, sentence in enumerate(sentences):
        for i, part in enumerate(parts):
            place = lax.rem(me - part + groups, groups) * span + key
            live = place < src_ref[me, sentence]
            bias_ref[j, pl.ds(i * span, span), :] = jnp.where(live, 0.0, MASKED)


def cross_units(bounds, half):
    units = [(t, 0, None) for t in range(half // TILE)]
    middle = half // 2
    last = jnp.int32(1)
    for bound in bounds[1:-1]:
        last = last + jnp.where(bound < middle, 1, 0)
    ends = bounds[1:]
    column = iota((1, 2 * TILE), 1) % TILE
    for u in range(len(ends) + 1):
        early = u < last
        sentence = jnp.where(early, u + 1, u)
        tile = jnp.where(early, 0, 1)
        low, high = jnp.int32(0), ends[0]
        for k in range(1, len(ends)):
            low = jnp.where(sentence == k + 1, ends[k - 1], low)
            high = jnp.where(sentence == k + 1, ends[k], high)
        row = column + tile * TILE
        units.append((tile + half // TILE, sentence, (row >= low) & (row < high)))
    return units


def own_sides(both):
    return jnp.concatenate([both[:SIDE, :TILE], both[SIDE:, TILE:]], axis=0)


def side_rows(row):
    even = jnp.broadcast_to(row[:, :TILE], (SIDE, TILE))
    return jnp.concatenate([even, jnp.broadcast_to(row[:, TILE:], (SIDE, TILE))], axis=0)


def tile_columns(tile):
    if isinstance(tile, int):
        return pl.ds(tile * TILE, TILE)
    return pl.ds(pl.multiple_of(tile * TILE, TILE), TILE)


def self_forward_kernel(
    groups,
    me_ref,
    len_ref,
    src_ref,
    target_ref,
    w_qkv_ref,
    w_out_ref,
    wq_ref,
    gain_ref,
    bias_row_ref,
    memory_ref,
    wkv_ref,
    sorted_ref,
    qkv_ref,
    norm_ref,
    attn_t_ref,
    hidden_ref,
    query_ref,
    part_ref,
    top_ref,
    sum_ref,
    pair_out_ref,
    bias_ref,
    live_ref,
    q_pack_ref,
    value_t_ref,
    cross_value_t_ref,
    pair_ref,
    copy_sem,
):
    rows, width = target_ref.shape
    half = rows // 2
    me = me_ref[0]
    order, start, bounds = sentence_order(me, len_ref)
    count, span = pair_ref.shape[0], pair_ref.shape[1]
    copies = []
    for j in range(count):
        block = memory_ref[me * count + order[j]]
        pair_ref[j] = dot(block, wkv_ref[...]).astype(BF16)
        copy = pltpu.make_async_copy(
            pair_ref.at[j], pair_out_ref.at[j, pl.ds(0, span), :], copy_sem.at[j]
        )
        copy.start()
        copies.append(copy)
    sorted_rows = dot(sort_matrix(rows, start), target_ref[...]).astype(BF16)
    sorted_ref[...] = sorted_rows
    fill_self_bias(bias_ref, bounds, half)
    queries = (dot(sorted_rows, w_qkv_ref[:, :width]).astype(BF16) * 0.125).astype(BF16)
    qkv_ref[:, :width] = queries
    pack_heads(q_pack_ref, lambda first, size: queries[first : first + size], width)
    qkv_ref[:, width : 2 * width] = dot(sorted_rows, w_qkv_ref[:, width : 2 * width]).astype(BF16)
    values = dot(sorted_rows, w_qkv_ref[:, 2 * width :]).astype(BF16)
    qkv_ref[:, 2 * width :] = values
    value_t_ref[...] = values.T
    tiles = rows // TILE

    def self_step(pair):
        slab = slab_of(pair)
        for t in range(tiles):
            first, size = self_keys(t, half)
            keys = qkv_ref[pl.ds(first, size), slab_of(pair, width)]
            scores = dot_nt(keys, q_pack_ref[t, :, slab]) + bias_ref[t, :size, :]
            top = jnp.max(scores, axis=0, keepdims=True)
            weights = jnp.exp(scores - top)
            total = jnp.sum(weights, axis=0, keepdims=True)
            probs = (weights * (1.0 / total)).astype(BF16)
            both = dot(value_t_ref[slab, pl.ds(first, size)], probs)
            attn_t_ref[slab, tile_columns(t)] = own_sides(both).astype(BF16)
            norm_ref[pl.ds(pair * tiles + t, 1), :] = top + jnp.log(total)

    each_pair(self_step)
    hidden = sorted_rows.astype(F32) + dot(attn_t_ref[...].T, w_out_ref[...])
    hidden_ref[...] = hidden
    unit, _ = norm_parts(hidden)
    normed = (unit * gain_ref[0:1] + bias_row_ref[0:1]).astype(BF16)
    query_ref[...] = (dot(normed, wq_ref[...]).astype(BF16) * 0.125).astype(BF16)

    pack_heads(q_pack_ref, lambda first, size: query_ref[first : first + size, :], width)
    fill_live_bias(live_ref, me, groups, [0], span, src_ref, order)
    for j in range(count):
        cross_value_t_ref[j] = pair_ref[j, :, width:].T
    units = cross_units(bounds, half)

    def cross_step(pair):
        slab = slab_of(pair)
        for tile, sentence, columns in units:
            scores = dot_nt(pair_ref[sentence, :, slab], q_pack_ref[tile, :, slab]) + live_ref[sentence]
            top = jnp.max(scores, axis=0, keepdims=True)
            weights = jnp.exp(scores - top)
            total = jnp.sum(weights, axis=0, keepdims=True)
            result = own_sides(dot(cross_value_t_ref[sentence, slab, :], weights.astype(BF16)))
            here = tile_columns(tile)
            row = pl.ds(pair * tiles + tile, 1)
            if columns is not None:
                result = jnp.where(columns[:, :TILE], result, part_ref[slab, here])
                top = jnp.where(columns, top, top_ref[row, :])
                total = jnp.where(columns, total, sum_ref[row, :])
            part_ref[slab, here] = result
            top_ref[row, :] = top
            sum_ref[row, :] = total

    part_ref[...] = jnp.zeros_like(part_ref)
    top_ref[...] = jnp.zeros_like(top_ref)
    sum_ref[...] = jnp.ones_like(sum_ref)
    each_pair(cross_step)
    for copy in copies:
        copy.wait()


def middle_kernel(
    groups,
    me_ref,
    len_ref,
    src_ref,
    hidden_one_ref,
    query_ref,
    part_ref,
    top_ref,
    sum_ref,
    wkv_ref,
    gain_ref,
    bias_row_ref,
    wo_hbm,
    w_up_hbm,
    w_down_hbm,
    grad_out_hbm,
    pair_in_hbm,
    *refs,
):
    came_refs = refs[: groups - 1]
    (
        out_ref,
        norm_ref,
        along_ref,
        keep_hbm,
        send_hbm,
        grad_hidden_ref,
        grad_attn_ref,
        ln_ref,
        pair_hbm,
        wo_ref,
        w_up_ref,
        w_down_ref,
        grad_out_ref,
        pair_ref,
        halves_ref,
        live_ref,
        q_pack_ref,
        value_t_ref,
        attn_t_ref,
        active_ref,
        slope_ref,
        grad_upper_ref,
        load_sem,
        pair_sem,
        store_sem,
    ) = refs[groups - 1 :]
    rows, width = hidden_one_ref.shape
    half = rows // 2
    me = me_ref[0]
    count, away = pair_ref.shape[0], pair_ref.shape[1]
    span = away // (groups - 1)
    loads = [
        pltpu.make_async_copy(source, there, load_sem.at[i])
        for i, (source, there) in enumerate(
            [(wo_hbm, wo_ref), (w_up_hbm, w_up_ref), (w_down_hbm, w_down_ref), (grad_out_hbm, grad_out_ref)]
        )
    ]
    for copy in loads:
        copy.start()
    order, start, bounds = sentence_order(me, len_ref)
    fill_live_bias(live_ref, me, groups, list(range(1, groups)), span, src_ref, order)
    pack_heads(q_pack_ref, lambda first, size: query_ref[first : first + size, :], width)
    pair_copies = []
    for j in range(count):
        for part in range(1, groups):
            block = came_refs[part - 1][order[j]]
            pair_ref[j, pl.ds((part - 1) * span, span), :] = dot(block, wkv_ref[...]).astype(BF16)
        value_t_ref[j] = pair_ref[j, :, width:].T
        copy = pltpu.make_async_copy(pair_ref.at[j], pair_hbm.at[j, pl.ds(span, away), :], pair_sem.at[j])
        copy.start()
        pair_copies.append(copy)
    units = cross_units(bounds, half)
    tiles = rows // TILE

    def cross_step(pair):
        slab = slab_of(pair)
        for tile, sentence, columns in units:
            here = tile_columns(tile)
            row = pl.ds(pair * tiles + tile, 1)
            scores = dot_nt(pair_ref[sentence, :, slab], q_pack_ref[tile, :, slab]) + live_ref[sentence]
            before = top_ref[row, :]
            top = jnp.maximum(jnp.max(scores, axis=0, keepdims=True), before)
            weights = jnp.exp(scores - top)
            scale = jnp.exp(before - top)
            total = jnp.sum(weights, axis=0, keepdims=True) + sum_ref[row, :] * scale
            result = own_sides(dot(value_t_ref[sentence, slab, :], weights.astype(BF16)))
            result = (result + part_ref[slab, here] * side_rows(scale)) * side_rows(1.0 / total)
            norm = top + jnp.log(total)
            if columns is not None:
                result = jnp.where(columns[:, :TILE], result, attn_t_ref[slab, here])
                norm = jnp.where(columns, norm, norm_ref[row, :])
            attn_t_ref[slab, here] = result
            norm_ref[row, :] = norm

    attn_t_ref[...] = jnp.zeros_like(attn_t_ref)
    norm_ref[...] = jnp.zeros_like(norm_ref)
    each_pair(cross_step)
    attn_t_low = attn_t_ref[...].astype(BF16)
    loads[0].wait()
    unit_one, _ = norm_parts(hidden_one_ref[...])
    normed_one = unit_one * gain_ref[0:1] + bias_row_ref[0:1]
    hidden_two = normed_one + dot(attn_t_low.T, wo_ref[...])
    unit_two, inverse_two = norm_parts(hidden_two)
    normed_two = unit_two * gain_ref[1:2] + bias_row_ref[1:2]
    normed_two_low = normed_two.astype(BF16)
    chunk = width
    chunks = w_down_ref.shape[0] // chunk
    loads[1].wait()
    loads[2].wait()

    def up_step(c, carry):
        cols = pl.ds(pl.multiple_of(c * chunk, chunk), chunk)
        upper = dot(normed_two_low, w_up_ref[:, cols])
        sigma = 0.5 * jnp.tanh(0.5 * upper) + 0.5
        active = (upper * sigma).astype(BF16)
        active_ref[:, cols] = active
        slope_ref[:, cols] = sigma * (1.0 + upper * (1.0 - sigma))
        return carry

    lax.fori_loop(0, chunks, up_step, 0)

    unit_three, inverse_three = norm_parts(normed_two + dot(active_ref[...], w_down_ref[...]))
    result = (unit_three * gain_ref[2:3] + bias_row_ref[2:3]).astype(BF16)
    out_ref[...] = dot(unsort_matrix(rows, start), result).astype(BF16)
    loads[3].wait()
    upstream = dot(sort_matrix(rows, start), grad_out_ref[...])
    grad_three, gain_three, bias_three = norm_backward(upstream, unit_three, inverse_three, gain_ref[2:3])
    grad_down = grad_three.astype(BF16)
    normed_two_t = normed_two_low.T

    def down_step(c, carry):
        cols = pl.ds(pl.multiple_of(c * chunk, chunk), chunk)
        grad_upper = (dot_nt(grad_down, w_down_ref[cols, :]) * slope_ref[:, cols]).astype(BF16)
        down_part = dot_tn(active_ref[:, cols], grad_down).astype(BF16)
        up_part = dot(normed_two_t, grad_upper).astype(BF16)
        half_index, here = c // (chunks // 2), lax.rem(c, chunks // 2)
        down_rows = pl.ds(pl.multiple_of(here * chunk, chunk), chunk)
        up_rows = pl.ds(pl.multiple_of((chunks // 2 + here) * chunk, chunk), chunk)
        halves_ref[half_index, down_rows, :] = down_part
        halves_ref[half_index, up_rows, :] = up_part
        grad_upper_ref[:, cols] = grad_upper
        return carry

    lax.fori_loop(0, chunks, down_step, 0)

    most = chunks * chunk
    core = me_ref[1]
    stores = [
        pltpu.make_async_copy(
            halves_ref.at[half_index, pl.ds(first, size)], there.at[pl.ds(first, size)], store_sem.at[i]
        )
        for i, (half_index, there, first, size) in enumerate(
            [
                (1 - core, send_hbm, 0, most),
                (core, keep_hbm, 0, most),
                (1 - core, send_hbm, most, halves_ref.shape[1] - most),
                (core, keep_hbm, most, halves_ref.shape[1] - most),
            ]
        )
    ]
    stores[0].start()
    stores[1].start()
    upstream_two = grad_three + dot_nt(grad_upper_ref[...], w_up_ref[...])
    grad_two, gain_two, bias_two = norm_backward(upstream_two, unit_two, inverse_two, gain_ref[1:2])
    grad_two_low = grad_two.astype(BF16)
    wo_grad = dot(attn_t_low, grad_two_low).astype(BF16)
    used = most + width // 2
    for half_index in range(2):
        piece = wo_grad[half_index * (width // 2) : (half_index + 1) * (width // 2)]
        halves_ref[half_index, pl.ds(most, width // 2), :] = piece
        if halves_ref.shape[1] > used:
            halves_ref[half_index, used:, :] = jnp.zeros((halves_ref.shape[1] - used, width), BF16)
    stores[2].start()
    stores[3].start()
    grad_hidden_ref[...] = grad_two
    grad_attn = dot_nt(grad_two_low, wo_ref[...]).astype(BF16)
    grad_attn_ref[...] = grad_attn
    product = grad_attn.T.astype(F32) * attn_t_ref[...]
    for pair in range(PAIRS):
        for side in range(2):
            first = pair * SLAB + side * SIDE
            along = jnp.sum(product[first : first + SIDE], axis=0, keepdims=True)
            for t in range(tiles):
                along_ref[pair * tiles + t : pair * tiles + t + 1, side * TILE : (side + 1) * TILE] = along[
                    :, t * TILE : (t + 1) * TILE
                ]
    ln_ref[...] = jnp.concatenate([gain_two, gain_three, bias_two, bias_three], axis=0)
    for copy in pair_copies + stores:
        copy.wait()


def cross_backward_kernel(
    groups,
    block,
    me_ref,
    len_ref,
    src_ref,
    query_ref,
    norm_ref,
    along_ref,
    grad_attn_ref,
    pair_hbm,
    pair_grad_ref,
    query_grad_t_ref,
    pair_ref,
    live_ref,
    q_pack_ref,
    g_pack_ref,
    key_t_ref,
    query_sum_ref,
    sum_ref,
    load_sem,
):
    rows, width = query_ref.shape
    half = rows // 2
    me = me_ref[0]
    sentences, places = pair_ref.shape[0], pair_ref.shape[1]
    first_sentence = 0 if block == 0 else 1
    load = pltpu.make_async_copy(pair_hbm.at[pl.ds(first_sentence, sentences)], pair_ref, load_sem.at[0])
    load.start()
    order, start, bounds = sentence_order(me, len_ref)
    mine = order[:1] if block == 0 else order[1:]
    fill_live_bias(live_ref, me, groups, list(range(groups)), places // groups, src_ref, mine)
    low = block * half
    pack_heads(q_pack_ref, lambda first, size: query_ref[low + first : low + first + size, :], width)
    pack_heads(g_pack_ref, lambda first, size: grad_attn_ref[low + first : low + first + size, :], width)
    tiles, per = rows // TILE, half // TILE
    units = cross_units(bounds, half)
    units = units[:per] if block == 0 else units[per:]
    load.wait()
    for j in range(sentences):
        key_t_ref[j] = pair_ref[j, :, :width].T

    def pair_step(pair):
        slab, value_slab = slab_of(pair), slab_of(pair, width)
        query_sum_ref[...] = jnp.zeros_like(query_sum_ref)
        sum_ref[...] = jnp.zeros_like(sum_ref)
        for tile, sentence, columns in units:
            j = sentence - first_sentence
            t = tile - block * per
            here = tile_columns(t)
            row = pl.ds(pair * tiles + tile, 1)
            q_rows, g_rows = q_pack_ref[t, :, slab], g_pack_ref[t, :, slab]
            norm = norm_ref[row, :]
            if columns is not None:
                norm = jnp.where(columns, norm, -MASKED)
            scores = dot_nt(pair_ref[j, :, slab], q_rows) + live_ref[j]
            probs = jnp.exp(scores - norm)
            grad_probs = dot_nt(pair_ref[j, :, value_slab], g_rows)
            grad_scores = (probs * (grad_probs - along_ref[row, :])).astype(BF16)
            sum_ref[j, :, :SLAB] += dot(grad_scores, q_rows)
            sum_ref[j, :, SLAB:] += dot(probs.astype(BF16), g_rows)
            query_sum_ref[:, here] += own_sides(dot(key_t_ref[j, slab, :], grad_scores))
        query_grad_t_ref[slab, :] = (query_sum_ref[...] * 0.125).astype(BF16)
        pair_grad_ref[:, :, slab] = sum_ref[:, :, :SLAB].astype(BF16)
        pair_grad_ref[:, :, value_slab] = sum_ref[:, :, SLAB:].astype(BF16)

    for pair in range(PAIRS):
        pair_step(pair)


def memory_weight_kernel(groups, me_ref, len_ref, pair_grad_long_ref, pair_grad_rest_ref, memory_ref, *refs):
    came_refs = refs[: groups - 1]
    wkv_grad_ref, total_ref = refs[groups - 1 :]
    width = memory_ref.shape[2]
    me = me_ref[0]
    count = len_ref.shape[1]
    span = pair_grad_long_ref.shape[1] // groups
    order, _, _ = sentence_order(me, len_ref)
    for j in range(count):
        pair_grad_ref, here = (pair_grad_long_ref, 0) if j == 0 else (pair_grad_rest_ref, j - 1)
        blocks = [memory_ref[me * count + order[j]]] + [ref[order[j]] for ref in came_refs]
        term = dot_tn(jnp.concatenate(blocks, axis=0), pair_grad_ref[here])
        if j == 0:
            total_ref[...] = term
        else:
            total_ref[...] += term
    wkv_grad_ref[0] = total_ref[:, :width].astype(BF16)
    wkv_grad_ref[1] = total_ref[:, width:].astype(BF16)


def memory_grad_kernel(pieces, me_ref, len_ref, pair_grad_long_ref, pair_grad_rest_ref, wkv_ref, *outs):
    count = len_ref.shape[1]
    order, _, _ = sentence_order(me_ref[0], len_ref)
    for j in range(count):
        pair_grad_ref, here = (pair_grad_long_ref, 0) if j == 0 else (pair_grad_rest_ref, j - 1)
        for (first, size), out in zip(pieces, outs):
            out[order[j]] = dot_nt(pair_grad_ref[here, pl.ds(first, size), :], wkv_ref[...]).astype(BF16)


def first_norm_backward_kernel(
    me_ref,
    hidden_one_ref,
    query_grad_t_long_ref,
    query_grad_t_rest_ref,
    grad_hidden_two_ref,
    wq_ref,
    w_out_ref,
    self_attn_t_ref,
    gain_ref,
    bias_row_ref,
    ln_in_ref,
    wkv_grad_ref,
    keep_ref,
    send_ref,
    grad_hidden_ref,
    grad_self_ref,
):
    width = wq_ref.shape[0]
    unit_one, inverse_one = norm_parts(hidden_one_ref[...])
    normed_one = (unit_one * gain_ref[0:1] + bias_row_ref[0:1]).astype(BF16)
    query_grad = jnp.concatenate([query_grad_t_long_ref[...].T, query_grad_t_rest_ref[...].T], axis=0)
    upstream = grad_hidden_two_ref[...] + dot_nt(query_grad, wq_ref[...])
    grad_one, gain_one, bias_one = norm_backward(upstream, unit_one, inverse_one, gain_ref[0:1])
    grad_hidden_ref[...] = grad_one
    grad_one_low = grad_one.astype(BF16)
    grad_self_ref[...] = dot_nt(grad_one_low, w_out_ref[...]).astype(BF16)
    wq_grad = dot_tn(normed_one, query_grad).astype(BF16)
    w_out_grad = dot(self_attn_t_ref[...], grad_one_low).astype(BF16)
    norms = jnp.concatenate(
        [gain_one, ln_in_ref[0:2], bias_one, ln_in_ref[2:4], jnp.zeros((LN_ROWS - 6, width), F32)], axis=0
    ).astype(BF16)

    def halves(low_ref, high_ref):
        low_ref[:width, :] = wq_grad
        low_ref[width : 2 * width, :] = wkv_grad_ref[0]
        high_ref[:width, :] = wkv_grad_ref[1]
        high_ref[width : 2 * width, :] = w_out_grad

    @pl.when(me_ref[1] == 0)
    def _():
        halves(keep_ref, send_ref)

    @pl.when(me_ref[1] != 0)
    def _():
        halves(send_ref, keep_ref)

    keep_ref[2 * width :, :] = norms
    send_ref[2 * width :, :] = norms


def self_backward_kernel(
    me_ref,
    len_ref,
    qkv_ref,
    norm_ref,
    grad_attn_ref,
    sorted_ref,
    grad_triple_ref,
    *refs,
):
    keep_refs, send_refs = refs[:LAST_PARTS], refs[LAST_PARTS : 2 * LAST_PARTS]
    self_backward(
        me_ref,
        len_ref,
        qkv_ref,
        norm_ref,
        grad_attn_ref,
        sorted_ref,
        grad_triple_ref,
        keep_refs,
        send_refs,
        *refs[2 * LAST_PARTS :],
    )


def self_backward(
    me_ref,
    len_ref,
    qkv_ref,
    norm_ref,
    grad_attn_ref,
    sorted_ref,
    grad_triple_ref,
    keep_refs,
    send_refs,
    bias_ref,
    q_pack_ref,
    g_pack_ref,
    key_t_ref,
    query_grad_t_ref,
):
    rows, width = sorted_ref.shape
    half = rows // 2
    _, _, bounds = sentence_order(me_ref[0], len_ref)
    fill_self_bias(bias_ref, bounds, half)
    pack_heads(q_pack_ref, lambda first, size: qkv_ref[first : first + size, :width], width)
    pack_heads(g_pack_ref, lambda first, size: grad_attn_ref[first : first + size, :], width)
    key_t_ref[...] = qkv_ref[:, width : 2 * width].T
    tiles, per = rows // TILE, half // TILE

    def pair_step(pair):
        slab, key_slab, value_slab = slab_of(pair), slab_of(pair, width), slab_of(pair, 2 * width)
        sums = [[None, None] for _ in range(tiles)]
        for t in range(tiles):
            first, size = self_keys(t, half)
            span = pl.ds(first, size)
            q_rows, g_rows = q_pack_ref[t, :, slab], g_pack_ref[t, :, slab]
            scores = dot_nt(qkv_ref[span, key_slab], q_rows) + bias_ref[t, :size, :]
            probs = jnp.exp(scores - norm_ref[pl.ds(pair * tiles + t, 1), :])
            grad_probs = dot_nt(qkv_ref[span, value_slab], g_rows)
            along = jnp.sum(probs * grad_probs, axis=0, keepdims=True)
            grad_scores = (probs * (grad_probs - along)).astype(BF16)
            parts = dot(grad_scores, q_rows), dot(probs.astype(BF16), g_rows)
            for i in range(size // TILE):
                spot = sums[first // TILE + i]
                for k in range(2):
                    piece = parts[k][i * TILE : (i + 1) * TILE]
                    spot[k] = piece if spot[k] is None else spot[k] + piece
            query_grad_t_ref[slab, tile_columns(t)] = (
                own_sides(dot(key_t_ref[slab, span], grad_scores)) * 0.125
            ).astype(BF16)
        for t in range(tiles):
            grad_triple_ref[pl.ds(t * TILE, TILE), key_slab] = sums[t][0].astype(BF16)
            grad_triple_ref[pl.ds(t * TILE, TILE), value_slab] = sums[t][1].astype(BF16)

    for pair in range(PAIRS):
        pair_step(pair)
    grad_triple_ref[:, :width] = query_grad_t_ref[...].T
    sorted_t = sorted_ref[...].T
    grads = [
        dot(sorted_t, grad_triple_ref[:, part * width : (part + 1) * width]).astype(BF16)
        for part in range(3)
    ]
    short = width // 2

    low = jnp.concatenate([grads[0], grads[1][:short]], axis=0)
    high = jnp.concatenate([grads[1][short:], grads[2]], axis=0)
    size = keep_refs[0].shape[0]

    def halves(low_refs, high_refs):
        for i in range(LAST_PARTS):
            low_refs[i][...] = low[i * size : (i + 1) * size]
            high_refs[i][...] = high[i * size : (i + 1) * size]

    @pl.when(me_ref[1] == 0)
    def _():
        halves(keep_refs, send_refs)

    @pl.when(me_ref[1] != 0)
    def _():
        halves(send_refs, keep_refs)


def target_kernel(me_ref, len_ref, grad_triple_ref, w_qkv_ref, grad_hidden_ref, grad_target_ref):
    rows = grad_hidden_ref.shape[0]
    _, start, _ = sentence_order(me_ref[0], len_ref)
    result = grad_hidden_ref[...] + dot_nt(grad_triple_ref[...], w_qkv_ref[...])
    grad_target_ref[...] = dot(unsort_matrix(rows, start), result.astype(BF16)).astype(BF16)


def tree_sum(terms):
    while len(terms) > 1:
        terms = [terms[i] + terms[i + 1] for i in range(0, len(terms), 2)]
    return terms[0]


def rows_of(ref, first, count):
    return ref[pl.ds(pl.multiple_of(first, 16), count), :].astype(F32)


def first_split_kernel(segments, ln, peers, spot_ref, *refs):
    ins, refs = refs[: 2 * segments], refs[2 * segments :]
    extra = LN_ROWS if ln else 0
    if segments == 1 and not ln:
        for d, out in enumerate(refs):
            size = out.shape[0]
            first = (spot_ref[2] ^ d) * size
            out[...] = (rows_of(ins[0], first, size) + rows_of(ins[1], first, size)).astype(BF16)
        return
    outs, sum_ref = refs[:-1], refs[-1]
    size = outs[0].shape[0] - extra
    used = 0
    for i in range(segments):
        keep_ref, came_ref = ins[2 * i], ins[2 * i + 1]
        count = keep_ref.shape[0] - (extra if i == 0 else 0)
        sum_ref[used : used + count, :] = (rows_of(keep_ref, 0, count) + rows_of(came_ref, 0, count)).astype(BF16)
        if i == 0 and ln:
            tail = (rows_of(keep_ref, count, LN_ROWS) + rows_of(came_ref, count, LN_ROWS)).astype(BF16)
        used += count
    if sum_ref.shape[0] > used:
        sum_ref[used:, :] = jnp.zeros((sum_ref.shape[0] - used, sum_ref.shape[1]), BF16)
    for d, out in enumerate(outs):
        out[:size, :] = sum_ref[pl.ds(pl.multiple_of((spot_ref[2] ^ d) * size, 16), size), :]
        if ln:
            out[size:, :] = tail


def split_kernel(stage, ln, peers, spot_ref, *refs):
    ins, outs = refs[:peers], refs[peers:]
    extra = LN_ROWS if ln else 0
    size = outs[0].shape[0] - extra
    if ln:
        tail = tree_sum([rows_of(ref, size * len(outs), LN_ROWS) for ref in ins]).astype(BF16)
    for d, out in enumerate(outs):
        first = (spot_ref[2 + stage] ^ d) * size
        out[:size, :] = tree_sum([rows_of(ref, first, size) for ref in ins]).astype(BF16)
        if ln:
            out[size:, :] = tail


def total_kernel(ln, count, *refs):
    ins, outs = refs[:count], refs[count:]
    size = outs[0].shape[0]
    outs[0][...] = tree_sum([rows_of(ref, 0, size) for ref in ins]).astype(BF16)
    if ln:
        norms = tree_sum([rows_of(ref, size, LN_ROWS) for ref in ins])
        outs[1][...] = norms[:3]
        outs[2][...] = norms[3:6]


def join_kernel(stage, spot_ref, *refs):
    out_ref = refs[-1]
    for d, ref in enumerate(refs[:-1]):
        size = ref.shape[0]
        out_ref[pl.ds(pl.multiple_of((spot_ref[2 + stage] ^ d) * size, 16), size), :] = ref[...]


def finish_kernel(items, peers, twisted, pieces, held, spot_ref, *refs):
    arrays, refs = refs[: len(items)], refs[len(items) + held :]
    outs, (wide_ref, sem) = refs[:-2], refs[-2:]
    core = spot_ref[1]
    size, width = wide_ref.shape[1:]
    copies = []
    for k, ref in enumerate(arrays):
        wide_ref[k] = ref[...].astype(F32)
        d, other = items[k]
        half = 1 - core if other else core
        place = spot_ref[3 if twisted and other else 2] ^ d
        for i in range(2):
            for j in range(peers):
                cut = []
                for piece_half, first, rows, out, row, col in pieces:
                    low, high = max(first, j * size), min(first + rows, (j + 1) * size)
                    if piece_half == i and low < high:
                        there = outs[out].at[pl.ds(row + low - first, high - low), pl.ds(col, width)]
                        here = wide_ref.at[k, pl.ds(low - j * size, high - low), :]
                        cut.append(pltpu.make_async_copy(here, there, sem.at[k, len(cut)]))
                copies.append(((half == i) & (place == j), cut))
                _start_all(*copies[-1])
    for chosen, cut in copies:
        _wait_all(chosen, cut)


def _start_all(chosen, cut):
    @pl.when(chosen)
    def _():
        for copy in cut:
            copy.start()


def _wait_all(chosen, cut):
    @pl.when(chosen)
    def _():
        for copy in cut:
            copy.wait()


class Summing:
    def __init__(self, rows, width, ln):
        self.width, self.ln = width, ln
        self.dp, self.mem = lax.axis_size("dp"), lax.axis_size("mem")
        z_size = 4
        x_size = self.dp // (2 * z_size)
        self.sizes = (x_size, self.mem, z_size)
        self.twisted = x_size == self.mem
        self.chunk = -(-rows // (16 * math.prod(self.sizes))) * 16
        self.rows = self.chunk * math.prod(self.sizes)

    def after(self, stage):
        return self.rows // math.prod(self.sizes[:stage])

    def axis(self, stage, core):
        return 1 - stage if self.twisted and core == 1 and stage < 2 else stage

    def coords(self, dp, mem):
        return [dp // 2 % self.sizes[0], mem, dp // (2 * self.sizes[0])], dp % 2

    def spot(self, me, dp):
        (x, mem, z), core = self.coords(dp, me)
        if self.twisted:
            x, mem = jnp.where(core == 0, x, mem), jnp.where(core == 0, mem, x)
        return jnp.stack([me, core, x, mem, z]).astype(jnp.int32)

    def permute(self, array, stage, offset):
        pairs = []
        for dp in range(self.dp):
            for mem in range(self.mem):
                spots, core = self.coords(dp, mem)
                if stage is None:
                    core ^= offset
                else:
                    spots[self.axis(stage, core)] ^= offset
                to_dp = (spots[2] * self.sizes[0] + spots[0]) * 2 + core
                pairs.append((dp * self.mem + mem, to_dp * self.mem + spots[1]))
        return lax.ppermute(array, ("dp", "mem"), pairs)

    def core_swap(self, send):
        return self.permute(send, None, 1)

    def swap(self, arrays, stage):
        return [arrays[0]] + [self.permute(array, stage, d) for d, array in enumerate(arrays) if d > 0]

    def spread(self, stage, array):
        return [array] + [self.permute(array, stage, d) for d in range(1, self.sizes[stage])]

    def messages(self, stage):
        size = self.after(stage + 1) + (LN_ROWS if self.ln else 0)
        return [((size, self.width), BF16)] * self.sizes[stage]

    def first_split(self, spot, *arrays):
        kernel = functools.partial(first_split_kernel, len(arrays) // 2, self.ln, self.sizes[0])
        scratch = [] if len(arrays) == 2 and not self.ln else [((self.rows, self.width), BF16)]
        return call(kernel, self.messages(0), scratch, 1, spot, *arrays, work=0.01)

    def split(self, stage, spot, arrays, work=0.01):
        kernel = functools.partial(split_kernel, stage, self.ln, self.sizes[stage - 1])
        return call(kernel, self.messages(stage), [], 1, spot, *arrays, work=work)

    def total(self, arrays, work=0.01):
        outs = [((self.chunk, self.width), BF16)]
        if self.ln:
            outs = outs + [((3, self.width), F32)] * 2
        return call(functools.partial(total_kernel, self.ln, self.sizes[2]), outs, [], 0, *arrays, work=work)

    def join(self, stage, spot, arrays, work=0.01):
        outs = [((self.after(stage), self.width), BF16)]
        return call(functools.partial(join_kernel, stage), outs, [], 1, spot, *arrays, work=work)[0]

    def finish(self, spot, arrays, items, pieces, outs, held=()):
        kernel = functools.partial(finish_kernel, items, self.sizes[0], self.twisted, pieces, len(held))
        size = self.after(1)
        scratch = [((len(arrays), size, self.width), F32), pltpu.SemaphoreType.DMA((len(arrays), len(pieces)))]
        aliases = {1 + len(arrays) + i: i for i in range(len(held))}
        return call(
            kernel,
            outs,
            scratch,
            1,
            spot,
            *arrays,
            *held,
            work=1,
            vmem=40,
            hbm_in=len(held),
            hbm_out=len(outs),
            aliases=aliases,
        )


def call(kernel, outs, scratch, scalars, *arrays, work=0.5, vmem=0, hbm_in=0, hbm_out=0, aliases=None):
    plain = len(arrays) - scalars - hbm_in
    if not vmem:
        blocks = [(array.shape, array.dtype) for array in arrays[scalars:]] + outs
        blocks = blocks + [entry for entry in scratch if isinstance(entry, tuple)]
        vmem = max(16, sum(math.prod(shape) * jnp.dtype(kind).itemsize for shape, kind in blocks) // MIB + 7)
    specs = [pl.BlockSpec(memory_space=pltpu.SMEM)] * scalars
    specs = specs + [pl.BlockSpec(memory_space=pltpu.VMEM)] * plain
    specs = specs + [pl.BlockSpec(memory_space=pl.ANY)] * hbm_in
    out_specs = [pl.BlockSpec(memory_space=pltpu.VMEM)] * (len(outs) - hbm_out)
    out_specs = out_specs + [pl.BlockSpec(memory_space=pl.ANY)] * hbm_out
    return pl.pallas_call(
        kernel,
        out_shape=[jax.ShapeDtypeStruct(shape, kind) for shape, kind in outs],
        in_specs=specs,
        out_specs=out_specs,
        scratch_shapes=[pltpu.VMEM(*entry) if isinstance(entry, tuple) else entry for entry in scratch],
        input_output_aliases=aliases or {},
        compiler_params=pltpu.CompilerParams(vmem_limit_bytes=vmem * MIB),
        cost_estimate=pl.CostEstimate(flops=int(work * 1e9), bytes_accessed=int(work * 3e6), transcendentals=0),
    )(*arrays)


def middle(
    groups, first_sum, stats, spot, tgt_len, src_len, hidden_one, query, part, part_top, part_sum, wkv_cross,
    ln_gain, ln_bias, wo_cross, w_up, w_down, grad_out, pair_mine, came,
):
    rows, width = hidden_one.shape
    half, tiles = rows // 2, rows // TILE
    hidden_width = w_down.shape[0]
    count, places, _ = pair_mine.shape
    away = places // groups * (groups - 1)
    arrays = [spot, tgt_len, src_len, hidden_one, query, part, part_top, part_sum, wkv_cross, ln_gain, ln_bias]
    stay = [wo_cross, w_up, w_down, grad_out, pair_mine]

    def kernel(*refs):
        ins, refs = refs[: len(arrays)], refs[len(arrays) :]
        came_refs, refs = refs[: len(came)], refs[len(came) :]
        stay_refs, refs = refs[: len(stay)], refs[len(stay) :]
        outs, refs = refs[:9], refs[9:]
        middle_kernel(groups, *ins, *stay_refs, *came_refs, *outs[:3], *outs[6:8], *outs[3:6], outs[8], *refs)

    result_out, cross_norm, cross_along, grad_hidden_two, grad_attn, ln_part, keep_one, send_one, pair_all = call(
        kernel,
        [
            ((rows, width), BF16),
            (stats, F32),
            (stats, F32),
            ((rows, width), F32),
            ((rows, width), BF16),
            ((4, width), F32),
            ((first_sum.rows, width), BF16),
            ((first_sum.rows, width), BF16),
            ((count, places, 2 * width), BF16),
        ],
        [
            ((width, width), BF16),
            ((width, hidden_width), BF16),
            ((hidden_width, width), BF16),
            ((rows, width), BF16),
            ((count, away, 2 * width), BF16),
            ((2, first_sum.rows, width), BF16),
            ((count, away, 2 * TILE), F32),
            ((tiles, 2 * TILE, width), BF16),
            ((count, width, away), BF16),
            ((width, rows), F32),
            ((rows, hidden_width), BF16),
            ((rows, hidden_width), F32),
            ((rows, hidden_width), BF16),
            pltpu.SemaphoreType.DMA((4,)),
            pltpu.SemaphoreType.DMA((count,)),
            pltpu.SemaphoreType.DMA((4,)),
        ],
        3,
        *arrays,
        *came,
        *stay,
        vmem=60,
        hbm_in=len(stay),
        hbm_out=3,
        aliases={len(arrays) + len(came) + len(stay) - 1: 8},
    )
    return result_out, cross_norm, cross_along, keep_one, send_one, grad_hidden_two, grad_attn, ln_part, pair_all


def body(
    target,
    memory,
    grad_out,
    tgt_len,
    src_len,
    w_qkv,
    w_out,
    wq_cross,
    wkv_cross,
    wo_cross,
    w_up,
    w_down,
    ln_gain,
    ln_bias,
):
    rows, width = target.shape
    half = rows // 2
    tiles = rows // TILE
    hidden_width = w_down.shape[0]
    groups = lax.axis_size("mem")
    me = lax.axis_index("mem")
    count = tgt_len.shape[1]
    span = memory.shape[1]
    places, away = groups * span, (groups - 1) * span
    dp = lax.axis_index("dp")
    short = width // 2
    first_sum = Summing(hidden_width + short, width, False)
    second_sum = Summing(3 * width + short, width, True)
    spot = first_sum.spot(me, dp)
    stats = (PAIRS * tiles, 2 * TILE)

    came = []
    for shift in range(1, groups):
        pairs = [(i, (i + shift) % groups) for i in range(groups)]
        sent = lax.dynamic_slice_in_dim(memory, ((me + shift) % groups) * count, count, 0)
        came.append(lax.ppermute(sent, "mem", pairs))

    sorted_rows, qkv, self_norm, self_attn_t, hidden_one, query, part, part_top, part_sum, pair_mine = call(
        functools.partial(self_forward_kernel, groups),
        [
            ((rows, width), BF16),
            ((rows, 3 * width), BF16),
            (stats, F32),
            ((width, rows), BF16),
            ((rows, width), F32),
            ((rows, width), BF16),
            ((width, rows), F32),
            (stats, F32),
            (stats, F32),
            ((count, places, 2 * width), BF16),
        ],
        [
            ((tiles, half, 2 * TILE), F32),
            ((count, span, 2 * TILE), F32),
            ((tiles, 2 * TILE, width), BF16),
            ((width, rows), BF16),
            ((count, width, span), BF16),
            ((count, span, 2 * width), BF16),
            pltpu.SemaphoreType.DMA((count,)),
        ],
        3,
        spot,
        tgt_len,
        src_len,
        target,
        w_qkv,
        w_out,
        wq_cross,
        ln_gain,
        ln_bias,
        memory,
        wkv_cross,
        vmem=60,
        hbm_out=1,
    )
    result_out, cross_norm, cross_along, keep_one, send_one, grad_hidden_two, grad_attn, ln_part, pair_all = middle(
        groups, first_sum, stats, spot, tgt_len, src_len, hidden_one, query, part, part_top, part_sum, wkv_cross,
        ln_gain, ln_bias, wo_cross, w_up, w_down, grad_out, pair_mine, came,
    )
    came_one = first_sum.core_swap(send_one)

    def cross_backward(block):
        sentences = 1 if block == 0 else count - 1
        return call(
            functools.partial(cross_backward_kernel, groups, block),
            [((sentences, places, 2 * width), BF16), ((width, half), BF16)],
            [
                ((sentences, places, 2 * width), BF16),
                ((sentences, places, 2 * TILE), F32),
                ((half // TILE, 2 * TILE, width), BF16),
                ((half // TILE, 2 * TILE, width), BF16),
                ((sentences, width, places), BF16),
                ((SLAB, half), F32),
                ((sentences, places, 2 * SLAB), F32),
                pltpu.SemaphoreType.DMA((1,)),
            ],
            3,
            spot,
            tgt_len,
            src_len,
            query,
            cross_norm,
            cross_along,
            grad_attn,
            pair_all,
            work=10,
            vmem=58 if block == 0 else 32,
            hbm_in=1,
        )

    pair_grad_long, query_grad_t_long = cross_backward(0)
    came_one, pair_grad_long = lax.optimization_barrier((came_one, pair_grad_long))
    parts_one = first_sum.first_split(spot, keep_one, came_one)
    parts_one, pair_all = lax.optimization_barrier((parts_one, pair_all))
    parts_one = first_sum.swap(parts_one, 0)
    pair_grad_rest, query_grad_t_rest = cross_backward(1)
    (wkv_grad,) = call(
        functools.partial(memory_weight_kernel, groups),
        [((2, width, width), BF16)],
        [((width, 2 * width), F32)],
        2,
        spot,
        tgt_len,
        pair_grad_long,
        pair_grad_rest,
        memory,
        *came,
        work=1,
        vmem=32,
    )
    keep_mid, send_mid, grad_hidden_one, grad_self = call(
        first_norm_backward_kernel,
        [
            ((2 * width + LN_ROWS, width), BF16),
            ((2 * width + LN_ROWS, width), BF16),
            ((rows, width), F32),
            ((rows, width), BF16),
        ],
        [],
        1,
        spot,
        hidden_one,
        query_grad_t_long,
        query_grad_t_rest,
        grad_hidden_two,
        wq_cross,
        w_out,
        self_attn_t,
        ln_gain,
        ln_bias,
        ln_part,
        wkv_grad,
        work=0.1,
        vmem=24,
    )
    def memory_grad(pieces, pair_grad_long):
        return call(
            functools.partial(memory_grad_kernel, pieces),
            [((count, size, width), BF16) for _, size in pieces],
            [],
            2,
            spot,
            tgt_len,
            pair_grad_long,
            pair_grad_rest,
            wkv_cross,
            work=0.01,
            vmem=32,
        )

    def send_back(grads):
        return [
            lax.ppermute(array, "mem", [(k, (k - 1 - i) % groups) for k in range(groups)])
            for i, array in enumerate(grads)
        ]

    parts_one, grad_self = lax.optimization_barrier((parts_one, grad_self))
    parts_one = first_sum.split(1, spot, parts_one)
    parts_one, grad_self, pair_grad_long = lax.optimization_barrier((parts_one, grad_self, pair_grad_long))
    parts_one = first_sum.swap(parts_one, 1)
    grad_late = memory_grad(
        [(part * span + span // 2, span // 2) for part in range(1, groups)], pair_grad_long
    )
    backs_late = send_back(grad_late)
    grad_late, grad_self = lax.optimization_barrier((grad_late, grad_self))
    grad_triple, *last = call(
        self_backward_kernel,
        [((rows, 3 * width), BF16)] + [(((width + short) // LAST_PARTS, width), BF16)] * (2 * LAST_PARTS),
        [
            ((tiles, half, 2 * TILE), F32),
            ((tiles, 2 * TILE, width), BF16),
            ((tiles, 2 * TILE, width), BF16),
            ((width, rows), BF16),
            ((width, rows), BF16),
        ],
        2,
        spot,
        tgt_len,
        qkv,
        self_norm,
        grad_self,
        sorted_rows,
        work=0.1,
        vmem=28,
    )
    came_mid = second_sum.core_swap(send_mid)
    parts_one, last, came_mid, pair_grad_long = lax.optimization_barrier(
        (parts_one, last, came_mid, pair_grad_long)
    )
    keep_last = last[:LAST_PARTS]
    came_last = [second_sum.core_swap(part) for part in last[LAST_PARTS:]]
    parts_one = first_sum.split(2, spot, parts_one)
    came_mid, parts_one = lax.optimization_barrier((came_mid, parts_one))
    parts_two = second_sum.first_split(
        spot, keep_mid, came_mid, *[part for both in zip(keep_last, came_last) for part in both]
    )
    parts_one = first_sum.swap(parts_one, 2)
    parts_two, pair_grad_long, grad_triple = lax.optimization_barrier((parts_two, pair_grad_long, grad_triple))
    parts_two = second_sum.swap(parts_two, 0)
    grad_mine, *grad_away = memory_grad(
        [(0, span)] + [(part * span, span // 2) for part in range(1, groups)], pair_grad_long
    )
    backs_late, grad_triple = lax.optimization_barrier((backs_late, grad_triple))
    (grad_target,) = call(
        target_kernel,
        [((rows, width), BF16)],
        [],
        2,
        spot,
        tgt_len,
        grad_triple,
        w_qkv,
        grad_hidden_one,
        work=30,
        vmem=16,
    )
    parts_one, grad_away, grad_target = lax.optimization_barrier((parts_one, grad_away, grad_target))
    spread_one = first_sum.spread(2, first_sum.total(parts_one)[0])
    backs_early = send_back(grad_away)
    parts_two = second_sum.swap(second_sum.split(1, spot, parts_two), 1)
    joined_one = first_sum.join(2, spot, spread_one, work=0.01)
    spread_one = first_sum.spread(1, joined_one)
    parts_two, joined_one = lax.optimization_barrier((parts_two, joined_one))
    parts_two = second_sum.split(2, spot, parts_two, work=0.01)
    spread_one, _ = lax.optimization_barrier((spread_one, parts_two))
    parts_two = second_sum.swap(parts_two, 2)
    joined_one = first_sum.join(1, spot, spread_one)
    spread_one = first_sum.spread(0, joined_one)
    parts_two, joined_one = lax.optimization_barrier((parts_two, joined_one))
    sum_two, *norm_sums = second_sum.total(parts_two, work=0.01)
    spread_two = second_sum.spread(2, sum_two)
    spread_two, backs_early = lax.optimization_barrier((spread_two, backs_early))
    spread_two = second_sum.spread(1, second_sum.join(2, spot, spread_two, work=6.3))
    joined_two = second_sum.join(1, spot, spread_two)
    spread_one, joined_two = lax.optimization_barrier((spread_one, joined_two))
    other_one = [first_sum.core_swap(array) for array in spread_one]
    chunks = hidden_width // width
    pieces = []
    for chunk in range(chunks):
        side, here = chunk // (chunks // 2), chunk % (chunks // 2)
        pieces.append((side, here * width, width, 0, chunk * width, 0))
        pieces.append((side, (chunks // 2 + here) * width, width, 1, 0, chunk * width))
    for side in range(2):
        pieces.append((side, chunks * width, short, 2, side * short, 0))
    grad_w_down, grad_w_up, grad_wo = first_sum.finish(
        spot,
        spread_one + other_one,
        [(d, other) for other in range(2) for d in range(len(spread_one))],
        pieces,
        [((hidden_width, width), F32), ((width, hidden_width), F32), ((width, width), F32)],
    )
    spread_two = second_sum.spread(0, joined_two)
    pieces = [
        (0, 0, width, 0, 0, 0),
        (0, width, width, 1, 0, 0),
        (0, 2 * width, width, 2, 0, 0),
        (0, 3 * width, short, 2, 0, width),
        (1, 0, width, 1, 0, width),
        (1, width, width, 3, 0, 0),
        (1, 2 * width, short, 2, short, width),
        (1, 2 * width + short, width, 2, 0, 2 * width),
    ]
    outs = [
        ((width, width), F32),
        ((width, 2 * width), F32),
        ((width, 3 * width), F32),
        ((width, width), F32),
    ]
    other_two = [second_sum.core_swap(spread_two[0])]
    own_two, grad_w_down = lax.optimization_barrier((spread_two[0], grad_w_down))
    held = second_sum.finish(spot, [own_two] + other_two, [(0, 0), (0, 1)], pieces, outs)
    spread_two, held = lax.optimization_barrier((spread_two, held))
    other_two = [second_sum.core_swap(array) for array in spread_two[1:]]
    offsets = range(1, len(spread_two))
    held = second_sum.finish(spot, spread_two[1:], [(d, 0) for d in offsets], pieces, outs, held)
    other_two, held = lax.optimization_barrier((other_two, held))
    grad_wq, grad_wkv, grad_w_qkv, grad_w_out = second_sum.finish(
        spot, other_two, [(d, 1) for d in offsets], pieces, outs, held
    )
    grad_memory = jnp.zeros(memory.shape, BF16)
    grad_memory = lax.dynamic_update_slice(grad_memory, grad_mine, (me * count, 0, 0))
    for part, backs in enumerate((backs_early, backs_late)):
        for i, grads in enumerate(backs):
            owner = (me + i + 1) % groups
            grad_memory = lax.dynamic_update_slice(grad_memory, grads, (owner * count, part * (span // 2), 0))
    return (
        result_out,
        grad_target,
        grad_memory,
        grad_w_qkv,
        grad_w_out,
        grad_wq,
        grad_wkv,
        grad_wo,
        grad_w_up,
        grad_w_down,
        *norm_sums,
    )


def solution(mesh):
    rows_spec = P(("dp", "mem"), None)
    memory_spec = P("dp", "mem", None)
    return jax.shard_map(
        body,
        mesh=mesh,
        in_specs=(rows_spec, memory_spec, rows_spec, P("dp", None), P("dp", None)) + (P(),) * 9,
        out_specs=(rows_spec, rows_spec, memory_spec) + (P(),) * 9,
        check_vma=False,
    )
```

```python
import functools
import math

import jax
import jax.numpy as jnp
from jax import lax
from jax.experimental import pallas as pl
from jax.experimental.pallas import tpu as pltpu
from jax.sharding import PartitionSpec as P

HEADS = 8
PAIRS = HEADS // 2
SLAB = 128
SIDE = SLAB // 2
TILE = 128
MASKED = -1e30
EPSILON = 1e-05
F32 = jnp.float32
BF16 = jnp.bfloat16
MIB = 1024 * 1024
LN_ROWS = 16
LAST_PARTS = 2


def dot(left, right):
    return jnp.dot(left, right, preferred_element_type=F32)


def dot_nt(left, right):
    return lax.dot_general(left, right, (((1,), (1,)), ((), ())), preferred_element_type=F32)


def dot_tn(left, right):
    return lax.dot_general(left, right, (((0,), (0,)), ((), ())), preferred_element_type=F32)


def iota(shape, axis):
    return lax.broadcasted_iota(jnp.int32, shape, axis)


def norm_parts(hidden):
    centre = hidden - jnp.mean(hidden, axis=-1, keepdims=True)
    inverse = lax.rsqrt(jnp.mean(centre * centre, axis=-1, keepdims=True) + EPSILON)
    return centre * inverse, inverse


def norm_backward(upstream, unit, inverse, gain_row):
    scaled = upstream * gain_row
    shifted = (
        scaled
        - jnp.mean(scaled, axis=-1, keepdims=True)
        - unit * jnp.mean(scaled * unit, axis=-1, keepdims=True)
    )
    gain_grad = jnp.sum(upstream * unit, axis=0, keepdims=True)
    return inverse * shifted, gain_grad, jnp.sum(upstream, axis=0, keepdims=True)


def sentence_order(me, len_ref):
    count = len_ref.shape[1]
    lengths = [len_ref[me, k] for k in range(count)]
    longest, best, start, running = jnp.int32(0), lengths[0], jnp.int32(0), jnp.int32(0)
    for k in range(1, count):
        running = running + lengths[k - 1]
        more = lengths[k] > best
        longest = jnp.where(more, k, longest)
        start = jnp.where(more, running, start)
        best = jnp.where(more, lengths[k], best)
    order = [longest] + [jnp.where(k < longest, k, k + 1) for k in range(count - 1)]
    bounds = [jnp.int32(0)]
    for k in range(1, count):
        bounds.append(bounds[-1] + len_ref[me, order[k]])
    return order, start, bounds


def moved_rows(index, start, half):
    return jnp.where(index < start, index + half, jnp.where(index < start + half, index - start, index))


def sort_matrix(rows, start):
    spot = moved_rows(iota((rows, rows), 1), start, rows // 2)
    return jnp.where(spot == iota((rows, rows), 0), 1.0, 0.0).astype(BF16)


def unsort_matrix(rows, start):
    spot = moved_rows(iota((rows, rows), 0), start, rows // 2)
    return jnp.where(spot == iota((rows, rows), 1), 1.0, 0.0).astype(BF16)


def side_masks(width):
    side = iota((1, width), 1) % SLAB
    first = jnp.where(side < SLAB // 2, 1.0, 0.0)
    return first.astype(BF16), (1.0 - first).astype(BF16)


def each_pair(step):
    def advance(pair, carry):
        step(pair)
        return carry

    lax.fori_loop(0, PAIRS, advance, 0)


def slab_of(pair, first=0):
    if isinstance(pair, int):
        return pl.ds(first + pair * SLAB, SLAB)
    return pl.ds(pl.multiple_of(first + pair * SLAB, SLAB), SLAB)


def pack_heads(out_ref, rows, width):
    even, odd = side_masks(width)
    for t in range(out_ref.shape[0]):
        tile = rows(t * TILE, TILE)
        out_ref[t, :TILE, :] = tile * even
        out_ref[t, TILE:, :] = tile * odd


def fill_self_bias(bias_ref, bounds, half):
    for t in range(bias_ref.shape[0]):
        block, inner = t // (half // TILE), t % (half // TILE)
        key = iota((half, 2 * TILE), 0)
        query = iota((half, 2 * TILE), 1) % TILE + inner * TILE
        allowed = key <= query
        if block == 1:
            first = jnp.zeros((half, 2 * TILE), jnp.int32)
            for bound in bounds[1:-1]:
                first = jnp.where(query >= bound, bound, first)
            allowed = allowed & (key >= first)
        bias_ref[t] = jnp.where(allowed, 0.0, MASKED)


def self_keys(t, half):
    per = half // TILE
    return (t // per) * half, (t % per + 1) * TILE


def fill_live_bias(bias_ref, me, groups, parts, span, src_ref, sentences):
    key = iota((span, bias_ref.shape[2]), 0)
    for j, sentence in enumerate(sentences):
        for i, part in enumerate(parts):
            place = lax.rem(me - part + groups, groups) * span + key
            live = place < src_ref[me, sentence]
            bias_ref[j, pl.ds(i * span, span), :] = jnp.where(live, 0.0, MASKED)


def cross_units(bounds, half):
    units = [(t, 0, None) for t in range(half // TILE)]
    middle = half // 2
    last = jnp.int32(1)
    for bound in bounds[1:-1]:
        last = last + jnp.where(bound < middle, 1, 0)
    ends = bounds[1:]
    column = iota((1, 2 * TILE), 1) % TILE
    for u in range(len(ends) + 1):
        early = u < last
        sentence = jnp.where(early, u + 1, u)
        tile = jnp.where(early, 0, 1)
        low, high = jnp.int32(0), ends[0]
        for k in range(1, len(ends)):
            low = jnp.where(sentence == k + 1, ends[k - 1], low)
            high = jnp.where(sentence == k + 1, ends[k], high)
        row = column + tile * TILE
        units.append((tile + half // TILE, sentence, (row >= low) & (row < high)))
    return units


def own_sides(both):
    return jnp.concatenate([both[:SIDE, :TILE], both[SIDE:, TILE:]], axis=0)


def side_rows(row):
    even = jnp.broadcast_to(row[:, :TILE], (SIDE, TILE))
    return jnp.concatenate([even, jnp.broadcast_to(row[:, TILE:], (SIDE, TILE))], axis=0)


def tile_columns(tile):
    if isinstance(tile, int):
        return pl.ds(tile * TILE, TILE)
    return pl.ds(pl.multiple_of(tile * TILE, TILE), TILE)


def self_forward_kernel(
    groups,
    me_ref,
    len_ref,
    src_ref,
    target_ref,
    w_qkv_ref,
    w_out_ref,
    wq_ref,
    gain_ref,
    bias_row_ref,
    memory_ref,
    wkv_ref,
    sorted_ref,
    qkv_ref,
    norm_ref,
    attn_t_ref,
    hidden_ref,
    query_ref,
    part_ref,
    top_ref,
    sum_ref,
    pair_out_ref,
    bias_ref,
    live_ref,
    q_pack_ref,
    value_t_ref,
    cross_value_t_ref,
    pair_ref,
    copy_sem,
):
    rows, width = target_ref.shape
    half = rows // 2
    me = me_ref[0]
    order, start, bounds = sentence_order(me, len_ref)
    count, span = pair_ref.shape[0], pair_ref.shape[1]
    copies = []
    for j in range(count):
        block = memory_ref[me * count + order[j]]
        pair_ref[j] = dot(block, wkv_ref[...]).astype(BF16)
        copy = pltpu.make_async_copy(
            pair_ref.at[j], pair_out_ref.at[j, pl.ds(0, span), :], copy_sem.at[j]
        )
        copy.start()
        copies.append(copy)
    sorted_rows = dot(sort_matrix(rows, start), target_ref[...]).astype(BF16)
    sorted_ref[...] = sorted_rows
    fill_self_bias(bias_ref, bounds, half)
    queries = (dot(sorted_rows, w_qkv_ref[:, :width]).astype(BF16) * 0.125).astype(BF16)
    qkv_ref[:, :width] = queries
    pack_heads(q_pack_ref, lambda first, size: queries[first : first + size], width)
    qkv_ref[:, width : 2 * width] = dot(sorted_rows, w_qkv_ref[:, width : 2 * width]).astype(BF16)
    values = dot(sorted_rows, w_qkv_ref[:, 2 * width :]).astype(BF16)
    qkv_ref[:, 2 * width :] = values
    value_t_ref[...] = values.T
    tiles = rows // TILE

    def self_step(pair):
        slab = slab_of(pair)
        for t in range(tiles):
            first, size = self_keys(t, half)
            keys = qkv_ref[pl.ds(first, size), slab_of(pair, width)]
            scores = dot_nt(keys, q_pack_ref[t, :, slab]) + bias_ref[t, :size, :]
            top = jnp.max(scores, axis=0, keepdims=True)
            weights = jnp.exp(scores - top)
            total = jnp.sum(weights, axis=0, keepdims=True)
            probs = (weights * (1.0 / total)).astype(BF16)
            both = dot(value_t_ref[slab, pl.ds(first, size)], probs)
            attn_t_ref[slab, tile_columns(t)] = own_sides(both).astype(BF16)
            norm_ref[pl.ds(pair * tiles + t, 1), :] = top + jnp.log(total)

    each_pair(self_step)
    hidden = sorted_rows.astype(F32) + dot(attn_t_ref[...].T, w_out_ref[...])
    hidden_ref[...] = hidden
    unit, _ = norm_parts(hidden)
    normed = (unit * gain_ref[0:1] + bias_row_ref[0:1]).astype(BF16)
    query_ref[...] = (dot(normed, wq_ref[...]).astype(BF16) * 0.125).astype(BF16)

    pack_heads(q_pack_ref, lambda first, size: query_ref[first : first + size, :], width)
    fill_live_bias(live_ref, me, groups, [0], span, src_ref, order)
    for j in range(count):
        cross_value_t_ref[j] = pair_ref[j, :, width:].T
    units = cross_units(bounds, half)

    def cross_step(pair):
        slab = slab_of(pair)
        for tile, sentence, columns in units:
            scores = dot_nt(pair_ref[sentence, :, slab], q_pack_ref[tile, :, slab]) + live_ref[sentence]
            top = jnp.max(scores, axis=0, keepdims=True)
            weights = jnp.exp(scores - top)
            total = jnp.sum(weights, axis=0, keepdims=True)
            result = own_sides(dot(cross_value_t_ref[sentence, slab, :], weights.astype(BF16)))
            here = tile_columns(tile)
            row = pl.ds(pair * tiles + tile, 1)
            if columns is not None:
                result = jnp.where(columns[:, :TILE], result, part_ref[slab, here])
                top = jnp.where(columns, top, top_ref[row, :])
                total = jnp.where(columns, total, sum_ref[row, :])
            part_ref[slab, here] = result
            top_ref[row, :] = top
            sum_ref[row, :] = total

    part_ref[...] = jnp.zeros_like(part_ref)
    top_ref[...] = jnp.zeros_like(top_ref)
    sum_ref[...] = jnp.ones_like(sum_ref)
    each_pair(cross_step)
    for copy in copies:
        copy.wait()


def middle_kernel(
    groups,
    me_ref,
    len_ref,
    src_ref,
    hidden_one_ref,
    query_ref,
    part_ref,
    top_ref,
    sum_ref,
    wkv_ref,
    gain_ref,
    bias_row_ref,
    wo_hbm,
    w_up_hbm,
    w_down_hbm,
    grad_out_hbm,
    pair_in_hbm,
    *refs,
):
    came_refs = refs[: groups - 1]
    (
        out_ref,
        norm_ref,
        along_ref,
        keep_hbm,
        send_hbm,
        grad_hidden_ref,
        grad_attn_ref,
        ln_ref,
        pair_hbm,
        wo_ref,
        w_up_ref,
        w_down_ref,
        grad_out_ref,
        pair_ref,
        halves_ref,
        live_ref,
        q_pack_ref,
        value_t_ref,
        attn_t_ref,
        active_ref,
        slope_ref,
        grad_upper_ref,
        load_sem,
        pair_sem,
        store_sem,
    ) = refs[groups - 1 :]
    rows, width = hidden_one_ref.shape
    half = rows // 2
    me = me_ref[0]
    count, away = pair_ref.shape[0], pair_ref.shape[1]
    span = away // (groups - 1)
    loads = [
        pltpu.make_async_copy(source, there, load_sem.at[i])
        for i, (source, there) in enumerate(
            [(wo_hbm, wo_ref), (w_up_hbm, w_up_ref), (w_down_hbm, w_down_ref), (grad_out_hbm, grad_out_ref)]
        )
    ]
    for copy in loads:
        copy.start()
    order, start, bounds = sentence_order(me, len_ref)
    fill_live_bias(live_ref, me, groups, list(range(1, groups)), span, src_ref, order)
    pack_heads(q_pack_ref, lambda first, size: query_ref[first : first + size, :], width)
    pair_copies = []
    for j in range(count):
        for part in range(1, groups):
            block = came_refs[part - 1][order[j]]
            pair_ref[j, pl.ds((part - 1) * span, span), :] = dot(block, wkv_ref[...]).astype(BF16)
        value_t_ref[j] = pair_ref[j, :, width:].T
        copy = pltpu.make_async_copy(pair_ref.at[j], pair_hbm.at[j, pl.ds(span, away), :], pair_sem.at[j])
        copy.start()
        pair_copies.append(copy)
    units = cross_units(bounds, half)
    tiles = rows // TILE

    def cross_step(pair):
        slab = slab_of(pair)
        for tile, sentence, columns in units:
            here = tile_columns(tile)
            row = pl.ds(pair * tiles + tile, 1)
            scores = dot_nt(pair_ref[sentence, :, slab], q_pack_ref[tile, :, slab]) + live_ref[sentence]
            before = top_ref[row, :]
            top = jnp.maximum(jnp.max(scores, axis=0, keepdims=True), before)
            weights = jnp.exp(scores - top)
            scale = jnp.exp(before - top)
            total = jnp.sum(weights, axis=0, keepdims=True) + sum_ref[row, :] * scale
            result = own_sides(dot(value_t_ref[sentence, slab, :], weights.astype(BF16)))
            result = (result + part_ref[slab, here] * side_rows(scale)) * side_rows(1.0 / total)
            norm = top + jnp.log(total)
            if columns is not None:
                result = jnp.where(columns[:, :TILE], result, attn_t_ref[slab, here])
                norm = jnp.where(columns, norm, norm_ref[row, :])
            attn_t_ref[slab, here] = result
            norm_ref[row, :] = norm

    attn_t_ref[...] = jnp.zeros_like(attn_t_ref)
    norm_ref[...] = jnp.zeros_like(norm_ref)
    each_pair(cross_step)
    attn_t_low = attn_t_ref[...].astype(BF16)
    loads[0].wait()
    unit_one, _ = norm_parts(hidden_one_ref[...])
    normed_one = unit_one * gain_ref[0:1] + bias_row_ref[0:1]
    hidden_two = normed_one + dot(attn_t_low.T, wo_ref[...])
    unit_two, inverse_two = norm_parts(hidden_two)
    normed_two = unit_two * gain_ref[1:2] + bias_row_ref[1:2]
    normed_two_low = normed_two.astype(BF16)
    chunk = width
    chunks = w_down_ref.shape[0] // chunk
    loads[1].wait()
    loads[2].wait()

    def up_step(c, carry):
        cols = pl.ds(pl.multiple_of(c * chunk, chunk), chunk)
        upper = dot(normed_two_low, w_up_ref[:, cols])
        sigma = 0.5 * jnp.tanh(0.5 * upper) + 0.5
        active = (upper * sigma).astype(BF16)
        active_ref[:, cols] = active
        slope_ref[:, cols] = sigma * (1.0 + upper * (1.0 - sigma))
        return carry

    lax.fori_loop(0, chunks, up_step, 0)

    unit_three, inverse_three = norm_parts(normed_two + dot(active_ref[...], w_down_ref[...]))
    result = (unit_three * gain_ref[2:3] + bias_row_ref[2:3]).astype(BF16)
    out_ref[...] = dot(unsort_matrix(rows, start), result).astype(BF16)
    loads[3].wait()
    upstream = dot(sort_matrix(rows, start), grad_out_ref[...])
    grad_three, gain_three, bias_three = norm_backward(upstream, unit_three, inverse_three, gain_ref[2:3])
    grad_down = grad_three.astype(BF16)
    normed_two_t = normed_two_low.T

    def down_step(c, carry):
        cols = pl.ds(pl.multiple_of(c * chunk, chunk), chunk)
        grad_upper = (dot_nt(grad_down, w_down_ref[cols, :]) * slope_ref[:, cols]).astype(BF16)
        down_part = dot_tn(active_ref[:, cols], grad_down).astype(BF16)
        up_part = dot(normed_two_t, grad_upper).astype(BF16)
        half_index, here = c // (chunks // 2), lax.rem(c, chunks // 2)
        down_rows = pl.ds(pl.multiple_of(here * chunk, chunk), chunk)
        up_rows = pl.ds(pl.multiple_of((chunks // 2 + here) * chunk, chunk), chunk)
        halves_ref[half_index, down_rows, :] = down_part
        halves_ref[half_index, up_rows, :] = up_part
        grad_upper_ref[:, cols] = grad_upper
        return carry

    lax.fori_loop(0, chunks, down_step, 0)

    most = chunks * chunk
    core = me_ref[1]
    stores = [
        pltpu.make_async_copy(
            halves_ref.at[half_index, pl.ds(first, size)], there.at[pl.ds(first, size)], store_sem.at[i]
        )
        for i, (half_index, there, first, size) in enumerate(
            [
                (1 - core, send_hbm, 0, most),
                (core, keep_hbm, 0, most),
                (1 - core, send_hbm, most, halves_ref.shape[1] - most),
                (core, keep_hbm, most, halves_ref.shape[1] - most),
            ]
        )
    ]
    stores[0].start()
    stores[1].start()
    upstream_two = grad_three + dot_nt(grad_upper_ref[...], w_up_ref[...])
    grad_two, gain_two, bias_two = norm_backward(upstream_two, unit_two, inverse_two, gain_ref[1:2])
    grad_two_low = grad_two.astype(BF16)
    wo_grad = dot(attn_t_low, grad_two_low).astype(BF16)
    used = most + width // 2
    for half_index in range(2):
        piece = wo_grad[half_index * (width // 2) : (half_index + 1) * (width // 2)]
        halves_ref[half_index, pl.ds(most, width // 2), :] = piece
        if halves_ref.shape[1] > used:
            halves_ref[half_index, used:, :] = jnp.zeros((halves_ref.shape[1] - used, width), BF16)
    stores[2].start()
    stores[3].start()
    grad_hidden_ref[...] = grad_two
    grad_attn = dot_nt(grad_two_low, wo_ref[...]).astype(BF16)
    grad_attn_ref[...] = grad_attn
    product = grad_attn.T.astype(F32) * attn_t_ref[...]
    for pair in range(PAIRS):
        for side in range(2):
            first = pair * SLAB + side * SIDE
            along = jnp.sum(product[first : first + SIDE], axis=0, keepdims=True)
            for t in range(tiles):
                along_ref[pair * tiles + t : pair * tiles + t + 1, side * TILE : (side + 1) * TILE] = along[
                    :, t * TILE : (t + 1) * TILE
                ]
    ln_ref[...] = jnp.concatenate([gain_two, gain_three, bias_two, bias_three], axis=0)
    for copy in pair_copies + stores:
        copy.wait()


def cross_backward_kernel(
    groups,
    block,
    me_ref,
    len_ref,
    src_ref,
    query_ref,
    norm_ref,
    along_ref,
    grad_attn_ref,
    pair_hbm,
    pair_grad_ref,
    query_grad_t_ref,
    pair_ref,
    live_ref,
    q_pack_ref,
    g_pack_ref,
    key_t_ref,
    query_sum_ref,
    sum_ref,
    load_sem,
):
    rows, width = query_ref.shape
    half = rows // 2
    me = me_ref[0]
    sentences, places = pair_ref.shape[0], pair_ref.shape[1]
    first_sentence = 0 if block == 0 else 1
    load = pltpu.make_async_copy(pair_hbm.at[pl.ds(first_sentence, sentences)], pair_ref, load_sem.at[0])
    load.start()
    order, start, bounds = sentence_order(me, len_ref)
    mine = order[:1] if block == 0 else order[1:]
    fill_live_bias(live_ref, me, groups, list(range(groups)), places // groups, src_ref, mine)
    low = block * half
    pack_heads(q_pack_ref, lambda first, size: query_ref[low + first : low + first + size, :], width)
    pack_heads(g_pack_ref, lambda first, size: grad_attn_ref[low + first : low + first + size, :], width)
    tiles, per = rows // TILE, half // TILE
    units = cross_units(bounds, half)
    units = units[:per] if block == 0 else units[per:]
    load.wait()
    for j in range(sentences):
        key_t_ref[j] = pair_ref[j, :, :width].T

    def pair_step(pair):
        slab, value_slab = slab_of(pair), slab_of(pair, width)
        query_sum_ref[...] = jnp.zeros_like(query_sum_ref)
        sum_ref[...] = jnp.zeros_like(sum_ref)
        for tile, sentence, columns in units:
            j = sentence - first_sentence
            t = tile - block * per
            here = tile_columns(t)
            row = pl.ds(pair * tiles + tile, 1)
            q_rows, g_rows = q_pack_ref[t, :, slab], g_pack_ref[t, :, slab]
            norm = norm_ref[row, :]
            if columns is not None:
                norm = jnp.where(columns, norm, -MASKED)
            scores = dot_nt(pair_ref[j, :, slab], q_rows) + live_ref[j]
            probs = jnp.exp(scores - norm)
            grad_probs = dot_nt(pair_ref[j, :, value_slab], g_rows)
            grad_scores = (probs * (grad_probs - along_ref[row, :])).astype(BF16)
            sum_ref[j, :, :SLAB] += dot(grad_scores, q_rows)
            sum_ref[j, :, SLAB:] += dot(probs.astype(BF16), g_rows)
            query_sum_ref[:, here] += own_sides(dot(key_t_ref[j, slab, :], grad_scores))
        query_grad_t_ref[slab, :] = (query_sum_ref[...] * 0.125).astype(BF16)
        pair_grad_ref[:, :, slab] = sum_ref[:, :, :SLAB].astype(BF16)
        pair_grad_ref[:, :, value_slab] = sum_ref[:, :, SLAB:].astype(BF16)

    for pair in range(PAIRS):
        pair_step(pair)


def memory_weight_kernel(groups, me_ref, len_ref, pair_grad_long_ref, pair_grad_rest_ref, memory_ref, *refs):
    came_refs = refs[: groups - 1]
    wkv_grad_ref, total_ref = refs[groups - 1 :]
    width = memory_ref.shape[2]
    me = me_ref[0]
    count = len_ref.shape[1]
    span = pair_grad_long_ref.shape[1] // groups
    order, _, _ = sentence_order(me, len_ref)
    for j in range(count):
        pair_grad_ref, here = (pair_grad_long_ref, 0) if j == 0 else (pair_grad_rest_ref, j - 1)
        blocks = [memory_ref[me * count + order[j]]] + [ref[order[j]] for ref in came_refs]
        term = dot_tn(jnp.concatenate(blocks, axis=0), pair_grad_ref[here])
        if j == 0:
            total_ref[...] = term
        else:
            total_ref[...] += term
    wkv_grad_ref[0] = total_ref[:, :width].astype(BF16)
    wkv_grad_ref[1] = total_ref[:, width:].astype(BF16)


def memory_grad_kernel(pieces, me_ref, len_ref, pair_grad_long_ref, pair_grad_rest_ref, wkv_ref, *outs):
    count = len_ref.shape[1]
    order, _, _ = sentence_order(me_ref[0], len_ref)
    for j in range(count):
        pair_grad_ref, here = (pair_grad_long_ref, 0) if j == 0 else (pair_grad_rest_ref, j - 1)
        for (first, size), out in zip(pieces, outs):
            out[order[j]] = dot_nt(pair_grad_ref[here, pl.ds(first, size), :], wkv_ref[...]).astype(BF16)


def first_norm_backward_kernel(
    me_ref,
    hidden_one_ref,
    query_grad_t_long_ref,
    query_grad_t_rest_ref,
    grad_hidden_two_ref,
    wq_ref,
    w_out_ref,
    self_attn_t_ref,
    gain_ref,
    bias_row_ref,
    ln_in_ref,
    wkv_grad_ref,
    keep_ref,
    send_ref,
    grad_hidden_ref,
    grad_self_ref,
):
    width = wq_ref.shape[0]
    unit_one, inverse_one = norm_parts(hidden_one_ref[...])
    normed_one = (unit_one * gain_ref[0:1] + bias_row_ref[0:1]).astype(BF16)
    query_grad = jnp.concatenate([query_grad_t_long_ref[...].T, query_grad_t_rest_ref[...].T], axis=0)
    upstream = grad_hidden_two_ref[...] + dot_nt(query_grad, wq_ref[...])
    grad_one, gain_one, bias_one = norm_backward(upstream, unit_one, inverse_one, gain_ref[0:1])
    grad_hidden_ref[...] = grad_one
    grad_one_low = grad_one.astype(BF16)
    grad_self_ref[...] = dot_nt(grad_one_low, w_out_ref[...]).astype(BF16)
    wq_grad = dot_tn(normed_one, query_grad).astype(BF16)
    w_out_grad = dot(self_attn_t_ref[...], grad_one_low).astype(BF16)
    norms = jnp.concatenate(
        [gain_one, ln_in_ref[0:2], bias_one, ln_in_ref[2:4], jnp.zeros((LN_ROWS - 6, width), F32)], axis=0
    ).astype(BF16)

    def halves(low_ref, high_ref):
        low_ref[:width, :] = wq_grad
        low_ref[width : 2 * width, :] = wkv_grad_ref[0]
        high_ref[:width, :] = wkv_grad_ref[1]
        high_ref[width : 2 * width, :] = w_out_grad

    @pl.when(me_ref[1] == 0)
    def _():
        halves(keep_ref, send_ref)

    @pl.when(me_ref[1] != 0)
    def _():
        halves(send_ref, keep_ref)

    keep_ref[2 * width :, :] = norms
    send_ref[2 * width :, :] = norms


def self_backward_kernel(
    me_ref,
    len_ref,
    qkv_ref,
    norm_ref,
    grad_attn_ref,
    sorted_ref,
    grad_triple_ref,
    *refs,
):
    keep_refs, send_refs = refs[:LAST_PARTS], refs[LAST_PARTS : 2 * LAST_PARTS]
    self_backward(
        me_ref,
        len_ref,
        qkv_ref,
        norm_ref,
        grad_attn_ref,
        sorted_ref,
        grad_triple_ref,
        keep_refs,
        send_refs,
        *refs[2 * LAST_PARTS :],
    )


def self_backward(
    me_ref,
    len_ref,
    qkv_ref,
    norm_ref,
    grad_attn_ref,
    sorted_ref,
    grad_triple_ref,
    keep_refs,
    send_refs,
    bias_ref,
    q_pack_ref,
    g_pack_ref,
    key_t_ref,
    query_grad_t_ref,
):
    rows, width = sorted_ref.shape
    half = rows // 2
    _, _, bounds = sentence_order(me_ref[0], len_ref)
    fill_self_bias(bias_ref, bounds, half)
    pack_heads(q_pack_ref, lambda first, size: qkv_ref[first : first + size, :width], width)
    pack_heads(g_pack_ref, lambda first, size: grad_attn_ref[first : first + size, :], width)
    key_t_ref[...] = qkv_ref[:, width : 2 * width].T
    tiles, per = rows // TILE, half // TILE

    def pair_step(pair):
        slab, key_slab, value_slab = slab_of(pair), slab_of(pair, width), slab_of(pair, 2 * width)
        sums = [[None, None] for _ in range(tiles)]
        for t in range(tiles):
            first, size = self_keys(t, half)
            span = pl.ds(first, size)
            q_rows, g_rows = q_pack_ref[t, :, slab], g_pack_ref[t, :, slab]
            scores = dot_nt(qkv_ref[span, key_slab], q_rows) + bias_ref[t, :size, :]
            probs = jnp.exp(scores - norm_ref[pl.ds(pair * tiles + t, 1), :])
            grad_probs = dot_nt(qkv_ref[span, value_slab], g_rows)
            along = jnp.sum(probs * grad_probs, axis=0, keepdims=True)
            grad_scores = (probs * (grad_probs - along)).astype(BF16)
            parts = dot(grad_scores, q_rows), dot(probs.astype(BF16), g_rows)
            for i in range(size // TILE):
                spot = sums[first // TILE + i]
                for k in range(2):
                    piece = parts[k][i * TILE : (i + 1) * TILE]
                    spot[k] = piece if spot[k] is None else spot[k] + piece
            query_grad_t_ref[slab, tile_columns(t)] = (
                own_sides(dot(key_t_ref[slab, span], grad_scores)) * 0.125
            ).astype(BF16)
        for t in range(tiles):
            grad_triple_ref[pl.ds(t * TILE, TILE), key_slab] = sums[t][0].astype(BF16)
            grad_triple_ref[pl.ds(t * TILE, TILE), value_slab] = sums[t][1].astype(BF16)

    for pair in range(PAIRS):
        pair_step(pair)
    grad_triple_ref[:, :width] = query_grad_t_ref[...].T
    sorted_t = sorted_ref[...].T
    grads = [
        dot(sorted_t, grad_triple_ref[:, part * width : (part + 1) * width]).astype(BF16)
        for part in range(3)
    ]
    short = width // 2

    low = jnp.concatenate([grads[0], grads[1][:short]], axis=0)
    high = jnp.concatenate([grads[1][short:], grads[2]], axis=0)
    size = keep_refs[0].shape[0]

    def halves(low_refs, high_refs):
        for i in range(LAST_PARTS):
            low_refs[i][...] = low[i * size : (i + 1) * size]
            high_refs[i][...] = high[i * size : (i + 1) * size]

    @pl.when(me_ref[1] == 0)
    def _():
        halves(keep_refs, send_refs)

    @pl.when(me_ref[1] != 0)
    def _():
        halves(send_refs, keep_refs)


def target_kernel(me_ref, len_ref, grad_triple_ref, w_qkv_ref, grad_hidden_ref, grad_target_ref):
    rows = grad_hidden_ref.shape[0]
    _, start, _ = sentence_order(me_ref[0], len_ref)
    result = grad_hidden_ref[...] + dot_nt(grad_triple_ref[...], w_qkv_ref[...])
    grad_target_ref[...] = dot(unsort_matrix(rows, start), result.astype(BF16)).astype(BF16)


def tree_sum(terms):
    while len(terms) > 1:
        terms = [terms[i] + terms[i + 1] for i in range(0, len(terms), 2)]
    return terms[0]


def rows_of(ref, first, count):
    return ref[pl.ds(pl.multiple_of(first, 16), count), :].astype(F32)


def first_split_kernel(segments, ln, peers, spot_ref, *refs):
    ins, refs = refs[: 2 * segments], refs[2 * segments :]
    extra = LN_ROWS if ln else 0
    if segments == 1 and not ln:
        for d, out in enumerate(refs):
            size = out.shape[0]
            first = (spot_ref[2] ^ d) * size
            out[...] = (rows_of(ins[0], first, size) + rows_of(ins[1], first, size)).astype(BF16)
        return
    outs, sum_ref = refs[:-1], refs[-1]
    size = outs[0].shape[0] - extra
    used = 0
    for i in range(segments):
        keep_ref, came_ref = ins[2 * i], ins[2 * i + 1]
        count = keep_ref.shape[0] - (extra if i == 0 else 0)
        sum_ref[used : used + count, :] = (rows_of(keep_ref, 0, count) + rows_of(came_ref, 0, count)).astype(BF16)
        if i == 0 and ln:
            tail = (rows_of(keep_ref, count, LN_ROWS) + rows_of(came_ref, count, LN_ROWS)).astype(BF16)
        used += count
    if sum_ref.shape[0] > used:
        sum_ref[used:, :] = jnp.zeros((sum_ref.shape[0] - used, sum_ref.shape[1]), BF16)
    for d, out in enumerate(outs):
        out[:size, :] = sum_ref[pl.ds(pl.multiple_of((spot_ref[2] ^ d) * size, 16), size), :]
        if ln:
            out[size:, :] = tail


def split_kernel(stage, ln, peers, spot_ref, *refs):
    ins, outs = refs[:peers], refs[peers:]
    extra = LN_ROWS if ln else 0
    size = outs[0].shape[0] - extra
    if ln:
        tail = tree_sum([rows_of(ref, size * len(outs), LN_ROWS) for ref in ins]).astype(BF16)
    for d, out in enumerate(outs):
        first = (spot_ref[2 + stage] ^ d) * size
        out[:size, :] = tree_sum([rows_of(ref, first, size) for ref in ins]).astype(BF16)
        if ln:
            out[size:, :] = tail


def total_kernel(ln, count, *refs):
    ins, outs = refs[:count], refs[count:]
    size = outs[0].shape[0]
    outs[0][...] = tree_sum([rows_of(ref, 0, size) for ref in ins]).astype(BF16)
    if ln:
        norms = tree_sum([rows_of(ref, size, LN_ROWS) for ref in ins])
        outs[1][...] = norms[:3]
        outs[2][...] = norms[3:6]


def join_kernel(stage, spot_ref, *refs):
    out_ref = refs[-1]
    for d, ref in enumerate(refs[:-1]):
        size = ref.shape[0]
        out_ref[pl.ds(pl.multiple_of((spot_ref[2 + stage] ^ d) * size, 16), size), :] = ref[...]


def finish_kernel(offsets, peers, twisted, pieces, held, spot_ref, *refs):
    arrays, refs = refs[: 2 * len(offsets)], refs[2 * len(offsets) + held :]
    outs, (wide_ref, sem) = refs[:-2], refs[-2:]
    core = spot_ref[1]
    size, width = wide_ref.shape[1:]
    copies = []
    for k, ref in enumerate(arrays):
        wide_ref[k] = ref[...].astype(F32)
        d, other = offsets[k // 2], k % 2
        half = 1 - core if other else core
        place = spot_ref[3 if twisted and other else 2] ^ d
        for i in range(2):
            for j in range(peers):
                cut = []
                for piece_half, first, rows, out, row, col in pieces:
                    low, high = max(first, j * size), min(first + rows, (j + 1) * size)
                    if piece_half == i and low < high:
                        there = outs[out].at[pl.ds(row + low - first, high - low), pl.ds(col, width)]
                        here = wide_ref.at[k, pl.ds(low - j * size, high - low), :]
                        cut.append(pltpu.make_async_copy(here, there, sem.at[k, len(cut)]))
                copies.append(((half == i) & (place == j), cut))
                _start_all(*copies[-1])
    for chosen, cut in copies:
        _wait_all(chosen, cut)


def _start_all(chosen, cut):
    @pl.when(chosen)
    def _():
        for copy in cut:
            copy.start()


def _wait_all(chosen, cut):
    @pl.when(chosen)
    def _():
        for copy in cut:
            copy.wait()


class Summing:
    def __init__(self, rows, width, ln):
        self.width, self.ln = width, ln
        self.dp, self.mem = lax.axis_size("dp"), lax.axis_size("mem")
        z_size = 4
        x_size = self.dp // (2 * z_size)
        self.sizes = (x_size, self.mem, z_size)
        self.twisted = x_size == self.mem
        self.chunk = -(-rows // (16 * math.prod(self.sizes))) * 16
        self.rows = self.chunk * math.prod(self.sizes)

    def after(self, stage):
        return self.rows // math.prod(self.sizes[:stage])

    def axis(self, stage, core):
        return 1 - stage if self.twisted and core == 1 and stage < 2 else stage

    def coords(self, dp, mem):
        return [dp // 2 % self.sizes[0], mem, dp // (2 * self.sizes[0])], dp % 2

    def spot(self, me, dp):
        (x, mem, z), core = self.coords(dp, me)
        if self.twisted:
            x, mem = jnp.where(core == 0, x, mem), jnp.where(core == 0, mem, x)
        return jnp.stack([me, core, x, mem, z]).astype(jnp.int32)

    def permute(self, array, stage, offset):
        pairs = []
        for dp in range(self.dp):
            for mem in range(self.mem):
                spots, core = self.coords(dp, mem)
                if stage is None:
                    core ^= offset
                else:
                    spots[self.axis(stage, core)] ^= offset
                to_dp = (spots[2] * self.sizes[0] + spots[0]) * 2 + core
                pairs.append((dp * self.mem + mem, to_dp * self.mem + spots[1]))
        return lax.ppermute(array, ("dp", "mem"), pairs)

    def core_swap(self, send):
        return self.permute(send, None, 1)

    def swap(self, arrays, stage):
        return [arrays[0]] + [self.permute(array, stage, d) for d, array in enumerate(arrays) if d > 0]

    def spread(self, stage, array):
        return [array] + [self.permute(array, stage, d) for d in range(1, self.sizes[stage])]

    def messages(self, stage):
        size = self.after(stage + 1) + (LN_ROWS if self.ln else 0)
        return [((size, self.width), BF16)] * self.sizes[stage]

    def first_split(self, spot, *arrays):
        kernel = functools.partial(first_split_kernel, len(arrays) // 2, self.ln, self.sizes[0])
        scratch = [] if len(arrays) == 2 and not self.ln else [((self.rows, self.width), BF16)]
        return call(kernel, self.messages(0), scratch, 1, spot, *arrays, work=0.01)

    def split(self, stage, spot, arrays, work=0.01):
        kernel = functools.partial(split_kernel, stage, self.ln, self.sizes[stage - 1])
        return call(kernel, self.messages(stage), [], 1, spot, *arrays, work=work)

    def total(self, arrays, work=0.01):
        outs = [((self.chunk, self.width), BF16)]
        if self.ln:
            outs = outs + [((3, self.width), F32)] * 2
        return call(functools.partial(total_kernel, self.ln, self.sizes[2]), outs, [], 0, *arrays, work=work)

    def join(self, stage, spot, arrays, work=0.01):
        outs = [((self.after(stage), self.width), BF16)]
        return call(functools.partial(join_kernel, stage), outs, [], 1, spot, *arrays, work=work)[0]

    def finish(self, spot, mine, others, offsets, pieces, outs, held=()):
        kernel = functools.partial(finish_kernel, offsets, self.sizes[0], self.twisted, pieces, len(held))
        arrays = [array for d in offsets for array in (mine[d], others[d])]
        size = self.after(1)
        scratch = [((len(arrays), size, self.width), F32), pltpu.SemaphoreType.DMA((len(arrays), len(pieces)))]
        aliases = {1 + len(arrays) + i: i for i in range(len(held))}
        return call(
            kernel,
            outs,
            scratch,
            1,
            spot,
            *arrays,
            *held,
            work=1,
            vmem=40,
            hbm_in=len(held),
            hbm_out=len(outs),
            aliases=aliases,
        )


def call(kernel, outs, scratch, scalars, *arrays, work=0.5, vmem=0, hbm_in=0, hbm_out=0, aliases=None):
    plain = len(arrays) - scalars - hbm_in
    if not vmem:
        blocks = [(array.shape, array.dtype) for array in arrays[scalars:]] + outs
        blocks = blocks + [entry for entry in scratch if isinstance(entry, tuple)]
        vmem = max(16, sum(math.prod(shape) * jnp.dtype(kind).itemsize for shape, kind in blocks) // MIB + 7)
    specs = [pl.BlockSpec(memory_space=pltpu.SMEM)] * scalars
    specs = specs + [pl.BlockSpec(memory_space=pltpu.VMEM)] * plain
    specs = specs + [pl.BlockSpec(memory_space=pl.ANY)] * hbm_in
    out_specs = [pl.BlockSpec(memory_space=pltpu.VMEM)] * (len(outs) - hbm_out)
    out_specs = out_specs + [pl.BlockSpec(memory_space=pl.ANY)] * hbm_out
    return pl.pallas_call(
        kernel,
        out_shape=[jax.ShapeDtypeStruct(shape, kind) for shape, kind in outs],
        in_specs=specs,
        out_specs=out_specs,
        scratch_shapes=[pltpu.VMEM(*entry) if isinstance(entry, tuple) else entry for entry in scratch],
        input_output_aliases=aliases or {},
        compiler_params=pltpu.CompilerParams(vmem_limit_bytes=vmem * MIB),
        cost_estimate=pl.CostEstimate(flops=int(work * 1e9), bytes_accessed=int(work * 3e6), transcendentals=0),
    )(*arrays)


def middle(
    groups, first_sum, stats, spot, tgt_len, src_len, hidden_one, query, part, part_top, part_sum, wkv_cross,
    ln_gain, ln_bias, wo_cross, w_up, w_down, grad_out, pair_mine, came,
):
    rows, width = hidden_one.shape
    half, tiles = rows // 2, rows // TILE
    hidden_width = w_down.shape[0]
    count, places, _ = pair_mine.shape
    away = places // groups * (groups - 1)
    arrays = [spot, tgt_len, src_len, hidden_one, query, part, part_top, part_sum, wkv_cross, ln_gain, ln_bias]
    stay = [wo_cross, w_up, w_down, grad_out, pair_mine]

    def kernel(*refs):
        ins, refs = refs[: len(arrays)], refs[len(arrays) :]
        came_refs, refs = refs[: len(came)], refs[len(came) :]
        stay_refs, refs = refs[: len(stay)], refs[len(stay) :]
        outs, refs = refs[:9], refs[9:]
        middle_kernel(groups, *ins, *stay_refs, *came_refs, *outs[:3], *outs[6:8], *outs[3:6], outs[8], *refs)

    result_out, cross_norm, cross_along, grad_hidden_two, grad_attn, ln_part, keep_one, send_one, pair_all = call(
        kernel,
        [
            ((rows, width), BF16),
            (stats, F32),
            (stats, F32),
            ((rows, width), F32),
            ((rows, width), BF16),
            ((4, width), F32),
            ((first_sum.rows, width), BF16),
            ((first_sum.rows, width), BF16),
            ((count, places, 2 * width), BF16),
        ],
        [
            ((width, width), BF16),
            ((width, hidden_width), BF16),
            ((hidden_width, width), BF16),
            ((rows, width), BF16),
            ((count, away, 2 * width), BF16),
            ((2, first_sum.rows, width), BF16),
            ((count, away, 2 * TILE), F32),
            ((tiles, 2 * TILE, width), BF16),
            ((count, width, away), BF16),
            ((width, rows), F32),
            ((rows, hidden_width), BF16),
            ((rows, hidden_width), F32),
            ((rows, hidden_width), BF16),
            pltpu.SemaphoreType.DMA((4,)),
            pltpu.SemaphoreType.DMA((count,)),
            pltpu.SemaphoreType.DMA((4,)),
        ],
        3,
        *arrays,
        *came,
        *stay,
        vmem=60,
        hbm_in=len(stay),
        hbm_out=3,
        aliases={len(arrays) + len(came) + len(stay) - 1: 8},
    )
    return result_out, cross_norm, cross_along, keep_one, send_one, grad_hidden_two, grad_attn, ln_part, pair_all


def body(
    target,
    memory,
    grad_out,
    tgt_len,
    src_len,
    w_qkv,
    w_out,
    wq_cross,
    wkv_cross,
    wo_cross,
    w_up,
    w_down,
    ln_gain,
    ln_bias,
):
    rows, width = target.shape
    half = rows // 2
    tiles = rows // TILE
    hidden_width = w_down.shape[0]
    groups = lax.axis_size("mem")
    me = lax.axis_index("mem")
    count = tgt_len.shape[1]
    span = memory.shape[1]
    places, away = groups * span, (groups - 1) * span
    dp = lax.axis_index("dp")
    short = width // 2
    first_sum = Summing(hidden_width + short, width, False)
    second_sum = Summing(3 * width + short, width, True)
    spot = first_sum.spot(me, dp)
    stats = (PAIRS * tiles, 2 * TILE)

    came = []
    for shift in range(1, groups):
        pairs = [(i, (i + shift) % groups) for i in range(groups)]
        sent = lax.dynamic_slice_in_dim(memory, ((me + shift) % groups) * count, count, 0)
        came.append(lax.ppermute(sent, "mem", pairs))

    sorted_rows, qkv, self_norm, self_attn_t, hidden_one, query, part, part_top, part_sum, pair_mine = call(
        functools.partial(self_forward_kernel, groups),
        [
            ((rows, width), BF16),
            ((rows, 3 * width), BF16),
            (stats, F32),
            ((width, rows), BF16),
            ((rows, width), F32),
            ((rows, width), BF16),
            ((width, rows), F32),
            (stats, F32),
            (stats, F32),
            ((count, places, 2 * width), BF16),
        ],
        [
            ((tiles, half, 2 * TILE), F32),
            ((count, span, 2 * TILE), F32),
            ((tiles, 2 * TILE, width), BF16),
            ((width, rows), BF16),
            ((count, width, span), BF16),
            ((count, span, 2 * width), BF16),
            pltpu.SemaphoreType.DMA((count,)),
        ],
        3,
        spot,
        tgt_len,
        src_len,
        target,
        w_qkv,
        w_out,
        wq_cross,
        ln_gain,
        ln_bias,
        memory,
        wkv_cross,
        vmem=60,
        hbm_out=1,
    )
    result_out, cross_norm, cross_along, keep_one, send_one, grad_hidden_two, grad_attn, ln_part, pair_all = middle(
        groups, first_sum, stats, spot, tgt_len, src_len, hidden_one, query, part, part_top, part_sum, wkv_cross,
        ln_gain, ln_bias, wo_cross, w_up, w_down, grad_out, pair_mine, came,
    )
    came_one = first_sum.core_swap(send_one)

    def cross_backward(block):
        sentences = 1 if block == 0 else count - 1
        return call(
            functools.partial(cross_backward_kernel, groups, block),
            [((sentences, places, 2 * width), BF16), ((width, half), BF16)],
            [
                ((sentences, places, 2 * width), BF16),
                ((sentences, places, 2 * TILE), F32),
                ((half // TILE, 2 * TILE, width), BF16),
                ((half // TILE, 2 * TILE, width), BF16),
                ((sentences, width, places), BF16),
                ((SLAB, half), F32),
                ((sentences, places, 2 * SLAB), F32),
                pltpu.SemaphoreType.DMA((1,)),
            ],
            3,
            spot,
            tgt_len,
            src_len,
            query,
            cross_norm,
            cross_along,
            grad_attn,
            pair_all,
            work=10,
            vmem=58 if block == 0 else 32,
            hbm_in=1,
        )

    pair_grad_long, query_grad_t_long = cross_backward(0)
    came_one, pair_grad_long = lax.optimization_barrier((came_one, pair_grad_long))
    parts_one = first_sum.first_split(spot, keep_one, came_one)
    parts_one, pair_all = lax.optimization_barrier((parts_one, pair_all))
    parts_one = first_sum.swap(parts_one, 0)
    pair_grad_rest, query_grad_t_rest = cross_backward(1)
    (wkv_grad,) = call(
        functools.partial(memory_weight_kernel, groups),
        [((2, width, width), BF16)],
        [((width, 2 * width), F32)],
        2,
        spot,
        tgt_len,
        pair_grad_long,
        pair_grad_rest,
        memory,
        *came,
        work=1,
        vmem=32,
    )
    keep_mid, send_mid, grad_hidden_one, grad_self = call(
        first_norm_backward_kernel,
        [
            ((2 * width + LN_ROWS, width), BF16),
            ((2 * width + LN_ROWS, width), BF16),
            ((rows, width), F32),
            ((rows, width), BF16),
        ],
        [],
        1,
        spot,
        hidden_one,
        query_grad_t_long,
        query_grad_t_rest,
        grad_hidden_two,
        wq_cross,
        w_out,
        self_attn_t,
        ln_gain,
        ln_bias,
        ln_part,
        wkv_grad,
        work=0.1,
        vmem=24,
    )
    def memory_grad(pieces, pair_grad_long):
        return call(
            functools.partial(memory_grad_kernel, pieces),
            [((count, size, width), BF16) for _, size in pieces],
            [],
            2,
            spot,
            tgt_len,
            pair_grad_long,
            pair_grad_rest,
            wkv_cross,
            work=0.01,
            vmem=32,
        )

    def send_back(grads):
        return [
            lax.ppermute(array, "mem", [(k, (k - 1 - i) % groups) for k in range(groups)])
            for i, array in enumerate(grads)
        ]

    parts_one, grad_self = lax.optimization_barrier((parts_one, grad_self))
    parts_one = first_sum.split(1, spot, parts_one)
    parts_one, grad_self, pair_grad_long = lax.optimization_barrier((parts_one, grad_self, pair_grad_long))
    parts_one = first_sum.swap(parts_one, 1)
    grad_late = memory_grad(
        [(part * span + span // 2, span // 2) for part in range(1, groups)], pair_grad_long
    )
    backs_late = send_back(grad_late)
    grad_late, grad_self = lax.optimization_barrier((grad_late, grad_self))
    grad_triple, *last = call(
        self_backward_kernel,
        [((rows, 3 * width), BF16)] + [(((width + short) // LAST_PARTS, width), BF16)] * (2 * LAST_PARTS),
        [
            ((tiles, half, 2 * TILE), F32),
            ((tiles, 2 * TILE, width), BF16),
            ((tiles, 2 * TILE, width), BF16),
            ((width, rows), BF16),
            ((width, rows), BF16),
        ],
        2,
        spot,
        tgt_len,
        qkv,
        self_norm,
        grad_self,
        sorted_rows,
        work=0.1,
        vmem=28,
    )
    came_mid = second_sum.core_swap(send_mid)
    parts_one, last, came_mid, pair_grad_long = lax.optimization_barrier(
        (parts_one, last, came_mid, pair_grad_long)
    )
    keep_last = last[:LAST_PARTS]
    came_last = [second_sum.core_swap(part) for part in last[LAST_PARTS:]]
    parts_one = first_sum.split(2, spot, parts_one)
    came_mid, parts_one = lax.optimization_barrier((came_mid, parts_one))
    parts_two = second_sum.first_split(
        spot, keep_mid, came_mid, *[part for both in zip(keep_last, came_last) for part in both]
    )
    parts_one = first_sum.swap(parts_one, 2)
    parts_two, pair_grad_long, grad_triple = lax.optimization_barrier((parts_two, pair_grad_long, grad_triple))
    parts_two = second_sum.swap(parts_two, 0)
    grad_mine, *grad_away = memory_grad(
        [(0, span)] + [(part * span, span // 2) for part in range(1, groups)], pair_grad_long
    )
    backs_late, grad_triple = lax.optimization_barrier((backs_late, grad_triple))
    (grad_target,) = call(
        target_kernel,
        [((rows, width), BF16)],
        [],
        2,
        spot,
        tgt_len,
        grad_triple,
        w_qkv,
        grad_hidden_one,
        work=30,
        vmem=16,
    )
    parts_one, grad_away, grad_target = lax.optimization_barrier((parts_one, grad_away, grad_target))
    spread_one = first_sum.spread(2, first_sum.total(parts_one)[0])
    backs_early = send_back(grad_away)
    parts_two = second_sum.swap(second_sum.split(1, spot, parts_two), 1)
    joined_one = first_sum.join(2, spot, spread_one, work=0.01)
    spread_one = first_sum.spread(1, joined_one)
    parts_two, joined_one = lax.optimization_barrier((parts_two, joined_one))
    parts_two = second_sum.split(2, spot, parts_two, work=0.01)
    spread_one, _ = lax.optimization_barrier((spread_one, parts_two))
    parts_two = second_sum.swap(parts_two, 2)
    joined_one = first_sum.join(1, spot, spread_one)
    spread_one = first_sum.spread(0, joined_one)
    parts_two, joined_one = lax.optimization_barrier((parts_two, joined_one))
    sum_two, *norm_sums = second_sum.total(parts_two, work=0.01)
    spread_two = second_sum.spread(2, sum_two)
    spread_two, backs_early = lax.optimization_barrier((spread_two, backs_early))
    spread_two = second_sum.spread(1, second_sum.join(2, spot, spread_two, work=6.3))
    joined_two = second_sum.join(1, spot, spread_two)
    spread_one, joined_two = lax.optimization_barrier((spread_one, joined_two))
    other_one = [first_sum.core_swap(array) for array in spread_one]
    chunks = hidden_width // width
    pieces = []
    for chunk in range(chunks):
        side, here = chunk // (chunks // 2), chunk % (chunks // 2)
        pieces.append((side, here * width, width, 0, chunk * width, 0))
        pieces.append((side, (chunks // 2 + here) * width, width, 1, 0, chunk * width))
    for side in range(2):
        pieces.append((side, chunks * width, short, 2, side * short, 0))
    grad_w_down, grad_w_up, grad_wo = first_sum.finish(
        spot,
        spread_one,
        other_one,
        list(range(len(spread_one))),
        pieces,
        [((hidden_width, width), F32), ((width, hidden_width), F32), ((width, width), F32)],
    )
    spread_two = second_sum.spread(0, joined_two)
    pieces = [
        (0, 0, width, 0, 0, 0),
        (0, width, width, 1, 0, 0),
        (0, 2 * width, width, 2, 0, 0),
        (0, 3 * width, short, 2, 0, width),
        (1, 0, width, 1, 0, width),
        (1, width, width, 3, 0, 0),
        (1, 2 * width, short, 2, short, width),
        (1, 2 * width + short, width, 2, 0, 2 * width),
    ]
    outs = [
        ((width, width), F32),
        ((width, 2 * width), F32),
        ((width, 3 * width), F32),
        ((width, width), F32),
    ]
    other_two = [second_sum.core_swap(spread_two[0])]
    own_two, grad_w_down = lax.optimization_barrier((spread_two[0], grad_w_down))
    held = second_sum.finish(spot, [own_two], other_two, [0], pieces, outs)
    spread_two, held = lax.optimization_barrier((spread_two, held))
    other_two = other_two + [second_sum.core_swap(array) for array in spread_two[1:]]
    grad_wq, grad_wkv, grad_w_qkv, grad_w_out = second_sum.finish(
        spot, spread_two, other_two, list(range(1, len(spread_two))), pieces, outs, held
    )
    grad_memory = jnp.zeros(memory.shape, BF16)
    grad_memory = lax.dynamic_update_slice(grad_memory, grad_mine, (me * count, 0, 0))
    for part, backs in enumerate((backs_early, backs_late)):
        for i, grads in enumerate(backs):
            owner = (me + i + 1) % groups
            grad_memory = lax.dynamic_update_slice(grad_memory, grads, (owner * count, part * (span // 2), 0))
    return (
        result_out,
        grad_target,
        grad_memory,
        grad_w_qkv,
        grad_w_out,
        grad_wq,
        grad_wkv,
        grad_wo,
        grad_w_up,
        grad_w_down,
        *norm_sums,
    )


def solution(mesh):
    rows_spec = P(("dp", "mem"), None)
    memory_spec = P("dp", "mem", None)
    return jax.shard_map(
        body,
        mesh=mesh,
        in_specs=(rows_spec, memory_spec, rows_spec, P("dp", None), P("dp", None)) + (P(),) * 9,
        out_specs=(rows_spec, rows_spec, memory_spec) + (P(),) * 9,
        check_vma=False,
    )
```
